32 devices in a mesh: ep: 8 (over z, y), tp: 4 (over x, core).
Axes of the slice: x: 2, y: 2, z: 4, core: 2. Of those that a mesh axis runs over, the one named last changes fastest.
Arguments:
- inputs: bfloat16 [8192, 2048], P('ep'), may hold values from -6 to 6
- attn_gain: float32 [2048], replicated, may hold values from 0.5 to 1.5
- w_query: bfloat16 [2048, 4096], P(None, 'tp'), may hold values from -0.125 to 0.125
- key_weight_matrix: bfloat16 [2048, 512], P(None, 'tp'), may hold values from -0.125 to 0.125
- value_weight_matrix: bfloat16 [2048, 512], P(None, 'tp'), may hold values from -0.125 to 0.125
- query_gain: float32 [128], replicated, may hold values from 0.5 to 1.5
- key_gain: float32 [128], replicated, may hold values from 0.5 to 1.5
- w_out: bfloat16 [4096, 2048], P('tp'), may hold values from -1 to 1
- route_gain: float32 [2048], replicated, may hold values from 0.5 to 1.5
- w_router: bfloat16 [2048, 32], replicated, may hold values from -0.0625 to 0.0625
- w_gate: bfloat16 [32, 2048, 768], P('ep', None, 'tp'), may hold values from -0.125 to 0.125
- w_up: bfloat16 [32, 2048, 768], P('ep', None, 'tp'), may hold values from -0.125 to 0.125
- w_down: bfloat16 [32, 768, 2048], P('ep', 'tp'), may hold values from -0.625 to 0.625
- routes: int32 [8192, 8], replicated, may hold values from 0 to 31, all different within a row; in each aligned block of 256 rows (0 to 255, 256 to 511, ...) at most 96 rows name the same one
- image_starts: int32 [8, 2], P('ep'), may hold values from 0 to 768, as said below
- cotangent: bfloat16 [8192, 2048], P(('ep', 'tp')), may hold values from -6 to 6
Outputs:
- output: bfloat16 [8192, 2048], P(('ep', 'tp'))
- aux_loss: float32 [], replicated
- inputs_grad: float32 [8192, 2048], P(('ep', 'tp'))
- attn_gain_grad: float32 [2048], replicated
- w_query_grad: float32 [2048, 4096], P('ep', 'tp')
- w_key_grad: float32 [2048, 512], P('ep', 'tp')
- w_value_grad: float32 [2048, 512], P('ep', 'tp')
- query_gain_grad: float32 [128], replicated
- key_gain_grad: float32 [128], replicated
- w_out_grad: float32 [4096, 2048], P('tp', 'ep')
- route_gain_grad: float32 [2048], replicated
- w_router_grad: float32 [2048, 32], replicated
- w_gate_grad: float32 [32, 2048, 768], P('ep', None, 'tp')
- w_up_grad: float32 [32, 2048, 768], P('ep', None, 'tp')
- w_down_grad: float32 [32, 768, 2048], P('ep', 'tp')
The draws below stay inside these ranges and needn't reach their ends.
Inputs may be any that keep to these rules, and one draw needn't show every extreme that they name: `routes`: each row names 8 different experts; within the rows of one device, the aligned blocks of 256 rows, no expert is named more than 96 times. `image_starts`: row s holds the first tokens of the two image spans of sequence s, each 256 tokens long; the first span starts in the first half of the sequence, the second in the second half.
All inputs are finite; a program needn't handle non-finite values.
Results may differ from the reference program's by a relative error of at most 0.025.
Values may be sent and summed in bfloat16 or wider, within the bound.
A program may use at most 704 MiB of HBM per device.

```python
import math
import jax
import jax.numpy as jnp
import numpy as np
from jax import lax

MODEL_WIDTH = 2048
QUERY_HEADS = 32
KEY_VALUE_HEADS = 4
HEAD_SIZE = 128
FF = 768
TOPK = 8
SEQUENCE_TOKENS = 1024
IMG = 256
EXPERTS = 32
TOKENS = 8192
ROWS = 256
CAP = 96
N_EP = 8


def draw_image_starts(key, part):
    key = jax.random.fold_in(key, 11)
    first_key, second_key = jax.random.split(key)
    first = jax.random.randint(first_key, (N_EP,), 0, SEQUENCE_TOKENS // 2 - IMG + 1)
    second = jax.random.randint(second_key, (N_EP,), SEQUENCE_TOKENS // 2, SEQUENCE_TOKENS - IMG + 1)
    first = first.at[0].set(0)
    second = second.at[N_EP - 1].set(SEQUENCE_TOKENS - IMG)
    return jnp.stack([first, second], axis=1).astype(jnp.int32)


def block_scale(own_key, shape, cuts, smallest, top_value):
    def one(dim, shards_of):
        draws = jax.random.uniform(jax.random.fold_in(jax.random.fold_in(own_key, 6), dim), (shards_of,), jnp.float32, smallest / len(cuts), top_value / len(cuts))
        return jnp.repeat(jnp.exp(draws), shape[dim] // shards_of).reshape((-1,) + (1,) * (len(shape) - dim - 1))

    factor_of = one(*cuts[0])
    for cut in cuts[1:]:
        factor_of = factor_of * one(*cut)
    return factor_of


def routed_block(stream_key, own, number, rows, number_of, top, bound, lean):
    sequence = jax.random.permutation(stream_key, number_of)
    crowded, ordinary = portions_of(number_of, rows * top, bound, lean, True), portions_of(number_of, rows * top, bound, lean, False)
    places = jnp.arange(number_of)

    def named(lengths, rotation):
        used = int((lengths > 0).sum())
        fixed = max(1, used // 4)
        passed = fixed + (places - fixed + rotation * (used - fixed)) % max(1, number_of - fixed)
        return jnp.zeros((number_of,), jnp.int32).at[sequence[jnp.where(places < fixed, places, passed)]].set(jnp.asarray(lengths, jnp.int32))

    lengths = jnp.where(number % 4 == 0, named(crowded, number // 4), named(ordinary, number - number // 4 - 1))
    mixed = jax.random.permutation(jax.random.fold_in(own, 3), number_of)
    giver, receiver = mixed[0:number_of // 2 * 2:2], mixed[1:number_of // 2 * 2:2]
    margin = jnp.minimum(lengths[giver] - 1, bound - lengths[receiver]) // 2
    margin = jnp.where((giver == sequence[0]) | (receiver == sequence[0]) | (lengths[receiver] == 0), 0, jnp.maximum(margin, 0))
    passed = jax.random.randint(jax.random.fold_in(own, 4), (number_of // 2,), 0, 1 << 20) % (margin + 1)
    lengths = lengths.at[giver].add(-passed).at[receiver].add(passed)
    items = jnp.searchsorted(jnp.cumsum(lengths), jnp.arange(rows * top), side="right").astype(jnp.int32)
    listing = items.reshape(top, rows).T
    listing = listing[jax.random.permutation(jax.random.fold_in(own, 1), rows)]
    rotation = jax.random.randint(jax.random.fold_in(own, 2), (rows, 1), 0, top)
    return jnp.take_along_axis(listing, (jnp.arange(top)[None, :] + rotation) % top, axis=1)


def portions_of(amount, total, most, lean, full):
    loads = [(1 << 20) // math.isqrt(standing ** lean) + 1 for standing in range(1, amount + 1)]
    largest = most if full else min(most, max(-(-total // amount), total * loads[0] // sum(loads)))
    least = 1 if total - largest >= amount - 1 else 0
    given, surplus = [largest] + [least] * (amount - 1), total - largest - least * (amount - 1)
    while surplus > 0:
        candidates = [i for i in range(1, amount) if given[i] < largest] or [i for i in range(1, amount) if given[i] < most]
        pool, budget = sum([loads[i] for i in candidates]), surplus
        for i in candidates:
            more = min(most - given[i], max(1, budget * loads[i] // pool), surplus)
            given[i] = given[i] + more
            surplus = surplus - more
    return np.array(given)


def gaussian(stream_key, shape, spread, reach, shards=(), kind=jnp.bfloat16):
    level = block_scale(stream_key, shape, shards, -0.22, 0.18) if shards else 1.0
    array = jax.random.normal(stream_key, shape, jnp.float32) * spread * level
    return jnp.minimum(jnp.maximum(array, -reach), reach).astype(kind)


def setup_inputs(seed: int = 0) -> dict:
    arg_keys = jax.random.split(jax.random.key(seed), 17)
    inputs = gaussian(arg_keys[0], (TOKENS, MODEL_WIDTH), 1.0, 6.0, ((0, 8),))
    attn_gain = jnp.clip(1.0 + 0.1 * jax.random.normal(arg_keys[1], (MODEL_WIDTH,), jnp.float32), 0.5, 1.5)
    w_query = gaussian(arg_keys[2], (MODEL_WIDTH, QUERY_HEADS * HEAD_SIZE), MODEL_WIDTH ** -0.5, 0.125, ((1, 4),))
    key_weight_matrix = gaussian(arg_keys[3], (MODEL_WIDTH, KEY_VALUE_HEADS * HEAD_SIZE), MODEL_WIDTH ** -0.5, 0.125, ((1, 4),))
    value_weight_matrix = gaussian(arg_keys[4], (MODEL_WIDTH, KEY_VALUE_HEADS * HEAD_SIZE), MODEL_WIDTH ** -0.5, 0.125, ((1, 4),))
    query_gain = jnp.clip(1.0 + 0.1 * jax.random.normal(arg_keys[5], (HEAD_SIZE,), jnp.float32), 0.5, 1.5)
    key_gain = jnp.clip(1.0 + 0.1 * jax.random.normal(arg_keys[6], (HEAD_SIZE,), jnp.float32), 0.5, 1.5)
    w_out = gaussian(arg_keys[7], (QUERY_HEADS * HEAD_SIZE, MODEL_WIDTH), (max(QUERY_HEADS * HEAD_SIZE // 128, 1)) ** -0.5, 1.0, ((0, 4),))
    route_gain = jnp.clip(1.0 + 0.1 * jax.random.normal(arg_keys[8], (MODEL_WIDTH,), jnp.float32), 0.5, 1.5)
    w_router = gaussian(arg_keys[9], (MODEL_WIDTH, EXPERTS), (4 * MODEL_WIDTH) ** -0.5, 0.0625)
    w_gate = gaussian(arg_keys[10], (EXPERTS, MODEL_WIDTH, FF), MODEL_WIDTH ** -0.5, 0.125, ((0, 8), (2, 4)))
    w_up = gaussian(arg_keys[11], (EXPERTS, MODEL_WIDTH, FF), MODEL_WIDTH ** -0.5, 0.125, ((0, 8), (2, 4)))
    w_down = gaussian(arg_keys[12], (EXPERTS, FF, MODEL_WIDTH), (FF // 8) ** -0.5, 0.625, ((0, 8), (1, 4)))
    routes_keys = jax.random.split(jax.random.fold_in(arg_keys[13], 1), TOKENS // ROWS)
    routes_turns = jax.random.permutation(jax.random.fold_in(arg_keys[13], 3), TOKENS // ROWS)
    routes = jax.vmap(lambda own, number: routed_block(jax.random.fold_in(arg_keys[13], 2), own, number, ROWS, EXPERTS, TOPK, CAP, 1))(routes_keys, routes_turns).reshape((TOKENS, TOPK))
    image_starts = draw_image_starts(jax.random.fold_in(arg_keys[16], 71), 0)
    cotangent = gaussian(arg_keys[15], (TOKENS, MODEL_WIDTH), 1.0, 6.0, ((0, 32),))
    return dict(inputs=inputs, attn_gain=attn_gain, w_query=w_query, key_weight_matrix=key_weight_matrix, value_weight_matrix=value_weight_matrix, query_gain=query_gain, key_gain=key_gain, w_out=w_out, route_gain=route_gain, w_router=w_router, w_gate=w_gate, w_up=w_up, w_down=w_down, routes=routes, image_starts=image_starts, cotangent=cotangent)


EPS = 1e-06
AUX = 0.04
THETA = 1000000.0
PRECISION_HIGH = lax.Precision.HIGHEST

@jax.custom_vjp
def lower_precision(v):
    return lax.optimization_barrier(v.astype(jnp.bfloat16)).astype(jnp.float32)

@jax.custom_vjp
def lower_precision_back(v):
    return v

def low_keep(v):
    return (lower_precision(v), None)

def low_pass(kept, grad):
    return (grad,)

def back_keep(v):
    return (v, None)

def back_low(kept, grad):
    return (lower_precision(grad),)
lower_precision.defvjp(low_keep, low_pass)
lower_precision_back.defvjp(back_keep, back_low)

def rms_scale(value_rows):
    return lax.rsqrt(lax.optimization_barrier(jnp.mean(value_rows * value_rows, axis=-1, keepdims=True)) + EPS)

def plain_softmax(value_rows):
    top = lax.optimization_barrier(jnp.max(value_rows, axis=-1, keepdims=True))
    expo = jnp.exp(value_rows - top)
    return expo / lax.optimization_barrier(jnp.sum(expo, axis=-1, keepdims=True))

def rope_tables(length, size):
    half = size // 2
    freq = jnp.exp(-jnp.log(THETA) * (2.0 * jnp.arange(half, dtype=jnp.float32)) / size)
    angle = jnp.arange(length, dtype=jnp.float32)[:, None] * freq[None, :]
    cosine = jnp.cos(angle)
    sine = jnp.sin(angle)
    return (jnp.concatenate([cosine, cosine], axis=-1), jnp.concatenate([sine, sine], axis=-1))

def rotate(value_rows):
    half = value_rows.shape[-1] // 2
    return jnp.concatenate([-value_rows[..., half:], value_rows[..., :half]], axis=-1)

def apply_rope(value_rows, cosine, sine):
    return value_rows * cosine[:, None, :] + rotate(value_rows) * sine[:, None, :]

def span_ids(positions, span):
    first = (positions >= span[0]) & (positions < span[0] + IMG)
    second = (positions >= span[1]) & (positions < span[1] + IMG)
    return jnp.where(first, 0, jnp.where(second, 1, -1))

def allowed(query_pos, key_pos, span):
    query_span = span_ids(query_pos, span)
    key_span = span_ids(key_pos, span)
    causal = key_pos[None, :] <= query_pos[:, None]
    same = (query_span[:, None] == key_span[None, :]) & (query_span[:, None] >= 0)
    return causal | same

def masked_softmax(scores, mask):
    return plain_softmax(jnp.where(mask, scores, -1e+30))

def pair_slots(block_routes, experts):
    flat = block_routes.reshape(-1)
    onehot = (flat[:, None] == jnp.arange(experts, dtype=jnp.int32)[None, :]).astype(jnp.int32)
    before = jnp.cumsum(onehot, axis=0) - onehot
    return lax.optimization_barrier(jnp.sum(before * onehot, axis=1))

def route_tables(routes):
    blocks_count = TOKENS // ROWS
    blocks = routes.reshape(blocks_count, ROWS, TOPK)
    slots = jax.vmap(lambda one: pair_slots(one, EXPERTS))(blocks)
    flat_routes = routes.reshape(blocks_count, ROWS * TOPK)
    column = jnp.arange(blocks_count, dtype=jnp.int32)[:, None] * CAP + slots
    pair_ids = jnp.arange(TOKENS * TOPK, dtype=jnp.int32).reshape(blocks_count, ROWS * TOPK)
    table = jnp.full((EXPERTS, blocks_count * CAP), -1, jnp.int32)
    table = table.at[flat_routes, column].set(pair_ids)
    global_pos = (flat_routes * (blocks_count * CAP) + column).reshape(-1)
    return (table, global_pos)

def attend(seq_x, span, attn_gain, w_query, key_weight_matrix, value_weight_matrix, query_gain, key_gain, w_out):
    normalized_input = lower_precision(seq_x * rms_scale(seq_x) * attn_gain)
    queries = lower_precision_back(jnp.dot(normalized_input, w_query, precision=PRECISION_HIGH)).reshape(SEQUENCE_TOKENS, QUERY_HEADS, HEAD_SIZE)
    key_rows = lower_precision_back(jnp.dot(normalized_input, key_weight_matrix, precision=PRECISION_HIGH)).reshape(SEQUENCE_TOKENS, KEY_VALUE_HEADS, HEAD_SIZE)
    value_rows = lower_precision_back(lower_precision(jnp.dot(normalized_input, value_weight_matrix, precision=PRECISION_HIGH))).reshape(SEQUENCE_TOKENS, KEY_VALUE_HEADS, HEAD_SIZE)
    cosine, sine = rope_tables(SEQUENCE_TOKENS, HEAD_SIZE)
    query_rotated = lower_precision(apply_rope(queries * rms_scale(queries) * query_gain, cosine, sine))
    query_rotated = query_rotated.reshape(SEQUENCE_TOKENS, KEY_VALUE_HEADS, QUERY_HEADS // KEY_VALUE_HEADS, HEAD_SIZE)
    k_rot = lower_precision(apply_rope(key_rows * rms_scale(key_rows) * key_gain, cosine, sine))
    raw = jnp.einsum('qkgd,skd->kgqs', query_rotated, k_rot, precision=PRECISION_HIGH)
    scores = lower_precision_back(raw) * HEAD_SIZE ** (-0.5)
    positions = jnp.arange(SEQUENCE_TOKENS, dtype=jnp.int32)
    probs = masked_softmax(scores, allowed(positions, positions, span))
    heads = jnp.einsum('kgqs,skd->qkgd', lower_precision(probs), value_rows, precision=PRECISION_HIGH)
    heads = lower_precision_back(lower_precision(heads)).reshape(SEQUENCE_TOKENS, QUERY_HEADS * HEAD_SIZE)
    return lower_precision_back(jnp.dot(heads, w_out, precision=PRECISION_HIGH))

def reference(inputs, attn_gain, w_query, key_weight_matrix, value_weight_matrix, query_gain, key_gain, w_out, route_gain, w_router, w_gate, w_up, w_down, routes, image_starts, cotangent):
    floats = tuple((a.astype(jnp.float32) for a in (inputs, attn_gain, w_query, key_weight_matrix, value_weight_matrix, query_gain, key_gain, w_out, route_gain, w_router, w_gate, w_up, w_down)))
    table, global_pos = route_tables(routes)
    expert_ids = jnp.arange(EXPERTS, dtype=jnp.int32)
    counts = lax.optimization_barrier(jnp.sum((routes[:, :, None] == expert_ids[None, None, :]).astype(jnp.float32), axis=(0, 1)))
    share = counts / (TOKENS * TOPK)

    def forward(x_in, g_attn, wq, wk, wv, gq, gk, wo, g_route, wr, wg, wu, wd):

        def one_sequence(args):
            return attend(args[0], args[1], g_attn, wq, wk, wv, gq, gk, wo)
        branch = lax.map(jax.checkpoint(one_sequence), (x_in.reshape(N_EP, SEQUENCE_TOKENS, MODEL_WIDTH), image_starts))
        hidden = x_in + branch.reshape(TOKENS, MODEL_WIDTH)
        moe_in = lower_precision(hidden * rms_scale(hidden) * g_route)
        logits = lower_precision_back(jnp.dot(moe_in, wr, precision=PRECISION_HIGH))
        router_probs = plain_softmax(logits)
        gates = plain_softmax(jnp.take_along_axis(logits, routes, axis=1))
        loss = EXPERTS * jnp.sum(share * lax.optimization_barrier(jnp.mean(router_probs, axis=0)))

        def run_expert(args):
            gate_w, up_w, down_w, members = args
            valid = (members >= 0).astype(jnp.float32)
            token = jnp.where(members >= 0, members // TOPK, 0)
            rows = lower_precision_back(moe_in[token]) * valid[:, None]
            gate_pre = lower_precision_back(jnp.dot(rows, gate_w, precision=PRECISION_HIGH))
            up_pre = lower_precision_back(jnp.dot(rows, up_w, precision=PRECISION_HIGH))
            act = lower_precision(gate_pre * jax.nn.sigmoid(gate_pre) * up_pre)
            return lower_precision_back(lower_precision(jnp.dot(act, down_w, precision=PRECISION_HIGH)))
        slot_out = lax.map(jax.checkpoint(run_expert), (wg, wu, wd, table))
        pair_out = slot_out.reshape(-1, MODEL_WIDTH)[global_pos].reshape(TOKENS, TOPK, MODEL_WIDTH)
        output = hidden + lax.optimization_barrier(jnp.sum(gates[:, :, None] * pair_out, axis=1))
        return (output, loss)
    (output, loss), pullback = jax.vjp(forward, *floats)
    grads = pullback((cotangent.astype(jnp.float32), jnp.asarray(AUX * TOKENS, jnp.float32)))
    return (output.astype(jnp.bfloat16), loss, grads[0], grads[1], grads[2], grads[3], grads[4], grads[5], grads[6], grads[7], grads[8], grads[9], grads[10], grads[11], grads[12])
```

```python
import jax
import jax.numpy as jnp
from jax import lax
from jax.sharding import PartitionSpec as P

IMG = 256


EPS = 1e-06
AUX = 0.04
THETA = 1000000.0


def rms_scale(value_rows):
    return lax.rsqrt(jnp.mean(value_rows * value_rows, axis=-1, keepdims=True) + EPS)


def plain_softmax(value_rows):
    top = jnp.max(value_rows, axis=-1, keepdims=True)
    expo = jnp.exp(value_rows - top)
    return expo / jnp.sum(expo, axis=-1, keepdims=True)


def rope_tables(length, size):
    half = size // 2
    freq = jnp.exp(-jnp.log(THETA) * (2.0 * jnp.arange(half, dtype=jnp.float32)) / size)
    angle = jnp.arange(length, dtype=jnp.float32)[:, None] * freq[None, :]
    cosine = jnp.cos(angle)
    sine = jnp.sin(angle)
    return (jnp.concatenate([cosine, cosine], axis=-1), jnp.concatenate([sine, sine], axis=-1))


def rotate(value_rows):
    half = value_rows.shape[-1] // 2
    return jnp.concatenate([-value_rows[..., half:], value_rows[..., :half]], axis=-1)


def rotate_back(value_rows):
    half = value_rows.shape[-1] // 2
    return jnp.concatenate([value_rows[..., half:], -value_rows[..., :half]], axis=-1)


def apply_rope(value_rows, cosine, sine):
    return value_rows * cosine[:, None, :] + rotate(value_rows) * sine[:, None, :]


def undo_rope(grads, cosine, sine):
    return grads * cosine[:, None, :] + rotate_back(grads * sine[:, None, :])


def span_ids(positions, span):
    first = (positions >= span[0]) & (positions < span[0] + IMG)
    second = (positions >= span[1]) & (positions < span[1] + IMG)
    return jnp.where(first, 0, jnp.where(second, 1, -1))


def allowed(query_pos, key_pos, span):
    query_span = span_ids(query_pos, span)
    key_span = span_ids(key_pos, span)
    causal = key_pos[None, :] <= query_pos[:, None]
    same = (query_span[:, None] == key_span[None, :]) & (query_span[:, None] >= 0)
    return causal | same


def head_norm_back(grads, value_rows, scale, gain):
    gain_part = jnp.sum(grads * value_rows * scale, axis=(0, 1))
    inner = grads * gain
    back = scale * inner - value_rows * scale**3 * jnp.mean(
        inner * value_rows, axis=-1, keepdims=True
    )
    return (back, gain_part)


def block_probs(q_block, start, k_rot, span, factor):
    length = k_rot.shape[0]
    scores = (
        jnp.einsum("qkgd,skd->kgqs", q_block, k_rot, preferred_element_type=jnp.float32) * factor
    )
    query_pos = start + jnp.arange(q_block.shape[0], dtype=jnp.int32)
    mask = allowed(query_pos, jnp.arange(length, dtype=jnp.int32), span)
    return plain_softmax(jnp.where(mask[None, None], scores, -1e30))


def on_device(
    inputs,
    attn_gain,
    w_query,
    key_weight_matrix,
    value_weight_matrix,
    query_gain,
    key_gain,
    w_out,
    route_gain,
    w_router,
    w_gate,
    w_up,
    w_down,
    routes,
    image_starts,
    cotangent,
):
    tp_count = lax.axis_size("tp")
    ep_count = lax.axis_size("ep")
    tp_index = lax.axis_index("tp")
    ep_index = lax.axis_index("ep")
    length = inputs.shape[0]
    width = inputs.shape[1]
    rows = cotangent.shape[0]
    head_dim = query_gain.shape[0]
    local_heads = w_query.shape[1] // head_dim
    local_kv = key_weight_matrix.shape[1] // head_dim
    group = local_heads // local_kv
    local_experts = w_gate.shape[0]
    experts = local_experts * ep_count
    top = routes.shape[1]
    capacity = 3 * rows * top // (2 * experts)
    factor = head_dim ** (-0.5)
    span = image_starts[0]
    cot_all = lax.all_gather(cotangent, "ep")
    w_all = lax.all_gather(
        jnp.stack([w_gate.transpose(0, 2, 1), w_up.transpose(0, 2, 1), w_down]), "tp"
    )
    inputs_f = inputs.astype(jnp.float32)
    attn_scale = rms_scale(inputs_f)
    normalized_input = (inputs_f * attn_scale * attn_gain).astype(jnp.bfloat16)
    queries = jnp.dot(normalized_input, w_query, preferred_element_type=jnp.float32).reshape(
        length, local_heads, head_dim
    )
    key_rows = jnp.dot(
        normalized_input, key_weight_matrix, preferred_element_type=jnp.float32
    ).reshape(length, local_kv, head_dim)
    values_low = (
        jnp.dot(normalized_input, value_weight_matrix, preferred_element_type=jnp.float32)
        .astype(jnp.bfloat16)
        .reshape(length, local_kv, head_dim)
    )
    cosine, sine = rope_tables(length, head_dim)
    q_scale = rms_scale(queries)
    k_scale = rms_scale(key_rows)
    query_rotated = apply_rope(queries * q_scale * query_gain, cosine, sine).astype(jnp.bfloat16)
    k_rot = apply_rope(key_rows * k_scale * key_gain, cosine, sine).astype(jnp.bfloat16)
    block = min(512, length)
    nblocks = length // block
    q_blocks = query_rotated.reshape(nblocks, block, local_kv, group, head_dim)
    starts = jnp.arange(nblocks, dtype=jnp.int32) * block

    def forward_block(args):
        q_block, start = args
        probs = block_probs(q_block, start, k_rot, span, factor)
        return jnp.einsum(
            "kgqs,skd->qkgd",
            probs.astype(jnp.bfloat16),
            values_low,
            preferred_element_type=jnp.float32,
        )

    heads_low = (
        lax.map(forward_block, (q_blocks, starts))
        .reshape(length, local_heads * head_dim)
        .astype(jnp.bfloat16)
    )
    part = heads_low
    attn_rows = lax.psum_scatter(
        jnp.dot(part, w_out, preferred_element_type=jnp.float32).astype(jnp.bfloat16),
        "tp",
        scatter_dimension=0,
        tiled=True,
    ).astype(jnp.float32)
    x_rows = lax.dynamic_slice_in_dim(inputs_f, tp_index * rows, rows, 0)
    scale_rows = lax.dynamic_slice_in_dim(attn_scale, tp_index * rows, rows, 0)
    hidden = x_rows + attn_rows
    route_scale = rms_scale(hidden)
    moe_in = (hidden * route_scale * route_gain).astype(jnp.bfloat16)
    logits = jnp.dot(moe_in, w_router, preferred_element_type=jnp.float32)
    router_probs = plain_softmax(logits)
    block_id = ep_index * tp_count + tp_index
    my_routes = lax.dynamic_slice_in_dim(routes, block_id * rows, rows, 0)
    expert_ids = jnp.arange(experts, dtype=jnp.int32)
    pick = (my_routes[:, :, None] == expert_ids[None, None, :]).astype(jnp.float32)
    chosen = jnp.sum(pick * logits[:, None, :], axis=-1)
    gates = plain_softmax(chosen)
    seq_blocks = routes.reshape(ep_count, tp_count, rows, top)
    ring_routes = lax.dynamic_index_in_dim(seq_blocks, tp_index, 1, keepdims=False)
    tokens_all = lax.all_gather(moe_in, "ep")
    gates_all = lax.all_gather(gates, "ep")
    my_experts = ep_index * local_experts + jnp.arange(local_experts, dtype=jnp.int32)
    hit = ring_routes[:, None, :, :] == my_experts[None, :, None, None]
    mask = jnp.any(hit, axis=-1)
    gate_of = jnp.sum(jnp.where(hit, gates_all[:, None], 0.0), axis=-1)
    earlier = (jnp.arange(rows)[:, None] < jnp.arange(rows)[None, :]).astype(jnp.bfloat16)
    slots = jnp.einsum(
        "bet,tu->beu", mask.astype(jnp.bfloat16), earlier, preferred_element_type=jnp.float32
    ).astype(jnp.int32)
    place = mask[:, :, None, :] & (
        slots[:, :, None, :] == jnp.arange(capacity, dtype=jnp.int32)[None, None, :, None]
    )
    place_low = place.astype(jnp.bfloat16)
    slot_gate = jnp.sum(jnp.where(place, gate_of[:, :, None, :], 0.0), axis=-1)
    slot_gate = slot_gate.transpose(1, 0, 2).reshape(local_experts, ep_count * capacity, 1)

    def collect(values):
        return jnp.einsum(
            "bect,btw->ebcw", place_low, values, preferred_element_type=jnp.bfloat16
        ).reshape(local_experts, ep_count * capacity, width)

    def spread(values):
        return jnp.einsum(
            "bect,ebcw->btw",
            place_low,
            values.reshape(local_experts, ep_count, capacity, width),
            preferred_element_type=jnp.float32,
        ).astype(jnp.bfloat16)

    x_slots = collect(tokens_all)
    c_slots = collect(cot_all)
    wg = w_all[:, 0]
    wu = w_all[:, 1]
    wd = w_all[:, 2]
    gate_pre = jnp.einsum("enw,pefw->enpf", x_slots, wg, preferred_element_type=jnp.float32)
    up_pre = jnp.einsum("enw,pefw->enpf", x_slots, wu, preferred_element_type=jnp.float32)
    sig = jax.nn.sigmoid(gate_pre)
    act = gate_pre * sig * up_pre
    d_raw_act = jnp.einsum("enw,pefw->enpf", c_slots, wd, preferred_element_type=jnp.float32)
    g4 = slot_gate[..., None]
    d_gate_slots = jnp.sum(act * d_raw_act, axis=(2, 3))
    d_act = d_raw_act * g4
    d_gate = (d_act * up_pre * sig * (1.0 + gate_pre * (1.0 - sig))).astype(jnp.bfloat16)
    d_up = (d_act * gate_pre * sig).astype(jnp.bfloat16)
    act_low = (act * g4).astype(jnp.bfloat16)
    out_slots = jnp.einsum(
        "enpf,pefw->enw", act_low, wd, preferred_element_type=jnp.float32
    ).astype(jnp.bfloat16)
    d_in_slots = (
        jnp.einsum("enpf,pefw->enw", d_gate, wg, preferred_element_type=jnp.float32)
        + jnp.einsum("enpf,pefw->enw", d_up, wu, preferred_element_type=jnp.float32)
    ).astype(jnp.bfloat16)
    d_in_mine = lax.psum_scatter(spread(d_in_slots), "ep", scatter_dimension=0)
    out_mine = lax.psum_scatter(spread(out_slots), "ep", scatter_dimension=0)
    d_gate_tokens = jnp.sum(
        jnp.where(place, d_gate_slots.reshape(local_experts, ep_count, capacity).transpose(1, 0, 2)[..., None], 0.0),
        axis=2,
    )
    d_gates = lax.all_to_all(d_gate_tokens, "ep", split_axis=0, concat_axis=0, tiled=True)
    d_gates = d_gates.reshape(experts, rows).T
    grads_all = jnp.stack(
        [
            jnp.einsum("enpf,enw->pefw", d_gate, x_slots, preferred_element_type=jnp.float32),
            jnp.einsum("enpf,enw->pefw", d_up, x_slots, preferred_element_type=jnp.float32),
            jnp.einsum("enpf,enw->pefw", act_low, c_slots, preferred_element_type=jnp.float32),
        ],
        axis=1,
    ).astype(jnp.bfloat16)
    grads_mine = (
        lax.psum_scatter(grads_all.reshape(-1, width), "tp", scatter_dimension=0, tiled=True)
        .astype(jnp.float32)
        .reshape(3, local_experts, -1, width)
    )
    w_gate_grad = grads_mine[0].transpose(0, 2, 1)
    w_up_grad = grads_mine[1].transpose(0, 2, 1)
    w_down_grad = grads_mine[2]
    output = (hidden + out_mine.astype(jnp.float32)).astype(jnp.bfloat16)
    counts = jnp.sum(
        (routes[:, :, None] == expert_ids[None, None, :]).astype(jnp.float32), axis=(0, 1)
    )
    total_tokens = routes.shape[0]
    share = counts / (total_tokens * top)
    coeff = AUX * experts * share
    prob_local = jnp.sum(router_probs, axis=0)
    cot = cotangent.astype(jnp.float32)
    gate_dense = jnp.sum(pick * gates[:, :, None], axis=1)
    d_logits = gate_dense * (d_gates - jnp.sum(gate_dense * d_gates, axis=-1, keepdims=True))
    d_logits = d_logits + router_probs * (
        coeff - jnp.sum(router_probs * coeff, axis=-1, keepdims=True)
    )
    d_logits_low = d_logits.astype(jnp.bfloat16)
    router_part = jnp.einsum("rw,re->we", moe_in, d_logits_low, preferred_element_type=jnp.float32)
    d_moe = jnp.einsum("re,we->rw", d_logits_low, w_router, preferred_element_type=jnp.float32)
    d_moe = d_moe + d_in_mine.astype(jnp.float32)
    route_gain_part = jnp.sum(d_moe * hidden * route_scale, axis=0)
    inner = d_moe * route_gain
    d_hidden = (
        cot
        + route_scale * inner
        - hidden * route_scale**3 * jnp.mean(inner * hidden, axis=-1, keepdims=True)
    )
    d_attn = lax.all_gather(d_hidden.astype(jnp.bfloat16), "tp", axis=0, tiled=True).astype(
        d_hidden.dtype
    )
    d_attn_low = d_attn.astype(jnp.bfloat16)
    w_out_part = jnp.einsum("sh,sw->hw", heads_low, d_attn_low, preferred_element_type=jnp.float32)
    d_heads = jnp.einsum("sw,hw->sh", d_attn_low, w_out, preferred_element_type=jnp.float32).astype(
        jnp.bfloat16
    )
    d_head_blocks = d_heads.reshape(nblocks, block, local_kv, group, head_dim)

    def backward_block(carry, args):
        key_acc, value_acc = carry
        q_block, grad_block, start = args
        probs = block_probs(q_block, start, k_rot, span, factor)
        d_probs = jnp.einsum(
            "qkgd,skd->kgqs", grad_block, values_low, preferred_element_type=jnp.float32
        )
        d_scores = probs * (d_probs - jnp.sum(probs * d_probs, axis=-1, keepdims=True))
        d_raw = (d_scores * factor).astype(jnp.bfloat16)
        d_q = jnp.einsum("kgqs,skd->qkgd", d_raw, k_rot, preferred_element_type=jnp.float32)
        key_acc = key_acc + jnp.einsum(
            "kgqs,qkgd->skd", d_raw, q_block, preferred_element_type=jnp.float32
        )
        value_acc = value_acc + jnp.einsum(
            "kgqs,qkgd->skd",
            probs.astype(jnp.bfloat16),
            grad_block,
            preferred_element_type=jnp.float32,
        )
        return ((key_acc, value_acc), d_q)

    zeros_kv = jnp.zeros((length, local_kv, head_dim), jnp.float32)
    (d_krot, d_values_acc), d_qrot = lax.scan(
        backward_block, (zeros_kv, zeros_kv), (q_blocks, d_head_blocks, starts)
    )
    d_qrot = d_qrot.reshape(length, local_heads, head_dim)
    d_queries, query_gain_part = head_norm_back(
        undo_rope(d_qrot, cosine, sine), queries, q_scale, query_gain
    )
    d_keys, key_gain_part = head_norm_back(
        undo_rope(d_krot, cosine, sine), key_rows, k_scale, key_gain
    )
    d_queries = d_queries.astype(jnp.bfloat16).reshape(length, local_heads * head_dim)
    d_keys = d_keys.astype(jnp.bfloat16).reshape(length, local_kv * head_dim)
    d_values = d_values_acc.astype(jnp.bfloat16).reshape(length, local_kv * head_dim)
    w_query_part = jnp.einsum(
        "sw,sh->wh", normalized_input, d_queries, preferred_element_type=jnp.float32
    )
    w_key_part = jnp.einsum(
        "sw,sh->wh", normalized_input, d_keys, preferred_element_type=jnp.float32
    )
    w_value_part = jnp.einsum(
        "sw,sh->wh", normalized_input, d_values, preferred_element_type=jnp.float32
    )
    d_normed = jnp.einsum("sh,wh->sw", d_queries, w_query, preferred_element_type=jnp.float32)
    d_normed = d_normed + jnp.einsum(
        "sh,wh->sw", d_keys, key_weight_matrix, preferred_element_type=jnp.float32
    )
    d_normed = d_normed + jnp.einsum(
        "sh,wh->sw", d_values, value_weight_matrix, preferred_element_type=jnp.float32
    )
    d_mine = lax.psum_scatter(
        d_normed.astype(jnp.bfloat16), "tp", scatter_dimension=0, tiled=True
    ).astype(jnp.float32)
    attn_gain_part = jnp.sum(d_mine * x_rows * scale_rows, axis=0)
    inner = d_mine * attn_gain
    inputs_grad = (
        d_hidden
        + scale_rows * inner
        - x_rows * scale_rows**3 * jnp.mean(inner * x_rows, axis=-1, keepdims=True)
    )
    small = lax.psum(
        (router_part, attn_gain_part, route_gain_part, query_gain_part, key_gain_part, prob_local),
        ("ep", "tp"),
    )
    w_router_grad, attn_gain_grad, route_gain_grad, query_gain_grad, key_gain_grad, prob_all = small
    w_query_grad, w_key_grad, w_value_grad, w_out_grad = (
        lax.psum_scatter(
            w_query_part.astype(jnp.bfloat16), "ep", scatter_dimension=0, tiled=True
        ).astype(jnp.float32),
        lax.psum_scatter(
            w_key_part.astype(jnp.bfloat16), "ep", scatter_dimension=0, tiled=True
        ).astype(jnp.float32),
        lax.psum_scatter(
            w_value_part.astype(jnp.bfloat16), "ep", scatter_dimension=0, tiled=True
        ).astype(jnp.float32),
        lax.psum_scatter(
            w_out_part.astype(jnp.bfloat16), "ep", scatter_dimension=1, tiled=True
        ).astype(jnp.float32),
    )
    aux_loss = experts * jnp.sum(share * (prob_all / total_tokens))
    return (
        output,
        aux_loss,
        inputs_grad,
        attn_gain_grad,
        w_query_grad,
        w_key_grad,
        w_value_grad,
        query_gain_grad,
        key_gain_grad,
        w_out_grad,
        route_gain_grad,
        w_router_grad,
        w_gate_grad,
        w_up_grad,
        w_down_grad,
    )


def solution(mesh):
    return jax.shard_map(
        on_device,
        mesh=mesh,
        in_specs=(
            P("ep", None),
            P(),
            P(None, "tp"),
            P(None, "tp"),
            P(None, "tp"),
            P(),
            P(),
            P("tp", None),
            P(),
            P(),
            P("ep", None, "tp"),
            P("ep", None, "tp"),
            P("ep", "tp", None),
            P(),
            P("ep", None),
            P(("ep", "tp"), None),
        ),
        out_specs=(
            P(("ep", "tp"), None),
            P(),
            P(("ep", "tp"), None),
            P(),
            P("ep", "tp"),
            P("ep", "tp"),
            P("ep", "tp"),
            P(),
            P(),
            P("tp", "ep"),
            P(),
            P(),
            P("ep", None, "tp"),
            P("ep", None, "tp"),
            P("ep", "tp", None),
        ),
        check_vma=False,
    )
```

```python
import functools

import jax
import jax.numpy as jnp
from jax import lax
from jax.experimental import pallas as pl
from jax.experimental.pallas import tpu as pltpu
from jax.sharding import PartitionSpec as P

IMG = 256
EPS = 1e-06
AUX = 0.04
THETA = 1000000.0
MASKED = -1e30
NOWHERE = -(1 << 20)
BF = jnp.bfloat16
F32 = jnp.float32
VMEM_BYTES = 60 * 1024 * 1024


def dot_nn(a, b):
    return lax.dot_general(a, b, (((1,), (0,)), ((), ())), preferred_element_type=F32)


def dot_nt(a, b):
    return lax.dot_general(a, b, (((1,), (1,)), ((), ())), preferred_element_type=F32)


def dot_tn(a, b):
    return lax.dot_general(a, b, (((0,), (0,)), ((), ())), preferred_element_type=F32)


def params(**kw):
    return pltpu.CompilerParams(vmem_limit_bytes=VMEM_BYTES, **kw)


def rms_scale(value_rows):
    return lax.rsqrt(jnp.mean(value_rows * value_rows, axis=-1, keepdims=True) + EPS)


def plain_softmax(value_rows):
    top = jnp.max(value_rows, axis=-1, keepdims=True)
    expo = jnp.exp(value_rows - top)
    return expo / jnp.sum(expo, axis=-1, keepdims=True)


def rope_tables(length, size):
    half = size // 2
    freq = jnp.exp(-jnp.log(THETA) * (2.0 * jnp.arange(half, dtype=F32)) / size)
    angle = jnp.arange(length, dtype=F32)[:, None] * freq[None, :]
    cosine = jnp.cos(angle)
    sine = jnp.sin(angle)
    return (jnp.concatenate([cosine, cosine], axis=-1), jnp.concatenate([-sine, sine], axis=-1))


def turn(rows, cosine, sine):
    return rows * cosine + pltpu.roll(rows, rows.shape[-1] // 2, 1) * sine


def turn_back(rows, cosine, sine):
    return rows * cosine - pltpu.roll(rows, rows.shape[-1] // 2, 1) * sine


def fill_bias(span_ref, bias, chunk=256):
    keys, length = bias.shape
    query = lax.broadcasted_iota(jnp.int32, (1, length), 1)

    def spans(pos):
        first = (pos >= span_ref[0, 0]) & (pos < span_ref[0, 0] + IMG)
        second = (pos >= span_ref[0, 1]) & (pos < span_ref[0, 1] + IMG)
        return jnp.where(first, 0, jnp.where(second, 1, -1))

    query_span = spans(query)
    query_other = jnp.where(query_span < 0, -2, query_span)
    for start in range(0, keys, chunk):
        key = start + lax.broadcasted_iota(jnp.int32, (chunk, 1), 0)
        ok = (key <= query) | (spans(key) == query_other)
        bias[start : start + chunk, :] = jnp.where(ok, 0.0, MASKED)


def query_tiles(length):
    tile = min(IMG, length)
    return [
        (start, tile, min(length, start + tile + -(-IMG // tile) * tile))
        for start in range(0, length, tile)
    ]


def attention_kernel(
    span_ref, q_ref, k_ref, v_ref, cos_ref, sin_ref, qg_ref, kg_ref, out_ref, lse_ref,
    bias, k_rot, v_t,
):
    factor = q_ref.shape[-1] ** (-0.5)
    cosine, sine = cos_ref[...], sin_ref[...]

    @pl.when(pl.program_id(0) == 0)
    def _():
        fill_bias(span_ref, bias)
        k = k_ref[...]
        k_rot[...] = turn(k * rms_scale(k) * kg_ref[...], cosine, sine).astype(BF)
        v_t[...] = v_ref[...].astype(F32).T.astype(BF)

    q = q_ref[...]
    q_rot = turn(q * rms_scale(q) * qg_ref[...], cosine, sine).astype(BF)
    for start, tile, keys in query_tiles(q.shape[0]):
        cols = slice(start, start + tile)
        s = dot_nt(k_rot[:keys, :], q_rot[cols, :]) * factor + bias[:keys, cols]
        top = jnp.max(s, axis=0, keepdims=True)
        p = jnp.exp(s - top)
        total = jnp.sum(p, axis=0, keepdims=True)
        o_t = dot_nn(v_t[:, :keys], p.astype(BF)) / total
        out_ref[cols, :] = o_t.T.astype(BF)
        lse_ref[0, :, cols] = top + jnp.log(total)


def attention(span, q, k, v, cosine, sine, q_gain, k_gain):
    length, size = k.shape
    heads = q.shape[1] // size
    whole = pl.BlockSpec((length, size), lambda h: (0, 0))
    head = pl.BlockSpec((length, size), lambda h: (0, h))
    gain = pl.BlockSpec((1, size), lambda h: (0, 0))
    return pl.pallas_call(
        attention_kernel,
        grid=(heads,),
        in_specs=[
            pl.BlockSpec(memory_space=pltpu.SMEM), head, whole, whole, whole, whole, gain, gain,
        ],
        out_specs=[head, pl.BlockSpec((1, 1, length), lambda h: (h, 0, 0))],
        out_shape=[
            jax.ShapeDtypeStruct((length, heads * size), BF),
            jax.ShapeDtypeStruct((heads, 1, length), F32),
        ],
        scratch_shapes=[
            pltpu.VMEM((length, length), F32),
            pltpu.VMEM((length, size), BF),
            pltpu.VMEM((size, length), BF),
        ],
        compiler_params=params(),
        name="attention",
    )(span, q, k, v, cosine, sine, q_gain, k_gain)


def norm_back(grads, rows, gain):
    scale = rms_scale(rows)
    gain_part = jnp.sum(grads * rows * scale, axis=0, keepdims=True)
    inner = grads * gain
    mean = jnp.mean(inner * rows, axis=-1, keepdims=True)
    return scale * inner - rows * (scale * scale * scale * mean), gain_part


def attention_back_kernel(
    span_ref, q_ref, k_ref, v_ref, grad_ref, lse_ref, cos_ref, sin_ref, qg_ref, kg_ref,
    dq_ref, dk_ref, dv_ref, dqg_ref, dkg_ref,
    bias, k_rot, k_t, dk_acc, dv_acc, dq_t,
):
    factor = q_ref.shape[-1] ** (-0.5)
    cosine, sine = cos_ref[...], sin_ref[...]
    step = pl.program_id(0)

    @pl.when(step == 0)
    def _():
        fill_bias(span_ref, bias)
        k = k_ref[...]
        rotated = turn(k * rms_scale(k) * kg_ref[...], cosine, sine)
        k_rot[...] = rotated.astype(BF)
        k_t[...] = rotated.T.astype(BF)
        dk_acc[...] = jnp.zeros_like(dk_acc)
        dv_acc[...] = jnp.zeros_like(dv_acc)
        dqg_ref[...] = jnp.zeros_like(dqg_ref)

    q = q_ref[...]
    q_rot = turn(q * rms_scale(q) * qg_ref[...], cosine, sine).astype(BF)
    for start, tile, keys in query_tiles(q.shape[0]):
        cols = slice(start, start + tile)
        s = dot_nt(k_rot[:keys, :], q_rot[cols, :]) * factor + bias[:keys, cols]
        p = jnp.exp(s - lse_ref[0, :, cols])
        grad = grad_ref[cols, :]
        dp = dot_nt(v_ref[:keys, :], grad)
        mean = jnp.sum(p * dp, axis=0, keepdims=True)
        raw = (p * (dp - mean) * factor).astype(BF)
        dq_t[:, cols] = dot_nn(k_t[:, :keys], raw)
        dk_acc[:keys, :] += dot_nn(raw, q_rot[cols, :])
        dv_acc[:keys, :] += dot_nn(p.astype(BF), grad)
    back, gain_part = norm_back(turn_back(dq_t[...].T, cosine, sine), q, qg_ref[...])
    dq_ref[...] = back.astype(BF)
    dqg_ref[...] += gain_part

    @pl.when(step == pl.num_programs(0) - 1)
    def _():
        back, gain_part = norm_back(turn_back(dk_acc[...], cosine, sine), k_ref[...], kg_ref[...])
        dk_ref[...] = back.astype(BF)
        dkg_ref[...] = gain_part
        dv_ref[...] = dv_acc[...].astype(BF)


def attention_back(span, q, k, v, grads, lse, cosine, sine, q_gain, k_gain):
    length, size = k.shape
    heads = q.shape[1] // size
    whole = pl.BlockSpec((length, size), lambda h: (0, 0))
    head = pl.BlockSpec((length, size), lambda h: (0, h))
    gain = pl.BlockSpec((1, size), lambda h: (0, 0))
    return pl.pallas_call(
        attention_back_kernel,
        grid=(heads,),
        in_specs=[
            pl.BlockSpec(memory_space=pltpu.SMEM), head, whole, whole, head,
            pl.BlockSpec((1, 1, length), lambda h: (h, 0, 0)), whole, whole, gain, gain,
        ],
        out_specs=[head, whole, whole, gain, gain],
        out_shape=[
            jax.ShapeDtypeStruct((length, heads * size), BF),
            jax.ShapeDtypeStruct((length, size), BF),
            jax.ShapeDtypeStruct((length, size), BF),
            jax.ShapeDtypeStruct((1, size), F32),
            jax.ShapeDtypeStruct((1, size), F32),
        ],
        scratch_shapes=[
            pltpu.VMEM((length, length), F32),
            pltpu.VMEM((length, size), BF),
            pltpu.VMEM((size, length), BF),
            pltpu.VMEM((length, size), F32),
            pltpu.VMEM((length, size), F32),
            pltpu.VMEM((size, length), F32),
        ],
        compiler_params=params(),
        name="attention_back",
    )(span, q, k, v, grads, lse, cosine, sine, q_gain, k_gain)


def select_kernel(slot_ref, x_ref, c_ref, xs_ref, cs_ref):
    local, _, capacity, width = xs_ref.shape
    rows = x_ref.shape[1]
    place = jnp.concatenate(
        [
            (
                slot_ref[0, e : e + 1, :]
                == lax.broadcasted_iota(jnp.int32, (capacity, rows), 0)
            ).astype(F32)
            for e in range(local)
        ],
        axis=0,
    ).astype(BF)
    xs_ref[...] = dot_nn(place, x_ref[0]).astype(BF).reshape(xs_ref.shape)
    cs_ref[...] = dot_nn(place, c_ref[0]).astype(BF).reshape(cs_ref.shape)


def select_rows(slots, tokens, cots, capacity):
    blocks, local, rows = slots.shape
    width = tokens.shape[-1]
    block = pl.BlockSpec((1, rows, width), lambda b: (b, 0, 0))
    out = pl.BlockSpec((local, 1, capacity, width), lambda b: (0, b, 0, 0))
    shape = jax.ShapeDtypeStruct((local, blocks, capacity, width), BF)
    return pl.pallas_call(
        select_kernel,
        grid=(blocks,),
        in_specs=[pl.BlockSpec((1, local, rows), lambda b: (b, 0, 0)), block, block],
        out_specs=[out, out],
        out_shape=[shape, shape],
        compiler_params=params(),
        name="select_rows",
    )(slots, tokens, cots)


def expert_kernel(x_ref, c_ref, w_ref, gate_ref, out_ref, dx_ref, act_ref, dg_ref, du_ref, dgate_ref):
    width = x_ref.shape[-1]
    x, c = x_ref[0], c_ref[0]
    w_gate = w_ref[:, 0, 0].reshape(-1, width)
    w_up = w_ref[:, 1, 0].reshape(-1, width)
    w_down = w_ref[:, 2, 0].reshape(-1, width)
    gate = gate_ref[0]
    gate_pre = dot_nt(x, w_gate)
    up_pre = dot_nt(x, w_up)
    raw = dot_nt(c, w_down)
    sig = jax.nn.sigmoid(gate_pre)
    silu = gate_pre * sig
    act = silu * up_pre
    dgate_ref[0] = jnp.sum(act * raw, axis=-1, keepdims=True)
    act_low = (act * gate).astype(BF)
    d_act = raw * gate
    d_gate = (d_act * up_pre * sig * (1.0 + gate_pre * (1.0 - sig))).astype(BF)
    d_up = (d_act * silu).astype(BF)
    act_ref[0] = act_low
    dg_ref[0] = d_gate
    du_ref[0] = d_up
    out_ref[0] = dot_nn(act_low, w_down).astype(BF)
    dx_ref[0] = (dot_nn(d_gate, w_gate) + dot_nn(d_up, w_up)).astype(BF)


def experts_both_ways(x_slots, c_slots, w_all, slot_gate):
    local, number, width = x_slots.shape
    parts, _, _, hidden, _ = w_all.shape
    tile = number // 2
    wide = pl.BlockSpec((1, tile, width), lambda e, i: (e, i, 0))
    mid = pl.BlockSpec((1, tile, parts * hidden), lambda e, i: (e, i, 0))
    thin = pl.BlockSpec((1, tile, 1), lambda e, i: (e, i, 0))
    wide_shape = jax.ShapeDtypeStruct((local, number, width), BF)
    mid_shape = jax.ShapeDtypeStruct((local, number, parts * hidden), BF)
    return pl.pallas_call(
        expert_kernel,
        grid=(local, 2),
        in_specs=[
            wide, wide,
            pl.BlockSpec((parts, 3, 1, hidden, width), lambda e, i: (0, 0, e, 0, 0)),
            thin,
        ],
        out_specs=[wide, wide, mid, mid, mid, thin],
        out_shape=[
            wide_shape, wide_shape, mid_shape, mid_shape, mid_shape,
            jax.ShapeDtypeStruct((local, number, 1), F32),
        ],
        compiler_params=params(),
        name="experts_both_ways",
    )(x_slots, c_slots, w_all, slot_gate)


def expert_grads_kernel(x_ref, c_ref, act_ref, dg_ref, du_ref, out_ref):
    parts, _, _, hidden, width = out_ref.shape
    x, c = x_ref[0], c_ref[0]
    for kind, (left, right) in enumerate(((dg_ref, x), (du_ref, x), (act_ref, c))):
        grad = dot_tn(left[0], right).astype(BF)
        out_ref[:, kind, 0] = grad.reshape(parts, hidden, width)


def expert_grads(x_slots, c_slots, act, d_gate, d_up, parts):
    local, number, width = x_slots.shape
    inner = act.shape[-1]
    wide = pl.BlockSpec((1, number, width), lambda e: (e, 0, 0))
    mid = pl.BlockSpec((1, number, inner), lambda e: (e, 0, 0))
    return pl.pallas_call(
        expert_grads_kernel,
        grid=(local,),
        in_specs=[wide, wide, mid, mid, mid],
        out_specs=pl.BlockSpec(
            (parts, 3, 1, inner // parts, width), lambda e: (0, 0, e, 0, 0)
        ),
        out_shape=jax.ShapeDtypeStruct((parts, 3, local, inner // parts, width), BF),
        compiler_params=params(),
        name="expert_grads",
    )(x_slots, c_slots, act, d_gate, d_up)


def combine_kernel(slot_ref, dx_ref, out_ref, dx_sum_ref, out_sum_ref):
    local, _, capacity, width = dx_ref.shape
    rows = slot_ref.shape[1]
    lane = lax.broadcasted_iota(jnp.int32, (rows, local * capacity), 1)
    hit = lane == slot_ref[0, :, 0:1]
    for e in range(1, local):
        hit = hit | (lane == slot_ref[0, :, e : e + 1] + e * capacity)
    place = hit.astype(F32).astype(BF)
    dx_sum_ref[0] = dot_nn(place, dx_ref[...].reshape(-1, width)).astype(BF)
    out_sum_ref[0] = dot_nn(place, out_ref[...].reshape(-1, width)).astype(BF)


def combine_rows(slots_t, dx, out):
    blocks, rows, local = slots_t.shape
    _, _, capacity, width = dx.shape
    slot = pl.BlockSpec((local, 1, capacity, width), lambda b: (0, b, 0, 0))
    block = pl.BlockSpec((1, rows, width), lambda b: (b, 0, 0))
    shape = jax.ShapeDtypeStruct((blocks, rows, width), BF)
    return pl.pallas_call(
        combine_kernel,
        grid=(blocks,),
        in_specs=[pl.BlockSpec((1, rows, local), lambda b: (b, 0, 0)), slot, slot],
        out_specs=[block, block],
        out_shape=[shape, shape],
        compiler_params=params(),
        name="combine_rows",
    )(slots_t, dx, out)


def on_device(
    inputs,
    attn_gain,
    w_query,
    key_weight_matrix,
    value_weight_matrix,
    query_gain,
    key_gain,
    w_out,
    route_gain,
    w_router,
    w_gate,
    w_up,
    w_down,
    routes,
    image_starts,
    cotangent,
):
    tp_count = lax.axis_size("tp")
    ep_count = lax.axis_size("ep")
    tp_index = lax.axis_index("tp")
    ep_index = lax.axis_index("ep")
    length = inputs.shape[0]
    width = inputs.shape[1]
    rows = cotangent.shape[0]
    head_dim = query_gain.shape[0]
    local_experts = w_gate.shape[0]
    experts = local_experts * ep_count
    top = routes.shape[1]
    capacity = -(-(3 * rows * top // (2 * experts)) // 16) * 16

    w_all = lax.all_gather(
        jnp.stack([w_gate.transpose(0, 2, 1), w_up.transpose(0, 2, 1), w_down]), "tp"
    )
    cot_all = lax.all_gather(cotangent, "ep")

    inputs_f = inputs.astype(F32)
    attn_scale = rms_scale(inputs_f)
    normed = (inputs_f * attn_scale * attn_gain).astype(BF)
    queries = dot_nn(normed, w_query)
    key_rows = dot_nn(normed, key_weight_matrix)
    values = dot_nn(normed, value_weight_matrix).astype(BF)
    cosine, sine = rope_tables(length, head_dim)
    q_gain, k_gain = query_gain[None], key_gain[None]
    heads, lse = attention(
        image_starts, queries, key_rows, values, cosine, sine, q_gain, k_gain
    )
    attn_rows = lax.psum_scatter(
        dot_nn(heads, w_out).astype(BF), "tp", scatter_dimension=0, tiled=True
    ).astype(F32)
    x_rows = lax.dynamic_slice_in_dim(inputs, tp_index * rows, rows, 0).astype(F32)
    scale_rows = lax.dynamic_slice_in_dim(attn_scale, tp_index * rows, rows, 0)
    hidden = x_rows + attn_rows
    route_scale = rms_scale(hidden)
    moe_in = (hidden * route_scale * route_gain).astype(BF)
    tokens_all = lax.all_gather(moe_in, "ep")

    logits = dot_nn(moe_in, w_router)
    router_probs = plain_softmax(logits)
    expert_ids = jnp.arange(experts, dtype=jnp.int32)
    ring_routes = lax.dynamic_index_in_dim(
        routes.reshape(ep_count, tp_count, rows, top), tp_index, 1, keepdims=False
    )
    my_routes = lax.dynamic_index_in_dim(ring_routes, ep_index, 0, keepdims=False)

    def routed_softmax(scores, picked):
        kept = jnp.where(picked, scores, MASKED)
        expo = jnp.where(picked, jnp.exp(kept - jnp.max(kept, axis=-1, keepdims=True)), 0.0)
        return expo / jnp.sum(expo, axis=-1, keepdims=True)

    my_pick = jnp.any(my_routes[:, :, None] == expert_ids[None, None, :], axis=1)
    gates = routed_softmax(logits, my_pick)
    all_pick = jnp.any(ring_routes[..., None] == expert_ids, axis=2)
    gates_all = routed_softmax(dot_nn(tokens_all.reshape(-1, width), w_router).reshape(ep_count, rows, experts), all_pick)
    gate_of = lax.dynamic_slice_in_dim(gates_all, ep_index * local_experts, local_experts, 2)
    mask = lax.dynamic_slice_in_dim(all_pick, ep_index * local_experts, local_experts, 2)
    earlier = (jnp.arange(rows)[:, None] > jnp.arange(rows)[None, :]).astype(BF)
    slots_t = jnp.einsum(
        "tu,bue->bte", earlier, mask.astype(BF), preferred_element_type=F32
    ).astype(jnp.int32)
    slots_t = jnp.where(mask, slots_t, NOWHERE)
    slots = slots_t.transpose(0, 2, 1)
    place = slots[:, :, None, :] == jnp.arange(capacity, dtype=jnp.int32)[:, None]
    slot_gate = jnp.sum(jnp.where(place, gate_of.transpose(0, 2, 1)[:, :, None, :], 0.0), axis=-1)
    slot_gate = slot_gate.transpose(1, 0, 2).reshape(local_experts, ep_count * capacity, 1)

    x_slots, c_slots = select_rows(slots, tokens_all, cot_all, capacity)
    flat = (local_experts, ep_count * capacity, width)
    deep = (local_experts, ep_count, capacity, width)
    x_slots, c_slots = x_slots.reshape(flat), c_slots.reshape(flat)
    out_slots, dx_slots, act, d_gate, d_up, d_gate_slots = experts_both_ways(
        x_slots, c_slots, w_all, slot_gate
    )
    dx_part, out_part = combine_rows(slots_t, dx_slots.reshape(deep), out_slots.reshape(deep))
    dx_mine = lax.psum_scatter(dx_part, "ep", scatter_dimension=0)
    out_mine = lax.psum_scatter(out_part, "ep", scatter_dimension=0)
    d_gate_tokens = jnp.sum(
        jnp.where(
            place,
            d_gate_slots.reshape(local_experts, ep_count, capacity).transpose(1, 0, 2)[..., None],
            0.0,
        ),
        axis=2,
    )
    d_gates = lax.all_to_all(d_gate_tokens, "ep", split_axis=0, concat_axis=0, tiled=True)
    d_gates = d_gates.reshape(experts, rows).T
    grads_all = expert_grads(x_slots, c_slots, act, d_gate, d_up, tp_count)
    grads_mine = (
        lax.psum_scatter(grads_all.reshape(-1, width), "tp", scatter_dimension=0, tiled=True)
        .astype(F32)
        .reshape(3, local_experts, -1, width)
    )
    w_gate_grad = grads_mine[0].transpose(0, 2, 1)
    w_up_grad = grads_mine[1].transpose(0, 2, 1)
    w_down_grad = grads_mine[2]
    output = (hidden + out_mine.astype(F32)).astype(BF)

    counts = jnp.sum((routes[:, :, None] == expert_ids[None, None, :]).astype(F32), axis=(0, 1))
    total_tokens = routes.shape[0]
    share = counts / (total_tokens * top)
    coeff = AUX * experts * share
    prob_local = jnp.sum(router_probs, axis=0)
    cot = cotangent.astype(F32)
    d_logits = gates * (d_gates - jnp.sum(gates * d_gates, axis=-1, keepdims=True))
    d_logits = d_logits + router_probs * (
        coeff - jnp.sum(router_probs * coeff, axis=-1, keepdims=True)
    )
    d_logits_low = d_logits.astype(BF)
    router_part = dot_tn(moe_in, d_logits_low)
    d_moe = dot_nt(d_logits_low, w_router) + dx_mine.astype(F32)
    d_hidden, route_gain_part = norm_back(d_moe, hidden, route_gain[None])
    d_hidden = d_hidden + cot

    d_branch = lax.all_gather(d_hidden.astype(BF), "tp", axis=0, tiled=True)
    w_out_part = dot_tn(heads, d_branch)
    d_heads = dot_nt(d_branch, w_out).astype(BF)
    d_queries, d_keys, d_values, query_gain_part, key_gain_part = attention_back(
        image_starts, queries, key_rows, values, d_heads, lse, cosine, sine, q_gain, k_gain
    )
    w_query_part = dot_tn(normed, d_queries)
    w_key_part = dot_tn(normed, d_keys)
    w_value_part = dot_tn(normed, d_values)
    d_normed = (
        dot_nt(d_queries, w_query)
        + dot_nt(d_keys, key_weight_matrix)
        + dot_nt(d_values, value_weight_matrix)
    )
    d_mine = lax.psum_scatter(
        d_normed.astype(BF), "tp", scatter_dimension=0, tiled=True
    ).astype(F32)
    attn_gain_part = jnp.sum(d_mine * x_rows * scale_rows, axis=0)
    inner = d_mine * attn_gain
    inputs_grad = (
        d_hidden
        + scale_rows * inner
        - x_rows * scale_rows**3 * jnp.mean(inner * x_rows, axis=-1, keepdims=True)
    )
    small = lax.psum(
        (
            router_part,
            attn_gain_part,
            route_gain_part[0],
            query_gain_part[0],
            key_gain_part[0],
            prob_local,
        ),
        ("ep", "tp"),
    )
    w_router_grad, attn_gain_grad, route_gain_grad, query_gain_grad, key_gain_grad, prob_all = small

    def over_sequences(part, dim):
        return lax.psum_scatter(part.astype(BF), "ep", scatter_dimension=dim, tiled=True).astype(F32)

    w_query_grad = over_sequences(w_query_part, 0)
    w_key_grad = over_sequences(w_key_part, 0)
    w_value_grad = over_sequences(w_value_part, 0)
    w_out_grad = over_sequences(w_out_part, 1)
    aux_loss = experts * jnp.sum(share * (prob_all / total_tokens))
    return (
        output,
        aux_loss,
        inputs_grad,
        attn_gain_grad,
        w_query_grad,
        w_key_grad,
        w_value_grad,
        query_gain_grad,
        key_gain_grad,
        w_out_grad,
        route_gain_grad,
        w_router_grad,
        w_gate_grad,
        w_up_grad,
        w_down_grad,
    )


def solution(mesh):
    return jax.shard_map(
        on_device,
        mesh=mesh,
        in_specs=(
            P("ep", None),
            P(),
            P(None, "tp"),
            P(None, "tp"),
            P(None, "tp"),
            P(),
            P(),
            P("tp", None),
            P(),
            P(),
            P("ep", None, "tp"),
            P("ep", None, "tp"),
            P("ep", "tp", None),
            P(),
            P("ep", None),
            P(("ep", "tp"), None),
        ),
        out_specs=(
            P(("ep", "tp"), None),
            P(),
            P(("ep", "tp"), None),
            P(),
            P("ep", "tp"),
            P("ep", "tp"),
            P("ep", "tp"),
            P(),
            P(),
            P("tp", "ep"),
            P(),
            P(),
            P("ep", None, "tp"),
            P("ep", None, "tp"),
            P("ep", "tp", None),
        ),
        check_vma=False,
    )
```

```python
import functools

import jax
import jax.numpy as jnp
from jax import lax
from jax.experimental import pallas as pl
from jax.experimental.pallas import tpu as pltpu
from jax.sharding import PartitionSpec as P

IMG = 256
EPS = 1e-06
AUX = 0.04
THETA = 1000000.0
MASKED = -1e30
NOWHERE = -(1 << 20)
BF = jnp.bfloat16
F32 = jnp.float32
VMEM_BYTES = 60 * 1024 * 1024


def dot_nn(a, b):
    return lax.dot_general(a, b, (((1,), (0,)), ((), ())), preferred_element_type=F32)


def dot_nt(a, b):
    return lax.dot_general(a, b, (((1,), (1,)), ((), ())), preferred_element_type=F32)


def dot_tn(a, b):
    return lax.dot_general(a, b, (((0,), (0,)), ((), ())), preferred_element_type=F32)


def params(**kw):
    return pltpu.CompilerParams(vmem_limit_bytes=VMEM_BYTES, **kw)


def rms_scale(value_rows):
    return lax.rsqrt(jnp.mean(value_rows * value_rows, axis=-1, keepdims=True) + EPS)


def plain_softmax(value_rows):
    top = jnp.max(value_rows, axis=-1, keepdims=True)
    expo = jnp.exp(value_rows - top)
    return expo / jnp.sum(expo, axis=-1, keepdims=True)


def rope_tables(length, size):
    half = size // 2
    freq = jnp.exp(-jnp.log(THETA) * (2.0 * jnp.arange(half, dtype=F32)) / size)
    angle = jnp.arange(length, dtype=F32)[:, None] * freq[None, :]
    cosine = jnp.cos(angle)
    sine = jnp.sin(angle)
    return (jnp.concatenate([cosine, cosine], axis=-1), jnp.concatenate([-sine, sine], axis=-1))


def turn(rows, cosine, sine):
    return rows * cosine + pltpu.roll(rows, rows.shape[-1] // 2, 1) * sine


def turn_back(rows, cosine, sine):
    return rows * cosine - pltpu.roll(rows, rows.shape[-1] // 2, 1) * sine


def fill_bias(span_ref, bias, chunk=256):
    keys, length = bias.shape
    query = lax.broadcasted_iota(jnp.int32, (1, length), 1)

    def spans(pos):
        first = (pos >= span_ref[0, 0]) & (pos < span_ref[0, 0] + IMG)
        second = (pos >= span_ref[0, 1]) & (pos < span_ref[0, 1] + IMG)
        return jnp.where(first, 0, jnp.where(second, 1, -1))

    query_span = spans(query)
    query_other = jnp.where(query_span < 0, -2, query_span)
    for start in range(0, keys, chunk):
        key = start + lax.broadcasted_iota(jnp.int32, (chunk, 1), 0)
        ok = (key <= query) | (spans(key) == query_other)
        bias[start : start + chunk, :] = jnp.where(ok, 0.0, MASKED)


def query_tiles(length):
    tile = min(IMG, length)
    return [
        (start, tile, min(length, start + tile + -(-IMG // tile) * tile))
        for start in range(0, length, tile)
    ]


def attention_kernel(
    span_ref, q_ref, k_ref, v_ref, cos_ref, sin_ref, qg_ref, kg_ref, out_ref, lse_ref,
    bias, k_rot, v_t,
):
    factor = q_ref.shape[-1] ** (-0.5)
    cosine, sine = cos_ref[...], sin_ref[...]

    @pl.when(pl.program_id(0) == 0)
    def _():
        fill_bias(span_ref, bias)
        k = k_ref[...]
        k_rot[...] = turn(k * rms_scale(k) * kg_ref[...], cosine, sine).astype(BF)
        v_t[...] = v_ref[...].astype(F32).T.astype(BF)

    q = q_ref[...]
    q_rot = turn(q * rms_scale(q) * qg_ref[...], cosine, sine).astype(BF)
    for start, tile, keys in query_tiles(q.shape[0]):
        cols = slice(start, start + tile)
        s = dot_nt(k_rot[:keys, :], q_rot[cols, :]) * factor + bias[:keys, cols]
        top = jnp.max(s, axis=0, keepdims=True)
        p = jnp.exp(s - top)
        total = jnp.sum(p, axis=0, keepdims=True)
        o_t = dot_nn(v_t[:, :keys], p.astype(BF)) / total
        out_ref[cols, :] = o_t.T.astype(BF)
        lse_ref[0, :, cols] = top + jnp.log(total)


def attention(span, q, k, v, cosine, sine, q_gain, k_gain):
    length, size = k.shape
    heads = q.shape[1] // size
    whole = pl.BlockSpec((length, size), lambda h: (0, 0))
    head = pl.BlockSpec((length, size), lambda h: (0, h))
    gain = pl.BlockSpec((1, size), lambda h: (0, 0))
    return pl.pallas_call(
        attention_kernel,
        grid=(heads,),
        in_specs=[
            pl.BlockSpec(memory_space=pltpu.SMEM), head, whole, whole, whole, whole, gain, gain,
        ],
        out_specs=[head, pl.BlockSpec((1, 1, length), lambda h: (h, 0, 0))],
        out_shape=[
            jax.ShapeDtypeStruct((length, heads * size), BF),
            jax.ShapeDtypeStruct((heads, 1, length), F32),
        ],
        scratch_shapes=[
            pltpu.VMEM((length, length), F32),
            pltpu.VMEM((length, size), BF),
            pltpu.VMEM((size, length), BF),
        ],
        compiler_params=params(),
        name="attention",
    )(span, q, k, v, cosine, sine, q_gain, k_gain)


def norm_back(grads, rows, gain):
    scale = rms_scale(rows)
    gain_part = jnp.sum(grads * rows * scale, axis=0, keepdims=True)
    inner = grads * gain
    mean = jnp.mean(inner * rows, axis=-1, keepdims=True)
    return scale * inner - rows * (scale * scale * scale * mean), gain_part


def attention_back_kernel(
    span_ref, q_ref, k_ref, v_ref, grad_ref, lse_ref, cos_ref, sin_ref, qg_ref, kg_ref,
    dq_ref, dk_ref, dv_ref, dqg_ref, dkg_ref,
    bias, k_rot, k_t, dk_acc, dv_acc, dq_t,
):
    factor = q_ref.shape[-1] ** (-0.5)
    cosine, sine = cos_ref[...], sin_ref[...]
    step = pl.program_id(0)

    @pl.when(step == 0)
    def _():
        fill_bias(span_ref, bias)
        k = k_ref[...]
        rotated = turn(k * rms_scale(k) * kg_ref[...], cosine, sine)
        k_rot[...] = rotated.astype(BF)
        k_t[...] = rotated.T.astype(BF)
        dk_acc[...] = jnp.zeros_like(dk_acc)
        dv_acc[...] = jnp.zeros_like(dv_acc)
        dqg_ref[...] = jnp.zeros_like(dqg_ref)

    q = q_ref[...]
    q_rot = turn(q * rms_scale(q) * qg_ref[...], cosine, sine).astype(BF)
    for start, tile, keys in query_tiles(q.shape[0]):
        cols = slice(start, start + tile)
        s = dot_nt(k_rot[:keys, :], q_rot[cols, :]) * factor + bias[:keys, cols]
        p = jnp.exp(s - lse_ref[0, :, cols])
        grad = grad_ref[cols, :]
        dp = dot_nt(v_ref[:keys, :], grad)
        mean = jnp.sum(p * dp, axis=0, keepdims=True)
        raw = (p * (dp - mean) * factor).astype(BF)
        dq_t[:, cols] = dot_nn(k_t[:, :keys], raw)
        dk_acc[:keys, :] += dot_nn(raw, q_rot[cols, :])
        dv_acc[:keys, :] += dot_nn(p.astype(BF), grad)
    back, gain_part = norm_back(turn_back(dq_t[...].T, cosine, sine), q, qg_ref[...])
    dq_ref[...] = back.astype(BF)
    dqg_ref[...] += gain_part

    @pl.when(step == pl.num_programs(0) - 1)
    def _():
        back, gain_part = norm_back(turn_back(dk_acc[...], cosine, sine), k_ref[...], kg_ref[...])
        dk_ref[...] = back.astype(BF)
        dkg_ref[...] = gain_part
        dv_ref[...] = dv_acc[...].astype(BF)


def attention_back(span, q, k, v, grads, lse, cosine, sine, q_gain, k_gain):
    length, size = k.shape
    heads = q.shape[1] // size
    whole = pl.BlockSpec((length, size), lambda h: (0, 0))
    head = pl.BlockSpec((length, size), lambda h: (0, h))
    gain = pl.BlockSpec((1, size), lambda h: (0, 0))
    return pl.pallas_call(
        attention_back_kernel,
        grid=(heads,),
        in_specs=[
            pl.BlockSpec(memory_space=pltpu.SMEM), head, whole, whole, head,
            pl.BlockSpec((1, 1, length), lambda h: (h, 0, 0)), whole, whole, gain, gain,
        ],
        out_specs=[head, whole, whole, gain, gain],
        out_shape=[
            jax.ShapeDtypeStruct((length, heads * size), BF),
            jax.ShapeDtypeStruct((length, size), BF),
            jax.ShapeDtypeStruct((length, size), BF),
            jax.ShapeDtypeStruct((1, size), F32),
            jax.ShapeDtypeStruct((1, size), F32),
        ],
        scratch_shapes=[
            pltpu.VMEM((length, length), F32),
            pltpu.VMEM((length, size), BF),
            pltpu.VMEM((size, length), BF),
            pltpu.VMEM((length, size), F32),
            pltpu.VMEM((length, size), F32),
            pltpu.VMEM((size, length), F32),
        ],
        compiler_params=params(),
        name="attention_back",
    )(span, q, k, v, grads, lse, cosine, sine, q_gain, k_gain)


def select_kernel(slot_ref, x_ref, c_ref, xs_ref, cs_ref):
    local, _, capacity, width = xs_ref.shape
    rows = x_ref.shape[1]
    place = jnp.concatenate(
        [
            (
                slot_ref[0, e : e + 1, :]
                == lax.broadcasted_iota(jnp.int32, (capacity, rows), 0)
            ).astype(F32)
            for e in range(local)
        ],
        axis=0,
    ).astype(BF)
    xs_ref[...] = dot_nn(place, x_ref[0]).astype(BF).reshape(xs_ref.shape)
    cs_ref[...] = dot_nn(place, c_ref[0]).astype(BF).reshape(cs_ref.shape)


def select_rows(slots, tokens, cots, capacity):
    blocks, local, rows = slots.shape
    width = tokens.shape[-1]
    block = pl.BlockSpec((1, rows, width), lambda b: (b, 0, 0))
    out = pl.BlockSpec((local, 1, capacity, width), lambda b: (0, b, 0, 0))
    shape = jax.ShapeDtypeStruct((local, blocks, capacity, width), BF)
    return pl.pallas_call(
        select_kernel,
        grid=(blocks,),
        in_specs=[pl.BlockSpec((1, local, rows), lambda b: (b, 0, 0)), block, block],
        out_specs=[out, out],
        out_shape=[shape, shape],
        compiler_params=params(),
        name="select_rows",
    )(slots, tokens, cots)


def expert_kernel(
    x_ref, c_ref, wg_ref, w_ref, gate_ref, out_ref, dx_ref, act_ref, dg_ref, du_ref, dgate_ref
):
    width = x_ref.shape[-1]
    x, c = x_ref[0], c_ref[0]
    w_gate = wg_ref[:, 0, 0].reshape(-1, width)
    w_up = w_ref[:, 0, 0].reshape(-1, width)
    w_down = w_ref[:, 1, 0].reshape(-1, width)
    gate = gate_ref[0]
    gate_pre = dot_nt(x, w_gate)
    up_pre = dot_nt(x, w_up)
    raw = dot_nt(c, w_down)
    sig = jax.nn.sigmoid(gate_pre)
    silu = gate_pre * sig
    act = silu * up_pre
    dgate_ref[0] = jnp.sum(act * raw, axis=-1, keepdims=True)
    act_low = (act * gate).astype(BF)
    d_act = raw * gate
    d_gate = (d_act * up_pre * sig * (1.0 + gate_pre * (1.0 - sig))).astype(BF)
    d_up = (d_act * silu).astype(BF)
    act_ref[0] = act_low
    dg_ref[0] = d_gate
    du_ref[0] = d_up
    out_ref[0] = dot_nn(act_low, w_down).astype(BF)
    dx_ref[0] = (dot_nn(d_gate, w_gate) + dot_nn(d_up, w_up)).astype(BF)


def experts_both_ways(x_slots, c_slots, w_gate_all, w_rest_all, slot_gate):
    local, number, width = x_slots.shape
    parts, _, _, hidden, _ = w_gate_all.shape
    tile = number // 2
    wide = pl.BlockSpec((1, tile, width), lambda e, i: (e, i, 0))
    mid = pl.BlockSpec((1, tile, parts * hidden), lambda e, i: (e, i, 0))
    thin = pl.BlockSpec((1, tile, 1), lambda e, i: (e, i, 0))
    wide_shape = jax.ShapeDtypeStruct((local, number, width), BF)
    mid_shape = jax.ShapeDtypeStruct((local, number, parts * hidden), BF)
    return pl.pallas_call(
        expert_kernel,
        grid=(local, 2),
        in_specs=[
            wide, wide,
            pl.BlockSpec((parts, 1, 1, hidden, width), lambda e, i: (0, 0, e, 0, 0)),
            pl.BlockSpec((parts, 2, 1, hidden, width), lambda e, i: (0, 0, e, 0, 0)),
            thin,
        ],
        out_specs=[wide, wide, mid, mid, mid, thin],
        out_shape=[
            wide_shape, wide_shape, mid_shape, mid_shape, mid_shape,
            jax.ShapeDtypeStruct((local, number, 1), F32),
        ],
        compiler_params=params(),
        name="experts_both_ways",
    )(x_slots, c_slots, w_gate_all, w_rest_all, slot_gate)


def expert_grads_kernel(x_ref, c_ref, act_ref, dg_ref, du_ref, first_ref, rest_ref):
    parts, _, _, hidden, width = first_ref.shape
    x, c = x_ref[0], c_ref[0]
    first_ref[:, 0, 0] = dot_tn(dg_ref[0], x).astype(BF).reshape(parts, hidden, width)
    rest_ref[:, 0, 0] = dot_tn(du_ref[0], x).astype(BF).reshape(parts, hidden, width)
    rest_ref[:, 1, 0] = dot_tn(act_ref[0], c).astype(BF).reshape(parts, hidden, width)


def expert_grads(x_slots, c_slots, act, d_gate, d_up, parts):
    local, number, width = x_slots.shape
    inner = act.shape[-1]
    wide = pl.BlockSpec((1, number, width), lambda e: (e, 0, 0))
    mid = pl.BlockSpec((1, number, inner), lambda e: (e, 0, 0))
    return pl.pallas_call(
        expert_grads_kernel,
        grid=(local,),
        in_specs=[wide, wide, mid, mid, mid],
        out_specs=[
            pl.BlockSpec((parts, kinds, 1, inner // parts, width), lambda e: (0, 0, e, 0, 0))
            for kinds in (1, 2)
        ],
        out_shape=[
            jax.ShapeDtypeStruct((parts, kinds, local, inner // parts, width), BF)
            for kinds in (1, 2)
        ],
        compiler_params=params(),
        name="expert_grads",
    )(x_slots, c_slots, act, d_gate, d_up)


def combine_kernel(slot_ref, dx_ref, out_ref, dx_sum_ref, out_sum_ref):
    local, _, capacity, width = dx_ref.shape
    rows = slot_ref.shape[1]
    lane = lax.broadcasted_iota(jnp.int32, (rows, local * capacity), 1)
    hit = lane == slot_ref[0, :, 0:1]
    for e in range(1, local):
        hit = hit | (lane == slot_ref[0, :, e : e + 1] + e * capacity)
    place = hit.astype(F32).astype(BF)
    dx_sum_ref[0] = dot_nn(place, dx_ref[...].reshape(-1, width)).astype(BF)
    out_sum_ref[0] = dot_nn(place, out_ref[...].reshape(-1, width)).astype(BF)


def combine_rows(slots_t, dx, out):
    blocks, rows, local = slots_t.shape
    _, _, capacity, width = dx.shape
    slot = pl.BlockSpec((local, 1, capacity, width), lambda b: (0, b, 0, 0))
    block = pl.BlockSpec((1, rows, width), lambda b: (b, 0, 0))
    shape = jax.ShapeDtypeStruct((blocks, rows, width), BF)
    return pl.pallas_call(
        combine_kernel,
        grid=(blocks,),
        in_specs=[pl.BlockSpec((1, rows, local), lambda b: (b, 0, 0)), slot, slot],
        out_specs=[block, block],
        out_shape=[shape, shape],
        compiler_params=params(),
        name="combine_rows",
    )(slots_t, dx, out)


MESH = pl.DeviceIdType.MESH
ANY = pl.BlockSpec(memory_space=pl.ANY)
Z_AXIS = 4


def link_cost(us):
    return pl.CostEstimate(flops=0, bytes_accessed=int(us * 3.0e6), transcendentals=0)


def greet(partners):
    barrier = pltpu.get_barrier_semaphore()
    count = 0
    for there, device in partners:
        flag = jnp.asarray(there, jnp.int32)

        @pl.when(there)
        def _(device=device):
            pl.semaphore_signal(barrier, inc=1, device_id=device, device_id_type=MESH)

        count = count + flag
    pl.semaphore_wait(barrier, count)


def remote(src, dst, send, recv, device):
    return pltpu.make_async_remote_copy(
        src_ref=src, dst_ref=dst, send_sem=send, recv_sem=recv, device_id=device, device_id_type=MESH
    )


def ring_place():
    me = lax.axis_index("ep")
    z, y = me // 2, me % 2
    return me, z, y, {"ep": me + 2}, {"ep": me - 2}, {"ep": me + 1 - 2 * y}


def gather_ep_kernel(number, *refs):
    ins, outs = refs[:number], refs[number : 2 * number]
    own_sem, up_send, up_recv, dn_send, dn_recv, y_send, y_recv = refs[2 * number :]
    me, z, y, up, down, beside = ring_place()
    top = Z_AXIS - 1
    greet([(z < top, up), (z > 0, down), (z >= 0, beside)])

    def block(a, zt):
        return outs[a].at[zt * 2 + y]

    def upward(src, a, zt):
        return remote(src, block(a, zt), up_send.at[a, zt], up_recv.at[a, zt], up)

    def downward(src, a, zt):
        return remote(src, block(a, zt), dn_send.at[a, zt], dn_recv.at[a, zt], down)

    def sideways(src, a, zt):
        return remote(src, block(a, zt), y_send.at[a, zt], y_recv.at[a, zt], beside)

    for a in range(number):
        x = ins[a]

        @pl.when(z < top)
        def _(a=a, x=x):
            upward(x, a, z).start()

        @pl.when(z > 0)
        def _(a=a, x=x):
            downward(x, a, z).start()

        sideways(x, a, z).start()
        pltpu.make_async_copy(x, block(a, z), own_sem.at[a]).start()

    for d in range(1, Z_AXIS):
        for a in range(number):

            @pl.when(z >= d)
            def _(a=a, zt=z - d):
                upward(block(a, zt), a, zt).wait_recv()

                @pl.when(z < top)
                def _():
                    upward(block(a, zt), a, zt).start()

                sideways(block(a, zt), a, zt).start()

            @pl.when(z + d <= top)
            def _(a=a, zt=z + d):
                downward(block(a, zt), a, zt).wait_recv()

                @pl.when(z > 0)
                def _():
                    downward(block(a, zt), a, zt).start()

                sideways(block(a, zt), a, zt).start()

    for a in range(number):
        x, out = ins[a], outs[a]
        pltpu.make_async_copy(x, out.at[me], own_sem.at[a]).wait()
        for zt in range(Z_AXIS):
            src = out.at[zt * 2 + y]
            other = out.at[zt * 2 + 1 - y]
            remote(src, src, y_send.at[a, zt], y_recv.at[a, zt], beside).wait_send()
            remote(other, other, y_send.at[a, zt], y_recv.at[a, zt], beside).wait_recv()

            @pl.when((zt <= z) & (z < top))
            def _(src=src, zt=zt, a=a):
                remote(src, src, up_send.at[a, zt], up_recv.at[a, zt], up).wait_send()

            @pl.when((zt >= z) & (z > 0))
            def _(src=src, zt=zt, a=a):
                remote(src, src, dn_send.at[a, zt], dn_recv.at[a, zt], down).wait_send()


def gather_ep(arrays, number, name):
    count = len(arrays)
    ep_count = lax.axis_size("ep")
    if ep_count != 2 * Z_AXIS:
        return [lax.all_gather(a, "ep") for a in arrays]
    dma = pltpu.SemaphoreType.DMA
    return pl.pallas_call(
        functools.partial(gather_ep_kernel, count),
        in_specs=[ANY] * count,
        out_specs=[ANY] * count,
        out_shape=[jax.ShapeDtypeStruct((ep_count,) + a.shape, a.dtype) for a in arrays],
        scratch_shapes=[dma((count,))] + [dma((count, Z_AXIS))] * 6,
        compiler_params=params(collective_id=number, has_side_effects=True),
        cost_estimate=link_cost(80.0 * count),
        name=name,
    )(*arrays)


def add_rows(total, terms, chunk=32):
    @pl.loop(0, total.shape[0] // chunk)
    def _(i):
        rows = pl.ds(pl.multiple_of(i * chunk, chunk), chunk)
        value = terms[0][rows, :].astype(F32)
        for term in terms[1:]:
            value = value + term[rows, :].astype(F32)
        total[rows, :] = value.astype(total.dtype)


def scatter_order(z):
    table = ((3, 2, 1, 0), (3, 0, 2, 1), (0, 3, 1, 2), (0, 1, 2, 3))
    return [
        jnp.where(
            z == 0,
            table[0][k],
            jnp.where(z == 1, table[1][k], jnp.where(z == 2, table[2][k], table[3][k])),
        )
        for k in range(Z_AXIS)
    ]


def reduce_ep_kernel(number, *refs):
    ins, outs = refs[:number], refs[number : 2 * number]
    bufs = refs[2 * number : 6 * number]
    own_sem, up_send, up_recv, dn_send, dn_recv, y_send, y_recv = refs[6 * number :]
    me, z, y, up, down, beside = ring_place()
    top = Z_AXIS - 1
    order = scatter_order(z)
    greet([(z < top, up), (z > 0, down), (z >= 0, beside)])

    for zt in order:
        for a in range(number):
            mine, side = bufs[4 * a], bufs[4 * a + 1]
            remote(
                ins[a].at[zt * 2 + 1 - y], side.at[zt], y_send.at[a, zt], y_recv.at[a, zt], beside
            ).start()
            pltpu.make_async_copy(ins[a].at[zt * 2 + y], mine.at[zt], own_sem.at[a, zt]).start()

    for zt in order:
        for a in range(number):
            mine, side, below, above = bufs[4 * a : 4 * a + 4]
            pltpu.make_async_copy(ins[a].at[zt * 2 + y], mine.at[zt], own_sem.at[a, zt]).wait()
            remote(
                side.at[zt], side.at[zt], y_send.at[a, zt], y_recv.at[a, zt], beside
            ).wait_recv()

            def rising(a=a, mine=mine, below=below, zt=zt):
                return remote(
                    mine.at[zt], below.at[zt], up_send.at[a, zt], up_recv.at[a, zt], up
                )

            def falling(a=a, mine=mine, above=above, zt=zt):
                return remote(
                    mine.at[zt], above.at[zt], dn_send.at[a, zt], dn_recv.at[a, zt], down
                )

            @pl.when((zt > z) & (z == 0))
            def _(mine=mine, side=side, zt=zt):
                add_rows(mine.at[zt], [mine.at[zt], side.at[zt]])

            @pl.when((zt > z) & (z > 0))
            def _(mine=mine, side=side, below=below, zt=zt, rising=rising):
                rising().wait_recv()
                add_rows(mine.at[zt], [mine.at[zt], side.at[zt], below.at[zt]])

            @pl.when(zt > z)
            def _(rising=rising):
                rising().start()

            @pl.when((zt < z) & (z == top))
            def _(mine=mine, side=side, zt=zt):
                add_rows(mine.at[zt], [mine.at[zt], side.at[zt]])

            @pl.when((zt < z) & (z < top))
            def _(mine=mine, side=side, above=above, zt=zt, falling=falling):
                falling().wait_recv()
                add_rows(mine.at[zt], [mine.at[zt], side.at[zt], above.at[zt]])

            @pl.when(zt < z)
            def _(falling=falling):
                falling().start()

    for a in range(number):
        mine, side, below, above = bufs[4 * a : 4 * a + 4]
        own, beside_rows, low, high = mine.at[z], side.at[z], below.at[z], above.at[z]

        @pl.when(z > 0)
        def _(a=a, low=low):
            remote(low, low, up_send.at[a, z], up_recv.at[a, z], up).wait_recv()

        @pl.when(z < top)
        def _(a=a, high=high):
            remote(high, high, dn_send.at[a, z], dn_recv.at[a, z], down).wait_recv()

        @pl.when(z == 0)
        def _(a=a, own=own, beside_rows=beside_rows, high=high):
            add_rows(outs[a], [own, beside_rows, high])

        @pl.when(z == top)
        def _(a=a, own=own, beside_rows=beside_rows, low=low):
            add_rows(outs[a], [own, beside_rows, low])

        @pl.when((z > 0) & (z < top))
        def _(a=a, own=own, beside_rows=beside_rows, low=low, high=high):
            add_rows(outs[a], [own, beside_rows, low, high])

    for a in range(number):
        mine, side = bufs[4 * a], bufs[4 * a + 1]
        for zt in range(Z_AXIS):
            src = ins[a].at[zt * 2 + 1 - y]
            remote(src, src, y_send.at[a, zt], y_recv.at[a, zt], beside).wait_send()

            @pl.when(zt > z)
            def _(mine=mine, zt=zt, a=a):
                src = mine.at[zt]
                remote(src, src, up_send.at[a, zt], up_recv.at[a, zt], up).wait_send()

            @pl.when(zt < z)
            def _(mine=mine, zt=zt, a=a):
                src = mine.at[zt]
                remote(src, src, dn_send.at[a, zt], dn_recv.at[a, zt], down).wait_send()


def reduce_ep(parts, dtypes, number, name):
    count = len(parts)
    ep_count = lax.axis_size("ep")
    if ep_count != 2 * Z_AXIS:
        return [
            lax.psum_scatter(p, "ep", scatter_dimension=0).astype(t) for p, t in zip(parts, dtypes)
        ]
    dma = pltpu.SemaphoreType.DMA
    scratch = []
    for p in parts:
        scratch += [pltpu.VMEM((Z_AXIS,) + p.shape[1:], BF)] * 4
    return pl.pallas_call(
        functools.partial(reduce_ep_kernel, count),
        in_specs=[ANY] * count,
        out_specs=[pl.BlockSpec(memory_space=pltpu.VMEM)] * count,
        out_shape=[jax.ShapeDtypeStruct(p.shape[1:], t) for p, t in zip(parts, dtypes)],
        scratch_shapes=scratch + [dma((count, Z_AXIS))] * 7,
        compiler_params=params(collective_id=number, has_side_effects=True),
        cost_estimate=link_cost(80.0 * sum(p.size for p in parts) / 2**22),
        name=name,
    )(*parts)


def reduce_tp_kernel(part, out, mine, core_rows, x_rows, own_sem, core_send, core_recv, x_send, x_recv):
    me = lax.axis_index("tp")
    x, c = me // 2, me % 2
    other_core, other_x = {"tp": x * 2 + 1 - c}, {"tp": (1 - x) * 2 + c}
    greet([(x >= 0, other_core), (x >= 0, other_x)])
    half = out.shape[0] // 2

    def to_core(xt, h):
        rows = pl.ds(h * half, half)
        return remote(
            part.at[xt * 2 + 1 - c, rows], core_rows.at[xt, rows],
            core_send.at[xt, h], core_recv.at[xt, h], other_core,
        )

    def load(xt):
        return pltpu.make_async_copy(part.at[xt * 2 + c], mine.at[xt], own_sem.at[xt])

    def to_x(h):
        rows = pl.ds(h * half, half)
        return remote(mine.at[1 - x, rows], x_rows.at[rows], x_send.at[h], x_recv.at[h], other_x)

    for h in range(2):
        to_core(1 - x, h).start()
    load(1 - x).start()
    load(x).start()
    for h in range(2):
        to_core(x, h).start()
    load(1 - x).wait()
    for h in range(2):
        rows = pl.ds(h * half, half)
        to_core(1 - x, h).wait_recv()
        add_rows(mine.at[1 - x, rows], [mine.at[1 - x, rows], core_rows.at[1 - x, rows]])
        to_x(h).start()
    load(x).wait()
    for h in range(2):
        rows = pl.ds(h * half, half)
        to_core(x, h).wait_recv()
        to_x(h).wait_recv()
        add_rows(out.at[rows], [mine.at[x, rows], core_rows.at[x, rows], x_rows.at[rows]])
    for h in range(2):
        to_core(1 - x, h).wait_send()
        to_core(x, h).wait_send()
        to_x(h).wait_send()


def reduce_tp(rows, number, name):
    tp_count = lax.axis_size("tp")
    columns = rows.shape[1]
    if lax.axis_size("ep") != 2 * Z_AXIS:
        return lax.psum_scatter(rows, "tp", scatter_dimension=0, tiled=True).astype(F32)
    block = rows.shape[0] // tp_count
    dma = pltpu.SemaphoreType.DMA
    return pl.pallas_call(
        reduce_tp_kernel,
        in_specs=[ANY],
        out_specs=pl.BlockSpec(memory_space=pltpu.VMEM),
        out_shape=jax.ShapeDtypeStruct((block, columns), F32),
        scratch_shapes=[
            pltpu.VMEM((2, block, columns), BF),
            pltpu.VMEM((2, block, columns), BF),
            pltpu.VMEM((block, columns), BF),
            dma((2,)), dma((2, 2)), dma((2, 2)), dma((2,)), dma((2,)),
        ],
        compiler_params=params(collective_id=number, has_side_effects=True),
        cost_estimate=link_cost(40.0),
        name=name,
    )(rows.reshape(tp_count, block, columns))


def gather_tp_kernel(rows, out, own_sem, core_send, core_recv, x_send, x_recv):
    me = lax.axis_index("tp")
    x, c = me // 2, me % 2
    other_core, other_x = {"tp": x * 2 + 1 - c}, {"tp": (1 - x) * 2 + c}
    greet([(x >= 0, other_core), (x >= 0, other_x)])
    half = rows.shape[0] // 2
    far = (1 - x) * 2 + c

    def across(h):
        part = pl.ds(h * half, half)
        return remote(rows.at[part], out.at[me, part], x_send.at[h], x_recv.at[h], other_x)

    def arrived(h):
        part = pl.ds(h * half, half)
        return remote(out.at[far, part], out.at[far, part], x_send.at[h], x_recv.at[h], other_x)

    def beside(h):
        part = pl.ds(h * half, half)
        return remote(
            out.at[far, part], out.at[far, part], core_send.at[h], core_recv.at[h], other_core
        )

    own = pltpu.make_async_copy(rows, out.at[me], own_sem)
    near = remote(rows, out.at[me], core_send.at[2], core_recv.at[2], other_core)
    for h in range(2):
        across(h).start()
    near.start()
    own.start()
    for h in range(2):
        arrived(h).wait_recv()
        beside(h).start()
    own.wait()
    near.wait_send()
    other_near = out.at[x * 2 + 1 - c]
    remote(other_near, other_near, core_send.at[2], core_recv.at[2], other_core).wait_recv()
    for h in range(2):
        part = pl.ds(h * half, half)
        other_far = out.at[(1 - x) * 2 + 1 - c, part]
        across(h).wait_send()
        beside(h).wait_send()
        remote(other_far, other_far, core_send.at[h], core_recv.at[h], other_core).wait_recv()


def gather_tp(rows, number, name):
    tp_count = lax.axis_size("tp")
    if lax.axis_size("ep") != 2 * Z_AXIS:
        return lax.all_gather(rows, "tp", axis=0, tiled=True)
    dma = pltpu.SemaphoreType.DMA
    return pl.pallas_call(
        gather_tp_kernel,
        in_specs=[ANY],
        out_specs=ANY,
        out_shape=jax.ShapeDtypeStruct((tp_count,) + rows.shape, rows.dtype),
        scratch_shapes=[dma, dma((3,)), dma((3,)), dma((2,)), dma((2,))],
        compiler_params=params(collective_id=number, has_side_effects=True),
        cost_estimate=link_cost(20.0),
        name=name,
    )(rows).reshape(-1, rows.shape[1])


def sum_all_kernel(x, out, parts, own, send, recv, back_send, back_recv):
    ep_count, tp_count = lax.axis_size("ep"), lax.axis_size("tp")
    total = ep_count * tp_count
    me = lax.axis_index("ep") * tp_count + lax.axis_index("tp")

    def device(d):
        return {"ep": d // tp_count, "tp": d % tp_count}

    barrier = pltpu.get_barrier_semaphore()

    @pl.loop(1, total)
    def _(i):
        pl.semaphore_signal(
            barrier, inc=1, device_id=device(lax.rem(me + i, total)), device_id_type=MESH
        )

    pl.semaphore_wait(barrier, total - 1)

    def scatter(i):
        to = lax.rem(me + i, total)
        return remote(x.at[to], parts.at[me], send.at[i], recv.at[me], device(to))

    def arrived(i):
        origin = lax.rem(me + i, total)
        return remote(parts.at[origin], parts.at[origin], send.at[i], recv.at[origin], device(origin))

    def spread(i):
        to = lax.rem(me + i, total)
        return remote(own, out.at[me], back_send.at[i], back_recv.at[me], device(to))

    def returned(i):
        origin = lax.rem(me + i, total)
        return remote(
            out.at[origin], out.at[origin], back_send.at[i], back_recv.at[origin], device(origin)
        )

    @pl.loop(1, total)
    def _(i):
        scatter(i).start()

    parts[pl.ds(me, 1)] = x[pl.ds(me, 1)]

    @pl.loop(1, total)
    def _(i):
        arrived(i).wait_recv()

    own[...] = jnp.sum(parts[...], axis=0)

    @pl.loop(1, total)
    def _(i):
        spread(i).start()

    out[pl.ds(me, 1)] = own[...][None]

    @pl.loop(1, total)
    def _(i):
        scatter(i).wait_send()
        returned(i).wait_recv()
        spread(i).wait_send()


def sum_all(values, number, name):
    total = lax.axis_size("ep") * lax.axis_size("tp")
    flat = jnp.concatenate([v.reshape(-1) for v in values])
    lanes = 128
    rows = -(-flat.shape[0] // (total * lanes * 8)) * 8
    padded = jnp.pad(flat, (0, total * rows * lanes - flat.shape[0])).reshape(total, rows, lanes)
    if lax.axis_size("ep") != 2 * Z_AXIS:
        summed = lax.psum(padded, ("ep", "tp"))
    else:
        vmem = pl.BlockSpec(memory_space=pltpu.VMEM)
        dma = pltpu.SemaphoreType.DMA
        summed = pl.pallas_call(
            sum_all_kernel,
            in_specs=[vmem],
            out_specs=vmem,
            out_shape=jax.ShapeDtypeStruct(padded.shape, F32),
            scratch_shapes=[
                pltpu.VMEM(padded.shape, F32), pltpu.VMEM((rows, lanes), F32),
                dma((total,)), dma((total,)), dma((total,)), dma((total,)),
            ],
            compiler_params=params(collective_id=number, has_side_effects=True),
            cost_estimate=link_cost(15.0),
            name=name,
        )(padded)
    summed = summed.reshape(-1)
    out, at = [], 0
    for v in values:
        out.append(summed[at : at + v.size].reshape(v.shape))
        at += v.size
    return out


def on_device(
    inputs,
    attn_gain,
    w_query,
    key_weight_matrix,
    value_weight_matrix,
    query_gain,
    key_gain,
    w_out,
    route_gain,
    w_router,
    w_gate,
    w_up,
    w_down,
    routes,
    image_starts,
    cotangent,
):
    tp_count = lax.axis_size("tp")
    ep_count = lax.axis_size("ep")
    tp_index = lax.axis_index("tp")
    ep_index = lax.axis_index("ep")
    length = inputs.shape[0]
    width = inputs.shape[1]
    rows = cotangent.shape[0]
    head_dim = query_gain.shape[0]
    local_experts = w_gate.shape[0]
    experts = local_experts * ep_count
    top = routes.shape[1]
    capacity = -(-(3 * rows * top // (2 * experts)) // 16) * 16

    w_gate_all = lax.all_gather(w_gate.transpose(0, 2, 1)[None], "tp")

    inputs_f = inputs.astype(F32)
    attn_scale = rms_scale(inputs_f)
    normed = (inputs_f * attn_scale * attn_gain).astype(BF)
    queries = dot_nn(normed, w_query)
    key_rows = dot_nn(normed, key_weight_matrix)
    values = dot_nn(normed, value_weight_matrix).astype(BF)
    cosine, sine = rope_tables(length, head_dim)
    q_gain, k_gain = query_gain[None], key_gain[None]
    heads, lse = attention(
        image_starts, queries, key_rows, values, cosine, sine, q_gain, k_gain
    )
    heads, w_rest = lax.optimization_barrier(
        (heads, jnp.stack([w_up.transpose(0, 2, 1), w_down]))
    )
    w_rest_all = lax.all_gather(w_rest, "tp")
    attn_rows = reduce_tp(dot_nn(heads, w_out).astype(BF), 0, "reduce_attention")
    x_rows = lax.dynamic_slice_in_dim(inputs, tp_index * rows, rows, 0).astype(F32)
    scale_rows = lax.dynamic_slice_in_dim(attn_scale, tp_index * rows, rows, 0)
    hidden = x_rows + attn_rows
    route_scale = rms_scale(hidden)
    moe_in = (hidden * route_scale * route_gain).astype(BF)
    moe_in, w_gate_all = lax.optimization_barrier((moe_in, w_gate_all))
    tokens_all, cot_all = gather_ep([moe_in, cotangent], 1, "gather_rows")

    logits = dot_nn(moe_in, w_router)
    router_probs = plain_softmax(logits)
    expert_ids = jnp.arange(experts, dtype=jnp.int32)
    ring_routes = lax.dynamic_index_in_dim(
        routes.reshape(ep_count, tp_count, rows, top), tp_index, 1, keepdims=False
    )
    my_routes = lax.dynamic_index_in_dim(ring_routes, ep_index, 0, keepdims=False)

    def routed_softmax(scores, picked):
        kept = jnp.where(picked, scores, MASKED)
        expo = jnp.where(picked, jnp.exp(kept - jnp.max(kept, axis=-1, keepdims=True)), 0.0)
        return expo / jnp.sum(expo, axis=-1, keepdims=True)

    my_pick = jnp.any(my_routes[:, :, None] == expert_ids[None, None, :], axis=1)
    gates = routed_softmax(logits, my_pick)
    all_pick = jnp.any(ring_routes[..., None] == expert_ids, axis=2)
    gates_all = routed_softmax(dot_nn(tokens_all.reshape(-1, width), w_router).reshape(ep_count, rows, experts), all_pick)
    gate_of = lax.dynamic_slice_in_dim(gates_all, ep_index * local_experts, local_experts, 2)
    mask = lax.dynamic_slice_in_dim(all_pick, ep_index * local_experts, local_experts, 2)
    earlier = (jnp.arange(rows)[:, None] > jnp.arange(rows)[None, :]).astype(BF)
    slots_t = jnp.einsum(
        "tu,bue->bte", earlier, mask.astype(BF), preferred_element_type=F32
    ).astype(jnp.int32)
    slots_t = jnp.where(mask, slots_t, NOWHERE)
    slots = slots_t.transpose(0, 2, 1)
    place = slots[:, :, None, :] == jnp.arange(capacity, dtype=jnp.int32)[:, None]
    slot_gate = jnp.sum(jnp.where(place, gate_of.transpose(0, 2, 1)[:, :, None, :], 0.0), axis=-1)
    slot_gate = slot_gate.transpose(1, 0, 2).reshape(local_experts, ep_count * capacity, 1)

    x_slots, c_slots = select_rows(slots, tokens_all, cot_all, capacity)
    flat = (local_experts, ep_count * capacity, width)
    deep = (local_experts, ep_count, capacity, width)
    x_slots, c_slots = x_slots.reshape(flat), c_slots.reshape(flat)
    out_slots, dx_slots, act, d_gate, d_up, d_gate_slots = experts_both_ways(
        x_slots, c_slots, w_gate_all, w_rest_all, slot_gate
    )
    dx_part, out_part = combine_rows(slots_t, dx_slots.reshape(deep), out_slots.reshape(deep))
    first_grads, rest_grads = expert_grads(x_slots, c_slots, act, d_gate, d_up, tp_count)

    def over_rings(grads):
        return lax.psum_scatter(grads.reshape(-1, width), "tp", scatter_dimension=0, tiled=True)

    dx_part, first_grads, rest_grads = lax.optimization_barrier((dx_part, first_grads, rest_grads))
    first_mine = over_rings(first_grads)
    (dx_mine,) = reduce_ep([dx_part], [F32], 2, "reduce_input_grads")
    dx_mine, first_mine, rest_grads = lax.optimization_barrier((dx_mine, first_mine, rest_grads))
    rest_mine = over_rings(rest_grads).astype(F32).reshape(2, local_experts, -1, width)
    first_mine = first_mine.astype(F32).reshape(local_experts, -1, width)
    d_gate_tokens = jnp.sum(
        jnp.where(
            place,
            d_gate_slots.reshape(local_experts, ep_count, capacity).transpose(1, 0, 2)[..., None],
            0.0,
        ),
        axis=2,
    )
    d_gates = lax.all_to_all(d_gate_tokens, "ep", split_axis=0, concat_axis=0, tiled=True)
    d_gates = d_gates.reshape(experts, rows).T
    w_gate_grad = first_mine.transpose(0, 2, 1)
    w_up_grad = rest_mine[0].transpose(0, 2, 1)
    w_down_grad = rest_mine[1]

    counts = jnp.sum((routes[:, :, None] == expert_ids[None, None, :]).astype(F32), axis=(0, 1))
    total_tokens = routes.shape[0]
    share = counts / (total_tokens * top)
    coeff = AUX * experts * share
    prob_local = jnp.sum(router_probs, axis=0)
    cot = cotangent.astype(F32)
    d_logits = gates * (d_gates - jnp.sum(gates * d_gates, axis=-1, keepdims=True))
    d_logits = d_logits + router_probs * (
        coeff - jnp.sum(router_probs * coeff, axis=-1, keepdims=True)
    )
    d_logits_low = d_logits.astype(BF)
    router_part = dot_tn(moe_in, d_logits_low)
    d_moe = dot_nt(d_logits_low, w_router) + dx_mine
    d_hidden, route_gain_part = norm_back(d_moe, hidden, route_gain[None])
    d_hidden = d_hidden + cot

    d_branch = gather_tp(d_hidden.astype(BF), 3, "gather_branch")
    w_out_part = dot_tn(heads, d_branch)
    d_heads = dot_nt(d_branch, w_out).astype(BF)
    d_queries, d_keys, d_values, query_gain_part, key_gain_part = attention_back(
        image_starts, queries, key_rows, values, d_heads, lse, cosine, sine, q_gain, k_gain
    )
    w_query_part = dot_tn(normed, d_queries)
    w_key_part = dot_tn(normed, d_keys)
    w_value_part = dot_tn(normed, d_values)
    d_normed = (
        dot_nt(d_queries, w_query)
        + dot_nt(d_keys, key_weight_matrix)
        + dot_nt(d_values, value_weight_matrix)
    )
    d_mine = reduce_tp(d_normed.astype(BF), 4, "reduce_normed")
    attn_gain_part = jnp.sum(d_mine * x_rows * scale_rows, axis=0)
    inner = d_mine * attn_gain
    inputs_grad = (
        d_hidden
        + scale_rows * inner
        - x_rows * scale_rows**3 * jnp.mean(inner * x_rows, axis=-1, keepdims=True)
    )
    small = sum_all(
        [
            router_part,
            attn_gain_part,
            route_gain_part[0],
            query_gain_part[0],
            key_gain_part[0],
            prob_local,
        ],
        5,
        "sum_small",
    )
    w_router_grad, attn_gain_grad, route_gain_grad, query_gain_grad, key_gain_grad, prob_all = small

    def by_rows(part):
        return part.astype(BF).reshape(ep_count, -1, part.shape[1])

    w_out_blocks = w_out_part.astype(BF).reshape(-1, ep_count, width // ep_count).transpose(1, 0, 2)
    out_mine, w_query_grad, w_key_grad, w_value_grad, w_out_grad = reduce_ep(
        [
            out_part,
            by_rows(w_query_part),
            by_rows(w_key_part),
            by_rows(w_value_part),
            w_out_blocks,
        ],
        [F32] * 5,
        6,
        "reduce_outputs",
    )
    output = (hidden + out_mine).astype(BF)
    aux_loss = experts * jnp.sum(share * (prob_all / total_tokens))
    return (
        output,
        aux_loss,
        inputs_grad,
        attn_gain_grad,
        w_query_grad,
        w_key_grad,
        w_value_grad,
        query_gain_grad,
        key_gain_grad,
        w_out_grad,
        route_gain_grad,
        w_router_grad,
        w_gate_grad,
        w_up_grad,
        w_down_grad,
    )


def solution(mesh):
    return jax.shard_map(
        on_device,
        mesh=mesh,
        in_specs=(
            P("ep", None),
            P(),
            P(None, "tp"),
            P(None, "tp"),
            P(None, "tp"),
            P(),
            P(),
            P("tp", None),
            P(),
            P(),
            P("ep", None, "tp"),
            P("ep", None, "tp"),
            P("ep", "tp", None),
            P(),
            P("ep", None),
            P(("ep", "tp"), None),
        ),
        out_specs=(
            P(("ep", "tp"), None),
            P(),
            P(("ep", "tp"), None),
            P(),
            P("ep", "tp"),
            P("ep", "tp"),
            P("ep", "tp"),
            P(),
            P(),
            P("tp", "ep"),
            P(),
            P(),
            P("ep", None, "tp"),
            P("ep", None, "tp"),
            P("ep", "tp", None),
        ),
        check_vma=False,
    )
```

```python
import functools

import jax
import jax.numpy as jnp
from jax import lax
from jax.experimental import pallas as pl
from jax.experimental.pallas import tpu as pltpu
from jax.sharding import PartitionSpec as P

IMG = 256
EPS = 1e-06
AUX = 0.04
THETA = 1000000.0
MASKED = -1e30
NOWHERE = -(1 << 20)
BF = jnp.bfloat16
F32 = jnp.float32
VMEM_BYTES = 60 * 1024 * 1024


def dot_nn(a, b):
    return lax.dot_general(a, b, (((1,), (0,)), ((), ())), preferred_element_type=F32)


def dot_nt(a, b):
    return lax.dot_general(a, b, (((1,), (1,)), ((), ())), preferred_element_type=F32)


def dot_tn(a, b):
    return lax.dot_general(a, b, (((0,), (0,)), ((), ())), preferred_element_type=F32)


def params(**kw):
    return pltpu.CompilerParams(vmem_limit_bytes=VMEM_BYTES, **kw)


def rms_scale(value_rows):
    return lax.rsqrt(jnp.mean(value_rows * value_rows, axis=-1, keepdims=True) + EPS)


def plain_softmax(value_rows):
    top = jnp.max(value_rows, axis=-1, keepdims=True)
    expo = jnp.exp(value_rows - top)
    return expo / jnp.sum(expo, axis=-1, keepdims=True)


def rope_tables(length, size):
    half = size // 2
    freq = jnp.exp(-jnp.log(THETA) * (2.0 * jnp.arange(half, dtype=F32)) / size)
    angle = jnp.arange(length, dtype=F32)[:, None] * freq[None, :]
    cosine = jnp.cos(angle)
    sine = jnp.sin(angle)
    return (jnp.concatenate([cosine, cosine], axis=-1), jnp.concatenate([-sine, sine], axis=-1))


def turn(rows, cosine, sine):
    return rows * cosine + pltpu.roll(rows, rows.shape[-1] // 2, 1) * sine


def turn_back(rows, cosine, sine):
    return rows * cosine - pltpu.roll(rows, rows.shape[-1] // 2, 1) * sine


MESH = pl.DeviceIdType.MESH
ANY = pl.BlockSpec(memory_space=pl.ANY)
Z_AXIS = 4


def link_cost(us):
    return pl.CostEstimate(flops=0, bytes_accessed=int(us * 3.0e6), transcendentals=0)


def greet(partners):
    barrier = pltpu.get_barrier_semaphore()
    count = 0
    for there, device in partners:
        flag = jnp.asarray(there, jnp.int32)

        @pl.when(there)
        def _(device=device):
            pl.semaphore_signal(barrier, inc=1, device_id=device, device_id_type=MESH)

        count = count + flag
    pl.semaphore_wait(barrier, count)


def remote(src, dst, send, recv, device):
    return pltpu.make_async_remote_copy(
        src_ref=src, dst_ref=dst, send_sem=send, recv_sem=recv, device_id=device, device_id_type=MESH
    )


def ring_place():
    me = lax.axis_index("ep")
    z, y = me // 2, me % 2
    return me, z, y, {"ep": me + 2}, {"ep": me - 2}, {"ep": me + 1 - 2 * y}


class EpGather:
    def __init__(self, ins, outs, sems):
        self.ins, self.outs = ins, outs
        self.own_sem, self.up_send, self.up_recv, self.dn_send, self.dn_recv = sems[:5]
        self.y_send, self.y_recv = sems[5:]
        self.me, self.z, self.y, self.up, self.down, self.beside = ring_place()

    def partners(self):
        z = self.z
        return [(z < Z_AXIS - 1, self.up), (z > 0, self.down), (z >= 0, self.beside)]

    def block(self, a, zt):
        return self.outs[a].at[zt * 2 + self.y]

    def upward(self, src, a, zt):
        return remote(src, self.block(a, zt), self.up_send.at[a, zt], self.up_recv.at[a, zt], self.up)

    def downward(self, src, a, zt):
        return remote(src, self.block(a, zt), self.dn_send.at[a, zt], self.dn_recv.at[a, zt], self.down)

    def sideways(self, src, a, zt):
        return remote(src, self.block(a, zt), self.y_send.at[a, zt], self.y_recv.at[a, zt], self.beside)

    def start(self):
        z = self.z
        for a, x in enumerate(self.ins):

            @pl.when(z < Z_AXIS - 1)
            def _(a=a, x=x):
                self.upward(x, a, z).start()

            @pl.when(z > 0)
            def _(a=a, x=x):
                self.downward(x, a, z).start()

            self.sideways(x, a, z).start()
            pltpu.make_async_copy(x, self.block(a, z), self.own_sem.at[a]).start()

    def hop(self, d):
        z = self.z
        for a in range(len(self.ins)):

            @pl.when(z >= d)
            def _(a=a, zt=z - d):
                self.upward(self.block(a, zt), a, zt).wait_recv()

                @pl.when(z < Z_AXIS - 1)
                def _():
                    self.upward(self.block(a, zt), a, zt).start()

                self.sideways(self.block(a, zt), a, zt).start()

            @pl.when(z + d < Z_AXIS)
            def _(a=a, zt=z + d):
                self.downward(self.block(a, zt), a, zt).wait_recv()

                @pl.when(z > 0)
                def _():
                    self.downward(self.block(a, zt), a, zt).start()

                self.sideways(self.block(a, zt), a, zt).start()

    def own_done(self, a):
        pltpu.make_async_copy(self.ins[a], self.block(a, self.z), self.own_sem.at[a]).wait()

    def side_done(self, a, zt):
        other = self.outs[a].at[zt * 2 + 1 - self.y]
        remote(other, other, self.y_send.at[a, zt], self.y_recv.at[a, zt], self.beside).wait_recv()

    def sent(self, a):
        z = self.z
        for zt in range(Z_AXIS):
            src = self.block(a, zt)
            self.sideways(src, a, zt).wait_send()

            @pl.when((zt <= z) & (z < Z_AXIS - 1))
            def _(src=src, zt=zt):
                self.upward(src, a, zt).wait_send()

            @pl.when((zt >= z) & (z > 0))
            def _(src=src, zt=zt):
                self.downward(src, a, zt).wait_send()

    def finish(self):
        for a in range(len(self.ins)):
            self.own_done(a)
            for zt in range(Z_AXIS):
                self.side_done(a, zt)
            self.sent(a)


def gather_sems(count):
    dma = pltpu.SemaphoreType.DMA
    return [dma((count,))] + [dma((count, Z_AXIS))] * 6


def gather_ep_kernel(number, *refs):
    gather = EpGather(refs[:number], refs[number : 2 * number], refs[2 * number :])
    greet(gather.partners())
    gather.start()
    for d in range(1, Z_AXIS):
        gather.hop(d)
    gather.finish()


def gather_ep(arrays, number, name):
    count = len(arrays)
    ep_count = lax.axis_size("ep")
    if ep_count != 2 * Z_AXIS:
        return [lax.all_gather(a, "ep") for a in arrays]
    return pl.pallas_call(
        functools.partial(gather_ep_kernel, count),
        in_specs=[ANY] * count,
        out_specs=[ANY] * count,
        out_shape=[jax.ShapeDtypeStruct((ep_count,) + a.shape, a.dtype) for a in arrays],
        scratch_shapes=gather_sems(count),
        compiler_params=params(collective_id=number, has_side_effects=True),
        cost_estimate=link_cost(80.0 * count),
        name=name,
    )(*arrays)


def add_rows(total, terms, chunk=32):
    @pl.loop(0, total.shape[0] // chunk)
    def _(i):
        rows = pl.ds(pl.multiple_of(i * chunk, chunk), chunk)
        value = terms[0][rows, :].astype(F32)
        for term in terms[1:]:
            value = value + term[rows, :].astype(F32)
        total[rows, :] = value.astype(total.dtype)


def scatter_order(z):
    table = ((3, 2, 1, 0), (3, 0, 2, 1), (0, 3, 1, 2), (0, 1, 2, 3))
    return [
        jnp.where(
            z == 0,
            table[0][k],
            jnp.where(z == 1, table[1][k], jnp.where(z == 2, table[2][k], table[3][k])),
        )
        for k in range(Z_AXIS)
    ]


def reduce_ep_kernel(number, *refs):
    ins, outs = refs[:number], refs[number : 2 * number]
    bufs = refs[2 * number : 6 * number]
    own_sem, up_send, up_recv, dn_send, dn_recv, y_send, y_recv = refs[6 * number :]
    me, z, y, up, down, beside = ring_place()
    top = Z_AXIS - 1
    order = scatter_order(z)
    greet([(z < top, up), (z > 0, down), (z >= 0, beside)])

    for zt in order:
        for a in range(number):
            mine, side = bufs[4 * a], bufs[4 * a + 1]
            remote(
                ins[a].at[zt * 2 + 1 - y], side.at[zt], y_send.at[a, zt], y_recv.at[a, zt], beside
            ).start()
            pltpu.make_async_copy(ins[a].at[zt * 2 + y], mine.at[zt], own_sem.at[a, zt]).start()

    for zt in order:
        for a in range(number):
            mine, side, below, above = bufs[4 * a : 4 * a + 4]
            pltpu.make_async_copy(ins[a].at[zt * 2 + y], mine.at[zt], own_sem.at[a, zt]).wait()
            remote(
                side.at[zt], side.at[zt], y_send.at[a, zt], y_recv.at[a, zt], beside
            ).wait_recv()

            def rising(a=a, mine=mine, below=below, zt=zt):
                return remote(
                    mine.at[zt], below.at[zt], up_send.at[a, zt], up_recv.at[a, zt], up
                )

            def falling(a=a, mine=mine, above=above, zt=zt):
                return remote(
                    mine.at[zt], above.at[zt], dn_send.at[a, zt], dn_recv.at[a, zt], down
                )

            @pl.when((zt > z) & (z == 0))
            def _(mine=mine, side=side, zt=zt):
                add_rows(mine.at[zt], [mine.at[zt], side.at[zt]])

            @pl.when((zt > z) & (z > 0))
            def _(mine=mine, side=side, below=below, zt=zt, rising=rising):
                rising().wait_recv()
                add_rows(mine.at[zt], [mine.at[zt], side.at[zt], below.at[zt]])

            @pl.when(zt > z)
            def _(rising=rising):
                rising().start()

            @pl.when((zt < z) & (z == top))
            def _(mine=mine, side=side, zt=zt):
                add_rows(mine.at[zt], [mine.at[zt], side.at[zt]])

            @pl.when((zt < z) & (z < top))
            def _(mine=mine, side=side, above=above, zt=zt, falling=falling):
                falling().wait_recv()
                add_rows(mine.at[zt], [mine.at[zt], side.at[zt], above.at[zt]])

            @pl.when(zt < z)
            def _(falling=falling):
                falling().start()

    for a in range(number):
        mine, side, below, above = bufs[4 * a : 4 * a + 4]
        own, beside_rows, low, high = mine.at[z], side.at[z], below.at[z], above.at[z]

        @pl.when(z > 0)
        def _(a=a, low=low):
            remote(low, low, up_send.at[a, z], up_recv.at[a, z], up).wait_recv()

        @pl.when(z < top)
        def _(a=a, high=high):
            remote(high, high, dn_send.at[a, z], dn_recv.at[a, z], down).wait_recv()

        @pl.when(z == 0)
        def _(a=a, own=own, beside_rows=beside_rows, high=high):
            add_rows(outs[a], [own, beside_rows, high])

        @pl.when(z == top)
        def _(a=a, own=own, beside_rows=beside_rows, low=low):
            add_rows(outs[a], [own, beside_rows, low])

        @pl.when((z > 0) & (z < top))
        def _(a=a, own=own, beside_rows=beside_rows, low=low, high=high):
            add_rows(outs[a], [own, beside_rows, low, high])

    for a in range(number):
        mine, side = bufs[4 * a], bufs[4 * a + 1]
        for zt in range(Z_AXIS):
            src = ins[a].at[zt * 2 + 1 - y]
            remote(src, src, y_send.at[a, zt], y_recv.at[a, zt], beside).wait_send()

            @pl.when(zt > z)
            def _(mine=mine, zt=zt, a=a):
                src = mine.at[zt]
                remote(src, src, up_send.at[a, zt], up_recv.at[a, zt], up).wait_send()

            @pl.when(zt < z)
            def _(mine=mine, zt=zt, a=a):
                src = mine.at[zt]
                remote(src, src, dn_send.at[a, zt], dn_recv.at[a, zt], down).wait_send()


def reduce_ep(parts, dtypes, number, name):
    count = len(parts)
    ep_count = lax.axis_size("ep")
    if ep_count != 2 * Z_AXIS:
        return [
            lax.psum_scatter(p, "ep", scatter_dimension=0).astype(t) for p, t in zip(parts, dtypes)
        ]
    dma = pltpu.SemaphoreType.DMA
    scratch = []
    for p in parts:
        scratch += [pltpu.VMEM((Z_AXIS,) + p.shape[1:], BF)] * 4
    return pl.pallas_call(
        functools.partial(reduce_ep_kernel, count),
        in_specs=[ANY] * count,
        out_specs=[pl.BlockSpec(memory_space=pltpu.VMEM)] * count,
        out_shape=[jax.ShapeDtypeStruct(p.shape[1:], t) for p, t in zip(parts, dtypes)],
        scratch_shapes=scratch + [dma((count, Z_AXIS))] * 7,
        compiler_params=params(collective_id=number, has_side_effects=True),
        cost_estimate=link_cost(80.0 * sum(p.size for p in parts) / 2**22),
        name=name,
    )(*parts)


def reduce_tp_kernel(part, out, mine, core_rows, x_rows, own_sem, core_send, core_recv, x_send, x_recv):
    me = lax.axis_index("tp")
    x, c = me // 2, me % 2
    other_core, other_x = {"tp": x * 2 + 1 - c}, {"tp": (1 - x) * 2 + c}
    greet([(x >= 0, other_core), (x >= 0, other_x)])
    half = out.shape[0] // 2

    def to_core(xt, h):
        rows = pl.ds(h * half, half)
        return remote(
            part.at[xt * 2 + 1 - c, rows], core_rows.at[xt, rows],
            core_send.at[xt, h], core_recv.at[xt, h], other_core,
        )

    def load(xt):
        return pltpu.make_async_copy(part.at[xt * 2 + c], mine.at[xt], own_sem.at[xt])

    def to_x(h):
        rows = pl.ds(h * half, half)
        return remote(mine.at[1 - x, rows], x_rows.at[rows], x_send.at[h], x_recv.at[h], other_x)

    for h in range(2):
        to_core(1 - x, h).start()
    load(1 - x).start()
    load(x).start()
    for h in range(2):
        to_core(x, h).start()
    load(1 - x).wait()
    for h in range(2):
        rows = pl.ds(h * half, half)
        to_core(1 - x, h).wait_recv()
        add_rows(mine.at[1 - x, rows], [mine.at[1 - x, rows], core_rows.at[1 - x, rows]])
        to_x(h).start()
    load(x).wait()
    for h in range(2):
        rows = pl.ds(h * half, half)
        to_core(x, h).wait_recv()
        to_x(h).wait_recv()
        add_rows(out.at[rows], [mine.at[x, rows], core_rows.at[x, rows], x_rows.at[rows]])
    for h in range(2):
        to_core(1 - x, h).wait_send()
        to_core(x, h).wait_send()
        to_x(h).wait_send()


def reduce_tp(rows, number, name):
    tp_count = lax.axis_size("tp")
    columns = rows.shape[1]
    if lax.axis_size("ep") != 2 * Z_AXIS:
        return lax.psum_scatter(rows, "tp", scatter_dimension=0, tiled=True).astype(F32)
    block = rows.shape[0] // tp_count
    dma = pltpu.SemaphoreType.DMA
    return pl.pallas_call(
        reduce_tp_kernel,
        in_specs=[ANY],
        out_specs=pl.BlockSpec(memory_space=pltpu.VMEM),
        out_shape=jax.ShapeDtypeStruct((block, columns), F32),
        scratch_shapes=[
            pltpu.VMEM((2, block, columns), BF),
            pltpu.VMEM((2, block, columns), BF),
            pltpu.VMEM((block, columns), BF),
            dma((2,)), dma((2, 2)), dma((2, 2)), dma((2,)), dma((2,)),
        ],
        compiler_params=params(collective_id=number, has_side_effects=True),
        cost_estimate=link_cost(40.0),
        name=name,
    )(rows.reshape(tp_count, block, columns))


def gather_tp_kernel(rows, out, own_sem, core_send, core_recv, x_send, x_recv):
    me = lax.axis_index("tp")
    x, c = me // 2, me % 2
    other_core, other_x = {"tp": x * 2 + 1 - c}, {"tp": (1 - x) * 2 + c}
    greet([(x >= 0, other_core), (x >= 0, other_x)])
    half = rows.shape[0] // 2
    far = (1 - x) * 2 + c

    def across(h):
        part = pl.ds(h * half, half)
        return remote(rows.at[part], out.at[me, part], x_send.at[h], x_recv.at[h], other_x)

    def arrived(h):
        part = pl.ds(h * half, half)
        return remote(out.at[far, part], out.at[far, part], x_send.at[h], x_recv.at[h], other_x)

    def beside(h):
        part = pl.ds(h * half, half)
        return remote(
            out.at[far, part], out.at[far, part], core_send.at[h], core_recv.at[h], other_core
        )

    own = pltpu.make_async_copy(rows, out.at[me], own_sem)
    near = remote(rows, out.at[me], core_send.at[2], core_recv.at[2], other_core)
    for h in range(2):
        across(h).start()
    near.start()
    own.start()
    for h in range(2):
        arrived(h).wait_recv()
        beside(h).start()
    own.wait()
    near.wait_send()
    other_near = out.at[x * 2 + 1 - c]
    remote(other_near, other_near, core_send.at[2], core_recv.at[2], other_core).wait_recv()
    for h in range(2):
        part = pl.ds(h * half, half)
        other_far = out.at[(1 - x) * 2 + 1 - c, part]
        across(h).wait_send()
        beside(h).wait_send()
        remote(other_far, other_far, core_send.at[h], core_recv.at[h], other_core).wait_recv()


def gather_tp(rows, number, name):
    tp_count = lax.axis_size("tp")
    if lax.axis_size("ep") != 2 * Z_AXIS:
        return lax.all_gather(rows, "tp", axis=0, tiled=True)
    dma = pltpu.SemaphoreType.DMA
    return pl.pallas_call(
        gather_tp_kernel,
        in_specs=[ANY],
        out_specs=ANY,
        out_shape=jax.ShapeDtypeStruct((tp_count,) + rows.shape, rows.dtype),
        scratch_shapes=[dma, dma((3,)), dma((3,)), dma((2,)), dma((2,))],
        compiler_params=params(collective_id=number, has_side_effects=True),
        cost_estimate=link_cost(20.0),
        name=name,
    )(rows).reshape(-1, rows.shape[1])


def sum_all_kernel(x, out, parts, own, send, recv, back_send, back_recv):
    ep_count, tp_count = lax.axis_size("ep"), lax.axis_size("tp")
    total = ep_count * tp_count
    me = lax.axis_index("ep") * tp_count + lax.axis_index("tp")

    def device(d):
        return {"ep": d // tp_count, "tp": d % tp_count}

    barrier = pltpu.get_barrier_semaphore()

    @pl.loop(1, total)
    def _(i):
        pl.semaphore_signal(
            barrier, inc=1, device_id=device(lax.rem(me + i, total)), device_id_type=MESH
        )

    pl.semaphore_wait(barrier, total - 1)

    def scatter(i):
        to = lax.rem(me + i, total)
        return remote(x.at[to], parts.at[me], send.at[i], recv.at[me], device(to))

    def arrived(i):
        origin = lax.rem(me + i, total)
        return remote(parts.at[origin], parts.at[origin], send.at[i], recv.at[origin], device(origin))

    def spread(i):
        to = lax.rem(me + i, total)
        return remote(own, out.at[me], back_send.at[i], back_recv.at[me], device(to))

    def returned(i):
        origin = lax.rem(me + i, total)
        return remote(
            out.at[origin], out.at[origin], back_send.at[i], back_recv.at[origin], device(origin)
        )

    @pl.loop(1, total)
    def _(i):
        scatter(i).start()

    parts[pl.ds(me, 1)] = x[pl.ds(me, 1)]

    @pl.loop(1, total)
    def _(i):
        arrived(i).wait_recv()

    own[...] = jnp.sum(parts[...], axis=0)

    @pl.loop(1, total)
    def _(i):
        spread(i).start()

    out[pl.ds(me, 1)] = own[...][None]

    @pl.loop(1, total)
    def _(i):
        scatter(i).wait_send()
        returned(i).wait_recv()
        spread(i).wait_send()


def sum_all(values, number, name):
    total = lax.axis_size("ep") * lax.axis_size("tp")
    flat = jnp.concatenate([v.reshape(-1) for v in values])
    lanes = 128
    rows = -(-flat.shape[0] // (total * lanes * 8)) * 8
    padded = jnp.pad(flat, (0, total * rows * lanes - flat.shape[0])).reshape(total, rows, lanes)
    if lax.axis_size("ep") != 2 * Z_AXIS:
        summed = lax.psum(padded, ("ep", "tp"))
    else:
        vmem = pl.BlockSpec(memory_space=pltpu.VMEM)
        dma = pltpu.SemaphoreType.DMA
        summed = pl.pallas_call(
            sum_all_kernel,
            in_specs=[vmem],
            out_specs=vmem,
            out_shape=jax.ShapeDtypeStruct(padded.shape, F32),
            scratch_shapes=[
                pltpu.VMEM(padded.shape, F32), pltpu.VMEM((rows, lanes), F32),
                dma((total,)), dma((total,)), dma((total,)), dma((total,)),
            ],
            compiler_params=params(collective_id=number, has_side_effects=True),
            cost_estimate=link_cost(15.0),
            name=name,
        )(padded)
    summed = summed.reshape(-1)
    out, at = [], 0
    for v in values:
        out.append(summed[at : at + v.size].reshape(v.shape))
        at += v.size
    return out


def fill_bias(span_ref, bias, chunk=256):
    keys, length = bias.shape
    query = lax.broadcasted_iota(jnp.int32, (1, length), 1)

    def spans(pos):
        first = (pos >= span_ref[0, 0]) & (pos < span_ref[0, 0] + IMG)
        second = (pos >= span_ref[0, 1]) & (pos < span_ref[0, 1] + IMG)
        return jnp.where(first, 0, jnp.where(second, 1, -1))

    query_span = spans(query)
    query_other = jnp.where(query_span < 0, -2, query_span)
    for start in range(0, keys, chunk):
        key = start + lax.broadcasted_iota(jnp.int32, (chunk, 1), 0)
        ok = (key <= query) | (spans(key) == query_other)
        bias[start : start + chunk, :] = jnp.where(ok, 0.0, MASKED)


def query_tiles(length):
    tile = min(IMG, length)
    return [
        (start, tile, min(length, start + tile + -(-IMG // tile) * tile))
        for start in range(0, length, tile)
    ]


def attention_kernel(
    span_ref, q_ref, k_ref, v_ref, cos_ref, sin_ref, qg_ref, kg_ref, w_out_ref, cot_ref,
    out_ref, lse_ref, rows_ref, cots_ref,
    bias, k_rot, v_t, heads, part, core_rows, x_rows, core_send, core_recv, x_send, x_recv, *sems,
):
    factor = q_ref.shape[-1] ** (-0.5)
    cosine, sine = cos_ref[...], sin_ref[...]
    step = pl.program_id(0)
    size = q_ref.shape[-1]
    me = lax.axis_index("tp")
    x, c = me // 2, me % 2
    other_core, other_x = {"tp": x * 2 + 1 - c}, {"tp": (1 - x) * 2 + c}
    gather = EpGather([cot_ref], [cots_ref], sems)

    @pl.when(step == 0)
    def _():
        greet(gather.partners() + [(x >= 0, other_core), (x >= 0, other_x)])
        gather.start()
        fill_bias(span_ref, bias)
        k = k_ref[...]
        k_rot[...] = turn(k * rms_scale(k) * kg_ref[...], cosine, sine).astype(BF)
        v_t[...] = v_ref[...].astype(F32).T.astype(BF)

    q = q_ref[...]
    q_rot = turn(q * rms_scale(q) * qg_ref[...], cosine, sine).astype(BF)
    for start, tile, keys in query_tiles(q.shape[0]):
        cols = slice(start, start + tile)
        s = dot_nt(k_rot[:keys, :], q_rot[cols, :]) * factor + bias[:keys, cols]
        top = jnp.max(s, axis=0, keepdims=True)
        p = jnp.exp(s - top)
        total = jnp.sum(p, axis=0, keepdims=True)
        o_t = dot_nn(v_t[:, :keys], p.astype(BF)) / total
        rows = o_t.T.astype(BF)
        out_ref[cols, :] = rows
        heads[step, cols, :] = rows
        lse_ref[0, :, cols] = top + jnp.log(total)

    @pl.when(step == pl.num_programs(0) - 1)
    def _():
        count = heads.shape[0]
        block = rows_ref.shape[0]

        def project(tp):
            lines = pl.ds(pl.multiple_of(tp * block, block), block)
            rows = jnp.concatenate([heads[h, lines, :] for h in range(count)], axis=1)
            part[tp] = dot_nn(rows, w_out_ref[...]).astype(BF)

        def to_core(xt):
            return remote(
                part.at[xt * 2 + 1 - c], core_rows.at[xt],
                core_send.at[xt], core_recv.at[xt], other_core,
            )

        far, near = part.at[(1 - x) * 2 + c], part.at[x * 2 + c]
        to_x = remote(far, x_rows, x_send, x_recv, other_x)
        gather.hop(1)
        project((1 - x) * 2 + 1 - c)
        to_core(1 - x).start()
        project((1 - x) * 2 + c)
        to_core(1 - x).wait_recv()
        add_rows(far, [far, core_rows.at[1 - x]])
        to_x.start()
        project(x * 2 + 1 - c)
        to_core(x).start()
        project(x * 2 + c)
        gather.hop(2)
        to_core(x).wait_recv()
        gather.hop(3)
        to_x.wait_recv()
        add_rows(rows_ref, [near, core_rows.at[x], x_rows])
        gather.finish()
        to_core(1 - x).wait_send()
        to_core(x).wait_send()
        to_x.wait_send()


def plain_attention_kernel(
    span_ref, q_ref, k_ref, v_ref, cos_ref, sin_ref, qg_ref, kg_ref, out_ref, lse_ref,
    bias, k_rot, v_t,
):
    factor = q_ref.shape[-1] ** (-0.5)
    cosine, sine = cos_ref[...], sin_ref[...]

    @pl.when(pl.program_id(0) == 0)
    def _():
        fill_bias(span_ref, bias)
        k = k_ref[...]
        k_rot[...] = turn(k * rms_scale(k) * kg_ref[...], cosine, sine).astype(BF)
        v_t[...] = v_ref[...].astype(F32).T.astype(BF)

    q = q_ref[...]
    q_rot = turn(q * rms_scale(q) * qg_ref[...], cosine, sine).astype(BF)
    for start, tile, keys in query_tiles(q.shape[0]):
        cols = slice(start, start + tile)
        s = dot_nt(k_rot[:keys, :], q_rot[cols, :]) * factor + bias[:keys, cols]
        top = jnp.max(s, axis=0, keepdims=True)
        p = jnp.exp(s - top)
        total = jnp.sum(p, axis=0, keepdims=True)
        o_t = dot_nn(v_t[:, :keys], p.astype(BF)) / total
        out_ref[cols, :] = o_t.T.astype(BF)
        lse_ref[0, :, cols] = top + jnp.log(total)


def attention(span, q, k, v, cosine, sine, q_gain, k_gain, w_out, cotangent, number):
    length, size = k.shape
    heads = q.shape[1] // size
    whole = pl.BlockSpec((length, size), lambda h: (0, 0))
    head = pl.BlockSpec((length, size), lambda h: (0, h))
    gain = pl.BlockSpec((1, size), lambda h: (0, 0))
    in_specs = [
        pl.BlockSpec(memory_space=pltpu.SMEM), head, whole, whole, whole, whole, gain, gain,
    ]
    out_specs = [head, pl.BlockSpec((1, 1, length), lambda h: (h, 0, 0))]
    out_shape = [
        jax.ShapeDtypeStruct((length, heads * size), BF),
        jax.ShapeDtypeStruct((heads, 1, length), F32),
    ]
    scratch = [
        pltpu.VMEM((length, length), F32),
        pltpu.VMEM((length, size), BF),
        pltpu.VMEM((size, length), BF),
    ]
    args = (span, q, k, v, cosine, sine, q_gain, k_gain)
    ep_count, tp_count = lax.axis_size("ep"), lax.axis_size("tp")
    if ep_count != 2 * Z_AXIS:
        out, lse = pl.pallas_call(
            plain_attention_kernel,
            grid=(heads,),
            in_specs=in_specs,
            out_specs=out_specs,
            out_shape=out_shape,
            scratch_shapes=scratch,
            compiler_params=params(),
            name="plain_attention",
        )(*args)
        rows = lax.psum_scatter(
            dot_nn(out, w_out).astype(BF), "tp", scatter_dimension=0, tiled=True
        )
        return out, lse, rows.astype(F32), lax.all_gather(cotangent, "ep")
    block, width = cotangent.shape
    dma = pltpu.SemaphoreType.DMA
    return pl.pallas_call(
        attention_kernel,
        grid=(heads,),
        in_specs=in_specs + [pl.BlockSpec(w_out.shape, lambda h: (0, 0)), ANY],
        out_specs=out_specs + [pl.BlockSpec((block, width), lambda h: (0, 0)), ANY],
        out_shape=out_shape
        + [
            jax.ShapeDtypeStruct((block, width), F32),
            jax.ShapeDtypeStruct((ep_count, block, width), BF),
        ],
        scratch_shapes=scratch
        + [
            pltpu.VMEM((heads, length, size), BF),
            pltpu.VMEM((tp_count, block, width), BF),
            pltpu.VMEM((2, block, width), BF),
            pltpu.VMEM((block, width), BF),
            dma((2,)), dma((2,)), dma, dma,
        ]
        + gather_sems(1),
        compiler_params=params(collective_id=number, has_side_effects=True),
        cost_estimate=link_cost(90.0),
        name="attention",
    )(*args, w_out, cotangent)


def norm_back(grads, rows, gain):
    scale = rms_scale(rows)
    gain_part = jnp.sum(grads * rows * scale, axis=0, keepdims=True)
    inner = grads * gain
    mean = jnp.mean(inner * rows, axis=-1, keepdims=True)
    return scale * inner - rows * (scale * scale * scale * mean), gain_part


def attention_back_kernel(
    span_ref, q_ref, k_ref, v_ref, grad_ref, lse_ref, cos_ref, sin_ref, qg_ref, kg_ref,
    dq_ref, dk_ref, dv_ref, dqg_ref, dkg_ref,
    bias, k_rot, k_t, dk_acc, dv_acc, dq_t,
):
    factor = q_ref.shape[-1] ** (-0.5)
    cosine, sine = cos_ref[...], sin_ref[...]
    step = pl.program_id(0)

    @pl.when(step == 0)
    def _():
        fill_bias(span_ref, bias)
        k = k_ref[...]
        rotated = turn(k * rms_scale(k) * kg_ref[...], cosine, sine)
        k_rot[...] = rotated.astype(BF)
        k_t[...] = rotated.T.astype(BF)
        dk_acc[...] = jnp.zeros_like(dk_acc)
        dv_acc[...] = jnp.zeros_like(dv_acc)
        dqg_ref[...] = jnp.zeros_like(dqg_ref)

    q = q_ref[...]
    q_rot = turn(q * rms_scale(q) * qg_ref[...], cosine, sine).astype(BF)
    for start, tile, keys in query_tiles(q.shape[0]):
        cols = slice(start, start + tile)
        s = dot_nt(k_rot[:keys, :], q_rot[cols, :]) * factor + bias[:keys, cols]
        p = jnp.exp(s - lse_ref[0, :, cols])
        grad = grad_ref[cols, :]
        dp = dot_nt(v_ref[:keys, :], grad)
        mean = jnp.sum(p * dp, axis=0, keepdims=True)
        raw = (p * (dp - mean) * factor).astype(BF)
        dq_t[:, cols] = dot_nn(k_t[:, :keys], raw)
        dk_acc[:keys, :] += dot_nn(raw, q_rot[cols, :])
        dv_acc[:keys, :] += dot_nn(p.astype(BF), grad)
    back, gain_part = norm_back(turn_back(dq_t[...].T, cosine, sine), q, qg_ref[...])
    dq_ref[...] = back.astype(BF)
    dqg_ref[...] += gain_part

    @pl.when(step == pl.num_programs(0) - 1)
    def _():
        back, gain_part = norm_back(turn_back(dk_acc[...], cosine, sine), k_ref[...], kg_ref[...])
        dk_ref[...] = back.astype(BF)
        dkg_ref[...] = gain_part
        dv_ref[...] = dv_acc[...].astype(BF)


def attention_back(span, q, k, v, grads, lse, cosine, sine, q_gain, k_gain):
    length, size = k.shape
    heads = q.shape[1] // size
    whole = pl.BlockSpec((length, size), lambda h: (0, 0))
    head = pl.BlockSpec((length, size), lambda h: (0, h))
    gain = pl.BlockSpec((1, size), lambda h: (0, 0))
    return pl.pallas_call(
        attention_back_kernel,
        grid=(heads,),
        in_specs=[
            pl.BlockSpec(memory_space=pltpu.SMEM), head, whole, whole, head,
            pl.BlockSpec((1, 1, length), lambda h: (h, 0, 0)), whole, whole, gain, gain,
        ],
        out_specs=[head, whole, whole, gain, gain],
        out_shape=[
            jax.ShapeDtypeStruct((length, heads * size), BF),
            jax.ShapeDtypeStruct((length, size), BF),
            jax.ShapeDtypeStruct((length, size), BF),
            jax.ShapeDtypeStruct((1, size), F32),
            jax.ShapeDtypeStruct((1, size), F32),
        ],
        scratch_shapes=[
            pltpu.VMEM((length, length), F32),
            pltpu.VMEM((length, size), BF),
            pltpu.VMEM((size, length), BF),
            pltpu.VMEM((length, size), F32),
            pltpu.VMEM((length, size), F32),
            pltpu.VMEM((size, length), F32),
        ],
        compiler_params=params(),
        name="attention_back",
    )(span, q, k, v, grads, lse, cosine, sine, q_gain, k_gain)


def select_kernel(slot_ref, x_ref, c_ref, xs_ref, cs_ref):
    local, _, capacity, width = xs_ref.shape
    rows = x_ref.shape[1]
    place = jnp.concatenate(
        [
            (
                slot_ref[0, e : e + 1, :]
                == lax.broadcasted_iota(jnp.int32, (capacity, rows), 0)
            ).astype(F32)
            for e in range(local)
        ],
        axis=0,
    ).astype(BF)
    xs_ref[...] = dot_nn(place, x_ref[0]).astype(BF).reshape(xs_ref.shape)
    cs_ref[...] = dot_nn(place, c_ref[0]).astype(BF).reshape(cs_ref.shape)


def select_rows(slots, tokens, cots, capacity):
    blocks, local, rows = slots.shape
    width = tokens.shape[-1]
    block = pl.BlockSpec((1, rows, width), lambda b: (b, 0, 0))
    out = pl.BlockSpec((local, 1, capacity, width), lambda b: (0, b, 0, 0))
    shape = jax.ShapeDtypeStruct((local, blocks, capacity, width), BF)
    return pl.pallas_call(
        select_kernel,
        grid=(blocks,),
        in_specs=[pl.BlockSpec((1, local, rows), lambda b: (b, 0, 0)), block, block],
        out_specs=[out, out],
        out_shape=[shape, shape],
        compiler_params=params(),
        name="select_rows",
    )(slots, tokens, cots)


def expert_kernel(
    x_ref, c_ref, wg_ref, w_ref, gate_ref, out_ref, dx_ref, act_ref, dg_ref, du_ref, dgate_ref
):
    width = x_ref.shape[-1]
    x, c = x_ref[0], c_ref[0]
    w_gate = wg_ref[:, 0, 0].reshape(-1, width)
    w_up = w_ref[:, 0, 0].reshape(-1, width)
    w_down = w_ref[:, 1, 0].reshape(-1, width)
    gate = gate_ref[0]
    gate_pre = dot_nt(x, w_gate)
    up_pre = dot_nt(x, w_up)
    raw = dot_nt(c, w_down)
    sig = jax.nn.sigmoid(gate_pre)
    silu = gate_pre * sig
    act = silu * up_pre
    dgate_ref[0] = jnp.sum(act * raw, axis=-1, keepdims=True)
    act_low = (act * gate).astype(BF)
    d_act = raw * gate
    d_gate = (d_act * up_pre * sig * (1.0 + gate_pre * (1.0 - sig))).astype(BF)
    d_up = (d_act * silu).astype(BF)
    act_ref[0] = act_low
    dg_ref[0] = d_gate
    du_ref[0] = d_up
    out_ref[0] = dot_nn(act_low, w_down).astype(BF)
    dx_ref[0] = (dot_nn(d_gate, w_gate) + dot_nn(d_up, w_up)).astype(BF)


def experts_both_ways(x_slots, c_slots, w_gate_all, w_rest_all, slot_gate):
    local, number, width = x_slots.shape
    parts, _, _, hidden, _ = w_gate_all.shape
    tile = number // 2
    wide = pl.BlockSpec((1, tile, width), lambda e, i: (e, i, 0))
    mid = pl.BlockSpec((1, tile, parts * hidden), lambda e, i: (e, i, 0))
    thin = pl.BlockSpec((1, tile, 1), lambda e, i: (e, i, 0))
    wide_shape = jax.ShapeDtypeStruct((local, number, width), BF)
    mid_shape = jax.ShapeDtypeStruct((local, number, parts * hidden), BF)
    return pl.pallas_call(
        expert_kernel,
        grid=(local, 2),
        in_specs=[
            wide, wide,
            pl.BlockSpec((parts, 1, 1, hidden, width), lambda e, i: (0, 0, e, 0, 0)),
            pl.BlockSpec((parts, 2, 1, hidden, width), lambda e, i: (0, 0, e, 0, 0)),
            thin,
        ],
        out_specs=[wide, wide, mid, mid, mid, thin],
        out_shape=[
            wide_shape, wide_shape, mid_shape, mid_shape, mid_shape,
            jax.ShapeDtypeStruct((local, number, 1), F32),
        ],
        compiler_params=params(),
        name="experts_both_ways",
    )(x_slots, c_slots, w_gate_all, w_rest_all, slot_gate)


def expert_grads_kernel(x_ref, c_ref, act_ref, dg_ref, du_ref, first_ref, rest_ref):
    parts, _, _, hidden, width = first_ref.shape
    x, c = x_ref[0], c_ref[0]
    first_ref[:, 0, 0] = dot_tn(dg_ref[0], x).astype(BF).reshape(parts, hidden, width)
    rest_ref[:, 0, 0] = dot_tn(du_ref[0], x).astype(BF).reshape(parts, hidden, width)
    rest_ref[:, 1, 0] = dot_tn(act_ref[0], c).astype(BF).reshape(parts, hidden, width)


def expert_grads(x_slots, c_slots, act, d_gate, d_up, parts):
    local, number, width = x_slots.shape
    inner = act.shape[-1]
    wide = pl.BlockSpec((1, number, width), lambda e: (e, 0, 0))
    mid = pl.BlockSpec((1, number, inner), lambda e: (e, 0, 0))
    return pl.pallas_call(
        expert_grads_kernel,
        grid=(local,),
        in_specs=[wide, wide, mid, mid, mid],
        out_specs=[
            pl.BlockSpec((parts, kinds, 1, inner // parts, width), lambda e: (0, 0, e, 0, 0))
            for kinds in (1, 2)
        ],
        out_shape=[
            jax.ShapeDtypeStruct((parts, kinds, local, inner // parts, width), BF)
            for kinds in (1, 2)
        ],
        compiler_params=params(),
        name="expert_grads",
    )(x_slots, c_slots, act, d_gate, d_up)


def combine_kernel(first_ref, slot_ref, dx_ref, out_ref, dgate_ref, dx_sum_ref, out_sum_ref, pay_ref):
    local, _, capacity, width = dx_ref.shape
    rows = slot_ref.shape[1]
    lane = lax.broadcasted_iota(jnp.int32, (rows, local * capacity), 1)
    column = lax.broadcasted_iota(jnp.int32, (rows, pay_ref.shape[2] // 2), 1)
    total = jnp.zeros((rows, local * capacity), F32)
    pay = jnp.zeros(column.shape, F32)
    for e in range(local):
        hit = lane == slot_ref[0, :, e : e + 1] + e * capacity
        total = jnp.where(hit, 1.0, total)
        value = jnp.sum(jnp.where(hit, dgate_ref[0], 0.0), axis=1, keepdims=True)
        pay = jnp.where(column == first_ref[0, 0] + e, value, pay)
    place = total.astype(BF)
    dx_sum_ref[0] = dot_nn(place, dx_ref[...].reshape(-1, width)).astype(BF)
    out_sum_ref[0] = dot_nn(place, out_ref[...].reshape(-1, width)).astype(BF)
    high = pay.astype(BF)
    pay_ref[0] = jnp.concatenate([high, (pay - high.astype(F32)).astype(BF)], axis=1)


def combine_rows(first, slots_t, dx, out, d_gate_slots, experts):
    blocks, rows, local = slots_t.shape
    _, _, capacity, width = dx.shape
    lanes = -(-experts // 128) * 128
    slot = pl.BlockSpec((local, 1, capacity, width), lambda b: (0, b, 0, 0))
    block = pl.BlockSpec((1, rows, width), lambda b: (b, 0, 0))
    shape = jax.ShapeDtypeStruct((blocks, rows, width), BF)
    return pl.pallas_call(
        combine_kernel,
        grid=(blocks,),
        in_specs=[
            pl.BlockSpec(memory_space=pltpu.SMEM),
            pl.BlockSpec((1, rows, local), lambda b: (b, 0, 0)), slot, slot,
            pl.BlockSpec((1, 1, local * capacity), lambda b: (b, 0, 0)),
        ],
        out_specs=[block, block, pl.BlockSpec((1, rows, 2 * lanes), lambda b: (b, 0, 0))],
        out_shape=[shape, shape, jax.ShapeDtypeStruct((blocks, rows, 2 * lanes), BF)],
        compiler_params=params(),
        name="combine_rows",
    )(first, slots_t, dx, out, d_gate_slots)


def on_device(
    inputs,
    attn_gain,
    w_query,
    key_weight_matrix,
    value_weight_matrix,
    query_gain,
    key_gain,
    w_out,
    route_gain,
    w_router,
    w_gate,
    w_up,
    w_down,
    routes,
    image_starts,
    cotangent,
):
    tp_count = lax.axis_size("tp")
    ep_count = lax.axis_size("ep")
    tp_index = lax.axis_index("tp")
    ep_index = lax.axis_index("ep")
    length = inputs.shape[0]
    width = inputs.shape[1]
    rows = cotangent.shape[0]
    head_dim = query_gain.shape[0]
    local_experts = w_gate.shape[0]
    experts = local_experts * ep_count
    top = routes.shape[1]
    capacity = -(-(3 * rows * top // (2 * experts)) // 16) * 16

    w_gate_all = lax.all_gather(w_gate.transpose(0, 2, 1)[None], "tp")

    inputs_f = inputs.astype(F32)
    attn_scale = rms_scale(inputs_f)
    normed = (inputs_f * attn_scale * attn_gain).astype(BF)
    queries = dot_nn(normed, w_query)
    key_rows = dot_nn(normed, key_weight_matrix)
    values = dot_nn(normed, value_weight_matrix).astype(BF)
    cosine, sine = rope_tables(length, head_dim)
    q_gain, k_gain = query_gain[None], key_gain[None]
    heads, lse, attn_rows, cot_all = attention(
        image_starts, queries, key_rows, values, cosine, sine, q_gain, k_gain, w_out, cotangent, 0
    )
    attn_rows, w_rest = lax.optimization_barrier(
        (attn_rows, jnp.stack([w_up.transpose(0, 2, 1), w_down]))
    )
    w_rest_all = lax.all_gather(w_rest, "tp")
    x_rows = lax.dynamic_slice_in_dim(inputs, tp_index * rows, rows, 0).astype(F32)
    scale_rows = lax.dynamic_slice_in_dim(attn_scale, tp_index * rows, rows, 0)
    hidden = x_rows + attn_rows
    route_scale = rms_scale(hidden)
    moe_in = (hidden * route_scale * route_gain).astype(BF)
    moe_in, w_gate_all = lax.optimization_barrier((moe_in, w_gate_all))
    (tokens_all,) = gather_ep([moe_in], 1, "gather_rows")

    logits = dot_nn(moe_in, w_router)
    router_probs = plain_softmax(logits)
    expert_ids = jnp.arange(experts, dtype=jnp.int32)
    ring_routes = lax.dynamic_index_in_dim(
        routes.reshape(ep_count, tp_count, rows, top), tp_index, 1, keepdims=False
    )
    my_routes = lax.dynamic_index_in_dim(ring_routes, ep_index, 0, keepdims=False)

    def routed_softmax(scores, picked):
        kept = jnp.where(picked, scores, MASKED)
        expo = jnp.where(picked, jnp.exp(kept - jnp.max(kept, axis=-1, keepdims=True)), 0.0)
        return expo / jnp.sum(expo, axis=-1, keepdims=True)

    my_pick = jnp.any(my_routes[:, :, None] == expert_ids[None, None, :], axis=1)
    gates = routed_softmax(logits, my_pick)
    all_pick = jnp.any(ring_routes[..., None] == expert_ids, axis=2)
    gates_all = routed_softmax(dot_nn(tokens_all.reshape(-1, width), w_router).reshape(ep_count, rows, experts), all_pick)
    gate_of = lax.dynamic_slice_in_dim(gates_all, ep_index * local_experts, local_experts, 2)
    mask = lax.dynamic_slice_in_dim(all_pick, ep_index * local_experts, local_experts, 2)
    earlier = (jnp.arange(rows)[:, None] > jnp.arange(rows)[None, :]).astype(BF)
    slots_t = jnp.einsum(
        "tu,bue->bte", earlier, mask.astype(BF), preferred_element_type=F32
    ).astype(jnp.int32)
    slots_t = jnp.where(mask, slots_t, NOWHERE)
    slots = slots_t.transpose(0, 2, 1)
    place = slots[:, :, None, :] == jnp.arange(capacity, dtype=jnp.int32)[:, None]
    slot_gate = jnp.sum(jnp.where(place, gate_of.transpose(0, 2, 1)[:, :, None, :], 0.0), axis=-1)
    slot_gate = slot_gate.transpose(1, 0, 2).reshape(local_experts, ep_count * capacity, 1)

    x_slots, c_slots = select_rows(slots, tokens_all, cot_all, capacity)
    flat = (local_experts, ep_count * capacity, width)
    deep = (local_experts, ep_count, capacity, width)
    x_slots, c_slots = x_slots.reshape(flat), c_slots.reshape(flat)
    out_slots, dx_slots, act, d_gate, d_up, d_gate_slots = experts_both_ways(
        x_slots, c_slots, w_gate_all, w_rest_all, slot_gate
    )
    dx_part, out_part, gate_part = combine_rows(
        (ep_index * local_experts).reshape(1, 1),
        slots_t,
        dx_slots.reshape(deep),
        out_slots.reshape(deep),
        d_gate_slots.reshape(local_experts, ep_count, capacity)
        .transpose(1, 0, 2)
        .reshape(ep_count, 1, local_experts * capacity),
        experts,
    )
    first_grads, rest_grads = expert_grads(x_slots, c_slots, act, d_gate, d_up, tp_count)

    def over_rings(grads):
        return lax.psum_scatter(grads.reshape(-1, width), "tp", scatter_dimension=0, tiled=True)

    dx_part, first_grads, rest_grads = lax.optimization_barrier((dx_part, first_grads, rest_grads))
    first_mine = over_rings(first_grads)
    dx_mine, gate_mine = reduce_ep([dx_part, gate_part], [F32, F32], 2, "reduce_input_grads")
    dx_mine, first_mine, rest_grads, out_part = lax.optimization_barrier(
        (dx_mine, first_mine, rest_grads, out_part)
    )
    out_mine = lax.psum_scatter(out_part, "ep", scatter_dimension=0)
    first_mine = first_mine.astype(F32).reshape(local_experts, -1, width)
    lanes = gate_mine.shape[1] // 2
    d_gates = gate_mine[:, :experts] + gate_mine[:, lanes : lanes + experts]
    w_gate_grad = first_mine.transpose(0, 2, 1)

    counts = jnp.sum((routes[:, :, None] == expert_ids[None, None, :]).astype(F32), axis=(0, 1))
    total_tokens = routes.shape[0]
    share = counts / (total_tokens * top)
    coeff = AUX * experts * share
    prob_local = jnp.sum(router_probs, axis=0)
    cot = cotangent.astype(F32)
    d_logits = gates * (d_gates - jnp.sum(gates * d_gates, axis=-1, keepdims=True))
    d_logits = d_logits + router_probs * (
        coeff - jnp.sum(router_probs * coeff, axis=-1, keepdims=True)
    )
    d_logits_low = d_logits.astype(BF)
    router_part = dot_tn(moe_in, d_logits_low)
    d_moe = dot_nt(d_logits_low, w_router) + dx_mine
    d_hidden, route_gain_part = norm_back(d_moe, hidden, route_gain[None])
    d_hidden = d_hidden + cot

    d_branch = gather_tp(d_hidden.astype(BF), 3, "gather_branch")
    d_heads = dot_nt(d_branch, w_out).astype(BF)
    d_queries, d_keys, d_values, query_gain_part, key_gain_part = attention_back(
        image_starts, queries, key_rows, values, d_heads, lse, cosine, sine, q_gain, k_gain
    )
    d_queries, out_mine, rest_grads = lax.optimization_barrier((d_queries, out_mine, rest_grads))
    rest_mine = over_rings(rest_grads).astype(F32).reshape(2, local_experts, -1, width)
    w_up_grad = rest_mine[0].transpose(0, 2, 1)
    w_down_grad = rest_mine[1]
    output = (hidden + out_mine.astype(F32)).astype(BF)
    w_out_part = dot_tn(d_branch, heads)
    w_query_part = dot_tn(normed, d_queries)
    w_key_part = dot_tn(normed, d_keys)
    w_value_part = dot_tn(normed, d_values)
    d_normed = (
        dot_nt(d_queries, w_query)
        + dot_nt(d_keys, key_weight_matrix)
        + dot_nt(d_values, value_weight_matrix)
    )
    d_mine = reduce_tp(d_normed.astype(BF), 4, "reduce_normed")
    attn_gain_part = jnp.sum(d_mine * x_rows * scale_rows, axis=0)
    inner = d_mine * attn_gain
    inputs_grad = (
        d_hidden
        + scale_rows * inner
        - x_rows * scale_rows**3 * jnp.mean(inner * x_rows, axis=-1, keepdims=True)
    )
    small = sum_all(
        [
            router_part,
            attn_gain_part,
            route_gain_part[0],
            query_gain_part[0],
            key_gain_part[0],
            prob_local,
        ],
        5,
        "sum_small",
    )
    w_router_grad, attn_gain_grad, route_gain_grad, query_gain_grad, key_gain_grad, prob_all = small

    def by_rows(part):
        return part.astype(BF).reshape(ep_count, -1, part.shape[1])

    w_query_grad, w_key_grad, w_value_grad, w_out_grad = reduce_ep(
        [by_rows(w_query_part), by_rows(w_key_part), by_rows(w_value_part), by_rows(w_out_part)],
        [F32] * 4,
        6,
        "reduce_projection_grads",
    )
    w_out_grad = w_out_grad.T
    aux_loss = experts * jnp.sum(share * (prob_all / total_tokens))
    return (
        output,
        aux_loss,
        inputs_grad,
        attn_gain_grad,
        w_query_grad,
        w_key_grad,
        w_value_grad,
        query_gain_grad,
        key_gain_grad,
        w_out_grad,
        route_gain_grad,
        w_router_grad,
        w_gate_grad,
        w_up_grad,
        w_down_grad,
    )


def solution(mesh):
    return jax.shard_map(
        on_device,
        mesh=mesh,
        in_specs=(
            P("ep", None),
            P(),
            P(None, "tp"),
            P(None, "tp"),
            P(None, "tp"),
            P(),
            P(),
            P("tp", None),
            P(),
            P(),
            P("ep", None, "tp"),
            P("ep", None, "tp"),
            P("ep", "tp", None),
            P(),
            P("ep", None),
            P(("ep", "tp"), None),
        ),
        out_specs=(
            P(("ep", "tp"), None),
            P(),
            P(("ep", "tp"), None),
            P(),
            P("ep", "tp"),
            P("ep", "tp"),
            P("ep", "tp"),
            P(),
            P(),
            P("tp", "ep"),
            P(),
            P(),
            P("ep", None, "tp"),
            P("ep", None, "tp"),
            P("ep", "tp", None),
        ),
        check_vma=False,
    )
```

```python
import functools

import jax
import jax.numpy as jnp
from jax import lax
from jax.experimental import pallas as pl
from jax.experimental.pallas import tpu as pltpu
from jax.sharding import PartitionSpec as P

IMG = 256
EPS = 1e-06
AUX = 0.04
THETA = 1000000.0
MASKED = -1e30
NOWHERE = -(1 << 20)
BF = jnp.bfloat16
F32 = jnp.float32
VMEM_BYTES = 60 * 1024 * 1024


def dot_nn(a, b):
    return lax.dot_general(a, b, (((1,), (0,)), ((), ())), preferred_element_type=F32)


def dot_nt(a, b):
    return lax.dot_general(a, b, (((1,), (1,)), ((), ())), preferred_element_type=F32)


def dot_tn(a, b):
    return lax.dot_general(a, b, (((0,), (0,)), ((), ())), preferred_element_type=F32)


def params(**kw):
    return pltpu.CompilerParams(vmem_limit_bytes=VMEM_BYTES, **kw)


def rms_scale(value_rows):
    return lax.rsqrt(jnp.mean(value_rows * value_rows, axis=-1, keepdims=True) + EPS)


def plain_softmax(value_rows):
    top = jnp.max(value_rows, axis=-1, keepdims=True)
    expo = jnp.exp(value_rows - top)
    return expo / jnp.sum(expo, axis=-1, keepdims=True)


def rope_tables(length, size):
    half = size // 2
    freq = jnp.exp(-jnp.log(THETA) * (2.0 * jnp.arange(half, dtype=F32)) / size)
    angle = jnp.arange(length, dtype=F32)[:, None] * freq[None, :]
    cosine = jnp.cos(angle)
    sine = jnp.sin(angle)
    return (jnp.concatenate([cosine, cosine], axis=-1), jnp.concatenate([-sine, sine], axis=-1))


def turn(rows, cosine, sine):
    return rows * cosine + pltpu.roll(rows, rows.shape[-1] // 2, 1) * sine


def turn_back(rows, cosine, sine):
    return rows * cosine - pltpu.roll(rows, rows.shape[-1] // 2, 1) * sine


MESH = pl.DeviceIdType.MESH
ANY = pl.BlockSpec(memory_space=pl.ANY)
Z_AXIS = 4


def link_cost(us):
    return pl.CostEstimate(flops=0, bytes_accessed=int(us * 3.0e6), transcendentals=0)


def greet(partners):
    barrier = pltpu.get_barrier_semaphore()
    count = 0
    for there, device in partners:
        flag = jnp.asarray(there, jnp.int32)

        @pl.when(there)
        def _(device=device):
            pl.semaphore_signal(barrier, inc=1, device_id=device, device_id_type=MESH)

        count = count + flag
    pl.semaphore_wait(barrier, count)


def remote(src, dst, send, recv, device):
    return pltpu.make_async_remote_copy(
        src_ref=src, dst_ref=dst, send_sem=send, recv_sem=recv, device_id=device, device_id_type=MESH
    )


def ring_place():
    me = lax.axis_index("ep")
    z, y = me // 2, me % 2
    return me, z, y, {"ep": me + 2}, {"ep": me - 2}, {"ep": me + 1 - 2 * y}


class EpGather:
    def __init__(self, ins, outs, sems):
        self.ins, self.outs = ins, outs
        self.own_sem, self.up_send, self.up_recv, self.dn_send, self.dn_recv = sems[:5]
        self.y_send, self.y_recv = sems[5:]
        self.me, self.z, self.y, self.up, self.down, self.beside = ring_place()

    def partners(self):
        z = self.z
        return [(z < Z_AXIS - 1, self.up), (z > 0, self.down), (z >= 0, self.beside)]

    def block(self, a, zt):
        return self.outs[a].at[zt * 2 + self.y]

    def upward(self, src, a, zt):
        return remote(src, self.block(a, zt), self.up_send.at[a, zt], self.up_recv.at[a, zt], self.up)

    def downward(self, src, a, zt):
        return remote(src, self.block(a, zt), self.dn_send.at[a, zt], self.dn_recv.at[a, zt], self.down)

    def sideways(self, src, a, zt):
        return remote(src, self.block(a, zt), self.y_send.at[a, zt], self.y_recv.at[a, zt], self.beside)

    def start(self):
        z = self.z
        for a, x in enumerate(self.ins):

            @pl.when(z < Z_AXIS - 1)
            def _(a=a, x=x):
                self.upward(x, a, z).start()

            @pl.when(z > 0)
            def _(a=a, x=x):
                self.downward(x, a, z).start()

            self.sideways(x, a, z).start()
            pltpu.make_async_copy(x, self.block(a, z), self.own_sem.at[a]).start()

    def hop(self, d):
        z = self.z
        for a in range(len(self.ins)):

            @pl.when(z >= d)
            def _(a=a, zt=z - d):
                self.upward(self.block(a, zt), a, zt).wait_recv()

                @pl.when(z < Z_AXIS - 1)
                def _():
                    self.upward(self.block(a, zt), a, zt).start()

                self.sideways(self.block(a, zt), a, zt).start()

            @pl.when(z + d < Z_AXIS)
            def _(a=a, zt=z + d):
                self.downward(self.block(a, zt), a, zt).wait_recv()

                @pl.when(z > 0)
                def _():
                    self.downward(self.block(a, zt), a, zt).start()

                self.sideways(self.block(a, zt), a, zt).start()

    def own_done(self, a):
        pltpu.make_async_copy(self.ins[a], self.block(a, self.z), self.own_sem.at[a]).wait()

    def side_done(self, a, zt):
        other = self.outs[a].at[zt * 2 + 1 - self.y]
        remote(other, other, self.y_send.at[a, zt], self.y_recv.at[a, zt], self.beside).wait_recv()

    def sent(self, a):
        z = self.z
        for zt in range(Z_AXIS):
            src = self.block(a, zt)
            self.sideways(src, a, zt).wait_send()

            @pl.when((zt <= z) & (z < Z_AXIS - 1))
            def _(src=src, zt=zt):
                self.upward(src, a, zt).wait_send()

            @pl.when((zt >= z) & (z > 0))
            def _(src=src, zt=zt):
                self.downward(src, a, zt).wait_send()

    def finish(self):
        for a in range(len(self.ins)):
            self.own_done(a)
            for zt in range(Z_AXIS):
                self.side_done(a, zt)
            self.sent(a)


def gather_sems(count):
    dma = pltpu.SemaphoreType.DMA
    return [dma((count,))] + [dma((count, Z_AXIS))] * 6


def gather_ep_kernel(number, *refs):
    gather = EpGather(refs[:number], refs[number : 2 * number], refs[2 * number :])
    greet(gather.partners())
    gather.start()
    for d in range(1, Z_AXIS):
        gather.hop(d)
    gather.finish()


def gather_ep(arrays, number, name):
    count = len(arrays)
    ep_count = lax.axis_size("ep")
    if ep_count != 2 * Z_AXIS:
        return [lax.all_gather(a, "ep") for a in arrays]
    return pl.pallas_call(
        functools.partial(gather_ep_kernel, count),
        in_specs=[ANY] * count,
        out_specs=[ANY] * count,
        out_shape=[jax.ShapeDtypeStruct((ep_count,) + a.shape, a.dtype) for a in arrays],
        scratch_shapes=gather_sems(count),
        compiler_params=params(collective_id=number, has_side_effects=True),
        cost_estimate=link_cost(80.0 * count),
        name=name,
    )(*arrays)


def add_rows(total, terms, chunk=32):
    @pl.loop(0, total.shape[0] // chunk)
    def _(i):
        rows = pl.ds(pl.multiple_of(i * chunk, chunk), chunk)
        value = terms[0][rows, :].astype(F32)
        for term in terms[1:]:
            value = value + term[rows, :].astype(F32)
        total[rows, :] = value.astype(total.dtype)


def scatter_order(z):
    table = ((3, 2, 1, 0), (3, 0, 2, 1), (0, 3, 1, 2), (0, 1, 2, 3))
    return [
        jnp.where(
            z == 0,
            table[0][k],
            jnp.where(z == 1, table[1][k], jnp.where(z == 2, table[2][k], table[3][k])),
        )
        for k in range(Z_AXIS)
    ]


class EpReduce:
    def __init__(self, ins, bufs, sems, loaded=True):
        self.ins, self.loaded = ins, loaded
        each = 3 if loaded else 2
        self.bufs = [bufs[each * a : each * a + each] for a in range(len(ins))]
        self.own_sem, self.up_send, self.up_recv, self.dn_send, self.dn_recv = sems[:5]
        self.y_send, self.y_recv = sems[5:]
        self.me, self.z, self.y, self.up, self.down, self.beside = ring_place()
        self.order = scatter_order(self.z)

    def partners(self):
        z = self.z
        return [(z < Z_AXIS - 1, self.up), (z > 0, self.down), (z >= 0, self.beside)]

    def mine(self, a, zt):
        return self.bufs[a][0].at[zt] if self.loaded else self.ins[a].at[zt * 2 + self.y]

    def side(self, a, zt):
        return self.bufs[a][-2].at[zt]

    def below(self, a, zt):
        return self.bufs[a][-1].at[zt]

    def above(self, a, zt, z):
        return self.bufs[a][-1].at[jnp.where(zt == z, Z_AXIS, zt)]

    def to_side(self, a, zt):
        src = self.ins[a].at[zt * 2 + 1 - self.y]
        return remote(src, self.side(a, zt), self.y_send.at[a, zt], self.y_recv.at[a, zt], self.beside)

    def load(self, a, zt):
        return pltpu.make_async_copy(
            self.ins[a].at[zt * 2 + self.y], self.mine(a, zt), self.own_sem.at[a, zt]
        )

    def rising(self, a, zt):
        return remote(
            self.mine(a, zt), self.below(a, zt), self.up_send.at[a, zt], self.up_recv.at[a, zt], self.up
        )

    def falling(self, a, zt):
        return remote(
            self.mine(a, zt), self.above(a, zt, self.z - 1),
            self.dn_send.at[a, zt], self.dn_recv.at[a, zt], self.down,
        )

    def send_side(self, k):
        for a in range(len(self.ins)):
            self.to_side(a, self.order[k]).start()
            if self.loaded:
                self.load(a, self.order[k]).start()

    def step(self, k):
        z, zt, last = self.z, self.order[k], Z_AXIS - 1
        for a in range(len(self.ins)):
            mine, side = self.mine(a, zt), self.side(a, zt)
            if self.loaded:
                self.load(a, zt).wait()
            self.to_side(a, zt).wait_recv()

            @pl.when(((zt > z) & (z == 0)) | ((zt < z) & (z == last)))
            def _(mine=mine, side=side):
                add_rows(mine, [mine, side])

            @pl.when((zt > z) & (z > 0))
            def _(a=a, mine=mine, side=side):
                self.rising(a, zt).wait_recv()
                add_rows(mine, [mine, side, self.below(a, zt)])

            @pl.when((zt < z) & (z < last))
            def _(a=a, mine=mine, side=side):
                self.falling(a, zt).wait_recv()
                add_rows(mine, [mine, side, self.above(a, zt, z)])

            @pl.when(zt > z)
            def _(a=a):
                self.rising(a, zt).start()

            @pl.when(zt < z)
            def _(a=a):
                self.falling(a, zt).start()

    def own(self, a, write):
        z, last = self.z, Z_AXIS - 1
        pair = [self.mine(a, z), self.side(a, z)]

        @pl.when(z > 0)
        def _():
            self.rising(a, z).wait_recv()

        @pl.when(z < last)
        def _():
            self.falling(a, z).wait_recv()

        @pl.when(z == 0)
        def _():
            write(pair + [self.above(a, z, z)])

        @pl.when(z == last)
        def _():
            write(pair + [self.below(a, z)])

        @pl.when((z > 0) & (z < last))
        def _():
            write(pair + [self.below(a, z), self.above(a, z, z)])

    def sent(self):
        z = self.z
        for a in range(len(self.ins)):
            for zt in range(Z_AXIS):
                self.to_side(a, zt).wait_send()

                @pl.when(zt > z)
                def _(a=a, zt=zt):
                    self.rising(a, zt).wait_send()

                @pl.when(zt < z)
                def _(a=a, zt=zt):
                    self.falling(a, zt).wait_send()


def reduce_scratch(shape, dtype, loaded=True):
    counts = ([Z_AXIS] if loaded else []) + [Z_AXIS, Z_AXIS + 1]
    return [pltpu.VMEM((n,) + tuple(shape), dtype) for n in counts]


def reduce_sems(count):
    return [pltpu.SemaphoreType.DMA((count, Z_AXIS))] * 7


def reduce_ep_kernel(number, *refs):
    ins, outs = refs[:number], refs[number : 2 * number]
    reduce = EpReduce(ins, refs[2 * number : 5 * number], refs[5 * number :])
    greet(reduce.partners())
    for k in range(Z_AXIS):
        reduce.send_side(k)
    for k in range(Z_AXIS):
        reduce.step(k)
    for a, out in enumerate(outs):
        reduce.own(a, functools.partial(add_rows, out))
    reduce.sent()


def reduce_ep(parts, dtypes, number, name):
    count = len(parts)
    ep_count = lax.axis_size("ep")
    if ep_count != 2 * Z_AXIS:
        return [
            lax.psum_scatter(p, "ep", scatter_dimension=0).astype(t) for p, t in zip(parts, dtypes)
        ]
    scratch = []
    for p in parts:
        scratch += reduce_scratch(p.shape[1:], BF)
    return pl.pallas_call(
        functools.partial(reduce_ep_kernel, count),
        in_specs=[ANY] * count,
        out_specs=[pl.BlockSpec(memory_space=pltpu.VMEM)] * count,
        out_shape=[jax.ShapeDtypeStruct(p.shape[1:], t) for p, t in zip(parts, dtypes)],
        scratch_shapes=scratch + reduce_sems(count),
        compiler_params=params(collective_id=number, has_side_effects=True),
        cost_estimate=link_cost(80.0 * sum(p.size for p in parts) / 2**22),
        name=name,
    )(*parts)


class SumAll:
    def __init__(self, x, out, parts, own, send, recv, back_send, back_recv):
        self.x, self.out, self.parts, self.own = x, out, parts, own
        self.send, self.recv, self.back_send, self.back_recv = send, recv, back_send, back_recv
        self.tp_count = lax.axis_size("tp")
        self.total = lax.axis_size("ep") * self.tp_count
        self.me = lax.axis_index("ep") * self.tp_count + lax.axis_index("tp")

    def device(self, d):
        return {"ep": d // self.tp_count, "tp": d % self.tp_count}

    def other(self, i):
        return lax.rem(self.me + i, self.total)

    def each(self, act):
        @pl.loop(1, self.total)
        def _(i):
            act(i)

    def greet(self):
        barrier = pltpu.get_barrier_semaphore()
        self.each(
            lambda i: pl.semaphore_signal(
                barrier, inc=1, device_id=self.device(self.other(i)), device_id_type=MESH
            )
        )
        pl.semaphore_wait(barrier, self.total - 1)

    def outward(self, i):
        to = self.other(i)
        return remote(
            self.x.at[to], self.parts.at[self.me], self.send.at[i], self.recv.at[self.me], self.device(to)
        )

    def inward(self, i):
        origin = self.other(i)
        rows = self.parts.at[origin]
        return remote(rows, rows, self.send.at[i], self.recv.at[origin], self.device(origin))

    def spread(self, i):
        to = self.other(i)
        return remote(
            self.own, self.out.at[self.me], self.back_send.at[i], self.back_recv.at[self.me], self.device(to)
        )

    def returned(self, i):
        origin = self.other(i)
        rows = self.out.at[origin]
        return remote(rows, rows, self.back_send.at[i], self.back_recv.at[origin], self.device(origin))

    def start(self):
        self.each(lambda i: self.outward(i).start())
        self.parts[pl.ds(self.me, 1)] = self.x[pl.ds(self.me, 1)]

    def add(self):
        self.each(lambda i: self.inward(i).wait_recv())
        self.own[...] = jnp.sum(self.parts[...], axis=0)
        self.each(lambda i: self.spread(i).start())
        self.out[pl.ds(self.me, 1)] = self.own[...][None]

    def finish(self):
        self.each(lambda i: self.outward(i).wait_send())
        self.each(lambda i: self.returned(i).wait_recv())
        self.each(lambda i: self.spread(i).wait_send())


def sum_scratch(rows, total):
    dma = pltpu.SemaphoreType.DMA
    return [
        pltpu.VMEM((total, rows, 128), F32), pltpu.VMEM((rows, 128), F32),
        dma((total,)), dma((total,)), dma((total,)), dma((total,)),
    ]


def pack_small(values, total):
    flat = jnp.concatenate([v.reshape(-1) for v in values])
    rows = -(-flat.shape[0] // (total * 128 * 8)) * 8
    return jnp.pad(flat, (0, total * rows * 128 - flat.shape[0])).reshape(total, rows, 128)


def unpack_small(summed, values):
    summed = summed.reshape(-1)
    out, at = [], 0
    for v in values:
        out.append(summed[at : at + v.size].reshape(v.shape))
        at += v.size
    return out


def fill_bias(span_ref, bias, chunk=256):
    keys, length = bias.shape
    query = lax.broadcasted_iota(jnp.int32, (1, length), 1)

    def spans(pos):
        first = (pos >= span_ref[0, 0]) & (pos < span_ref[0, 0] + IMG)
        second = (pos >= span_ref[0, 1]) & (pos < span_ref[0, 1] + IMG)
        return jnp.where(first, 0, jnp.where(second, 1, -1))

    query_span = spans(query)
    query_other = jnp.where(query_span < 0, -2, query_span)
    for start in range(0, keys, chunk):
        key = start + lax.broadcasted_iota(jnp.int32, (chunk, 1), 0)
        ok = (key <= query) | (spans(key) == query_other)
        bias[start : start + chunk, :] = jnp.where(ok, 0.0, MASKED)


def query_tiles(length):
    tile = min(IMG, length)
    return [
        (start, tile, min(length, start + tile + -(-IMG // tile) * tile))
        for start in range(0, length, tile)
    ]


def attention_kernel(
    span_ref, q_ref, k_ref, v_ref, cos_ref, sin_ref, qg_ref, kg_ref, w_out_ref, cot_ref,
    out_ref, lse_ref, rows_ref, cots_ref,
    bias, k_rot, v_t, heads, part, core_rows, x_rows, core_send, core_recv, x_send, x_recv, *sems,
):
    factor = q_ref.shape[-1] ** (-0.5)
    cosine, sine = cos_ref[...], sin_ref[...]
    step = pl.program_id(0)
    size = q_ref.shape[-1]
    me = lax.axis_index("tp")
    x, c = me // 2, me % 2
    other_core, other_x = {"tp": x * 2 + 1 - c}, {"tp": (1 - x) * 2 + c}
    gather = EpGather([cot_ref], [cots_ref], sems)

    @pl.when(step == 0)
    def _():
        greet(gather.partners() + [(x >= 0, other_core), (x >= 0, other_x)])
        gather.start()
        fill_bias(span_ref, bias)
        k = k_ref[...]
        k_rot[...] = turn(k * rms_scale(k) * kg_ref[...], cosine, sine).astype(BF)
        v_t[...] = v_ref[...].astype(F32).T.astype(BF)

    q = q_ref[...]
    q_rot = turn(q * rms_scale(q) * qg_ref[...], cosine, sine).astype(BF)
    for start, tile, keys in query_tiles(q.shape[0]):
        cols = slice(start, start + tile)
        s = dot_nt(k_rot[:keys, :], q_rot[cols, :]) * factor + bias[:keys, cols]
        top = jnp.max(s, axis=0, keepdims=True)
        p = jnp.exp(s - top)
        total = jnp.sum(p, axis=0, keepdims=True)
        o_t = dot_nn(v_t[:, :keys], p.astype(BF)) / total
        rows = o_t.T.astype(BF)
        out_ref[cols, :] = rows
        heads[step, cols, :] = rows
        lse_ref[0, :, cols] = top + jnp.log(total)

    @pl.when(step == pl.num_programs(0) - 1)
    def _():
        count = heads.shape[0]
        block = rows_ref.shape[0]

        def project(tp):
            lines = pl.ds(pl.multiple_of(tp * block, block), block)
            rows = jnp.concatenate([heads[h, lines, :] for h in range(count)], axis=1)
            part[tp] = dot_nn(rows, w_out_ref[...]).astype(BF)

        def to_core(xt):
            return remote(
                part.at[xt * 2 + 1 - c], core_rows.at[xt],
                core_send.at[xt], core_recv.at[xt], other_core,
            )

        far, near = part.at[(1 - x) * 2 + c], part.at[x * 2 + c]
        to_x = remote(far, x_rows, x_send, x_recv, other_x)
        gather.hop(1)
        project((1 - x) * 2 + 1 - c)
        to_core(1 - x).start()
        project((1 - x) * 2 + c)
        to_core(1 - x).wait_recv()
        add_rows(far, [far, core_rows.at[1 - x]])
        to_x.start()
        project(x * 2 + 1 - c)
        to_core(x).start()
        project(x * 2 + c)
        gather.hop(2)
        to_core(x).wait_recv()
        gather.hop(3)
        to_x.wait_recv()
        add_rows(rows_ref, [near, core_rows.at[x], x_rows])
        gather.finish()
        to_core(1 - x).wait_send()
        to_core(x).wait_send()
        to_x.wait_send()


def plain_attention_kernel(
    span_ref, q_ref, k_ref, v_ref, cos_ref, sin_ref, qg_ref, kg_ref, out_ref, lse_ref,
    bias, k_rot, v_t,
):
    factor = q_ref.shape[-1] ** (-0.5)
    cosine, sine = cos_ref[...], sin_ref[...]

    @pl.when(pl.program_id(0) == 0)
    def _():
        fill_bias(span_ref, bias)
        k = k_ref[...]
        k_rot[...] = turn(k * rms_scale(k) * kg_ref[...], cosine, sine).astype(BF)
        v_t[...] = v_ref[...].astype(F32).T.astype(BF)

    q = q_ref[...]
    q_rot = turn(q * rms_scale(q) * qg_ref[...], cosine, sine).astype(BF)
    for start, tile, keys in query_tiles(q.shape[0]):
        cols = slice(start, start + tile)
        s = dot_nt(k_rot[:keys, :], q_rot[cols, :]) * factor + bias[:keys, cols]
        top = jnp.max(s, axis=0, keepdims=True)
        p = jnp.exp(s - top)
        total = jnp.sum(p, axis=0, keepdims=True)
        o_t = dot_nn(v_t[:, :keys], p.astype(BF)) / total
        out_ref[cols, :] = o_t.T.astype(BF)
        lse_ref[0, :, cols] = top + jnp.log(total)


def attention(span, q, k, v, cosine, sine, q_gain, k_gain, w_out, cotangent, number):
    length, size = k.shape
    heads = q.shape[1] // size
    whole = pl.BlockSpec((length, size), lambda h: (0, 0))
    head = pl.BlockSpec((length, size), lambda h: (0, h))
    gain = pl.BlockSpec((1, size), lambda h: (0, 0))
    in_specs = [
        pl.BlockSpec(memory_space=pltpu.SMEM), head, whole, whole, whole, whole, gain, gain,
    ]
    out_specs = [head, pl.BlockSpec((1, 1, length), lambda h: (h, 0, 0))]
    out_shape = [
        jax.ShapeDtypeStruct((length, heads * size), BF),
        jax.ShapeDtypeStruct((heads, 1, length), F32),
    ]
    scratch = [
        pltpu.VMEM((length, length), F32),
        pltpu.VMEM((length, size), BF),
        pltpu.VMEM((size, length), BF),
    ]
    args = (span, q, k, v, cosine, sine, q_gain, k_gain)
    ep_count, tp_count = lax.axis_size("ep"), lax.axis_size("tp")
    if ep_count != 2 * Z_AXIS:
        out, lse = pl.pallas_call(
            plain_attention_kernel,
            grid=(heads,),
            in_specs=in_specs,
            out_specs=out_specs,
            out_shape=out_shape,
            scratch_shapes=scratch,
            compiler_params=params(),
            name="plain_attention",
        )(*args)
        rows = lax.psum_scatter(
            dot_nn(out, w_out).astype(BF), "tp", scatter_dimension=0, tiled=True
        )
        return out, lse, rows.astype(F32), lax.all_gather(cotangent, "ep")
    block, width = cotangent.shape
    dma = pltpu.SemaphoreType.DMA
    return pl.pallas_call(
        attention_kernel,
        grid=(heads,),
        in_specs=in_specs + [pl.BlockSpec(w_out.shape, lambda h: (0, 0)), ANY],
        out_specs=out_specs + [pl.BlockSpec((block, width), lambda h: (0, 0)), ANY],
        out_shape=out_shape
        + [
            jax.ShapeDtypeStruct((block, width), F32),
            jax.ShapeDtypeStruct((ep_count, block, width), BF),
        ],
        scratch_shapes=scratch
        + [
            pltpu.VMEM((heads, length, size), BF),
            pltpu.VMEM((tp_count, block, width), BF),
            pltpu.VMEM((2, block, width), BF),
            pltpu.VMEM((block, width), BF),
            dma((2,)), dma((2,)), dma, dma,
        ]
        + gather_sems(1),
        compiler_params=params(collective_id=number, has_side_effects=True),
        cost_estimate=link_cost(90.0),
        name="attention",
    )(*args, w_out, cotangent)


def norm_back(grads, rows, gain):
    scale = rms_scale(rows)
    gain_part = jnp.sum(grads * rows * scale, axis=0, keepdims=True)
    inner = grads * gain
    mean = jnp.mean(inner * rows, axis=-1, keepdims=True)
    return scale * inner - rows * (scale * scale * scale * mean), gain_part


def plain_attention_back_kernel(
    span_ref, q_ref, k_ref, v_ref, grad_ref, lse_ref, cos_ref, sin_ref, qg_ref, kg_ref,
    dq_ref, dk_ref, dv_ref, dqg_ref, dkg_ref,
    bias, k_rot, k_t, dk_acc, dv_acc, dq_t,
):
    factor = q_ref.shape[-1] ** (-0.5)
    cosine, sine = cos_ref[...], sin_ref[...]
    step = pl.program_id(0)

    @pl.when(step == 0)
    def _():
        fill_bias(span_ref, bias)
        k = k_ref[...]
        rotated = turn(k * rms_scale(k) * kg_ref[...], cosine, sine)
        k_rot[...] = rotated.astype(BF)
        k_t[...] = rotated.T.astype(BF)
        dk_acc[...] = jnp.zeros_like(dk_acc)
        dv_acc[...] = jnp.zeros_like(dv_acc)
        dqg_ref[...] = jnp.zeros_like(dqg_ref)

    q = q_ref[...]
    q_rot = turn(q * rms_scale(q) * qg_ref[...], cosine, sine).astype(BF)
    for start, tile, keys in query_tiles(q.shape[0]):
        cols = slice(start, start + tile)
        s = dot_nt(k_rot[:keys, :], q_rot[cols, :]) * factor + bias[:keys, cols]
        p = jnp.exp(s - lse_ref[0, :, cols])
        grad = grad_ref[cols, :]
        dp = dot_nt(v_ref[:keys, :], grad)
        mean = jnp.sum(p * dp, axis=0, keepdims=True)
        raw = (p * (dp - mean) * factor).astype(BF)
        dq_t[:, cols] = dot_nn(k_t[:, :keys], raw)
        dk_acc[:keys, :] += dot_nn(raw, q_rot[cols, :])
        dv_acc[:keys, :] += dot_nn(p.astype(BF), grad)
    back, gain_part = norm_back(turn_back(dq_t[...].T, cosine, sine), q, qg_ref[...])
    dq_ref[...] = back.astype(BF)
    dqg_ref[...] += gain_part

    @pl.when(step == pl.num_programs(0) - 1)
    def _():
        back, gain_part = norm_back(turn_back(dk_acc[...], cosine, sine), k_ref[...], kg_ref[...])
        dk_ref[...] = back.astype(BF)
        dkg_ref[...] = gain_part
        dv_ref[...] = dv_acc[...].astype(BF)


def plain_attention_back(span, q, k, v, grads, lse, cosine, sine, q_gain, k_gain):
    length, size = k.shape
    heads = q.shape[1] // size
    whole = pl.BlockSpec((length, size), lambda h: (0, 0))
    head = pl.BlockSpec((length, size), lambda h: (0, h))
    gain = pl.BlockSpec((1, size), lambda h: (0, 0))
    return pl.pallas_call(
        plain_attention_back_kernel,
        grid=(heads,),
        in_specs=[
            pl.BlockSpec(memory_space=pltpu.SMEM), head, whole, whole, head,
            pl.BlockSpec((1, 1, length), lambda h: (h, 0, 0)), whole, whole, gain, gain,
        ],
        out_specs=[head, whole, whole, gain, gain],
        out_shape=[
            jax.ShapeDtypeStruct((length, heads * size), BF),
            jax.ShapeDtypeStruct((length, size), BF),
            jax.ShapeDtypeStruct((length, size), BF),
            jax.ShapeDtypeStruct((1, size), F32),
            jax.ShapeDtypeStruct((1, size), F32),
        ],
        scratch_shapes=[
            pltpu.VMEM((length, length), F32),
            pltpu.VMEM((length, size), BF),
            pltpu.VMEM((size, length), BF),
            pltpu.VMEM((length, size), F32),
            pltpu.VMEM((length, size), F32),
            pltpu.VMEM((size, length), F32),
        ],
        compiler_params=params(),
        name="plain_attention_back",
    )(span, q, k, v, grads, lse, cosine, sine, q_gain, k_gain)


def attention_back_kernel(
    span_ref, q_ref, k_ref, v_ref, lse_ref, cos_ref, sin_ref, qg_ref, kg_ref,
    w_out_ref, rows_ref, part_ref, hidden_ref,
    dq_ref, dk_ref, dv_ref, dqg_ref, dkg_ref, branch_ref, output_ref,
    bias, k_rot, k_t, dk_acc, dv_acc, dq_t, branch, grads, mine, side, along,
    own_sem, out_sem, core_send, core_recv, x_send, x_recv, *sems,
):
    factor = q_ref.shape[-1] ** (-0.5)
    size = q_ref.shape[-1]
    cosine, sine = cos_ref[...], sin_ref[...]
    step = pl.program_id(0)
    me = lax.axis_index("tp")
    x, c = me // 2, me % 2
    other_core, other_x = {"tp": x * 2 + 1 - c}, {"tp": (1 - x) * 2 + c}
    reduce = EpReduce([part_ref], [mine, side, along], sems)
    block = rows_ref.shape[0]
    near_other, far, far_other = x * 2 + 1 - c, (1 - x) * 2 + c, (1 - x) * 2 + 1 - c

    def to_core(slot, src, tp):
        return remote(src, branch.at[tp], core_send.at[slot], core_recv.at[slot], other_core)

    def to_x(tp):
        return remote(rows_ref, branch.at[tp], x_send, x_recv, other_x)

    def own_rows():
        return pltpu.make_async_copy(rows_ref, branch.at[me], own_sem)

    def whole_branch():
        return pltpu.make_async_copy(branch, branch_ref, out_sem)

    @pl.when(step == 0)
    def _():
        greet(reduce.partners() + [(x >= 0, other_core), (x >= 0, other_x)])
        to_x(me).start()
        to_core(0, rows_ref, me).start()
        own_rows().start()
        for k in range(Z_AXIS):
            reduce.send_side(k)
        fill_bias(span_ref, bias)
        k = k_ref[...]
        rotated = turn(k * rms_scale(k) * kg_ref[...], cosine, sine)
        k_rot[...] = rotated.astype(BF)
        k_t[...] = rotated.T.astype(BF)
        dk_acc[...] = jnp.zeros_like(dk_acc)
        dv_acc[...] = jnp.zeros_like(dv_acc)
        dqg_ref[...] = jnp.zeros_like(dqg_ref)

        def head_grads(tp):
            lines = pl.ds(pl.multiple_of(tp * block, block), block)
            rows = dot_nt(branch[tp], w_out_ref[...]).astype(BF)
            for h in range(grads.shape[0]):
                grads[h, lines, :] = rows[:, h * size : (h + 1) * size]

        own_rows().wait()
        head_grads(me)
        to_core(0, rows_ref, near_other).wait_recv()
        head_grads(near_other)
        to_x(far).wait_recv()
        to_core(1, branch.at[far], far).start()
        head_grads(far)
        to_core(1, branch.at[far], far_other).wait_recv()
        head_grads(far_other)
        whole_branch().start()

    for k in range(Z_AXIS - 1):

        @pl.when(step == 2 * k + 1)
        def _(k=k):
            reduce.step(k)

    q = q_ref[...]
    q_rot = turn(q * rms_scale(q) * qg_ref[...], cosine, sine).astype(BF)
    for start, tile, keys in query_tiles(q.shape[0]):
        cols = slice(start, start + tile)
        s = dot_nt(k_rot[:keys, :], q_rot[cols, :]) * factor + bias[:keys, cols]
        p = jnp.exp(s - lse_ref[0, :, cols])
        grad = grads[step, cols, :]
        dp = dot_nt(v_ref[:keys, :], grad)
        mean = jnp.sum(p * dp, axis=0, keepdims=True)
        raw = (p * (dp - mean) * factor).astype(BF)
        dq_t[:, cols] = dot_nn(k_t[:, :keys], raw)
        dk_acc[:keys, :] += dot_nn(raw, q_rot[cols, :])
        dv_acc[:keys, :] += dot_nn(p.astype(BF), grad)
    back, gain_part = norm_back(turn_back(dq_t[...].T, cosine, sine), q, qg_ref[...])
    dq_ref[...] = back.astype(BF)
    dqg_ref[...] += gain_part

    @pl.when(step == pl.num_programs(0) - 1)
    def _():
        back, gain_part = norm_back(turn_back(dk_acc[...], cosine, sine), k_ref[...], kg_ref[...])
        dk_ref[...] = back.astype(BF)
        dkg_ref[...] = gain_part
        dv_ref[...] = dv_acc[...].astype(BF)
        reduce.step(Z_AXIS - 1)
        reduce.own(0, lambda terms: add_rows(output_ref, terms + [hidden_ref]))
        reduce.sent()
        whole_branch().wait()
        to_x(me).wait_send()
        to_core(0, rows_ref, me).wait_send()
        to_core(1, branch.at[far], far).wait_send()


def attention_back(
    span, q, k, v, lse, cosine, sine, q_gain, k_gain, w_out, d_rows, out_part, hidden, number
):
    length, size = k.shape
    heads = q.shape[1] // size
    ep_count, tp_count = lax.axis_size("ep"), lax.axis_size("tp")
    if ep_count != 2 * Z_AXIS:
        branch = lax.all_gather(d_rows, "tp", axis=0, tiled=True)
        grads = dot_nt(branch, w_out).astype(BF)
        mine = lax.psum_scatter(out_part, "ep", scatter_dimension=0)
        back = plain_attention_back(span, q, k, v, grads, lse, cosine, sine, q_gain, k_gain)
        return *back, branch, (hidden + mine.astype(F32)).astype(BF)
    block, width = d_rows.shape
    whole = pl.BlockSpec((length, size), lambda h: (0, 0))
    head = pl.BlockSpec((length, size), lambda h: (0, h))
    gain = pl.BlockSpec((1, size), lambda h: (0, 0))
    rows = pl.BlockSpec((block, width), lambda h: (0, 0))
    dma = pltpu.SemaphoreType.DMA
    *back, branch, output = pl.pallas_call(
        attention_back_kernel,
        grid=(heads,),
        in_specs=[
            pl.BlockSpec(memory_space=pltpu.SMEM), head, whole, whole,
            pl.BlockSpec((1, 1, length), lambda h: (h, 0, 0)), whole, whole, gain, gain,
            pl.BlockSpec(w_out.shape, lambda h: (0, 0)), ANY, ANY, rows,
        ],
        out_specs=[head, whole, whole, gain, gain, ANY, rows],
        out_shape=[
            jax.ShapeDtypeStruct((length, heads * size), BF),
            jax.ShapeDtypeStruct((length, size), BF),
            jax.ShapeDtypeStruct((length, size), BF),
            jax.ShapeDtypeStruct((1, size), F32),
            jax.ShapeDtypeStruct((1, size), F32),
            jax.ShapeDtypeStruct((tp_count, block, width), BF),
            jax.ShapeDtypeStruct((block, width), BF),
        ],
        scratch_shapes=[
            pltpu.VMEM((length, length), F32),
            pltpu.VMEM((length, size), BF),
            pltpu.VMEM((size, length), BF),
            pltpu.VMEM((length, size), F32),
            pltpu.VMEM((length, size), F32),
            pltpu.VMEM((size, length), F32),
            pltpu.VMEM((tp_count, block, width), BF),
            pltpu.VMEM((heads, length, size), BF),
        ]
        + reduce_scratch((block, width), BF)
        + [dma, dma, dma((2,)), dma((2,)), dma, dma]
        + reduce_sems(1),
        compiler_params=params(collective_id=number, has_side_effects=True),
        cost_estimate=link_cost(100.0),
        name="attention_back",
    )(span, q, k, v, lse, cosine, sine, q_gain, k_gain, w_out, d_rows, out_part, hidden)
    return *back, branch.reshape(-1, width), output


def projection_grads_kernel(
    normed, dq, dk, dv, heads, branch, wq, wk, wv, x_rows, d_hidden, gain, small,
    gq_ref, gk_ref, gv_ref, gout_ref, inputs_grad, gain_grad, small_sum,
    blocks, side, along, part, core_rows, far_rows, gain_own, gains,
    core_send, core_recv, x_send, x_recv, gain_send, gain_recv, *refs,
):
    me = lax.axis_index("tp")
    x, c = me // 2, me % 2
    other_core, other_x = {"tp": x * 2 + 1 - c}, {"tp": (1 - x) * 2 + c}
    sums = SumAll(small, small_sum, *refs[:6])
    reduce = EpReduce([blocks], [side, along], refs[6:], loaded=False)
    order, y = reduce.order, reduce.y
    rows, width = inputs_grad.shape
    nq, nk = dq.shape[1], dk.shape[1]

    sums.greet()
    sums.start()

    def fill(j):
        cols = pl.ds(pl.multiple_of(j * rows, rows), rows)
        left = normed[:, cols].T
        blocks[j, :, 0:nq] = dot_nn(left, dq[...]).astype(BF)
        blocks[j, :, nq : nq + nk] = dot_nn(left, dk[...]).astype(BF)
        blocks[j, :, nq + nk : nq + 2 * nk] = dot_nn(left, dv[...]).astype(BF)
        blocks[j, :, nq + 2 * nk :] = dot_nn(branch[:, cols].T, heads[...]).astype(BF)

    def spread_back(tp):
        lines = pl.ds(pl.multiple_of(tp * rows, rows), rows)
        for start in range(0, width, width // 4):
            cols = slice(start, start + width // 4)
            part[tp, :, cols] = (
                dot_nt(dq[lines, :], wq[cols, :])
                + dot_nt(dk[lines, :], wk[cols, :])
                + dot_nt(dv[lines, :], wv[cols, :])
            ).astype(BF)

    def to_core(xt):
        return remote(
            part.at[xt * 2 + 1 - c], core_rows.at[xt], core_send.at[xt], core_recv.at[xt], other_core
        )

    far, near = part.at[(1 - x) * 2 + c], part.at[x * 2 + c]
    to_x = remote(far, far_rows, x_send, x_recv, other_x)

    for k in range(2):
        fill(order[k] * 2 + 1 - y)
        reduce.send_side(k)
    spread_back((1 - x) * 2 + 1 - c)
    to_core(1 - x).start()
    spread_back((1 - x) * 2 + c)
    to_core(1 - x).wait_recv()
    add_rows(far, [far, core_rows.at[1 - x]])
    to_x.start()
    for k in range(2, Z_AXIS):
        fill(order[k] * 2 + 1 - y)
        reduce.send_side(k)
    fill(order[0] * 2 + y)
    reduce.step(0)
    spread_back(x * 2 + 1 - c)
    to_core(x).start()
    spread_back(x * 2 + c)
    for k in range(1, Z_AXIS):
        fill(order[k] * 2 + y)
    sums.add()
    reduce.step(1)
    to_core(x).wait_recv()
    to_x.wait_recv()

    chunk = 32
    gain_own[...] = jnp.zeros_like(gain_own)

    @pl.loop(0, rows // chunk)
    def _(i):
        lines = pl.ds(pl.multiple_of(i * chunk, chunk), chunk)
        grad = near[lines, :].astype(F32) + core_rows[x, lines, :].astype(F32)
        grad = grad + far_rows[lines, :].astype(F32)
        back, gain_part = norm_back(grad, x_rows[lines, :].astype(F32), gain[...])
        inputs_grad[lines, :] = d_hidden[lines, :] + back
        gain_own[...] += gain_part

    def tell(i):
        to = sums.other(i)
        return remote(
            gain_own, gains.at[sums.me], gain_send.at[i], gain_recv.at[sums.me], sums.device(to)
        )

    def heard(i):
        origin = sums.other(i)
        row = gains.at[origin]
        return remote(row, row, gain_send.at[i], gain_recv.at[origin], sums.device(origin))

    sums.each(lambda i: tell(i).start())
    gains[pl.ds(sums.me, 1)] = gain_own[...][None]
    reduce.step(2)
    reduce.step(3)

    def write(terms):
        n = rows // 2
        for h in range(2):
            lines = slice(h * n, (h + 1) * n)
            value = terms[0][lines, :].astype(F32)
            for term in terms[1:]:
                value = value + term[lines, :].astype(F32)
            gq_ref[lines, :] = value[:, 0:nq]
            gk_ref[lines, :] = value[:, nq : nq + nk]
            gv_ref[lines, :] = value[:, nq + nk : nq + 2 * nk]
            gout_ref[:, lines] = value[:, nq + 2 * nk :].T

    sums.each(lambda i: heard(i).wait_recv())
    gain_grad[...] = jnp.sum(gains[...], axis=0)
    reduce.own(0, write)
    reduce.sent()
    to_core(1 - x).wait_send()
    to_core(x).wait_send()
    to_x.wait_send()
    sums.each(lambda i: tell(i).wait_send())
    sums.finish()


def projection_grads(
    normed, dq, dk, dv, heads, branch, wq, wk, wv, x_rows, d_hidden, gain, small_values, number
):
    rows, width = x_rows.shape
    ep_count, tp_count = lax.axis_size("ep"), lax.axis_size("tp")
    total = ep_count * tp_count
    small = pack_small(small_values, total)
    if ep_count != 2 * Z_AXIS:

        def over_sequences(part, dim):
            return lax.psum_scatter(
                part.astype(BF), "ep", scatter_dimension=dim, tiled=True
            ).astype(F32)

        d_normed = (dot_nt(dq, wq) + dot_nt(dk, wk) + dot_nt(dv, wv)).astype(BF)
        d_mine = lax.psum_scatter(d_normed, "tp", scatter_dimension=0, tiled=True)
        back, gain_part = norm_back(d_mine.astype(F32), x_rows.astype(F32), gain)
        gain_sum, small_sum = lax.psum((gain_part, small), ("ep", "tp"))
        return (
            over_sequences(dot_tn(normed, dq), 0),
            over_sequences(dot_tn(normed, dk), 0),
            over_sequences(dot_tn(normed, dv), 0),
            over_sequences(dot_tn(heads, branch), 1),
            d_hidden + back,
            gain_sum,
            unpack_small(small_sum, small_values),
        )
    nq, nk = dq.shape[1], dk.shape[1]
    nh = heads.shape[1]
    columns = nq + 2 * nk + nh
    vmem = pl.BlockSpec(memory_space=pltpu.VMEM)
    dma = pltpu.SemaphoreType.DMA
    *grads, small_sum = pl.pallas_call(
        projection_grads_kernel,
        in_specs=[vmem] * 13,
        out_specs=[vmem] * 7,
        out_shape=[
            jax.ShapeDtypeStruct((rows, nq), F32),
            jax.ShapeDtypeStruct((rows, nk), F32),
            jax.ShapeDtypeStruct((rows, nk), F32),
            jax.ShapeDtypeStruct((nh, rows), F32),
            jax.ShapeDtypeStruct((rows, width), F32),
            jax.ShapeDtypeStruct((1, width), F32),
            jax.ShapeDtypeStruct(small.shape, F32),
        ],
        scratch_shapes=[pltpu.VMEM((ep_count, rows, columns), BF)]
        + reduce_scratch((rows, columns), BF, loaded=False)
        + [
            pltpu.VMEM((tp_count, rows, width), BF),
            pltpu.VMEM((2, rows, width), BF),
            pltpu.VMEM((rows, width), BF),
            pltpu.VMEM((1, width), F32),
            pltpu.VMEM((total, 1, width), F32),
            dma((2,)), dma((2,)), dma, dma, dma((total,)), dma((total,)),
        ]
        + sum_scratch(small.shape[1], total)
        + reduce_sems(1),
        compiler_params=params(collective_id=number, has_side_effects=True),
        cost_estimate=link_cost(110.0),
        name="projection_grads",
    )(normed, dq, dk, dv, heads, branch, wq, wk, wv, x_rows, d_hidden, gain, small)
    return *grads, unpack_small(small_sum, small_values)


def select_kernel(slot_ref, x_ref, c_ref, xs_ref, cs_ref):
    local, _, capacity, width = xs_ref.shape
    rows = x_ref.shape[1]
    place = jnp.concatenate(
        [
            (
                slot_ref[0, e : e + 1, :]
                == lax.broadcasted_iota(jnp.int32, (capacity, rows), 0)
            ).astype(F32)
            for e in range(local)
        ],
        axis=0,
    ).astype(BF)
    xs_ref[...] = dot_nn(place, x_ref[0]).astype(BF).reshape(xs_ref.shape)
    cs_ref[...] = dot_nn(place, c_ref[0]).astype(BF).reshape(cs_ref.shape)


def select_rows(slots, tokens, cots, capacity):
    blocks, local, rows = slots.shape
    width = tokens.shape[-1]
    block = pl.BlockSpec((1, rows, width), lambda b: (b, 0, 0))
    out = pl.BlockSpec((local, 1, capacity, width), lambda b: (0, b, 0, 0))
    shape = jax.ShapeDtypeStruct((local, blocks, capacity, width), BF)
    return pl.pallas_call(
        select_kernel,
        grid=(blocks,),
        in_specs=[pl.BlockSpec((1, local, rows), lambda b: (b, 0, 0)), block, block],
        out_specs=[out, out],
        out_shape=[shape, shape],
        compiler_params=params(),
        name="select_rows",
    )(slots, tokens, cots)


def expert_kernel(
    x_ref, c_ref, wg_ref, w_ref, gate_ref, out_ref, dx_ref, act_ref, dg_ref, du_ref, dgate_ref
):
    width = x_ref.shape[-1]
    x, c = x_ref[0], c_ref[0]
    w_gate = wg_ref[:, 0, 0].reshape(-1, width)
    w_up = w_ref[:, 0, 0].reshape(-1, width)
    w_down = w_ref[:, 1, 0].reshape(-1, width)
    gate = gate_ref[0]
    gate_pre = dot_nt(x, w_gate)
    up_pre = dot_nt(x, w_up)
    raw = dot_nt(c, w_down)
    sig = jax.nn.sigmoid(gate_pre)
    silu = gate_pre * sig
    act = silu * up_pre
    dgate_ref[0] = jnp.sum(act * raw, axis=-1, keepdims=True)
    act_low = (act * gate).astype(BF)
    d_act = raw * gate
    d_gate = (d_act * up_pre * sig * (1.0 + gate_pre * (1.0 - sig))).astype(BF)
    d_up = (d_act * silu).astype(BF)
    act_ref[0] = act_low
    dg_ref[0] = d_gate
    du_ref[0] = d_up
    out_ref[0] = dot_nn(act_low, w_down).astype(BF)
    dx_ref[0] = (dot_nn(d_gate, w_gate) + dot_nn(d_up, w_up)).astype(BF)


def experts_both_ways(x_slots, c_slots, w_gate_all, w_rest_all, slot_gate):
    local, number, width = x_slots.shape
    parts, _, _, hidden, _ = w_gate_all.shape
    tile = number // 2
    wide = pl.BlockSpec((1, tile, width), lambda e, i: (e, i, 0))
    mid = pl.BlockSpec((1, tile, parts * hidden), lambda e, i: (e, i, 0))
    thin = pl.BlockSpec((1, tile, 1), lambda e, i: (e, i, 0))
    wide_shape = jax.ShapeDtypeStruct((local, number, width), BF)
    mid_shape = jax.ShapeDtypeStruct((local, number, parts * hidden), BF)
    return pl.pallas_call(
        expert_kernel,
        grid=(local, 2),
        in_specs=[
            wide, wide,
            pl.BlockSpec((parts, 1, 1, hidden, width), lambda e, i: (0, 0, e, 0, 0)),
            pl.BlockSpec((parts, 2, 1, hidden, width), lambda e, i: (0, 0, e, 0, 0)),
            thin,
        ],
        out_specs=[wide, wide, mid, mid, mid, thin],
        out_shape=[
            wide_shape, wide_shape, mid_shape, mid_shape, mid_shape,
            jax.ShapeDtypeStruct((local, number, 1), F32),
        ],
        compiler_params=params(),
        name="experts_both_ways",
    )(x_slots, c_slots, w_gate_all, w_rest_all, slot_gate)


def expert_grads_kernel(x_ref, c_ref, act_ref, dg_ref, du_ref, first_ref, rest_ref):
    parts, _, _, hidden, width = first_ref.shape
    x, c = x_ref[0], c_ref[0]
    first_ref[:, 0, 0] = dot_tn(dg_ref[0], x).astype(BF).reshape(parts, hidden, width)
    rest_ref[:, 0, 0] = dot_tn(du_ref[0], x).astype(BF).reshape(parts, hidden, width)
    rest_ref[:, 1, 0] = dot_tn(act_ref[0], c).astype(BF).reshape(parts, hidden, width)


def expert_grads(x_slots, c_slots, act, d_gate, d_up, parts):
    local, number, width = x_slots.shape
    inner = act.shape[-1]
    wide = pl.BlockSpec((1, number, width), lambda e: (e, 0, 0))
    mid = pl.BlockSpec((1, number, inner), lambda e: (e, 0, 0))
    return pl.pallas_call(
        expert_grads_kernel,
        grid=(local,),
        in_specs=[wide, wide, mid, mid, mid],
        out_specs=[
            pl.BlockSpec((parts, kinds, 1, inner // parts, width), lambda e: (0, 0, e, 0, 0))
            for kinds in (1, 2)
        ],
        out_shape=[
            jax.ShapeDtypeStruct((parts, kinds, local, inner // parts, width), BF)
            for kinds in (1, 2)
        ],
        compiler_params=params(),
        name="expert_grads",
    )(x_slots, c_slots, act, d_gate, d_up)


def combine_kernel(first_ref, slot_ref, dx_ref, out_ref, dgate_ref, dx_sum_ref, out_sum_ref, pay_ref):
    local, _, capacity, width = dx_ref.shape
    rows = slot_ref.shape[1]
    lane = lax.broadcasted_iota(jnp.int32, (rows, local * capacity), 1)
    half = pay_ref.shape[2] // 2
    column = lax.broadcasted_iota(jnp.int32, (rows, 2 * half), 1)
    total = jnp.zeros((rows, local * capacity), F32)
    pay = jnp.zeros(column.shape, F32)
    for e in range(local):
        hit = lane == slot_ref[0, :, e : e + 1] + e * capacity
        total = jnp.where(hit, 1.0, total)
        value = jnp.sum(jnp.where(hit, dgate_ref[0], 0.0), axis=1, keepdims=True)
        high = value.astype(BF).astype(F32)
        pay = jnp.where(column == first_ref[0, 0] + e, high, pay)
        pay = jnp.where(column == first_ref[0, 0] + e + half, value - high, pay)
    place = total.astype(BF)
    dx_sum_ref[0] = dot_nn(place, dx_ref[...].reshape(-1, width)).astype(BF)
    out_sum_ref[0] = dot_nn(place, out_ref[...].reshape(-1, width)).astype(BF)
    pay_ref[0] = pay.astype(BF)


def combine_rows(first, slots_t, dx, out, d_gate_slots, experts):
    blocks, rows, local = slots_t.shape
    _, _, capacity, width = dx.shape
    lanes = -(-2 * experts // 128) * 128
    slot = pl.BlockSpec((local, 1, capacity, width), lambda b: (0, b, 0, 0))
    block = pl.BlockSpec((1, rows, width), lambda b: (b, 0, 0))
    shape = jax.ShapeDtypeStruct((blocks, rows, width), BF)
    return pl.pallas_call(
        combine_kernel,
        grid=(blocks,),
        in_specs=[
            pl.BlockSpec(memory_space=pltpu.SMEM),
            pl.BlockSpec((1, rows, local), lambda b: (b, 0, 0)), slot, slot,
            pl.BlockSpec((1, 1, local * capacity), lambda b: (b, 0, 0)),
        ],
        out_specs=[block, block, pl.BlockSpec((1, rows, lanes), lambda b: (b, 0, 0))],
        out_shape=[shape, shape, jax.ShapeDtypeStruct((blocks, rows, lanes), BF)],
        compiler_params=params(),
        name="combine_rows",
    )(first, slots_t, dx, out, d_gate_slots)


def on_device(
    inputs,
    attn_gain,
    w_query,
    key_weight_matrix,
    value_weight_matrix,
    query_gain,
    key_gain,
    w_out,
    route_gain,
    w_router,
    w_gate,
    w_up,
    w_down,
    routes,
    image_starts,
    cotangent,
):
    tp_count = lax.axis_size("tp")
    ep_count = lax.axis_size("ep")
    tp_index = lax.axis_index("tp")
    ep_index = lax.axis_index("ep")
    length = inputs.shape[0]
    width = inputs.shape[1]
    rows = cotangent.shape[0]
    head_dim = query_gain.shape[0]
    local_experts = w_gate.shape[0]
    experts = local_experts * ep_count
    top = routes.shape[1]
    capacity = -(-(3 * rows * top // (2 * experts)) // 16) * 16

    w_gate_all = lax.all_gather(w_gate.transpose(0, 2, 1)[None], "tp")

    inputs_f = inputs.astype(F32)
    attn_scale = rms_scale(inputs_f)
    normed = (inputs_f * attn_scale * attn_gain).astype(BF)
    queries = dot_nn(normed, w_query)
    key_rows = dot_nn(normed, key_weight_matrix)
    values = dot_nn(normed, value_weight_matrix).astype(BF)
    cosine, sine = rope_tables(length, head_dim)
    q_gain, k_gain = query_gain[None], key_gain[None]
    heads, lse, attn_rows, cot_all = attention(
        image_starts, queries, key_rows, values, cosine, sine, q_gain, k_gain, w_out, cotangent, 0
    )
    attn_rows, w_rest = lax.optimization_barrier(
        (attn_rows, jnp.stack([w_up.transpose(0, 2, 1), w_down]))
    )
    w_rest_all = lax.all_gather(w_rest, "tp")
    x_rows = lax.dynamic_slice_in_dim(inputs, tp_index * rows, rows, 0)
    hidden = x_rows.astype(F32) + attn_rows
    route_scale = rms_scale(hidden)
    moe_in = (hidden * route_scale * route_gain).astype(BF)
    moe_in, w_gate_all = lax.optimization_barrier((moe_in, w_gate_all))
    (tokens_all,) = gather_ep([moe_in], 1, "gather_rows")

    logits = dot_nn(moe_in, w_router)
    router_probs = plain_softmax(logits)
    expert_ids = jnp.arange(experts, dtype=jnp.int32)
    ring_routes = lax.dynamic_index_in_dim(
        routes.reshape(ep_count, tp_count, rows, top), tp_index, 1, keepdims=False
    )
    my_routes = lax.dynamic_index_in_dim(ring_routes, ep_index, 0, keepdims=False)

    def routed_softmax(scores, picked):
        kept = jnp.where(picked, scores, MASKED)
        expo = jnp.where(picked, jnp.exp(kept - jnp.max(kept, axis=-1, keepdims=True)), 0.0)
        return expo / jnp.sum(expo, axis=-1, keepdims=True)

    my_pick = jnp.any(my_routes[:, :, None] == expert_ids[None, None, :], axis=1)
    gates = routed_softmax(logits, my_pick)
    all_pick = jnp.any(ring_routes[..., None] == expert_ids, axis=2)
    gates_all = routed_softmax(dot_nn(tokens_all.reshape(-1, width), w_router).reshape(ep_count, rows, experts), all_pick)
    gate_of = lax.dynamic_slice_in_dim(gates_all, ep_index * local_experts, local_experts, 2)
    mask = lax.dynamic_slice_in_dim(all_pick, ep_index * local_experts, local_experts, 2)
    earlier = (jnp.arange(rows)[:, None] > jnp.arange(rows)[None, :]).astype(BF)
    slots_t = jnp.einsum(
        "tu,bue->bte", earlier, mask.astype(BF), preferred_element_type=F32
    ).astype(jnp.int32)
    slots_t = jnp.where(mask, slots_t, NOWHERE)
    slots = slots_t.transpose(0, 2, 1)
    place = slots[:, :, None, :] == jnp.arange(capacity, dtype=jnp.int32)[:, None]
    slot_gate = jnp.sum(jnp.where(place, gate_of.transpose(0, 2, 1)[:, :, None, :], 0.0), axis=-1)
    slot_gate = slot_gate.transpose(1, 0, 2).reshape(local_experts, ep_count * capacity, 1)

    x_slots, c_slots = select_rows(slots, tokens_all, cot_all, capacity)
    flat = (local_experts, ep_count * capacity, width)
    deep = (local_experts, ep_count, capacity, width)
    x_slots, c_slots = x_slots.reshape(flat), c_slots.reshape(flat)
    out_slots, dx_slots, act, d_gate, d_up, d_gate_slots = experts_both_ways(
        x_slots, c_slots, w_gate_all, w_rest_all, slot_gate
    )
    dx_part, out_part, gate_part = combine_rows(
        (ep_index * local_experts).reshape(1, 1),
        slots_t,
        dx_slots.reshape(deep),
        out_slots.reshape(deep),
        d_gate_slots.reshape(local_experts, ep_count, capacity)
        .transpose(1, 0, 2)
        .reshape(ep_count, 1, local_experts * capacity),
        experts,
    )
    first_grads, rest_grads = expert_grads(x_slots, c_slots, act, d_gate, d_up, tp_count)

    def over_rings(grads):
        return lax.psum_scatter(grads.reshape(-1, width), "tp", scatter_dimension=0, tiled=True)

    dx_part, first_grads, rest_grads = lax.optimization_barrier((dx_part, first_grads, rest_grads))
    first_mine = over_rings(first_grads)
    dx_mine, gate_mine = reduce_ep([dx_part, gate_part], [F32, F32], 2, "reduce_input_grads")
    dx_mine, first_mine, rest_grads = lax.optimization_barrier((dx_mine, first_mine, rest_grads))
    rest_mine = over_rings(rest_grads).astype(F32).reshape(2, local_experts, -1, width)
    first_mine = first_mine.astype(F32).reshape(local_experts, -1, width)
    lanes = gate_mine.shape[1] // 2
    d_gates = gate_mine[:, :experts] + gate_mine[:, lanes : lanes + experts]
    w_gate_grad = first_mine.transpose(0, 2, 1)
    w_up_grad = rest_mine[0].transpose(0, 2, 1)
    w_down_grad = rest_mine[1]

    counts = jnp.sum((routes[:, :, None] == expert_ids[None, None, :]).astype(F32), axis=(0, 1))
    total_tokens = routes.shape[0]
    share = counts / (total_tokens * top)
    coeff = AUX * experts * share
    prob_local = jnp.sum(router_probs, axis=0)
    cot = cotangent.astype(F32)
    d_logits = gates * (d_gates - jnp.sum(gates * d_gates, axis=-1, keepdims=True))
    d_logits = d_logits + router_probs * (
        coeff - jnp.sum(router_probs * coeff, axis=-1, keepdims=True)
    )
    d_logits_low = d_logits.astype(BF)
    router_part = dot_tn(moe_in, d_logits_low)
    d_moe = dot_nt(d_logits_low, w_router) + dx_mine
    d_hidden, route_gain_part = norm_back(d_moe, hidden, route_gain[None])
    d_hidden = d_hidden + cot

    d_queries, d_keys, d_values, query_gain_part, key_gain_part, d_branch, output = attention_back(
        image_starts, queries, key_rows, values, lse, cosine, sine, q_gain, k_gain,
        w_out, d_hidden.astype(BF), out_part, hidden, 3,
    )
    w_query_grad, w_key_grad, w_value_grad, w_out_grad, inputs_grad, attn_gain_grad, small = projection_grads(
        normed, d_queries, d_keys, d_values, heads, d_branch,
        w_query, key_weight_matrix, value_weight_matrix,
        x_rows, d_hidden, attn_gain[None],
        [router_part, route_gain_part[0], query_gain_part[0], key_gain_part[0], prob_local],
        5,
    )
    w_router_grad, route_gain_grad, query_gain_grad, key_gain_grad, prob_all = small
    attn_gain_grad = attn_gain_grad[0]
    aux_loss = experts * jnp.sum(share * (prob_all / total_tokens))
    return (
        output,
        aux_loss,
        inputs_grad,
        attn_gain_grad,
        w_query_grad,
        w_key_grad,
        w_value_grad,
        query_gain_grad,
        key_gain_grad,
        w_out_grad,
        route_gain_grad,
        w_router_grad,
        w_gate_grad,
        w_up_grad,
        w_down_grad,
    )


def solution(mesh):
    return jax.shard_map(
        on_device,
        mesh=mesh,
        in_specs=(
            P("ep", None),
            P(),
            P(None, "tp"),
            P(None, "tp"),
            P(None, "tp"),
            P(),
            P(),
            P("tp", None),
            P(),
            P(),
            P("ep", None, "tp"),
            P("ep", None, "tp"),
            P("ep", "tp", None),
            P(),
            P("ep", None),
            P(("ep", "tp"), None),
        ),
        out_specs=(
            P(("ep", "tp"), None),
            P(),
            P(("ep", "tp"), None),
            P(),
            P("ep", "tp"),
            P("ep", "tp"),
            P("ep", "tp"),
            P(),
            P(),
            P("tp", "ep"),
            P(),
            P(),
            P("ep", None, "tp"),
            P("ep", None, "tp"),
            P("ep", "tp", None),
        ),
        check_vma=False,
    )
```

```python
import functools

import jax
import jax.numpy as jnp
from jax import lax
from jax.experimental import pallas as pl
from jax.experimental.pallas import tpu as pltpu
from jax.sharding import PartitionSpec as P

IMG = 256
EPS = 1e-06
AUX = 0.04
THETA = 1000000.0
MASKED = -1e30
NOWHERE = -(1 << 20)
BF = jnp.bfloat16
F32 = jnp.float32
VMEM_BYTES = 60 * 1024 * 1024


def dot_nn(a, b):
    return lax.dot_general(a, b, (((1,), (0,)), ((), ())), preferred_element_type=F32)


def dot_nt(a, b):
    return lax.dot_general(a, b, (((1,), (1,)), ((), ())), preferred_element_type=F32)


def dot_tn(a, b):
    return lax.dot_general(a, b, (((0,), (0,)), ((), ())), preferred_element_type=F32)


def params(**kw):
    return pltpu.CompilerParams(vmem_limit_bytes=VMEM_BYTES, **kw)


def rms_scale(value_rows):
    return lax.rsqrt(jnp.mean(value_rows * value_rows, axis=-1, keepdims=True) + EPS)


def plain_softmax(value_rows):
    top = jnp.max(value_rows, axis=-1, keepdims=True)
    expo = jnp.exp(value_rows - top)
    return expo / jnp.sum(expo, axis=-1, keepdims=True)


def rope_tables(length, size):
    half = size // 2
    freq = jnp.exp(-jnp.log(THETA) * (2.0 * jnp.arange(half, dtype=F32)) / size)
    angle = jnp.arange(length, dtype=F32)[:, None] * freq[None, :]
    cosine = jnp.cos(angle)
    sine = jnp.sin(angle)
    return (jnp.concatenate([cosine, cosine], axis=-1), jnp.concatenate([-sine, sine], axis=-1))


def turn(rows, cosine, sine):
    return rows * cosine + pltpu.roll(rows, rows.shape[-1] // 2, 1) * sine


def turn_back(rows, cosine, sine):
    return rows * cosine - pltpu.roll(rows, rows.shape[-1] // 2, 1) * sine


MESH = pl.DeviceIdType.MESH
ANY = pl.BlockSpec(memory_space=pl.ANY)
Z_AXIS = 4


def link_cost(us):
    return pl.CostEstimate(flops=0, bytes_accessed=int(us * 3.0e6), transcendentals=0)


def greet(partners):
    barrier = pltpu.get_barrier_semaphore()
    count = 0
    for there, device in partners:
        flag = jnp.asarray(there, jnp.int32)

        @pl.when(there)
        def _(device=device):
            pl.semaphore_signal(barrier, inc=1, device_id=device, device_id_type=MESH)

        count = count + flag
    pl.semaphore_wait(barrier, count)


def remote(src, dst, send, recv, device):
    return pltpu.make_async_remote_copy(
        src_ref=src, dst_ref=dst, send_sem=send, recv_sem=recv, device_id=device, device_id_type=MESH
    )


def ring_place():
    me = lax.axis_index("ep")
    z, y = me // 2, me % 2
    return me, z, y, {"ep": me + 2}, {"ep": me - 2}, {"ep": me + 1 - 2 * y}


class EpGather:
    def __init__(self, ins, outs, sems):
        self.ins, self.outs = ins, outs
        self.own_sem, self.up_send, self.up_recv, self.dn_send, self.dn_recv = sems[:5]
        self.y_send, self.y_recv = sems[5:]
        self.me, self.z, self.y, self.up, self.down, self.beside = ring_place()

    def partners(self):
        z = self.z
        return [(z < Z_AXIS - 1, self.up), (z > 0, self.down), (z >= 0, self.beside)]

    def block(self, a, zt):
        return self.outs[a].at[zt * 2 + self.y]

    def upward(self, src, a, zt):
        return remote(src, self.block(a, zt), self.up_send.at[a, zt], self.up_recv.at[a, zt], self.up)

    def downward(self, src, a, zt):
        return remote(src, self.block(a, zt), self.dn_send.at[a, zt], self.dn_recv.at[a, zt], self.down)

    def sideways(self, src, a, zt):
        return remote(src, self.block(a, zt), self.y_send.at[a, zt], self.y_recv.at[a, zt], self.beside)

    def start(self):
        z = self.z
        for a, x in enumerate(self.ins):

            @pl.when(z < Z_AXIS - 1)
            def _(a=a, x=x):
                self.upward(x, a, z).start()

            @pl.when(z > 0)
            def _(a=a, x=x):
                self.downward(x, a, z).start()

            self.sideways(x, a, z).start()
            pltpu.make_async_copy(x, self.block(a, z), self.own_sem.at[a]).start()

    def hop(self, d):
        z = self.z
        for a in range(len(self.ins)):

            @pl.when(z >= d)
            def _(a=a, zt=z - d):
                self.upward(self.block(a, zt), a, zt).wait_recv()

                @pl.when(z < Z_AXIS - 1)
                def _():
                    self.upward(self.block(a, zt), a, zt).start()

                self.sideways(self.block(a, zt), a, zt).start()

            @pl.when(z + d < Z_AXIS)
            def _(a=a, zt=z + d):
                self.downward(self.block(a, zt), a, zt).wait_recv()

                @pl.when(z > 0)
                def _():
                    self.downward(self.block(a, zt), a, zt).start()

                self.sideways(self.block(a, zt), a, zt).start()

    def own_done(self, a):
        pltpu.make_async_copy(self.ins[a], self.block(a, self.z), self.own_sem.at[a]).wait()

    def side_done(self, a, zt):
        other = self.outs[a].at[zt * 2 + 1 - self.y]
        remote(other, other, self.y_send.at[a, zt], self.y_recv.at[a, zt], self.beside).wait_recv()

    def sent(self, a):
        z = self.z
        for zt in range(Z_AXIS):
            src = self.block(a, zt)
            self.sideways(src, a, zt).wait_send()

            @pl.when((zt <= z) & (z < Z_AXIS - 1))
            def _(src=src, zt=zt):
                self.upward(src, a, zt).wait_send()

            @pl.when((zt >= z) & (z > 0))
            def _(src=src, zt=zt):
                self.downward(src, a, zt).wait_send()

    def finish(self):
        for a in range(len(self.ins)):
            self.own_done(a)
            for zt in range(Z_AXIS):
                self.side_done(a, zt)
            self.sent(a)


def gather_sems(count):
    dma = pltpu.SemaphoreType.DMA
    return [dma((count,))] + [dma((count, Z_AXIS))] * 6


def halves(ref, axis):
    n = ref.shape[axis] // 2
    lead = (slice(None),) * axis
    return [ref.at[lead + (pl.ds(h * n, n),)] for h in range(2)]


def gather_ep_kernel(x, out, *sems):
    gather = EpGather(halves(x, 0), halves(out, 1), sems)
    greet(gather.partners())
    gather.start()
    for d in range(1, Z_AXIS):
        gather.hop(d)
    gather.finish()


def gather_ep(rows, number, name):
    ep_count = lax.axis_size("ep")
    if ep_count != 2 * Z_AXIS:
        return lax.all_gather(rows, "ep")
    return pl.pallas_call(
        gather_ep_kernel,
        in_specs=[ANY],
        out_specs=ANY,
        out_shape=jax.ShapeDtypeStruct((ep_count,) + rows.shape, rows.dtype),
        scratch_shapes=gather_sems(2),
        compiler_params=params(collective_id=number, has_side_effects=True),
        cost_estimate=link_cost(85.0),
        name=name,
    )(rows)


def add_rows(total, terms, chunk=32):
    @pl.loop(0, total.shape[0] // chunk)
    def _(i):
        rows = pl.ds(pl.multiple_of(i * chunk, chunk), chunk)
        value = terms[0][rows, :].astype(F32)
        for term in terms[1:]:
            value = value + term[rows, :].astype(F32)
        total[rows, :] = value.astype(total.dtype)


def scatter_order(z):
    table = ((3, 2, 1, 0), (3, 0, 2, 1), (0, 3, 1, 2), (0, 1, 2, 3))
    return [
        jnp.where(
            z == 0,
            table[0][k],
            jnp.where(z == 1, table[1][k], jnp.where(z == 2, table[2][k], table[3][k])),
        )
        for k in range(Z_AXIS)
    ]


class EpReduce:
    def __init__(self, ins, bufs, sems, loaded=True):
        self.ins, self.loaded = ins, loaded
        each = 3 if loaded else 2
        self.bufs = [bufs[each * a : each * a + each] for a in range(len(ins))]
        self.own_sem, self.up_send, self.up_recv, self.dn_send, self.dn_recv = sems[:5]
        self.y_send, self.y_recv = sems[5:]
        self.me, self.z, self.y, self.up, self.down, self.beside = ring_place()
        self.order = scatter_order(self.z)

    def partners(self):
        z = self.z
        return [(z < Z_AXIS - 1, self.up), (z > 0, self.down), (z >= 0, self.beside)]

    def mine(self, a, zt):
        return self.bufs[a][0].at[zt] if self.loaded else self.ins[a].at[zt * 2 + self.y]

    def side(self, a, zt):
        return self.bufs[a][-2].at[zt]

    def below(self, a, zt):
        return self.bufs[a][-1].at[zt]

    def above(self, a, zt, z):
        return self.bufs[a][-1].at[jnp.where(zt == z, Z_AXIS, zt)]

    def to_side(self, a, zt):
        src = self.ins[a].at[zt * 2 + 1 - self.y]
        return remote(src, self.side(a, zt), self.y_send.at[a, zt], self.y_recv.at[a, zt], self.beside)

    def load(self, a, zt):
        return pltpu.make_async_copy(
            self.ins[a].at[zt * 2 + self.y], self.mine(a, zt), self.own_sem.at[a, zt]
        )

    def rising(self, a, zt):
        return remote(
            self.mine(a, zt), self.below(a, zt), self.up_send.at[a, zt], self.up_recv.at[a, zt], self.up
        )

    def falling(self, a, zt):
        return remote(
            self.mine(a, zt), self.above(a, zt, self.z - 1),
            self.dn_send.at[a, zt], self.dn_recv.at[a, zt], self.down,
        )

    def send_side(self, k):
        for a in range(len(self.ins)):
            self.to_side(a, self.order[k]).start()
            if self.loaded:
                self.load(a, self.order[k]).start()

    def step(self, k):
        z, zt, last = self.z, self.order[k], Z_AXIS - 1
        for a in range(len(self.ins)):
            mine, side = self.mine(a, zt), self.side(a, zt)
            if self.loaded:
                self.load(a, zt).wait()
            self.to_side(a, zt).wait_recv()

            @pl.when(((zt > z) & (z == 0)) | ((zt < z) & (z == last)))
            def _(mine=mine, side=side):
                add_rows(mine, [mine, side])

            @pl.when((zt > z) & (z > 0))
            def _(a=a, mine=mine, side=side):
                self.rising(a, zt).wait_recv()
                add_rows(mine, [mine, side, self.below(a, zt)])

            @pl.when((zt < z) & (z < last))
            def _(a=a, mine=mine, side=side):
                self.falling(a, zt).wait_recv()
                add_rows(mine, [mine, side, self.above(a, zt, z)])

            @pl.when(zt > z)
            def _(a=a):
                self.rising(a, zt).start()

            @pl.when(zt < z)
            def _(a=a):
                self.falling(a, zt).start()

    def own(self, a, write):
        z, last = self.z, Z_AXIS - 1
        pair = [self.mine(a, z), self.side(a, z)]

        @pl.when(z > 0)
        def _():
            self.rising(a, z).wait_recv()

        @pl.when(z < last)
        def _():
            self.falling(a, z).wait_recv()

        @pl.when(z == 0)
        def _():
            write(pair + [self.above(a, z, z)])

        @pl.when(z == last)
        def _():
            write(pair + [self.below(a, z)])

        @pl.when((z > 0) & (z < last))
        def _():
            write(pair + [self.below(a, z), self.above(a, z, z)])

    def sent(self):
        z = self.z
        for a in range(len(self.ins)):
            for zt in range(Z_AXIS):
                self.to_side(a, zt).wait_send()

                @pl.when(zt > z)
                def _(a=a, zt=zt):
                    self.rising(a, zt).wait_send()

                @pl.when(zt < z)
                def _(a=a, zt=zt):
                    self.falling(a, zt).wait_send()


def reduce_scratch(shape, dtype, loaded=True):
    counts = ([Z_AXIS] if loaded else []) + [Z_AXIS, Z_AXIS + 1]
    return [pltpu.VMEM((n,) + tuple(shape), dtype) for n in counts]


def reduce_sems(count):
    return [pltpu.SemaphoreType.DMA((count, Z_AXIS))] * 7


def reduce_ep_kernel(part, extra, out, extra_out, *refs):
    reduce = EpReduce(halves(part, 1) + [extra], refs[:9], refs[9:])
    greet(reduce.partners())
    for k in range(Z_AXIS):
        reduce.send_side(k)
    for k in range(Z_AXIS):
        reduce.step(k)
    for a, rows in enumerate(halves(out, 0) + [extra_out]):
        reduce.own(a, functools.partial(add_rows, rows))
    reduce.sent()


def reduce_ep(part, extra, number, name):
    ep_count = lax.axis_size("ep")
    if ep_count != 2 * Z_AXIS:
        return [lax.psum_scatter(p, "ep", scatter_dimension=0).astype(F32) for p in (part, extra)]
    _, rows, columns = part.shape
    half = reduce_scratch((rows // 2, columns), BF)
    return pl.pallas_call(
        reduce_ep_kernel,
        in_specs=[ANY] * 2,
        out_specs=[pl.BlockSpec(memory_space=pltpu.VMEM)] * 2,
        out_shape=[jax.ShapeDtypeStruct(p.shape[1:], F32) for p in (part, extra)],
        scratch_shapes=half + half + reduce_scratch(extra.shape[1:], BF) + reduce_sems(3),
        compiler_params=params(collective_id=number, has_side_effects=True),
        cost_estimate=link_cost(90.0),
        name=name,
    )(part, extra)


class SumAll:
    def __init__(self, x, out, parts, own, send, recv, back_send, back_recv):
        self.x, self.out, self.parts, self.own = x, out, parts, own
        self.send, self.recv, self.back_send, self.back_recv = send, recv, back_send, back_recv
        self.tp_count = lax.axis_size("tp")
        self.total = lax.axis_size("ep") * self.tp_count
        self.me = lax.axis_index("ep") * self.tp_count + lax.axis_index("tp")

    def device(self, d):
        return {"ep": d // self.tp_count, "tp": d % self.tp_count}

    def other(self, i):
        return lax.rem(self.me + i, self.total)

    def each(self, act):
        @pl.loop(1, self.total)
        def _(i):
            act(i)

    def greet(self):
        barrier = pltpu.get_barrier_semaphore()
        self.each(
            lambda i: pl.semaphore_signal(
                barrier, inc=1, device_id=self.device(self.other(i)), device_id_type=MESH
            )
        )
        pl.semaphore_wait(barrier, self.total - 1)

    def outward(self, i):
        to = self.other(i)
        return remote(
            self.x.at[to], self.parts.at[self.me], self.send.at[i], self.recv.at[self.me], self.device(to)
        )

    def inward(self, i):
        origin = self.other(i)
        rows = self.parts.at[origin]
        return remote(rows, rows, self.send.at[i], self.recv.at[origin], self.device(origin))

    def spread(self, i):
        to = self.other(i)
        return remote(
            self.own, self.out.at[self.me], self.back_send.at[i], self.back_recv.at[self.me], self.device(to)
        )

    def returned(self, i):
        origin = self.other(i)
        rows = self.out.at[origin]
        return remote(rows, rows, self.back_send.at[i], self.back_recv.at[origin], self.device(origin))

    def start(self):
        self.each(lambda i: self.outward(i).start())
        self.parts[pl.ds(self.me, 1)] = self.x[pl.ds(self.me, 1)]

    def add(self):
        self.each(lambda i: self.inward(i).wait_recv())
        self.own[...] = jnp.sum(self.parts[...], axis=0)
        self.each(lambda i: self.spread(i).start())
        self.out[pl.ds(self.me, 1)] = self.own[...][None]

    def finish(self):
        self.each(lambda i: self.outward(i).wait_send())
        self.each(lambda i: self.returned(i).wait_recv())
        self.each(lambda i: self.spread(i).wait_send())


def sum_scratch(rows, total):
    dma = pltpu.SemaphoreType.DMA
    return [
        pltpu.VMEM((total, rows, 128), F32), pltpu.VMEM((rows, 128), F32),
        dma((total,)), dma((total,)), dma((total,)), dma((total,)),
    ]


def pack_small(values, total):
    flat = jnp.concatenate([v.reshape(-1) for v in values])
    rows = -(-flat.shape[0] // (total * 128 * 8)) * 8
    return jnp.pad(flat, (0, total * rows * 128 - flat.shape[0])).reshape(total, rows, 128)


def unpack_small(summed, values):
    summed = summed.reshape(-1)
    out, at = [], 0
    for v in values:
        out.append(summed[at : at + v.size].reshape(v.shape))
        at += v.size
    return out


def fill_bias(span_ref, bias, chunk=256):
    keys, length = bias.shape
    query = lax.broadcasted_iota(jnp.int32, (1, length), 1)

    def spans(pos):
        first = (pos >= span_ref[0, 0]) & (pos < span_ref[0, 0] + IMG)
        second = (pos >= span_ref[0, 1]) & (pos < span_ref[0, 1] + IMG)
        return jnp.where(first, 0, jnp.where(second, 1, -1))

    query_span = spans(query)
    query_other = jnp.where(query_span < 0, -2, query_span)
    for start in range(0, keys, chunk):
        key = start + lax.broadcasted_iota(jnp.int32, (chunk, 1), 0)
        ok = (key <= query) | (spans(key) == query_other)
        bias[start : start + chunk, :] = jnp.where(ok, 0.0, MASKED)


def query_tiles(length):
    tile = min(IMG, length)
    return [
        (start, tile, min(length, start + tile + -(-IMG // tile) * tile))
        for start in range(0, length, tile)
    ]


def attention_kernel(
    span_ref, q_ref, k_ref, v_ref, cos_ref, sin_ref, qg_ref, kg_ref, w_out_ref, cot_ref,
    out_ref, lse_ref, rows_ref, cots_ref,
    bias, k_rot, v_t, heads, part, core_rows, x_rows, core_send, core_recv, x_send, x_recv, *sems,
):
    factor = q_ref.shape[-1] ** (-0.5)
    cosine, sine = cos_ref[...], sin_ref[...]
    step = pl.program_id(0)
    size = q_ref.shape[-1]
    me = lax.axis_index("tp")
    x, c = me // 2, me % 2
    other_core, other_x = {"tp": x * 2 + 1 - c}, {"tp": (1 - x) * 2 + c}
    gather = EpGather(halves(cot_ref, 0), halves(cots_ref, 1), sems)

    @pl.when(step == 0)
    def _():
        greet(gather.partners() + [(x >= 0, other_core), (x >= 0, other_x)])
        gather.start()
        fill_bias(span_ref, bias)
        k = k_ref[...]
        k_rot[...] = turn(k * rms_scale(k) * kg_ref[...], cosine, sine).astype(BF)
        v_t[...] = v_ref[...].astype(F32).T.astype(BF)

    @pl.when(step == pl.num_programs(0) - 2)
    def _():
        gather.hop(1)

    q = q_ref[...]
    q_rot = turn(q * rms_scale(q) * qg_ref[...], cosine, sine).astype(BF)
    for start, tile, keys in query_tiles(q.shape[0]):
        cols = slice(start, start + tile)
        s = dot_nt(k_rot[:keys, :], q_rot[cols, :]) * factor + bias[:keys, cols]
        top = jnp.max(s, axis=0, keepdims=True)
        p = jnp.exp(s - top)
        total = jnp.sum(p, axis=0, keepdims=True)
        o_t = dot_nn(v_t[:, :keys], p.astype(BF)) / total
        rows = o_t.T.astype(BF)
        out_ref[cols, :] = rows
        heads[step, cols, :] = rows
        lse_ref[0, :, cols] = top + jnp.log(total)

    @pl.when(step == pl.num_programs(0) - 1)
    def _():
        count = heads.shape[0]
        block = rows_ref.shape[0]

        def project(tp):
            lines = pl.ds(pl.multiple_of(tp * block, block), block)
            rows = jnp.concatenate([heads[h, lines, :] for h in range(count)], axis=1)
            part[tp] = dot_nn(rows, w_out_ref[...]).astype(BF)

        def to_core(xt):
            return remote(
                part.at[xt * 2 + 1 - c], core_rows.at[xt],
                core_send.at[xt], core_recv.at[xt], other_core,
            )

        far, near = part.at[(1 - x) * 2 + c], part.at[x * 2 + c]
        to_x = remote(far, x_rows, x_send, x_recv, other_x)
        project((1 - x) * 2 + 1 - c)
        to_core(1 - x).start()
        project((1 - x) * 2 + c)
        to_core(1 - x).wait_recv()
        add_rows(far, [far, core_rows.at[1 - x]])
        to_x.start()
        project(x * 2 + 1 - c)
        to_core(x).start()
        project(x * 2 + c)
        gather.hop(2)
        to_core(x).wait_recv()
        gather.hop(3)
        to_x.wait_recv()
        add_rows(rows_ref, [near, core_rows.at[x], x_rows])
        gather.finish()
        to_core(1 - x).wait_send()
        to_core(x).wait_send()
        to_x.wait_send()


def plain_attention_kernel(
    span_ref, q_ref, k_ref, v_ref, cos_ref, sin_ref, qg_ref, kg_ref, out_ref, lse_ref,
    bias, k_rot, v_t,
):
    factor = q_ref.shape[-1] ** (-0.5)
    cosine, sine = cos_ref[...], sin_ref[...]

    @pl.when(pl.program_id(0) == 0)
    def _():
        fill_bias(span_ref, bias)
        k = k_ref[...]
        k_rot[...] = turn(k * rms_scale(k) * kg_ref[...], cosine, sine).astype(BF)
        v_t[...] = v_ref[...].astype(F32).T.astype(BF)

    q = q_ref[...]
    q_rot = turn(q * rms_scale(q) * qg_ref[...], cosine, sine).astype(BF)
    for start, tile, keys in query_tiles(q.shape[0]):
        cols = slice(start, start + tile)
        s = dot_nt(k_rot[:keys, :], q_rot[cols, :]) * factor + bias[:keys, cols]
        top = jnp.max(s, axis=0, keepdims=True)
        p = jnp.exp(s - top)
        total = jnp.sum(p, axis=0, keepdims=True)
        o_t = dot_nn(v_t[:, :keys], p.astype(BF)) / total
        out_ref[cols, :] = o_t.T.astype(BF)
        lse_ref[0, :, cols] = top + jnp.log(total)


def attention(span, q, k, v, cosine, sine, q_gain, k_gain, w_out, cotangent, number):
    length, size = k.shape
    heads = q.shape[1] // size
    whole = pl.BlockSpec((length, size), lambda h: (0, 0))
    head = pl.BlockSpec((length, size), lambda h: (0, h))
    gain = pl.BlockSpec((1, size), lambda h: (0, 0))
    in_specs = [
        pl.BlockSpec(memory_space=pltpu.SMEM), head, whole, whole, whole, whole, gain, gain,
    ]
    out_specs = [head, pl.BlockSpec((1, 1, length), lambda h: (h, 0, 0))]
    out_shape = [
        jax.ShapeDtypeStruct((length, heads * size), BF),
        jax.ShapeDtypeStruct((heads, 1, length), F32),
    ]
    scratch = [
        pltpu.VMEM((length, length), F32),
        pltpu.VMEM((length, size), BF),
        pltpu.VMEM((size, length), BF),
    ]
    args = (span, q, k, v, cosine, sine, q_gain, k_gain)
    ep_count, tp_count = lax.axis_size("ep"), lax.axis_size("tp")
    if ep_count != 2 * Z_AXIS:
        out, lse = pl.pallas_call(
            plain_attention_kernel,
            grid=(heads,),
            in_specs=in_specs,
            out_specs=out_specs,
            out_shape=out_shape,
            scratch_shapes=scratch,
            compiler_params=params(),
            name="plain_attention",
        )(*args)
        rows = lax.psum_scatter(
            dot_nn(out, w_out).astype(BF), "tp", scatter_dimension=0, tiled=True
        )
        return out, lse, rows.astype(F32), lax.all_gather(cotangent, "ep")
    block, width = cotangent.shape
    dma = pltpu.SemaphoreType.DMA
    return pl.pallas_call(
        attention_kernel,
        grid=(heads,),
        in_specs=in_specs + [pl.BlockSpec(w_out.shape, lambda h: (0, 0)), ANY],
        out_specs=out_specs + [pl.BlockSpec((block, width), lambda h: (0, 0)), ANY],
        out_shape=out_shape
        + [
            jax.ShapeDtypeStruct((block, width), F32),
            jax.ShapeDtypeStruct((ep_count, block, width), BF),
        ],
        scratch_shapes=scratch
        + [
            pltpu.VMEM((heads, length, size), BF),
            pltpu.VMEM((tp_count, block, width), BF),
            pltpu.VMEM((2, block, width), BF),
            pltpu.VMEM((block, width), BF),
            dma((2,)), dma((2,)), dma, dma,
        ]
        + gather_sems(2),
        compiler_params=params(collective_id=number, has_side_effects=True),
        cost_estimate=link_cost(90.0),
        name="attention",
    )(*args, w_out, cotangent)


def norm_back(grads, rows, gain):
    scale = rms_scale(rows)
    gain_part = jnp.sum(grads * rows * scale, axis=0, keepdims=True)
    inner = grads * gain
    mean = jnp.mean(inner * rows, axis=-1, keepdims=True)
    return scale * inner - rows * (scale * scale * scale * mean), gain_part


def plain_attention_back_kernel(
    span_ref, q_ref, k_ref, v_ref, grad_ref, lse_ref, cos_ref, sin_ref, qg_ref, kg_ref,
    dq_ref, dk_ref, dv_ref, dqg_ref, dkg_ref,
    bias, k_rot, k_t, dk_acc, dv_acc, dq_t,
):
    factor = q_ref.shape[-1] ** (-0.5)
    cosine, sine = cos_ref[...], sin_ref[...]
    step = pl.program_id(0)

    @pl.when(step == 0)
    def _():
        fill_bias(span_ref, bias)
        k = k_ref[...]
        rotated = turn(k * rms_scale(k) * kg_ref[...], cosine, sine)
        k_rot[...] = rotated.astype(BF)
        k_t[...] = rotated.T.astype(BF)
        dk_acc[...] = jnp.zeros_like(dk_acc)
        dv_acc[...] = jnp.zeros_like(dv_acc)
        dqg_ref[...] = jnp.zeros_like(dqg_ref)

    q = q_ref[...]
    q_rot = turn(q * rms_scale(q) * qg_ref[...], cosine, sine).astype(BF)
    for start, tile, keys in query_tiles(q.shape[0]):
        cols = slice(start, start + tile)
        s = dot_nt(k_rot[:keys, :], q_rot[cols, :]) * factor + bias[:keys, cols]
        p = jnp.exp(s - lse_ref[0, :, cols])
        grad = grad_ref[cols, :]
        dp = dot_nt(v_ref[:keys, :], grad)
        mean = jnp.sum(p * dp, axis=0, keepdims=True)
        raw = (p * (dp - mean) * factor).astype(BF)
        dq_t[:, cols] = dot_nn(k_t[:, :keys], raw)
        dk_acc[:keys, :] += dot_nn(raw, q_rot[cols, :])
        dv_acc[:keys, :] += dot_nn(p.astype(BF), grad)
    back, gain_part = norm_back(turn_back(dq_t[...].T, cosine, sine), q, qg_ref[...])
    dq_ref[...] = back.astype(BF)
    dqg_ref[...] += gain_part

    @pl.when(step == pl.num_programs(0) - 1)
    def _():
        back, gain_part = norm_back(turn_back(dk_acc[...], cosine, sine), k_ref[...], kg_ref[...])
        dk_ref[...] = back.astype(BF)
        dkg_ref[...] = gain_part
        dv_ref[...] = dv_acc[...].astype(BF)


def plain_attention_back(span, q, k, v, grads, lse, cosine, sine, q_gain, k_gain):
    length, size = k.shape
    heads = q.shape[1] // size
    whole = pl.BlockSpec((length, size), lambda h: (0, 0))
    head = pl.BlockSpec((length, size), lambda h: (0, h))
    gain = pl.BlockSpec((1, size), lambda h: (0, 0))
    return pl.pallas_call(
        plain_attention_back_kernel,
        grid=(heads,),
        in_specs=[
            pl.BlockSpec(memory_space=pltpu.SMEM), head, whole, whole, head,
            pl.BlockSpec((1, 1, length), lambda h: (h, 0, 0)), whole, whole, gain, gain,
        ],
        out_specs=[head, whole, whole, gain, gain],
        out_shape=[
            jax.ShapeDtypeStruct((length, heads * size), BF),
            jax.ShapeDtypeStruct((length, size), BF),
            jax.ShapeDtypeStruct((length, size), BF),
            jax.ShapeDtypeStruct((1, size), F32),
            jax.ShapeDtypeStruct((1, size), F32),
        ],
        scratch_shapes=[
            pltpu.VMEM((length, length), F32),
            pltpu.VMEM((length, size), BF),
            pltpu.VMEM((size, length), BF),
            pltpu.VMEM((length, size), F32),
            pltpu.VMEM((length, size), F32),
            pltpu.VMEM((size, length), F32),
        ],
        compiler_params=params(),
        name="plain_attention_back",
    )(span, q, k, v, grads, lse, cosine, sine, q_gain, k_gain)


def attention_back_kernel(
    span_ref, q_ref, k_ref, v_ref, lse_ref, cos_ref, sin_ref, qg_ref, kg_ref,
    w_out_ref, rows_ref, part_ref, hidden_ref,
    dq_ref, dk_ref, dv_ref, dqg_ref, dkg_ref, branch_ref, output_ref,
    bias, k_rot, k_t, dk_acc, dv_acc, dq_t, branch, grads,
    own_sem, out_sem, core_send, core_recv, x_send, x_recv, *refs,
):
    factor = q_ref.shape[-1] ** (-0.5)
    size = q_ref.shape[-1]
    cosine, sine = cos_ref[...], sin_ref[...]
    step = pl.program_id(0)
    me = lax.axis_index("tp")
    x, c = me // 2, me % 2
    other_core, other_x = {"tp": x * 2 + 1 - c}, {"tp": (1 - x) * 2 + c}
    reduce = EpReduce(halves(part_ref, 1), refs[:6], refs[6:])
    block = rows_ref.shape[0]
    near_other, far, far_other = x * 2 + 1 - c, (1 - x) * 2 + c, (1 - x) * 2 + 1 - c

    def to_core(slot, src, tp):
        return remote(src, branch.at[tp], core_send.at[slot], core_recv.at[slot], other_core)

    def to_x(tp):
        return remote(rows_ref, branch.at[tp], x_send, x_recv, other_x)

    def own_rows():
        return pltpu.make_async_copy(rows_ref, branch.at[me], own_sem)

    def whole_branch():
        return pltpu.make_async_copy(branch, branch_ref, out_sem)

    @pl.when(step == 0)
    def _():
        greet(reduce.partners() + [(x >= 0, other_core), (x >= 0, other_x)])
        to_x(me).start()
        to_core(0, rows_ref, me).start()
        own_rows().start()
        for k in range(Z_AXIS):
            reduce.send_side(k)
        fill_bias(span_ref, bias)
        k = k_ref[...]
        rotated = turn(k * rms_scale(k) * kg_ref[...], cosine, sine)
        k_rot[...] = rotated.astype(BF)
        k_t[...] = rotated.T.astype(BF)
        dk_acc[...] = jnp.zeros_like(dk_acc)
        dv_acc[...] = jnp.zeros_like(dv_acc)
        dqg_ref[...] = jnp.zeros_like(dqg_ref)

        def head_grads(tp):
            lines = pl.ds(pl.multiple_of(tp * block, block), block)
            rows = dot_nt(branch[tp], w_out_ref[...]).astype(BF)
            for h in range(grads.shape[0]):
                grads[h, lines, :] = rows[:, h * size : (h + 1) * size]

        own_rows().wait()
        head_grads(me)
        to_core(0, rows_ref, near_other).wait_recv()
        head_grads(near_other)
        reduce.step(0)
        to_x(far).wait_recv()
        to_core(1, branch.at[far], far).start()
        head_grads(far)
        to_core(1, branch.at[far], far_other).wait_recv()
        head_grads(far_other)
        whole_branch().start()

    for k, head in ((1, 1), (2, 5)):

        @pl.when(step == head)
        def _(k=k):
            reduce.step(k)

    q = q_ref[...]
    q_rot = turn(q * rms_scale(q) * qg_ref[...], cosine, sine).astype(BF)
    for start, tile, keys in query_tiles(q.shape[0]):
        cols = slice(start, start + tile)
        s = dot_nt(k_rot[:keys, :], q_rot[cols, :]) * factor + bias[:keys, cols]
        p = jnp.exp(s - lse_ref[0, :, cols])
        grad = grads[step, cols, :]
        dp = dot_nt(v_ref[:keys, :], grad)
        mean = jnp.sum(p * dp, axis=0, keepdims=True)
        raw = (p * (dp - mean) * factor).astype(BF)
        dq_t[:, cols] = dot_nn(k_t[:, :keys], raw)
        dk_acc[:keys, :] += dot_nn(raw, q_rot[cols, :])
        dv_acc[:keys, :] += dot_nn(p.astype(BF), grad)
    back, gain_part = norm_back(turn_back(dq_t[...].T, cosine, sine), q, qg_ref[...])
    dq_ref[...] = back.astype(BF)
    dqg_ref[...] += gain_part

    @pl.when(step == pl.num_programs(0) - 1)
    def _():
        back, gain_part = norm_back(turn_back(dk_acc[...], cosine, sine), k_ref[...], kg_ref[...])
        dk_ref[...] = back.astype(BF)
        dkg_ref[...] = gain_part
        dv_ref[...] = dv_acc[...].astype(BF)
        reduce.step(Z_AXIS - 1)
        pairs = zip(halves(output_ref, 0), halves(hidden_ref, 0))
        for a, (rows, residual) in enumerate(pairs):
            reduce.own(a, lambda terms, rows=rows, residual=residual: add_rows(rows, terms + [residual]))
        reduce.sent()
        whole_branch().wait()
        to_x(me).wait_send()
        to_core(0, rows_ref, me).wait_send()
        to_core(1, branch.at[far], far).wait_send()


def attention_back(
    span, q, k, v, lse, cosine, sine, q_gain, k_gain, w_out, d_rows, out_part, hidden, number
):
    length, size = k.shape
    heads = q.shape[1] // size
    ep_count, tp_count = lax.axis_size("ep"), lax.axis_size("tp")
    if ep_count != 2 * Z_AXIS:
        branch = lax.all_gather(d_rows, "tp", axis=0, tiled=True)
        grads = dot_nt(branch, w_out).astype(BF)
        mine = lax.psum_scatter(out_part, "ep", scatter_dimension=0)
        back = plain_attention_back(span, q, k, v, grads, lse, cosine, sine, q_gain, k_gain)
        return *back, branch, (hidden + mine.astype(F32)).astype(BF)
    block, width = d_rows.shape
    whole = pl.BlockSpec((length, size), lambda h: (0, 0))
    head = pl.BlockSpec((length, size), lambda h: (0, h))
    gain = pl.BlockSpec((1, size), lambda h: (0, 0))
    rows = pl.BlockSpec((block, width), lambda h: (0, 0))
    dma = pltpu.SemaphoreType.DMA
    *back, branch, output = pl.pallas_call(
        attention_back_kernel,
        grid=(heads,),
        in_specs=[
            pl.BlockSpec(memory_space=pltpu.SMEM), head, whole, whole,
            pl.BlockSpec((1, 1, length), lambda h: (h, 0, 0)), whole, whole, gain, gain,
            pl.BlockSpec(w_out.shape, lambda h: (0, 0)), ANY, ANY, rows,
        ],
        out_specs=[head, whole, whole, gain, gain, ANY, rows],
        out_shape=[
            jax.ShapeDtypeStruct((length, heads * size), BF),
            jax.ShapeDtypeStruct((length, size), BF),
            jax.ShapeDtypeStruct((length, size), BF),
            jax.ShapeDtypeStruct((1, size), F32),
            jax.ShapeDtypeStruct((1, size), F32),
            jax.ShapeDtypeStruct((tp_count, block, width), BF),
            jax.ShapeDtypeStruct((block, width), BF),
        ],
        scratch_shapes=[
            pltpu.VMEM((length, length), F32),
            pltpu.VMEM((length, size), BF),
            pltpu.VMEM((size, length), BF),
            pltpu.VMEM((length, size), F32),
            pltpu.VMEM((length, size), F32),
            pltpu.VMEM((size, length), F32),
            pltpu.VMEM((tp_count, block, width), BF),
            pltpu.VMEM((heads, length, size), BF),
        ]
        + [dma, dma, dma((2,)), dma((2,)), dma, dma]
        + reduce_scratch((block // 2, width), BF) * 2
        + reduce_sems(2),
        compiler_params=params(collective_id=number, has_side_effects=True),
        cost_estimate=link_cost(100.0),
        name="attention_back",
    )(span, q, k, v, lse, cosine, sine, q_gain, k_gain, w_out, d_rows, out_part, hidden)
    return *back, branch.reshape(-1, width), output


def projection_grads_kernel(
    normed, dq, dk, dv, heads, branch, wq, wk, wv, x_rows, d_hidden, gain, small,
    gq_ref, gk_ref, gv_ref, gout_ref, inputs_grad, gain_grad, small_sum,
    blocks, out_blocks, part, core_rows, far_rows, gain_own, gains,
    core_send, core_recv, x_send, x_recv, gain_send, gain_recv, *refs,
):
    me = lax.axis_index("tp")
    x, c = me // 2, me % 2
    other_core, other_x = {"tp": x * 2 + 1 - c}, {"tp": (1 - x) * 2 + c}
    sums = SumAll(small, small_sum, *refs[:6])
    reduce = EpReduce([blocks, out_blocks], refs[6:10], refs[10:], loaded=False)
    order, y = reduce.order, reduce.y
    rows, width = inputs_grad.shape
    nq, nk = dq.shape[1], dk.shape[1]

    sums.greet()
    sums.start()

    def fill(j):
        cols = pl.ds(pl.multiple_of(j * rows, rows), rows)
        left = normed[:, cols].T
        blocks[j, :, 0:nq] = dot_nn(left, dq[...]).astype(BF)
        blocks[j, :, nq : nq + nk] = dot_nn(left, dk[...]).astype(BF)
        blocks[j, :, nq + nk : nq + 2 * nk] = dot_nn(left, dv[...]).astype(BF)
        out_blocks[j] = dot_nn(branch[:, cols].T, heads[...]).astype(BF)

    def spread_back(tp):
        lines = pl.ds(pl.multiple_of(tp * rows, rows), rows)
        for start in range(0, width, width // 4):
            cols = slice(start, start + width // 4)
            part[tp, :, cols] = (
                dot_nt(dq[lines, :], wq[cols, :])
                + dot_nt(dk[lines, :], wk[cols, :])
                + dot_nt(dv[lines, :], wv[cols, :])
            ).astype(BF)

    def to_core(xt):
        return remote(
            part.at[xt * 2 + 1 - c], core_rows.at[xt], core_send.at[xt], core_recv.at[xt], other_core
        )

    far, near = part.at[(1 - x) * 2 + c], part.at[x * 2 + c]
    to_x = remote(far, far_rows, x_send, x_recv, other_x)

    for k in range(2):
        fill(order[k] * 2 + 1 - y)
        reduce.send_side(k)
    spread_back((1 - x) * 2 + 1 - c)
    to_core(1 - x).start()
    spread_back((1 - x) * 2 + c)
    to_core(1 - x).wait_recv()
    add_rows(far, [far, core_rows.at[1 - x]])
    to_x.start()
    for k in range(2, Z_AXIS):
        fill(order[k] * 2 + 1 - y)
        reduce.send_side(k)
    fill(order[0] * 2 + y)
    reduce.step(0)
    spread_back(x * 2 + 1 - c)
    to_core(x).start()
    spread_back(x * 2 + c)
    for k in range(1, Z_AXIS):
        fill(order[k] * 2 + y)
    reduce.step(1)
    to_core(x).wait_recv()
    to_x.wait_recv()

    chunk = 32
    gain_own[...] = jnp.zeros_like(gain_own)

    @pl.loop(0, rows // chunk)
    def _(i):
        lines = pl.ds(pl.multiple_of(i * chunk, chunk), chunk)
        grad = near[lines, :].astype(F32) + core_rows[x, lines, :].astype(F32)
        grad = grad + far_rows[lines, :].astype(F32)
        back, gain_part = norm_back(grad, x_rows[lines, :].astype(F32), gain[...])
        inputs_grad[lines, :] = d_hidden[lines, :] + back
        gain_own[...] += gain_part

    def tell(i):
        to = sums.other(i)
        return remote(
            gain_own, gains.at[sums.me], gain_send.at[i], gain_recv.at[sums.me], sums.device(to)
        )

    def heard(i):
        origin = sums.other(i)
        row = gains.at[origin]
        return remote(row, row, gain_send.at[i], gain_recv.at[origin], sums.device(origin))

    sums.each(lambda i: tell(i).start())
    gains[pl.ds(sums.me, 1)] = gain_own[...][None]
    reduce.step(2)
    sums.add()
    reduce.step(3)

    def total_of(terms, lines):
        value = terms[0][lines, :].astype(F32)
        for term in terms[1:]:
            value = value + term[lines, :].astype(F32)
        return value

    def write(terms):
        for start in range(0, rows, 128):
            lines = slice(start, start + 128)
            value = total_of(terms, lines)
            gq_ref[lines, :] = value[:, 0:nq]
            gk_ref[lines, :] = value[:, nq : nq + nk]
            gv_ref[lines, :] = value[:, nq + nk :]

    def write_out(terms):
        for start in range(0, rows, 128):
            lines = slice(start, start + 128)
            gout_ref[:, lines] = total_of(terms, lines).T

    sums.each(lambda i: heard(i).wait_recv())
    gain_grad[...] = jnp.sum(gains[...], axis=0)
    reduce.own(0, write)
    reduce.own(1, write_out)
    reduce.sent()
    to_core(1 - x).wait_send()
    to_core(x).wait_send()
    to_x.wait_send()
    sums.each(lambda i: tell(i).wait_send())
    sums.finish()


def projection_grads(
    normed, dq, dk, dv, heads, branch, wq, wk, wv, x_rows, d_hidden, gain, small_values, number
):
    rows, width = x_rows.shape
    ep_count, tp_count = lax.axis_size("ep"), lax.axis_size("tp")
    total = ep_count * tp_count
    small = pack_small(small_values, total)
    if ep_count != 2 * Z_AXIS:

        def over_sequences(part, dim):
            return lax.psum_scatter(
                part.astype(BF), "ep", scatter_dimension=dim, tiled=True
            ).astype(F32)

        d_normed = (dot_nt(dq, wq) + dot_nt(dk, wk) + dot_nt(dv, wv)).astype(BF)
        d_mine = lax.psum_scatter(d_normed, "tp", scatter_dimension=0, tiled=True)
        back, gain_part = norm_back(d_mine.astype(F32), x_rows.astype(F32), gain)
        gain_sum, small_sum = lax.psum((gain_part, small), ("ep", "tp"))
        return (
            over_sequences(dot_tn(normed, dq), 0),
            over_sequences(dot_tn(normed, dk), 0),
            over_sequences(dot_tn(normed, dv), 0),
            over_sequences(dot_tn(heads, branch), 1),
            d_hidden + back,
            gain_sum,
            unpack_small(small_sum, small_values),
        )
    nq, nk = dq.shape[1], dk.shape[1]
    nh = heads.shape[1]
    vmem = pl.BlockSpec(memory_space=pltpu.VMEM)
    dma = pltpu.SemaphoreType.DMA
    *grads, small_sum = pl.pallas_call(
        projection_grads_kernel,
        in_specs=[vmem] * 13,
        out_specs=[vmem] * 7,
        out_shape=[
            jax.ShapeDtypeStruct((rows, nq), F32),
            jax.ShapeDtypeStruct((rows, nk), F32),
            jax.ShapeDtypeStruct((rows, nk), F32),
            jax.ShapeDtypeStruct((nh, rows), F32),
            jax.ShapeDtypeStruct((rows, width), F32),
            jax.ShapeDtypeStruct((1, width), F32),
            jax.ShapeDtypeStruct(small.shape, F32),
        ],
        scratch_shapes=[
            pltpu.VMEM((ep_count, rows, nq + 2 * nk), BF),
            pltpu.VMEM((ep_count, rows, nh), BF),
            pltpu.VMEM((tp_count, rows, width), BF),
            pltpu.VMEM((2, rows, width), BF),
            pltpu.VMEM((rows, width), BF),
            pltpu.VMEM((1, width), F32),
            pltpu.VMEM((total, 1, width), F32),
            dma((2,)), dma((2,)), dma, dma, dma((total,)), dma((total,)),
        ]
        + sum_scratch(small.shape[1], total)
        + reduce_scratch((rows, nq + 2 * nk), BF, loaded=False)
        + reduce_scratch((rows, nh), BF, loaded=False)
        + reduce_sems(2),
        compiler_params=params(collective_id=number, has_side_effects=True),
        cost_estimate=link_cost(110.0),
        name="projection_grads",
    )(normed, dq, dk, dv, heads, branch, wq, wk, wv, x_rows, d_hidden, gain, small)
    return *grads, unpack_small(small_sum, small_values)


def select_kernel(slot_ref, x_ref, c_ref, xs_ref, cs_ref):
    local, _, capacity, width = xs_ref.shape
    rows = x_ref.shape[1]
    place = jnp.concatenate(
        [
            (
                slot_ref[0, e : e + 1, :]
                == lax.broadcasted_iota(jnp.int32, (capacity, rows), 0)
            ).astype(F32)
            for e in range(local)
        ],
        axis=0,
    ).astype(BF)
    xs_ref[...] = dot_nn(place, x_ref[0]).astype(BF).reshape(xs_ref.shape)
    cs_ref[...] = dot_nn(place, c_ref[0]).astype(BF).reshape(cs_ref.shape)


def select_rows(slots, tokens, cots, capacity):
    blocks, local, rows = slots.shape
    width = tokens.shape[-1]
    block = pl.BlockSpec((1, rows, width), lambda b: (b, 0, 0))
    out = pl.BlockSpec((local, 1, capacity, width), lambda b: (0, b, 0, 0))
    shape = jax.ShapeDtypeStruct((local, blocks, capacity, width), BF)
    return pl.pallas_call(
        select_kernel,
        grid=(blocks,),
        in_specs=[pl.BlockSpec((1, local, rows), lambda b: (b, 0, 0)), block, block],
        out_specs=[out, out],
        out_shape=[shape, shape],
        compiler_params=params(),
        name="select_rows",
    )(slots, tokens, cots)


def pack_kernel(gate_ref, up_ref, down_ref, out_ref):
    for kind, ref in enumerate((gate_ref, up_ref, down_ref)):
        out_ref[kind, 0] = ref[0]


def pack_weights(weights, first, count):
    _, hidden, width = weights[0].shape
    block = pl.BlockSpec((1, hidden, width), lambda e: (first + e, 0, 0))
    return pl.pallas_call(
        pack_kernel,
        grid=(count,),
        in_specs=[block] * 3,
        out_specs=pl.BlockSpec((3, 1, hidden, width), lambda e: (0, e, 0, 0)),
        out_shape=jax.ShapeDtypeStruct((3, count, hidden, width), BF),
        compiler_params=params(),
        name="pack_weights",
    )(*weights)


def expert_kernel(
    x_ref, c_ref, w_ref, gate_ref, out_ref, dx_ref, act_ref, dg_ref, du_ref, dgate_ref
):
    width = x_ref.shape[-1]
    x, c = x_ref[0], c_ref[0]
    w_gate = w_ref[:, 0, 0].reshape(-1, width)
    w_up = w_ref[:, 1, 0].reshape(-1, width)
    w_down = w_ref[:, 2, 0].reshape(-1, width)
    gate = gate_ref[0]
    gate_pre = dot_nt(x, w_gate)
    up_pre = dot_nt(x, w_up)
    raw = dot_nt(c, w_down)
    sig = jax.nn.sigmoid(gate_pre)
    silu = gate_pre * sig
    act = silu * up_pre
    dgate_ref[0] = jnp.sum(act * raw, axis=-1, keepdims=True)
    act_low = (act * gate).astype(BF)
    d_act = raw * gate
    d_gate = (d_act * up_pre * sig * (1.0 + gate_pre * (1.0 - sig))).astype(BF)
    d_up = (d_act * silu).astype(BF)
    act_ref[0] = act_low
    dg_ref[0] = d_gate
    du_ref[0] = d_up
    out_ref[0] = dot_nn(act_low, w_down).astype(BF)
    dx_ref[0] = (dot_nn(d_gate, w_gate) + dot_nn(d_up, w_up)).astype(BF)


def experts_both_ways(x_slots, c_slots, w_all, slot_gate, first):
    _, number, width = x_slots.shape
    parts, _, local, hidden, _ = w_all.shape
    tile = number // 2
    taken = pl.BlockSpec((1, tile, width), lambda e, i: (first + e, i, 0))
    wide = pl.BlockSpec((1, tile, width), lambda e, i: (e, i, 0))
    mid = pl.BlockSpec((1, tile, parts * hidden), lambda e, i: (e, i, 0))
    thin = pl.BlockSpec((1, tile, 1), lambda e, i: (e, i, 0))
    wide_shape = jax.ShapeDtypeStruct((local, number, width), BF)
    mid_shape = jax.ShapeDtypeStruct((local, number, parts * hidden), BF)
    return pl.pallas_call(
        expert_kernel,
        grid=(local, 2),
        in_specs=[
            taken, taken,
            pl.BlockSpec((parts, 3, 1, hidden, width), lambda e, i: (0, 0, e, 0, 0)),
            pl.BlockSpec((1, tile, 1), lambda e, i: (first + e, i, 0)),
        ],
        out_specs=[wide, wide, mid, mid, mid, thin],
        out_shape=[
            wide_shape, wide_shape, mid_shape, mid_shape, mid_shape,
            jax.ShapeDtypeStruct((local, number, 1), F32),
        ],
        compiler_params=params(),
        name="experts_both_ways",
    )(x_slots, c_slots, w_all, slot_gate)


def expert_grads_kernel(x_ref, c_ref, act_ref, dg_ref, du_ref, out_ref):
    parts, _, _, hidden, width = out_ref.shape
    x, c = x_ref[0], c_ref[0]
    out_ref[:, 0, 0] = dot_tn(dg_ref[0], x).astype(BF).reshape(parts, hidden, width)
    out_ref[:, 1, 0] = dot_tn(du_ref[0], x).astype(BF).reshape(parts, hidden, width)
    out_ref[:, 2, 0] = dot_tn(act_ref[0], c).astype(BF).reshape(parts, hidden, width)


def expert_grads(x_slots, c_slots, act, d_gate, d_up, parts, first):
    local, number, inner = act.shape
    width = x_slots.shape[-1]
    wide = pl.BlockSpec((1, number, width), lambda e: (first + e, 0, 0))
    mid = pl.BlockSpec((1, number, inner), lambda e: (e, 0, 0))
    return pl.pallas_call(
        expert_grads_kernel,
        grid=(local,),
        in_specs=[wide, wide, mid, mid, mid],
        out_specs=pl.BlockSpec(
            (parts, 3, 1, inner // parts, width), lambda e: (0, 0, e, 0, 0)
        ),
        out_shape=jax.ShapeDtypeStruct((parts, 3, local, inner // parts, width), BF),
        compiler_params=params(),
        name="expert_grads",
    )(x_slots, c_slots, act, d_gate, d_up)


def combine_kernel(
    first_ref, slot_ref, dxa_ref, dxb_ref, outa_ref, outb_ref, dgate_ref, dx_sum_ref, out_sum_ref, pay_ref
):
    _, _, capacity, width = dxa_ref.shape
    local = slot_ref.shape[2]
    rows = slot_ref.shape[1]
    lane = lax.broadcasted_iota(jnp.int32, (rows, local * capacity), 1)
    half = pay_ref.shape[2] // 2
    column = lax.broadcasted_iota(jnp.int32, (rows, 2 * half), 1)
    total = jnp.zeros((rows, local * capacity), F32)
    pay = jnp.zeros(column.shape, F32)
    for e in range(local):
        hit = lane == slot_ref[0, :, e : e + 1] + e * capacity
        total = jnp.where(hit, 1.0, total)
        value = jnp.sum(jnp.where(hit, dgate_ref[0], 0.0), axis=1, keepdims=True)
        high = value.astype(BF).astype(F32)
        pay = jnp.where(column == first_ref[0, 0] + e, high, pay)
        pay = jnp.where(column == first_ref[0, 0] + e + half, value - high, pay)
    place = total.astype(BF)

    def both(a_ref, b_ref):
        pair = [ref[...].reshape(-1, width) for ref in (a_ref, b_ref)]
        return dot_nn(place, jnp.concatenate(pair, axis=0)).astype(BF)

    dx_sum_ref[0] = both(dxa_ref, dxb_ref)
    out_sum_ref[0] = both(outa_ref, outb_ref)
    pay_ref[0] = pay.astype(BF)


def combine_rows(first, slots_t, dx, out, d_gate_slots, experts):
    blocks, rows, local = slots_t.shape
    _, _, capacity, width = dx[0].shape
    lanes = -(-2 * experts // 128) * 128
    slot = pl.BlockSpec((local // 2, 1, capacity, width), lambda b: (0, b, 0, 0))
    block = pl.BlockSpec((1, rows, width), lambda b: (b, 0, 0))
    shape = jax.ShapeDtypeStruct((blocks, rows, width), BF)
    return pl.pallas_call(
        combine_kernel,
        grid=(blocks,),
        in_specs=[
            pl.BlockSpec(memory_space=pltpu.SMEM),
            pl.BlockSpec((1, rows, local), lambda b: (b, 0, 0)), slot, slot, slot, slot,
            pl.BlockSpec((1, 1, local * capacity), lambda b: (b, 0, 0)),
        ],
        out_specs=[block, block, pl.BlockSpec((1, rows, lanes), lambda b: (b, 0, 0))],
        out_shape=[shape, shape, jax.ShapeDtypeStruct((blocks, rows, lanes), BF)],
        compiler_params=params(),
        name="combine_rows",
    )(first, slots_t, *dx, *out, d_gate_slots)


def on_device(
    inputs,
    attn_gain,
    w_query,
    key_weight_matrix,
    value_weight_matrix,
    query_gain,
    key_gain,
    w_out,
    route_gain,
    w_router,
    w_gate,
    w_up,
    w_down,
    routes,
    image_starts,
    cotangent,
):
    tp_count = lax.axis_size("tp")
    ep_count = lax.axis_size("ep")
    tp_index = lax.axis_index("tp")
    ep_index = lax.axis_index("ep")
    length = inputs.shape[0]
    width = inputs.shape[1]
    rows = cotangent.shape[0]
    head_dim = query_gain.shape[0]
    local_experts = w_gate.shape[0]
    experts = local_experts * ep_count
    top = routes.shape[1]
    capacity = -(-(3 * rows * top // (2 * experts)) // 16) * 16

    pair = local_experts // 2

    weights = (w_gate.transpose(0, 2, 1), w_up.transpose(0, 2, 1), w_down)
    w_first = lax.all_gather(pack_weights(weights, 0, pair), "tp")

    inputs_f = inputs.astype(F32)
    attn_scale = rms_scale(inputs_f)
    normed = (inputs_f * attn_scale * attn_gain).astype(BF)
    queries = dot_nn(normed, w_query)
    key_rows = dot_nn(normed, key_weight_matrix)
    values = dot_nn(normed, value_weight_matrix).astype(BF)
    cosine, sine = rope_tables(length, head_dim)
    q_gain, k_gain = query_gain[None], key_gain[None]
    queries, second = lax.optimization_barrier((queries, pack_weights(weights, pair, pair)))
    w_second = lax.all_gather(second, "tp")
    heads, lse, attn_rows, cot_all = attention(
        image_starts, queries, key_rows, values, cosine, sine, q_gain, k_gain, w_out, cotangent, 0
    )
    x_rows = lax.dynamic_slice_in_dim(inputs, tp_index * rows, rows, 0)
    hidden = x_rows.astype(F32) + attn_rows
    route_scale = rms_scale(hidden)
    moe_in = (hidden * route_scale * route_gain).astype(BF)
    moe_in, w_first = lax.optimization_barrier((moe_in, w_first))
    tokens_all = gather_ep(moe_in, 1, "gather_rows")

    logits = dot_nn(moe_in, w_router)
    router_probs = plain_softmax(logits)
    expert_ids = jnp.arange(experts, dtype=jnp.int32)
    ring_routes = lax.dynamic_index_in_dim(
        routes.reshape(ep_count, tp_count, rows, top), tp_index, 1, keepdims=False
    )
    my_routes = lax.dynamic_index_in_dim(ring_routes, ep_index, 0, keepdims=False)

    def routed_softmax(scores, picked):
        kept = jnp.where(picked, scores, MASKED)
        expo = jnp.where(picked, jnp.exp(kept - jnp.max(kept, axis=-1, keepdims=True)), 0.0)
        return expo / jnp.sum(expo, axis=-1, keepdims=True)

    my_pick = jnp.any(my_routes[:, :, None] == expert_ids[None, None, :], axis=1)
    gates = routed_softmax(logits, my_pick)
    all_pick = jnp.any(ring_routes[..., None] == expert_ids, axis=2)
    gates_all = routed_softmax(dot_nn(tokens_all.reshape(-1, width), w_router).reshape(ep_count, rows, experts), all_pick)
    gate_of = lax.dynamic_slice_in_dim(gates_all, ep_index * local_experts, local_experts, 2)
    mask = lax.dynamic_slice_in_dim(all_pick, ep_index * local_experts, local_experts, 2)
    earlier = (jnp.arange(rows)[:, None] > jnp.arange(rows)[None, :]).astype(BF)
    slots_t = jnp.einsum(
        "tu,bue->bte", earlier, mask.astype(BF), preferred_element_type=F32
    ).astype(jnp.int32)
    slots_t = jnp.where(mask, slots_t, NOWHERE)
    slots = slots_t.transpose(0, 2, 1)
    place = slots[:, :, None, :] == jnp.arange(capacity, dtype=jnp.int32)[:, None]
    slot_gate = jnp.sum(jnp.where(place, gate_of.transpose(0, 2, 1)[:, :, None, :], 0.0), axis=-1)
    slot_gate = slot_gate.transpose(1, 0, 2).reshape(local_experts, ep_count * capacity, 1)

    x_slots, c_slots = select_rows(slots, tokens_all, cot_all, capacity)
    flat = (local_experts, ep_count * capacity, width)
    x_slots, c_slots = x_slots.reshape(flat), c_slots.reshape(flat)

    def over_rings(grads):
        return lax.psum_scatter(grads.reshape(-1, width), "tp", scatter_dimension=0, tiled=True)

    out_a, dx_a, *inner_a, dg_a = experts_both_ways(x_slots, c_slots, w_first, slot_gate, 0)
    grads_a = expert_grads(x_slots, c_slots, *inner_a, tp_count, 0)
    x_slots, grads_a = lax.optimization_barrier((x_slots, grads_a))
    mine_a = over_rings(grads_a)
    out_b, dx_b, *inner_b, dg_b = experts_both_ways(x_slots, c_slots, w_second, slot_gate, pair)
    grads_b = expert_grads(x_slots, c_slots, *inner_b, tp_count, pair)
    deep = (pair, ep_count, capacity, width)
    dx_part, out_part, gate_part = combine_rows(
        (ep_index * local_experts).reshape(1, 1),
        slots_t,
        [dx_a.reshape(deep), dx_b.reshape(deep)],
        [out_a.reshape(deep), out_b.reshape(deep)],
        jnp.concatenate([dg_a, dg_b])
        .reshape(local_experts, ep_count, capacity)
        .transpose(1, 0, 2)
        .reshape(ep_count, 1, local_experts * capacity),
        experts,
    )
    dx_part, grads_b = lax.optimization_barrier((dx_part, grads_b))
    dx_mine, gate_mine = reduce_ep(dx_part, gate_part, 2, "reduce_input_grads")
    dx_mine, mine_a, grads_b = lax.optimization_barrier((dx_mine, mine_a, grads_b))
    mine_b = over_rings(grads_b)
    mine_a, mine_b = [m.reshape(3, pair, -1, width) for m in (mine_a, mine_b)]
    w_gate_grad, w_up_grad = [
        jnp.concatenate([mine_a[i], mine_b[i]]).transpose(0, 2, 1).astype(F32) for i in range(2)
    ]
    w_down_grad = jnp.concatenate([mine_a[2], mine_b[2]]).astype(F32)
    lanes = gate_mine.shape[1] // 2
    d_gates = gate_mine[:, :experts] + gate_mine[:, lanes : lanes + experts]
    counts = jnp.sum((routes[:, :, None] == expert_ids[None, None, :]).astype(F32), axis=(0, 1))
    total_tokens = routes.shape[0]
    share = counts / (total_tokens * top)
    coeff = AUX * experts * share
    prob_local = jnp.sum(router_probs, axis=0)
    cot = cotangent.astype(F32)
    d_logits = gates * (d_gates - jnp.sum(gates * d_gates, axis=-1, keepdims=True))
    d_logits = d_logits + router_probs * (
        coeff - jnp.sum(router_probs * coeff, axis=-1, keepdims=True)
    )
    d_logits_low = d_logits.astype(BF)
    router_part = dot_tn(moe_in, d_logits_low)
    d_moe = dot_nt(d_logits_low, w_router) + dx_mine
    d_hidden, route_gain_part = norm_back(d_moe, hidden, route_gain[None])
    d_hidden = d_hidden + cot

    d_queries, d_keys, d_values, query_gain_part, key_gain_part, d_branch, output = attention_back(
        image_starts, queries, key_rows, values, lse, cosine, sine, q_gain, k_gain,
        w_out, d_hidden.astype(BF), out_part, hidden, 3,
    )
    w_query_grad, w_key_grad, w_value_grad, w_out_grad, inputs_grad, attn_gain_grad, small = projection_grads(
        normed, d_queries, d_keys, d_values, heads, d_branch,
        w_query, key_weight_matrix, value_weight_matrix,
        x_rows, d_hidden, attn_gain[None],
        [router_part, route_gain_part[0], query_gain_part[0], key_gain_part[0], prob_local],
        5,
    )
    w_router_grad, route_gain_grad, query_gain_grad, key_gain_grad, prob_all = small
    attn_gain_grad = attn_gain_grad[0]
    aux_loss = experts * jnp.sum(share * (prob_all / total_tokens))
    return (
        output,
        aux_loss,
        inputs_grad,
        attn_gain_grad,
        w_query_grad,
        w_key_grad,
        w_value_grad,
        query_gain_grad,
        key_gain_grad,
        w_out_grad,
        route_gain_grad,
        w_router_grad,
        w_gate_grad,
        w_up_grad,
        w_down_grad,
    )


def solution(mesh):
    return jax.shard_map(
        on_device,
        mesh=mesh,
        in_specs=(
            P("ep", None),
            P(),
            P(None, "tp"),
            P(None, "tp"),
            P(None, "tp"),
            P(),
            P(),
            P("tp", None),
            P(),
            P(),
            P("ep", None, "tp"),
            P("ep", None, "tp"),
            P("ep", "tp", None),
            P(),
            P("ep", None),
            P(("ep", "tp"), None),
        ),
        out_specs=(
            P(("ep", "tp"), None),
            P(),
            P(("ep", "tp"), None),
            P(),
            P("ep", "tp"),
            P("ep", "tp"),
            P("ep", "tp"),
            P(),
            P(),
            P("tp", "ep"),
            P(),
            P(),
            P("ep", None, "tp"),
            P("ep", None, "tp"),
            P("ep", "tp", None),
        ),
        check_vma=False,
    )
```

```python
import functools

import jax
import jax.numpy as jnp
from jax import lax
from jax.experimental import pallas as pl
from jax.experimental.pallas import tpu as pltpu
from jax.sharding import PartitionSpec as P

IMG = 256
EPS = 1e-06
AUX = 0.04
THETA = 1000000.0
MASKED = -1e30
NOWHERE = -(1 << 20)
BF = jnp.bfloat16
F32 = jnp.float32
VMEM_BYTES = 60 * 1024 * 1024


def dot_nn(a, b):
    return lax.dot_general(a, b, (((1,), (0,)), ((), ())), preferred_element_type=F32)


def dot_nt(a, b):
    return lax.dot_general(a, b, (((1,), (1,)), ((), ())), preferred_element_type=F32)


def dot_tn(a, b):
    return lax.dot_general(a, b, (((0,), (0,)), ((), ())), preferred_element_type=F32)


def params(**kw):
    return pltpu.CompilerParams(vmem_limit_bytes=VMEM_BYTES, **kw)


def rms_scale(value_rows):
    return lax.rsqrt(jnp.mean(value_rows * value_rows, axis=-1, keepdims=True) + EPS)


def plain_softmax(value_rows):
    top = jnp.max(value_rows, axis=-1, keepdims=True)
    expo = jnp.exp(value_rows - top)
    return expo / jnp.sum(expo, axis=-1, keepdims=True)


def rope_tables(length, size):
    half = size // 2
    freq = jnp.exp(-jnp.log(THETA) * (2.0 * jnp.arange(half, dtype=F32)) / size)
    angle = jnp.arange(length, dtype=F32)[:, None] * freq[None, :]
    cosine = jnp.cos(angle)
    sine = jnp.sin(angle)
    return (jnp.concatenate([cosine, cosine], axis=-1), jnp.concatenate([-sine, sine], axis=-1))


def turn(rows, cosine, sine):
    return rows * cosine + pltpu.roll(rows, rows.shape[-1] // 2, 1) * sine


def turn_back(rows, cosine, sine):
    return rows * cosine - pltpu.roll(rows, rows.shape[-1] // 2, 1) * sine


MESH = pl.DeviceIdType.MESH
ANY = pl.BlockSpec(memory_space=pl.ANY)
Z_AXIS = 4


def link_cost(us):
    return pl.CostEstimate(flops=0, bytes_accessed=int(us * 3.0e6), transcendentals=0)


def greet(partners):
    barrier = pltpu.get_barrier_semaphore()
    count = 0
    for there, device in partners:
        flag = jnp.asarray(there, jnp.int32)

        @pl.when(there)
        def _(device=device):
            pl.semaphore_signal(barrier, inc=1, device_id=device, device_id_type=MESH)

        count = count + flag
    pl.semaphore_wait(barrier, count)


def remote(src, dst, send, recv, device):
    return pltpu.make_async_remote_copy(
        src_ref=src, dst_ref=dst, send_sem=send, recv_sem=recv, device_id=device, device_id_type=MESH
    )


def ring_place():
    me = lax.axis_index("ep")
    z, y = me // 2, me % 2
    return me, z, y, {"ep": me + 2}, {"ep": me - 2}, {"ep": me + 1 - 2 * y}


class EpGather:
    def __init__(self, ins, outs, sems):
        self.ins, self.outs = ins, outs
        self.own_sem, self.up_send, self.up_recv, self.dn_send, self.dn_recv = sems[:5]
        self.y_send, self.y_recv = sems[5:]
        self.me, self.z, self.y, self.up, self.down, self.beside = ring_place()

    def partners(self):
        z = self.z
        return [(z < Z_AXIS - 1, self.up), (z > 0, self.down), (z >= 0, self.beside)]

    def block(self, a, zt):
        return self.outs[a].at[zt * 2 + self.y]

    def upward(self, src, a, zt):
        return remote(src, self.block(a, zt), self.up_send.at[a, zt], self.up_recv.at[a, zt], self.up)

    def downward(self, src, a, zt):
        return remote(src, self.block(a, zt), self.dn_send.at[a, zt], self.dn_recv.at[a, zt], self.down)

    def sideways(self, src, a, zt):
        return remote(src, self.block(a, zt), self.y_send.at[a, zt], self.y_recv.at[a, zt], self.beside)

    def start(self):
        z = self.z
        for a, x in enumerate(self.ins):

            @pl.when(z < Z_AXIS - 1)
            def _(a=a, x=x):
                self.upward(x, a, z).start()

            @pl.when(z > 0)
            def _(a=a, x=x):
                self.downward(x, a, z).start()

            self.sideways(x, a, z).start()
            pltpu.make_async_copy(x, self.block(a, z), self.own_sem.at[a]).start()

    def hop(self, d):
        z = self.z
        for a in range(len(self.ins)):

            @pl.when(z >= d)
            def _(a=a, zt=z - d):
                self.upward(self.block(a, zt), a, zt).wait_recv()

                @pl.when(z < Z_AXIS - 1)
                def _():
                    self.upward(self.block(a, zt), a, zt).start()

                self.sideways(self.block(a, zt), a, zt).start()

            @pl.when(z + d < Z_AXIS)
            def _(a=a, zt=z + d):
                self.downward(self.block(a, zt), a, zt).wait_recv()

                @pl.when(z > 0)
                def _():
                    self.downward(self.block(a, zt), a, zt).start()

                self.sideways(self.block(a, zt), a, zt).start()

    def own_done(self, a):
        pltpu.make_async_copy(self.ins[a], self.block(a, self.z), self.own_sem.at[a]).wait()

    def side_done(self, a, zt):
        other = self.outs[a].at[zt * 2 + 1 - self.y]
        remote(other, other, self.y_send.at[a, zt], self.y_recv.at[a, zt], self.beside).wait_recv()

    def sent(self, a):
        z = self.z
        for zt in range(Z_AXIS):
            src = self.block(a, zt)
            self.sideways(src, a, zt).wait_send()

            @pl.when((zt <= z) & (z < Z_AXIS - 1))
            def _(src=src, zt=zt):
                self.upward(src, a, zt).wait_send()

            @pl.when((zt >= z) & (z > 0))
            def _(src=src, zt=zt):
                self.downward(src, a, zt).wait_send()

    def finish(self):
        for a in range(len(self.ins)):
            self.own_done(a)
            for zt in range(Z_AXIS):
                self.side_done(a, zt)
            self.sent(a)


def gather_sems(count):
    dma = pltpu.SemaphoreType.DMA
    return [dma((count,))] + [dma((count, Z_AXIS))] * 6


def halves(ref, axis):
    n = ref.shape[axis] // 2
    lead = (slice(None),) * axis
    return [ref.at[lead + (pl.ds(h * n, n),)] for h in range(2)]


def one_hot(slots, capacity):
    local, rows = slots.shape
    slot = lax.broadcasted_iota(jnp.int32, (capacity, rows), 0)
    return [slot == slots[e : e + 1, :] for e in range(local)]


def gather_select_kernel(
    x_ref, cots_ref, slots_ref, picks_ref, router_ref, xs_ref, cs_ref, gate_ref,
    tokens, cots, chosen, load_sem, store_sem, *sems,
):
    local, _, capacity, width = xs_ref.shape
    blocks = tokens.shape[0]
    gather = EpGather(halves(x_ref, 0), halves(tokens, 1), sems)
    z, y = gather.z, gather.y
    greet(gather.partners())
    gather.start()

    def chosen_rows(j, rows):
        hits = one_hot(slots_ref[j], capacity)
        place = jnp.concatenate([h.astype(F32) for h in hits], axis=0).astype(BF)
        return dot_nn(place, rows).astype(BF).reshape(local, capacity, width), hits

    def load(j, slot):
        return pltpu.make_async_copy(cots_ref.at[j], cots.at[slot], load_sem.at[slot])

    def store(to, j, slot):
        return pltpu.make_async_copy(chosen.at[slot], to.at[:, j], store_sem.at[slot])

    load(0, 0).start()

    @pl.loop(0, blocks)
    def _(j):
        slot = lax.rem(j, 2)

        @pl.when(j + 1 < blocks)
        def _():
            load(j + 1, 1 - slot).start()

        load(j, slot).wait()

        @pl.when(j >= 2)
        def _():
            store(cs_ref, j - 2, slot).wait()

        chosen[slot] = chosen_rows(j, cots[slot])[0]
        store(cs_ref, j, slot).start()

    store(cs_ref, blocks - 2, 0).wait()
    store(cs_ref, blocks - 1, 1).wait()

    def take(j):
        rows = tokens[j]
        chosen[0], hits = chosen_rows(j, rows)
        copy = store(xs_ref, j, 0)
        copy.start()
        logits = dot_nt(router_ref[...], rows)
        picked = picks_ref[j] > 0
        kept = jnp.where(picked, logits, MASKED)
        expo = jnp.exp(kept - jnp.max(kept, axis=0, keepdims=True))
        expo = jnp.where(picked, expo, 0.0)
        gates = expo / jnp.sum(expo, axis=0, keepdims=True)
        for e, hit in enumerate(hits):
            gate_ref[e, j] = jnp.sum(jnp.where(hit, gates[e : e + 1, :], 0.0), axis=1, keepdims=True)
        copy.wait()

    for a in range(2):
        gather.own_done(a)
    take(gather.me)
    for d in range(1, Z_AXIS + 1):
        if d < Z_AXIS:
            gather.hop(d)

        @pl.loop(0, 4)
        def _(i, d=d):
            beside = i >= 2
            far = jnp.where(beside, d - 1, d)
            zt = jnp.where(lax.rem(i, 2) == 0, z - far, z + far)
            there = (zt >= 0) & (zt < Z_AXIS) & ((i < 3) | (d > 1))

            @pl.when(there & beside)
            def _():
                for a in range(2):
                    gather.side_done(a, zt)

            @pl.when(there)
            def _():
                take(zt * 2 + jnp.where(beside, 1 - y, y))

    for a in range(2):
        gather.sent(a)


def gather_select(rows, cot_all, slots, picks, router, capacity, number):
    ep_count = lax.axis_size("ep")
    _, local, block = slots.shape
    width = rows.shape[1]
    vmem = pl.BlockSpec(memory_space=pltpu.VMEM)
    dma = pltpu.SemaphoreType.DMA
    shape = (local, ep_count, capacity, width)
    return pl.pallas_call(
        gather_select_kernel,
        in_specs=[ANY, ANY, vmem, vmem, vmem],
        out_specs=[ANY, ANY, vmem],
        out_shape=[
            jax.ShapeDtypeStruct(shape, BF),
            jax.ShapeDtypeStruct(shape, BF),
            jax.ShapeDtypeStruct(shape[:3] + (1,), F32),
        ],
        scratch_shapes=[
            pltpu.VMEM((ep_count, block, width), BF),
            pltpu.VMEM((2, block, width), BF),
            pltpu.VMEM((2, local, capacity, width), BF),
            dma((2,)), dma((2,)),
        ]
        + gather_sems(2),
        compiler_params=params(collective_id=number, has_side_effects=True),
        cost_estimate=link_cost(90.0),
        name="gather_select",
    )(rows, cot_all, slots, picks, router)


def add_rows(total, terms, chunk=32):
    @pl.loop(0, total.shape[0] // chunk)
    def _(i):
        rows = pl.ds(pl.multiple_of(i * chunk, chunk), chunk)
        value = terms[0][rows, :].astype(F32)
        for term in terms[1:]:
            value = value + term[rows, :].astype(F32)
        total[rows, :] = value.astype(total.dtype)


def scatter_order(z):
    table = ((3, 2, 1, 0), (3, 0, 2, 1), (0, 3, 1, 2), (0, 1, 2, 3))
    return [
        jnp.where(
            z == 0,
            table[0][k],
            jnp.where(z == 1, table[1][k], jnp.where(z == 2, table[2][k], table[3][k])),
        )
        for k in range(Z_AXIS)
    ]


class EpReduce:
    def __init__(self, ins, bufs, sems, loaded=True):
        self.ins, self.loaded = ins, loaded
        each = 3 if loaded else 2
        self.bufs = [bufs[each * a : each * a + each] for a in range(len(ins))]
        self.own_sem, self.up_send, self.up_recv, self.dn_send, self.dn_recv = sems[:5]
        self.y_send, self.y_recv = sems[5:]
        self.me, self.z, self.y, self.up, self.down, self.beside = ring_place()
        self.order = scatter_order(self.z)

    def partners(self):
        z = self.z
        return [(z < Z_AXIS - 1, self.up), (z > 0, self.down), (z >= 0, self.beside)]

    def mine(self, a, zt):
        return self.bufs[a][0].at[zt] if self.loaded else self.ins[a].at[zt * 2 + self.y]

    def side(self, a, zt):
        return self.bufs[a][-2].at[zt]

    def below(self, a, zt):
        return self.bufs[a][-1].at[zt]

    def above(self, a, zt, z):
        return self.bufs[a][-1].at[jnp.where(zt == z, Z_AXIS, zt)]

    def to_side(self, a, zt):
        src = self.ins[a].at[zt * 2 + 1 - self.y]
        return remote(src, self.side(a, zt), self.y_send.at[a, zt], self.y_recv.at[a, zt], self.beside)

    def load(self, a, zt):
        return pltpu.make_async_copy(
            self.ins[a].at[zt * 2 + self.y], self.mine(a, zt), self.own_sem.at[a, zt]
        )

    def rising(self, a, zt):
        return remote(
            self.mine(a, zt), self.below(a, zt), self.up_send.at[a, zt], self.up_recv.at[a, zt], self.up
        )

    def falling(self, a, zt):
        return remote(
            self.mine(a, zt), self.above(a, zt, self.z - 1),
            self.dn_send.at[a, zt], self.dn_recv.at[a, zt], self.down,
        )

    def send_side(self, k):
        for a in range(len(self.ins)):
            self.to_side(a, self.order[k]).start()
            if self.loaded:
                self.load(a, self.order[k]).start()

    def step(self, k):
        z, zt, last = self.z, self.order[k], Z_AXIS - 1
        for a in range(len(self.ins)):
            mine, side = self.mine(a, zt), self.side(a, zt)
            if self.loaded:
                self.load(a, zt).wait()
            self.to_side(a, zt).wait_recv()

            @pl.when(((zt > z) & (z == 0)) | ((zt < z) & (z == last)))
            def _(mine=mine, side=side):
                add_rows(mine, [mine, side])

            @pl.when((zt > z) & (z > 0))
            def _(a=a, mine=mine, side=side):
                self.rising(a, zt).wait_recv()
                add_rows(mine, [mine, side, self.below(a, zt)])

            @pl.when((zt < z) & (z < last))
            def _(a=a, mine=mine, side=side):
                self.falling(a, zt).wait_recv()
                add_rows(mine, [mine, side, self.above(a, zt, z)])

            @pl.when(zt > z)
            def _(a=a):
                self.rising(a, zt).start()

            @pl.when(zt < z)
            def _(a=a):
                self.falling(a, zt).start()

    def own(self, a, write):
        z, last = self.z, Z_AXIS - 1
        pair = [self.mine(a, z), self.side(a, z)]

        @pl.when(z > 0)
        def _():
            self.rising(a, z).wait_recv()

        @pl.when(z < last)
        def _():
            self.falling(a, z).wait_recv()

        @pl.when(z == 0)
        def _():
            write(pair + [self.above(a, z, z)])

        @pl.when(z == last)
        def _():
            write(pair + [self.below(a, z)])

        @pl.when((z > 0) & (z < last))
        def _():
            write(pair + [self.below(a, z), self.above(a, z, z)])

    def sent(self):
        z = self.z
        for a in range(len(self.ins)):
            for zt in range(Z_AXIS):
                self.to_side(a, zt).wait_send()

                @pl.when(zt > z)
                def _(a=a, zt=zt):
                    self.rising(a, zt).wait_send()

                @pl.when(zt < z)
                def _(a=a, zt=zt):
                    self.falling(a, zt).wait_send()


def reduce_scratch(shape, dtype, loaded=True):
    counts = ([Z_AXIS] if loaded else []) + [Z_AXIS, Z_AXIS + 1]
    return [pltpu.VMEM((n,) + tuple(shape), dtype) for n in counts]


def reduce_sems(count):
    return [pltpu.SemaphoreType.DMA((count, Z_AXIS))] * 7


def token_hits(slots, capacity):
    rows, local = slots.shape
    lane = lax.broadcasted_iota(jnp.int32, (rows, local * capacity), 1)
    return [lane == slots[:, e : e + 1] + e * capacity for e in range(local)]


class SlotSums:
    def __init__(self, slots, first, second, buf, sem):
        self.slots, self.pair, self.buf, self.sem = slots, (first, second), buf, sem
        self.capacity = first.shape[2]

    def copies(self, j, at):
        n = self.pair[0].shape[0]
        return [
            pltpu.make_async_copy(
                ref.at[:, j], self.buf.at[at, pl.ds(i * n, n)], self.sem.at[at, i]
            )
            for i, ref in enumerate(self.pair)
        ]

    def fetch(self, j, at):
        for copy in self.copies(j, at):
            copy.start()

    def add(self, j, at, out):
        for copy in self.copies(j, at):
            copy.wait()
        place = jnp.zeros((), F32)
        for hit in token_hits(self.slots[j], self.capacity):
            place = jnp.where(hit, 1.0, place)
        rows = self.buf[at].reshape(-1, out.shape[1])
        out[...] = dot_nn(place.astype(BF), rows).astype(BF)

    def run(self, blocks, out, then):
        self.fetch(blocks[0], 0)
        for n, j in enumerate(blocks):
            if n + 1 < len(blocks):
                self.fetch(blocks[n + 1], (n + 1) % 2)
            self.add(j, n % 2, out.at[j])
            then(n)


def slot_sums_scratch(local, capacity, width):
    return [
        pltpu.VMEM((2, local, capacity, width), BF),
        pltpu.SemaphoreType.DMA((2, 2)),
    ]


def input_grads_kernel(
    slots, dgate, dx_a, dx_b, xs, cs, act, d_gate, d_up,
    out, gate_out, grads,
    part, gates, buf, sem, x_in, c_in, h_in, w_buf, in_sem, w_sem, *refs,
):
    sums = SlotSums(slots, dx_a, dx_b, buf, sem)
    reduce = EpReduce(halves(part, 1) + [gates], refs[:6], refs[6:], loaded=False)
    order, y = reduce.order, reduce.y
    pair, number, inner = act.shape
    parts, _, _, hidden, width = grads.shape
    first = xs.shape[0] - pair
    pieces = width // x_in.shape[1]
    wide = x_in.shape[1]
    greet(reduce.partners())

    def cols(piece):
        return pl.ds(piece * wide, wide)

    def wide_copies(unit):
        e, piece = unit // pieces, unit % pieces
        return [
            pltpu.make_async_copy(xs.at[first + e, :, cols(piece)], x_in, in_sem.at[0]),
            pltpu.make_async_copy(cs.at[first + e, :, cols(piece)], c_in, in_sem.at[1]),
        ]

    def inner_copies(e):
        return [
            pltpu.make_async_copy(ref.at[e], h_in.at[kind], in_sem.at[2 + kind])
            for kind, ref in enumerate((d_gate, d_up, act))
        ]

    def written(unit):
        e, piece = unit // pieces, unit % pieces
        return pltpu.make_async_copy(w_buf, grads.at[:, :, e, :, cols(piece)], w_sem)

    def prepare(unit):
        for copy in wide_copies(unit) + (inner_copies(unit // pieces) if unit % pieces == 0 else []):
            copy.start()

    def weights(unit):
        for copy in wide_copies(unit) + (inner_copies(unit // pieces) if unit % pieces == 0 else []):
            copy.wait()
        if unit > 0:
            written(unit - 1).wait()
        for kind, right in enumerate((x_in, x_in, c_in)):
            grad = dot_tn(h_in[kind], right[...]).astype(BF)
            w_buf[:, kind] = grad.reshape(parts, hidden, wide)
        written(unit).start()
        if unit + 1 < pair * pieces:
            prepare(unit + 1)

    def payload(j):
        lanes = gates.shape[2]
        column = lax.broadcasted_iota(jnp.int32, (gates.shape[1], lanes), 1)
        pay = jnp.zeros(column.shape, F32)
        mine = reduce.me * slots.shape[2]
        for e, hit in enumerate(token_hits(slots[j], sums.capacity)):
            value = jnp.sum(jnp.where(hit, dgate[j], 0.0), axis=1, keepdims=True)
            high = value.astype(BF).astype(F32)
            pay = jnp.where(column == mine + e, high, pay)
            pay = jnp.where(column == mine + e + lanes // 2, value - high, pay)
        gates[j] = pay.astype(BF)

    def send(k):
        payload(order[k] * 2 + 1 - y)
        reduce.send_side(k)

    units = pair * pieces
    done = [units * (k + 1) // Z_AXIS for k in range(Z_AXIS)]
    sums.run([order[k] * 2 + 1 - y for k in range(Z_AXIS)], part, send)
    prepare(0)
    sums.run(
        [order[k] * 2 + y for k in range(Z_AXIS)], part, lambda k: payload(order[k] * 2 + y)
    )
    for k in range(Z_AXIS):
        for unit in range(done[k - 1] if k else 0, done[k]):
            weights(unit)
        reduce.step(k)
    for a, rows in enumerate(halves(out, 0) + [gate_out]):
        reduce.own(a, functools.partial(add_rows, rows))
    reduce.sent()
    written(units - 1).wait()


def input_grads(slots_t, dgate, dx, x_slots, c_slots, inner, experts, tp_count, number):
    ep_count, rows, local = slots_t.shape
    pair, _, capacity, width = dx[0].shape
    count, hidden = inner[0].shape[1:]
    lanes = -(-2 * experts // 128) * 128
    wide = width // 2
    dma = pltpu.SemaphoreType.DMA
    vmem = pl.BlockSpec(memory_space=pltpu.VMEM)
    half = reduce_scratch((rows // 2, width), BF, loaded=False)
    return pl.pallas_call(
        input_grads_kernel,
        in_specs=[vmem, vmem] + [ANY] * 7,
        out_specs=[vmem, vmem, ANY],
        out_shape=[
            jax.ShapeDtypeStruct((rows, width), F32),
            jax.ShapeDtypeStruct((rows, lanes), F32),
            jax.ShapeDtypeStruct((tp_count, 3, pair, hidden // tp_count, width), BF),
        ],
        scratch_shapes=[
            pltpu.VMEM((ep_count, rows, width), BF),
            pltpu.VMEM((ep_count, rows, lanes), BF),
        ]
        + slot_sums_scratch(local, capacity, width)
        + [
            pltpu.VMEM((count, wide), BF),
            pltpu.VMEM((count, wide), BF),
            pltpu.VMEM((3, count, hidden), BF),
            pltpu.VMEM((tp_count, 3, hidden // tp_count, wide), BF),
            dma((5,)), dma,
        ]
        + half + half
        + reduce_scratch((rows, lanes), BF, loaded=False)
        + reduce_sems(3),
        compiler_params=params(collective_id=number, has_side_effects=True),
        cost_estimate=link_cost(100.0),
        name="input_grads",
    )(slots_t, dgate, *dx, x_slots, c_slots, *inner)


class SumAll:
    def __init__(self, x, out, parts, own, send, recv, back_send, back_recv):
        self.x, self.out, self.parts, self.own = x, out, parts, own
        self.send, self.recv, self.back_send, self.back_recv = send, recv, back_send, back_recv
        self.tp_count = lax.axis_size("tp")
        self.total = lax.axis_size("ep") * self.tp_count
        self.me = lax.axis_index("ep") * self.tp_count + lax.axis_index("tp")

    def device(self, d):
        return {"ep": d // self.tp_count, "tp": d % self.tp_count}

    def other(self, i):
        return lax.rem(self.me + i, self.total)

    def each(self, act):
        @pl.loop(1, self.total)
        def _(i):
            act(i)

    def greet(self):
        barrier = pltpu.get_barrier_semaphore()
        self.each(
            lambda i: pl.semaphore_signal(
                barrier, inc=1, device_id=self.device(self.other(i)), device_id_type=MESH
            )
        )
        pl.semaphore_wait(barrier, self.total - 1)

    def outward(self, i):
        to = self.other(i)
        return remote(
            self.x.at[to], self.parts.at[self.me], self.send.at[i], self.recv.at[self.me], self.device(to)
        )

    def inward(self, i):
        origin = self.other(i)
        rows = self.parts.at[origin]
        return remote(rows, rows, self.send.at[i], self.recv.at[origin], self.device(origin))

    def spread(self, i):
        to = self.other(i)
        return remote(
            self.own, self.out.at[self.me], self.back_send.at[i], self.back_recv.at[self.me], self.device(to)
        )

    def returned(self, i):
        origin = self.other(i)
        rows = self.out.at[origin]
        return remote(rows, rows, self.back_send.at[i], self.back_recv.at[origin], self.device(origin))

    def start(self):
        self.each(lambda i: self.outward(i).start())
        self.parts[pl.ds(self.me, 1)] = self.x[pl.ds(self.me, 1)]

    def add(self):
        self.each(lambda i: self.inward(i).wait_recv())
        self.own[...] = jnp.sum(self.parts[...], axis=0)
        self.each(lambda i: self.spread(i).start())
        self.out[pl.ds(self.me, 1)] = self.own[...][None]

    def finish(self):
        self.each(lambda i: self.outward(i).wait_send())
        self.each(lambda i: self.returned(i).wait_recv())
        self.each(lambda i: self.spread(i).wait_send())


def sum_scratch(rows, total):
    dma = pltpu.SemaphoreType.DMA
    return [
        pltpu.VMEM((total, rows, 128), F32), pltpu.VMEM((rows, 128), F32),
        dma((total,)), dma((total,)), dma((total,)), dma((total,)),
    ]


def pack_small(values, total):
    flat = jnp.concatenate([v.reshape(-1) for v in values])
    rows = -(-flat.shape[0] // (total * 128 * 8)) * 8
    return jnp.pad(flat, (0, total * rows * 128 - flat.shape[0])).reshape(total, rows, 128)


def unpack_small(summed, values):
    summed = summed.reshape(-1)
    out, at = [], 0
    for v in values:
        out.append(summed[at : at + v.size].reshape(v.shape))
        at += v.size
    return out


def fill_bias(span_ref, bias, chunk=256):
    keys, length = bias.shape
    query = lax.broadcasted_iota(jnp.int32, (1, length), 1)

    def spans(pos):
        first = (pos >= span_ref[0, 0]) & (pos < span_ref[0, 0] + IMG)
        second = (pos >= span_ref[0, 1]) & (pos < span_ref[0, 1] + IMG)
        return jnp.where(first, 0, jnp.where(second, 1, -1))

    query_span = spans(query)
    query_other = jnp.where(query_span < 0, -2, query_span)
    for start in range(0, keys, chunk):
        key = start + lax.broadcasted_iota(jnp.int32, (chunk, 1), 0)
        ok = (key <= query) | (spans(key) == query_other)
        bias[start : start + chunk, :] = jnp.where(ok, 0.0, MASKED)


def query_tiles(length):
    tile = min(IMG, length)
    return [
        (start, tile, min(length, start + tile + -(-IMG // tile) * tile))
        for start in range(0, length, tile)
    ]


def attention_kernel(
    span_ref, q_ref, k_ref, v_ref, cos_ref, sin_ref, qg_ref, kg_ref, w_out_ref, cot_ref,
    out_ref, lse_ref, rows_ref, cots_ref,
    bias, k_rot, v_t, heads, part, core_rows, x_rows, core_send, core_recv, x_send, x_recv, *sems,
):
    factor = q_ref.shape[-1] ** (-0.5)
    cosine, sine = cos_ref[...], sin_ref[...]
    step = pl.program_id(0)
    size = q_ref.shape[-1]
    me = lax.axis_index("tp")
    x, c = me // 2, me % 2
    other_core, other_x = {"tp": x * 2 + 1 - c}, {"tp": (1 - x) * 2 + c}
    gather = EpGather(halves(cot_ref, 0), halves(cots_ref, 1), sems)

    @pl.when(step == 0)
    def _():
        greet(gather.partners() + [(x >= 0, other_core), (x >= 0, other_x)])
        gather.start()
        fill_bias(span_ref, bias)
        k = k_ref[...]
        k_rot[...] = turn(k * rms_scale(k) * kg_ref[...], cosine, sine).astype(BF)
        v_t[...] = v_ref[...].astype(F32).T.astype(BF)

    @pl.when(step == pl.num_programs(0) - 2)
    def _():
        gather.hop(1)

    q = q_ref[...]
    q_rot = turn(q * rms_scale(q) * qg_ref[...], cosine, sine).astype(BF)
    for start, tile, keys in query_tiles(q.shape[0]):
        cols = slice(start, start + tile)
        s = dot_nt(k_rot[:keys, :], q_rot[cols, :]) * factor + bias[:keys, cols]
        top = jnp.max(s, axis=0, keepdims=True)
        p = jnp.exp(s - top)
        total = jnp.sum(p, axis=0, keepdims=True)
        o_t = dot_nn(v_t[:, :keys], p.astype(BF)) / total
        rows = o_t.T.astype(BF)
        out_ref[cols, :] = rows
        heads[step, cols, :] = rows
        lse_ref[0, :, cols] = top + jnp.log(total)

    @pl.when(step == pl.num_programs(0) - 1)
    def _():
        count = heads.shape[0]
        block = rows_ref.shape[0]

        def project(tp):
            lines = pl.ds(pl.multiple_of(tp * block, block), block)
            rows = jnp.concatenate([heads[h, lines, :] for h in range(count)], axis=1)
            part[tp] = dot_nn(rows, w_out_ref[...]).astype(BF)

        def to_core(xt):
            return remote(
                part.at[xt * 2 + 1 - c], core_rows.at[xt],
                core_send.at[xt], core_recv.at[xt], other_core,
            )

        far, near = part.at[(1 - x) * 2 + c], part.at[x * 2 + c]
        to_x = remote(far, x_rows, x_send, x_recv, other_x)
        project((1 - x) * 2 + 1 - c)
        to_core(1 - x).start()
        project((1 - x) * 2 + c)
        to_core(1 - x).wait_recv()
        add_rows(far, [far, core_rows.at[1 - x]])
        to_x.start()
        project(x * 2 + 1 - c)
        to_core(x).start()
        project(x * 2 + c)
        gather.hop(2)
        to_core(x).wait_recv()
        gather.hop(3)
        to_x.wait_recv()
        add_rows(rows_ref, [near, core_rows.at[x], x_rows])
        gather.finish()
        to_core(1 - x).wait_send()
        to_core(x).wait_send()
        to_x.wait_send()


def plain_attention_kernel(
    span_ref, q_ref, k_ref, v_ref, cos_ref, sin_ref, qg_ref, kg_ref, out_ref, lse_ref,
    bias, k_rot, v_t,
):
    factor = q_ref.shape[-1] ** (-0.5)
    cosine, sine = cos_ref[...], sin_ref[...]

    @pl.when(pl.program_id(0) == 0)
    def _():
        fill_bias(span_ref, bias)
        k = k_ref[...]
        k_rot[...] = turn(k * rms_scale(k) * kg_ref[...], cosine, sine).astype(BF)
        v_t[...] = v_ref[...].astype(F32).T.astype(BF)

    q = q_ref[...]
    q_rot = turn(q * rms_scale(q) * qg_ref[...], cosine, sine).astype(BF)
    for start, tile, keys in query_tiles(q.shape[0]):
        cols = slice(start, start + tile)
        s = dot_nt(k_rot[:keys, :], q_rot[cols, :]) * factor + bias[:keys, cols]
        top = jnp.max(s, axis=0, keepdims=True)
        p = jnp.exp(s - top)
        total = jnp.sum(p, axis=0, keepdims=True)
        o_t = dot_nn(v_t[:, :keys], p.astype(BF)) / total
        out_ref[cols, :] = o_t.T.astype(BF)
        lse_ref[0, :, cols] = top + jnp.log(total)


def attention(span, q, k, v, cosine, sine, q_gain, k_gain, w_out, cotangent, number):
    length, size = k.shape
    heads = q.shape[1] // size
    whole = pl.BlockSpec((length, size), lambda h: (0, 0))
    head = pl.BlockSpec((length, size), lambda h: (0, h))
    gain = pl.BlockSpec((1, size), lambda h: (0, 0))
    in_specs = [
        pl.BlockSpec(memory_space=pltpu.SMEM), head, whole, whole, whole, whole, gain, gain,
    ]
    out_specs = [head, pl.BlockSpec((1, 1, length), lambda h: (h, 0, 0))]
    out_shape = [
        jax.ShapeDtypeStruct((length, heads * size), BF),
        jax.ShapeDtypeStruct((heads, 1, length), F32),
    ]
    scratch = [
        pltpu.VMEM((length, length), F32),
        pltpu.VMEM((length, size), BF),
        pltpu.VMEM((size, length), BF),
    ]
    args = (span, q, k, v, cosine, sine, q_gain, k_gain)
    ep_count, tp_count = lax.axis_size("ep"), lax.axis_size("tp")
    if ep_count != 2 * Z_AXIS:
        out, lse = pl.pallas_call(
            plain_attention_kernel,
            grid=(heads,),
            in_specs=in_specs,
            out_specs=out_specs,
            out_shape=out_shape,
            scratch_shapes=scratch,
            compiler_params=params(),
            name="plain_attention",
        )(*args)
        rows = lax.psum_scatter(
            dot_nn(out, w_out).astype(BF), "tp", scatter_dimension=0, tiled=True
        )
        return out, lse, rows.astype(F32), lax.all_gather(cotangent, "ep")
    block, width = cotangent.shape
    dma = pltpu.SemaphoreType.DMA
    return pl.pallas_call(
        attention_kernel,
        grid=(heads,),
        in_specs=in_specs + [pl.BlockSpec(w_out.shape, lambda h: (0, 0)), ANY],
        out_specs=out_specs + [pl.BlockSpec((block, width), lambda h: (0, 0)), ANY],
        out_shape=out_shape
        + [
            jax.ShapeDtypeStruct((block, width), F32),
            jax.ShapeDtypeStruct((ep_count, block, width), BF),
        ],
        scratch_shapes=scratch
        + [
            pltpu.VMEM((heads, length, size), BF),
            pltpu.VMEM((tp_count, block, width), BF),
            pltpu.VMEM((2, block, width), BF),
            pltpu.VMEM((block, width), BF),
            dma((2,)), dma((2,)), dma, dma,
        ]
        + gather_sems(2),
        compiler_params=params(collective_id=number, has_side_effects=True),
        cost_estimate=link_cost(90.0),
        name="attention",
    )(*args, w_out, cotangent)


def norm_back(grads, rows, gain):
    scale = rms_scale(rows)
    gain_part = jnp.sum(grads * rows * scale, axis=0, keepdims=True)
    inner = grads * gain
    mean = jnp.mean(inner * rows, axis=-1, keepdims=True)
    return scale * inner - rows * (scale * scale * scale * mean), gain_part


def plain_attention_back_kernel(
    span_ref, q_ref, k_ref, v_ref, grad_ref, lse_ref, cos_ref, sin_ref, qg_ref, kg_ref,
    dq_ref, dk_ref, dv_ref, dqg_ref, dkg_ref,
    bias, k_rot, k_t, dk_acc, dv_acc, dq_t,
):
    factor = q_ref.shape[-1] ** (-0.5)
    cosine, sine = cos_ref[...], sin_ref[...]
    step = pl.program_id(0)

    @pl.when(step == 0)
    def _():
        fill_bias(span_ref, bias)
        k = k_ref[...]
        rotated = turn(k * rms_scale(k) * kg_ref[...], cosine, sine)
        k_rot[...] = rotated.astype(BF)
        k_t[...] = rotated.T.astype(BF)
        dk_acc[...] = jnp.zeros_like(dk_acc)
        dv_acc[...] = jnp.zeros_like(dv_acc)
        dqg_ref[...] = jnp.zeros_like(dqg_ref)

    q = q_ref[...]
    q_rot = turn(q * rms_scale(q) * qg_ref[...], cosine, sine).astype(BF)
    for start, tile, keys in query_tiles(q.shape[0]):
        cols = slice(start, start + tile)
        s = dot_nt(k_rot[:keys, :], q_rot[cols, :]) * factor + bias[:keys, cols]
        p = jnp.exp(s - lse_ref[0, :, cols])
        grad = grad_ref[cols, :]
        dp = dot_nt(v_ref[:keys, :], grad)
        mean = jnp.sum(p * dp, axis=0, keepdims=True)
        raw = (p * (dp - mean) * factor).astype(BF)
        dq_t[:, cols] = dot_nn(k_t[:, :keys], raw)
        dk_acc[:keys, :] += dot_nn(raw, q_rot[cols, :])
        dv_acc[:keys, :] += dot_nn(p.astype(BF), grad)
    back, gain_part = norm_back(turn_back(dq_t[...].T, cosine, sine), q, qg_ref[...])
    dq_ref[...] = back.astype(BF)
    dqg_ref[...] += gain_part

    @pl.when(step == pl.num_programs(0) - 1)
    def _():
        back, gain_part = norm_back(turn_back(dk_acc[...], cosine, sine), k_ref[...], kg_ref[...])
        dk_ref[...] = back.astype(BF)
        dkg_ref[...] = gain_part
        dv_ref[...] = dv_acc[...].astype(BF)


def plain_attention_back(span, q, k, v, grads, lse, cosine, sine, q_gain, k_gain):
    length, size = k.shape
    heads = q.shape[1] // size
    whole = pl.BlockSpec((length, size), lambda h: (0, 0))
    head = pl.BlockSpec((length, size), lambda h: (0, h))
    gain = pl.BlockSpec((1, size), lambda h: (0, 0))
    return pl.pallas_call(
        plain_attention_back_kernel,
        grid=(heads,),
        in_specs=[
            pl.BlockSpec(memory_space=pltpu.SMEM), head, whole, whole, head,
            pl.BlockSpec((1, 1, length), lambda h: (h, 0, 0)), whole, whole, gain, gain,
        ],
        out_specs=[head, whole, whole, gain, gain],
        out_shape=[
            jax.ShapeDtypeStruct((length, heads * size), BF),
            jax.ShapeDtypeStruct((length, size), BF),
            jax.ShapeDtypeStruct((length, size), BF),
            jax.ShapeDtypeStruct((1, size), F32),
            jax.ShapeDtypeStruct((1, size), F32),
        ],
        scratch_shapes=[
            pltpu.VMEM((length, length), F32),
            pltpu.VMEM((length, size), BF),
            pltpu.VMEM((size, length), BF),
            pltpu.VMEM((length, size), F32),
            pltpu.VMEM((length, size), F32),
            pltpu.VMEM((size, length), F32),
        ],
        compiler_params=params(),
        name="plain_attention_back",
    )(span, q, k, v, grads, lse, cosine, sine, q_gain, k_gain)


def attention_back_kernel(
    span_ref, q_ref, k_ref, v_ref, lse_ref, cos_ref, sin_ref, qg_ref, kg_ref,
    w_out_ref, rows_ref, slots_ref, out_a, out_b, hidden_ref,
    dq_ref, dk_ref, dv_ref, dqg_ref, dkg_ref, branch_ref, output_ref,
    bias, k_rot, k_t, dk_acc, dv_acc, dq_t, branch, grads, part, buf, sem,
    own_sem, out_sem, core_send, core_recv, x_send, x_recv, *refs,
):
    factor = q_ref.shape[-1] ** (-0.5)
    size = q_ref.shape[-1]
    cosine, sine = cos_ref[...], sin_ref[...]
    step = pl.program_id(0)
    me = lax.axis_index("tp")
    x, c = me // 2, me % 2
    other_core, other_x = {"tp": x * 2 + 1 - c}, {"tp": (1 - x) * 2 + c}
    reduce = EpReduce(halves(part, 1), refs[:4], refs[4:], loaded=False)
    sums = SlotSums(slots_ref, out_a, out_b, buf, sem)
    order, y = reduce.order, reduce.y
    block = rows_ref.shape[0]
    near_other, far, far_other = x * 2 + 1 - c, (1 - x) * 2 + c, (1 - x) * 2 + 1 - c

    def to_core(slot, src, tp):
        return remote(src, branch.at[tp], core_send.at[slot], core_recv.at[slot], other_core)

    def to_x(tp):
        return remote(rows_ref, branch.at[tp], x_send, x_recv, other_x)

    def own_rows():
        return pltpu.make_async_copy(rows_ref, branch.at[me], own_sem)

    def whole_branch():
        return pltpu.make_async_copy(branch, branch_ref, out_sem)

    @pl.when(step == 0)
    def _():
        greet(reduce.partners() + [(x >= 0, other_core), (x >= 0, other_x)])
        to_x(me).start()
        to_core(0, rows_ref, me).start()
        own_rows().start()
        sums.run([order[k] * 2 + 1 - y for k in range(Z_AXIS)], part, reduce.send_side)
        fill_bias(span_ref, bias)
        k = k_ref[...]
        rotated = turn(k * rms_scale(k) * kg_ref[...], cosine, sine)
        k_rot[...] = rotated.astype(BF)
        k_t[...] = rotated.T.astype(BF)
        dk_acc[...] = jnp.zeros_like(dk_acc)
        dv_acc[...] = jnp.zeros_like(dv_acc)
        dqg_ref[...] = jnp.zeros_like(dqg_ref)

        def head_grads(tp):
            lines = pl.ds(pl.multiple_of(tp * block, block), block)
            rows = dot_nt(branch[tp], w_out_ref[...]).astype(BF)
            for h in range(grads.shape[0]):
                grads[h, lines, :] = rows[:, h * size : (h + 1) * size]

        own_rows().wait()
        head_grads(me)
        to_core(0, rows_ref, near_other).wait_recv()
        head_grads(near_other)
        sums.run([order[k] * 2 + y for k in range(Z_AXIS)], part, lambda k: None)
        reduce.step(0)
        to_x(far).wait_recv()
        to_core(1, branch.at[far], far).start()
        head_grads(far)
        to_core(1, branch.at[far], far_other).wait_recv()
        head_grads(far_other)
        whole_branch().start()

    for k, head in ((1, 1), (2, 5)):

        @pl.when(step == head)
        def _(k=k):
            reduce.step(k)

    q = q_ref[...]
    q_rot = turn(q * rms_scale(q) * qg_ref[...], cosine, sine).astype(BF)
    for start, tile, keys in query_tiles(q.shape[0]):
        cols = slice(start, start + tile)
        s = dot_nt(k_rot[:keys, :], q_rot[cols, :]) * factor + bias[:keys, cols]
        p = jnp.exp(s - lse_ref[0, :, cols])
        grad = grads[step, cols, :]
        dp = dot_nt(v_ref[:keys, :], grad)
        mean = jnp.sum(p * dp, axis=0, keepdims=True)
        raw = (p * (dp - mean) * factor).astype(BF)
        dq_t[:, cols] = dot_nn(k_t[:, :keys], raw)
        dk_acc[:keys, :] += dot_nn(raw, q_rot[cols, :])
        dv_acc[:keys, :] += dot_nn(p.astype(BF), grad)
    back, gain_part = norm_back(turn_back(dq_t[...].T, cosine, sine), q, qg_ref[...])
    dq_ref[...] = back.astype(BF)
    dqg_ref[...] += gain_part

    @pl.when(step == pl.num_programs(0) - 1)
    def _():
        back, gain_part = norm_back(turn_back(dk_acc[...], cosine, sine), k_ref[...], kg_ref[...])
        dk_ref[...] = back.astype(BF)
        dkg_ref[...] = gain_part
        dv_ref[...] = dv_acc[...].astype(BF)
        reduce.step(Z_AXIS - 1)
        pairs = zip(halves(output_ref, 0), halves(hidden_ref, 0))
        for a, (rows, residual) in enumerate(pairs):
            reduce.own(a, lambda terms, rows=rows, residual=residual: add_rows(rows, terms + [residual]))
        reduce.sent()
        whole_branch().wait()
        to_x(me).wait_send()
        to_core(0, rows_ref, me).wait_send()
        to_core(1, branch.at[far], far).wait_send()


def attention_back(
    span, q, k, v, lse, cosine, sine, q_gain, k_gain, w_out, d_rows, slots_t, out, hidden, number
):
    length, size = k.shape
    heads = q.shape[1] // size
    ep_count, tp_count = lax.axis_size("ep"), lax.axis_size("tp")
    if ep_count != 2 * Z_AXIS:
        branch = lax.all_gather(d_rows, "tp", axis=0, tiled=True)
        grads = dot_nt(branch, w_out).astype(BF)
        mine = lax.psum_scatter(out, "ep", scatter_dimension=0)
        back = plain_attention_back(span, q, k, v, grads, lse, cosine, sine, q_gain, k_gain)
        return *back, branch, (hidden + mine.astype(F32)).astype(BF)
    block, width = d_rows.shape
    whole = pl.BlockSpec((length, size), lambda h: (0, 0))
    head = pl.BlockSpec((length, size), lambda h: (0, h))
    gain = pl.BlockSpec((1, size), lambda h: (0, 0))
    rows = pl.BlockSpec((block, width), lambda h: (0, 0))
    dma = pltpu.SemaphoreType.DMA
    *back, branch, output = pl.pallas_call(
        attention_back_kernel,
        grid=(heads,),
        in_specs=[
            pl.BlockSpec(memory_space=pltpu.SMEM), head, whole, whole,
            pl.BlockSpec((1, 1, length), lambda h: (h, 0, 0)), whole, whole, gain, gain,
            pl.BlockSpec(w_out.shape, lambda h: (0, 0), pipeline_mode=pl.Buffered(1)), ANY,
            pl.BlockSpec(slots_t.shape, lambda h: (0, 0, 0), pipeline_mode=pl.Buffered(1)), ANY, ANY,
            pl.BlockSpec((block, width), lambda h: (0, 0), pipeline_mode=pl.Buffered(1)),
        ],
        out_specs=[head, whole, whole, gain, gain, ANY, rows],
        out_shape=[
            jax.ShapeDtypeStruct((length, heads * size), BF),
            jax.ShapeDtypeStruct((length, size), BF),
            jax.ShapeDtypeStruct((length, size), BF),
            jax.ShapeDtypeStruct((1, size), F32),
            jax.ShapeDtypeStruct((1, size), F32),
            jax.ShapeDtypeStruct((tp_count, block, width), BF),
            jax.ShapeDtypeStruct((block, width), BF),
        ],
        scratch_shapes=[
            pltpu.VMEM((length, length), F32),
            pltpu.VMEM((length, size), BF),
            pltpu.VMEM((size, length), BF),
            pltpu.VMEM((length, size), F32),
            pltpu.VMEM((length, size), F32),
            pltpu.VMEM((size, length), F32),
            pltpu.VMEM((tp_count, block, width), BF),
            pltpu.VMEM((heads, length, size), BF),
        ]
        + [pltpu.VMEM((ep_count, block, width), BF)]
        + slot_sums_scratch(slots_t.shape[2], out[0].shape[2], width)
        + [dma, dma, dma((2,)), dma((2,)), dma, dma]
        + reduce_scratch((block // 2, width), BF, loaded=False) * 2
        + reduce_sems(2),
        compiler_params=params(collective_id=number, has_side_effects=True),
        cost_estimate=link_cost(100.0),
        name="attention_back",
    )(span, q, k, v, lse, cosine, sine, q_gain, k_gain, w_out, d_rows, slots_t, *out, hidden)
    return *back, branch.reshape(-1, width), output


def projection_grads_kernel(
    normed, dq, dk, dv, heads, branch, wq, wk, wv, x_rows, d_hidden, gain, small,
    gq_ref, gk_ref, gv_ref, gout_ref, inputs_grad, gain_grad, small_sum,
    blocks, out_blocks, part, core_rows, far_rows, gain_own, gains,
    core_send, core_recv, x_send, x_recv, gain_send, gain_recv, *refs,
):
    me = lax.axis_index("tp")
    x, c = me // 2, me % 2
    other_core, other_x = {"tp": x * 2 + 1 - c}, {"tp": (1 - x) * 2 + c}
    sums = SumAll(small, small_sum, *refs[:6])
    reduce = EpReduce([blocks, out_blocks], refs[6:10], refs[10:], loaded=False)
    order, y = reduce.order, reduce.y
    rows, width = inputs_grad.shape
    nq, nk = dq.shape[1], dk.shape[1]

    sums.greet()
    sums.start()

    def fill(j):
        cols = pl.ds(pl.multiple_of(j * rows, rows), rows)
        left = normed[:, cols].T
        blocks[j, :, 0:nq] = dot_nn(left, dq[...]).astype(BF)
        blocks[j, :, nq : nq + nk] = dot_nn(left, dk[...]).astype(BF)
        blocks[j, :, nq + nk : nq + 2 * nk] = dot_nn(left, dv[...]).astype(BF)
        out_blocks[j] = dot_nn(branch[:, cols].T, heads[...]).astype(BF)

    def spread_back(tp):
        lines = pl.ds(pl.multiple_of(tp * rows, rows), rows)
        for start in range(0, width, width // 4):
            cols = slice(start, start + width // 4)
            part[tp, :, cols] = (
                dot_nt(dq[lines, :], wq[cols, :])
                + dot_nt(dk[lines, :], wk[cols, :])
                + dot_nt(dv[lines, :], wv[cols, :])
            ).astype(BF)

    def to_core(xt):
        return remote(
            part.at[xt * 2 + 1 - c], core_rows.at[xt], core_send.at[xt], core_recv.at[xt], other_core
        )

    far, near = part.at[(1 - x) * 2 + c], part.at[x * 2 + c]
    to_x = remote(far, far_rows, x_send, x_recv, other_x)

    for k in range(2):
        fill(order[k] * 2 + 1 - y)
        reduce.send_side(k)
    spread_back((1 - x) * 2 + 1 - c)
    to_core(1 - x).start()
    spread_back((1 - x) * 2 + c)
    to_core(1 - x).wait_recv()
    add_rows(far, [far, core_rows.at[1 - x]])
    to_x.start()
    for k in range(2, Z_AXIS):
        fill(order[k] * 2 + 1 - y)
        reduce.send_side(k)
    fill(order[0] * 2 + y)
    reduce.step(0)
    spread_back(x * 2 + 1 - c)
    to_core(x).start()
    spread_back(x * 2 + c)
    for k in range(1, Z_AXIS):
        fill(order[k] * 2 + y)
    reduce.step(1)
    to_core(x).wait_recv()
    to_x.wait_recv()

    chunk = 32
    gain_own[...] = jnp.zeros_like(gain_own)

    @pl.loop(0, rows // chunk)
    def _(i):
        lines = pl.ds(pl.multiple_of(i * chunk, chunk), chunk)
        grad = near[lines, :].astype(F32) + core_rows[x, lines, :].astype(F32)
        grad = grad + far_rows[lines, :].astype(F32)
        back, gain_part = norm_back(grad, x_rows[lines, :].astype(F32), gain[...])
        inputs_grad[lines, :] = d_hidden[lines, :] + back
        gain_own[...] += gain_part

    def tell(i):
        to = sums.other(i)
        return remote(
            gain_own, gains.at[sums.me], gain_send.at[i], gain_recv.at[sums.me], sums.device(to)
        )

    def heard(i):
        origin = sums.other(i)
        row = gains.at[origin]
        return remote(row, row, gain_send.at[i], gain_recv.at[origin], sums.device(origin))

    sums.each(lambda i: tell(i).start())
    gains[pl.ds(sums.me, 1)] = gain_own[...][None]
    reduce.step(2)
    sums.add()
    reduce.step(3)

    def total_of(terms, lines):
        value = terms[0][lines, :].astype(F32)
        for term in terms[1:]:
            value = value + term[lines, :].astype(F32)
        return value

    def write(terms):
        for start in range(0, rows, 128):
            lines = slice(start, start + 128)
            value = total_of(terms, lines)
            gq_ref[lines, :] = value[:, 0:nq]
            gk_ref[lines, :] = value[:, nq : nq + nk]
            gv_ref[lines, :] = value[:, nq + nk :]

    def write_out(terms):
        for start in range(0, rows, 128):
            lines = slice(start, start + 128)
            gout_ref[:, lines] = total_of(terms, lines).T

    sums.each(lambda i: heard(i).wait_recv())
    gain_grad[...] = jnp.sum(gains[...], axis=0)
    reduce.own(0, write)
    reduce.own(1, write_out)
    reduce.sent()
    to_core(1 - x).wait_send()
    to_core(x).wait_send()
    to_x.wait_send()
    sums.each(lambda i: tell(i).wait_send())
    sums.finish()


def projection_grads(
    normed, dq, dk, dv, heads, branch, wq, wk, wv, x_rows, d_hidden, gain, small_values, number
):
    rows, width = x_rows.shape
    ep_count, tp_count = lax.axis_size("ep"), lax.axis_size("tp")
    total = ep_count * tp_count
    small = pack_small(small_values, total)
    if ep_count != 2 * Z_AXIS:

        def over_sequences(part, dim):
            return lax.psum_scatter(
                part.astype(BF), "ep", scatter_dimension=dim, tiled=True
            ).astype(F32)

        d_normed = (dot_nt(dq, wq) + dot_nt(dk, wk) + dot_nt(dv, wv)).astype(BF)
        d_mine = lax.psum_scatter(d_normed, "tp", scatter_dimension=0, tiled=True)
        back, gain_part = norm_back(d_mine.astype(F32), x_rows.astype(F32), gain)
        gain_sum, small_sum = lax.psum((gain_part, small), ("ep", "tp"))
        return (
            over_sequences(dot_tn(normed, dq), 0),
            over_sequences(dot_tn(normed, dk), 0),
            over_sequences(dot_tn(normed, dv), 0),
            over_sequences(dot_tn(heads, branch), 1),
            d_hidden + back,
            gain_sum,
            unpack_small(small_sum, small_values),
        )
    nq, nk = dq.shape[1], dk.shape[1]
    nh = heads.shape[1]
    vmem = pl.BlockSpec(memory_space=pltpu.VMEM)
    dma = pltpu.SemaphoreType.DMA
    *grads, small_sum = pl.pallas_call(
        projection_grads_kernel,
        in_specs=[vmem] * 13,
        out_specs=[vmem] * 7,
        out_shape=[
            jax.ShapeDtypeStruct((rows, nq), F32),
            jax.ShapeDtypeStruct((rows, nk), F32),
            jax.ShapeDtypeStruct((rows, nk), F32),
            jax.ShapeDtypeStruct((nh, rows), F32),
            jax.ShapeDtypeStruct((rows, width), F32),
            jax.ShapeDtypeStruct((1, width), F32),
            jax.ShapeDtypeStruct(small.shape, F32),
        ],
        scratch_shapes=[
            pltpu.VMEM((ep_count, rows, nq + 2 * nk), BF),
            pltpu.VMEM((ep_count, rows, nh), BF),
            pltpu.VMEM((tp_count, rows, width), BF),
            pltpu.VMEM((2, rows, width), BF),
            pltpu.VMEM((rows, width), BF),
            pltpu.VMEM((1, width), F32),
            pltpu.VMEM((total, 1, width), F32),
            dma((2,)), dma((2,)), dma, dma, dma((total,)), dma((total,)),
        ]
        + sum_scratch(small.shape[1], total)
        + reduce_scratch((rows, nq + 2 * nk), BF, loaded=False)
        + reduce_scratch((rows, nh), BF, loaded=False)
        + reduce_sems(2),
        compiler_params=params(collective_id=number, has_side_effects=True),
        cost_estimate=link_cost(110.0),
        name="projection_grads",
    )(normed, dq, dk, dv, heads, branch, wq, wk, wv, x_rows, d_hidden, gain, small)
    return *grads, unpack_small(small_sum, small_values)


def select_kernel(slot_ref, x_ref, c_ref, xs_ref, cs_ref):
    local, _, capacity, width = xs_ref.shape
    rows = x_ref.shape[1]
    place = jnp.concatenate(
        [
            (
                slot_ref[0, e : e + 1, :]
                == lax.broadcasted_iota(jnp.int32, (capacity, rows), 0)
            ).astype(F32)
            for e in range(local)
        ],
        axis=0,
    ).astype(BF)
    xs_ref[...] = dot_nn(place, x_ref[0]).astype(BF).reshape(xs_ref.shape)
    cs_ref[...] = dot_nn(place, c_ref[0]).astype(BF).reshape(cs_ref.shape)


def select_rows(slots, tokens, cots, capacity):
    blocks, local, rows = slots.shape
    width = tokens.shape[-1]
    block = pl.BlockSpec((1, rows, width), lambda b: (b, 0, 0))
    out = pl.BlockSpec((local, 1, capacity, width), lambda b: (0, b, 0, 0))
    shape = jax.ShapeDtypeStruct((local, blocks, capacity, width), BF)
    return pl.pallas_call(
        select_kernel,
        grid=(blocks,),
        in_specs=[pl.BlockSpec((1, local, rows), lambda b: (b, 0, 0)), block, block],
        out_specs=[out, out],
        out_shape=[shape, shape],
        compiler_params=params(),
        name="select_rows",
    )(slots, tokens, cots)


def pack_kernel(gate_ref, up_ref, down_ref, out_ref):
    for kind, ref in enumerate((gate_ref, up_ref, down_ref)):
        out_ref[kind, 0] = ref[0]


def pack_weights(weights, first, count):
    _, hidden, width = weights[0].shape
    block = pl.BlockSpec((1, hidden, width), lambda e: (first + e, 0, 0))
    return pl.pallas_call(
        pack_kernel,
        grid=(count,),
        in_specs=[block] * 3,
        out_specs=pl.BlockSpec((3, 1, hidden, width), lambda e: (0, e, 0, 0)),
        out_shape=jax.ShapeDtypeStruct((3, count, hidden, width), BF),
        compiler_params=params(),
        name="pack_weights",
    )(*weights)


def expert_kernel(
    x_ref, c_ref, w_ref, gate_ref, out_ref, dx_ref, act_ref, dg_ref, du_ref, dgate_ref
):
    width = x_ref.shape[-1]
    x, c = x_ref[0], c_ref[0]
    w_gate = w_ref[:, 0, 0].reshape(-1, width)
    w_up = w_ref[:, 1, 0].reshape(-1, width)
    w_down = w_ref[:, 2, 0].reshape(-1, width)
    gate = gate_ref[0]
    gate_pre = dot_nt(x, w_gate)
    up_pre = dot_nt(x, w_up)
    raw = dot_nt(c, w_down)
    sig = jax.nn.sigmoid(gate_pre)
    silu = gate_pre * sig
    act = silu * up_pre
    dgate_ref[0] = jnp.sum(act * raw, axis=-1, keepdims=True)
    act_low = (act * gate).astype(BF)
    d_act = raw * gate
    d_gate = (d_act * up_pre * sig * (1.0 + gate_pre * (1.0 - sig))).astype(BF)
    d_up = (d_act * silu).astype(BF)
    act_ref[0] = act_low
    dg_ref[0] = d_gate
    du_ref[0] = d_up
    out_ref[0] = dot_nn(act_low, w_down).astype(BF)
    dx_ref[0] = (dot_nn(d_gate, w_gate) + dot_nn(d_up, w_up)).astype(BF)


def experts_both_ways(x_slots, c_slots, w_all, slot_gate, first):
    _, number, width = x_slots.shape
    parts, _, local, hidden, _ = w_all.shape
    tile = number // 2
    taken = pl.BlockSpec((1, tile, width), lambda e, i: (first + e, i, 0))
    wide = pl.BlockSpec((1, tile, width), lambda e, i: (e, i, 0))
    mid = pl.BlockSpec((1, tile, parts * hidden), lambda e, i: (e, i, 0))
    thin = pl.BlockSpec((1, tile, 1), lambda e, i: (e, i, 0))
    wide_shape = jax.ShapeDtypeStruct((local, number, width), BF)
    mid_shape = jax.ShapeDtypeStruct((local, number, parts * hidden), BF)
    return pl.pallas_call(
        expert_kernel,
        grid=(local, 2),
        in_specs=[
            taken, taken,
            pl.BlockSpec((parts, 3, 1, hidden, width), lambda e, i: (0, 0, e, 0, 0)),
            pl.BlockSpec((1, tile, 1), lambda e, i: (first + e, i, 0)),
        ],
        out_specs=[wide, wide, mid, mid, mid, thin],
        out_shape=[
            wide_shape, wide_shape, mid_shape, mid_shape, mid_shape,
            jax.ShapeDtypeStruct((local, number, 1), F32),
        ],
        compiler_params=params(),
        name="experts_both_ways",
    )(x_slots, c_slots, w_all, slot_gate)


def expert_grads_kernel(x_ref, c_ref, act_ref, dg_ref, du_ref, out_ref):
    parts, _, _, hidden, width = out_ref.shape
    x, c = x_ref[0], c_ref[0]
    out_ref[:, 0, 0] = dot_tn(dg_ref[0], x).astype(BF).reshape(parts, hidden, width)
    out_ref[:, 1, 0] = dot_tn(du_ref[0], x).astype(BF).reshape(parts, hidden, width)
    out_ref[:, 2, 0] = dot_tn(act_ref[0], c).astype(BF).reshape(parts, hidden, width)


def expert_grads(x_slots, c_slots, act, d_gate, d_up, parts, first):
    local, number, inner = act.shape
    width = x_slots.shape[-1]
    wide = pl.BlockSpec((1, number, width), lambda e: (first + e, 0, 0))
    mid = pl.BlockSpec((1, number, inner), lambda e: (e, 0, 0))
    return pl.pallas_call(
        expert_grads_kernel,
        grid=(local,),
        in_specs=[wide, wide, mid, mid, mid],
        out_specs=pl.BlockSpec(
            (parts, 3, 1, inner // parts, width), lambda e: (0, 0, e, 0, 0)
        ),
        out_shape=jax.ShapeDtypeStruct((parts, 3, local, inner // parts, width), BF),
        compiler_params=params(),
        name="expert_grads",
    )(x_slots, c_slots, act, d_gate, d_up)


def combine_kernel(
    first_ref, slot_ref, dxa_ref, dxb_ref, outa_ref, outb_ref, dgate_ref, dx_sum_ref, out_sum_ref, pay_ref
):
    _, _, capacity, width = dxa_ref.shape
    local = slot_ref.shape[2]
    rows = slot_ref.shape[1]
    lane = lax.broadcasted_iota(jnp.int32, (rows, local * capacity), 1)
    half = pay_ref.shape[2] // 2
    column = lax.broadcasted_iota(jnp.int32, (rows, 2 * half), 1)
    total = jnp.zeros((rows, local * capacity), F32)
    pay = jnp.zeros(column.shape, F32)
    for e in range(local):
        hit = lane == slot_ref[0, :, e : e + 1] + e * capacity
        total = jnp.where(hit, 1.0, total)
        value = jnp.sum(jnp.where(hit, dgate_ref[0], 0.0), axis=1, keepdims=True)
        high = value.astype(BF).astype(F32)
        pay = jnp.where(column == first_ref[0, 0] + e, high, pay)
        pay = jnp.where(column == first_ref[0, 0] + e + half, value - high, pay)
    place = total.astype(BF)

    def both(a_ref, b_ref):
        pair = [ref[...].reshape(-1, width) for ref in (a_ref, b_ref)]
        return dot_nn(place, jnp.concatenate(pair, axis=0)).astype(BF)

    dx_sum_ref[0] = both(dxa_ref, dxb_ref)
    out_sum_ref[0] = both(outa_ref, outb_ref)
    pay_ref[0] = pay.astype(BF)


def combine_rows(first, slots_t, dx, out, d_gate_slots, experts):
    blocks, rows, local = slots_t.shape
    _, _, capacity, width = dx[0].shape
    lanes = -(-2 * experts // 128) * 128
    slot = pl.BlockSpec((local // 2, 1, capacity, width), lambda b: (0, b, 0, 0))
    block = pl.BlockSpec((1, rows, width), lambda b: (b, 0, 0))
    shape = jax.ShapeDtypeStruct((blocks, rows, width), BF)
    return pl.pallas_call(
        combine_kernel,
        grid=(blocks,),
        in_specs=[
            pl.BlockSpec(memory_space=pltpu.SMEM),
            pl.BlockSpec((1, rows, local), lambda b: (b, 0, 0)), slot, slot, slot, slot,
            pl.BlockSpec((1, 1, local * capacity), lambda b: (b, 0, 0)),
        ],
        out_specs=[block, block, pl.BlockSpec((1, rows, lanes), lambda b: (b, 0, 0))],
        out_shape=[shape, shape, jax.ShapeDtypeStruct((blocks, rows, lanes), BF)],
        compiler_params=params(),
        name="combine_rows",
    )(first, slots_t, *dx, *out, d_gate_slots)


def on_device(
    inputs,
    attn_gain,
    w_query,
    key_weight_matrix,
    value_weight_matrix,
    query_gain,
    key_gain,
    w_out,
    route_gain,
    w_router,
    w_gate,
    w_up,
    w_down,
    routes,
    image_starts,
    cotangent,
):
    tp_count = lax.axis_size("tp")
    ep_count = lax.axis_size("ep")
    tp_index = lax.axis_index("tp")
    ep_index = lax.axis_index("ep")
    length = inputs.shape[0]
    width = inputs.shape[1]
    rows = cotangent.shape[0]
    head_dim = query_gain.shape[0]
    local_experts = w_gate.shape[0]
    experts = local_experts * ep_count
    top = routes.shape[1]
    capacity = -(-(3 * rows * top // (2 * experts)) // 16) * 16

    pair = local_experts // 2

    weights = (w_gate.transpose(0, 2, 1), w_up.transpose(0, 2, 1), w_down)
    w_first = lax.all_gather(pack_weights(weights, 0, pair), "tp")

    inputs_f = inputs.astype(F32)
    attn_scale = rms_scale(inputs_f)
    normed = (inputs_f * attn_scale * attn_gain).astype(BF)
    queries = dot_nn(normed, w_query)
    key_rows = dot_nn(normed, key_weight_matrix)
    values = dot_nn(normed, value_weight_matrix).astype(BF)
    cosine, sine = rope_tables(length, head_dim)
    q_gain, k_gain = query_gain[None], key_gain[None]
    queries, second = lax.optimization_barrier((queries, pack_weights(weights, pair, pair)))
    w_second = lax.all_gather(second, "tp")
    heads, lse, attn_rows, cot_all = attention(
        image_starts, queries, key_rows, values, cosine, sine, q_gain, k_gain, w_out, cotangent, 0
    )
    x_rows = lax.dynamic_slice_in_dim(inputs, tp_index * rows, rows, 0)
    hidden = x_rows.astype(F32) + attn_rows
    route_scale = rms_scale(hidden)
    moe_in = (hidden * route_scale * route_gain).astype(BF)
    moe_in, w_first = lax.optimization_barrier((moe_in, w_first))
    logits = dot_nn(moe_in, w_router)
    router_probs = plain_softmax(logits)
    expert_ids = jnp.arange(experts, dtype=jnp.int32)
    ring_routes = lax.dynamic_index_in_dim(
        routes.reshape(ep_count, tp_count, rows, top), tp_index, 1, keepdims=False
    )
    my_routes = lax.dynamic_index_in_dim(ring_routes, ep_index, 0, keepdims=False)

    def routed_softmax(scores, picked):
        kept = jnp.where(picked, scores, MASKED)
        expo = jnp.where(picked, jnp.exp(kept - jnp.max(kept, axis=-1, keepdims=True)), 0.0)
        return expo / jnp.sum(expo, axis=-1, keepdims=True)

    my_pick = jnp.any(my_routes[:, :, None] == expert_ids[None, None, :], axis=1)
    gates = routed_softmax(logits, my_pick)
    all_pick = jnp.any(ring_routes[..., None] == expert_ids, axis=2)
    mask = lax.dynamic_slice_in_dim(all_pick, ep_index * local_experts, local_experts, 2)
    earlier = (jnp.arange(rows)[:, None] > jnp.arange(rows)[None, :]).astype(BF)
    slots_t = jnp.einsum(
        "tu,bue->bte", earlier, mask.astype(BF), preferred_element_type=F32
    ).astype(jnp.int32)
    slots_t = jnp.where(mask, slots_t, NOWHERE)
    slots = slots_t.transpose(0, 2, 1)
    ring = ep_count == 2 * Z_AXIS
    if ring:
        turned = lax.rem(expert_ids + ep_index * local_experts, experts)
        x_slots, c_slots, slot_gate = gather_select(
            moe_in,
            cot_all,
            slots,
            all_pick.astype(jnp.int32)[..., turned].transpose(0, 2, 1),
            w_router.T[turned],
            capacity,
            1,
        )
        slot_gate = slot_gate.reshape(local_experts, ep_count * capacity, 1)
    else:
        tokens_all = lax.all_gather(moe_in, "ep")
        logits_all = dot_nn(tokens_all.reshape(-1, width), w_router).reshape(ep_count, rows, experts)
        gate_of = lax.dynamic_slice_in_dim(
            routed_softmax(logits_all, all_pick), ep_index * local_experts, local_experts, 2
        )
        place = slots[:, :, None, :] == jnp.arange(capacity, dtype=jnp.int32)[:, None]
        slot_gate = jnp.sum(
            jnp.where(place, gate_of.transpose(0, 2, 1)[:, :, None, :], 0.0), axis=-1
        )
        slot_gate = slot_gate.transpose(1, 0, 2).reshape(local_experts, ep_count * capacity, 1)
        x_slots, c_slots = select_rows(slots, tokens_all, cot_all, capacity)
    flat = (local_experts, ep_count * capacity, width)
    x_slots, c_slots = x_slots.reshape(flat), c_slots.reshape(flat)

    def over_rings(grads):
        return lax.psum_scatter(grads.reshape(-1, width), "tp", scatter_dimension=0, tiled=True)

    out_a, dx_a, *inner_a, dg_a = experts_both_ways(x_slots, c_slots, w_first, slot_gate, 0)
    grads_a = expert_grads(x_slots, c_slots, *inner_a, tp_count, 0)
    x_slots, grads_a = lax.optimization_barrier((x_slots, grads_a))
    mine_a = over_rings(grads_a)
    out_b, dx_b, *inner_b, dg_b = experts_both_ways(x_slots, c_slots, w_second, slot_gate, pair)
    deep = (pair, ep_count, capacity, width)
    dx_slots = [dx_a.reshape(deep), dx_b.reshape(deep)]
    out_slots = [out_a.reshape(deep), out_b.reshape(deep)]
    d_gate_slots = (
        jnp.concatenate([dg_a, dg_b])
        .reshape(local_experts, ep_count, capacity)
        .transpose(1, 0, 2)
        .reshape(ep_count, 1, local_experts * capacity)
    )
    if ring:
        dx_mine, gate_mine, grads_b = input_grads(
            slots_t, d_gate_slots, dx_slots, x_slots, c_slots, inner_b, experts, tp_count, 2
        )
    else:
        grads_b = expert_grads(x_slots, c_slots, *inner_b, tp_count, pair)
        dx_part, out_slots, gate_part = combine_rows(
            (ep_index * local_experts).reshape(1, 1), slots_t, dx_slots, out_slots, d_gate_slots, experts
        )
        dx_mine = lax.psum_scatter(dx_part, "ep", scatter_dimension=0).astype(F32)
        gate_mine = lax.psum_scatter(gate_part, "ep", scatter_dimension=0).astype(F32)
    dx_mine, mine_a, grads_b = lax.optimization_barrier((dx_mine, mine_a, grads_b))
    mine_b = over_rings(grads_b)
    mine_a, mine_b = [m.reshape(3, pair, -1, width) for m in (mine_a, mine_b)]
    w_gate_grad, w_up_grad = [
        jnp.concatenate([mine_a[i], mine_b[i]]).transpose(0, 2, 1).astype(F32) for i in range(2)
    ]
    w_down_grad = jnp.concatenate([mine_a[2], mine_b[2]]).astype(F32)
    lanes = gate_mine.shape[1] // 2
    d_gates = gate_mine[:, :experts] + gate_mine[:, lanes : lanes + experts]
    counts = jnp.sum((routes[:, :, None] == expert_ids[None, None, :]).astype(F32), axis=(0, 1))
    total_tokens = routes.shape[0]
    share = counts / (total_tokens * top)
    coeff = AUX * experts * share
    prob_local = jnp.sum(router_probs, axis=0)
    cot = cotangent.astype(F32)
    d_logits = gates * (d_gates - jnp.sum(gates * d_gates, axis=-1, keepdims=True))
    d_logits = d_logits + router_probs * (
        coeff - jnp.sum(router_probs * coeff, axis=-1, keepdims=True)
    )
    d_logits_low = d_logits.astype(BF)
    router_part = dot_tn(moe_in, d_logits_low)
    d_moe = dot_nt(d_logits_low, w_router) + dx_mine
    d_hidden, route_gain_part = norm_back(d_moe, hidden, route_gain[None])
    d_hidden = d_hidden + cot

    d_queries, d_keys, d_values, query_gain_part, key_gain_part, d_branch, output = attention_back(
        image_starts, queries, key_rows, values, lse, cosine, sine, q_gain, k_gain,
        w_out, d_hidden.astype(BF), slots_t, out_slots, hidden, 3,
    )
    w_query_grad, w_key_grad, w_value_grad, w_out_grad, inputs_grad, attn_gain_grad, small = projection_grads(
        normed, d_queries, d_keys, d_values, heads, d_branch,
        w_query, key_weight_matrix, value_weight_matrix,
        x_rows, d_hidden, attn_gain[None],
        [router_part, route_gain_part[0], query_gain_part[0], key_gain_part[0], prob_local],
        5,
    )
    w_router_grad, route_gain_grad, query_gain_grad, key_gain_grad, prob_all = small
    attn_gain_grad = attn_gain_grad[0]
    aux_loss = experts * jnp.sum(share * (prob_all / total_tokens))
    return (
        output,
        aux_loss,
        inputs_grad,
        attn_gain_grad,
        w_query_grad,
        w_key_grad,
        w_value_grad,
        query_gain_grad,
        key_gain_grad,
        w_out_grad,
        route_gain_grad,
        w_router_grad,
        w_gate_grad,
        w_up_grad,
        w_down_grad,
    )


def solution(mesh):
    return jax.shard_map(
        on_device,
        mesh=mesh,
        in_specs=(
            P("ep", None),
            P(),
            P(None, "tp"),
            P(None, "tp"),
            P(None, "tp"),
            P(),
            P(),
            P("tp", None),
            P(),
            P(),
            P("ep", None, "tp"),
            P("ep", None, "tp"),
            P("ep", "tp", None),
            P(),
            P("ep", None),
            P(("ep", "tp"), None),
        ),
        out_specs=(
            P(("ep", "tp"), None),
            P(),
            P(("ep", "tp"), None),
            P(),
            P("ep", "tp"),
            P("ep", "tp"),
            P("ep", "tp"),
            P(),
            P(),
            P("tp", "ep"),
            P(),
            P(),
            P("ep", None, "tp"),
            P("ep", None, "tp"),
            P("ep", "tp", None),
        ),
        check_vma=False,
    )
```

```python
import functools

import jax
import jax.numpy as jnp
from jax import lax
from jax.experimental import pallas as pl
from jax.experimental.pallas import tpu as pltpu
from jax.sharding import PartitionSpec as P

IMG = 256
EPS = 1e-06
AUX = 0.04
THETA = 1000000.0
MASKED = -1e30
NOWHERE = -(1 << 20)
BF = jnp.bfloat16
F32 = jnp.float32
VMEM_BYTES = 60 * 1024 * 1024


def dot_nn(a, b):
    return lax.dot_general(a, b, (((1,), (0,)), ((), ())), preferred_element_type=F32)


def dot_nt(a, b):
    return lax.dot_general(a, b, (((1,), (1,)), ((), ())), preferred_element_type=F32)


def dot_tn(a, b):
    return lax.dot_general(a, b, (((0,), (0,)), ((), ())), preferred_element_type=F32)


def params(**kw):
    return pltpu.CompilerParams(vmem_limit_bytes=VMEM_BYTES, **kw)


def rms_scale(value_rows):
    return lax.rsqrt(jnp.mean(value_rows * value_rows, axis=-1, keepdims=True) + EPS)


def plain_softmax(value_rows):
    top = jnp.max(value_rows, axis=-1, keepdims=True)
    expo = jnp.exp(value_rows - top)
    return expo / jnp.sum(expo, axis=-1, keepdims=True)


def rope_tables(length, size):
    half = size // 2
    freq = jnp.exp(-jnp.log(THETA) * (2.0 * jnp.arange(half, dtype=F32)) / size)
    angle = jnp.arange(length, dtype=F32)[:, None] * freq[None, :]
    cosine = jnp.cos(angle)
    sine = jnp.sin(angle)
    return (jnp.concatenate([cosine, cosine], axis=-1), jnp.concatenate([-sine, sine], axis=-1))


def turn(rows, cosine, sine):
    return rows * cosine + pltpu.roll(rows, rows.shape[-1] // 2, 1) * sine


def turn_back(rows, cosine, sine):
    return rows * cosine - pltpu.roll(rows, rows.shape[-1] // 2, 1) * sine


MESH = pl.DeviceIdType.MESH
ANY = pl.BlockSpec(memory_space=pl.ANY)
Z_AXIS = 4


def link_cost(us):
    return pl.CostEstimate(flops=0, bytes_accessed=int(us * 3.0e6), transcendentals=0)


def greet(partners):
    barrier = pltpu.get_barrier_semaphore()
    count = 0
    for there, device in partners:
        flag = jnp.asarray(there, jnp.int32)

        @pl.when(there)
        def _(device=device):
            pl.semaphore_signal(barrier, inc=1, device_id=device, device_id_type=MESH)

        count = count + flag
    pl.semaphore_wait(barrier, count)


def remote(src, dst, send, recv, device):
    return pltpu.make_async_remote_copy(
        src_ref=src, dst_ref=dst, send_sem=send, recv_sem=recv, device_id=device, device_id_type=MESH
    )


def ring_place():
    me = lax.axis_index("ep")
    z, y = me // 2, me % 2
    return me, z, y, {"ep": me + 2}, {"ep": me - 2}, {"ep": me + 1 - 2 * y}


def ring_pieces(ref, axis):
    unit = ref.shape[axis] // 16
    lead = (slice(None),) * axis
    return [
        ref.at[lead + (pl.ds(start * unit, count * unit),)]
        for start, count in ((0, 7), (7, 6), (13, 3))
    ]


class EpGather:
    def __init__(self, ins, outs, sems):
        self.ins, self.outs = ins, outs
        self.own_sem, self.up_send, self.up_recv, self.dn_send, self.dn_recv = sems[:5]
        self.y_send, self.y_recv = sems[5:]
        self.me, self.z, self.y, self.up, self.down, self.beside = ring_place()
        self.last = len(ins) - 1
        self.streams = [(a, a, self.y) for a in range(len(ins))]
        self.other = (self.last, len(ins), 1 - self.y)

    def partners(self):
        z = self.z
        return [(z < Z_AXIS - 1, self.up), (z > 0, self.down), (z >= 0, self.beside)]

    def block(self, a, zt, y):
        return self.outs[a].at[zt * 2 + y]

    def upward(self, src, stream, zt):
        a, i, y = stream
        return remote(src, self.block(a, zt, y), self.up_send.at[i, zt], self.up_recv.at[i, zt], self.up)

    def downward(self, src, stream, zt):
        a, i, y = stream
        return remote(src, self.block(a, zt, y), self.dn_send.at[i, zt], self.dn_recv.at[i, zt], self.down)

    def sideways(self, src, a, zt):
        return remote(
            src, self.block(a, zt, self.y), self.y_send.at[a, zt], self.y_recv.at[a, zt], self.beside
        )

    def both_ways(self, src, stream):
        z = self.z

        @pl.when(z < Z_AXIS - 1)
        def _():
            self.upward(src, stream, z).start()

        @pl.when(z > 0)
        def _():
            self.downward(src, stream, z).start()

    def start(self):
        self.sideways(self.ins[self.last], self.last, self.z).start()
        for stream in self.streams:
            a = stream[0]
            self.both_ways(self.ins[a], stream)
            if a != self.last:
                self.sideways(self.ins[a], a, self.z).start()
            pltpu.make_async_copy(self.ins[a], self.block(a, self.z, self.y), self.own_sem.at[a]).start()

    def cross(self):
        self.side_arrived(self.last, self.z)
        self.both_ways(self.block(self.last, self.z, 1 - self.y), self.other)

    def hop(self, d):
        z = self.z
        for stream in [self.other] + self.streams:
            a, _, y = stream

            @pl.when(z >= d)
            def _(a=a, y=y, stream=stream, zt=z - d):
                rows = self.block(a, zt, y)
                self.upward(rows, stream, zt).wait_recv()

                @pl.when(z < Z_AXIS - 1)
                def _():
                    self.upward(rows, stream, zt).start()

                if a != self.last:
                    self.sideways(rows, a, zt).start()

            @pl.when(z + d < Z_AXIS)
            def _(a=a, y=y, stream=stream, zt=z + d):
                rows = self.block(a, zt, y)
                self.downward(rows, stream, zt).wait_recv()

                @pl.when(z > 0)
                def _():
                    self.downward(rows, stream, zt).start()

                if a != self.last:
                    self.sideways(rows, a, zt).start()

    def own_done(self):
        for a, x in enumerate(self.ins):
            pltpu.make_async_copy(x, self.block(a, self.z, self.y), self.own_sem.at[a]).wait()

    def side_arrived(self, a, zt):
        rows = self.block(a, zt, 1 - self.y)
        remote(rows, rows, self.y_send.at[a, zt], self.y_recv.at[a, zt], self.beside).wait_recv()

    def side_done(self, zt):
        for a in range(self.last):
            self.side_arrived(a, zt)

    def sent(self):
        z = self.z
        self.sideways(self.block(self.last, z, self.y), self.last, z).wait_send()
        for stream in self.streams + [self.other]:
            a, _, y = stream
            for zt in range(Z_AXIS):
                src = self.block(a, zt, y)
                if a != self.last:
                    self.sideways(src, a, zt).wait_send()

                @pl.when((zt <= z) & (z < Z_AXIS - 1))
                def _(src=src, zt=zt, stream=stream):
                    self.upward(src, stream, zt).wait_send()

                @pl.when((zt >= z) & (z > 0))
                def _(src=src, zt=zt, stream=stream):
                    self.downward(src, stream, zt).wait_send()

    def finish(self):
        self.own_done()
        for zt in range(Z_AXIS):
            self.side_done(zt)
        self.sent()


def gather_sems():
    dma = pltpu.SemaphoreType.DMA
    return [dma((3,))] + [dma((4, Z_AXIS))] * 6


def one_hot(slots, capacity):
    local, rows = slots.shape
    slot = lax.broadcasted_iota(jnp.int32, (capacity, rows), 0)
    return [slot == slots[e : e + 1, :] for e in range(local)]


def gather_select_kernel(
    x_ref, cots_ref, slots_ref, picks_ref, router_ref, xs_ref, cs_ref, gate_ref,
    tokens, cots, chosen, load_sem, store_sem, *sems,
):
    local, _, capacity, width = xs_ref.shape
    blocks = tokens.shape[0]
    gather = EpGather(ring_pieces(x_ref, 0), ring_pieces(tokens, 1), sems)
    z, y = gather.z, gather.y
    greet(gather.partners())
    gather.start()

    def chosen_rows(j, rows):
        hits = one_hot(slots_ref[j], capacity)
        place = jnp.concatenate([h.astype(F32) for h in hits], axis=0).astype(BF)
        return dot_nn(place, rows).astype(BF).reshape(local, capacity, width), hits

    def load(j, slot):
        return pltpu.make_async_copy(cots_ref.at[j], cots.at[slot], load_sem.at[slot])

    def store(to, j, slot):
        return pltpu.make_async_copy(chosen.at[slot], to.at[:, j], store_sem.at[slot])

    load(0, 0).start()

    @pl.loop(0, blocks)
    def _(j):
        slot = lax.rem(j, 2)

        @pl.when(j + 1 < blocks)
        def _():
            load(j + 1, 1 - slot).start()

        load(j, slot).wait()

        @pl.when(j >= 2)
        def _():
            store(cs_ref, j - 2, slot).wait()

        chosen[slot] = chosen_rows(j, cots[slot])[0]
        store(cs_ref, j, slot).start()

    store(cs_ref, blocks - 2, 0).wait()
    store(cs_ref, blocks - 1, 1).wait()
    gather.cross()

    def take(j):
        rows = tokens[j]
        chosen[0], hits = chosen_rows(j, rows)
        copy = store(xs_ref, j, 0)
        copy.start()
        logits = dot_nt(router_ref[...], rows)
        picked = picks_ref[j] > 0
        kept = jnp.where(picked, logits, MASKED)
        expo = jnp.exp(kept - jnp.max(kept, axis=0, keepdims=True))
        expo = jnp.where(picked, expo, 0.0)
        gates = expo / jnp.sum(expo, axis=0, keepdims=True)
        for e, hit in enumerate(hits):
            gate_ref[e, j] = jnp.sum(jnp.where(hit, gates[e : e + 1, :], 0.0), axis=1, keepdims=True)
        copy.wait()

    gather.own_done()
    take(gather.me)
    for d in range(1, Z_AXIS + 1):
        if d < Z_AXIS:
            gather.hop(d)

        @pl.loop(0, 4)
        def _(i, d=d):
            beside = i >= 2
            far = jnp.where(beside, d - 1, d)
            zt = jnp.where(lax.rem(i, 2) == 0, z - far, z + far)
            there = (zt >= 0) & (zt < Z_AXIS) & ((i < 3) | (d > 1))

            @pl.when(there & beside)
            def _():
                gather.side_done(zt)

            @pl.when(there)
            def _():
                take(zt * 2 + jnp.where(beside, 1 - y, y))

    gather.sent()


def gather_select(rows, cot_all, slots, picks, router, capacity, number):
    ep_count = lax.axis_size("ep")
    _, local, block = slots.shape
    width = rows.shape[1]
    vmem = pl.BlockSpec(memory_space=pltpu.VMEM)
    dma = pltpu.SemaphoreType.DMA
    shape = (local, ep_count, capacity, width)
    return pl.pallas_call(
        gather_select_kernel,
        in_specs=[ANY, ANY, vmem, vmem, vmem],
        out_specs=[ANY, ANY, vmem],
        out_shape=[
            jax.ShapeDtypeStruct(shape, BF),
            jax.ShapeDtypeStruct(shape, BF),
            jax.ShapeDtypeStruct(shape[:3] + (1,), F32),
        ],
        scratch_shapes=[
            pltpu.VMEM((ep_count, block, width), BF),
            pltpu.VMEM((2, block, width), BF),
            pltpu.VMEM((2, local, capacity, width), BF),
            dma((2,)), dma((2,)),
        ]
        + gather_sems(),
        compiler_params=params(collective_id=number, has_side_effects=True),
        cost_estimate=link_cost(90.0),
        name="gather_select",
    )(rows, cot_all, slots, picks, router)


def add_rows(total, terms, chunk=16):
    @pl.loop(0, total.shape[0] // chunk)
    def _(i):
        rows = pl.ds(pl.multiple_of(i * chunk, chunk), chunk)
        value = terms[0][rows, :].astype(F32)
        for term in terms[1:]:
            value = value + term[rows, :].astype(F32)
        total[rows, :] = value.astype(total.dtype)


def scatter_order(z):
    table = ((3, 2, 1, 0), (3, 0, 2, 1), (0, 3, 1, 2), (0, 1, 2, 3))
    return [
        jnp.where(
            z == 0,
            table[0][k],
            jnp.where(z == 1, table[1][k], jnp.where(z == 2, table[2][k], table[3][k])),
        )
        for k in range(Z_AXIS)
    ]


class EpReduce:
    def __init__(self, ins, by_z, bufs, sems):
        self.ins, self.by_z = ins, by_z
        self.bufs = [bufs[2 * a : 2 * a + 2] for a in range(len(ins))]
        self.up_send, self.up_recv, self.dn_send, self.dn_recv, self.y_send, self.y_recv = sems
        self.me, self.z, self.y, self.up, self.down, self.beside = ring_place()
        self.order = scatter_order(self.z)
        self.streams = [(a, 0, self.y) for a in range(len(ins))]
        self.crossing = [(a, 1, 1 - self.y) for a in range(len(ins)) if by_z[a]]

    def partners(self):
        z = self.z
        return [(z < Z_AXIS - 1, self.up), (z > 0, self.down), (z >= 0, self.beside)]

    def mine(self, stream, zt):
        return self.ins[stream[0]].at[zt * 2 + stream[2]]

    def side(self, a, zt):
        return self.bufs[a][0].at[0 if self.by_z[a] else zt]

    def below(self, stream, zt):
        return self.bufs[stream[0]][1].at[stream[1] * (Z_AXIS + 1) + zt]

    def above(self, stream, zt, z):
        return self.below(stream, jnp.where(zt == z, Z_AXIS, zt))

    def to_side(self, a, zt):
        src = self.ins[a].at[zt * 2 + 1 - self.y]
        return remote(src, self.side(a, zt), self.y_send.at[a, zt], self.y_recv.at[a, zt], self.beside)

    def rising(self, stream, zt):
        i = 2 * stream[0] + stream[1]
        return remote(
            self.mine(stream, zt), self.below(stream, zt), self.up_send.at[i, zt], self.up_recv.at[i, zt], self.up
        )

    def falling(self, stream, zt):
        i = 2 * stream[0] + stream[1]
        return remote(
            self.mine(stream, zt), self.above(stream, zt, self.z - 1),
            self.dn_send.at[i, zt], self.dn_recv.at[i, zt], self.down,
        )

    def send_side(self, k):
        for a, by_z in enumerate(self.by_z):
            if not by_z:
                self.to_side(a, self.order[k]).start()

    def step(self, k):
        z, zt, last = self.z, self.order[k], Z_AXIS - 1
        late = [s for s in self.streams if not self.by_z[s[0]]]
        early = [s for s in self.streams if self.by_z[s[0]]]
        for stream in self.crossing + early + late:
            a = stream[0]
            mine = self.mine(stream, zt)
            terms = [mine]
            if not self.by_z[a]:
                self.to_side(a, zt).wait_recv()
                terms = [mine, self.side(a, zt)]
                ends = ((zt > z) & (z == 0)) | ((zt < z) & (z == last))

                @pl.when(ends)
                def _(mine=mine, terms=terms):
                    add_rows(mine, terms)

            @pl.when((zt > z) & (z > 0))
            def _(stream=stream, mine=mine, terms=terms):
                self.rising(stream, zt).wait_recv()
                add_rows(mine, terms + [self.below(stream, zt)])

            @pl.when((zt < z) & (z < last))
            def _(stream=stream, mine=mine, terms=terms):
                self.falling(stream, zt).wait_recv()
                add_rows(mine, terms + [self.above(stream, zt, z)])

            @pl.when(zt > z)
            def _(stream=stream):
                self.rising(stream, zt).start()

            @pl.when(zt < z)
            def _(stream=stream):
                self.falling(stream, zt).start()

        if k == last:
            for stream in self.crossing:
                rows = self.mine(stream, z)
                self.gathered(stream, [rows], functools.partial(add_rows, rows))
                self.to_side(stream[0], z).start()

    def gathered(self, stream, terms, write):
        z, last = self.z, Z_AXIS - 1

        @pl.when(z > 0)
        def _():
            self.rising(stream, z).wait_recv()

        @pl.when(z < last)
        def _():
            self.falling(stream, z).wait_recv()

        @pl.when(z == 0)
        def _():
            write(terms + [self.above(stream, z, z)])

        @pl.when(z == last)
        def _():
            write(terms + [self.below(stream, z)])

        @pl.when((z > 0) & (z < last))
        def _():
            write(terms + [self.below(stream, z), self.above(stream, z, z)])

    def own(self, a, write):
        if self.by_z[a]:
            self.to_side(a, self.z).wait_recv()
        stream = self.streams[a]
        self.gathered(stream, [self.mine(stream, self.z), self.side(a, self.z)], write)

    def sent(self):
        z = self.z
        for stream in self.streams + self.crossing:
            a = stream[0]
            for zt in range(Z_AXIS):
                if not self.by_z[a]:
                    self.to_side(a, zt).wait_send()

                @pl.when(zt > z)
                def _(stream=stream, zt=zt):
                    self.rising(stream, zt).wait_send()

                @pl.when(zt < z)
                def _(stream=stream, zt=zt):
                    self.falling(stream, zt).wait_send()

        for stream in self.crossing:
            self.to_side(stream[0], z).wait_send()


def reduce_scratch(rows, columns):
    unit = rows // 16
    out = []
    for count, slots in ((7, (Z_AXIS, Z_AXIS + 1)), (6, (Z_AXIS, Z_AXIS + 1)), (3, (1, 2 * (Z_AXIS + 1)))):
        out += [pltpu.VMEM((n, count * unit, columns), BF) for n in slots]
    return out


BY_Z = [False, False, True]


def reduce_sems(count):
    dma = pltpu.SemaphoreType.DMA
    return [dma((2 * count, Z_AXIS))] * 4 + [dma((count, Z_AXIS))] * 2


def token_hits(slots, capacity):
    rows, local = slots.shape
    lane = lax.broadcasted_iota(jnp.int32, (rows, local * capacity), 1)
    return [lane == slots[:, e : e + 1] + e * capacity for e in range(local)]


class SlotSums:
    def __init__(self, slots, first, second, buf, sem):
        self.slots, self.pair, self.buf, self.sem = slots, (first, second), buf, sem
        self.capacity = first.shape[2]

    def copies(self, j, at):
        n = self.pair[0].shape[0]
        return [
            pltpu.make_async_copy(
                ref.at[:, j], self.buf.at[at, pl.ds(i * n, n)], self.sem.at[at, i]
            )
            for i, ref in enumerate(self.pair)
        ]

    def fetch(self, j, at):
        for copy in self.copies(j, at):
            copy.start()

    def add(self, j, at, out):
        for copy in self.copies(j, at):
            copy.wait()
        place = jnp.zeros((), F32)
        for hit in token_hits(self.slots[j], self.capacity):
            place = jnp.where(hit, 1.0, place)
        rows = self.buf[at].reshape(-1, out.shape[1])
        out[...] = dot_nn(place.astype(BF), rows).astype(BF)

    def run(self, blocks, out, then):
        self.fetch(blocks[0], 0)
        for n, j in enumerate(blocks):
            if n + 1 < len(blocks):
                self.fetch(blocks[n + 1], (n + 1) % 2)
            self.add(j, n % 2, out.at[j])
            then(n)


def slot_sums_scratch(local, capacity, width):
    return [
        pltpu.VMEM((2, local, capacity, width), BF),
        pltpu.SemaphoreType.DMA((2, 2)),
    ]


def input_grads_kernel(
    slots, dgate, dx_a, dx_b, xs, cs, act, d_gate, d_up,
    out, gate_out, grads,
    part, gates, buf, sem, x_in, c_in, h_in, w_buf, in_sem, w_sem, *refs,
):
    sums = SlotSums(slots, dx_a, dx_b, buf, sem)
    reduce = EpReduce(ring_pieces(part, 1) + [gates], BY_Z + [False], refs[:8], refs[8:])
    order, y = reduce.order, reduce.y
    pair, number, inner = act.shape
    parts, _, _, hidden, width = grads.shape
    first = xs.shape[0] - pair
    pieces = width // x_in.shape[1]
    wide = x_in.shape[1]
    greet(reduce.partners())

    def cols(piece):
        return pl.ds(piece * wide, wide)

    def wide_copies(unit):
        e, piece = unit // pieces, unit % pieces
        return [
            pltpu.make_async_copy(xs.at[first + e, :, cols(piece)], x_in, in_sem.at[0]),
            pltpu.make_async_copy(cs.at[first + e, :, cols(piece)], c_in, in_sem.at[1]),
        ]

    def inner_copies(e):
        return [
            pltpu.make_async_copy(ref.at[e], h_in.at[kind], in_sem.at[2 + kind])
            for kind, ref in enumerate((d_gate, d_up, act))
        ]

    def written(unit):
        e, piece = unit // pieces, unit % pieces
        return pltpu.make_async_copy(w_buf, grads.at[:, :, e, :, cols(piece)], w_sem)

    def prepare(unit):
        for copy in wide_copies(unit) + (inner_copies(unit // pieces) if unit % pieces == 0 else []):
            copy.start()

    def weights(unit):
        for copy in wide_copies(unit) + (inner_copies(unit // pieces) if unit % pieces == 0 else []):
            copy.wait()
        if unit > 0:
            written(unit - 1).wait()
        for kind, right in enumerate((x_in, x_in, c_in)):
            grad = dot_tn(h_in[kind], right[...]).astype(BF)
            w_buf[:, kind] = grad.reshape(parts, hidden, wide)
        written(unit).start()
        if unit + 1 < pair * pieces:
            prepare(unit + 1)

    def payload(j):
        lanes = gates.shape[2]
        column = lax.broadcasted_iota(jnp.int32, (gates.shape[1], lanes), 1)
        pay = jnp.zeros(column.shape, F32)
        mine = reduce.me * slots.shape[2]
        for e, hit in enumerate(token_hits(slots[j], sums.capacity)):
            value = jnp.sum(jnp.where(hit, dgate[j], 0.0), axis=1, keepdims=True)
            high = value.astype(BF).astype(F32)
            pay = jnp.where(column == mine + e, high, pay)
            pay = jnp.where(column == mine + e + lanes // 2, value - high, pay)
        gates[j] = pay.astype(BF)

    def send(k):
        payload(order[k] * 2 + 1 - y)
        reduce.send_side(k)

    units = pair * pieces
    done = [units * (k + 1) // Z_AXIS for k in range(Z_AXIS)]
    sums.run([order[k] * 2 + 1 - y for k in range(Z_AXIS)], part, send)
    prepare(0)
    sums.run(
        [order[k] * 2 + y for k in range(Z_AXIS)], part, lambda k: payload(order[k] * 2 + y)
    )
    for k in range(Z_AXIS):
        for unit in range(done[k - 1] if k else 0, done[k]):
            weights(unit)
        reduce.step(k)
    for a, rows in enumerate(ring_pieces(out, 0) + [gate_out]):
        reduce.own(a, functools.partial(add_rows, rows))
    reduce.sent()
    written(units - 1).wait()


def input_grads(slots_t, dgate, dx, x_slots, c_slots, inner, experts, tp_count, number):
    ep_count, rows, local = slots_t.shape
    pair, _, capacity, width = dx[0].shape
    count, hidden = inner[0].shape[1:]
    lanes = -(-2 * experts // 128) * 128
    wide = width // 2
    dma = pltpu.SemaphoreType.DMA
    vmem = pl.BlockSpec(memory_space=pltpu.VMEM)
    return pl.pallas_call(
        input_grads_kernel,
        in_specs=[vmem, vmem] + [ANY] * 7,
        out_specs=[vmem, vmem, ANY],
        out_shape=[
            jax.ShapeDtypeStruct((rows, width), F32),
            jax.ShapeDtypeStruct((rows, lanes), F32),
            jax.ShapeDtypeStruct((tp_count, 3, pair, hidden // tp_count, width), BF),
        ],
        scratch_shapes=[
            pltpu.VMEM((ep_count, rows, width), BF),
            pltpu.VMEM((ep_count, rows, lanes), BF),
        ]
        + slot_sums_scratch(local, capacity, width)
        + [
            pltpu.VMEM((count, wide), BF),
            pltpu.VMEM((count, wide), BF),
            pltpu.VMEM((3, count, hidden), BF),
            pltpu.VMEM((tp_count, 3, hidden // tp_count, wide), BF),
            dma((5,)), dma,
        ]
        + reduce_scratch(rows, width)
        + [pltpu.VMEM((n, rows, lanes), BF) for n in (Z_AXIS, Z_AXIS + 1)]
        + reduce_sems(4),
        compiler_params=params(collective_id=number, has_side_effects=True),
        cost_estimate=link_cost(100.0),
        name="input_grads",
    )(slots_t, dgate, *dx, x_slots, c_slots, *inner)


class SumAll:
    def __init__(self, x, out, parts, own, send, recv, back_send, back_recv):
        self.x, self.out, self.parts, self.own = x, out, parts, own
        self.send, self.recv, self.back_send, self.back_recv = send, recv, back_send, back_recv
        self.tp_count = lax.axis_size("tp")
        self.total = lax.axis_size("ep") * self.tp_count
        self.me = lax.axis_index("ep") * self.tp_count + lax.axis_index("tp")

    def device(self, d):
        return {"ep": d // self.tp_count, "tp": d % self.tp_count}

    def other(self, i):
        return lax.rem(self.me + i, self.total)

    def each(self, act):
        @pl.loop(1, self.total)
        def _(i):
            act(i)

    def greet(self):
        barrier = pltpu.get_barrier_semaphore()
        self.each(
            lambda i: pl.semaphore_signal(
                barrier, inc=1, device_id=self.device(self.other(i)), device_id_type=MESH
            )
        )
        pl.semaphore_wait(barrier, self.total - 1)

    def outward(self, i):
        to = self.other(i)
        return remote(
            self.x.at[to], self.parts.at[self.me], self.send.at[i], self.recv.at[self.me], self.device(to)
        )

    def inward(self, i):
        origin = self.other(i)
        rows = self.parts.at[origin]
        return remote(rows, rows, self.send.at[i], self.recv.at[origin], self.device(origin))

    def spread(self, i):
        to = self.other(i)
        return remote(
            self.own, self.out.at[self.me], self.back_send.at[i], self.back_recv.at[self.me], self.device(to)
        )

    def returned(self, i):
        origin = self.other(i)
        rows = self.out.at[origin]
        return remote(rows, rows, self.back_send.at[i], self.back_recv.at[origin], self.device(origin))

    def start(self):
        self.each(lambda i: self.outward(i).start())
        self.parts[pl.ds(self.me, 1)] = self.x[pl.ds(self.me, 1)]

    def add(self):
        self.each(lambda i: self.inward(i).wait_recv())
        self.own[...] = jnp.sum(self.parts[...], axis=0)
        self.each(lambda i: self.spread(i).start())
        self.out[pl.ds(self.me, 1)] = self.own[...][None]

    def finish(self):
        self.each(lambda i: self.outward(i).wait_send())
        self.each(lambda i: self.returned(i).wait_recv())
        self.each(lambda i: self.spread(i).wait_send())


def sum_scratch(rows, total):
    dma = pltpu.SemaphoreType.DMA
    return [
        pltpu.VMEM((total, rows, 128), F32), pltpu.VMEM((rows, 128), F32),
        dma((total,)), dma((total,)), dma((total,)), dma((total,)),
    ]


def pack_small(values, total):
    flat = jnp.concatenate([v.reshape(-1) for v in values])
    rows = -(-flat.shape[0] // (total * 128 * 8)) * 8
    return jnp.pad(flat, (0, total * rows * 128 - flat.shape[0])).reshape(total, rows, 128)


def unpack_small(summed, values):
    summed = summed.reshape(-1)
    out, at = [], 0
    for v in values:
        out.append(summed[at : at + v.size].reshape(v.shape))
        at += v.size
    return out


def fill_bias(span_ref, bias, chunk=256):
    keys, length = bias.shape
    query = lax.broadcasted_iota(jnp.int32, (1, length), 1)

    def spans(pos):
        first = (pos >= span_ref[0, 0]) & (pos < span_ref[0, 0] + IMG)
        second = (pos >= span_ref[0, 1]) & (pos < span_ref[0, 1] + IMG)
        return jnp.where(first, 0, jnp.where(second, 1, -1))

    query_span = spans(query)
    query_other = jnp.where(query_span < 0, -2, query_span)
    for start in range(0, keys, chunk):
        key = start + lax.broadcasted_iota(jnp.int32, (chunk, 1), 0)
        ok = (key <= query) | (spans(key) == query_other)
        bias[start : start + chunk, :] = jnp.where(ok, 0.0, MASKED)


def query_tiles(length):
    tile = min(IMG, length)
    return [
        (start, tile, min(length, start + tile + -(-IMG // tile) * tile))
        for start in range(0, length, tile)
    ]


def attention_kernel(
    span_ref, q_ref, k_ref, v_ref, cos_ref, sin_ref, qg_ref, kg_ref, w_out_ref, cot_ref,
    out_ref, lse_ref, rows_ref, cots_ref,
    bias, k_rot, v_t, heads, part, core_rows, x_rows, core_send, core_recv, x_send, x_recv, *sems,
):
    factor = q_ref.shape[-1] ** (-0.5)
    cosine, sine = cos_ref[...], sin_ref[...]
    step = pl.program_id(0)
    size = q_ref.shape[-1]
    me = lax.axis_index("tp")
    x, c = me // 2, me % 2
    other_core, other_x = {"tp": x * 2 + 1 - c}, {"tp": (1 - x) * 2 + c}
    gather = EpGather(ring_pieces(cot_ref, 0), ring_pieces(cots_ref, 1), sems)

    @pl.when(step == 0)
    def _():
        greet(gather.partners() + [(x >= 0, other_core), (x >= 0, other_x)])
        gather.start()
        fill_bias(span_ref, bias)
        k = k_ref[...]
        k_rot[...] = turn(k * rms_scale(k) * kg_ref[...], cosine, sine).astype(BF)
        v_t[...] = v_ref[...].astype(F32).T.astype(BF)

    @pl.when(step == 2)
    def _():
        gather.cross()

    @pl.when(step == pl.num_programs(0) - 2)
    def _():
        gather.hop(1)

    q = q_ref[...]
    q_rot = turn(q * rms_scale(q) * qg_ref[...], cosine, sine).astype(BF)
    for start, tile, keys in query_tiles(q.shape[0]):
        cols = slice(start, start + tile)
        s = dot_nt(k_rot[:keys, :], q_rot[cols, :]) * factor + bias[:keys, cols]
        top = jnp.max(s, axis=0, keepdims=True)
        p = jnp.exp(s - top)
        total = jnp.sum(p, axis=0, keepdims=True)
        o_t = dot_nn(v_t[:, :keys], p.astype(BF)) / total
        rows = o_t.T.astype(BF)
        out_ref[cols, :] = rows
        heads[step, cols, :] = rows
        lse_ref[0, :, cols] = top + jnp.log(total)

    @pl.when(step == pl.num_programs(0) - 1)
    def _():
        count = heads.shape[0]
        block = rows_ref.shape[0]

        def project(tp):
            lines = pl.ds(pl.multiple_of(tp * block, block), block)
            rows = jnp.concatenate([heads[h, lines, :] for h in range(count)], axis=1)
            part[tp] = dot_nn(rows, w_out_ref[...]).astype(BF)

        def to_core(xt):
            return remote(
                part.at[xt * 2 + 1 - c], core_rows.at[xt],
                core_send.at[xt], core_recv.at[xt], other_core,
            )

        far, near = part.at[(1 - x) * 2 + c], part.at[x * 2 + c]
        to_x = remote(far, x_rows, x_send, x_recv, other_x)
        project((1 - x) * 2 + 1 - c)
        to_core(1 - x).start()
        project((1 - x) * 2 + c)
        to_core(1 - x).wait_recv()
        add_rows(far, [far, core_rows.at[1 - x]])
        to_x.start()
        project(x * 2 + 1 - c)
        to_core(x).start()
        project(x * 2 + c)
        gather.hop(2)
        to_core(x).wait_recv()
        gather.hop(3)
        to_x.wait_recv()
        add_rows(rows_ref, [near, core_rows.at[x], x_rows])
        gather.finish()
        to_core(1 - x).wait_send()
        to_core(x).wait_send()
        to_x.wait_send()


def plain_attention_kernel(
    span_ref, q_ref, k_ref, v_ref, cos_ref, sin_ref, qg_ref, kg_ref, out_ref, lse_ref,
    bias, k_rot, v_t,
):
    factor = q_ref.shape[-1] ** (-0.5)
    cosine, sine = cos_ref[...], sin_ref[...]

    @pl.when(pl.program_id(0) == 0)
    def _():
        fill_bias(span_ref, bias)
        k = k_ref[...]
        k_rot[...] = turn(k * rms_scale(k) * kg_ref[...], cosine, sine).astype(BF)
        v_t[...] = v_ref[...].astype(F32).T.astype(BF)

    q = q_ref[...]
    q_rot = turn(q * rms_scale(q) * qg_ref[...], cosine, sine).astype(BF)
    for start, tile, keys in query_tiles(q.shape[0]):
        cols = slice(start, start + tile)
        s = dot_nt(k_rot[:keys, :], q_rot[cols, :]) * factor + bias[:keys, cols]
        top = jnp.max(s, axis=0, keepdims=True)
        p = jnp.exp(s - top)
        total = jnp.sum(p, axis=0, keepdims=True)
        o_t = dot_nn(v_t[:, :keys], p.astype(BF)) / total
        out_ref[cols, :] = o_t.T.astype(BF)
        lse_ref[0, :, cols] = top + jnp.log(total)


def attention(span, q, k, v, cosine, sine, q_gain, k_gain, w_out, cotangent, number):
    length, size = k.shape
    heads = q.shape[1] // size
    whole = pl.BlockSpec((length, size), lambda h: (0, 0))
    head = pl.BlockSpec((length, size), lambda h: (0, h))
    gain = pl.BlockSpec((1, size), lambda h: (0, 0))
    in_specs = [
        pl.BlockSpec(memory_space=pltpu.SMEM), head, whole, whole, whole, whole, gain, gain,
    ]
    out_specs = [head, pl.BlockSpec((1, 1, length), lambda h: (h, 0, 0))]
    out_shape = [
        jax.ShapeDtypeStruct((length, heads * size), BF),
        jax.ShapeDtypeStruct((heads, 1, length), F32),
    ]
    scratch = [
        pltpu.VMEM((length, length), F32),
        pltpu.VMEM((length, size), BF),
        pltpu.VMEM((size, length), BF),
    ]
    args = (span, q, k, v, cosine, sine, q_gain, k_gain)
    ep_count, tp_count = lax.axis_size("ep"), lax.axis_size("tp")
    if ep_count != 2 * Z_AXIS:
        out, lse = pl.pallas_call(
            plain_attention_kernel,
            grid=(heads,),
            in_specs=in_specs,
            out_specs=out_specs,
            out_shape=out_shape,
            scratch_shapes=scratch,
            compiler_params=params(),
            name="plain_attention",
        )(*args)
        rows = lax.psum_scatter(
            dot_nn(out, w_out).astype(BF), "tp", scatter_dimension=0, tiled=True
        )
        return out, lse, rows.astype(F32), lax.all_gather(cotangent, "ep")
    block, width = cotangent.shape
    dma = pltpu.SemaphoreType.DMA
    return pl.pallas_call(
        attention_kernel,
        grid=(heads,),
        in_specs=in_specs + [pl.BlockSpec(w_out.shape, lambda h: (0, 0)), ANY],
        out_specs=out_specs + [pl.BlockSpec((block, width), lambda h: (0, 0)), ANY],
        out_shape=out_shape
        + [
            jax.ShapeDtypeStruct((block, width), F32),
            jax.ShapeDtypeStruct((ep_count, block, width), BF),
        ],
        scratch_shapes=scratch
        + [
            pltpu.VMEM((heads, length, size), BF),
            pltpu.VMEM((tp_count, block, width), BF),
            pltpu.VMEM((2, block, width), BF),
            pltpu.VMEM((block, width), BF),
            dma((2,)), dma((2,)), dma, dma,
        ]
        + gather_sems(),
        compiler_params=params(collective_id=number, has_side_effects=True),
        cost_estimate=link_cost(90.0),
        name="attention",
    )(*args, w_out, cotangent)


def norm_back(grads, rows, gain):
    scale = rms_scale(rows)
    gain_part = jnp.sum(grads * rows * scale, axis=0, keepdims=True)
    inner = grads * gain
    mean = jnp.mean(inner * rows, axis=-1, keepdims=True)
    return scale * inner - rows * (scale * scale * scale * mean), gain_part


def plain_attention_back_kernel(
    span_ref, q_ref, k_ref, v_ref, grad_ref, lse_ref, cos_ref, sin_ref, qg_ref, kg_ref,
    dq_ref, dk_ref, dv_ref, dqg_ref, dkg_ref,
    bias, k_rot, k_t, dk_acc, dv_acc, dq_t,
):
    factor = q_ref.shape[-1] ** (-0.5)
    cosine, sine = cos_ref[...], sin_ref[...]
    step = pl.program_id(0)

    @pl.when(step == 0)
    def _():
        fill_bias(span_ref, bias)
        k = k_ref[...]
        rotated = turn(k * rms_scale(k) * kg_ref[...], cosine, sine)
        k_rot[...] = rotated.astype(BF)
        k_t[...] = rotated.T.astype(BF)
        dk_acc[...] = jnp.zeros_like(dk_acc)
        dv_acc[...] = jnp.zeros_like(dv_acc)
        dqg_ref[...] = jnp.zeros_like(dqg_ref)

    q = q_ref[...]
    q_rot = turn(q * rms_scale(q) * qg_ref[...], cosine, sine).astype(BF)
    for start, tile, keys in query_tiles(q.shape[0]):
        cols = slice(start, start + tile)
        s = dot_nt(k_rot[:keys, :], q_rot[cols, :]) * factor + bias[:keys, cols]
        p = jnp.exp(s - lse_ref[0, :, cols])
        grad = grad_ref[cols, :]
        dp = dot_nt(v_ref[:keys, :], grad)
        mean = jnp.sum(p * dp, axis=0, keepdims=True)
        raw = (p * (dp - mean) * factor).astype(BF)
        dq_t[:, cols] = dot_nn(k_t[:, :keys], raw)
        dk_acc[:keys, :] += dot_nn(raw, q_rot[cols, :])
        dv_acc[:keys, :] += dot_nn(p.astype(BF), grad)
    back, gain_part = norm_back(turn_back(dq_t[...].T, cosine, sine), q, qg_ref[...])
    dq_ref[...] = back.astype(BF)
    dqg_ref[...] += gain_part

    @pl.when(step == pl.num_programs(0) - 1)
    def _():
        back, gain_part = norm_back(turn_back(dk_acc[...], cosine, sine), k_ref[...], kg_ref[...])
        dk_ref[...] = back.astype(BF)
        dkg_ref[...] = gain_part
        dv_ref[...] = dv_acc[...].astype(BF)


def plain_attention_back(span, q, k, v, grads, lse, cosine, sine, q_gain, k_gain):
    length, size = k.shape
    heads = q.shape[1] // size
    whole = pl.BlockSpec((length, size), lambda h: (0, 0))
    head = pl.BlockSpec((length, size), lambda h: (0, h))
    gain = pl.BlockSpec((1, size), lambda h: (0, 0))
    return pl.pallas_call(
        plain_attention_back_kernel,
        grid=(heads,),
        in_specs=[
            pl.BlockSpec(memory_space=pltpu.SMEM), head, whole, whole, head,
            pl.BlockSpec((1, 1, length), lambda h: (h, 0, 0)), whole, whole, gain, gain,
        ],
        out_specs=[head, whole, whole, gain, gain],
        out_shape=[
            jax.ShapeDtypeStruct((length, heads * size), BF),
            jax.ShapeDtypeStruct((length, size), BF),
            jax.ShapeDtypeStruct((length, size), BF),
            jax.ShapeDtypeStruct((1, size), F32),
            jax.ShapeDtypeStruct((1, size), F32),
        ],
        scratch_shapes=[
            pltpu.VMEM((length, length), F32),
            pltpu.VMEM((length, size), BF),
            pltpu.VMEM((size, length), BF),
            pltpu.VMEM((length, size), F32),
            pltpu.VMEM((length, size), F32),
            pltpu.VMEM((size, length), F32),
        ],
        compiler_params=params(),
        name="plain_attention_back",
    )(span, q, k, v, grads, lse, cosine, sine, q_gain, k_gain)


def attention_back_kernel(
    span_ref, q_ref, k_ref, v_ref, lse_ref, cos_ref, sin_ref, qg_ref, kg_ref,
    w_out_ref, rows_ref, slots_ref, out_a, out_b, hidden_ref,
    dq_ref, dk_ref, dv_ref, dqg_ref, dkg_ref, branch_ref, output_ref,
    bias, k_rot, k_t, dk_acc, dv_acc, dq_t, branch, grads, part, buf, sem,
    own_sem, out_sem, core_send, core_recv, x_send, x_recv, *refs,
):
    factor = q_ref.shape[-1] ** (-0.5)
    size = q_ref.shape[-1]
    cosine, sine = cos_ref[...], sin_ref[...]
    step = pl.program_id(0)
    me = lax.axis_index("tp")
    x, c = me // 2, me % 2
    other_core, other_x = {"tp": x * 2 + 1 - c}, {"tp": (1 - x) * 2 + c}
    reduce = EpReduce(ring_pieces(part, 1), BY_Z, refs[:6], refs[6:])
    sums = SlotSums(slots_ref, out_a, out_b, buf, sem)
    order, y = reduce.order, reduce.y
    block = rows_ref.shape[0]
    near_other, far, far_other = x * 2 + 1 - c, (1 - x) * 2 + c, (1 - x) * 2 + 1 - c

    def to_core(slot, src, tp):
        return remote(src, branch.at[tp], core_send.at[slot], core_recv.at[slot], other_core)

    def to_x(tp):
        return remote(rows_ref, branch.at[tp], x_send, x_recv, other_x)

    def own_rows():
        return pltpu.make_async_copy(rows_ref, branch.at[me], own_sem)

    def whole_branch():
        return pltpu.make_async_copy(branch, branch_ref, out_sem)

    @pl.when(step == 0)
    def _():
        greet(reduce.partners() + [(x >= 0, other_core), (x >= 0, other_x)])
        to_x(me).start()
        to_core(0, rows_ref, me).start()
        own_rows().start()
        sums.run([order[k] * 2 + 1 - y for k in range(Z_AXIS)], part, reduce.send_side)
        fill_bias(span_ref, bias)
        k = k_ref[...]
        rotated = turn(k * rms_scale(k) * kg_ref[...], cosine, sine)
        k_rot[...] = rotated.astype(BF)
        k_t[...] = rotated.T.astype(BF)
        dk_acc[...] = jnp.zeros_like(dk_acc)
        dv_acc[...] = jnp.zeros_like(dv_acc)
        dqg_ref[...] = jnp.zeros_like(dqg_ref)

        def head_grads(tp):
            lines = pl.ds(pl.multiple_of(tp * block, block), block)
            rows = dot_nt(branch[tp], w_out_ref[...]).astype(BF)
            for h in range(grads.shape[0]):
                grads[h, lines, :] = rows[:, h * size : (h + 1) * size]

        own_rows().wait()
        head_grads(me)
        to_core(0, rows_ref, near_other).wait_recv()
        head_grads(near_other)
        sums.run([order[k] * 2 + y for k in range(Z_AXIS)], part, lambda k: None)
        reduce.step(0)
        to_x(far).wait_recv()
        to_core(1, branch.at[far], far).start()
        head_grads(far)
        to_core(1, branch.at[far], far_other).wait_recv()
        head_grads(far_other)
        whole_branch().start()

    for k, head in ((1, 1), (2, 5)):

        @pl.when(step == head)
        def _(k=k):
            reduce.step(k)

    q = q_ref[...]
    q_rot = turn(q * rms_scale(q) * qg_ref[...], cosine, sine).astype(BF)
    for start, tile, keys in query_tiles(q.shape[0]):
        cols = slice(start, start + tile)
        s = dot_nt(k_rot[:keys, :], q_rot[cols, :]) * factor + bias[:keys, cols]
        p = jnp.exp(s - lse_ref[0, :, cols])
        grad = grads[step, cols, :]
        dp = dot_nt(v_ref[:keys, :], grad)
        mean = jnp.sum(p * dp, axis=0, keepdims=True)
        raw = (p * (dp - mean) * factor).astype(BF)
        dq_t[:, cols] = dot_nn(k_t[:, :keys], raw)
        dk_acc[:keys, :] += dot_nn(raw, q_rot[cols, :])
        dv_acc[:keys, :] += dot_nn(p.astype(BF), grad)
    back, gain_part = norm_back(turn_back(dq_t[...].T, cosine, sine), q, qg_ref[...])
    dq_ref[...] = back.astype(BF)
    dqg_ref[...] += gain_part

    @pl.when(step == pl.num_programs(0) - 1)
    def _():
        back, gain_part = norm_back(turn_back(dk_acc[...], cosine, sine), k_ref[...], kg_ref[...])
        dk_ref[...] = back.astype(BF)
        dkg_ref[...] = gain_part
        dv_ref[...] = dv_acc[...].astype(BF)
        reduce.step(Z_AXIS - 1)
        pairs = zip(ring_pieces(output_ref, 0), ring_pieces(hidden_ref, 0))
        for a, (rows, residual) in enumerate(pairs):
            reduce.own(a, lambda terms, rows=rows, residual=residual: add_rows(rows, terms + [residual]))
        reduce.sent()
        whole_branch().wait()
        to_x(me).wait_send()
        to_core(0, rows_ref, me).wait_send()
        to_core(1, branch.at[far], far).wait_send()


def attention_back(
    span, q, k, v, lse, cosine, sine, q_gain, k_gain, w_out, d_rows, slots_t, out, hidden, number
):
    length, size = k.shape
    heads = q.shape[1] // size
    ep_count, tp_count = lax.axis_size("ep"), lax.axis_size("tp")
    if ep_count != 2 * Z_AXIS:
        branch = lax.all_gather(d_rows, "tp", axis=0, tiled=True)
        grads = dot_nt(branch, w_out).astype(BF)
        mine = lax.psum_scatter(out, "ep", scatter_dimension=0)
        back = plain_attention_back(span, q, k, v, grads, lse, cosine, sine, q_gain, k_gain)
        return *back, branch, (hidden + mine.astype(F32)).astype(BF)
    block, width = d_rows.shape
    whole = pl.BlockSpec((length, size), lambda h: (0, 0))
    head = pl.BlockSpec((length, size), lambda h: (0, h))
    gain = pl.BlockSpec((1, size), lambda h: (0, 0))
    rows = pl.BlockSpec((block, width), lambda h: (0, 0))
    dma = pltpu.SemaphoreType.DMA
    *back, branch, output = pl.pallas_call(
        attention_back_kernel,
        grid=(heads,),
        in_specs=[
            pl.BlockSpec(memory_space=pltpu.SMEM), head, whole, whole,
            pl.BlockSpec((1, 1, length), lambda h: (h, 0, 0)), whole, whole, gain, gain,
            pl.BlockSpec(w_out.shape, lambda h: (0, 0), pipeline_mode=pl.Buffered(1)), ANY,
            pl.BlockSpec(slots_t.shape, lambda h: (0, 0, 0), pipeline_mode=pl.Buffered(1)), ANY, ANY,
            pl.BlockSpec((block, width), lambda h: (0, 0), pipeline_mode=pl.Buffered(1)),
        ],
        out_specs=[head, whole, whole, gain, gain, ANY, rows],
        out_shape=[
            jax.ShapeDtypeStruct((length, heads * size), BF),
            jax.ShapeDtypeStruct((length, size), BF),
            jax.ShapeDtypeStruct((length, size), BF),
            jax.ShapeDtypeStruct((1, size), F32),
            jax.ShapeDtypeStruct((1, size), F32),
            jax.ShapeDtypeStruct((tp_count, block, width), BF),
            jax.ShapeDtypeStruct((block, width), BF),
        ],
        scratch_shapes=[
            pltpu.VMEM((length, length), F32),
            pltpu.VMEM((length, size), BF),
            pltpu.VMEM((size, length), BF),
            pltpu.VMEM((length, size), F32),
            pltpu.VMEM((length, size), F32),
            pltpu.VMEM((size, length), F32),
            pltpu.VMEM((tp_count, block, width), BF),
            pltpu.VMEM((heads, length, size), BF),
        ]
        + [pltpu.VMEM((ep_count, block, width), BF)]
        + slot_sums_scratch(slots_t.shape[2], out[0].shape[2], width)
        + [dma, dma, dma((2,)), dma((2,)), dma, dma]
        + reduce_scratch(block, width)
        + reduce_sems(3),
        compiler_params=params(collective_id=number, has_side_effects=True),
        cost_estimate=link_cost(100.0),
        name="attention_back",
    )(span, q, k, v, lse, cosine, sine, q_gain, k_gain, w_out, d_rows, slots_t, *out, hidden)
    return *back, branch.reshape(-1, width), output


def projection_grads_kernel(
    normed, dq, dk, dv, heads, branch, wq, wk, wv, x_rows, d_hidden, gain, small,
    gq_ref, gk_ref, gv_ref, gout_ref, inputs_grad, gain_grad, small_sum,
    blocks, out_blocks, gout, part, core_rows, far_rows, gain_own, gains,
    core_send, core_recv, x_send, x_recv, gain_send, gain_recv, *refs,
):
    me = lax.axis_index("tp")
    x, c = me // 2, me % 2
    other_core, other_x = {"tp": x * 2 + 1 - c}, {"tp": (1 - x) * 2 + c}
    sums = SumAll(small, small_sum, *refs[:6])
    reduce = EpReduce(
        ring_pieces(blocks, 1) + ring_pieces(out_blocks, 1), BY_Z * 2, refs[6:18], refs[18:]
    )
    order, y = reduce.order, reduce.y
    rows, width = inputs_grad.shape
    nq, nk = dq.shape[1], dk.shape[1]

    sums.greet()
    sums.start()

    def fill(j):
        cols = pl.ds(pl.multiple_of(j * rows, rows), rows)
        left = normed[:, cols].T
        blocks[j, :, 0:nq] = dot_nn(left, dq[...]).astype(BF)
        blocks[j, :, nq : nq + nk] = dot_nn(left, dk[...]).astype(BF)
        blocks[j, :, nq + nk : nq + 2 * nk] = dot_nn(left, dv[...]).astype(BF)
        out_blocks[j] = dot_nn(branch[:, cols].T, heads[...]).astype(BF)

    def spread_back(tp):
        lines = pl.ds(pl.multiple_of(tp * rows, rows), rows)
        for start in range(0, width, width // 4):
            cols = slice(start, start + width // 4)
            part[tp, :, cols] = (
                dot_nt(dq[lines, :], wq[cols, :])
                + dot_nt(dk[lines, :], wk[cols, :])
                + dot_nt(dv[lines, :], wv[cols, :])
            ).astype(BF)

    def to_core(xt):
        return remote(
            part.at[xt * 2 + 1 - c], core_rows.at[xt], core_send.at[xt], core_recv.at[xt], other_core
        )

    far, near = part.at[(1 - x) * 2 + c], part.at[x * 2 + c]
    to_x = remote(far, far_rows, x_send, x_recv, other_x)

    for k in range(2):
        fill(order[k] * 2 + 1 - y)
        reduce.send_side(k)
    spread_back((1 - x) * 2 + 1 - c)
    to_core(1 - x).start()
    spread_back((1 - x) * 2 + c)
    to_core(1 - x).wait_recv()
    add_rows(far, [far, core_rows.at[1 - x]])
    to_x.start()
    for k in range(2, Z_AXIS):
        fill(order[k] * 2 + 1 - y)
        reduce.send_side(k)
    fill(order[0] * 2 + y)
    reduce.step(0)
    spread_back(x * 2 + 1 - c)
    to_core(x).start()
    spread_back(x * 2 + c)
    for k in range(1, Z_AXIS):
        fill(order[k] * 2 + y)
    reduce.step(1)
    to_core(x).wait_recv()
    to_x.wait_recv()

    chunk = 32
    gain_own[...] = jnp.zeros_like(gain_own)

    @pl.loop(0, rows // chunk)
    def _(i):
        lines = pl.ds(pl.multiple_of(i * chunk, chunk), chunk)
        grad = near[lines, :].astype(F32) + core_rows[x, lines, :].astype(F32)
        grad = grad + far_rows[lines, :].astype(F32)
        back, gain_part = norm_back(grad, x_rows[lines, :].astype(F32), gain[...])
        inputs_grad[lines, :] = d_hidden[lines, :] + back
        gain_own[...] += gain_part

    def tell(i):
        to = sums.other(i)
        return remote(
            gain_own, gains.at[sums.me], gain_send.at[i], gain_recv.at[sums.me], sums.device(to)
        )

    def heard(i):
        origin = sums.other(i)
        row = gains.at[origin]
        return remote(row, row, gain_send.at[i], gain_recv.at[origin], sums.device(origin))

    sums.each(lambda i: tell(i).start())
    gains[pl.ds(sums.me, 1)] = gain_own[...][None]
    reduce.step(2)
    sums.add()
    reduce.step(3)

    def total_of(terms):
        value = terms[0][...].astype(F32)
        for term in terms[1:]:
            value = value + term[...].astype(F32)
        return value

    sums.each(lambda i: heard(i).wait_recv())
    gain_grad[...] = jnp.sum(gains[...], axis=0)
    results = zip(*[ring_pieces(ref, 0) for ref in (gq_ref, gk_ref, gv_ref)])
    for a, (to_q, to_k, to_v) in enumerate(results):

        def write(terms, to_q=to_q, to_k=to_k, to_v=to_v):
            value = total_of(terms)
            to_q[...] = value[:, 0:nq]
            to_k[...] = value[:, nq : nq + nk]
            to_v[...] = value[:, nq + nk :]

        reduce.own(a, write)
    for a, rows_to in enumerate(ring_pieces(gout, 0)):

        def write_out(terms, rows_to=rows_to):
            rows_to[...] = total_of(terms)

        reduce.own(3 + a, write_out)
    gout_ref[...] = gout[...].T
    reduce.sent()
    to_core(1 - x).wait_send()
    to_core(x).wait_send()
    to_x.wait_send()
    sums.each(lambda i: tell(i).wait_send())
    sums.finish()


def projection_grads(
    normed, dq, dk, dv, heads, branch, wq, wk, wv, x_rows, d_hidden, gain, small_values, number
):
    rows, width = x_rows.shape
    ep_count, tp_count = lax.axis_size("ep"), lax.axis_size("tp")
    total = ep_count * tp_count
    small = pack_small(small_values, total)
    if ep_count != 2 * Z_AXIS:

        def over_sequences(part, dim):
            return lax.psum_scatter(
                part.astype(BF), "ep", scatter_dimension=dim, tiled=True
            ).astype(F32)

        d_normed = (dot_nt(dq, wq) + dot_nt(dk, wk) + dot_nt(dv, wv)).astype(BF)
        d_mine = lax.psum_scatter(d_normed, "tp", scatter_dimension=0, tiled=True)
        back, gain_part = norm_back(d_mine.astype(F32), x_rows.astype(F32), gain)
        gain_sum, small_sum = lax.psum((gain_part, small), ("ep", "tp"))
        return (
            over_sequences(dot_tn(normed, dq), 0),
            over_sequences(dot_tn(normed, dk), 0),
            over_sequences(dot_tn(normed, dv), 0),
            over_sequences(dot_tn(heads, branch), 1),
            d_hidden + back,
            gain_sum,
            unpack_small(small_sum, small_values),
        )
    nq, nk = dq.shape[1], dk.shape[1]
    nh = heads.shape[1]
    vmem = pl.BlockSpec(memory_space=pltpu.VMEM)
    dma = pltpu.SemaphoreType.DMA
    *grads, small_sum = pl.pallas_call(
        projection_grads_kernel,
        in_specs=[vmem] * 13,
        out_specs=[vmem] * 7,
        out_shape=[
            jax.ShapeDtypeStruct((rows, nq), F32),
            jax.ShapeDtypeStruct((rows, nk), F32),
            jax.ShapeDtypeStruct((rows, nk), F32),
            jax.ShapeDtypeStruct((nh, rows), F32),
            jax.ShapeDtypeStruct((rows, width), F32),
            jax.ShapeDtypeStruct((1, width), F32),
            jax.ShapeDtypeStruct(small.shape, F32),
        ],
        scratch_shapes=[
            pltpu.VMEM((ep_count, rows, nq + 2 * nk), BF),
            pltpu.VMEM((ep_count, rows, nh), BF),
            pltpu.VMEM((rows, nh), F32),
            pltpu.VMEM((tp_count, rows, width), BF),
            pltpu.VMEM((2, rows, width), BF),
            pltpu.VMEM((rows, width), BF),
            pltpu.VMEM((1, width), F32),
            pltpu.VMEM((total, 1, width), F32),
            dma((2,)), dma((2,)), dma, dma, dma((total,)), dma((total,)),
        ]
        + sum_scratch(small.shape[1], total)
        + reduce_scratch(rows, nq + 2 * nk)
        + reduce_scratch(rows, nh)
        + reduce_sems(6),
        compiler_params=params(collective_id=number, has_side_effects=True),
        cost_estimate=link_cost(110.0),
        name="projection_grads",
    )(normed, dq, dk, dv, heads, branch, wq, wk, wv, x_rows, d_hidden, gain, small)
    return *grads, unpack_small(small_sum, small_values)


def select_kernel(slot_ref, x_ref, c_ref, xs_ref, cs_ref):
    local, _, capacity, width = xs_ref.shape
    rows = x_ref.shape[1]
    place = jnp.concatenate(
        [
            (
                slot_ref[0, e : e + 1, :]
                == lax.broadcasted_iota(jnp.int32, (capacity, rows), 0)
            ).astype(F32)
            for e in range(local)
        ],
        axis=0,
    ).astype(BF)
    xs_ref[...] = dot_nn(place, x_ref[0]).astype(BF).reshape(xs_ref.shape)
    cs_ref[...] = dot_nn(place, c_ref[0]).astype(BF).reshape(cs_ref.shape)


def select_rows(slots, tokens, cots, capacity):
    blocks, local, rows = slots.shape
    width = tokens.shape[-1]
    block = pl.BlockSpec((1, rows, width), lambda b: (b, 0, 0))
    out = pl.BlockSpec((local, 1, capacity, width), lambda b: (0, b, 0, 0))
    shape = jax.ShapeDtypeStruct((local, blocks, capacity, width), BF)
    return pl.pallas_call(
        select_kernel,
        grid=(blocks,),
        in_specs=[pl.BlockSpec((1, local, rows), lambda b: (b, 0, 0)), block, block],
        out_specs=[out, out],
        out_shape=[shape, shape],
        compiler_params=params(),
        name="select_rows",
    )(slots, tokens, cots)


def pack_kernel(gate_ref, up_ref, down_ref, out_ref):
    for kind, ref in enumerate((gate_ref, up_ref, down_ref)):
        out_ref[kind, 0] = ref[0]


def pack_weights(weights, first, count):
    _, hidden, width = weights[0].shape
    block = pl.BlockSpec((1, hidden, width), lambda e: (first + e, 0, 0))
    return pl.pallas_call(
        pack_kernel,
        grid=(count,),
        in_specs=[block] * 3,
        out_specs=pl.BlockSpec((3, 1, hidden, width), lambda e: (0, e, 0, 0)),
        out_shape=jax.ShapeDtypeStruct((3, count, hidden, width), BF),
        compiler_params=params(),
        name="pack_weights",
    )(*weights)


def expert_kernel(
    x_ref, c_ref, w_ref, gate_ref, out_ref, dx_ref, act_ref, dg_ref, du_ref, dgate_ref
):
    width = x_ref.shape[-1]
    x, c = x_ref[0], c_ref[0]
    w_gate = w_ref[:, 0, 0].reshape(-1, width)
    w_up = w_ref[:, 1, 0].reshape(-1, width)
    w_down = w_ref[:, 2, 0].reshape(-1, width)
    gate = gate_ref[0]
    gate_pre = dot_nt(x, w_gate)
    up_pre = dot_nt(x, w_up)
    raw = dot_nt(c, w_down)
    sig = jax.nn.sigmoid(gate_pre)
    silu = gate_pre * sig
    act = silu * up_pre
    dgate_ref[0] = jnp.sum(act * raw, axis=-1, keepdims=True)
    act_low = (act * gate).astype(BF)
    d_act = raw * gate
    d_gate = (d_act * up_pre * sig * (1.0 + gate_pre * (1.0 - sig))).astype(BF)
    d_up = (d_act * silu).astype(BF)
    act_ref[0] = act_low
    dg_ref[0] = d_gate
    du_ref[0] = d_up
    out_ref[0] = dot_nn(act_low, w_down).astype(BF)
    dx_ref[0] = (dot_nn(d_gate, w_gate) + dot_nn(d_up, w_up)).astype(BF)


def experts_both_ways(x_slots, c_slots, w_all, slot_gate, first):
    _, number, width = x_slots.shape
    parts, _, local, hidden, _ = w_all.shape
    tile = number // 2
    taken = pl.BlockSpec((1, tile, width), lambda e, i: (first + e, i, 0))
    wide = pl.BlockSpec((1, tile, width), lambda e, i: (e, i, 0))
    mid = pl.BlockSpec((1, tile, parts * hidden), lambda e, i: (e, i, 0))
    thin = pl.BlockSpec((1, tile, 1), lambda e, i: (e, i, 0))
    wide_shape = jax.ShapeDtypeStruct((local, number, width), BF)
    mid_shape = jax.ShapeDtypeStruct((local, number, parts * hidden), BF)
    return pl.pallas_call(
        expert_kernel,
        grid=(local, 2),
        in_specs=[
            taken, taken,
            pl.BlockSpec((parts, 3, 1, hidden, width), lambda e, i: (0, 0, e, 0, 0)),
            pl.BlockSpec((1, tile, 1), lambda e, i: (first + e, i, 0)),
        ],
        out_specs=[wide, wide, mid, mid, mid, thin],
        out_shape=[
            wide_shape, wide_shape, mid_shape, mid_shape, mid_shape,
            jax.ShapeDtypeStruct((local, number, 1), F32),
        ],
        compiler_params=params(),
        name="experts_both_ways",
    )(x_slots, c_slots, w_all, slot_gate)


def expert_grads_kernel(x_ref, c_ref, act_ref, dg_ref, du_ref, out_ref):
    parts, _, _, hidden, width = out_ref.shape
    x, c = x_ref[0], c_ref[0]
    out_ref[:, 0, 0] = dot_tn(dg_ref[0], x).astype(BF).reshape(parts, hidden, width)
    out_ref[:, 1, 0] = dot_tn(du_ref[0], x).astype(BF).reshape(parts, hidden, width)
    out_ref[:, 2, 0] = dot_tn(act_ref[0], c).astype(BF).reshape(parts, hidden, width)


def expert_grads(x_slots, c_slots, act, d_gate, d_up, parts, first):
    local, number, inner = act.shape
    width = x_slots.shape[-1]
    wide = pl.BlockSpec((1, number, width), lambda e: (first + e, 0, 0))
    mid = pl.BlockSpec((1, number, inner), lambda e: (e, 0, 0))
    return pl.pallas_call(
        expert_grads_kernel,
        grid=(local,),
        in_specs=[wide, wide, mid, mid, mid],
        out_specs=pl.BlockSpec(
            (parts, 3, 1, inner // parts, width), lambda e: (0, 0, e, 0, 0)
        ),
        out_shape=jax.ShapeDtypeStruct((parts, 3, local, inner // parts, width), BF),
        compiler_params=params(),
        name="expert_grads",
    )(x_slots, c_slots, act, d_gate, d_up)


def combine_kernel(
    first_ref, slot_ref, dxa_ref, dxb_ref, outa_ref, outb_ref, dgate_ref, dx_sum_ref, out_sum_ref, pay_ref
):
    _, _, capacity, width = dxa_ref.shape
    local = slot_ref.shape[2]
    rows = slot_ref.shape[1]
    lane = lax.broadcasted_iota(jnp.int32, (rows, local * capacity), 1)
    half = pay_ref.shape[2] // 2
    column = lax.broadcasted_iota(jnp.int32, (rows, 2 * half), 1)
    total = jnp.zeros((rows, local * capacity), F32)
    pay = jnp.zeros(column.shape, F32)
    for e in range(local):
        hit = lane == slot_ref[0, :, e : e + 1] + e * capacity
        total = jnp.where(hit, 1.0, total)
        value = jnp.sum(jnp.where(hit, dgate_ref[0], 0.0), axis=1, keepdims=True)
        high = value.astype(BF).astype(F32)
        pay = jnp.where(column == first_ref[0, 0] + e, high, pay)
        pay = jnp.where(column == first_ref[0, 0] + e + half, value - high, pay)
    place = total.astype(BF)

    def both(a_ref, b_ref):
        pair = [ref[...].reshape(-1, width) for ref in (a_ref, b_ref)]
        return dot_nn(place, jnp.concatenate(pair, axis=0)).astype(BF)

    dx_sum_ref[0] = both(dxa_ref, dxb_ref)
    out_sum_ref[0] = both(outa_ref, outb_ref)
    pay_ref[0] = pay.astype(BF)


def combine_rows(first, slots_t, dx, out, d_gate_slots, experts):
    blocks, rows, local = slots_t.shape
    _, _, capacity, width = dx[0].shape
    lanes = -(-2 * experts // 128) * 128
    slot = pl.BlockSpec((local // 2, 1, capacity, width), lambda b: (0, b, 0, 0))
    block = pl.BlockSpec((1, rows, width), lambda b: (b, 0, 0))
    shape = jax.ShapeDtypeStruct((blocks, rows, width), BF)
    return pl.pallas_call(
        combine_kernel,
        grid=(blocks,),
        in_specs=[
            pl.BlockSpec(memory_space=pltpu.SMEM),
            pl.BlockSpec((1, rows, local), lambda b: (b, 0, 0)), slot, slot, slot, slot,
            pl.BlockSpec((1, 1, local * capacity), lambda b: (b, 0, 0)),
        ],
        out_specs=[block, block, pl.BlockSpec((1, rows, lanes), lambda b: (b, 0, 0))],
        out_shape=[shape, shape, jax.ShapeDtypeStruct((blocks, rows, lanes), BF)],
        compiler_params=params(),
        name="combine_rows",
    )(first, slots_t, *dx, *out, d_gate_slots)


def on_device(
    inputs,
    attn_gain,
    w_query,
    key_weight_matrix,
    value_weight_matrix,
    query_gain,
    key_gain,
    w_out,
    route_gain,
    w_router,
    w_gate,
    w_up,
    w_down,
    routes,
    image_starts,
    cotangent,
):
    tp_count = lax.axis_size("tp")
    ep_count = lax.axis_size("ep")
    tp_index = lax.axis_index("tp")
    ep_index = lax.axis_index("ep")
    length = inputs.shape[0]
    width = inputs.shape[1]
    rows = cotangent.shape[0]
    head_dim = query_gain.shape[0]
    local_experts = w_gate.shape[0]
    experts = local_experts * ep_count
    top = routes.shape[1]
    capacity = -(-(3 * rows * top // (2 * experts)) // 16) * 16

    pair = local_experts // 2

    weights = (w_gate.transpose(0, 2, 1), w_up.transpose(0, 2, 1), w_down)
    w_first = lax.all_gather(pack_weights(weights, 0, pair), "tp")

    inputs_f = inputs.astype(F32)
    attn_scale = rms_scale(inputs_f)
    normed = (inputs_f * attn_scale * attn_gain).astype(BF)
    queries = dot_nn(normed, w_query)
    key_rows = dot_nn(normed, key_weight_matrix)
    values = dot_nn(normed, value_weight_matrix).astype(BF)
    cosine, sine = rope_tables(length, head_dim)
    q_gain, k_gain = query_gain[None], key_gain[None]
    queries, second = lax.optimization_barrier((queries, pack_weights(weights, pair, pair)))
    w_second = lax.all_gather(second, "tp")
    heads, lse, attn_rows, cot_all = attention(
        image_starts, queries, key_rows, values, cosine, sine, q_gain, k_gain, w_out, cotangent, 0
    )
    x_rows = lax.dynamic_slice_in_dim(inputs, tp_index * rows, rows, 0)
    hidden = x_rows.astype(F32) + attn_rows
    route_scale = rms_scale(hidden)
    moe_in = (hidden * route_scale * route_gain).astype(BF)
    moe_in, w_first = lax.optimization_barrier((moe_in, w_first))
    logits = dot_nn(moe_in, w_router)
    router_probs = plain_softmax(logits)
    expert_ids = jnp.arange(experts, dtype=jnp.int32)
    ring_routes = lax.dynamic_index_in_dim(
        routes.reshape(ep_count, tp_count, rows, top), tp_index, 1, keepdims=False
    )
    my_routes = lax.dynamic_index_in_dim(ring_routes, ep_index, 0, keepdims=False)

    def routed_softmax(scores, picked):
        kept = jnp.where(picked, scores, MASKED)
        expo = jnp.where(picked, jnp.exp(kept - jnp.max(kept, axis=-1, keepdims=True)), 0.0)
        return expo / jnp.sum(expo, axis=-1, keepdims=True)

    my_pick = jnp.any(my_routes[:, :, None] == expert_ids[None, None, :], axis=1)
    gates = routed_softmax(logits, my_pick)
    all_pick = jnp.any(ring_routes[..., None] == expert_ids, axis=2)
    mask = lax.dynamic_slice_in_dim(all_pick, ep_index * local_experts, local_experts, 2)
    earlier = (jnp.arange(rows)[:, None] > jnp.arange(rows)[None, :]).astype(BF)
    slots_t = jnp.einsum(
        "tu,bue->bte", earlier, mask.astype(BF), preferred_element_type=F32
    ).astype(jnp.int32)
    slots_t = jnp.where(mask, slots_t, NOWHERE)
    slots = slots_t.transpose(0, 2, 1)
    ring = ep_count == 2 * Z_AXIS
    if ring:
        turned = lax.rem(expert_ids + ep_index * local_experts, experts)
        x_slots, c_slots, slot_gate = gather_select(
            moe_in,
            cot_all,
            slots,
            all_pick.astype(jnp.int32)[..., turned].transpose(0, 2, 1),
            w_router.T[turned],
            capacity,
            1,
        )
        slot_gate = slot_gate.reshape(local_experts, ep_count * capacity, 1)
    else:
        tokens_all = lax.all_gather(moe_in, "ep")
        logits_all = dot_nn(tokens_all.reshape(-1, width), w_router).reshape(ep_count, rows, experts)
        gate_of = lax.dynamic_slice_in_dim(
            routed_softmax(logits_all, all_pick), ep_index * local_experts, local_experts, 2
        )
        place = slots[:, :, None, :] == jnp.arange(capacity, dtype=jnp.int32)[:, None]
        slot_gate = jnp.sum(
            jnp.where(place, gate_of.transpose(0, 2, 1)[:, :, None, :], 0.0), axis=-1
        )
        slot_gate = slot_gate.transpose(1, 0, 2).reshape(local_experts, ep_count * capacity, 1)
        x_slots, c_slots = select_rows(slots, tokens_all, cot_all, capacity)
    flat = (local_experts, ep_count * capacity, width)
    x_slots, c_slots = x_slots.reshape(flat), c_slots.reshape(flat)

    def over_rings(grads):
        return lax.psum_scatter(grads.reshape(-1, width), "tp", scatter_dimension=0, tiled=True)

    out_a, dx_a, *inner_a, dg_a = experts_both_ways(x_slots, c_slots, w_first, slot_gate, 0)
    grads_a = expert_grads(x_slots, c_slots, *inner_a, tp_count, 0)
    x_slots, grads_a = lax.optimization_barrier((x_slots, grads_a))
    mine_a = over_rings(grads_a)
    out_b, dx_b, *inner_b, dg_b = experts_both_ways(x_slots, c_slots, w_second, slot_gate, pair)
    deep = (pair, ep_count, capacity, width)
    dx_slots = [dx_a.reshape(deep), dx_b.reshape(deep)]
    out_slots = [out_a.reshape(deep), out_b.reshape(deep)]
    d_gate_slots = (
        jnp.concatenate([dg_a, dg_b])
        .reshape(local_experts, ep_count, capacity)
        .transpose(1, 0, 2)
        .reshape(ep_count, 1, local_experts * capacity)
    )
    if ring:
        dx_mine, gate_mine, grads_b = input_grads(
            slots_t, d_gate_slots, dx_slots, x_slots, c_slots, inner_b, experts, tp_count, 2
        )
    else:
        grads_b = expert_grads(x_slots, c_slots, *inner_b, tp_count, pair)
        dx_part, out_slots, gate_part = combine_rows(
            (ep_index * local_experts).reshape(1, 1), slots_t, dx_slots, out_slots, d_gate_slots, experts
        )
        dx_mine = lax.psum_scatter(dx_part, "ep", scatter_dimension=0).astype(F32)
        gate_mine = lax.psum_scatter(gate_part, "ep", scatter_dimension=0).astype(F32)
    dx_mine, mine_a, grads_b = lax.optimization_barrier((dx_mine, mine_a, grads_b))
    mine_b = over_rings(grads_b)
    mine_a, mine_b = [m.reshape(3, pair, -1, width) for m in (mine_a, mine_b)]
    w_gate_grad, w_up_grad = [
        jnp.concatenate([mine_a[i], mine_b[i]]).transpose(0, 2, 1).astype(F32) for i in range(2)
    ]
    w_down_grad = jnp.concatenate([mine_a[2], mine_b[2]]).astype(F32)
    lanes = gate_mine.shape[1] // 2
    d_gates = gate_mine[:, :experts] + gate_mine[:, lanes : lanes + experts]
    counts = jnp.sum((routes[:, :, None] == expert_ids[None, None, :]).astype(F32), axis=(0, 1))
    total_tokens = routes.shape[0]
    share = counts / (total_tokens * top)
    coeff = AUX * experts * share
    prob_local = jnp.sum(router_probs, axis=0)
    cot = cotangent.astype(F32)
    d_logits = gates * (d_gates - jnp.sum(gates * d_gates, axis=-1, keepdims=True))
    d_logits = d_logits + router_probs * (
        coeff - jnp.sum(router_probs * coeff, axis=-1, keepdims=True)
    )
    d_logits_low = d_logits.astype(BF)
    router_part = dot_tn(moe_in, d_logits_low)
    d_moe = dot_nt(d_logits_low, w_router) + dx_mine
    d_hidden, route_gain_part = norm_back(d_moe, hidden, route_gain[None])
    d_hidden = d_hidden + cot

    d_queries, d_keys, d_values, query_gain_part, key_gain_part, d_branch, output = attention_back(
        image_starts, queries, key_rows, values, lse, cosine, sine, q_gain, k_gain,
        w_out, d_hidden.astype(BF), slots_t, out_slots, hidden, 3,
    )
    w_query_grad, w_key_grad, w_value_grad, w_out_grad, inputs_grad, attn_gain_grad, small = projection_grads(
        normed, d_queries, d_keys, d_values, heads, d_branch,
        w_query, key_weight_matrix, value_weight_matrix,
        x_rows, d_hidden, attn_gain[None],
        [router_part, route_gain_part[0], query_gain_part[0], key_gain_part[0], prob_local],
        5,
    )
    w_router_grad, route_gain_grad, query_gain_grad, key_gain_grad, prob_all = small
    attn_gain_grad = attn_gain_grad[0]
    aux_loss = experts * jnp.sum(share * (prob_all / total_tokens))
    return (
        output,
        aux_loss,
        inputs_grad,
        attn_gain_grad,
        w_query_grad,
        w_key_grad,
        w_value_grad,
        query_gain_grad,
        key_gain_grad,
        w_out_grad,
        route_gain_grad,
        w_router_grad,
        w_gate_grad,
        w_up_grad,
        w_down_grad,
    )


def solution(mesh):
    return jax.shard_map(
        on_device,
        mesh=mesh,
        in_specs=(
            P("ep", None),
            P(),
            P(None, "tp"),
            P(None, "tp"),
            P(None, "tp"),
            P(),
            P(),
            P("tp", None),
            P(),
            P(),
            P("ep", None, "tp"),
            P("ep", None, "tp"),
            P("ep", "tp", None),
            P(),
            P("ep", None),
            P(("ep", "tp"), None),
        ),
        out_specs=(
            P(("ep", "tp"), None),
            P(),
            P(("ep", "tp"), None),
            P(),
            P("ep", "tp"),
            P("ep", "tp"),
            P("ep", "tp"),
            P(),
            P(),
            P("tp", "ep"),
            P(),
            P(),
            P("ep", None, "tp"),
            P("ep", None, "tp"),
            P("ep", "tp", None),
        ),
        check_vma=False,
    )
```

```python
import functools

import jax
import jax.numpy as jnp
import numpy as np
from jax import lax
from jax.experimental import pallas as pl
from jax.experimental.pallas import tpu as pltpu
from jax.sharding import PartitionSpec as P

IMG = 256
EPS = 1e-06
AUX = 0.04
THETA = 1000000.0
MASKED = -1e30
NOWHERE = -(1 << 20)
BF = jnp.bfloat16
F32 = jnp.float32
VMEM_BYTES = 60 * 1024 * 1024


def dot_nn(a, b):
    return lax.dot_general(a, b, (((1,), (0,)), ((), ())), preferred_element_type=F32)


def dot_nt(a, b):
    return lax.dot_general(a, b, (((1,), (1,)), ((), ())), preferred_element_type=F32)


def dot_tn(a, b):
    return lax.dot_general(a, b, (((0,), (0,)), ((), ())), preferred_element_type=F32)


def params(**kw):
    return pltpu.CompilerParams(vmem_limit_bytes=VMEM_BYTES, **kw)


def rms_scale(value_rows):
    return lax.rsqrt(jnp.mean(value_rows * value_rows, axis=-1, keepdims=True) + EPS)


def plain_softmax(value_rows):
    top = jnp.max(value_rows, axis=-1, keepdims=True)
    expo = jnp.exp(value_rows - top)
    return expo / jnp.sum(expo, axis=-1, keepdims=True)


def rope_tables(length, size):
    half = size // 2
    freq = THETA ** (-2.0 * np.arange(half) / size)
    angle = np.arange(length)[:, None] * freq[None, :]
    cosine, sine = np.cos(angle), np.sin(angle)
    tables = (np.concatenate([cosine, cosine], axis=-1), np.concatenate([-sine, sine], axis=-1))
    return tuple(jnp.asarray(t, F32) for t in tables)


def turn(rows, cosine, sine):
    return rows * cosine + pltpu.roll(rows, rows.shape[-1] // 2, 1) * sine


def turn_back(rows, cosine, sine):
    return rows * cosine - pltpu.roll(rows, rows.shape[-1] // 2, 1) * sine


MESH = pl.DeviceIdType.MESH
ANY = pl.BlockSpec(memory_space=pl.ANY)
Z_AXIS = 4


def link_cost(us):
    return pl.CostEstimate(flops=0, bytes_accessed=int(us * 3.0e6), transcendentals=0)


def greet(partners):
    barrier = pltpu.get_barrier_semaphore()
    count = 0
    for there, device in partners:
        flag = jnp.asarray(there, jnp.int32)

        @pl.when(there)
        def _(device=device):
            pl.semaphore_signal(barrier, inc=1, device_id=device, device_id_type=MESH)

        count = count + flag
    pl.semaphore_wait(barrier, count)


def remote(src, dst, send, recv, device):
    return pltpu.make_async_remote_copy(
        src_ref=src, dst_ref=dst, send_sem=send, recv_sem=recv, device_id=device, device_id_type=MESH
    )


def ring_place():
    me = lax.axis_index("ep")
    z, y = me // 2, me % 2
    return me, z, y, {"ep": me + 2}, {"ep": me - 2}, {"ep": me + 1 - 2 * y}


def ring_pieces(ref, axis):
    unit = ref.shape[axis] // 16
    lead = (slice(None),) * axis
    return [
        ref.at[lead + (pl.ds(start * unit, count * unit),)]
        for start, count in ((0, 7), (7, 6), (13, 3))
    ]


class EpGather:
    def __init__(self, ins, outs, sems):
        self.ins, self.outs = ins, outs
        self.own_sem, self.up_send, self.up_recv, self.dn_send, self.dn_recv = sems[:5]
        self.y_send, self.y_recv = sems[5:]
        self.me, self.z, self.y, self.up, self.down, self.beside = ring_place()
        self.last = len(ins) - 1
        self.streams = [(a, a, self.y) for a in range(len(ins))]
        self.other = (self.last, len(ins), 1 - self.y)

    def partners(self):
        z = self.z
        return [(z < Z_AXIS - 1, self.up), (z > 0, self.down), (z >= 0, self.beside)]

    def block(self, a, zt, y):
        return self.outs[a].at[zt * 2 + y]

    def upward(self, src, stream, zt):
        a, i, y = stream
        return remote(src, self.block(a, zt, y), self.up_send.at[i, zt], self.up_recv.at[i, zt], self.up)

    def downward(self, src, stream, zt):
        a, i, y = stream
        return remote(src, self.block(a, zt, y), self.dn_send.at[i, zt], self.dn_recv.at[i, zt], self.down)

    def sideways(self, src, a, zt):
        return remote(
            src, self.block(a, zt, self.y), self.y_send.at[a, zt], self.y_recv.at[a, zt], self.beside
        )

    def both_ways(self, src, stream):
        z = self.z

        @pl.when(z < Z_AXIS - 1)
        def _():
            self.upward(src, stream, z).start()

        @pl.when(z > 0)
        def _():
            self.downward(src, stream, z).start()

    def start(self):
        self.sideways(self.ins[self.last], self.last, self.z).start()
        for stream in self.streams:
            a = stream[0]
            self.both_ways(self.ins[a], stream)
            if a != self.last:
                self.sideways(self.ins[a], a, self.z).start()
            pltpu.make_async_copy(self.ins[a], self.block(a, self.z, self.y), self.own_sem.at[a]).start()

    def cross(self):
        self.side_arrived(self.last, self.z)
        self.both_ways(self.block(self.last, self.z, 1 - self.y), self.other)

    def hop(self, d):
        z = self.z
        for stream in [self.other] + self.streams:
            a, _, y = stream

            @pl.when(z >= d)
            def _(a=a, y=y, stream=stream, zt=z - d):
                rows = self.block(a, zt, y)
                self.upward(rows, stream, zt).wait_recv()

                @pl.when(z < Z_AXIS - 1)
                def _():
                    self.upward(rows, stream, zt).start()

                if a != self.last:
                    self.sideways(rows, a, zt).start()

            @pl.when(z + d < Z_AXIS)
            def _(a=a, y=y, stream=stream, zt=z + d):
                rows = self.block(a, zt, y)
                self.downward(rows, stream, zt).wait_recv()

                @pl.when(z > 0)
                def _():
                    self.downward(rows, stream, zt).start()

                if a != self.last:
                    self.sideways(rows, a, zt).start()

    def own_done(self):
        for a, x in enumerate(self.ins):
            pltpu.make_async_copy(x, self.block(a, self.z, self.y), self.own_sem.at[a]).wait()

    def side_arrived(self, a, zt):
        rows = self.block(a, zt, 1 - self.y)
        remote(rows, rows, self.y_send.at[a, zt], self.y_recv.at[a, zt], self.beside).wait_recv()

    def side_done(self, zt):
        for a in range(self.last):
            self.side_arrived(a, zt)

    def sent(self):
        z = self.z
        self.sideways(self.block(self.last, z, self.y), self.last, z).wait_send()
        for stream in self.streams + [self.other]:
            a, _, y = stream
            for zt in range(Z_AXIS):
                src = self.block(a, zt, y)
                if a != self.last:
                    self.sideways(src, a, zt).wait_send()

                @pl.when((zt <= z) & (z < Z_AXIS - 1))
                def _(src=src, zt=zt, stream=stream):
                    self.upward(src, stream, zt).wait_send()

                @pl.when((zt >= z) & (z > 0))
                def _(src=src, zt=zt, stream=stream):
                    self.downward(src, stream, zt).wait_send()

    def finish(self):
        self.own_done()
        for zt in range(Z_AXIS):
            self.side_done(zt)
        self.sent()


def gather_sems():
    dma = pltpu.SemaphoreType.DMA
    return [dma((3,))] + [dma((4, Z_AXIS))] * 6


def one_hot(slots, capacity):
    local, rows = slots.shape
    slot = lax.broadcasted_iota(jnp.int32, (capacity, rows), 0)
    return [slot == slots[e : e + 1, :] for e in range(local)]


def gather_select_kernel(
    x_ref, cots_ref, slots_ref, picks_ref, router_ref, xs_ref, cs_ref, gate_ref,
    tokens, cots, chosen, load_sem, store_sem, *sems,
):
    local, _, capacity, width = xs_ref.shape
    blocks = tokens.shape[0]
    gather = EpGather(ring_pieces(x_ref, 0), ring_pieces(tokens, 1), sems)
    z, y = gather.z, gather.y
    greet(gather.partners())
    gather.start()

    def chosen_rows(j, rows):
        hits = one_hot(slots_ref[j], capacity)
        place = jnp.concatenate([h.astype(F32) for h in hits], axis=0).astype(BF)
        return dot_nn(place, rows).astype(BF).reshape(local, capacity, width), hits

    def load(j, slot):
        return pltpu.make_async_copy(cots_ref.at[j], cots.at[slot], load_sem.at[slot])

    def store(to, j, slot):
        return pltpu.make_async_copy(chosen.at[slot], to.at[:, j], store_sem.at[slot])

    load(0, 0).start()

    @pl.loop(0, blocks)
    def _(j):
        slot = lax.rem(j, 2)

        @pl.when(j + 1 < blocks)
        def _():
            load(j + 1, 1 - slot).start()

        load(j, slot).wait()

        @pl.when(j == 3)
        def _():
            gather.cross()

        @pl.when(j >= 2)
        def _():
            store(cs_ref, j - 2, slot).wait()

        chosen[slot] = chosen_rows(j, cots[slot])[0]
        store(cs_ref, j, slot).start()

    store(cs_ref, blocks - 2, 0).wait()
    store(cs_ref, blocks - 1, 1).wait()

    def take(j):
        rows = tokens[j]
        chosen[0], hits = chosen_rows(j, rows)
        copy = store(xs_ref, j, 0)
        copy.start()
        logits = dot_nt(router_ref[...], rows)
        picked = picks_ref[j] > 0
        kept = jnp.where(picked, logits, MASKED)
        expo = jnp.exp(kept - jnp.max(kept, axis=0, keepdims=True))
        expo = jnp.where(picked, expo, 0.0)
        gates = expo / jnp.sum(expo, axis=0, keepdims=True)
        for e, hit in enumerate(hits):
            gate_ref[e, j] = jnp.sum(jnp.where(hit, gates[e : e + 1, :], 0.0), axis=1, keepdims=True)
        copy.wait()

    gather.own_done()
    take(gather.me)
    for d in range(1, Z_AXIS + 1):
        if d < Z_AXIS:
            gather.hop(d)

        @pl.loop(0, 4)
        def _(i, d=d):
            beside = i >= 2
            far = jnp.where(beside, d - 1, d)
            zt = jnp.where(lax.rem(i, 2) == 0, z - far, z + far)
            there = (zt >= 0) & (zt < Z_AXIS) & ((i < 3) | (d > 1))

            @pl.when(there & beside)
            def _():
                gather.side_done(zt)

            @pl.when(there)
            def _():
                take(zt * 2 + jnp.where(beside, 1 - y, y))

    gather.sent()


def gather_select(rows, cot_all, slots, picks, router, capacity, number):
    ep_count = lax.axis_size("ep")
    _, local, block = slots.shape
    width = rows.shape[1]
    vmem = pl.BlockSpec(memory_space=pltpu.VMEM)
    dma = pltpu.SemaphoreType.DMA
    shape = (local, ep_count, capacity, width)
    return pl.pallas_call(
        gather_select_kernel,
        in_specs=[ANY, ANY, vmem, vmem, vmem],
        out_specs=[ANY, ANY, vmem],
        out_shape=[
            jax.ShapeDtypeStruct(shape, BF),
            jax.ShapeDtypeStruct(shape, BF),
            jax.ShapeDtypeStruct(shape[:3] + (1,), F32),
        ],
        scratch_shapes=[
            pltpu.VMEM((ep_count, block, width), BF),
            pltpu.VMEM((2, block, width), BF),
            pltpu.VMEM((2, local, capacity, width), BF),
            dma((2,)), dma((2,)),
        ]
        + gather_sems(),
        compiler_params=params(collective_id=number, has_side_effects=True),
        cost_estimate=link_cost(90.0),
        name="gather_select",
    )(rows, cot_all, slots, picks, router)


def add_rows(total, terms, chunk=16):
    @pl.loop(0, total.shape[0] // chunk)
    def _(i):
        rows = pl.ds(pl.multiple_of(i * chunk, chunk), chunk)
        value = terms[0][rows, :].astype(F32)
        for term in terms[1:]:
            value = value + term[rows, :].astype(F32)
        total[rows, :] = value.astype(total.dtype)


def scatter_order(z):
    table = ((3, 2, 1, 0), (3, 0, 2, 1), (0, 3, 1, 2), (0, 1, 2, 3))
    return [
        jnp.where(
            z == 0,
            table[0][k],
            jnp.where(z == 1, table[1][k], jnp.where(z == 2, table[2][k], table[3][k])),
        )
        for k in range(Z_AXIS)
    ]


class EpReduce:
    def __init__(self, ins, by_z, bufs, sems):
        self.ins, self.by_z = ins, by_z
        self.bufs = [bufs[2 * a : 2 * a + 2] for a in range(len(ins))]
        self.up_send, self.up_recv, self.dn_send, self.dn_recv, self.y_send, self.y_recv = sems
        self.me, self.z, self.y, self.up, self.down, self.beside = ring_place()
        self.order = scatter_order(self.z)
        self.streams = [(a, 0, self.y) for a in range(len(ins))]
        self.crossing = [(a, 1, 1 - self.y) for a in range(len(ins)) if by_z[a]]

    def partners(self):
        z = self.z
        return [(z < Z_AXIS - 1, self.up), (z > 0, self.down), (z >= 0, self.beside)]

    def mine(self, stream, zt):
        return self.ins[stream[0]].at[zt * 2 + stream[2]]

    def side(self, a, zt):
        return self.bufs[a][0].at[0 if self.by_z[a] else zt]

    def below(self, stream, zt):
        return self.bufs[stream[0]][1].at[stream[1] * (Z_AXIS + 1) + zt]

    def above(self, stream, zt, z):
        return self.below(stream, jnp.where(zt == z, Z_AXIS, zt))

    def to_side(self, a, zt):
        src = self.ins[a].at[zt * 2 + 1 - self.y]
        return remote(src, self.side(a, zt), self.y_send.at[a, zt], self.y_recv.at[a, zt], self.beside)

    def rising(self, stream, zt):
        i = 2 * stream[0] + stream[1]
        return remote(
            self.mine(stream, zt), self.below(stream, zt), self.up_send.at[i, zt], self.up_recv.at[i, zt], self.up
        )

    def falling(self, stream, zt):
        i = 2 * stream[0] + stream[1]
        return remote(
            self.mine(stream, zt), self.above(stream, zt, self.z - 1),
            self.dn_send.at[i, zt], self.dn_recv.at[i, zt], self.down,
        )

    def send_side(self, k):
        for a, by_z in enumerate(self.by_z):
            if not by_z:
                self.to_side(a, self.order[k]).start()

    def step_y(self, k):
        self.step(k, [s for s in self.streams if not self.by_z[s[0]]])

    def step_z(self, k):
        self.step(k, self.crossing + [s for s in self.streams if self.by_z[s[0]]])
        if k == Z_AXIS - 1:
            for stream in self.crossing:
                rows = self.mine(stream, self.z)
                self.gathered(stream, [rows], functools.partial(add_rows, rows))
                self.to_side(stream[0], self.z).start()

    def step(self, k, streams):
        z, zt, last = self.z, self.order[k], Z_AXIS - 1
        for stream in streams:
            a = stream[0]
            mine = self.mine(stream, zt)
            terms = [mine]
            if not self.by_z[a]:
                self.to_side(a, zt).wait_recv()
                terms = [mine, self.side(a, zt)]
                ends = ((zt > z) & (z == 0)) | ((zt < z) & (z == last))

                @pl.when(ends)
                def _(mine=mine, terms=terms):
                    add_rows(mine, terms)

            @pl.when((zt > z) & (z > 0))
            def _(stream=stream, mine=mine, terms=terms):
                self.rising(stream, zt).wait_recv()
                add_rows(mine, terms + [self.below(stream, zt)])

            @pl.when((zt < z) & (z < last))
            def _(stream=stream, mine=mine, terms=terms):
                self.falling(stream, zt).wait_recv()
                add_rows(mine, terms + [self.above(stream, zt, z)])

            @pl.when(zt > z)
            def _(stream=stream):
                self.rising(stream, zt).start()

            @pl.when(zt < z)
            def _(stream=stream):
                self.falling(stream, zt).start()

    def gathered(self, stream, terms, write):
        z, last = self.z, Z_AXIS - 1

        @pl.when(z > 0)
        def _():
            self.rising(stream, z).wait_recv()

        @pl.when(z < last)
        def _():
            self.falling(stream, z).wait_recv()

        @pl.when(z == 0)
        def _():
            write(terms + [self.above(stream, z, z)])

        @pl.when(z == last)
        def _():
            write(terms + [self.below(stream, z)])

        @pl.when((z > 0) & (z < last))
        def _():
            write(terms + [self.below(stream, z), self.above(stream, z, z)])

    def own(self, a, write):
        if self.by_z[a]:
            self.to_side(a, self.z).wait_recv()
        stream = self.streams[a]
        self.gathered(stream, [self.mine(stream, self.z), self.side(a, self.z)], write)

    def sent(self):
        z = self.z
        for stream in self.streams + self.crossing:
            a = stream[0]
            for zt in range(Z_AXIS):
                if not self.by_z[a]:
                    self.to_side(a, zt).wait_send()

                @pl.when(zt > z)
                def _(stream=stream, zt=zt):
                    self.rising(stream, zt).wait_send()

                @pl.when(zt < z)
                def _(stream=stream, zt=zt):
                    self.falling(stream, zt).wait_send()

        for stream in self.crossing:
            self.to_side(stream[0], z).wait_send()


def reduce_scratch(rows, columns):
    unit = rows // 16
    out = []
    for count, slots in ((7, (Z_AXIS, Z_AXIS + 1)), (6, (Z_AXIS, Z_AXIS + 1)), (3, (1, 2 * (Z_AXIS + 1)))):
        out += [pltpu.VMEM((n, count * unit, columns), BF) for n in slots]
    return out


BY_Z = [False, False, True]


def reduce_sems(count):
    dma = pltpu.SemaphoreType.DMA
    return [dma((2 * count, Z_AXIS))] * 4 + [dma((count, Z_AXIS))] * 2


def token_hits(slots, capacity):
    rows, local = slots.shape
    lane = lax.broadcasted_iota(jnp.int32, (rows, local * capacity), 1)
    return [lane == slots[:, e : e + 1] + e * capacity for e in range(local)]


class SlotSums:
    def __init__(self, slots, first, second, buf, sem):
        self.slots, self.pair, self.buf, self.sem = slots, (first, second), buf, sem
        self.capacity = first.shape[2]

    def copies(self, j, at):
        n = self.pair[0].shape[0]
        return [
            pltpu.make_async_copy(
                ref.at[:, j], self.buf.at[at, pl.ds(i * n, n)], self.sem.at[at, i]
            )
            for i, ref in enumerate(self.pair)
        ]

    def fetch(self, j, at):
        for copy in self.copies(j, at):
            copy.start()

    def add(self, j, at, out):
        for copy in self.copies(j, at):
            copy.wait()
        place = jnp.zeros((), F32)
        for hit in token_hits(self.slots[j], self.capacity):
            place = jnp.where(hit, 1.0, place)
        rows = self.buf[at].reshape(-1, out.shape[1])
        out[...] = dot_nn(place.astype(BF), rows).astype(BF)

    def run(self, blocks, out, then):
        self.fetch(blocks[0], 0)
        for n, j in enumerate(blocks):
            if n + 1 < len(blocks):
                self.fetch(blocks[n + 1], (n + 1) % 2)
            self.add(j, n % 2, out.at[j])
            then(n)


def slot_sums_scratch(local, capacity, width):
    return [
        pltpu.VMEM((2, local, capacity, width), BF),
        pltpu.SemaphoreType.DMA((2, 2)),
    ]


def input_grads_kernel(
    slots, dgate, dx_a, dx_b, xs, cs, act, d_gate, d_up,
    residual, moe_in, cot, route_gain, gate_dense, probs, coeff, router,
    d_hidden, d_rows, router_part, gain_part, grads,
    out, gate_out, part, gates, buf, sem, x_in, c_in, h_in, w_buf, in_sem, w_sem, *refs,
):
    sums = SlotSums(slots, dx_a, dx_b, buf, sem)
    reduce = EpReduce(ring_pieces(part, 1) + [gates], BY_Z + [False], refs[:8], refs[8:])
    order, y = reduce.order, reduce.y
    pair, number, inner = act.shape
    parts, _, _, hidden, width = grads.shape
    first = xs.shape[0] - pair
    pieces = width // x_in.shape[1]
    wide = x_in.shape[1]
    greet(reduce.partners())

    def cols(piece):
        return pl.ds(piece * wide, wide)

    def wide_copies(unit):
        e, piece = unit // pieces, unit % pieces
        return [
            pltpu.make_async_copy(xs.at[first + e, :, cols(piece)], x_in, in_sem.at[0]),
            pltpu.make_async_copy(cs.at[first + e, :, cols(piece)], c_in, in_sem.at[1]),
        ]

    def inner_copies(e):
        return [
            pltpu.make_async_copy(ref.at[e], h_in.at[kind], in_sem.at[2 + kind])
            for kind, ref in enumerate((d_gate, d_up, act))
        ]

    def written(unit):
        e, piece = unit // pieces, unit % pieces
        return pltpu.make_async_copy(w_buf, grads.at[:, :, e, :, cols(piece)], w_sem)

    def prepare(unit):
        for copy in wide_copies(unit) + (inner_copies(unit // pieces) if unit % pieces == 0 else []):
            copy.start()

    def weights(unit):
        for copy in wide_copies(unit) + (inner_copies(unit // pieces) if unit % pieces == 0 else []):
            copy.wait()
        if unit > 0:
            written(unit - 1).wait()
        for kind, right in enumerate((x_in, x_in, c_in)):
            grad = dot_tn(h_in[kind], right[...]).astype(BF)
            w_buf[:, kind] = grad.reshape(parts, hidden, wide)
        written(unit).start()
        if unit + 1 < pair * pieces:
            prepare(unit + 1)

    def payload(j):
        lanes = gates.shape[2]
        column = lax.broadcasted_iota(jnp.int32, (gates.shape[1], lanes), 1)
        pay = jnp.zeros(column.shape, F32)
        mine = reduce.me * slots.shape[2]
        for e, hit in enumerate(token_hits(slots[j], sums.capacity)):
            value = jnp.sum(jnp.where(hit, dgate[j], 0.0), axis=1, keepdims=True)
            high = value.astype(BF).astype(F32)
            pay = jnp.where(column == mine + e, high, pay)
            pay = jnp.where(column == mine + e + lanes // 2, value - high, pay)
        gates[j] = pay.astype(BF)

    def send(k):
        payload(order[k] * 2 + 1 - y)
        reduce.send_side(k)

    units = pair * pieces
    done = [units * (k + 1) // Z_AXIS for k in range(Z_AXIS)]
    sums.run([order[k] * 2 + 1 - y for k in range(Z_AXIS)], part, send)
    prepare(0)
    sums.run(
        [order[k] * 2 + y for k in range(Z_AXIS)], part, lambda k: payload(order[k] * 2 + y)
    )
    reduce.step_z(0)
    reduce.step_z(1)
    for k in range(Z_AXIS):
        for unit in range(done[k - 1] if k else 0, done[k]):
            weights(unit)
        reduce.step_y(k)
        if k == 0:
            reduce.step_z(2)
            reduce.step_z(3)
    for a, rows in enumerate(ring_pieces(out, 0) + [gate_out]):
        reduce.own(a, functools.partial(add_rows, rows))

    experts, lanes = gate_dense.shape[1], gates.shape[2]
    d_gates = gate_out[:, 0:experts] + gate_out[:, lanes // 2 : lanes // 2 + experts]
    gate, prob = gate_dense[...], probs[...]
    d_logits = gate * (d_gates - jnp.sum(gate * d_gates, axis=-1, keepdims=True))
    d_logits = d_logits + prob * (coeff[...] - jnp.sum(prob * coeff[...], axis=-1, keepdims=True))
    d_low = d_logits.astype(BF)
    router_part[...] = dot_tn(d_low, moe_in[...])
    out[...] += dot_nn(d_low, router[...])
    gain_part[...] = jnp.zeros_like(gain_part)
    chunk = 16

    @pl.loop(0, out.shape[0] // chunk)
    def _(i):
        lines = pl.ds(pl.multiple_of(i * chunk, chunk), chunk)
        back, gain_rows = norm_back(out[lines, :], residual[lines, :], route_gain[...])
        total = back + cot[lines, :].astype(F32)
        d_hidden[lines, :] = total
        d_rows[lines, :] = total.astype(BF)
        gain_part[...] += gain_rows

    reduce.sent()
    written(units - 1).wait()


def input_grads(slots_t, dgate, dx, x_slots, c_slots, inner, row_values, experts, tp_count, number):
    ep_count, rows, local = slots_t.shape
    pair, _, capacity, width = dx[0].shape
    count, hidden = inner[0].shape[1:]
    lanes = -(-2 * experts // 128) * 128
    wide = width // 2
    dma = pltpu.SemaphoreType.DMA
    vmem = pl.BlockSpec(memory_space=pltpu.VMEM)
    return pl.pallas_call(
        input_grads_kernel,
        in_specs=[vmem, vmem] + [ANY] * 7 + [vmem] * 8,
        out_specs=[vmem] * 4 + [ANY],
        out_shape=[
            jax.ShapeDtypeStruct((rows, width), F32),
            jax.ShapeDtypeStruct((rows, width), BF),
            jax.ShapeDtypeStruct((experts, width), F32),
            jax.ShapeDtypeStruct((1, width), F32),
            jax.ShapeDtypeStruct((tp_count, 3, pair, hidden // tp_count, width), BF),
        ],
        scratch_shapes=[
            pltpu.VMEM((rows, width), F32),
            pltpu.VMEM((rows, lanes), F32),
            pltpu.VMEM((ep_count, rows, width), BF),
            pltpu.VMEM((ep_count, rows, lanes), BF),
        ]
        + slot_sums_scratch(local, capacity, width)
        + [
            pltpu.VMEM((count, wide), BF),
            pltpu.VMEM((count, wide), BF),
            pltpu.VMEM((3, count, hidden), BF),
            pltpu.VMEM((tp_count, 3, hidden // tp_count, wide), BF),
            dma((5,)), dma,
        ]
        + reduce_scratch(rows, width)
        + [pltpu.VMEM((n, rows, lanes), BF) for n in (Z_AXIS, Z_AXIS + 1)]
        + reduce_sems(4),
        compiler_params=params(collective_id=number, has_side_effects=True),
        cost_estimate=link_cost(100.0),
        name="input_grads",
    )(slots_t, dgate, *dx, x_slots, c_slots, *inner, *row_values)


class Exchange:
    def __init__(self, axis, send, recv):
        self.axis, self.send, self.recv = axis, send, recv
        self.count, self.me = lax.axis_size(axis), lax.axis_index(axis)

    def each(self, act):
        for i in range(1, self.count):
            act(i, lax.rem(self.me + i, self.count))

    def to(self, src, dst, i, other):
        return remote(src, dst, self.send.at[i], self.recv.at[self.me], {self.axis: other})

    def start(self, src_of, dst):
        self.each(lambda i, other: self.to(src_of(other), dst.at[self.me], i, other).start())

    def arrived(self, dst):
        self.each(
            lambda i, other: remote(
                dst.at[other], dst.at[other], self.send.at[i], self.recv.at[other], {self.axis: other}
            ).wait_recv()
        )

    def sent(self, src_of, dst):
        self.each(lambda i, other: self.to(src_of(other), dst.at[self.me], i, other).wait_send())


class SumAll:
    def __init__(self, x, out, over_tp, own_tp, over_ep, own, ring, sems):
        self.x, self.out, self.over_tp, self.own_tp = x, out, over_tp, own_tp
        self.over_ep, self.own, self.ring = over_ep, own, ring
        self.first = Exchange("tp", sems[0], sems[1])
        self.second = Exchange("ep", sems[2], sems[3])
        self.third = Exchange("ep", sems[4], sems[5])
        self.fourth = Exchange("tp", sems[6], sems[7])

    def slice_tp(self, t):
        return self.x.at[t]

    def slice_ep(self, e):
        return self.own_tp.at[e]

    def start(self):
        self.first.start(self.slice_tp, self.over_tp)
        me = self.first.me
        self.over_tp[pl.ds(me, 1)] = self.x[pl.ds(me, 1)]

    def across(self):
        self.first.arrived(self.over_tp)
        self.own_tp[...] = jnp.sum(self.over_tp[...], axis=0)
        self.second.start(self.slice_ep, self.over_ep)
        me = self.second.me
        self.over_ep[pl.ds(me, 1)] = self.own_tp[pl.ds(me, 1)]

    def back(self):
        self.second.arrived(self.over_ep)
        self.own[...] = jnp.sum(self.over_ep[...], axis=0)
        self.third.start(lambda e: self.own, self.ring)
        self.ring[pl.ds(self.third.me, 1)] = self.own[...][None]

    def home(self):
        self.third.arrived(self.ring)
        self.fourth.start(lambda t: self.ring, self.out)
        self.out[pl.ds(self.fourth.me, 1)] = self.ring[...][None]

    def finish(self):
        self.fourth.arrived(self.out)
        self.first.sent(self.slice_tp, self.over_tp)
        self.second.sent(self.slice_ep, self.over_ep)
        self.third.sent(lambda e: self.own, self.ring)
        self.fourth.sent(lambda t: self.ring, self.out)


def exchange_sems(axis):
    return [pltpu.SemaphoreType.DMA((lax.axis_size(axis),))] * 2


def sum_scratch(shape):
    tp, ep, rows, lanes = shape
    return [
        pltpu.VMEM(shape, F32), pltpu.VMEM((ep, rows, lanes), F32), pltpu.VMEM((ep, rows, lanes), F32),
        pltpu.VMEM((rows, lanes), F32), pltpu.VMEM((ep, rows, lanes), F32),
    ] + [sem for axis in ("tp", "ep", "ep", "tp") for sem in exchange_sems(axis)]


def pack_small(values, tp, ep):
    total = tp * ep
    flat = jnp.concatenate([v.reshape(-1) for v in values])
    rows = -(-flat.shape[0] // (total * 128 * 8)) * 8
    return jnp.pad(flat, (0, total * rows * 128 - flat.shape[0])).reshape(tp, ep, rows, 128)


def unpack_small(summed, values):
    summed = summed.reshape(-1)
    out, at = [], 0
    for v in values:
        out.append(summed[at : at + v.size].reshape(v.shape))
        at += v.size
    return out


def fill_bias(span_ref, bias, chunk=256):
    keys, length = bias.shape
    query = lax.broadcasted_iota(jnp.int32, (1, length), 1)

    def spans(pos):
        first = (pos >= span_ref[0, 0]) & (pos < span_ref[0, 0] + IMG)
        second = (pos >= span_ref[0, 1]) & (pos < span_ref[0, 1] + IMG)
        return jnp.where(first, 0, jnp.where(second, 1, -1))

    query_span = spans(query)
    query_other = jnp.where(query_span < 0, -2, query_span)
    for start in range(0, keys, chunk):
        key = start + lax.broadcasted_iota(jnp.int32, (chunk, 1), 0)
        ok = (key <= query) | (spans(key) == query_other)
        bias[start : start + chunk, :] = jnp.where(ok, 0.0, MASKED)


def query_tiles(length):
    tile = min(IMG, length)
    return [
        (start, tile, min(length, start + tile + -(-IMG // tile) * tile))
        for start in range(0, length, tile)
    ]


def attention_kernel(
    span_ref, q_ref, k_ref, v_ref, cos_ref, sin_ref, qg_ref, kg_ref, w_out_ref, cot_ref, x_ref, gain_ref,
    out_ref, lse_ref, rows_ref, moe_ref, cots_ref,
    bias, k_rot, v_t, heads, part, core_rows, x_rows, core_send, core_recv, x_send, x_recv, *sems,
):
    factor = q_ref.shape[-1] ** (-0.5)
    cosine, sine = cos_ref[...], sin_ref[...]
    step = pl.program_id(0)
    size = q_ref.shape[-1]
    me = lax.axis_index("tp")
    x, c = me // 2, me % 2
    other_core, other_x = {"tp": x * 2 + 1 - c}, {"tp": (1 - x) * 2 + c}
    gather = EpGather(ring_pieces(cot_ref, 0), ring_pieces(cots_ref, 1), sems)

    @pl.when(step == 0)
    def _():
        greet(gather.partners() + [(x >= 0, other_core), (x >= 0, other_x)])
        gather.start()
        fill_bias(span_ref, bias)
        k = k_ref[...]
        k_rot[...] = turn(k * rms_scale(k) * kg_ref[...], cosine, sine).astype(BF)
        v_t[...] = v_ref[...].astype(F32).T.astype(BF)

    @pl.when(step == 2)
    def _():
        gather.cross()

    @pl.when(step == pl.num_programs(0) - 2)
    def _():
        gather.hop(1)

    q = q_ref[...]
    q_rot = turn(q * rms_scale(q) * qg_ref[...], cosine, sine).astype(BF)
    for start, tile, keys in query_tiles(q.shape[0]):
        cols = slice(start, start + tile)
        s = dot_nt(k_rot[:keys, :], q_rot[cols, :]) * factor + bias[:keys, cols]
        top = jnp.max(s, axis=0, keepdims=True)
        p = jnp.exp(s - top)
        total = jnp.sum(p, axis=0, keepdims=True)
        o_t = dot_nn(v_t[:, :keys], p.astype(BF)) / total
        rows = o_t.T.astype(BF)
        out_ref[cols, :] = rows
        heads[step, cols, :] = rows
        lse_ref[0, :, cols] = top + jnp.log(total)

    @pl.when(step == pl.num_programs(0) - 1)
    def _():
        count = heads.shape[0]
        block = rows_ref.shape[0]

        def project(tp):
            lines = pl.ds(pl.multiple_of(tp * block, block), block)
            rows = jnp.concatenate([heads[h, lines, :] for h in range(count)], axis=1)
            part[tp] = dot_nn(rows, w_out_ref[...]).astype(BF)

        def to_core(xt):
            return remote(
                part.at[xt * 2 + 1 - c], core_rows.at[xt],
                core_send.at[xt], core_recv.at[xt], other_core,
            )

        far, near = part.at[(1 - x) * 2 + c], part.at[x * 2 + c]
        to_x = remote(far, x_rows, x_send, x_recv, other_x)
        project((1 - x) * 2 + 1 - c)
        to_core(1 - x).start()
        project((1 - x) * 2 + c)
        to_core(1 - x).wait_recv()
        add_rows(far, [far, core_rows.at[1 - x]])
        to_x.start()
        project(x * 2 + 1 - c)
        to_core(x).start()
        project(x * 2 + c)
        gather.hop(2)
        to_core(x).wait_recv()
        gather.hop(3)
        to_x.wait_recv()
        chunk = 16

        @pl.loop(0, block // chunk)
        def _(i):
            lines = pl.ds(pl.multiple_of(i * chunk, chunk), chunk)
            total = near[lines, :].astype(F32) + core_rows[x, lines, :].astype(F32)
            hidden = x_ref[lines, :].astype(F32) + (total + x_rows[lines, :].astype(F32))
            rows_ref[lines, :] = hidden
            moe_ref[lines, :] = (hidden * rms_scale(hidden) * gain_ref[...]).astype(BF)

        gather.finish()
        to_core(1 - x).wait_send()
        to_core(x).wait_send()
        to_x.wait_send()


def plain_attention_kernel(
    span_ref, q_ref, k_ref, v_ref, cos_ref, sin_ref, qg_ref, kg_ref, out_ref, lse_ref,
    bias, k_rot, v_t,
):
    factor = q_ref.shape[-1] ** (-0.5)
    cosine, sine = cos_ref[...], sin_ref[...]

    @pl.when(pl.program_id(0) == 0)
    def _():
        fill_bias(span_ref, bias)
        k = k_ref[...]
        k_rot[...] = turn(k * rms_scale(k) * kg_ref[...], cosine, sine).astype(BF)
        v_t[...] = v_ref[...].astype(F32).T.astype(BF)

    q = q_ref[...]
    q_rot = turn(q * rms_scale(q) * qg_ref[...], cosine, sine).astype(BF)
    for start, tile, keys in query_tiles(q.shape[0]):
        cols = slice(start, start + tile)
        s = dot_nt(k_rot[:keys, :], q_rot[cols, :]) * factor + bias[:keys, cols]
        top = jnp.max(s, axis=0, keepdims=True)
        p = jnp.exp(s - top)
        total = jnp.sum(p, axis=0, keepdims=True)
        o_t = dot_nn(v_t[:, :keys], p.astype(BF)) / total
        out_ref[cols, :] = o_t.T.astype(BF)
        lse_ref[0, :, cols] = top + jnp.log(total)


def attention(span, q, k, v, cosine, sine, q_gain, k_gain, w_out, cotangent, x_rows, route_gain, number):
    length, size = k.shape
    heads = q.shape[1] // size
    whole = pl.BlockSpec((length, size), lambda h: (0, 0))
    head = pl.BlockSpec((length, size), lambda h: (0, h))
    gain = pl.BlockSpec((1, size), lambda h: (0, 0))
    in_specs = [
        pl.BlockSpec(memory_space=pltpu.SMEM), head, whole, whole, whole, whole, gain, gain,
    ]
    out_specs = [head, pl.BlockSpec((1, 1, length), lambda h: (h, 0, 0))]
    out_shape = [
        jax.ShapeDtypeStruct((length, heads * size), BF),
        jax.ShapeDtypeStruct((heads, 1, length), F32),
    ]
    scratch = [
        pltpu.VMEM((length, length), F32),
        pltpu.VMEM((length, size), BF),
        pltpu.VMEM((size, length), BF),
    ]
    args = (span, q, k, v, cosine, sine, q_gain, k_gain)
    ep_count, tp_count = lax.axis_size("ep"), lax.axis_size("tp")
    if ep_count != 2 * Z_AXIS:
        out, lse = pl.pallas_call(
            plain_attention_kernel,
            grid=(heads,),
            in_specs=in_specs,
            out_specs=out_specs,
            out_shape=out_shape,
            scratch_shapes=scratch,
            compiler_params=params(),
            name="plain_attention",
        )(*args)
        rows = lax.psum_scatter(
            dot_nn(out, w_out).astype(BF), "tp", scatter_dimension=0, tiled=True
        )
        hidden = x_rows.astype(F32) + rows.astype(F32)
        moe_in = (hidden * rms_scale(hidden) * route_gain).astype(BF)
        return out, lse, hidden, moe_in, lax.all_gather(cotangent, "ep")
    block, width = cotangent.shape
    dma = pltpu.SemaphoreType.DMA
    return pl.pallas_call(
        attention_kernel,
        grid=(heads,),
        in_specs=in_specs
        + [
            pl.BlockSpec(w_out.shape, lambda h: (0, 0), pipeline_mode=pl.Buffered(1)), ANY,
            pl.BlockSpec((block, width), lambda h: (0, 0)),
            pl.BlockSpec((1, width), lambda h: (0, 0)),
        ],
        out_specs=out_specs + [pl.BlockSpec((block, width), lambda h: (0, 0))] * 2 + [ANY],
        out_shape=out_shape
        + [
            jax.ShapeDtypeStruct((block, width), F32),
            jax.ShapeDtypeStruct((block, width), BF),
            jax.ShapeDtypeStruct((ep_count, block, width), BF),
        ],
        scratch_shapes=scratch
        + [
            pltpu.VMEM((heads, length, size), BF),
            pltpu.VMEM((tp_count, block, width), BF),
            pltpu.VMEM((2, block, width), BF),
            pltpu.VMEM((block, width), BF),
            dma((2,)), dma((2,)), dma, dma,
        ]
        + gather_sems(),
        compiler_params=params(collective_id=number, has_side_effects=True),
        cost_estimate=link_cost(90.0),
        name="attention",
    )(*args, w_out, cotangent, x_rows, route_gain)


def norm_back(grads, rows, gain):
    scale = rms_scale(rows)
    gain_part = jnp.sum(grads * rows * scale, axis=0, keepdims=True)
    inner = grads * gain
    mean = jnp.mean(inner * rows, axis=-1, keepdims=True)
    return scale * inner - rows * (scale * scale * scale * mean), gain_part


def plain_attention_back_kernel(
    span_ref, q_ref, k_ref, v_ref, grad_ref, lse_ref, cos_ref, sin_ref, qg_ref, kg_ref,
    dq_ref, dk_ref, dv_ref, dqg_ref, dkg_ref,
    bias, k_rot, k_t, dk_acc, dv_acc, dq_t,
):
    factor = q_ref.shape[-1] ** (-0.5)
    cosine, sine = cos_ref[...], sin_ref[...]
    step = pl.program_id(0)

    @pl.when(step == 0)
    def _():
        fill_bias(span_ref, bias)
        k = k_ref[...]
        rotated = turn(k * rms_scale(k) * kg_ref[...], cosine, sine)
        k_rot[...] = rotated.astype(BF)
        k_t[...] = rotated.T.astype(BF)
        dk_acc[...] = jnp.zeros_like(dk_acc)
        dv_acc[...] = jnp.zeros_like(dv_acc)
        dqg_ref[...] = jnp.zeros_like(dqg_ref)

    q = q_ref[...]
    q_rot = turn(q * rms_scale(q) * qg_ref[...], cosine, sine).astype(BF)
    for start, tile, keys in query_tiles(q.shape[0]):
        cols = slice(start, start + tile)
        s = dot_nt(k_rot[:keys, :], q_rot[cols, :]) * factor + bias[:keys, cols]
        p = jnp.exp(s - lse_ref[0, :, cols])
        grad = grad_ref[cols, :]
        dp = dot_nt(v_ref[:keys, :], grad)
        mean = jnp.sum(p * dp, axis=0, keepdims=True)
        raw = (p * (dp - mean) * factor).astype(BF)
        dq_t[:, cols] = dot_nn(k_t[:, :keys], raw)
        dk_acc[:keys, :] += dot_nn(raw, q_rot[cols, :])
        dv_acc[:keys, :] += dot_nn(p.astype(BF), grad)
    back, gain_part = norm_back(turn_back(dq_t[...].T, cosine, sine), q, qg_ref[...])
    dq_ref[...] = back.astype(BF)
    dqg_ref[...] += gain_part

    @pl.when(step == pl.num_programs(0) - 1)
    def _():
        back, gain_part = norm_back(turn_back(dk_acc[...], cosine, sine), k_ref[...], kg_ref[...])
        dk_ref[...] = back.astype(BF)
        dkg_ref[...] = gain_part
        dv_ref[...] = dv_acc[...].astype(BF)


def plain_attention_back(span, q, k, v, grads, lse, cosine, sine, q_gain, k_gain):
    length, size = k.shape
    heads = q.shape[1] // size
    whole = pl.BlockSpec((length, size), lambda h: (0, 0))
    head = pl.BlockSpec((length, size), lambda h: (0, h))
    gain = pl.BlockSpec((1, size), lambda h: (0, 0))
    return pl.pallas_call(
        plain_attention_back_kernel,
        grid=(heads,),
        in_specs=[
            pl.BlockSpec(memory_space=pltpu.SMEM), head, whole, whole, head,
            pl.BlockSpec((1, 1, length), lambda h: (h, 0, 0)), whole, whole, gain, gain,
        ],
        out_specs=[head, whole, whole, gain, gain],
        out_shape=[
            jax.ShapeDtypeStruct((length, heads * size), BF),
            jax.ShapeDtypeStruct((length, size), BF),
            jax.ShapeDtypeStruct((length, size), BF),
            jax.ShapeDtypeStruct((1, size), F32),
            jax.ShapeDtypeStruct((1, size), F32),
        ],
        scratch_shapes=[
            pltpu.VMEM((length, length), F32),
            pltpu.VMEM((length, size), BF),
            pltpu.VMEM((size, length), BF),
            pltpu.VMEM((length, size), F32),
            pltpu.VMEM((length, size), F32),
            pltpu.VMEM((size, length), F32),
        ],
        compiler_params=params(),
        name="plain_attention_back",
    )(span, q, k, v, grads, lse, cosine, sine, q_gain, k_gain)


def attention_back_kernel(
    span_ref, q_ref, k_ref, v_ref, lse_ref, cos_ref, sin_ref, qg_ref, kg_ref,
    w_out_ref, rows_ref, slots_ref, out_a, out_b, hidden_ref,
    dq_ref, dk_ref, dv_ref, dqg_ref, dkg_ref, branch_ref, output_ref,
    bias, k_rot, k_t, dk_acc, dv_acc, dq_t, branch, grads, part, buf, sem,
    own_sem, out_sem, core_send, core_recv, x_send, x_recv, *refs,
):
    factor = q_ref.shape[-1] ** (-0.5)
    size = q_ref.shape[-1]
    cosine, sine = cos_ref[...], sin_ref[...]
    step = pl.program_id(0)
    me = lax.axis_index("tp")
    x, c = me // 2, me % 2
    other_core, other_x = {"tp": x * 2 + 1 - c}, {"tp": (1 - x) * 2 + c}
    reduce = EpReduce(ring_pieces(part, 1), BY_Z, refs[:6], refs[6:])
    sums = SlotSums(slots_ref, out_a, out_b, buf, sem)
    order, y = reduce.order, reduce.y
    block = rows_ref.shape[0]
    near_other, far, far_other = x * 2 + 1 - c, (1 - x) * 2 + c, (1 - x) * 2 + 1 - c

    def to_core(slot, src, tp):
        return remote(src, branch.at[tp], core_send.at[slot], core_recv.at[slot], other_core)

    def to_x(tp):
        return remote(rows_ref, branch.at[tp], x_send, x_recv, other_x)

    def own_rows():
        return pltpu.make_async_copy(rows_ref, branch.at[me], own_sem)

    def whole_branch():
        return pltpu.make_async_copy(branch, branch_ref, out_sem)

    @pl.when(step == 0)
    def _():
        greet(reduce.partners() + [(x >= 0, other_core), (x >= 0, other_x)])
        to_x(me).start()
        to_core(0, rows_ref, me).start()
        own_rows().start()
        sums.run([order[k] * 2 + 1 - y for k in range(Z_AXIS)], part, reduce.send_side)
        fill_bias(span_ref, bias)
        k = k_ref[...]
        rotated = turn(k * rms_scale(k) * kg_ref[...], cosine, sine)
        k_rot[...] = rotated.astype(BF)
        k_t[...] = rotated.T.astype(BF)
        dk_acc[...] = jnp.zeros_like(dk_acc)
        dv_acc[...] = jnp.zeros_like(dv_acc)
        dqg_ref[...] = jnp.zeros_like(dqg_ref)

        def head_grads(tp):
            lines = pl.ds(pl.multiple_of(tp * block, block), block)
            rows = dot_nt(branch[tp], w_out_ref[...]).astype(BF)
            for h in range(grads.shape[0]):
                grads[h, lines, :] = rows[:, h * size : (h + 1) * size]

        own_rows().wait()
        head_grads(me)
        to_core(0, rows_ref, near_other).wait_recv()
        head_grads(near_other)
        sums.run([order[k] * 2 + y for k in range(Z_AXIS)], part, lambda k: None)
        reduce.step_z(0)
        reduce.step_z(1)
        reduce.step_y(0)
        to_x(far).wait_recv()
        to_core(1, branch.at[far], far).start()
        head_grads(far)
        to_core(1, branch.at[far], far_other).wait_recv()
        head_grads(far_other)
        whole_branch().start()
        reduce.step_z(2)
        reduce.step_z(3)

    for k, head in ((1, 1), (2, 5)):

        @pl.when(step == head)
        def _(k=k):
            reduce.step_y(k)

    q = q_ref[...]
    q_rot = turn(q * rms_scale(q) * qg_ref[...], cosine, sine).astype(BF)
    for start, tile, keys in query_tiles(q.shape[0]):
        cols = slice(start, start + tile)
        s = dot_nt(k_rot[:keys, :], q_rot[cols, :]) * factor + bias[:keys, cols]
        p = jnp.exp(s - lse_ref[0, :, cols])
        grad = grads[step, cols, :]
        dp = dot_nt(v_ref[:keys, :], grad)
        mean = jnp.sum(p * dp, axis=0, keepdims=True)
        raw = (p * (dp - mean) * factor).astype(BF)
        dq_t[:, cols] = dot_nn(k_t[:, :keys], raw)
        dk_acc[:keys, :] += dot_nn(raw, q_rot[cols, :])
        dv_acc[:keys, :] += dot_nn(p.astype(BF), grad)
    back, gain_part = norm_back(turn_back(dq_t[...].T, cosine, sine), q, qg_ref[...])
    dq_ref[...] = back.astype(BF)
    dqg_ref[...] += gain_part

    @pl.when(step == pl.num_programs(0) - 1)
    def _():
        back, gain_part = norm_back(turn_back(dk_acc[...], cosine, sine), k_ref[...], kg_ref[...])
        dk_ref[...] = back.astype(BF)
        dkg_ref[...] = gain_part
        dv_ref[...] = dv_acc[...].astype(BF)
        reduce.step_y(Z_AXIS - 1)
        pairs = zip(ring_pieces(output_ref, 0), ring_pieces(hidden_ref, 0))
        for a, (rows, residual) in enumerate(pairs):
            reduce.own(a, lambda terms, rows=rows, residual=residual: add_rows(rows, terms + [residual]))
        reduce.sent()
        whole_branch().wait()
        to_x(me).wait_send()
        to_core(0, rows_ref, me).wait_send()
        to_core(1, branch.at[far], far).wait_send()


def attention_back(
    span, q, k, v, lse, cosine, sine, q_gain, k_gain, w_out, d_rows, slots_t, out, hidden, number
):
    length, size = k.shape
    heads = q.shape[1] // size
    ep_count, tp_count = lax.axis_size("ep"), lax.axis_size("tp")
    if ep_count != 2 * Z_AXIS:
        branch = lax.all_gather(d_rows, "tp", axis=0, tiled=True)
        grads = dot_nt(branch, w_out).astype(BF)
        mine = lax.psum_scatter(out, "ep", scatter_dimension=0)
        back = plain_attention_back(span, q, k, v, grads, lse, cosine, sine, q_gain, k_gain)
        return *back, branch, (hidden + mine.astype(F32)).astype(BF)
    block, width = d_rows.shape
    whole = pl.BlockSpec((length, size), lambda h: (0, 0))
    head = pl.BlockSpec((length, size), lambda h: (0, h))
    gain = pl.BlockSpec((1, size), lambda h: (0, 0))
    rows = pl.BlockSpec((block, width), lambda h: (0, 0))
    dma = pltpu.SemaphoreType.DMA
    *back, branch, output = pl.pallas_call(
        attention_back_kernel,
        grid=(heads,),
        in_specs=[
            pl.BlockSpec(memory_space=pltpu.SMEM), head, whole, whole,
            pl.BlockSpec((1, 1, length), lambda h: (h, 0, 0)), whole, whole, gain, gain,
            pl.BlockSpec(w_out.shape, lambda h: (0, 0), pipeline_mode=pl.Buffered(1)), ANY,
            pl.BlockSpec(slots_t.shape, lambda h: (0, 0, 0), pipeline_mode=pl.Buffered(1)), ANY, ANY,
            pl.BlockSpec((block, width), lambda h: (0, 0), pipeline_mode=pl.Buffered(1)),
        ],
        out_specs=[head, whole, whole, gain, gain, ANY, rows],
        out_shape=[
            jax.ShapeDtypeStruct((length, heads * size), BF),
            jax.ShapeDtypeStruct((length, size), BF),
            jax.ShapeDtypeStruct((length, size), BF),
            jax.ShapeDtypeStruct((1, size), F32),
            jax.ShapeDtypeStruct((1, size), F32),
            jax.ShapeDtypeStruct((tp_count, block, width), BF),
            jax.ShapeDtypeStruct((block, width), BF),
        ],
        scratch_shapes=[
            pltpu.VMEM((length, length), F32),
            pltpu.VMEM((length, size), BF),
            pltpu.VMEM((size, length), BF),
            pltpu.VMEM((length, size), F32),
            pltpu.VMEM((length, size), F32),
            pltpu.VMEM((size, length), F32),
            pltpu.VMEM((tp_count, block, width), BF),
            pltpu.VMEM((heads, length, size), BF),
        ]
        + [pltpu.VMEM((ep_count, block, width), BF)]
        + slot_sums_scratch(slots_t.shape[2], out[0].shape[2], width)
        + [dma, dma, dma((2,)), dma((2,)), dma, dma]
        + reduce_scratch(block, width)
        + reduce_sems(3),
        compiler_params=params(collective_id=number, has_side_effects=True),
        cost_estimate=link_cost(100.0),
        name="attention_back",
    )(span, q, k, v, lse, cosine, sine, q_gain, k_gain, w_out, d_rows, slots_t, *out, hidden)
    return *back, branch.reshape(-1, width), output


def projection_grads_kernel(
    normed, dq, dk, dv, heads, branch, wq_hbm, wk, wv, x_rows, d_hbm, gain, small,
    gq_ref, gk_ref, gv_ref, gout_ref, inputs_grad, gain_grad, small_sum,
    blocks, out_blocks, gout, part, core_rows, far_rows, gain_own, tp_gains, tp_gain, ep_gains, wq, d_hidden,
    core_send, core_recv, x_send, x_recv, wq_sem, d_sem, *refs,
):
    me = lax.axis_index("tp")
    x, c = me // 2, me % 2
    other_core, other_x = {"tp": x * 2 + 1 - c}, {"tp": (1 - x) * 2 + c}
    sums = SumAll(small, small_sum, *refs[:5], refs[5:13])
    over_tp, over_ep = Exchange("tp", refs[13], refs[14]), Exchange("ep", refs[15], refs[16])
    reduce = EpReduce(
        ring_pieces(blocks, 1) + ring_pieces(out_blocks, 1), BY_Z * 2, refs[17:29], refs[29:]
    )
    order, y = reduce.order, reduce.y
    rows, width = inputs_grad.shape
    nq, nk = dq.shape[1], dk.shape[1]

    load_wq = pltpu.make_async_copy(wq_hbm, wq, wq_sem)
    load_d = pltpu.make_async_copy(d_hbm, d_hidden, d_sem)
    load_wq.start()
    load_d.start()
    everyone = []
    for exchange in (over_tp, over_ep):
        exchange.each(
            lambda i, other, axis=exchange.axis: everyone.append((other >= 0, {axis: other}))
        )
    greet(everyone)

    def fill(j):
        cols = pl.ds(pl.multiple_of(j * rows, rows), rows)
        left = normed[:, cols].T
        blocks[j, :, 0:nq] = dot_nn(left, dq[...]).astype(BF)
        blocks[j, :, nq : nq + nk] = dot_nn(left, dk[...]).astype(BF)
        blocks[j, :, nq + nk : nq + 2 * nk] = dot_nn(left, dv[...]).astype(BF)
        out_blocks[j] = dot_nn(branch[:, cols].T, heads[...]).astype(BF)

    def spread_back(tp):
        lines = pl.ds(pl.multiple_of(tp * rows, rows), rows)
        for start in range(0, width, width // 4):
            cols = slice(start, start + width // 4)
            part[tp, :, cols] = (
                dot_nt(dq[lines, :], wq[cols, :])
                + dot_nt(dk[lines, :], wk[cols, :])
                + dot_nt(dv[lines, :], wv[cols, :])
            ).astype(BF)

    def to_core(xt):
        return remote(
            part.at[xt * 2 + 1 - c], core_rows.at[xt], core_send.at[xt], core_recv.at[xt], other_core
        )

    far, near = part.at[(1 - x) * 2 + c], part.at[x * 2 + c]
    to_x = remote(far, far_rows, x_send, x_recv, other_x)

    for k in range(2):
        fill(order[k] * 2 + 1 - y)
        reduce.send_side(k)
    load_wq.wait()
    spread_back((1 - x) * 2 + 1 - c)
    to_core(1 - x).start()
    spread_back((1 - x) * 2 + c)
    to_core(1 - x).wait_recv()
    add_rows(far, [far, core_rows.at[1 - x]])
    to_x.start()
    for k in range(2, Z_AXIS):
        fill(order[k] * 2 + 1 - y)
        reduce.send_side(k)
    sums.start()
    fill(order[0] * 2 + y)
    reduce.step_z(0)
    fill(order[1] * 2 + y)
    reduce.step_z(1)
    reduce.step_y(0)
    fill(order[2] * 2 + y)
    reduce.step_z(2)
    sums.across()
    fill(order[3] * 2 + y)
    reduce.step_z(3)
    spread_back(x * 2 + 1 - c)
    to_core(x).start()
    spread_back(x * 2 + c)
    reduce.step_y(1)
    sums.back()
    to_core(x).wait_recv()
    to_x.wait_recv()
    load_d.wait()

    chunk = 32
    gain_own[...] = jnp.zeros_like(gain_own)

    @pl.loop(0, rows // chunk)
    def _(i):
        lines = pl.ds(pl.multiple_of(i * chunk, chunk), chunk)
        grad = near[lines, :].astype(F32) + core_rows[x, lines, :].astype(F32)
        grad = grad + far_rows[lines, :].astype(F32)
        back, gain_part = norm_back(grad, x_rows[lines, :].astype(F32), gain[...])
        inputs_grad[lines, :] = d_hidden[lines, :] + back
        gain_own[...] += gain_part

    over_tp.start(lambda t: gain_own, tp_gains)
    tp_gains[pl.ds(over_tp.me, 1)] = gain_own[...][None]
    sums.home()
    reduce.step_y(2)
    over_tp.arrived(tp_gains)
    tp_gain[...] = jnp.sum(tp_gains[...], axis=0)
    over_ep.start(lambda e: tp_gain, ep_gains)
    ep_gains[pl.ds(over_ep.me, 1)] = tp_gain[...][None]
    reduce.step_y(3)

    def total_of(terms):
        value = terms[0][...].astype(F32)
        for term in terms[1:]:
            value = value + term[...].astype(F32)
        return value

    over_ep.arrived(ep_gains)
    gain_grad[...] = jnp.sum(ep_gains[...], axis=0)
    results = zip(*[ring_pieces(ref, 0) for ref in (gq_ref, gk_ref, gv_ref)])
    for a, (to_q, to_k, to_v) in enumerate(results):

        def write(terms, to_q=to_q, to_k=to_k, to_v=to_v):
            value = total_of(terms)
            to_q[...] = value[:, 0:nq]
            to_k[...] = value[:, nq : nq + nk]
            to_v[...] = value[:, nq + nk :]

        reduce.own(a, write)
    for a, rows_to in enumerate(ring_pieces(gout, 0)):

        def write_out(terms, rows_to=rows_to):
            rows_to[...] = total_of(terms)

        reduce.own(3 + a, write_out)
    gout_ref[...] = gout[...].T
    reduce.sent()
    to_core(1 - x).wait_send()
    to_core(x).wait_send()
    to_x.wait_send()
    over_tp.sent(lambda t: gain_own, tp_gains)
    over_ep.sent(lambda e: tp_gain, ep_gains)
    sums.finish()


def projection_grads(
    normed, dq, dk, dv, heads, branch, wq, wk, wv, x_rows, d_hidden, gain, small_values, number
):
    rows, width = x_rows.shape
    ep_count, tp_count = lax.axis_size("ep"), lax.axis_size("tp")
    small = pack_small(small_values, tp_count, ep_count)
    if ep_count != 2 * Z_AXIS:

        def over_sequences(part, dim):
            return lax.psum_scatter(
                part.astype(BF), "ep", scatter_dimension=dim, tiled=True
            ).astype(F32)

        d_normed = (dot_nt(dq, wq) + dot_nt(dk, wk) + dot_nt(dv, wv)).astype(BF)
        d_mine = lax.psum_scatter(d_normed, "tp", scatter_dimension=0, tiled=True)
        back, gain_part = norm_back(d_mine.astype(F32), x_rows.astype(F32), gain)
        gain_sum, small_sum = lax.psum((gain_part, small), ("ep", "tp"))
        return (
            over_sequences(dot_tn(normed, dq), 0),
            over_sequences(dot_tn(normed, dk), 0),
            over_sequences(dot_tn(normed, dv), 0),
            over_sequences(dot_tn(heads, branch), 1),
            d_hidden + back,
            gain_sum,
            unpack_small(small_sum, small_values),
        )
    nq, nk = dq.shape[1], dk.shape[1]
    nh = heads.shape[1]
    vmem = pl.BlockSpec(memory_space=pltpu.VMEM)
    dma = pltpu.SemaphoreType.DMA
    *grads, small_sum = pl.pallas_call(
        projection_grads_kernel,
        in_specs=[vmem] * 6 + [ANY] + [vmem] * 3 + [ANY] + [vmem] * 2,
        out_specs=[vmem] * 7,
        out_shape=[
            jax.ShapeDtypeStruct((rows, nq), F32),
            jax.ShapeDtypeStruct((rows, nk), F32),
            jax.ShapeDtypeStruct((rows, nk), F32),
            jax.ShapeDtypeStruct((nh, rows), F32),
            jax.ShapeDtypeStruct((rows, width), F32),
            jax.ShapeDtypeStruct((1, width), F32),
            jax.ShapeDtypeStruct(small.shape, F32),
        ],
        scratch_shapes=[
            pltpu.VMEM((ep_count, rows, nq + 2 * nk), BF),
            pltpu.VMEM((ep_count, rows, nh), BF),
            pltpu.VMEM((rows, nh), F32),
            pltpu.VMEM((tp_count, rows, width), BF),
            pltpu.VMEM((2, rows, width), BF),
            pltpu.VMEM((rows, width), BF),
            pltpu.VMEM((1, width), F32),
            pltpu.VMEM((tp_count, 1, width), F32),
            pltpu.VMEM((1, width), F32),
            pltpu.VMEM((ep_count, 1, width), F32),
            pltpu.VMEM(wq.shape, BF),
            pltpu.VMEM((rows, width), F32),
            dma((2,)), dma((2,)), dma, dma, dma, dma,
        ]
        + sum_scratch(small.shape)
        + exchange_sems("tp")
        + exchange_sems("ep")
        + reduce_scratch(rows, nq + 2 * nk)
        + reduce_scratch(rows, nh)
        + reduce_sems(6),
        compiler_params=params(collective_id=number, has_side_effects=True),
        cost_estimate=link_cost(110.0),
        name="projection_grads",
    )(normed, dq, dk, dv, heads, branch, wq, wk, wv, x_rows, d_hidden, gain, small)
    return *grads, unpack_small(small_sum, small_values)


def select_kernel(slot_ref, x_ref, c_ref, xs_ref, cs_ref):
    local, _, capacity, width = xs_ref.shape
    rows = x_ref.shape[1]
    place = jnp.concatenate(
        [
            (
                slot_ref[0, e : e + 1, :]
                == lax.broadcasted_iota(jnp.int32, (capacity, rows), 0)
            ).astype(F32)
            for e in range(local)
        ],
        axis=0,
    ).astype(BF)
    xs_ref[...] = dot_nn(place, x_ref[0]).astype(BF).reshape(xs_ref.shape)
    cs_ref[...] = dot_nn(place, c_ref[0]).astype(BF).reshape(cs_ref.shape)


def select_rows(slots, tokens, cots, capacity):
    blocks, local, rows = slots.shape
    width = tokens.shape[-1]
    block = pl.BlockSpec((1, rows, width), lambda b: (b, 0, 0))
    out = pl.BlockSpec((local, 1, capacity, width), lambda b: (0, b, 0, 0))
    shape = jax.ShapeDtypeStruct((local, blocks, capacity, width), BF)
    return pl.pallas_call(
        select_kernel,
        grid=(blocks,),
        in_specs=[pl.BlockSpec((1, local, rows), lambda b: (b, 0, 0)), block, block],
        out_specs=[out, out],
        out_shape=[shape, shape],
        compiler_params=params(),
        name="select_rows",
    )(slots, tokens, cots)


def pack_kernel(gate_ref, up_ref, down_ref, out_ref):
    for kind, ref in enumerate((gate_ref, up_ref, down_ref)):
        out_ref[kind, 0] = ref[0]


def pack_weights(weights, first, count):
    _, hidden, width = weights[0].shape
    block = pl.BlockSpec((1, hidden, width), lambda e: (first + e, 0, 0))
    return pl.pallas_call(
        pack_kernel,
        grid=(count,),
        in_specs=[block] * 3,
        out_specs=pl.BlockSpec((3, 1, hidden, width), lambda e: (0, e, 0, 0)),
        out_shape=jax.ShapeDtypeStruct((3, count, hidden, width), BF),
        compiler_params=params(),
        name="pack_weights",
    )(*weights)


def expert_kernel(
    x_ref, c_ref, w_ref, gate_ref, out_ref, dx_ref, act_ref, dg_ref, du_ref, dgate_ref
):
    width = x_ref.shape[-1]
    x, c = x_ref[0], c_ref[0]
    w_gate = w_ref[:, 0, 0].reshape(-1, width)
    w_up = w_ref[:, 1, 0].reshape(-1, width)
    w_down = w_ref[:, 2, 0].reshape(-1, width)
    gate = gate_ref[0]
    gate_pre = dot_nt(x, w_gate)
    up_pre = dot_nt(x, w_up)
    raw = dot_nt(c, w_down)
    sig = jax.nn.sigmoid(gate_pre)
    silu = gate_pre * sig
    act = silu * up_pre
    dgate_ref[0] = jnp.sum(act * raw, axis=-1, keepdims=True)
    act_low = (act * gate).astype(BF)
    d_act = raw * gate
    d_gate = (d_act * up_pre * sig * (1.0 + gate_pre * (1.0 - sig))).astype(BF)
    d_up = (d_act * silu).astype(BF)
    act_ref[0] = act_low
    dg_ref[0] = d_gate
    du_ref[0] = d_up
    out_ref[0] = dot_nn(act_low, w_down).astype(BF)
    dx_ref[0] = (dot_nn(d_gate, w_gate) + dot_nn(d_up, w_up)).astype(BF)


def experts_both_ways(x_slots, c_slots, w_all, slot_gate, first):
    _, number, width = x_slots.shape
    parts, _, local, hidden, _ = w_all.shape
    tile = number // 2
    taken = pl.BlockSpec((1, tile, width), lambda e, i: (first + e, i, 0))
    wide = pl.BlockSpec((1, tile, width), lambda e, i: (e, i, 0))
    mid = pl.BlockSpec((1, tile, parts * hidden), lambda e, i: (e, i, 0))
    thin = pl.BlockSpec((1, tile, 1), lambda e, i: (e, i, 0))
    wide_shape = jax.ShapeDtypeStruct((local, number, width), BF)
    mid_shape = jax.ShapeDtypeStruct((local, number, parts * hidden), BF)
    return pl.pallas_call(
        expert_kernel,
        grid=(local, 2),
        in_specs=[
            taken, taken,
            pl.BlockSpec((parts, 3, 1, hidden, width), lambda e, i: (0, 0, e, 0, 0)),
            pl.BlockSpec((1, tile, 1), lambda e, i: (first + e, i, 0)),
        ],
        out_specs=[wide, wide, mid, mid, mid, thin],
        out_shape=[
            wide_shape, wide_shape, mid_shape, mid_shape, mid_shape,
            jax.ShapeDtypeStruct((local, number, 1), F32),
        ],
        compiler_params=params(),
        name="experts_both_ways",
    )(x_slots, c_slots, w_all, slot_gate)


def expert_grads_kernel(x_ref, c_ref, act_ref, dg_ref, du_ref, out_ref):
    parts, _, _, hidden, width = out_ref.shape
    x, c = x_ref[0], c_ref[0]
    out_ref[:, 0, 0] = dot_tn(dg_ref[0], x).astype(BF).reshape(parts, hidden, width)
    out_ref[:, 1, 0] = dot_tn(du_ref[0], x).astype(BF).reshape(parts, hidden, width)
    out_ref[:, 2, 0] = dot_tn(act_ref[0], c).astype(BF).reshape(parts, hidden, width)


def expert_grads(x_slots, c_slots, act, d_gate, d_up, parts, first):
    local, number, inner = act.shape
    width = x_slots.shape[-1]
    wide = pl.BlockSpec((1, number, width), lambda e: (first + e, 0, 0))
    mid = pl.BlockSpec((1, number, inner), lambda e: (e, 0, 0))
    return pl.pallas_call(
        expert_grads_kernel,
        grid=(local,),
        in_specs=[wide, wide, mid, mid, mid],
        out_specs=pl.BlockSpec(
            (parts, 3, 1, inner // parts, width), lambda e: (0, 0, e, 0, 0)
        ),
        out_shape=jax.ShapeDtypeStruct((parts, 3, local, inner // parts, width), BF),
        compiler_params=params(),
        name="expert_grads",
    )(x_slots, c_slots, act, d_gate, d_up)


def combine_kernel(
    first_ref, slot_ref, dxa_ref, dxb_ref, outa_ref, outb_ref, dgate_ref, dx_sum_ref, out_sum_ref, pay_ref
):
    _, _, capacity, width = dxa_ref.shape
    local = slot_ref.shape[2]
    rows = slot_ref.shape[1]
    lane = lax.broadcasted_iota(jnp.int32, (rows, local * capacity), 1)
    half = pay_ref.shape[2] // 2
    column = lax.broadcasted_iota(jnp.int32, (rows, 2 * half), 1)
    total = jnp.zeros((rows, local * capacity), F32)
    pay = jnp.zeros(column.shape, F32)
    for e in range(local):
        hit = lane == slot_ref[0, :, e : e + 1] + e * capacity
        total = jnp.where(hit, 1.0, total)
        value = jnp.sum(jnp.where(hit, dgate_ref[0], 0.0), axis=1, keepdims=True)
        high = value.astype(BF).astype(F32)
        pay = jnp.where(column == first_ref[0, 0] + e, high, pay)
        pay = jnp.where(column == first_ref[0, 0] + e + half, value - high, pay)
    place = total.astype(BF)

    def both(a_ref, b_ref):
        pair = [ref[...].reshape(-1, width) for ref in (a_ref, b_ref)]
        return dot_nn(place, jnp.concatenate(pair, axis=0)).astype(BF)

    dx_sum_ref[0] = both(dxa_ref, dxb_ref)
    out_sum_ref[0] = both(outa_ref, outb_ref)
    pay_ref[0] = pay.astype(BF)


def combine_rows(first, slots_t, dx, out, d_gate_slots, experts):
    blocks, rows, local = slots_t.shape
    _, _, capacity, width = dx[0].shape
    lanes = -(-2 * experts // 128) * 128
    slot = pl.BlockSpec((local // 2, 1, capacity, width), lambda b: (0, b, 0, 0))
    block = pl.BlockSpec((1, rows, width), lambda b: (b, 0, 0))
    shape = jax.ShapeDtypeStruct((blocks, rows, width), BF)
    return pl.pallas_call(
        combine_kernel,
        grid=(blocks,),
        in_specs=[
            pl.BlockSpec(memory_space=pltpu.SMEM),
            pl.BlockSpec((1, rows, local), lambda b: (b, 0, 0)), slot, slot, slot, slot,
            pl.BlockSpec((1, 1, local * capacity), lambda b: (b, 0, 0)),
        ],
        out_specs=[block, block, pl.BlockSpec((1, rows, lanes), lambda b: (b, 0, 0))],
        out_shape=[shape, shape, jax.ShapeDtypeStruct((blocks, rows, lanes), BF)],
        compiler_params=params(),
        name="combine_rows",
    )(first, slots_t, *dx, *out, d_gate_slots)


def on_device(
    inputs,
    attn_gain,
    w_query,
    key_weight_matrix,
    value_weight_matrix,
    query_gain,
    key_gain,
    w_out,
    route_gain,
    w_router,
    w_gate,
    w_up,
    w_down,
    routes,
    image_starts,
    cotangent,
):
    tp_count = lax.axis_size("tp")
    ep_count = lax.axis_size("ep")
    tp_index = lax.axis_index("tp")
    ep_index = lax.axis_index("ep")
    length = inputs.shape[0]
    width = inputs.shape[1]
    rows = cotangent.shape[0]
    head_dim = query_gain.shape[0]
    local_experts = w_gate.shape[0]
    experts = local_experts * ep_count
    top = routes.shape[1]
    capacity = -(-(3 * rows * top // (2 * experts)) // 16) * 16

    pair = local_experts // 2

    weights = (w_gate.transpose(0, 2, 1), w_up.transpose(0, 2, 1), w_down)
    w_first = lax.all_gather(pack_weights(weights, 0, pair), "tp")

    inputs_f = inputs.astype(F32)
    attn_scale = rms_scale(inputs_f)
    normed = (inputs_f * attn_scale * attn_gain).astype(BF)
    queries = dot_nn(normed, w_query)
    key_rows = dot_nn(normed, key_weight_matrix)
    values = dot_nn(normed, value_weight_matrix).astype(BF)
    cosine, sine = rope_tables(length, head_dim)
    q_gain, k_gain = query_gain[None], key_gain[None]
    queries, second = lax.optimization_barrier((queries, pack_weights(weights, pair, pair)))
    w_second = lax.all_gather(second, "tp")
    x_rows = lax.dynamic_slice_in_dim(inputs, tp_index * rows, rows, 0)
    heads, lse, hidden, moe_in, cot_all = attention(
        image_starts, queries, key_rows, values, cosine, sine, q_gain, k_gain,
        w_out, cotangent, x_rows, route_gain[None], 0,
    )
    logits = dot_nn(moe_in, w_router)
    router_probs = plain_softmax(logits)
    expert_ids = jnp.arange(experts, dtype=jnp.int32)
    ring_routes = lax.dynamic_index_in_dim(
        routes.reshape(ep_count, tp_count, rows, top), tp_index, 1, keepdims=False
    )
    my_routes = lax.dynamic_index_in_dim(ring_routes, ep_index, 0, keepdims=False)

    def routed_softmax(scores, picked):
        kept = jnp.where(picked, scores, MASKED)
        expo = jnp.where(picked, jnp.exp(kept - jnp.max(kept, axis=-1, keepdims=True)), 0.0)
        return expo / jnp.sum(expo, axis=-1, keepdims=True)

    my_pick = jnp.any(my_routes[:, :, None] == expert_ids[None, None, :], axis=1)
    gates = routed_softmax(logits, my_pick)
    all_pick = jnp.any(ring_routes[..., None] == expert_ids, axis=2)
    mask = lax.dynamic_slice_in_dim(all_pick, ep_index * local_experts, local_experts, 2)
    earlier = (jnp.arange(rows)[:, None] > jnp.arange(rows)[None, :]).astype(BF)
    slots_t = jnp.einsum(
        "tu,bue->bte", earlier, mask.astype(BF), preferred_element_type=F32
    ).astype(jnp.int32)
    slots_t = jnp.where(mask, slots_t, NOWHERE)
    slots = slots_t.transpose(0, 2, 1)
    ring = ep_count == 2 * Z_AXIS
    if ring:
        turned = lax.rem(expert_ids + ep_index * local_experts, experts)
        x_slots, c_slots, slot_gate = gather_select(
            moe_in,
            cot_all,
            slots,
            all_pick.astype(jnp.int32)[..., turned].transpose(0, 2, 1),
            w_router.T[turned],
            capacity,
            1,
        )
        slot_gate = slot_gate.reshape(local_experts, ep_count * capacity, 1)
    else:
        tokens_all = lax.all_gather(moe_in, "ep")
        logits_all = dot_nn(tokens_all.reshape(-1, width), w_router).reshape(ep_count, rows, experts)
        gate_of = lax.dynamic_slice_in_dim(
            routed_softmax(logits_all, all_pick), ep_index * local_experts, local_experts, 2
        )
        place = slots[:, :, None, :] == jnp.arange(capacity, dtype=jnp.int32)[:, None]
        slot_gate = jnp.sum(
            jnp.where(place, gate_of.transpose(0, 2, 1)[:, :, None, :], 0.0), axis=-1
        )
        slot_gate = slot_gate.transpose(1, 0, 2).reshape(local_experts, ep_count * capacity, 1)
        x_slots, c_slots = select_rows(slots, tokens_all, cot_all, capacity)
    flat = (local_experts, ep_count * capacity, width)
    x_slots, c_slots = x_slots.reshape(flat), c_slots.reshape(flat)

    def over_rings(grads):
        return lax.psum_scatter(grads.reshape(-1, width), "tp", scatter_dimension=0, tiled=True)

    out_a, dx_a, *inner_a, dg_a = experts_both_ways(x_slots, c_slots, w_first, slot_gate, 0)
    grads_a = expert_grads(x_slots, c_slots, *inner_a, tp_count, 0)
    x_slots, grads_a = lax.optimization_barrier((x_slots, grads_a))
    mine_a = over_rings(grads_a)
    out_b, dx_b, *inner_b, dg_b = experts_both_ways(x_slots, c_slots, w_second, slot_gate, pair)
    deep = (pair, ep_count, capacity, width)
    dx_slots = [dx_a.reshape(deep), dx_b.reshape(deep)]
    out_slots = [out_a.reshape(deep), out_b.reshape(deep)]
    d_gate_slots = (
        jnp.concatenate([dg_a, dg_b])
        .reshape(local_experts, ep_count, capacity)
        .transpose(1, 0, 2)
        .reshape(ep_count, 1, local_experts * capacity)
    )
    counts = jnp.sum((routes[:, :, None] == expert_ids[None, None, :]).astype(F32), axis=(0, 1))
    total_tokens = routes.shape[0]
    share = counts / (total_tokens * top)
    coeff = AUX * experts * share
    if ring:
        d_hidden, d_rows, router_part, route_gain_part, grads_b = input_grads(
            slots_t, d_gate_slots, dx_slots, x_slots, c_slots, inner_b,
            [
                hidden, moe_in, cotangent, route_gain[None], gates, router_probs,
                coeff[None], w_router.T,
            ],
            experts, tp_count, 2,
        )
    else:
        grads_b = expert_grads(x_slots, c_slots, *inner_b, tp_count, pair)
        dx_part, out_slots, gate_part = combine_rows(
            (ep_index * local_experts).reshape(1, 1), slots_t, dx_slots, out_slots, d_gate_slots, experts
        )
        dx_mine = lax.psum_scatter(dx_part, "ep", scatter_dimension=0).astype(F32)
        gate_mine = lax.psum_scatter(gate_part, "ep", scatter_dimension=0).astype(F32)
        lanes = gate_mine.shape[1] // 2
        d_gates = gate_mine[:, :experts] + gate_mine[:, lanes : lanes + experts]
        d_logits = gates * (d_gates - jnp.sum(gates * d_gates, axis=-1, keepdims=True))
        d_logits = d_logits + router_probs * (
            coeff - jnp.sum(router_probs * coeff, axis=-1, keepdims=True)
        )
        d_low = d_logits.astype(BF)
        router_part = dot_tn(d_low, moe_in)
        d_moe = dot_nt(d_low, w_router) + dx_mine
        back, route_gain_part = norm_back(d_moe, hidden, route_gain[None])
        d_hidden = cotangent.astype(F32) + back
        d_rows = d_hidden.astype(BF)
    d_rows, mine_a, grads_b = lax.optimization_barrier((d_rows, mine_a, grads_b))
    mine_b = over_rings(grads_b)
    mine_a, mine_b = [m.reshape(3, pair, -1, width) for m in (mine_a, mine_b)]
    w_gate_grad, w_up_grad = [
        jnp.concatenate([mine_a[i], mine_b[i]]).transpose(0, 2, 1).astype(F32) for i in range(2)
    ]
    w_down_grad = jnp.concatenate([mine_a[2], mine_b[2]]).astype(F32)
    prob_local = jnp.sum(router_probs, axis=0)
    d_queries, d_keys, d_values, query_gain_part, key_gain_part, d_branch, output = attention_back(
        image_starts, queries, key_rows, values, lse, cosine, sine, q_gain, k_gain,
        w_out, d_rows, slots_t, out_slots, hidden, 3,
    )
    w_query_grad, w_key_grad, w_value_grad, w_out_grad, inputs_grad, attn_gain_grad, small = projection_grads(
        normed, d_queries, d_keys, d_values, heads, d_branch,
        w_query, key_weight_matrix, value_weight_matrix,
        x_rows, d_hidden, attn_gain[None],
        [router_part, route_gain_part[0], query_gain_part[0], key_gain_part[0], prob_local],
        5,
    )
    w_router_grad, route_gain_grad, query_gain_grad, key_gain_grad, prob_all = small
    w_router_grad = w_router_grad.T
    attn_gain_grad = attn_gain_grad[0]
    aux_loss = experts * jnp.sum(share * (prob_all / total_tokens))
    return (
        output,
        aux_loss,
        inputs_grad,
        attn_gain_grad,
        w_query_grad,
        w_key_grad,
        w_value_grad,
        query_gain_grad,
        key_gain_grad,
        w_out_grad,
        route_gain_grad,
        w_router_grad,
        w_gate_grad,
        w_up_grad,
        w_down_grad,
    )


def solution(mesh):
    return jax.shard_map(
        on_device,
        mesh=mesh,
        in_specs=(
            P("ep", None),
            P(),
            P(None, "tp"),
            P(None, "tp"),
            P(None, "tp"),
            P(),
            P(),
            P("tp", None),
            P(),
            P(),
            P("ep", None, "tp"),
            P("ep", None, "tp"),
            P("ep", "tp", None),
            P(),
            P("ep", None),
            P(("ep", "tp"), None),
        ),
        out_specs=(
            P(("ep", "tp"), None),
            P(),
            P(("ep", "tp"), None),
            P(),
            P("ep", "tp"),
            P("ep", "tp"),
            P("ep", "tp"),
            P(),
            P(),
            P("tp", "ep"),
            P(),
            P(),
            P("ep", None, "tp"),
            P("ep", None, "tp"),
            P("ep", "tp", None),
        ),
        check_vma=False,
    )
```

```python
import functools

import jax
import jax.numpy as jnp
import numpy as np
from jax import lax
from jax.experimental import pallas as pl
from jax.experimental.pallas import tpu as pltpu
from jax.sharding import PartitionSpec as P

IMG = 256
EPS = 1e-06
AUX = 0.04
THETA = 1000000.0
MASKED = -1e30
NOWHERE = -(1 << 20)
BF = jnp.bfloat16
F32 = jnp.float32
VMEM_BYTES = 60 * 1024 * 1024


def dot_nn(a, b):
    return lax.dot_general(a, b, (((1,), (0,)), ((), ())), preferred_element_type=F32)


def dot_nt(a, b):
    return lax.dot_general(a, b, (((1,), (1,)), ((), ())), preferred_element_type=F32)


def dot_tn(a, b):
    return lax.dot_general(a, b, (((0,), (0,)), ((), ())), preferred_element_type=F32)


def params(**kw):
    return pltpu.CompilerParams(vmem_limit_bytes=VMEM_BYTES, **kw)


def rms_scale(value_rows):
    return lax.rsqrt(jnp.mean(value_rows * value_rows, axis=-1, keepdims=True) + EPS)


def plain_softmax(value_rows):
    top = jnp.max(value_rows, axis=-1, keepdims=True)
    expo = jnp.exp(value_rows - top)
    return expo / jnp.sum(expo, axis=-1, keepdims=True)


def rope_tables(length, size):
    half = size // 2
    freq = THETA ** (-2.0 * np.arange(half) / size)
    angle = np.arange(length)[:, None] * freq[None, :]
    cosine, sine = np.cos(angle), np.sin(angle)
    tables = (np.concatenate([cosine, cosine], axis=-1), np.concatenate([-sine, sine], axis=-1))
    return tuple(jnp.asarray(t, F32) for t in tables)


def turn(rows, cosine, sine):
    return rows * cosine + pltpu.roll(rows, rows.shape[-1] // 2, 1) * sine


def turn_back(rows, cosine, sine):
    return rows * cosine - pltpu.roll(rows, rows.shape[-1] // 2, 1) * sine


MESH = pl.DeviceIdType.MESH
ANY = pl.BlockSpec(memory_space=pl.ANY)
Z_AXIS = 4


def link_cost(us):
    return pl.CostEstimate(flops=0, bytes_accessed=int(us * 3.0e6), transcendentals=0)


def greet(partners):
    barrier = pltpu.get_barrier_semaphore()
    count = 0
    for there, device in partners:
        flag = jnp.asarray(there, jnp.int32)

        @pl.when(there)
        def _(device=device):
            pl.semaphore_signal(barrier, inc=1, device_id=device, device_id_type=MESH)

        count = count + flag
    pl.semaphore_wait(barrier, count)


def remote(src, dst, send, recv, device):
    return pltpu.make_async_remote_copy(
        src_ref=src, dst_ref=dst, send_sem=send, recv_sem=recv, device_id=device, device_id_type=MESH
    )


def ring_place():
    me = lax.axis_index("ep")
    z, y = me // 2, me % 2
    return me, z, y, {"ep": me + 2}, {"ep": me - 2}, {"ep": me + 1 - 2 * y}


def ring_pieces(ref, axis):
    unit = ref.shape[axis] // 16
    lead = (slice(None),) * axis
    return [
        ref.at[lead + (pl.ds(start * unit, count * unit),)]
        for start, count in ((0, 7), (7, 6), (13, 3))
    ]


class EpGather:
    def __init__(self, ins, outs, sems):
        self.ins, self.outs = ins, outs
        self.own_sem, self.up_send, self.up_recv, self.dn_send, self.dn_recv = sems[:5]
        self.y_send, self.y_recv = sems[5:]
        self.me, self.z, self.y, self.up, self.down, self.beside = ring_place()
        self.last = len(ins) - 1
        self.streams = [(a, a, self.y) for a in range(len(ins))]
        self.other = (self.last, len(ins), 1 - self.y)

    def partners(self):
        z = self.z
        return [(z < Z_AXIS - 1, self.up), (z > 0, self.down), (z >= 0, self.beside)]

    def block(self, a, zt, y):
        return self.outs[a].at[zt * 2 + y]

    def upward(self, src, stream, zt):
        a, i, y = stream
        return remote(src, self.block(a, zt, y), self.up_send.at[i, zt], self.up_recv.at[i, zt], self.up)

    def downward(self, src, stream, zt):
        a, i, y = stream
        return remote(src, self.block(a, zt, y), self.dn_send.at[i, zt], self.dn_recv.at[i, zt], self.down)

    def sideways(self, src, a, zt):
        return remote(
            src, self.block(a, zt, self.y), self.y_send.at[a, zt], self.y_recv.at[a, zt], self.beside
        )

    def both_ways(self, src, stream):
        z = self.z

        @pl.when(z < Z_AXIS - 1)
        def _():
            self.upward(src, stream, z).start()

        @pl.when(z > 0)
        def _():
            self.downward(src, stream, z).start()

    def start(self):
        self.sideways(self.ins[self.last], self.last, self.z).start()
        for stream in self.streams:
            a = stream[0]
            self.both_ways(self.ins[a], stream)
            if a != self.last:
                self.sideways(self.ins[a], a, self.z).start()
            pltpu.make_async_copy(self.ins[a], self.block(a, self.z, self.y), self.own_sem.at[a]).start()

    def cross(self):
        self.side_arrived(self.last, self.z)
        self.both_ways(self.block(self.last, self.z, 1 - self.y), self.other)

    def hop(self, d):
        z = self.z
        for stream in [self.other] + self.streams:
            a, _, y = stream

            @pl.when(z >= d)
            def _(a=a, y=y, stream=stream, zt=z - d):
                rows = self.block(a, zt, y)
                self.upward(rows, stream, zt).wait_recv()

                @pl.when(z < Z_AXIS - 1)
                def _():
                    self.upward(rows, stream, zt).start()

                if a != self.last:
                    self.sideways(rows, a, zt).start()

            @pl.when(z + d < Z_AXIS)
            def _(a=a, y=y, stream=stream, zt=z + d):
                rows = self.block(a, zt, y)
                self.downward(rows, stream, zt).wait_recv()

                @pl.when(z > 0)
                def _():
                    self.downward(rows, stream, zt).start()

                if a != self.last:
                    self.sideways(rows, a, zt).start()

    def own_done(self):
        for a, x in enumerate(self.ins):
            pltpu.make_async_copy(x, self.block(a, self.z, self.y), self.own_sem.at[a]).wait()

    def side_arrived(self, a, zt):
        rows = self.block(a, zt, 1 - self.y)
        remote(rows, rows, self.y_send.at[a, zt], self.y_recv.at[a, zt], self.beside).wait_recv()

    def side_done(self, zt):
        for a in range(self.last):
            self.side_arrived(a, zt)

    def sent(self):
        z = self.z
        self.sideways(self.block(self.last, z, self.y), self.last, z).wait_send()
        for stream in self.streams + [self.other]:
            a, _, y = stream
            for zt in range(Z_AXIS):
                src = self.block(a, zt, y)
                if a != self.last:
                    self.sideways(src, a, zt).wait_send()

                @pl.when((zt <= z) & (z < Z_AXIS - 1))
                def _(src=src, zt=zt, stream=stream):
                    self.upward(src, stream, zt).wait_send()

                @pl.when((zt >= z) & (z > 0))
                def _(src=src, zt=zt, stream=stream):
                    self.downward(src, stream, zt).wait_send()

    def finish(self):
        self.own_done()
        for zt in range(Z_AXIS):
            self.side_done(zt)
        self.sent()


def gather_sems():
    dma = pltpu.SemaphoreType.DMA
    return [dma((3,))] + [dma((4, Z_AXIS))] * 6


def one_hot(slots, capacity):
    local, rows = slots.shape
    slot = lax.broadcasted_iota(jnp.int32, (capacity, rows), 0)
    return [slot == slots[e : e + 1, :] for e in range(local)]


def gather_select_kernel(
    x_ref, cots_ref, slots_ref, picks_ref, router_ref, xs_ref, cs_ref, gate_ref,
    tokens, cots, chosen, load_sem, store_sem, *sems,
):
    local, _, capacity, width = xs_ref.shape
    blocks = tokens.shape[0]
    gather = EpGather(ring_pieces(x_ref, 0), ring_pieces(tokens, 1), sems)
    z, y = gather.z, gather.y
    greet(gather.partners())
    gather.start()

    def chosen_rows(j, rows):
        hits = one_hot(slots_ref[j], capacity)
        place = jnp.concatenate([h.astype(F32) for h in hits], axis=0).astype(BF)
        return dot_nn(place, rows).astype(BF).reshape(local, capacity, width), hits

    def load(j, slot):
        return pltpu.make_async_copy(cots_ref.at[j], cots.at[slot], load_sem.at[slot])

    def store(to, j, slot):
        return pltpu.make_async_copy(chosen.at[slot], to.at[:, j], store_sem.at[slot])

    load(0, 0).start()

    @pl.loop(0, blocks)
    def _(j):
        slot = lax.rem(j, 2)

        @pl.when(j + 1 < blocks)
        def _():
            load(j + 1, 1 - slot).start()

        load(j, slot).wait()

        @pl.when(j == 3)
        def _():
            gather.cross()

        @pl.when(j >= 2)
        def _():
            store(cs_ref, j - 2, slot).wait()

        chosen[slot] = chosen_rows(j, cots[slot])[0]
        store(cs_ref, j, slot).start()

    store(cs_ref, blocks - 2, 0).wait()
    store(cs_ref, blocks - 1, 1).wait()

    def take(j):
        rows = tokens[j]
        chosen[0], hits = chosen_rows(j, rows)
        copy = store(xs_ref, j, 0)
        copy.start()
        logits = dot_nt(router_ref[...], rows)
        picked = picks_ref[j] > 0
        kept = jnp.where(picked, logits, MASKED)
        expo = jnp.exp(kept - jnp.max(kept, axis=0, keepdims=True))
        expo = jnp.where(picked, expo, 0.0)
        gates = expo / jnp.sum(expo, axis=0, keepdims=True)
        for e, hit in enumerate(hits):
            gate_ref[e, j] = jnp.sum(jnp.where(hit, gates[e : e + 1, :], 0.0), axis=1, keepdims=True)
        copy.wait()

    gather.own_done()
    take(gather.me)
    for d in range(1, Z_AXIS + 1):
        if d < Z_AXIS:
            gather.hop(d)

        @pl.loop(0, 4)
        def _(i, d=d):
            beside = i >= 2
            far = jnp.where(beside, d - 1, d)
            zt = jnp.where(lax.rem(i, 2) == 0, z - far, z + far)
            there = (zt >= 0) & (zt < Z_AXIS) & ((i < 3) | (d > 1))

            @pl.when(there & beside)
            def _():
                gather.side_done(zt)

            @pl.when(there)
            def _():
                take(zt * 2 + jnp.where(beside, 1 - y, y))

    gather.sent()


def gather_select(rows, cot_all, slots, picks, router, capacity, number):
    ep_count = lax.axis_size("ep")
    _, local, block = slots.shape
    width = rows.shape[1]
    vmem = pl.BlockSpec(memory_space=pltpu.VMEM)
    dma = pltpu.SemaphoreType.DMA
    shape = (local, ep_count, capacity, width)
    return pl.pallas_call(
        gather_select_kernel,
        in_specs=[ANY, ANY, vmem, vmem, vmem],
        out_specs=[ANY, ANY, vmem],
        out_shape=[
            jax.ShapeDtypeStruct(shape, BF),
            jax.ShapeDtypeStruct(shape, BF),
            jax.ShapeDtypeStruct(shape[:3] + (1,), F32),
        ],
        scratch_shapes=[
            pltpu.VMEM((ep_count, block, width), BF),
            pltpu.VMEM((2, block, width), BF),
            pltpu.VMEM((2, local, capacity, width), BF),
            dma((2,)), dma((2,)),
        ]
        + gather_sems(),
        compiler_params=params(collective_id=number, has_side_effects=True),
        cost_estimate=link_cost(90.0),
        name="gather_select",
    )(rows, cot_all, slots, picks, router)


def add_rows(total, terms, chunk=16):
    @pl.loop(0, total.shape[0] // chunk)
    def _(i):
        rows = pl.ds(pl.multiple_of(i * chunk, chunk), chunk)
        value = terms[0][rows, :].astype(F32)
        for term in terms[1:]:
            value = value + term[rows, :].astype(F32)
        total[rows, :] = value.astype(total.dtype)


def scatter_order(z):
    table = ((3, 2, 1, 0), (3, 0, 2, 1), (0, 3, 1, 2), (0, 1, 2, 3))
    return [
        jnp.where(
            z == 0,
            table[0][k],
            jnp.where(z == 1, table[1][k], jnp.where(z == 2, table[2][k], table[3][k])),
        )
        for k in range(Z_AXIS)
    ]


class EpReduce:
    def __init__(self, ins, by_z, bufs, sems):
        self.ins, self.by_z = ins, by_z
        self.bufs = [bufs[2 * a : 2 * a + 2] for a in range(len(ins))]
        self.up_send, self.up_recv, self.dn_send, self.dn_recv, self.y_send, self.y_recv = sems
        self.me, self.z, self.y, self.up, self.down, self.beside = ring_place()
        self.order = scatter_order(self.z)
        self.streams = [(a, 0, self.y) for a in range(len(ins))]
        self.crossing = [(a, 1, 1 - self.y) for a in range(len(ins)) if by_z[a]]

    def partners(self):
        z = self.z
        return [(z < Z_AXIS - 1, self.up), (z > 0, self.down), (z >= 0, self.beside)]

    def mine(self, stream, zt):
        return self.ins[stream[0]].at[zt * 2 + stream[2]]

    def side(self, a, zt):
        return self.bufs[a][0].at[0 if self.by_z[a] else zt]

    def below(self, stream, zt):
        return self.bufs[stream[0]][1].at[stream[1] * (Z_AXIS + 1) + zt]

    def above(self, stream, zt, z):
        return self.below(stream, jnp.where(zt == z, Z_AXIS, zt))

    def to_side(self, a, zt):
        src = self.ins[a].at[zt * 2 + 1 - self.y]
        return remote(src, self.side(a, zt), self.y_send.at[a, zt], self.y_recv.at[a, zt], self.beside)

    def rising(self, stream, zt):
        i = 2 * stream[0] + stream[1]
        return remote(
            self.mine(stream, zt), self.below(stream, zt), self.up_send.at[i, zt], self.up_recv.at[i, zt], self.up
        )

    def falling(self, stream, zt):
        i = 2 * stream[0] + stream[1]
        return remote(
            self.mine(stream, zt), self.above(stream, zt, self.z - 1),
            self.dn_send.at[i, zt], self.dn_recv.at[i, zt], self.down,
        )

    def send_side(self, k):
        for a, by_z in enumerate(self.by_z):
            if not by_z:
                self.to_side(a, self.order[k]).start()

    def step_y(self, k):
        self.step(k, [s for s in self.streams if not self.by_z[s[0]]])

    def ends_y(self, k):
        @pl.when((self.z == 0) | (self.z == Z_AXIS - 1))
        def _():
            self.step_y(k)

    def middle_y(self, k):
        @pl.when((self.z > 0) & (self.z < Z_AXIS - 1))
        def _():
            self.step_y(k)

    def step_z(self, k):
        self.step(k, self.crossing + [s for s in self.streams if self.by_z[s[0]]])
        if k == Z_AXIS - 1:
            for stream in self.crossing:
                rows = self.mine(stream, self.z)
                self.gathered(stream, [rows], functools.partial(add_rows, rows))
                self.to_side(stream[0], self.z).start()

    def step(self, k, streams):
        z, zt, last = self.z, self.order[k], Z_AXIS - 1
        for stream in streams:
            a = stream[0]
            mine = self.mine(stream, zt)
            terms = [mine]
            if not self.by_z[a]:
                self.to_side(a, zt).wait_recv()
                terms = [mine, self.side(a, zt)]
                ends = ((zt > z) & (z == 0)) | ((zt < z) & (z == last))

                @pl.when(ends)
                def _(mine=mine, terms=terms):
                    add_rows(mine, terms)

            @pl.when((zt > z) & (z > 0))
            def _(stream=stream, mine=mine, terms=terms):
                self.rising(stream, zt).wait_recv()
                add_rows(mine, terms + [self.below(stream, zt)])

            @pl.when((zt < z) & (z < last))
            def _(stream=stream, mine=mine, terms=terms):
                self.falling(stream, zt).wait_recv()
                add_rows(mine, terms + [self.above(stream, zt, z)])

            @pl.when(zt > z)
            def _(stream=stream):
                self.rising(stream, zt).start()

            @pl.when(zt < z)
            def _(stream=stream):
                self.falling(stream, zt).start()

    def gathered(self, stream, terms, write):
        z, last = self.z, Z_AXIS - 1

        @pl.when(z > 0)
        def _():
            self.rising(stream, z).wait_recv()

        @pl.when(z < last)
        def _():
            self.falling(stream, z).wait_recv()

        @pl.when(z == 0)
        def _():
            write(terms + [self.above(stream, z, z)])

        @pl.when(z == last)
        def _():
            write(terms + [self.below(stream, z)])

        @pl.when((z > 0) & (z < last))
        def _():
            write(terms + [self.below(stream, z), self.above(stream, z, z)])

    def own(self, a, write):
        if self.by_z[a]:
            self.to_side(a, self.z).wait_recv()
        stream = self.streams[a]
        self.gathered(stream, [self.mine(stream, self.z), self.side(a, self.z)], write)

    def sent(self):
        z = self.z
        for stream in self.streams + self.crossing:
            a = stream[0]
            for zt in range(Z_AXIS):
                if not self.by_z[a]:
                    self.to_side(a, zt).wait_send()

                @pl.when(zt > z)
                def _(stream=stream, zt=zt):
                    self.rising(stream, zt).wait_send()

                @pl.when(zt < z)
                def _(stream=stream, zt=zt):
                    self.falling(stream, zt).wait_send()

        for stream in self.crossing:
            self.to_side(stream[0], z).wait_send()


def reduce_scratch(rows, columns):
    unit = rows // 16
    out = []
    for count, slots in ((7, (Z_AXIS, Z_AXIS + 1)), (6, (Z_AXIS, Z_AXIS + 1)), (3, (1, 2 * (Z_AXIS + 1)))):
        out += [pltpu.VMEM((n, count * unit, columns), BF) for n in slots]
    return out


BY_Z = [False, False, True]


def reduce_sems(count):
    dma = pltpu.SemaphoreType.DMA
    return [dma((2 * count, Z_AXIS))] * 4 + [dma((count, Z_AXIS))] * 2


def widen_kernel(a_ref, b_ref, gate_ref, up_ref, down_ref):
    for kind, out in enumerate((gate_ref, up_ref, down_ref)):
        for half, ref in enumerate((a_ref, b_ref)):

            @pl.when(pl.program_id(0) == half)
            def _(kind=kind, out=out, ref=ref):
                out[...] = ref[kind].astype(F32)


def widen_grads(a, b):
    _, pair, hidden, width = a.shape
    shape = jax.ShapeDtypeStruct((2 * pair, hidden, width), F32)
    tile = width // 2
    return pl.pallas_call(
        widen_kernel,
        grid=(2, pair, 2),
        in_specs=[
            pl.BlockSpec(
                (3, 1, hidden, tile),
                lambda h, e, i: (0, jnp.where(h == 0, e, pair - 1), 0, jnp.where(h == 0, i, 1)),
            ),
            pl.BlockSpec(
                (3, 1, hidden, tile),
                lambda h, e, i: (0, jnp.where(h == 0, 0, e), 0, jnp.where(h == 0, 0, i)),
            ),
        ],
        out_specs=[pl.BlockSpec((1, hidden, tile), lambda h, e, i: (h * pair + e, 0, i))] * 3,
        out_shape=[shape] * 3,
        compiler_params=params(),
        name="widen_grads",
    )(a, b)


def token_hits(slots, capacity):
    rows, local = slots.shape
    lane = lax.broadcasted_iota(jnp.int32, (rows, local * capacity), 1)
    return [lane == slots[:, e : e + 1] + e * capacity for e in range(local)]


class SlotSums:
    def __init__(self, slots, first, second, buf, sem):
        self.slots, self.pair, self.buf, self.sem = slots, (first, second), buf, sem
        self.capacity = first.shape[2]

    def copies(self, j, at):
        n = self.pair[0].shape[0]
        return [
            pltpu.make_async_copy(
                ref.at[:, j], self.buf.at[at, pl.ds(i * n, n)], self.sem.at[at, i]
            )
            for i, ref in enumerate(self.pair)
        ]

    def fetch(self, j, at):
        for copy in self.copies(j, at):
            copy.start()

    def add(self, j, at, out):
        for copy in self.copies(j, at):
            copy.wait()
        place = jnp.zeros((), F32)
        for hit in token_hits(self.slots[j], self.capacity):
            place = jnp.where(hit, 1.0, place)
        rows = self.buf[at].reshape(-1, out.shape[1])
        out[...] = dot_nn(place.astype(BF), rows).astype(BF)

    def run(self, blocks, out, then):
        self.fetch(blocks[0], 0)
        for n, j in enumerate(blocks):
            if n + 1 < len(blocks):
                self.fetch(blocks[n + 1], (n + 1) % 2)
            self.add(j, n % 2, out.at[j])
            then(n)


def slot_sums_scratch(local, capacity, width):
    return [
        pltpu.VMEM((2, local, capacity, width), BF),
        pltpu.SemaphoreType.DMA((2, 2)),
    ]


def input_grads_kernel(
    slots, dgate, dx_a, dx_b, xs, cs, act, d_gate, d_up,
    residual, moe_in, cot, route_gain, gate_dense, probs, coeff, router,
    d_hidden, d_rows, router_part, gain_part, grads,
    out, gate_out, part, gates, buf, sem, x_in, c_in, h_in, w_buf, in_sem, w_sem, *refs,
):
    sums = SlotSums(slots, dx_a, dx_b, buf, sem)
    reduce = EpReduce(ring_pieces(part, 1) + [gates], BY_Z + [False], refs[:8], refs[8:])
    order, y = reduce.order, reduce.y
    pair, number, inner = act.shape
    parts, _, _, hidden, width = grads.shape
    first = xs.shape[0] - pair
    pieces = width // x_in.shape[1]
    wide = x_in.shape[1]
    greet(reduce.partners())

    def cols(piece):
        return pl.ds(piece * wide, wide)

    def wide_copies(unit):
        e, piece = unit // pieces, unit % pieces
        return [
            pltpu.make_async_copy(xs.at[first + e, :, cols(piece)], x_in, in_sem.at[0]),
            pltpu.make_async_copy(cs.at[first + e, :, cols(piece)], c_in, in_sem.at[1]),
        ]

    def inner_copies(e):
        return [
            pltpu.make_async_copy(ref.at[e], h_in.at[kind], in_sem.at[2 + kind])
            for kind, ref in enumerate((d_gate, d_up, act))
        ]

    def written(unit):
        e, piece = unit // pieces, unit % pieces
        return pltpu.make_async_copy(w_buf, grads.at[:, :, e, :, cols(piece)], w_sem)

    def prepare(unit):
        for copy in wide_copies(unit) + (inner_copies(unit // pieces) if unit % pieces == 0 else []):
            copy.start()

    def weights(unit):
        for copy in wide_copies(unit) + (inner_copies(unit // pieces) if unit % pieces == 0 else []):
            copy.wait()
        if unit > 0:
            written(unit - 1).wait()
        for kind, right in enumerate((x_in, x_in, c_in)):
            grad = dot_tn(h_in[kind], right[...]).astype(BF)
            w_buf[:, kind] = grad.reshape(parts, hidden, wide)
        written(unit).start()
        if unit + 1 < pair * pieces:
            prepare(unit + 1)

    def payload(j):
        lanes = gates.shape[2]
        column = lax.broadcasted_iota(jnp.int32, (gates.shape[1], lanes), 1)
        pay = jnp.zeros(column.shape, F32)
        mine = reduce.me * slots.shape[2]
        for e, hit in enumerate(token_hits(slots[j], sums.capacity)):
            value = jnp.sum(jnp.where(hit, dgate[j], 0.0), axis=1, keepdims=True)
            high = value.astype(BF).astype(F32)
            pay = jnp.where(column == mine + e, high, pay)
            pay = jnp.where(column == mine + e + lanes // 2, value - high, pay)
        gates[j] = pay.astype(BF)

    def send(k):
        payload(order[k] * 2 + 1 - y)
        reduce.send_side(k)

    units = pair * pieces
    quarter = [range(units * k // Z_AXIS, units * (k + 1) // Z_AXIS) for k in range(Z_AXIS)]
    sums.run([order[k] * 2 + 1 - y for k in range(Z_AXIS)], part, send)
    prepare(0)
    sums.run(
        [order[k] * 2 + y for k in range(Z_AXIS)], part, lambda k: payload(order[k] * 2 + y)
    )
    reduce.step_z(0)
    reduce.ends_y(0)
    reduce.step_z(1)
    for k in range(Z_AXIS):
        for unit in quarter[k]:
            weights(unit)
        if k == 1:
            reduce.ends_y(1)
            reduce.middle_y(0)
            reduce.step_z(2)
            reduce.step_z(3)
        elif k == 2:
            reduce.ends_y(2)
    reduce.middle_y(1)
    reduce.middle_y(2)
    reduce.step_y(3)
    for a, rows in enumerate(ring_pieces(out, 0) + [gate_out]):
        reduce.own(a, functools.partial(add_rows, rows))

    experts, lanes = gate_dense.shape[1], gates.shape[2]
    d_gates = gate_out[:, 0:experts] + gate_out[:, lanes // 2 : lanes // 2 + experts]
    gate, prob = gate_dense[...], probs[...]
    d_logits = gate * (d_gates - jnp.sum(gate * d_gates, axis=-1, keepdims=True))
    d_logits = d_logits + prob * (coeff[...] - jnp.sum(prob * coeff[...], axis=-1, keepdims=True))
    d_low = d_logits.astype(BF)
    router_part[...] = dot_tn(d_low, moe_in[...])
    out[...] += dot_nn(d_low, router[...])
    gain_part[...] = jnp.zeros_like(gain_part)
    chunk = 16

    @pl.loop(0, out.shape[0] // chunk)
    def _(i):
        lines = pl.ds(pl.multiple_of(i * chunk, chunk), chunk)
        back, gain_rows = norm_back(out[lines, :], residual[lines, :], route_gain[...])
        total = back + cot[lines, :].astype(F32)
        d_hidden[lines, :] = total
        d_rows[lines, :] = total.astype(BF)
        gain_part[...] += gain_rows

    reduce.sent()
    written(units - 1).wait()


def input_grads(slots_t, dgate, dx, x_slots, c_slots, inner, row_values, experts, tp_count, number):
    ep_count, rows, local = slots_t.shape
    pair, _, capacity, width = dx[0].shape
    count, hidden = inner[0].shape[1:]
    lanes = -(-2 * experts // 128) * 128
    wide = width // 2
    dma = pltpu.SemaphoreType.DMA
    vmem = pl.BlockSpec(memory_space=pltpu.VMEM)
    return pl.pallas_call(
        input_grads_kernel,
        in_specs=[vmem, vmem] + [ANY] * 7 + [vmem] * 8,
        out_specs=[vmem] * 4 + [ANY],
        out_shape=[
            jax.ShapeDtypeStruct((rows, width), F32),
            jax.ShapeDtypeStruct((rows, width), BF),
            jax.ShapeDtypeStruct((experts, width), F32),
            jax.ShapeDtypeStruct((1, width), F32),
            jax.ShapeDtypeStruct((tp_count, 3, pair, hidden // tp_count, width), BF),
        ],
        scratch_shapes=[
            pltpu.VMEM((rows, width), F32),
            pltpu.VMEM((rows, lanes), F32),
            pltpu.VMEM((ep_count, rows, width), BF),
            pltpu.VMEM((ep_count, rows, lanes), BF),
        ]
        + slot_sums_scratch(local, capacity, width)
        + [
            pltpu.VMEM((count, wide), BF),
            pltpu.VMEM((count, wide), BF),
            pltpu.VMEM((3, count, hidden), BF),
            pltpu.VMEM((tp_count, 3, hidden // tp_count, wide), BF),
            dma((5,)), dma,
        ]
        + reduce_scratch(rows, width)
        + [pltpu.VMEM((n, rows, lanes), BF) for n in (Z_AXIS, Z_AXIS + 1)]
        + reduce_sems(4),
        compiler_params=params(collective_id=number, has_side_effects=True),
        cost_estimate=link_cost(100.0),
        name="input_grads",
    )(slots_t, dgate, *dx, x_slots, c_slots, *inner, *row_values)


class Exchange:
    def __init__(self, axis, send, recv):
        self.axis, self.send, self.recv = axis, send, recv
        self.count, self.me = lax.axis_size(axis), lax.axis_index(axis)

    def each(self, act):
        for i in range(1, self.count):
            act(i, lax.rem(self.me + i, self.count))

    def to(self, src, dst, i, other):
        return remote(src, dst, self.send.at[i], self.recv.at[self.me], {self.axis: other})

    def start(self, src_of, dst):
        self.each(lambda i, other: self.to(src_of(other), dst.at[self.me], i, other).start())

    def arrived(self, dst):
        self.each(
            lambda i, other: remote(
                dst.at[other], dst.at[other], self.send.at[i], self.recv.at[other], {self.axis: other}
            ).wait_recv()
        )

    def sent(self, src_of, dst):
        self.each(lambda i, other: self.to(src_of(other), dst.at[self.me], i, other).wait_send())


class SumAll:
    def __init__(self, x, out, over_tp, own_tp, over_ep, own, ring, sems):
        self.x, self.out, self.over_tp, self.own_tp = x, out, over_tp, own_tp
        self.over_ep, self.own, self.ring = over_ep, own, ring
        self.first = Exchange("tp", sems[0], sems[1])
        self.second = Exchange("ep", sems[2], sems[3])
        self.third = Exchange("ep", sems[4], sems[5])
        self.fourth = Exchange("tp", sems[6], sems[7])

    def slice_tp(self, t):
        return self.x.at[t]

    def slice_ep(self, e):
        return self.own_tp.at[e]

    def start(self):
        self.first.start(self.slice_tp, self.over_tp)
        me = self.first.me
        self.over_tp[pl.ds(me, 1)] = self.x[pl.ds(me, 1)]

    def across(self):
        self.first.arrived(self.over_tp)
        self.own_tp[...] = jnp.sum(self.over_tp[...], axis=0)
        self.second.start(self.slice_ep, self.over_ep)
        me = self.second.me
        self.over_ep[pl.ds(me, 1)] = self.own_tp[pl.ds(me, 1)]

    def back(self):
        self.second.arrived(self.over_ep)
        self.own[...] = jnp.sum(self.over_ep[...], axis=0)
        self.third.start(lambda e: self.own, self.ring)
        self.ring[pl.ds(self.third.me, 1)] = self.own[...][None]

    def home(self):
        self.third.arrived(self.ring)
        self.fourth.start(lambda t: self.ring, self.out)
        self.out[pl.ds(self.fourth.me, 1)] = self.ring[...][None]

    def finish(self):
        self.fourth.arrived(self.out)
        self.first.sent(self.slice_tp, self.over_tp)
        self.second.sent(self.slice_ep, self.over_ep)
        self.third.sent(lambda e: self.own, self.ring)
        self.fourth.sent(lambda t: self.ring, self.out)


def exchange_sems(axis):
    return [pltpu.SemaphoreType.DMA((lax.axis_size(axis),))] * 2


def sum_scratch(shape):
    tp, ep, rows, lanes = shape
    return [
        pltpu.VMEM(shape, F32), pltpu.VMEM((ep, rows, lanes), F32), pltpu.VMEM((ep, rows, lanes), F32),
        pltpu.VMEM((rows, lanes), F32), pltpu.VMEM((ep, rows, lanes), F32),
    ] + [sem for axis in ("tp", "ep", "ep", "tp") for sem in exchange_sems(axis)]


def pack_small(values, tp, ep):
    total = tp * ep
    flat = jnp.concatenate([v.reshape(-1) for v in values])
    rows = -(-flat.shape[0] // (total * 128 * 8)) * 8
    return jnp.pad(flat, (0, total * rows * 128 - flat.shape[0])).reshape(tp, ep, rows, 128)


def unpack_small(summed, values):
    summed = summed.reshape(-1)
    out, at = [], 0
    for v in values:
        out.append(summed[at : at + v.size].reshape(v.shape))
        at += v.size
    return out


def project_kernel(x_ref, gain_ref, wq_ref, wk_ref, wv_ref, normed_ref, q_ref, k_ref, v_ref):
    x = x_ref[...].astype(F32)
    normed = (x * rms_scale(x) * gain_ref[...]).astype(BF)
    normed_ref[...] = normed
    q_ref[...] = dot_nn(normed, wq_ref[...])
    k_ref[...] = dot_nn(normed, wk_ref[...])
    v_ref[...] = dot_nn(normed, wv_ref[...]).astype(BF)


def project(inputs, gain, wq, wk, wv):
    length, width = inputs.shape
    tile = min(256, length)

    def rows(columns):
        return pl.BlockSpec((tile, columns), lambda i: (i, 0))

    def fixed(array):
        return pl.BlockSpec(array.shape, lambda i: (0, 0), pipeline_mode=pl.Buffered(1))

    return pl.pallas_call(
        project_kernel,
        grid=(length // tile,),
        in_specs=[rows(width), fixed(gain), fixed(wq), fixed(wk), fixed(wv)],
        out_specs=[rows(width), rows(wq.shape[1]), rows(wk.shape[1]), rows(wv.shape[1])],
        out_shape=[
            jax.ShapeDtypeStruct((length, width), BF),
            jax.ShapeDtypeStruct((length, wq.shape[1]), F32),
            jax.ShapeDtypeStruct((length, wk.shape[1]), F32),
            jax.ShapeDtypeStruct((length, wv.shape[1]), BF),
        ],
        compiler_params=params(),
        name="project",
    )(inputs, gain, wq, wk, wv)


def fill_bias(span_ref, bias, chunk=256):
    keys, length = bias.shape
    query = lax.broadcasted_iota(jnp.int32, (1, length), 1)

    def spans(pos):
        first = (pos >= span_ref[0, 0]) & (pos < span_ref[0, 0] + IMG)
        second = (pos >= span_ref[0, 1]) & (pos < span_ref[0, 1] + IMG)
        return jnp.where(first, 0, jnp.where(second, 1, -1))

    query_span = spans(query)
    query_other = jnp.where(query_span < 0, -2, query_span)
    for start in range(0, keys, chunk):
        key = start + lax.broadcasted_iota(jnp.int32, (chunk, 1), 0)
        ok = (key <= query) | (spans(key) == query_other)
        bias[start : start + chunk, :] = jnp.where(ok, 0.0, MASKED)


def query_tiles(length):
    tile = min(IMG, length)
    return [
        (start, tile, min(length, start + tile + -(-IMG // tile) * tile))
        for start in range(0, length, tile)
    ]


def attention_kernel(
    span_ref, q_ref, k_ref, v_ref, cos_ref, sin_ref, qg_ref, kg_ref, w_out_ref, cot_ref, x_ref, gain_ref, wg_ref, wu_ref, wd_ref,
    out_ref, lse_ref, rows_ref, moe_ref, cots_ref, pack_ref,
    bias, k_rot, v_t, heads, part, core_rows, x_rows, core_send, core_recv, x_send, x_recv, pack_sem, *sems,
):
    factor = q_ref.shape[-1] ** (-0.5)
    cosine, sine = cos_ref[...], sin_ref[...]
    step = pl.program_id(0)
    size = q_ref.shape[-1]
    me = lax.axis_index("tp")
    x, c = me // 2, me % 2
    other_core, other_x = {"tp": x * 2 + 1 - c}, {"tp": (1 - x) * 2 + c}
    gather = EpGather(ring_pieces(cot_ref, 0), ring_pieces(cots_ref, 1), sems)
    pair = pack_ref.shape[1]
    packing = [
        pltpu.make_async_copy(ref.at[pl.ds(ref.shape[0] - pair, pair)], pack_ref.at[kind], pack_sem.at[kind])
        for kind, ref in enumerate((wg_ref, wu_ref, wd_ref))
    ]

    @pl.when(step == 0)
    def _():
        greet(gather.partners() + [(x >= 0, other_core), (x >= 0, other_x)])
        gather.start()
        for copy in packing:
            copy.start()
        fill_bias(span_ref, bias)
        k = k_ref[...]
        k_rot[...] = turn(k * rms_scale(k) * kg_ref[...], cosine, sine).astype(BF)
        v_t[...] = v_ref[...].astype(F32).T.astype(BF)

    @pl.when(step == 2)
    def _():
        gather.cross()

    @pl.when(step == pl.num_programs(0) - 2)
    def _():
        gather.hop(1)

    q = q_ref[...]
    q_rot = turn(q * rms_scale(q) * qg_ref[...], cosine, sine).astype(BF)
    for start, tile, keys in query_tiles(q.shape[0]):
        cols = slice(start, start + tile)
        s = dot_nt(k_rot[:keys, :], q_rot[cols, :]) * factor + bias[:keys, cols]
        top = jnp.max(s, axis=0, keepdims=True)
        p = jnp.exp(s - top)
        total = jnp.sum(p, axis=0, keepdims=True)
        o_t = dot_nn(v_t[:, :keys], p.astype(BF)) / total
        rows = o_t.T.astype(BF)
        out_ref[cols, :] = rows
        heads[step, cols, :] = rows
        lse_ref[0, :, cols] = top + jnp.log(total)

    @pl.when(step == pl.num_programs(0) - 1)
    def _():
        count = heads.shape[0]
        block = rows_ref.shape[0]

        def project(tp):
            lines = pl.ds(pl.multiple_of(tp * block, block), block)
            rows = jnp.concatenate([heads[h, lines, :] for h in range(count)], axis=1)
            part[tp] = dot_nn(rows, w_out_ref[...]).astype(BF)

        def to_core(xt):
            return remote(
                part.at[xt * 2 + 1 - c], core_rows.at[xt],
                core_send.at[xt], core_recv.at[xt], other_core,
            )

        far, near = part.at[(1 - x) * 2 + c], part.at[x * 2 + c]
        to_x = remote(far, x_rows, x_send, x_recv, other_x)
        project((1 - x) * 2 + 1 - c)
        to_core(1 - x).start()
        project((1 - x) * 2 + c)
        to_core(1 - x).wait_recv()
        add_rows(far, [far, core_rows.at[1 - x]])
        to_x.start()
        project(x * 2 + 1 - c)
        to_core(x).start()
        project(x * 2 + c)
        gather.hop(2)
        to_core(x).wait_recv()
        gather.hop(3)
        to_x.wait_recv()
        chunk = 16

        @pl.loop(0, block // chunk)
        def _(i):
            lines = pl.ds(pl.multiple_of(i * chunk, chunk), chunk)
            total = near[lines, :].astype(F32) + core_rows[x, lines, :].astype(F32)
            hidden = x_ref[lines, :].astype(F32) + (total + x_rows[lines, :].astype(F32))
            rows_ref[lines, :] = hidden
            moe_ref[lines, :] = (hidden * rms_scale(hidden) * gain_ref[...]).astype(BF)

        gather.finish()
        for copy in packing:
            copy.wait()
        to_core(1 - x).wait_send()
        to_core(x).wait_send()
        to_x.wait_send()


def plain_attention_kernel(
    span_ref, q_ref, k_ref, v_ref, cos_ref, sin_ref, qg_ref, kg_ref, out_ref, lse_ref,
    bias, k_rot, v_t,
):
    factor = q_ref.shape[-1] ** (-0.5)
    cosine, sine = cos_ref[...], sin_ref[...]

    @pl.when(pl.program_id(0) == 0)
    def _():
        fill_bias(span_ref, bias)
        k = k_ref[...]
        k_rot[...] = turn(k * rms_scale(k) * kg_ref[...], cosine, sine).astype(BF)
        v_t[...] = v_ref[...].astype(F32).T.astype(BF)

    q = q_ref[...]
    q_rot = turn(q * rms_scale(q) * qg_ref[...], cosine, sine).astype(BF)
    for start, tile, keys in query_tiles(q.shape[0]):
        cols = slice(start, start + tile)
        s = dot_nt(k_rot[:keys, :], q_rot[cols, :]) * factor + bias[:keys, cols]
        top = jnp.max(s, axis=0, keepdims=True)
        p = jnp.exp(s - top)
        total = jnp.sum(p, axis=0, keepdims=True)
        o_t = dot_nn(v_t[:, :keys], p.astype(BF)) / total
        out_ref[cols, :] = o_t.T.astype(BF)
        lse_ref[0, :, cols] = top + jnp.log(total)


def attention(span, q, k, v, cosine, sine, q_gain, k_gain, w_out, cotangent, x_rows, route_gain, weights, pair, number):
    length, size = k.shape
    heads = q.shape[1] // size
    whole = pl.BlockSpec((length, size), lambda h: (0, 0))
    head = pl.BlockSpec((length, size), lambda h: (0, h))
    gain = pl.BlockSpec((1, size), lambda h: (0, 0))
    in_specs = [
        pl.BlockSpec(memory_space=pltpu.SMEM), head, whole, whole, whole, whole, gain, gain,
    ]
    out_specs = [head, pl.BlockSpec((1, 1, length), lambda h: (h, 0, 0))]
    out_shape = [
        jax.ShapeDtypeStruct((length, heads * size), BF),
        jax.ShapeDtypeStruct((heads, 1, length), F32),
    ]
    scratch = [
        pltpu.VMEM((length, length), F32),
        pltpu.VMEM((length, size), BF),
        pltpu.VMEM((size, length), BF),
    ]
    args = (span, q, k, v, cosine, sine, q_gain, k_gain)
    ep_count, tp_count = lax.axis_size("ep"), lax.axis_size("tp")
    if ep_count != 2 * Z_AXIS:
        out, lse = pl.pallas_call(
            plain_attention_kernel,
            grid=(heads,),
            in_specs=in_specs,
            out_specs=out_specs,
            out_shape=out_shape,
            scratch_shapes=scratch,
            compiler_params=params(),
            name="plain_attention",
        )(*args)
        rows = lax.psum_scatter(
            dot_nn(out, w_out).astype(BF), "tp", scatter_dimension=0, tiled=True
        )
        hidden = x_rows.astype(F32) + rows.astype(F32)
        moe_in = (hidden * rms_scale(hidden) * route_gain).astype(BF)
        packed = pack_weights(weights, weights[0].shape[0] - pair, pair)
        return out, lse, hidden, moe_in, lax.all_gather(cotangent, "ep"), packed
    block, width = cotangent.shape
    dma = pltpu.SemaphoreType.DMA
    return pl.pallas_call(
        attention_kernel,
        grid=(heads,),
        in_specs=in_specs
        + [
            pl.BlockSpec(w_out.shape, lambda h: (0, 0), pipeline_mode=pl.Buffered(1)), ANY,
            pl.BlockSpec((block, width), lambda h: (0, 0)),
            pl.BlockSpec((1, width), lambda h: (0, 0)), ANY, ANY, ANY,
        ],
        out_specs=out_specs + [pl.BlockSpec((block, width), lambda h: (0, 0))] * 2 + [ANY] * 2,
        out_shape=out_shape
        + [
            jax.ShapeDtypeStruct((block, width), F32),
            jax.ShapeDtypeStruct((block, width), BF),
            jax.ShapeDtypeStruct((ep_count, block, width), BF),
            jax.ShapeDtypeStruct((3, pair) + weights[0].shape[1:], BF),
        ],
        scratch_shapes=scratch
        + [
            pltpu.VMEM((heads, length, size), BF),
            pltpu.VMEM((tp_count, block, width), BF),
            pltpu.VMEM((2, block, width), BF),
            pltpu.VMEM((block, width), BF),
            dma((2,)), dma((2,)), dma, dma, dma((3,)),
        ]
        + gather_sems(),
        compiler_params=params(collective_id=number, has_side_effects=True),
        cost_estimate=link_cost(90.0),
        name="attention",
    )(*args, w_out, cotangent, x_rows, route_gain, *weights)


def norm_back(grads, rows, gain):
    scale = rms_scale(rows)
    gain_part = jnp.sum(grads * rows * scale, axis=0, keepdims=True)
    inner = grads * gain
    mean = jnp.mean(inner * rows, axis=-1, keepdims=True)
    return scale * inner - rows * (scale * scale * scale * mean), gain_part


def plain_attention_back_kernel(
    span_ref, q_ref, k_ref, v_ref, grad_ref, lse_ref, cos_ref, sin_ref, qg_ref, kg_ref,
    dq_ref, dk_ref, dv_ref, dqg_ref, dkg_ref,
    bias, k_rot, k_t, dk_acc, dv_acc, dq_t,
):
    factor = q_ref.shape[-1] ** (-0.5)
    cosine, sine = cos_ref[...], sin_ref[...]
    step = pl.program_id(0)

    @pl.when(step == 0)
    def _():
        fill_bias(span_ref, bias)
        k = k_ref[...]
        rotated = turn(k * rms_scale(k) * kg_ref[...], cosine, sine)
        k_rot[...] = rotated.astype(BF)
        k_t[...] = rotated.T.astype(BF)
        dk_acc[...] = jnp.zeros_like(dk_acc)
        dv_acc[...] = jnp.zeros_like(dv_acc)
        dqg_ref[...] = jnp.zeros_like(dqg_ref)

    q = q_ref[...]
    q_rot = turn(q * rms_scale(q) * qg_ref[...], cosine, sine).astype(BF)
    for start, tile, keys in query_tiles(q.shape[0]):
        cols = slice(start, start + tile)
        s = dot_nt(k_rot[:keys, :], q_rot[cols, :]) * factor + bias[:keys, cols]
        p = jnp.exp(s - lse_ref[0, :, cols])
        grad = grad_ref[cols, :]
        dp = dot_nt(v_ref[:keys, :], grad)
        mean = jnp.sum(p * dp, axis=0, keepdims=True)
        raw = (p * (dp - mean) * factor).astype(BF)
        dq_t[:, cols] = dot_nn(k_t[:, :keys], raw)
        dk_acc[:keys, :] += dot_nn(raw, q_rot[cols, :])
        dv_acc[:keys, :] += dot_nn(p.astype(BF), grad)
    back, gain_part = norm_back(turn_back(dq_t[...].T, cosine, sine), q, qg_ref[...])
    dq_ref[...] = back.astype(BF)
    dqg_ref[...] += gain_part

    @pl.when(step == pl.num_programs(0) - 1)
    def _():
        back, gain_part = norm_back(turn_back(dk_acc[...], cosine, sine), k_ref[...], kg_ref[...])
        dk_ref[...] = back.astype(BF)
        dkg_ref[...] = gain_part
        dv_ref[...] = dv_acc[...].astype(BF)


def plain_attention_back(span, q, k, v, grads, lse, cosine, sine, q_gain, k_gain):
    length, size = k.shape
    heads = q.shape[1] // size
    whole = pl.BlockSpec((length, size), lambda h: (0, 0))
    head = pl.BlockSpec((length, size), lambda h: (0, h))
    gain = pl.BlockSpec((1, size), lambda h: (0, 0))
    return pl.pallas_call(
        plain_attention_back_kernel,
        grid=(heads,),
        in_specs=[
            pl.BlockSpec(memory_space=pltpu.SMEM), head, whole, whole, head,
            pl.BlockSpec((1, 1, length), lambda h: (h, 0, 0)), whole, whole, gain, gain,
        ],
        out_specs=[head, whole, whole, gain, gain],
        out_shape=[
            jax.ShapeDtypeStruct((length, heads * size), BF),
            jax.ShapeDtypeStruct((length, size), BF),
            jax.ShapeDtypeStruct((length, size), BF),
            jax.ShapeDtypeStruct((1, size), F32),
            jax.ShapeDtypeStruct((1, size), F32),
        ],
        scratch_shapes=[
            pltpu.VMEM((length, length), F32),
            pltpu.VMEM((length, size), BF),
            pltpu.VMEM((size, length), BF),
            pltpu.VMEM((length, size), F32),
            pltpu.VMEM((length, size), F32),
            pltpu.VMEM((size, length), F32),
        ],
        compiler_params=params(),
        name="plain_attention_back",
    )(span, q, k, v, grads, lse, cosine, sine, q_gain, k_gain)


def attention_back_kernel(
    span_ref, q_ref, k_ref, v_ref, lse_ref, cos_ref, sin_ref, qg_ref, kg_ref,
    w_out_ref, rows_ref, slots_ref, out_a, out_b, hidden_ref,
    dq_ref, dk_ref, dv_ref, dqg_ref, dkg_ref, branch_ref, output_ref,
    bias, k_rot, k_t, dk_acc, dv_acc, dq_t, branch, grads, part, buf, sem,
    own_sem, out_sem, core_send, core_recv, x_send, x_recv, *refs,
):
    factor = q_ref.shape[-1] ** (-0.5)
    size = q_ref.shape[-1]
    cosine, sine = cos_ref[...], sin_ref[...]
    step = pl.program_id(0)
    me = lax.axis_index("tp")
    x, c = me // 2, me % 2
    other_core, other_x = {"tp": x * 2 + 1 - c}, {"tp": (1 - x) * 2 + c}
    reduce = EpReduce(ring_pieces(part, 1), BY_Z, refs[:6], refs[6:])
    sums = SlotSums(slots_ref, out_a, out_b, buf, sem)
    order, y = reduce.order, reduce.y
    block = rows_ref.shape[0]
    near_other, far, far_other = x * 2 + 1 - c, (1 - x) * 2 + c, (1 - x) * 2 + 1 - c

    def to_core(slot, src, tp):
        return remote(src, branch.at[tp], core_send.at[slot], core_recv.at[slot], other_core)

    def to_x(tp):
        return remote(rows_ref, branch.at[tp], x_send, x_recv, other_x)

    def own_rows():
        return pltpu.make_async_copy(rows_ref, branch.at[me], own_sem)

    def whole_branch():
        return pltpu.make_async_copy(branch, branch_ref, out_sem)

    @pl.when(step == 0)
    def _():
        greet(reduce.partners() + [(x >= 0, other_core), (x >= 0, other_x)])
        to_x(me).start()
        to_core(0, rows_ref, me).start()
        own_rows().start()
        sums.run([order[k] * 2 + 1 - y for k in range(Z_AXIS)], part, reduce.send_side)
        fill_bias(span_ref, bias)
        k = k_ref[...]
        rotated = turn(k * rms_scale(k) * kg_ref[...], cosine, sine)
        k_rot[...] = rotated.astype(BF)
        k_t[...] = rotated.T.astype(BF)
        dk_acc[...] = jnp.zeros_like(dk_acc)
        dv_acc[...] = jnp.zeros_like(dv_acc)
        dqg_ref[...] = jnp.zeros_like(dqg_ref)

        def head_grads(tp):
            lines = pl.ds(pl.multiple_of(tp * block, block), block)
            rows = dot_nt(branch[tp], w_out_ref[...]).astype(BF)
            for h in range(grads.shape[0]):
                grads[h, lines, :] = rows[:, h * size : (h + 1) * size]

        own_rows().wait()
        head_grads(me)
        to_core(0, rows_ref, near_other).wait_recv()
        head_grads(near_other)
        sums.run([order[k] * 2 + y for k in range(Z_AXIS)], part, lambda k: None)
        reduce.step_z(0)
        reduce.ends_y(0)
        reduce.step_z(1)
        to_x(far).wait_recv()
        to_core(1, branch.at[far], far).start()
        head_grads(far)
        to_core(1, branch.at[far], far_other).wait_recv()
        head_grads(far_other)
        whole_branch().start()
        reduce.ends_y(1)
        reduce.middle_y(0)

    @pl.when(step == 1)
    def _():
        reduce.step_z(2)
        reduce.step_z(3)

    @pl.when(step == 4)
    def _():
        reduce.ends_y(2)

    @pl.when(step == 6)
    def _():
        reduce.middle_y(1)

    q = q_ref[...]
    q_rot = turn(q * rms_scale(q) * qg_ref[...], cosine, sine).astype(BF)
    for start, tile, keys in query_tiles(q.shape[0]):
        cols = slice(start, start + tile)
        s = dot_nt(k_rot[:keys, :], q_rot[cols, :]) * factor + bias[:keys, cols]
        p = jnp.exp(s - lse_ref[0, :, cols])
        grad = grads[step, cols, :]
        dp = dot_nt(v_ref[:keys, :], grad)
        mean = jnp.sum(p * dp, axis=0, keepdims=True)
        raw = (p * (dp - mean) * factor).astype(BF)
        dq_t[:, cols] = dot_nn(k_t[:, :keys], raw)
        dk_acc[:keys, :] += dot_nn(raw, q_rot[cols, :])
        dv_acc[:keys, :] += dot_nn(p.astype(BF), grad)
    back, gain_part = norm_back(turn_back(dq_t[...].T, cosine, sine), q, qg_ref[...])
    dq_ref[...] = back.astype(BF)
    dqg_ref[...] += gain_part

    @pl.when(step == pl.num_programs(0) - 1)
    def _():
        back, gain_part = norm_back(turn_back(dk_acc[...], cosine, sine), k_ref[...], kg_ref[...])
        dk_ref[...] = back.astype(BF)
        dkg_ref[...] = gain_part
        dv_ref[...] = dv_acc[...].astype(BF)
        reduce.middle_y(2)
        reduce.step_y(Z_AXIS - 1)
        pairs = zip(ring_pieces(output_ref, 0), ring_pieces(hidden_ref, 0))
        for a, (rows, residual) in enumerate(pairs):
            reduce.own(a, lambda terms, rows=rows, residual=residual: add_rows(rows, terms + [residual]))
        reduce.sent()
        whole_branch().wait()
        to_x(me).wait_send()
        to_core(0, rows_ref, me).wait_send()
        to_core(1, branch.at[far], far).wait_send()


def attention_back(
    span, q, k, v, lse, cosine, sine, q_gain, k_gain, w_out, d_rows, slots_t, out, hidden, number
):
    length, size = k.shape
    heads = q.shape[1] // size
    ep_count, tp_count = lax.axis_size("ep"), lax.axis_size("tp")
    if ep_count != 2 * Z_AXIS:
        branch = lax.all_gather(d_rows, "tp", axis=0, tiled=True)
        grads = dot_nt(branch, w_out).astype(BF)
        mine = lax.psum_scatter(out, "ep", scatter_dimension=0)
        back = plain_attention_back(span, q, k, v, grads, lse, cosine, sine, q_gain, k_gain)
        return *back, branch, (hidden + mine.astype(F32)).astype(BF)
    block, width = d_rows.shape
    whole = pl.BlockSpec((length, size), lambda h: (0, 0))
    head = pl.BlockSpec((length, size), lambda h: (0, h))
    gain = pl.BlockSpec((1, size), lambda h: (0, 0))
    rows = pl.BlockSpec((block, width), lambda h: (0, 0))
    dma = pltpu.SemaphoreType.DMA
    *back, branch, output = pl.pallas_call(
        attention_back_kernel,
        grid=(heads,),
        in_specs=[
            pl.BlockSpec(memory_space=pltpu.SMEM), head, whole, whole,
            pl.BlockSpec((1, 1, length), lambda h: (h, 0, 0)), whole, whole, gain, gain,
            pl.BlockSpec(w_out.shape, lambda h: (0, 0), pipeline_mode=pl.Buffered(1)), ANY,
            pl.BlockSpec(slots_t.shape, lambda h: (0, 0, 0), pipeline_mode=pl.Buffered(1)), ANY, ANY,
            pl.BlockSpec((block, width), lambda h: (0, 0), pipeline_mode=pl.Buffered(1)),
        ],
        out_specs=[head, whole, whole, gain, gain, ANY, rows],
        out_shape=[
            jax.ShapeDtypeStruct((length, heads * size), BF),
            jax.ShapeDtypeStruct((length, size), BF),
            jax.ShapeDtypeStruct((length, size), BF),
            jax.ShapeDtypeStruct((1, size), F32),
            jax.ShapeDtypeStruct((1, size), F32),
            jax.ShapeDtypeStruct((tp_count, block, width), BF),
            jax.ShapeDtypeStruct((block, width), BF),
        ],
        scratch_shapes=[
            pltpu.VMEM((length, length), F32),
            pltpu.VMEM((length, size), BF),
            pltpu.VMEM((size, length), BF),
            pltpu.VMEM((length, size), F32),
            pltpu.VMEM((length, size), F32),
            pltpu.VMEM((size, length), F32),
            pltpu.VMEM((tp_count, block, width), BF),
            pltpu.VMEM((heads, length, size), BF),
        ]
        + [pltpu.VMEM((ep_count, block, width), BF)]
        + slot_sums_scratch(slots_t.shape[2], out[0].shape[2], width)
        + [dma, dma, dma((2,)), dma((2,)), dma, dma]
        + reduce_scratch(block, width)
        + reduce_sems(3),
        compiler_params=params(collective_id=number, has_side_effects=True),
        cost_estimate=link_cost(100.0),
        name="attention_back",
    )(span, q, k, v, lse, cosine, sine, q_gain, k_gain, w_out, d_rows, slots_t, *out, hidden)
    return *back, branch.reshape(-1, width), output


def projection_grads_kernel(
    normed, dq, dk, dv, heads, branch, wq_hbm, wk, wv, x_rows, d_hbm, gain, small,
    gq_ref, gk_ref, gv_ref, gout_ref, inputs_grad, gain_grad, small_sum,
    blocks, out_blocks, gout, part, core_rows, far_rows, gain_own, tp_gains, tp_gain, ep_gains, wq, d_hidden,
    core_send, core_recv, x_send, x_recv, wq_sem, d_sem, *refs,
):
    me = lax.axis_index("tp")
    x, c = me // 2, me % 2
    other_core, other_x = {"tp": x * 2 + 1 - c}, {"tp": (1 - x) * 2 + c}
    sums = SumAll(small, small_sum, *refs[:5], refs[5:13])
    over_tp, over_ep = Exchange("tp", refs[13], refs[14]), Exchange("ep", refs[15], refs[16])
    reduce = EpReduce(
        ring_pieces(blocks, 1) + ring_pieces(out_blocks, 1), BY_Z * 2, refs[17:29], refs[29:]
    )
    order, y = reduce.order, reduce.y
    rows, width = inputs_grad.shape
    nq, nk = dq.shape[1], dk.shape[1]

    load_wq = pltpu.make_async_copy(wq_hbm, wq, wq_sem)
    load_d = pltpu.make_async_copy(d_hbm, d_hidden, d_sem)
    load_wq.start()
    load_d.start()
    everyone = []
    for exchange in (over_tp, over_ep):
        exchange.each(
            lambda i, other, axis=exchange.axis: everyone.append((other >= 0, {axis: other}))
        )
    greet(everyone)

    def fill(j):
        cols = pl.ds(pl.multiple_of(j * rows, rows), rows)
        left = normed[:, cols].T
        blocks[j, :, 0:nq] = dot_nn(left, dq[...]).astype(BF)
        blocks[j, :, nq : nq + nk] = dot_nn(left, dk[...]).astype(BF)
        blocks[j, :, nq + nk : nq + 2 * nk] = dot_nn(left, dv[...]).astype(BF)
        out_blocks[j] = dot_nn(branch[:, cols].T, heads[...]).astype(BF)

    def spread_back(tp):
        lines = pl.ds(pl.multiple_of(tp * rows, rows), rows)
        for start in range(0, width, width // 4):
            cols = slice(start, start + width // 4)
            part[tp, :, cols] = (
                dot_nt(dq[lines, :], wq[cols, :])
                + dot_nt(dk[lines, :], wk[cols, :])
                + dot_nt(dv[lines, :], wv[cols, :])
            ).astype(BF)

    def to_core(xt):
        return remote(
            part.at[xt * 2 + 1 - c], core_rows.at[xt], core_send.at[xt], core_recv.at[xt], other_core
        )

    far, near = part.at[(1 - x) * 2 + c], part.at[x * 2 + c]
    to_x = remote(far, far_rows, x_send, x_recv, other_x)

    def fill_side(k):
        fill(order[k] * 2 + 1 - y)
        reduce.send_side(k)

    def fill_own(k):
        fill(order[k] * 2 + y)

    fill_side(0)
    fill_side(1)
    load_wq.wait()
    spread_back((1 - x) * 2 + 1 - c)
    to_core(1 - x).start()
    fill_side(2)
    spread_back((1 - x) * 2 + c)
    to_core(1 - x).wait_recv()
    add_rows(far, [far, core_rows.at[1 - x]])
    to_x.start()
    fill_side(3)
    fill_own(0)
    reduce.step_z(0)
    reduce.ends_y(0)
    sums.start()
    fill_own(1)
    reduce.step_z(1)
    spread_back(x * 2 + 1 - c)
    to_core(x).start()
    spread_back(x * 2 + c)
    fill_own(2)
    reduce.step_z(2)
    fill_own(3)
    reduce.step_z(3)
    reduce.ends_y(1)
    reduce.middle_y(0)
    sums.across()
    to_core(x).wait_recv()
    to_x.wait_recv()
    load_d.wait()

    chunk = 32
    gain_own[...] = jnp.zeros_like(gain_own)

    @pl.loop(0, rows // chunk)
    def _(i):
        lines = pl.ds(pl.multiple_of(i * chunk, chunk), chunk)
        grad = near[lines, :].astype(F32) + core_rows[x, lines, :].astype(F32)
        grad = grad + far_rows[lines, :].astype(F32)
        back, gain_part = norm_back(grad, x_rows[lines, :].astype(F32), gain[...])
        inputs_grad[lines, :] = d_hidden[lines, :] + back
        gain_own[...] += gain_part

    over_tp.start(lambda t: gain_own, tp_gains)
    tp_gains[pl.ds(over_tp.me, 1)] = gain_own[...][None]
    sums.back()
    reduce.ends_y(2)
    reduce.middle_y(1)
    reduce.middle_y(2)
    sums.home()
    over_tp.arrived(tp_gains)
    tp_gain[...] = jnp.sum(tp_gains[...], axis=0)
    over_ep.start(lambda e: tp_gain, ep_gains)
    ep_gains[pl.ds(over_ep.me, 1)] = tp_gain[...][None]
    reduce.step_y(3)

    def total_of(terms):
        value = terms[0][...].astype(F32)
        for term in terms[1:]:
            value = value + term[...].astype(F32)
        return value

    over_ep.arrived(ep_gains)
    gain_grad[...] = jnp.sum(ep_gains[...], axis=0)
    results = zip(*[ring_pieces(ref, 0) for ref in (gq_ref, gk_ref, gv_ref)])
    for a, (to_q, to_k, to_v) in enumerate(results):

        def write(terms, to_q=to_q, to_k=to_k, to_v=to_v):
            value = total_of(terms)
            to_q[...] = value[:, 0:nq]
            to_k[...] = value[:, nq : nq + nk]
            to_v[...] = value[:, nq + nk :]

        reduce.own(a, write)
    for a, rows_to in enumerate(ring_pieces(gout, 0)):

        def write_out(terms, rows_to=rows_to):
            rows_to[...] = total_of(terms)

        reduce.own(3 + a, write_out)
    gout_ref[...] = gout[...].T
    reduce.sent()
    to_core(1 - x).wait_send()
    to_core(x).wait_send()
    to_x.wait_send()
    over_tp.sent(lambda t: gain_own, tp_gains)
    over_ep.sent(lambda e: tp_gain, ep_gains)
    sums.finish()


def projection_grads(
    normed, dq, dk, dv, heads, branch, wq, wk, wv, x_rows, d_hidden, gain, small_values, number
):
    rows, width = x_rows.shape
    ep_count, tp_count = lax.axis_size("ep"), lax.axis_size("tp")
    small = pack_small(small_values, tp_count, ep_count)
    if ep_count != 2 * Z_AXIS:

        def over_sequences(part, dim):
            return lax.psum_scatter(
                part.astype(BF), "ep", scatter_dimension=dim, tiled=True
            ).astype(F32)

        d_normed = (dot_nt(dq, wq) + dot_nt(dk, wk) + dot_nt(dv, wv)).astype(BF)
        d_mine = lax.psum_scatter(d_normed, "tp", scatter_dimension=0, tiled=True)
        back, gain_part = norm_back(d_mine.astype(F32), x_rows.astype(F32), gain)
        gain_sum, small_sum = lax.psum((gain_part, small), ("ep", "tp"))
        return (
            over_sequences(dot_tn(normed, dq), 0),
            over_sequences(dot_tn(normed, dk), 0),
            over_sequences(dot_tn(normed, dv), 0),
            over_sequences(dot_tn(heads, branch), 1),
            d_hidden + back,
            gain_sum,
            unpack_small(small_sum, small_values),
        )
    nq, nk = dq.shape[1], dk.shape[1]
    nh = heads.shape[1]
    vmem = pl.BlockSpec(memory_space=pltpu.VMEM)
    dma = pltpu.SemaphoreType.DMA
    *grads, small_sum = pl.pallas_call(
        projection_grads_kernel,
        in_specs=[vmem] * 6 + [ANY] + [vmem] * 3 + [ANY] + [vmem] * 2,
        out_specs=[vmem] * 7,
        out_shape=[
            jax.ShapeDtypeStruct((rows, nq), F32),
            jax.ShapeDtypeStruct((rows, nk), F32),
            jax.ShapeDtypeStruct((rows, nk), F32),
            jax.ShapeDtypeStruct((nh, rows), F32),
            jax.ShapeDtypeStruct((rows, width), F32),
            jax.ShapeDtypeStruct((1, width), F32),
            jax.ShapeDtypeStruct(small.shape, F32),
        ],
        scratch_shapes=[
            pltpu.VMEM((ep_count, rows, nq + 2 * nk), BF),
            pltpu.VMEM((ep_count, rows, nh), BF),
            pltpu.VMEM((rows, nh), F32),
            pltpu.VMEM((tp_count, rows, width), BF),
            pltpu.VMEM((2, rows, width), BF),
            pltpu.VMEM((rows, width), BF),
            pltpu.VMEM((1, width), F32),
            pltpu.VMEM((tp_count, 1, width), F32),
            pltpu.VMEM((1, width), F32),
            pltpu.VMEM((ep_count, 1, width), F32),
            pltpu.VMEM(wq.shape, BF),
            pltpu.VMEM((rows, width), F32),
            dma((2,)), dma((2,)), dma, dma, dma, dma,
        ]
        + sum_scratch(small.shape)
        + exchange_sems("tp")
        + exchange_sems("ep")
        + reduce_scratch(rows, nq + 2 * nk)
        + reduce_scratch(rows, nh)
        + reduce_sems(6),
        compiler_params=params(collective_id=number, has_side_effects=True),
        cost_estimate=link_cost(110.0),
        name="projection_grads",
    )(normed, dq, dk, dv, heads, branch, wq, wk, wv, x_rows, d_hidden, gain, small)
    return *grads, unpack_small(small_sum, small_values)


def select_kernel(slot_ref, x_ref, c_ref, xs_ref, cs_ref):
    local, _, capacity, width = xs_ref.shape
    rows = x_ref.shape[1]
    place = jnp.concatenate(
        [
            (
                slot_ref[0, e : e + 1, :]
                == lax.broadcasted_iota(jnp.int32, (capacity, rows), 0)
            ).astype(F32)
            for e in range(local)
        ],
        axis=0,
    ).astype(BF)
    xs_ref[...] = dot_nn(place, x_ref[0]).astype(BF).reshape(xs_ref.shape)
    cs_ref[...] = dot_nn(place, c_ref[0]).astype(BF).reshape(cs_ref.shape)


def select_rows(slots, tokens, cots, capacity):
    blocks, local, rows = slots.shape
    width = tokens.shape[-1]
    block = pl.BlockSpec((1, rows, width), lambda b: (b, 0, 0))
    out = pl.BlockSpec((local, 1, capacity, width), lambda b: (0, b, 0, 0))
    shape = jax.ShapeDtypeStruct((local, blocks, capacity, width), BF)
    return pl.pallas_call(
        select_kernel,
        grid=(blocks,),
        in_specs=[pl.BlockSpec((1, local, rows), lambda b: (b, 0, 0)), block, block],
        out_specs=[out, out],
        out_shape=[shape, shape],
        compiler_params=params(),
        name="select_rows",
    )(slots, tokens, cots)


def pack_kernel(gate_ref, up_ref, down_ref, out_ref):
    for kind, ref in enumerate((gate_ref, up_ref, down_ref)):
        out_ref[kind, 0] = ref[0]


def pack_weights(weights, first, count):
    _, hidden, width = weights[0].shape
    block = pl.BlockSpec((1, hidden, width), lambda e: (first + e, 0, 0))
    return pl.pallas_call(
        pack_kernel,
        grid=(count,),
        in_specs=[block] * 3,
        out_specs=pl.BlockSpec((3, 1, hidden, width), lambda e: (0, e, 0, 0)),
        out_shape=jax.ShapeDtypeStruct((3, count, hidden, width), BF),
        compiler_params=params(),
        name="pack_weights",
    )(*weights)


def expert_kernel(
    x_ref, c_ref, w_ref, gate_ref, out_ref, dx_ref, act_ref, dg_ref, du_ref, dgate_ref
):
    width = x_ref.shape[-1]
    x, c = x_ref[0], c_ref[0]
    w_gate = w_ref[:, 0, 0].reshape(-1, width)
    w_up = w_ref[:, 1, 0].reshape(-1, width)
    w_down = w_ref[:, 2, 0].reshape(-1, width)
    gate = gate_ref[0]
    gate_pre = dot_nt(x, w_gate)
    up_pre = dot_nt(x, w_up)
    raw = dot_nt(c, w_down)
    sig = jax.nn.sigmoid(gate_pre)
    silu = gate_pre * sig
    act = silu * up_pre
    dgate_ref[0] = jnp.sum(act * raw, axis=-1, keepdims=True)
    act_low = (act * gate).astype(BF)
    d_act = raw * gate
    d_gate = (d_act * up_pre * sig * (1.0 + gate_pre * (1.0 - sig))).astype(BF)
    d_up = (d_act * silu).astype(BF)
    act_ref[0] = act_low
    dg_ref[0] = d_gate
    du_ref[0] = d_up
    out_ref[0] = dot_nn(act_low, w_down).astype(BF)
    dx_ref[0] = (dot_nn(d_gate, w_gate) + dot_nn(d_up, w_up)).astype(BF)


def experts_both_ways(x_slots, c_slots, w_all, slot_gate, first):
    _, number, width = x_slots.shape
    parts, _, local, hidden, _ = w_all.shape
    tile = number // 2
    taken = pl.BlockSpec((1, tile, width), lambda e, i: (first + e, i, 0))
    wide = pl.BlockSpec((1, tile, width), lambda e, i: (e, i, 0))
    mid = pl.BlockSpec((1, tile, parts * hidden), lambda e, i: (e, i, 0))
    thin = pl.BlockSpec((1, tile, 1), lambda e, i: (e, i, 0))
    wide_shape = jax.ShapeDtypeStruct((local, number, width), BF)
    mid_shape = jax.ShapeDtypeStruct((local, number, parts * hidden), BF)
    return pl.pallas_call(
        expert_kernel,
        grid=(local, 2),
        in_specs=[
            taken, taken,
            pl.BlockSpec((parts, 3, 1, hidden, width), lambda e, i: (0, 0, e, 0, 0)),
            pl.BlockSpec((1, tile, 1), lambda e, i: (first + e, i, 0)),
        ],
        out_specs=[wide, wide, mid, mid, mid, thin],
        out_shape=[
            wide_shape, wide_shape, mid_shape, mid_shape, mid_shape,
            jax.ShapeDtypeStruct((local, number, 1), F32),
        ],
        compiler_params=params(),
        name="experts_both_ways",
    )(x_slots, c_slots, w_all, slot_gate)


def expert_grads_kernel(x_ref, c_ref, act_ref, dg_ref, du_ref, out_ref):
    parts, _, _, hidden, width = out_ref.shape
    x, c = x_ref[0], c_ref[0]
    out_ref[:, 0, 0] = dot_tn(dg_ref[0], x).astype(BF).reshape(parts, hidden, width)
    out_ref[:, 1, 0] = dot_tn(du_ref[0], x).astype(BF).reshape(parts, hidden, width)
    out_ref[:, 2, 0] = dot_tn(act_ref[0], c).astype(BF).reshape(parts, hidden, width)


def expert_grads(x_slots, c_slots, act, d_gate, d_up, parts, first):
    local, number, inner = act.shape
    width = x_slots.shape[-1]
    wide = pl.BlockSpec((1, number, width), lambda e: (first + e, 0, 0))
    mid = pl.BlockSpec((1, number, inner), lambda e: (e, 0, 0))
    return pl.pallas_call(
        expert_grads_kernel,
        grid=(local,),
        in_specs=[wide, wide, mid, mid, mid],
        out_specs=pl.BlockSpec(
            (parts, 3, 1, inner // parts, width), lambda e: (0, 0, e, 0, 0)
        ),
        out_shape=jax.ShapeDtypeStruct((parts, 3, local, inner // parts, width), BF),
        compiler_params=params(),
        name="expert_grads",
    )(x_slots, c_slots, act, d_gate, d_up)


def combine_kernel(
    first_ref, slot_ref, dxa_ref, dxb_ref, outa_ref, outb_ref, dgate_ref, dx_sum_ref, out_sum_ref, pay_ref
):
    _, _, capacity, width = dxa_ref.shape
    local = slot_ref.shape[2]
    rows = slot_ref.shape[1]
    lane = lax.broadcasted_iota(jnp.int32, (rows, local * capacity), 1)
    half = pay_ref.shape[2] // 2
    column = lax.broadcasted_iota(jnp.int32, (rows, 2 * half), 1)
    total = jnp.zeros((rows, local * capacity), F32)
    pay = jnp.zeros(column.shape, F32)
    for e in range(local):
        hit = lane == slot_ref[0, :, e : e + 1] + e * capacity
        total = jnp.where(hit, 1.0, total)
        value = jnp.sum(jnp.where(hit, dgate_ref[0], 0.0), axis=1, keepdims=True)
        high = value.astype(BF).astype(F32)
        pay = jnp.where(column == first_ref[0, 0] + e, high, pay)
        pay = jnp.where(column == first_ref[0, 0] + e + half, value - high, pay)
    place = total.astype(BF)

    def both(a_ref, b_ref):
        pair = [ref[...].reshape(-1, width) for ref in (a_ref, b_ref)]
        return dot_nn(place, jnp.concatenate(pair, axis=0)).astype(BF)

    dx_sum_ref[0] = both(dxa_ref, dxb_ref)
    out_sum_ref[0] = both(outa_ref, outb_ref)
    pay_ref[0] = pay.astype(BF)


def combine_rows(first, slots_t, dx, out, d_gate_slots, experts):
    blocks, rows, local = slots_t.shape
    _, _, capacity, width = dx[0].shape
    lanes = -(-2 * experts // 128) * 128
    slot = pl.BlockSpec((local // 2, 1, capacity, width), lambda b: (0, b, 0, 0))
    block = pl.BlockSpec((1, rows, width), lambda b: (b, 0, 0))
    shape = jax.ShapeDtypeStruct((blocks, rows, width), BF)
    return pl.pallas_call(
        combine_kernel,
        grid=(blocks,),
        in_specs=[
            pl.BlockSpec(memory_space=pltpu.SMEM),
            pl.BlockSpec((1, rows, local), lambda b: (b, 0, 0)), slot, slot, slot, slot,
            pl.BlockSpec((1, 1, local * capacity), lambda b: (b, 0, 0)),
        ],
        out_specs=[block, block, pl.BlockSpec((1, rows, lanes), lambda b: (b, 0, 0))],
        out_shape=[shape, shape, jax.ShapeDtypeStruct((blocks, rows, lanes), BF)],
        compiler_params=params(),
        name="combine_rows",
    )(first, slots_t, *dx, *out, d_gate_slots)


def on_device(
    inputs,
    attn_gain,
    w_query,
    key_weight_matrix,
    value_weight_matrix,
    query_gain,
    key_gain,
    w_out,
    route_gain,
    w_router,
    w_gate,
    w_up,
    w_down,
    routes,
    image_starts,
    cotangent,
):
    tp_count = lax.axis_size("tp")
    ep_count = lax.axis_size("ep")
    tp_index = lax.axis_index("tp")
    ep_index = lax.axis_index("ep")
    length = inputs.shape[0]
    width = inputs.shape[1]
    rows = cotangent.shape[0]
    head_dim = query_gain.shape[0]
    local_experts = w_gate.shape[0]
    experts = local_experts * ep_count
    top = routes.shape[1]
    capacity = -(-(3 * rows * top // (2 * experts)) // 16) * 16

    pair = local_experts // 2

    weights = (w_gate.transpose(0, 2, 1), w_up.transpose(0, 2, 1), w_down)
    w_first = lax.all_gather(pack_weights(weights, 0, pair), "tp")

    normed, queries, key_rows, values = project(
        inputs, attn_gain[None], w_query, key_weight_matrix, value_weight_matrix
    )
    cosine, sine = rope_tables(length, head_dim)
    q_gain, k_gain = query_gain[None], key_gain[None]
    x_rows = lax.dynamic_slice_in_dim(inputs, tp_index * rows, rows, 0)
    heads, lse, hidden, moe_in, cot_all, second = attention(
        image_starts, queries, key_rows, values, cosine, sine, q_gain, k_gain,
        w_out, cotangent, x_rows, route_gain[None], weights, pair, 0,
    )
    w_second = lax.all_gather(second, "tp")
    logits = dot_nn(moe_in, w_router)
    router_probs = plain_softmax(logits)
    expert_ids = jnp.arange(experts, dtype=jnp.int32)
    ring_routes = lax.dynamic_index_in_dim(
        routes.reshape(ep_count, tp_count, rows, top), tp_index, 1, keepdims=False
    )
    my_routes = lax.dynamic_index_in_dim(ring_routes, ep_index, 0, keepdims=False)

    def routed_softmax(scores, picked):
        kept = jnp.where(picked, scores, MASKED)
        expo = jnp.where(picked, jnp.exp(kept - jnp.max(kept, axis=-1, keepdims=True)), 0.0)
        return expo / jnp.sum(expo, axis=-1, keepdims=True)

    my_pick = jnp.any(my_routes[:, :, None] == expert_ids[None, None, :], axis=1)
    gates = routed_softmax(logits, my_pick)
    all_pick = jnp.any(ring_routes[..., None] == expert_ids, axis=2)
    mask = lax.dynamic_slice_in_dim(all_pick, ep_index * local_experts, local_experts, 2)
    earlier = (jnp.arange(rows)[:, None] > jnp.arange(rows)[None, :]).astype(BF)
    slots_t = jnp.einsum(
        "tu,bue->bte", earlier, mask.astype(BF), preferred_element_type=F32
    ).astype(jnp.int32)
    slots_t = jnp.where(mask, slots_t, NOWHERE)
    slots = slots_t.transpose(0, 2, 1)
    ring = ep_count == 2 * Z_AXIS
    if ring:
        turned = lax.rem(expert_ids + ep_index * local_experts, experts)
        x_slots, c_slots, slot_gate = gather_select(
            moe_in,
            cot_all,
            slots,
            all_pick.astype(jnp.int32)[..., turned].transpose(0, 2, 1),
            w_router.T[turned],
            capacity,
            1,
        )
        slot_gate = slot_gate.reshape(local_experts, ep_count * capacity, 1)
    else:
        tokens_all = lax.all_gather(moe_in, "ep")
        logits_all = dot_nn(tokens_all.reshape(-1, width), w_router).reshape(ep_count, rows, experts)
        gate_of = lax.dynamic_slice_in_dim(
            routed_softmax(logits_all, all_pick), ep_index * local_experts, local_experts, 2
        )
        place = slots[:, :, None, :] == jnp.arange(capacity, dtype=jnp.int32)[:, None]
        slot_gate = jnp.sum(
            jnp.where(place, gate_of.transpose(0, 2, 1)[:, :, None, :], 0.0), axis=-1
        )
        slot_gate = slot_gate.transpose(1, 0, 2).reshape(local_experts, ep_count * capacity, 1)
        x_slots, c_slots = select_rows(slots, tokens_all, cot_all, capacity)
    flat = (local_experts, ep_count * capacity, width)
    x_slots, c_slots = x_slots.reshape(flat), c_slots.reshape(flat)

    def over_rings(grads):
        return lax.psum_scatter(grads.reshape(-1, width), "tp", scatter_dimension=0, tiled=True)

    out_a, dx_a, *inner_a, dg_a = experts_both_ways(x_slots, c_slots, w_first, slot_gate, 0)
    grads_a = expert_grads(x_slots, c_slots, *inner_a, tp_count, 0)
    x_slots, grads_a = lax.optimization_barrier((x_slots, grads_a))
    mine_a = over_rings(grads_a)
    out_b, dx_b, *inner_b, dg_b = experts_both_ways(x_slots, c_slots, w_second, slot_gate, pair)
    deep = (pair, ep_count, capacity, width)
    dx_slots = [dx_a.reshape(deep), dx_b.reshape(deep)]
    out_slots = [out_a.reshape(deep), out_b.reshape(deep)]
    d_gate_slots = (
        jnp.concatenate([dg_a, dg_b])
        .reshape(local_experts, ep_count, capacity)
        .transpose(1, 0, 2)
        .reshape(ep_count, 1, local_experts * capacity)
    )
    counts = jnp.sum((routes[:, :, None] == expert_ids[None, None, :]).astype(F32), axis=(0, 1))
    total_tokens = routes.shape[0]
    share = counts / (total_tokens * top)
    coeff = AUX * experts * share
    if ring:
        d_hidden, d_rows, router_part, route_gain_part, grads_b = input_grads(
            slots_t, d_gate_slots, dx_slots, x_slots, c_slots, inner_b,
            [
                hidden, moe_in, cotangent, route_gain[None], gates, router_probs,
                coeff[None], w_router.T,
            ],
            experts, tp_count, 2,
        )
    else:
        grads_b = expert_grads(x_slots, c_slots, *inner_b, tp_count, pair)
        dx_part, out_slots, gate_part = combine_rows(
            (ep_index * local_experts).reshape(1, 1), slots_t, dx_slots, out_slots, d_gate_slots, experts
        )
        dx_mine = lax.psum_scatter(dx_part, "ep", scatter_dimension=0).astype(F32)
        gate_mine = lax.psum_scatter(gate_part, "ep", scatter_dimension=0).astype(F32)
        lanes = gate_mine.shape[1] // 2
        d_gates = gate_mine[:, :experts] + gate_mine[:, lanes : lanes + experts]
        d_logits = gates * (d_gates - jnp.sum(gates * d_gates, axis=-1, keepdims=True))
        d_logits = d_logits + router_probs * (
            coeff - jnp.sum(router_probs * coeff, axis=-1, keepdims=True)
        )
        d_low = d_logits.astype(BF)
        router_part = dot_tn(d_low, moe_in)
        d_moe = dot_nt(d_low, w_router) + dx_mine
        back, route_gain_part = norm_back(d_moe, hidden, route_gain[None])
        d_hidden = cotangent.astype(F32) + back
        d_rows = d_hidden.astype(BF)
    d_rows, mine_a, grads_b = lax.optimization_barrier((d_rows, mine_a, grads_b))
    mine_b = over_rings(grads_b)
    mine_a, mine_b = [m.reshape(3, pair, -1, width) for m in (mine_a, mine_b)]
    w_gate_grad, w_up_grad, w_down_grad = widen_grads(mine_a, mine_b)
    w_gate_grad, w_up_grad = w_gate_grad.transpose(0, 2, 1), w_up_grad.transpose(0, 2, 1)
    prob_local = jnp.sum(router_probs, axis=0)
    d_queries, d_keys, d_values, query_gain_part, key_gain_part, d_branch, output = attention_back(
        image_starts, queries, key_rows, values, lse, cosine, sine, q_gain, k_gain,
        w_out, d_rows, slots_t, out_slots, hidden, 3,
    )
    w_query_grad, w_key_grad, w_value_grad, w_out_grad, inputs_grad, attn_gain_grad, small = projection_grads(
        normed, d_queries, d_keys, d_values, heads, d_branch,
        w_query, key_weight_matrix, value_weight_matrix,
        x_rows, d_hidden, attn_gain[None],
        [router_part, route_gain_part[0], query_gain_part[0], key_gain_part[0], prob_local],
        5,
    )
    w_router_grad, route_gain_grad, query_gain_grad, key_gain_grad, prob_all = small
    w_router_grad = w_router_grad.T
    attn_gain_grad = attn_gain_grad[0]
    aux_loss = experts * jnp.sum(share * (prob_all / total_tokens))
    return (
        output,
        aux_loss,
        inputs_grad,
        attn_gain_grad,
        w_query_grad,
        w_key_grad,
        w_value_grad,
        query_gain_grad,
        key_gain_grad,
        w_out_grad,
        route_gain_grad,
        w_router_grad,
        w_gate_grad,
        w_up_grad,
        w_down_grad,
    )


def solution(mesh):
    return jax.shard_map(
        on_device,
        mesh=mesh,
        in_specs=(
            P("ep", None),
            P(),
            P(None, "tp"),
            P(None, "tp"),
            P(None, "tp"),
            P(),
            P(),
            P("tp", None),
            P(),
            P(),
            P("ep", None, "tp"),
            P("ep", None, "tp"),
            P("ep", "tp", None),
            P(),
            P("ep", None),
            P(("ep", "tp"), None),
        ),
        out_specs=(
            P(("ep", "tp"), None),
            P(),
            P(("ep", "tp"), None),
            P(),
            P("ep", "tp"),
            P("ep", "tp"),
            P("ep", "tp"),
            P(),
            P(),
            P("tp", "ep"),
            P(),
            P(),
            P("ep", None, "tp"),
            P("ep", None, "tp"),
            P("ep", "tp", None),
        ),
        check_vma=False,
    )
```

```python
import functools

import jax
import jax.numpy as jnp
import numpy as np
from jax import lax
from jax.experimental import pallas as pl
from jax.experimental.pallas import tpu as pltpu
from jax.sharding import PartitionSpec as P

IMG = 256
EPS = 1e-06
AUX = 0.04
THETA = 1000000.0
MASKED = -1e30
NOWHERE = -(1 << 20)
BF = jnp.bfloat16
F32 = jnp.float32
VMEM_BYTES = 60 * 1024 * 1024


def dot_nn(a, b):
    return lax.dot_general(a, b, (((1,), (0,)), ((), ())), preferred_element_type=F32)


def dot_nt(a, b):
    return lax.dot_general(a, b, (((1,), (1,)), ((), ())), preferred_element_type=F32)


def dot_tn(a, b):
    return lax.dot_general(a, b, (((0,), (0,)), ((), ())), preferred_element_type=F32)


def params(**kw):
    return pltpu.CompilerParams(vmem_limit_bytes=VMEM_BYTES, **kw)


def rms_scale(value_rows):
    return lax.rsqrt(jnp.mean(value_rows * value_rows, axis=-1, keepdims=True) + EPS)


def plain_softmax(value_rows):
    top = jnp.max(value_rows, axis=-1, keepdims=True)
    expo = jnp.exp(value_rows - top)
    return expo / jnp.sum(expo, axis=-1, keepdims=True)


def rope_tables(length, size):
    half = size // 2
    freq = THETA ** (-2.0 * np.arange(half) / size)
    angle = np.arange(length)[:, None] * freq[None, :]
    cosine, sine = np.cos(angle), np.sin(angle)
    tables = (np.concatenate([cosine, cosine], axis=-1), np.concatenate([-sine, sine], axis=-1))
    return tuple(jnp.asarray(t, F32) for t in tables)


def turn(rows, cosine, sine):
    return rows * cosine + pltpu.roll(rows, rows.shape[-1] // 2, 1) * sine


def turn_back(rows, cosine, sine):
    return rows * cosine - pltpu.roll(rows, rows.shape[-1] // 2, 1) * sine


MESH = pl.DeviceIdType.MESH
ANY = pl.BlockSpec(memory_space=pl.ANY)
Z_AXIS = 4


def link_cost(us):
    return pl.CostEstimate(flops=0, bytes_accessed=int(us * 3.0e6), transcendentals=0)


def greet(partners):
    barrier = pltpu.get_barrier_semaphore()
    count = 0
    for there, device in partners:
        flag = jnp.asarray(there, jnp.int32)

        @pl.when(there)
        def _(device=device):
            pl.semaphore_signal(barrier, inc=1, device_id=device, device_id_type=MESH)

        count = count + flag
    pl.semaphore_wait(barrier, count)


def remote(src, dst, send, recv, device):
    return pltpu.make_async_remote_copy(
        src_ref=src, dst_ref=dst, send_sem=send, recv_sem=recv, device_id=device, device_id_type=MESH
    )


def ring_place():
    me = lax.axis_index("ep")
    z, y = me // 2, me % 2
    return me, z, y, {"ep": me + 2}, {"ep": me - 2}, {"ep": me + 1 - 2 * y}


def ring_pieces(ref, axis):
    unit = ref.shape[axis] // 16
    lead = (slice(None),) * axis
    return [
        ref.at[lead + (pl.ds(start * unit, count * unit),)]
        for start, count in ((0, 7), (7, 6), (13, 3))
    ]


class EpGather:
    def __init__(self, ins, outs, sems):
        self.ins, self.outs = ins, outs
        self.own_sem, self.up_send, self.up_recv, self.dn_send, self.dn_recv = sems[:5]
        self.y_send, self.y_recv = sems[5:]
        self.me, self.z, self.y, self.up, self.down, self.beside = ring_place()
        self.last = len(ins) - 1
        self.streams = [(a, a, self.y) for a in range(len(ins))]
        self.other = (self.last, len(ins), 1 - self.y)

    def partners(self):
        z = self.z
        return [(z < Z_AXIS - 1, self.up), (z > 0, self.down), (z >= 0, self.beside)]

    def block(self, a, zt, y):
        return self.outs[a].at[zt * 2 + y]

    def upward(self, src, stream, zt):
        a, i, y = stream
        return remote(src, self.block(a, zt, y), self.up_send.at[i, zt], self.up_recv.at[i, zt], self.up)

    def downward(self, src, stream, zt):
        a, i, y = stream
        return remote(src, self.block(a, zt, y), self.dn_send.at[i, zt], self.dn_recv.at[i, zt], self.down)

    def sideways(self, src, a, zt):
        return remote(
            src, self.block(a, zt, self.y), self.y_send.at[a, zt], self.y_recv.at[a, zt], self.beside
        )

    def both_ways(self, src, stream):
        z = self.z

        @pl.when(z < Z_AXIS - 1)
        def _():
            self.upward(src, stream, z).start()

        @pl.when(z > 0)
        def _():
            self.downward(src, stream, z).start()

    def start(self):
        self.sideways(self.ins[self.last], self.last, self.z).start()
        for stream in self.streams:
            a = stream[0]
            self.both_ways(self.ins[a], stream)
            if a != self.last:
                self.sideways(self.ins[a], a, self.z).start()
            pltpu.make_async_copy(self.ins[a], self.block(a, self.z, self.y), self.own_sem.at[a]).start()

    def cross(self):
        self.side_arrived(self.last, self.z)
        self.both_ways(self.block(self.last, self.z, 1 - self.y), self.other)

    def hop(self, d):
        z = self.z
        for stream in [self.other] + self.streams:
            a, _, y = stream

            @pl.when(z >= d)
            def _(a=a, y=y, stream=stream, zt=z - d):
                rows = self.block(a, zt, y)
                self.upward(rows, stream, zt).wait_recv()

                @pl.when(z < Z_AXIS - 1)
                def _():
                    self.upward(rows, stream, zt).start()

                if a != self.last:
                    self.sideways(rows, a, zt).start()

            @pl.when(z + d < Z_AXIS)
            def _(a=a, y=y, stream=stream, zt=z + d):
                rows = self.block(a, zt, y)
                self.downward(rows, stream, zt).wait_recv()

                @pl.when(z > 0)
                def _():
                    self.downward(rows, stream, zt).start()

                if a != self.last:
                    self.sideways(rows, a, zt).start()

    def own_done(self):
        for a, x in enumerate(self.ins):
            pltpu.make_async_copy(x, self.block(a, self.z, self.y), self.own_sem.at[a]).wait()

    def side_arrived(self, a, zt):
        rows = self.block(a, zt, 1 - self.y)
        remote(rows, rows, self.y_send.at[a, zt], self.y_recv.at[a, zt], self.beside).wait_recv()

    def side_done(self, zt):
        for a in range(self.last):
            self.side_arrived(a, zt)

    def sent(self):
        z = self.z
        self.sideways(self.block(self.last, z, self.y), self.last, z).wait_send()
        for stream in self.streams + [self.other]:
            a, _, y = stream
            for zt in range(Z_AXIS):
                src = self.block(a, zt, y)
                if a != self.last:
                    self.sideways(src, a, zt).wait_send()

                @pl.when((zt <= z) & (z < Z_AXIS - 1))
                def _(src=src, zt=zt, stream=stream):
                    self.upward(src, stream, zt).wait_send()

                @pl.when((zt >= z) & (z > 0))
                def _(src=src, zt=zt, stream=stream):
                    self.downward(src, stream, zt).wait_send()

    def finish(self):
        self.own_done()
        for zt in range(Z_AXIS):
            self.side_done(zt)
        self.sent()


def gather_sems():
    dma = pltpu.SemaphoreType.DMA
    return [dma((3,))] + [dma((4, Z_AXIS))] * 6


def one_hot(slots, capacity):
    local, rows = slots.shape
    slot = lax.broadcasted_iota(jnp.int32, (capacity, rows), 0)
    return [slot == slots[e : e + 1, :] for e in range(local)]


def gather_select_kernel(
    x_ref, cots_ref, slots_ref, picks_ref, router_ref, xs_ref, cs_ref, gate_ref,
    tokens, cots, chosen, load_sem, store_sem, *sems,
):
    local, _, capacity, width = xs_ref.shape
    blocks = tokens.shape[0]
    gather = EpGather(ring_pieces(x_ref, 0), ring_pieces(tokens, 1), sems)
    z, y = gather.z, gather.y
    greet(gather.partners())
    gather.start()

    def chosen_rows(j, rows):
        hits = one_hot(slots_ref[j], capacity)
        place = jnp.concatenate([h.astype(F32) for h in hits], axis=0).astype(BF)
        return dot_nn(place, rows).astype(BF).reshape(local, capacity, width), hits

    def load(j, slot):
        return pltpu.make_async_copy(cots_ref.at[j], cots.at[slot], load_sem.at[slot])

    def store(to, j, slot):
        return pltpu.make_async_copy(chosen.at[slot], to.at[:, j], store_sem.at[slot])

    load(0, 0).start()

    @pl.loop(0, blocks)
    def _(j):
        slot = lax.rem(j, 2)

        @pl.when(j + 1 < blocks)
        def _():
            load(j + 1, 1 - slot).start()

        load(j, slot).wait()

        @pl.when(j == 3)
        def _():
            gather.cross()

        @pl.when(j >= 2)
        def _():
            store(cs_ref, j - 2, slot).wait()

        chosen[slot] = chosen_rows(j, cots[slot])[0]
        store(cs_ref, j, slot).start()

    store(cs_ref, blocks - 2, 0).wait()
    store(cs_ref, blocks - 1, 1).wait()

    def take(j):
        rows = tokens[j]
        chosen[0], hits = chosen_rows(j, rows)
        copy = store(xs_ref, j, 0)
        copy.start()
        logits = dot_nt(router_ref[...], rows)
        picked = picks_ref[j] > 0
        kept = jnp.where(picked, logits, MASKED)
        expo = jnp.exp(kept - jnp.max(kept, axis=0, keepdims=True))
        expo = jnp.where(picked, expo, 0.0)
        gates = expo / jnp.sum(expo, axis=0, keepdims=True)
        for e, hit in enumerate(hits):
            gate_ref[e, j] = jnp.sum(jnp.where(hit, gates[e : e + 1, :], 0.0), axis=1, keepdims=True)
        copy.wait()

    gather.own_done()
    take(gather.me)
    for d in range(1, Z_AXIS + 1):
        if d < Z_AXIS:
            gather.hop(d)

        @pl.loop(0, 4)
        def _(i, d=d):
            beside = i >= 2
            far = jnp.where(beside, d - 1, d)
            zt = jnp.where(lax.rem(i, 2) == 0, z - far, z + far)
            there = (zt >= 0) & (zt < Z_AXIS) & ((i < 3) | (d > 1))

            @pl.when(there & beside)
            def _():
                gather.side_done(zt)

            @pl.when(there)
            def _():
                take(zt * 2 + jnp.where(beside, 1 - y, y))

    gather.sent()


def gather_select(rows, cot_all, slots, picks, router, capacity, number):
    ep_count = lax.axis_size("ep")
    _, local, block = slots.shape
    width = rows.shape[1]
    vmem = pl.BlockSpec(memory_space=pltpu.VMEM)
    dma = pltpu.SemaphoreType.DMA
    shape = (local, ep_count, capacity, width)
    return pl.pallas_call(
        gather_select_kernel,
        in_specs=[ANY, ANY, vmem, vmem, vmem],
        out_specs=[ANY, ANY, vmem],
        out_shape=[
            jax.ShapeDtypeStruct(shape, BF),
            jax.ShapeDtypeStruct(shape, BF),
            jax.ShapeDtypeStruct(shape[:3] + (1,), F32),
        ],
        scratch_shapes=[
            pltpu.VMEM((ep_count, block, width), BF),
            pltpu.VMEM((2, block, width), BF),
            pltpu.VMEM((2, local, capacity, width), BF),
            dma((2,)), dma((2,)),
        ]
        + gather_sems(),
        compiler_params=params(collective_id=number, has_side_effects=True),
        cost_estimate=link_cost(90.0),
        name="gather_select",
    )(rows, cot_all, slots, picks, router)


def add_rows(total, terms, chunk=16):
    @pl.loop(0, total.shape[0] // chunk)
    def _(i):
        rows = pl.ds(pl.multiple_of(i * chunk, chunk), chunk)
        value = terms[0][rows, :].astype(F32)
        for term in terms[1:]:
            value = value + term[rows, :].astype(F32)
        total[rows, :] = value.astype(total.dtype)


def scatter_order(z):
    table = ((3, 2, 1, 0), (3, 0, 2, 1), (0, 3, 1, 2), (0, 1, 2, 3))
    return [
        jnp.where(
            z == 0,
            table[0][k],
            jnp.where(z == 1, table[1][k], jnp.where(z == 2, table[2][k], table[3][k])),
        )
        for k in range(Z_AXIS)
    ]


class EpReduce:
    def __init__(self, ins, by_z, bufs, sems):
        self.ins, self.by_z = ins, by_z
        self.bufs = [bufs[2 * a : 2 * a + 2] for a in range(len(ins))]
        self.up_send, self.up_recv, self.dn_send, self.dn_recv, self.y_send, self.y_recv = sems
        self.me, self.z, self.y, self.up, self.down, self.beside = ring_place()
        self.order = scatter_order(self.z)
        self.streams = [(a, 0, self.y) for a in range(len(ins))]
        self.crossing = [(a, 1, 1 - self.y) for a in range(len(ins)) if by_z[a]]

    def partners(self):
        z = self.z
        return [(z < Z_AXIS - 1, self.up), (z > 0, self.down), (z >= 0, self.beside)]

    def mine(self, stream, zt):
        return self.ins[stream[0]].at[zt * 2 + stream[2]]

    def side(self, a, zt):
        return self.bufs[a][0].at[0 if self.by_z[a] else zt]

    def below(self, stream, zt):
        return self.bufs[stream[0]][1].at[stream[1] * (Z_AXIS + 1) + zt]

    def above(self, stream, zt, z):
        return self.below(stream, jnp.where(zt == z, Z_AXIS, zt))

    def to_side(self, a, zt):
        src = self.ins[a].at[zt * 2 + 1 - self.y]
        return remote(src, self.side(a, zt), self.y_send.at[a, zt], self.y_recv.at[a, zt], self.beside)

    def rising(self, stream, zt):
        i = 2 * stream[0] + stream[1]
        return remote(
            self.mine(stream, zt), self.below(stream, zt), self.up_send.at[i, zt], self.up_recv.at[i, zt], self.up
        )

    def falling(self, stream, zt):
        i = 2 * stream[0] + stream[1]
        return remote(
            self.mine(stream, zt), self.above(stream, zt, self.z - 1),
            self.dn_send.at[i, zt], self.dn_recv.at[i, zt], self.down,
        )

    def send_side(self, k):
        for a, by_z in enumerate(self.by_z):
            if not by_z:
                self.to_side(a, self.order[k]).start()

    def step_y(self, k):
        self.step(k, [s for s in self.streams if not self.by_z[s[0]]])

    def step(self, k, streams):
        z, zt, last = self.z, self.order[k], Z_AXIS - 1
        for stream in streams:
            a = stream[0]
            mine = self.mine(stream, zt)
            terms = [mine]
            if not self.by_z[a]:
                self.to_side(a, zt).wait_recv()
                terms = [mine, self.side(a, zt)]
                ends = ((zt > z) & (z == 0)) | ((zt < z) & (z == last))

                @pl.when(ends)
                def _(mine=mine, terms=terms):
                    add_rows(mine, terms)

            @pl.when((zt > z) & (z > 0))
            def _(stream=stream, mine=mine, terms=terms):
                self.rising(stream, zt).wait_recv()
                add_rows(mine, terms + [self.below(stream, zt)])

            @pl.when((zt < z) & (z < last))
            def _(stream=stream, mine=mine, terms=terms):
                self.falling(stream, zt).wait_recv()
                add_rows(mine, terms + [self.above(stream, zt, z)])

            @pl.when(zt > z)
            def _(stream=stream):
                self.rising(stream, zt).start()

            @pl.when(zt < z)
            def _(stream=stream):
                self.falling(stream, zt).start()

    def gathered(self, stream, terms, write):
        z, last = self.z, Z_AXIS - 1

        @pl.when(z > 0)
        def _():
            self.rising(stream, z).wait_recv()

        @pl.when(z < last)
        def _():
            self.falling(stream, z).wait_recv()

        @pl.when(z == 0)
        def _():
            write(terms + [self.above(stream, z, z)])

        @pl.when(z == last)
        def _():
            write(terms + [self.below(stream, z)])

        @pl.when((z > 0) & (z < last))
        def _():
            write(terms + [self.below(stream, z), self.above(stream, z, z)])

    def own(self, a, write):
        if self.by_z[a]:
            self.to_side(a, self.z).wait_recv()
        stream = self.streams[a]
        self.gathered(stream, [self.mine(stream, self.z), self.side(a, self.z)], write)

    def sent(self):
        z = self.z
        for stream in self.streams + self.crossing:
            a = stream[0]
            for zt in range(Z_AXIS):
                if not self.by_z[a]:
                    self.to_side(a, zt).wait_send()

                @pl.when(zt > z)
                def _(stream=stream, zt=zt):
                    self.rising(stream, zt).wait_send()

                @pl.when(zt < z)
                def _(stream=stream, zt=zt):
                    self.falling(stream, zt).wait_send()

        for stream in self.crossing:
            self.to_side(stream[0], z).wait_send()


def reduce_scratch(rows, columns):
    return [pltpu.VMEM((n, rows // 2, columns), BF) for n in (Z_AXIS, Z_AXIS + 1)] * 2


BY_Z = [False, False]


def halves(ref, axis):
    n = ref.shape[axis] // 2
    lead = (slice(None),) * axis
    return [ref.at[lead + (pl.ds(h * n, n),)] for h in range(2)]


def reduce_sems(count):
    dma = pltpu.SemaphoreType.DMA
    return [dma((2 * count, Z_AXIS))] * 4 + [dma((count, Z_AXIS))] * 2


def widen_kernel(a_ref, b_ref, gate_ref, up_ref, down_ref):
    for kind, out in enumerate((gate_ref, up_ref, down_ref)):
        for half, ref in enumerate((a_ref, b_ref)):

            @pl.when(pl.program_id(0) == half)
            def _(kind=kind, out=out, ref=ref):
                out[...] = ref[kind].astype(F32)


def widen_grads(a, b):
    _, pair, hidden, width = a.shape
    shape = jax.ShapeDtypeStruct((2 * pair, hidden, width), F32)
    tile = width // 2
    return pl.pallas_call(
        widen_kernel,
        grid=(2, pair, 2),
        in_specs=[
            pl.BlockSpec(
                (3, 1, hidden, tile),
                lambda h, e, i: (0, jnp.where(h == 0, e, pair - 1), 0, jnp.where(h == 0, i, 1)),
            ),
            pl.BlockSpec(
                (3, 1, hidden, tile),
                lambda h, e, i: (0, jnp.where(h == 0, 0, e), 0, jnp.where(h == 0, 0, i)),
            ),
        ],
        out_specs=[pl.BlockSpec((1, hidden, tile), lambda h, e, i: (h * pair + e, 0, i))] * 3,
        out_shape=[shape] * 3,
        compiler_params=params(),
        name="widen_grads",
    )(a, b)


def token_hits(slots, capacity):
    rows, local = slots.shape
    lane = lax.broadcasted_iota(jnp.int32, (rows, local * capacity), 1)
    return [lane == slots[:, e : e + 1] + e * capacity for e in range(local)]


class SlotSums:
    def __init__(self, slots, first, second, buf, sem):
        self.slots, self.pair, self.buf, self.sem = slots, (first, second), buf, sem
        self.capacity = first.shape[2]

    def copies(self, j, at):
        n = self.pair[0].shape[0]
        return [
            pltpu.make_async_copy(
                ref.at[:, j], self.buf.at[at, pl.ds(i * n, n)], self.sem.at[at, i]
            )
            for i, ref in enumerate(self.pair)
        ]

    def fetch(self, j, at):
        for copy in self.copies(j, at):
            copy.start()

    def add(self, j, at, out):
        for copy in self.copies(j, at):
            copy.wait()
        place = jnp.zeros((), F32)
        for hit in token_hits(self.slots[j], self.capacity):
            place = jnp.where(hit, 1.0, place)
        rows = self.buf[at].reshape(-1, out.shape[1])
        out[...] = dot_nn(place.astype(BF), rows).astype(BF)

    def run(self, blocks, out, then):
        self.fetch(blocks[0], 0)
        for n, j in enumerate(blocks):
            if n + 1 < len(blocks):
                self.fetch(blocks[n + 1], (n + 1) % 2)
            self.add(j, n % 2, out.at[j])
            then(n)


def slot_sums_scratch(local, capacity, width):
    return [
        pltpu.VMEM((2, local, capacity, width), BF),
        pltpu.SemaphoreType.DMA((2, 2)),
    ]


def input_grads_kernel(
    slots, dgate, dx_a, dx_b, xs, cs, act, d_gate, d_up,
    residual, moe_in, cot, route_gain, gate_dense, probs, coeff, router,
    d_hidden, d_rows, router_part, gain_part, grads,
    out, gate_out, part, gates, buf, sem, x_in, c_in, h_in, w_buf, in_sem, w_sem, *refs,
):
    sums = SlotSums(slots, dx_a, dx_b, buf, sem)
    reduce = EpReduce(halves(part, 1) + [gates], BY_Z + [False], refs[:6], refs[6:])
    order, y = reduce.order, reduce.y
    pair, number, inner = act.shape
    parts, _, _, hidden, width = grads.shape
    first = xs.shape[0] - pair
    pieces = width // x_in.shape[1]
    wide = x_in.shape[1]
    greet(reduce.partners())

    def cols(piece):
        return pl.ds(piece * wide, wide)

    def wide_copies(unit):
        e, piece = unit // pieces, unit % pieces
        return [
            pltpu.make_async_copy(xs.at[first + e, :, cols(piece)], x_in, in_sem.at[0]),
            pltpu.make_async_copy(cs.at[first + e, :, cols(piece)], c_in, in_sem.at[1]),
        ]

    def inner_copies(e):
        return [
            pltpu.make_async_copy(ref.at[e], h_in.at[kind], in_sem.at[2 + kind])
            for kind, ref in enumerate((d_gate, d_up, act))
        ]

    def written(unit):
        e, piece = unit // pieces, unit % pieces
        return pltpu.make_async_copy(w_buf, grads.at[:, :, e, :, cols(piece)], w_sem)

    def prepare(unit):
        for copy in wide_copies(unit) + (inner_copies(unit // pieces) if unit % pieces == 0 else []):
            copy.start()

    def weights(unit):
        for copy in wide_copies(unit) + (inner_copies(unit // pieces) if unit % pieces == 0 else []):
            copy.wait()
        if unit > 0:
            written(unit - 1).wait()
        for kind, right in enumerate((x_in, x_in, c_in)):
            grad = dot_tn(h_in[kind], right[...]).astype(BF)
            w_buf[:, kind] = grad.reshape(parts, hidden, wide)
        written(unit).start()
        if unit + 1 < pair * pieces:
            prepare(unit + 1)

    def payload(j):
        lanes = gates.shape[2]
        column = lax.broadcasted_iota(jnp.int32, (gates.shape[1], lanes), 1)
        pay = jnp.zeros(column.shape, F32)
        mine = reduce.me * slots.shape[2]
        for e, hit in enumerate(token_hits(slots[j], sums.capacity)):
            value = jnp.sum(jnp.where(hit, dgate[j], 0.0), axis=1, keepdims=True)
            high = value.astype(BF).astype(F32)
            pay = jnp.where(column == mine + e, high, pay)
            pay = jnp.where(column == mine + e + lanes // 2, value - high, pay)
        gates[j] = pay.astype(BF)

    def send(k):
        payload(order[k] * 2 + 1 - y)
        reduce.send_side(k)

    units = pair * pieces
    quarter = [range(units * k // Z_AXIS, units * (k + 1) // Z_AXIS) for k in range(Z_AXIS)]
    sums.run([order[k] * 2 + 1 - y for k in range(Z_AXIS)], part, send)
    prepare(0)
    sums.run(
        [order[k] * 2 + y for k in range(Z_AXIS)], part, lambda k: payload(order[k] * 2 + y)
    )
    for k in range(Z_AXIS):
        for unit in quarter[k]:
            weights(unit)
        reduce.step_y(k)
    for a, rows in enumerate(halves(out, 0) + [gate_out]):
        reduce.own(a, functools.partial(add_rows, rows))

    experts, lanes = gate_dense.shape[1], gates.shape[2]
    d_gates = gate_out[:, 0:experts] + gate_out[:, lanes // 2 : lanes // 2 + experts]
    gate, prob = gate_dense[...], probs[...]
    d_logits = gate * (d_gates - jnp.sum(gate * d_gates, axis=-1, keepdims=True))
    d_logits = d_logits + prob * (coeff[...] - jnp.sum(prob * coeff[...], axis=-1, keepdims=True))
    d_low = d_logits.astype(BF)
    router_part[...] = dot_tn(d_low, moe_in[...])
    out[...] += dot_nn(d_low, router[...])
    gain_part[...] = jnp.zeros_like(gain_part)
    chunk = 16

    @pl.loop(0, out.shape[0] // chunk)
    def _(i):
        lines = pl.ds(pl.multiple_of(i * chunk, chunk), chunk)
        back, gain_rows = norm_back(out[lines, :], residual[lines, :], route_gain[...])
        total = back + cot[lines, :].astype(F32)
        d_hidden[lines, :] = total
        d_rows[lines, :] = total.astype(BF)
        gain_part[...] += gain_rows

    reduce.sent()
    written(units - 1).wait()


def input_grads(slots_t, dgate, dx, x_slots, c_slots, inner, row_values, experts, tp_count, number):
    ep_count, rows, local = slots_t.shape
    pair, _, capacity, width = dx[0].shape
    count, hidden = inner[0].shape[1:]
    lanes = -(-2 * experts // 128) * 128
    wide = width // 2
    dma = pltpu.SemaphoreType.DMA
    vmem = pl.BlockSpec(memory_space=pltpu.VMEM)
    return pl.pallas_call(
        input_grads_kernel,
        in_specs=[vmem, vmem] + [ANY] * 7 + [vmem] * 8,
        out_specs=[vmem] * 4 + [ANY],
        out_shape=[
            jax.ShapeDtypeStruct((rows, width), F32),
            jax.ShapeDtypeStruct((rows, width), BF),
            jax.ShapeDtypeStruct((experts, width), F32),
            jax.ShapeDtypeStruct((1, width), F32),
            jax.ShapeDtypeStruct((tp_count, 3, pair, hidden // tp_count, width), BF),
        ],
        scratch_shapes=[
            pltpu.VMEM((rows, width), F32),
            pltpu.VMEM((rows, lanes), F32),
            pltpu.VMEM((ep_count, rows, width), BF),
            pltpu.VMEM((ep_count, rows, lanes), BF),
        ]
        + slot_sums_scratch(local, capacity, width)
        + [
            pltpu.VMEM((count, wide), BF),
            pltpu.VMEM((count, wide), BF),
            pltpu.VMEM((3, count, hidden), BF),
            pltpu.VMEM((tp_count, 3, hidden // tp_count, wide), BF),
            dma((5,)), dma,
        ]
        + reduce_scratch(rows, width)
        + [pltpu.VMEM((n, rows, lanes), BF) for n in (Z_AXIS, Z_AXIS + 1)]
        + reduce_sems(3),
        compiler_params=params(collective_id=number, has_side_effects=True),
        cost_estimate=link_cost(100.0),
        name="input_grads",
    )(slots_t, dgate, *dx, x_slots, c_slots, *inner, *row_values)


class Exchange:
    def __init__(self, axis, send, recv):
        self.axis, self.send, self.recv = axis, send, recv
        self.count, self.me = lax.axis_size(axis), lax.axis_index(axis)

    def each(self, act):
        for i in range(1, self.count):
            act(i, lax.rem(self.me + i, self.count))

    def to(self, src, dst, i, other):
        return remote(src, dst, self.send.at[i], self.recv.at[self.me], {self.axis: other})

    def start(self, src_of, dst):
        self.each(lambda i, other: self.to(src_of(other), dst.at[self.me], i, other).start())

    def arrived(self, dst):
        self.each(
            lambda i, other: remote(
                dst.at[other], dst.at[other], self.send.at[i], self.recv.at[other], {self.axis: other}
            ).wait_recv()
        )

    def sent(self, src_of, dst):
        self.each(lambda i, other: self.to(src_of(other), dst.at[self.me], i, other).wait_send())


class SumAll:
    def __init__(self, x, out, over_tp, own_tp, over_ep, own, ring, sems):
        self.x, self.out, self.over_tp, self.own_tp = x, out, over_tp, own_tp
        self.over_ep, self.own, self.ring = over_ep, own, ring
        self.first = Exchange("tp", sems[0], sems[1])
        self.second = Exchange("ep", sems[2], sems[3])
        self.third = Exchange("ep", sems[4], sems[5])
        self.fourth = Exchange("tp", sems[6], sems[7])

    def slice_tp(self, t):
        return self.x.at[t]

    def slice_ep(self, e):
        return self.own_tp.at[e]

    def start(self):
        self.first.start(self.slice_tp, self.over_tp)
        me = self.first.me
        self.over_tp[pl.ds(me, 1)] = self.x[pl.ds(me, 1)]

    def across(self):
        self.first.arrived(self.over_tp)
        self.own_tp[...] = jnp.sum(self.over_tp[...], axis=0)
        self.second.start(self.slice_ep, self.over_ep)
        me = self.second.me
        self.over_ep[pl.ds(me, 1)] = self.own_tp[pl.ds(me, 1)]

    def back(self):
        self.second.arrived(self.over_ep)
        self.own[...] = jnp.sum(self.over_ep[...], axis=0)
        self.third.start(lambda e: self.own, self.ring)
        self.ring[pl.ds(self.third.me, 1)] = self.own[...][None]

    def home(self):
        self.third.arrived(self.ring)
        self.fourth.start(lambda t: self.ring, self.out)
        self.out[pl.ds(self.fourth.me, 1)] = self.ring[...][None]

    def finish(self):
        self.fourth.arrived(self.out)
        self.first.sent(self.slice_tp, self.over_tp)
        self.second.sent(self.slice_ep, self.over_ep)
        self.third.sent(lambda e: self.own, self.ring)
        self.fourth.sent(lambda t: self.ring, self.out)


def exchange_sems(axis):
    return [pltpu.SemaphoreType.DMA((lax.axis_size(axis),))] * 2


def sum_scratch(shape):
    tp, ep, rows, lanes = shape
    return [
        pltpu.VMEM(shape, F32), pltpu.VMEM((ep, rows, lanes), F32), pltpu.VMEM((ep, rows, lanes), F32),
        pltpu.VMEM((rows, lanes), F32), pltpu.VMEM((ep, rows, lanes), F32),
    ] + [sem for axis in ("tp", "ep", "ep", "tp") for sem in exchange_sems(axis)]


def pack_small(values, tp, ep):
    total = tp * ep
    flat = jnp.concatenate([v.reshape(-1) for v in values])
    rows = -(-flat.shape[0] // (total * 128 * 8)) * 8
    return jnp.pad(flat, (0, total * rows * 128 - flat.shape[0])).reshape(tp, ep, rows, 128)


def unpack_small(summed, values):
    summed = summed.reshape(-1)
    out, at = [], 0
    for v in values:
        out.append(summed[at : at + v.size].reshape(v.shape))
        at += v.size
    return out


def project_kernel(x_ref, gain_ref, wq_ref, wk_ref, wv_ref, normed_ref, q_ref, k_ref, v_ref):
    x = x_ref[...].astype(F32)
    normed = (x * rms_scale(x) * gain_ref[...]).astype(BF)
    normed_ref[...] = normed
    q_ref[...] = dot_nn(normed, wq_ref[...])
    k_ref[...] = dot_nn(normed, wk_ref[...])
    v_ref[...] = dot_nn(normed, wv_ref[...]).astype(BF)


def project(inputs, gain, wq, wk, wv):
    length, width = inputs.shape
    tile = min(256, length)

    def rows(columns):
        return pl.BlockSpec((tile, columns), lambda i: (i, 0))

    def fixed(array):
        return pl.BlockSpec(array.shape, lambda i: (0, 0), pipeline_mode=pl.Buffered(1))

    return pl.pallas_call(
        project_kernel,
        grid=(length // tile,),
        in_specs=[rows(width), fixed(gain), fixed(wq), fixed(wk), fixed(wv)],
        out_specs=[rows(width), rows(wq.shape[1]), rows(wk.shape[1]), rows(wv.shape[1])],
        out_shape=[
            jax.ShapeDtypeStruct((length, width), BF),
            jax.ShapeDtypeStruct((length, wq.shape[1]), F32),
            jax.ShapeDtypeStruct((length, wk.shape[1]), F32),
            jax.ShapeDtypeStruct((length, wv.shape[1]), BF),
        ],
        compiler_params=params(),
        name="project",
    )(inputs, gain, wq, wk, wv)


def fill_bias(span_ref, bias, chunk=256):
    keys, length = bias.shape
    query = lax.broadcasted_iota(jnp.int32, (1, length), 1)

    def spans(pos):
        first = (pos >= span_ref[0, 0]) & (pos < span_ref[0, 0] + IMG)
        second = (pos >= span_ref[0, 1]) & (pos < span_ref[0, 1] + IMG)
        return jnp.where(first, 0, jnp.where(second, 1, -1))

    query_span = spans(query)
    query_other = jnp.where(query_span < 0, -2, query_span)
    for start in range(0, keys, chunk):
        key = start + lax.broadcasted_iota(jnp.int32, (chunk, 1), 0)
        ok = (key <= query) | (spans(key) == query_other)
        bias[start : start + chunk, :] = jnp.where(ok, 0.0, MASKED)


def query_tiles(length):
    tile = min(IMG, length)
    return [
        (start, tile, min(length, start + tile + -(-IMG // tile) * tile))
        for start in range(0, length, tile)
    ]


def attention_kernel(
    span_ref, q_ref, k_ref, v_ref, cos_ref, sin_ref, qg_ref, kg_ref, w_out_ref, cot_ref, x_ref, gain_ref,
    out_ref, lse_ref, rows_ref, moe_ref, cots_ref,
    bias, k_rot, v_t, heads, part, core_rows, x_rows, core_send, core_recv, x_send, x_recv, *sems,
):
    factor = q_ref.shape[-1] ** (-0.5)
    cosine, sine = cos_ref[...], sin_ref[...]
    step = pl.program_id(0)
    size = q_ref.shape[-1]
    me = lax.axis_index("tp")
    x, c = me // 2, me % 2
    other_core, other_x = {"tp": x * 2 + 1 - c}, {"tp": (1 - x) * 2 + c}
    gather = EpGather(ring_pieces(cot_ref, 0), ring_pieces(cots_ref, 1), sems)

    @pl.when(step == 0)
    def _():
        greet(gather.partners() + [(x >= 0, other_core), (x >= 0, other_x)])
        gather.start()
        fill_bias(span_ref, bias)
        k = k_ref[...]
        k_rot[...] = turn(k * rms_scale(k) * kg_ref[...], cosine, sine).astype(BF)
        v_t[...] = v_ref[...].astype(F32).T.astype(BF)

    @pl.when(step == 2)
    def _():
        gather.cross()

    @pl.when(step == pl.num_programs(0) - 2)
    def _():
        gather.hop(1)

    q = q_ref[...]
    q_rot = turn(q * rms_scale(q) * qg_ref[...], cosine, sine).astype(BF)
    for start, tile, keys in query_tiles(q.shape[0]):
        cols = slice(start, start + tile)
        s = dot_nt(k_rot[:keys, :], q_rot[cols, :]) * factor + bias[:keys, cols]
        top = jnp.max(s, axis=0, keepdims=True)
        p = jnp.exp(s - top)
        total = jnp.sum(p, axis=0, keepdims=True)
        o_t = dot_nn(v_t[:, :keys], p.astype(BF)) / total
        rows = o_t.T.astype(BF)
        out_ref[cols, :] = rows
        heads[step, cols, :] = rows
        lse_ref[0, :, cols] = top + jnp.log(total)

    @pl.when(step == pl.num_programs(0) - 1)
    def _():
        count = heads.shape[0]
        block = rows_ref.shape[0]

        def project(tp):
            lines = pl.ds(pl.multiple_of(tp * block, block), block)
            rows = jnp.concatenate([heads[h, lines, :] for h in range(count)], axis=1)
            part[tp] = dot_nn(rows, w_out_ref[...]).astype(BF)

        def to_core(xt):
            return remote(
                part.at[xt * 2 + 1 - c], core_rows.at[xt],
                core_send.at[xt], core_recv.at[xt], other_core,
            )

        far, near = part.at[(1 - x) * 2 + c], part.at[x * 2 + c]
        to_x = remote(far, x_rows, x_send, x_recv, other_x)
        project((1 - x) * 2 + 1 - c)
        to_core(1 - x).start()
        project((1 - x) * 2 + c)
        to_core(1 - x).wait_recv()
        add_rows(far, [far, core_rows.at[1 - x]])
        to_x.start()
        project(x * 2 + 1 - c)
        to_core(x).start()
        project(x * 2 + c)
        gather.hop(2)
        to_core(x).wait_recv()
        gather.hop(3)
        to_x.wait_recv()
        chunk = 16

        @pl.loop(0, block // chunk)
        def _(i):
            lines = pl.ds(pl.multiple_of(i * chunk, chunk), chunk)
            total = near[lines, :].astype(F32) + core_rows[x, lines, :].astype(F32)
            hidden = x_ref[lines, :].astype(F32) + (total + x_rows[lines, :].astype(F32))
            rows_ref[lines, :] = hidden
            moe_ref[lines, :] = (hidden * rms_scale(hidden) * gain_ref[...]).astype(BF)

        gather.finish()
        to_core(1 - x).wait_send()
        to_core(x).wait_send()
        to_x.wait_send()


def plain_attention_kernel(
    span_ref, q_ref, k_ref, v_ref, cos_ref, sin_ref, qg_ref, kg_ref, out_ref, lse_ref,
    bias, k_rot, v_t,
):
    factor = q_ref.shape[-1] ** (-0.5)
    cosine, sine = cos_ref[...], sin_ref[...]

    @pl.when(pl.program_id(0) == 0)
    def _():
        fill_bias(span_ref, bias)
        k = k_ref[...]
        k_rot[...] = turn(k * rms_scale(k) * kg_ref[...], cosine, sine).astype(BF)
        v_t[...] = v_ref[...].astype(F32).T.astype(BF)

    q = q_ref[...]
    q_rot = turn(q * rms_scale(q) * qg_ref[...], cosine, sine).astype(BF)
    for start, tile, keys in query_tiles(q.shape[0]):
        cols = slice(start, start + tile)
        s = dot_nt(k_rot[:keys, :], q_rot[cols, :]) * factor + bias[:keys, cols]
        top = jnp.max(s, axis=0, keepdims=True)
        p = jnp.exp(s - top)
        total = jnp.sum(p, axis=0, keepdims=True)
        o_t = dot_nn(v_t[:, :keys], p.astype(BF)) / total
        out_ref[cols, :] = o_t.T.astype(BF)
        lse_ref[0, :, cols] = top + jnp.log(total)


def attention(span, q, k, v, cosine, sine, q_gain, k_gain, w_out, cotangent, x_rows, route_gain, number):
    length, size = k.shape
    heads = q.shape[1] // size
    whole = pl.BlockSpec((length, size), lambda h: (0, 0))
    head = pl.BlockSpec((length, size), lambda h: (0, h))
    gain = pl.BlockSpec((1, size), lambda h: (0, 0))
    in_specs = [
        pl.BlockSpec(memory_space=pltpu.SMEM), head, whole, whole, whole, whole, gain, gain,
    ]
    out_specs = [head, pl.BlockSpec((1, 1, length), lambda h: (h, 0, 0))]
    out_shape = [
        jax.ShapeDtypeStruct((length, heads * size), BF),
        jax.ShapeDtypeStruct((heads, 1, length), F32),
    ]
    scratch = [
        pltpu.VMEM((length, length), F32),
        pltpu.VMEM((length, size), BF),
        pltpu.VMEM((size, length), BF),
    ]
    args = (span, q, k, v, cosine, sine, q_gain, k_gain)
    ep_count, tp_count = lax.axis_size("ep"), lax.axis_size("tp")
    if ep_count != 2 * Z_AXIS:
        out, lse = pl.pallas_call(
            plain_attention_kernel,
            grid=(heads,),
            in_specs=in_specs,
            out_specs=out_specs,
            out_shape=out_shape,
            scratch_shapes=scratch,
            compiler_params=params(),
            name="plain_attention",
        )(*args)
        rows = lax.psum_scatter(
            dot_nn(out, w_out).astype(BF), "tp", scatter_dimension=0, tiled=True
        )
        hidden = x_rows.astype(F32) + rows.astype(F32)
        moe_in = (hidden * rms_scale(hidden) * route_gain).astype(BF)
        return out, lse, hidden, moe_in, lax.all_gather(cotangent, "ep")
    block, width = cotangent.shape
    dma = pltpu.SemaphoreType.DMA
    return pl.pallas_call(
        attention_kernel,
        grid=(heads,),
        in_specs=in_specs
        + [
            pl.BlockSpec(w_out.shape, lambda h: (0, 0), pipeline_mode=pl.Buffered(1)), ANY,
            pl.BlockSpec((block, width), lambda h: (0, 0)),
            pl.BlockSpec((1, width), lambda h: (0, 0)),
        ],
        out_specs=out_specs + [pl.BlockSpec((block, width), lambda h: (0, 0))] * 2 + [ANY],
        out_shape=out_shape
        + [
            jax.ShapeDtypeStruct((block, width), F32),
            jax.ShapeDtypeStruct((block, width), BF),
            jax.ShapeDtypeStruct((ep_count, block, width), BF),
        ],
        scratch_shapes=scratch
        + [
            pltpu.VMEM((heads, length, size), BF),
            pltpu.VMEM((tp_count, block, width), BF),
            pltpu.VMEM((2, block, width), BF),
            pltpu.VMEM((block, width), BF),
            dma((2,)), dma((2,)), dma, dma,
        ]
        + gather_sems(),
        compiler_params=params(collective_id=number, has_side_effects=True),
        cost_estimate=link_cost(90.0),
        name="attention",
    )(*args, w_out, cotangent, x_rows, route_gain)


def norm_back(grads, rows, gain):
    scale = rms_scale(rows)
    gain_part = jnp.sum(grads * rows * scale, axis=0, keepdims=True)
    inner = grads * gain
    mean = jnp.mean(inner * rows, axis=-1, keepdims=True)
    return scale * inner - rows * (scale * scale * scale * mean), gain_part


def plain_attention_back_kernel(
    span_ref, q_ref, k_ref, v_ref, grad_ref, lse_ref, cos_ref, sin_ref, qg_ref, kg_ref,
    dq_ref, dk_ref, dv_ref, dqg_ref, dkg_ref,
    bias, k_rot, k_t, dk_acc, dv_acc, dq_t,
):
    factor = q_ref.shape[-1] ** (-0.5)
    cosine, sine = cos_ref[...], sin_ref[...]
    step = pl.program_id(0)

    @pl.when(step == 0)
    def _():
        fill_bias(span_ref, bias)
        k = k_ref[...]
        rotated = turn(k * rms_scale(k) * kg_ref[...], cosine, sine)
        k_rot[...] = rotated.astype(BF)
        k_t[...] = rotated.T.astype(BF)
        dk_acc[...] = jnp.zeros_like(dk_acc)
        dv_acc[...] = jnp.zeros_like(dv_acc)
        dqg_ref[...] = jnp.zeros_like(dqg_ref)

    q = q_ref[...]
    q_rot = turn(q * rms_scale(q) * qg_ref[...], cosine, sine).astype(BF)
    for start, tile, keys in query_tiles(q.shape[0]):
        cols = slice(start, start + tile)
        s = dot_nt(k_rot[:keys, :], q_rot[cols, :]) * factor + bias[:keys, cols]
        p = jnp.exp(s - lse_ref[0, :, cols])
        grad = grad_ref[cols, :]
        dp = dot_nt(v_ref[:keys, :], grad)
        mean = jnp.sum(p * dp, axis=0, keepdims=True)
        raw = (p * (dp - mean) * factor).astype(BF)
        dq_t[:, cols] = dot_nn(k_t[:, :keys], raw)
        dk_acc[:keys, :] += dot_nn(raw, q_rot[cols, :])
        dv_acc[:keys, :] += dot_nn(p.astype(BF), grad)
    back, gain_part = norm_back(turn_back(dq_t[...].T, cosine, sine), q, qg_ref[...])
    dq_ref[...] = back.astype(BF)
    dqg_ref[...] += gain_part

    @pl.when(step == pl.num_programs(0) - 1)
    def _():
        back, gain_part = norm_back(turn_back(dk_acc[...], cosine, sine), k_ref[...], kg_ref[...])
        dk_ref[...] = back.astype(BF)
        dkg_ref[...] = gain_part
        dv_ref[...] = dv_acc[...].astype(BF)


def plain_attention_back(span, q, k, v, grads, lse, cosine, sine, q_gain, k_gain):
    length, size = k.shape
    heads = q.shape[1] // size
    whole = pl.BlockSpec((length, size), lambda h: (0, 0))
    head = pl.BlockSpec((length, size), lambda h: (0, h))
    gain = pl.BlockSpec((1, size), lambda h: (0, 0))
    return pl.pallas_call(
        plain_attention_back_kernel,
        grid=(heads,),
        in_specs=[
            pl.BlockSpec(memory_space=pltpu.SMEM), head, whole, whole, head,
            pl.BlockSpec((1, 1, length), lambda h: (h, 0, 0)), whole, whole, gain, gain,
        ],
        out_specs=[head, whole, whole, gain, gain],
        out_shape=[
            jax.ShapeDtypeStruct((length, heads * size), BF),
            jax.ShapeDtypeStruct((length, size), BF),
            jax.ShapeDtypeStruct((length, size), BF),
            jax.ShapeDtypeStruct((1, size), F32),
            jax.ShapeDtypeStruct((1, size), F32),
        ],
        scratch_shapes=[
            pltpu.VMEM((length, length), F32),
            pltpu.VMEM((length, size), BF),
            pltpu.VMEM((size, length), BF),
            pltpu.VMEM((length, size), F32),
            pltpu.VMEM((length, size), F32),
            pltpu.VMEM((size, length), F32),
        ],
        compiler_params=params(),
        name="plain_attention_back",
    )(span, q, k, v, grads, lse, cosine, sine, q_gain, k_gain)


def attention_back_kernel(
    span_ref, q_ref, k_ref, v_ref, lse_ref, cos_ref, sin_ref, qg_ref, kg_ref,
    w_out_ref, rows_ref, slots_ref, out_a, out_b, hidden_ref,
    dq_ref, dk_ref, dv_ref, dqg_ref, dkg_ref, branch_ref, output_ref,
    bias, k_rot, k_t, dk_acc, dv_acc, dq_t, branch, grads, part, buf, sem,
    own_sem, out_sem, core_send, core_recv, x_send, x_recv, *refs,
):
    factor = q_ref.shape[-1] ** (-0.5)
    size = q_ref.shape[-1]
    cosine, sine = cos_ref[...], sin_ref[...]
    step = pl.program_id(0)
    me = lax.axis_index("tp")
    x, c = me // 2, me % 2
    other_core, other_x = {"tp": x * 2 + 1 - c}, {"tp": (1 - x) * 2 + c}
    reduce = EpReduce(halves(part, 1), BY_Z, refs[:4], refs[4:])
    sums = SlotSums(slots_ref, out_a, out_b, buf, sem)
    order, y = reduce.order, reduce.y
    block = rows_ref.shape[0]
    near_other, far, far_other = x * 2 + 1 - c, (1 - x) * 2 + c, (1 - x) * 2 + 1 - c

    def to_core(slot, src, tp):
        return remote(src, branch.at[tp], core_send.at[slot], core_recv.at[slot], other_core)

    def to_x(tp):
        return remote(rows_ref, branch.at[tp], x_send, x_recv, other_x)

    def own_rows():
        return pltpu.make_async_copy(rows_ref, branch.at[me], own_sem)

    def whole_branch():
        return pltpu.make_async_copy(branch, branch_ref, out_sem)

    @pl.when(step == 0)
    def _():
        greet(reduce.partners() + [(x >= 0, other_core), (x >= 0, other_x)])
        to_x(me).start()
        to_core(0, rows_ref, me).start()
        own_rows().start()
        sums.run([order[k] * 2 + 1 - y for k in range(Z_AXIS)], part, reduce.send_side)
        fill_bias(span_ref, bias)
        k = k_ref[...]
        rotated = turn(k * rms_scale(k) * kg_ref[...], cosine, sine)
        k_rot[...] = rotated.astype(BF)
        k_t[...] = rotated.T.astype(BF)
        dk_acc[...] = jnp.zeros_like(dk_acc)
        dv_acc[...] = jnp.zeros_like(dv_acc)
        dqg_ref[...] = jnp.zeros_like(dqg_ref)

        def head_grads(tp):
            lines = pl.ds(pl.multiple_of(tp * block, block), block)
            rows = dot_nt(branch[tp], w_out_ref[...]).astype(BF)
            for h in range(grads.shape[0]):
                grads[h, lines, :] = rows[:, h * size : (h + 1) * size]

        own_rows().wait()
        head_grads(me)
        to_core(0, rows_ref, near_other).wait_recv()
        head_grads(near_other)
        sums.run([order[k] * 2 + y for k in range(Z_AXIS)], part, lambda k: None)
        reduce.step_y(0)
        to_x(far).wait_recv()
        to_core(1, branch.at[far], far).start()
        head_grads(far)
        to_core(1, branch.at[far], far_other).wait_recv()
        head_grads(far_other)
        whole_branch().start()

    for k, head in ((1, 1), (2, 5)):

        @pl.when(step == head)
        def _(k=k):
            reduce.step_y(k)

    q = q_ref[...]
    q_rot = turn(q * rms_scale(q) * qg_ref[...], cosine, sine).astype(BF)
    for start, tile, keys in query_tiles(q.shape[0]):
        cols = slice(start, start + tile)
        s = dot_nt(k_rot[:keys, :], q_rot[cols, :]) * factor + bias[:keys, cols]
        p = jnp.exp(s - lse_ref[0, :, cols])
        grad = grads[step, cols, :]
        dp = dot_nt(v_ref[:keys, :], grad)
        mean = jnp.sum(p * dp, axis=0, keepdims=True)
        raw = (p * (dp - mean) * factor).astype(BF)
        dq_t[:, cols] = dot_nn(k_t[:, :keys], raw)
        dk_acc[:keys, :] += dot_nn(raw, q_rot[cols, :])
        dv_acc[:keys, :] += dot_nn(p.astype(BF), grad)
    back, gain_part = norm_back(turn_back(dq_t[...].T, cosine, sine), q, qg_ref[...])
    dq_ref[...] = back.astype(BF)
    dqg_ref[...] += gain_part

    @pl.when(step == pl.num_programs(0) - 1)
    def _():
        back, gain_part = norm_back(turn_back(dk_acc[...], cosine, sine), k_ref[...], kg_ref[...])
        dk_ref[...] = back.astype(BF)
        dkg_ref[...] = gain_part
        dv_ref[...] = dv_acc[...].astype(BF)
        reduce.step_y(Z_AXIS - 1)
        pairs = zip(halves(output_ref, 0), halves(hidden_ref, 0))
        for a, (rows, residual) in enumerate(pairs):
            reduce.own(a, lambda terms, rows=rows, residual=residual: add_rows(rows, terms + [residual]))
        reduce.sent()
        whole_branch().wait()
        to_x(me).wait_send()
        to_core(0, rows_ref, me).wait_send()
        to_core(1, branch.at[far], far).wait_send()


def attention_back(
    span, q, k, v, lse, cosine, sine, q_gain, k_gain, w_out, d_rows, slots_t, out, hidden, number
):
    length, size = k.shape
    heads = q.shape[1] // size
    ep_count, tp_count = lax.axis_size("ep"), lax.axis_size("tp")
    if ep_count != 2 * Z_AXIS:
        branch = lax.all_gather(d_rows, "tp", axis=0, tiled=True)
        grads = dot_nt(branch, w_out).astype(BF)
        mine = lax.psum_scatter(out, "ep", scatter_dimension=0)
        back = plain_attention_back(span, q, k, v, grads, lse, cosine, sine, q_gain, k_gain)
        return *back, branch, (hidden + mine.astype(F32)).astype(BF)
    block, width = d_rows.shape
    whole = pl.BlockSpec((length, size), lambda h: (0, 0))
    head = pl.BlockSpec((length, size), lambda h: (0, h))
    gain = pl.BlockSpec((1, size), lambda h: (0, 0))
    rows = pl.BlockSpec((block, width), lambda h: (0, 0))
    dma = pltpu.SemaphoreType.DMA
    *back, branch, output = pl.pallas_call(
        attention_back_kernel,
        grid=(heads,),
        in_specs=[
            pl.BlockSpec(memory_space=pltpu.SMEM), head, whole, whole,
            pl.BlockSpec((1, 1, length), lambda h: (h, 0, 0)), whole, whole, gain, gain,
            pl.BlockSpec(w_out.shape, lambda h: (0, 0), pipeline_mode=pl.Buffered(1)), ANY,
            pl.BlockSpec(slots_t.shape, lambda h: (0, 0, 0), pipeline_mode=pl.Buffered(1)), ANY, ANY,
            pl.BlockSpec((block, width), lambda h: (0, 0), pipeline_mode=pl.Buffered(1)),
        ],
        out_specs=[head, whole, whole, gain, gain, ANY, rows],
        out_shape=[
            jax.ShapeDtypeStruct((length, heads * size), BF),
            jax.ShapeDtypeStruct((length, size), BF),
            jax.ShapeDtypeStruct((length, size), BF),
            jax.ShapeDtypeStruct((1, size), F32),
            jax.ShapeDtypeStruct((1, size), F32),
            jax.ShapeDtypeStruct((tp_count, block, width), BF),
            jax.ShapeDtypeStruct((block, width), BF),
        ],
        scratch_shapes=[
            pltpu.VMEM((length, length), F32),
            pltpu.VMEM((length, size), BF),
            pltpu.VMEM((size, length), BF),
            pltpu.VMEM((length, size), F32),
            pltpu.VMEM((length, size), F32),
            pltpu.VMEM((size, length), F32),
            pltpu.VMEM((tp_count, block, width), BF),
            pltpu.VMEM((heads, length, size), BF),
        ]
        + [pltpu.VMEM((ep_count, block, width), BF)]
        + slot_sums_scratch(slots_t.shape[2], out[0].shape[2], width)
        + [dma, dma, dma((2,)), dma((2,)), dma, dma]
        + reduce_scratch(block, width)
        + reduce_sems(2),
        compiler_params=params(collective_id=number, has_side_effects=True),
        cost_estimate=link_cost(100.0),
        name="attention_back",
    )(span, q, k, v, lse, cosine, sine, q_gain, k_gain, w_out, d_rows, slots_t, *out, hidden)
    return *back, branch.reshape(-1, width), output


def projection_grads_kernel(
    wq_part, wkv_part, wout_part, dq, dkv, wq_hbm, wkv, x_rows, d_hbm, gain, small,
    gq_ref, gk_ref, gv_ref, gout_ref, inputs_grad, gain_grad, small_sum,
    blocks, out_blocks, part, core_rows, far_rows, gain_own, tp_gains, tp_gain, ep_gains, wq, d_hidden,
    core_send, core_recv, x_send, x_recv, wq_sem, d_sem, fill_sem, *refs,
):
    me = lax.axis_index("tp")
    x, c = me // 2, me % 2
    other_core, other_x = {"tp": x * 2 + 1 - c}, {"tp": (1 - x) * 2 + c}
    sums = SumAll(small, small_sum, *refs[:5], refs[5:13])
    over_tp, over_ep = Exchange("tp", refs[13], refs[14]), Exchange("ep", refs[15], refs[16])
    reduce = EpReduce(
        [blocks, out_blocks], BY_Z, refs[17:21], refs[21:]
    )
    order, y = reduce.order, reduce.y
    rows, width = inputs_grad.shape
    nq, nkv = dq.shape[1], dkv.shape[1]

    load_wq = pltpu.make_async_copy(wq_hbm, wq, wq_sem)
    load_d = pltpu.make_async_copy(d_hbm, d_hidden, d_sem)
    everyone = []
    for exchange in (over_tp, over_ep):
        exchange.each(
            lambda i, other, axis=exchange.axis: everyone.append((other >= 0, {axis: other}))
        )
    greet(everyone)

    def fills(j):
        lines = pl.ds(pl.multiple_of(j * rows, rows), rows)
        places = (blocks.at[j, :, 0:nq], blocks.at[j, :, nq : nq + nkv], out_blocks.at[j])
        return [
            pltpu.make_async_copy(ref.at[lines], place, fill_sem.at[j, i])
            for i, (ref, place) in enumerate(zip((wq_part, wkv_part, wout_part), places))
        ]

    def spread_back(tp):
        lines = pl.ds(pl.multiple_of(tp * rows, rows), rows)
        for start in range(0, width, width // 4):
            cols = slice(start, start + width // 4)
            part[tp, :, cols] = (
                dot_nt(dq[lines, :], wq[cols, :]) + dot_nt(dkv[lines, :], wkv[cols, :])
            ).astype(BF)

    def to_core(xt):
        return remote(
            part.at[xt * 2 + 1 - c], core_rows.at[xt], core_send.at[xt], core_recv.at[xt], other_core
        )

    far, near = part.at[(1 - x) * 2 + c], part.at[x * 2 + c]
    to_x = remote(far, far_rows, x_send, x_recv, other_x)

    sides = [order[k] * 2 + 1 - y for k in range(Z_AXIS)]
    owns = [order[k] * 2 + y for k in range(Z_AXIS)]
    for j in sides:
        for copy in fills(j):
            copy.start()
    load_wq.start()
    for j in owns:
        for copy in fills(j):
            copy.start()
    load_d.start()
    for k, j in enumerate(sides):
        for copy in fills(j):
            copy.wait()
        reduce.send_side(k)
    load_wq.wait()
    spread_back((1 - x) * 2 + 1 - c)
    to_core(1 - x).start()
    spread_back((1 - x) * 2 + c)
    to_core(1 - x).wait_recv()
    add_rows(far, [far, core_rows.at[1 - x]])
    to_x.start()
    sums.start()
    for j in owns:
        for copy in fills(j):
            copy.wait()
    spread_back(x * 2 + 1 - c)
    to_core(x).start()
    spread_back(x * 2 + c)
    reduce.step_y(0)
    sums.across()
    load_d.wait()
    to_core(x).wait_recv()
    reduce.step_y(1)
    to_x.wait_recv()

    chunk = 32
    gain_own[...] = jnp.zeros_like(gain_own)

    @pl.loop(0, rows // chunk)
    def _(i):
        lines = pl.ds(pl.multiple_of(i * chunk, chunk), chunk)
        grad = near[lines, :].astype(F32) + core_rows[x, lines, :].astype(F32)
        grad = grad + far_rows[lines, :].astype(F32)
        back, gain_part = norm_back(grad, x_rows[lines, :].astype(F32), gain[...])
        inputs_grad[lines, :] = d_hidden[lines, :] + back
        gain_own[...] += gain_part

    over_tp.start(lambda t: gain_own, tp_gains)
    tp_gains[pl.ds(over_tp.me, 1)] = gain_own[...][None]
    sums.back()
    reduce.step_y(2)
    sums.home()
    over_tp.arrived(tp_gains)
    tp_gain[...] = jnp.sum(tp_gains[...], axis=0)
    over_ep.start(lambda e: tp_gain, ep_gains)
    ep_gains[pl.ds(over_ep.me, 1)] = tp_gain[...][None]
    reduce.step_y(3)

    def total_of(terms, lines):
        value = terms[0][lines, :].astype(F32)
        for term in terms[1:]:
            value = value + term[lines, :].astype(F32)
        return value

    over_ep.arrived(ep_gains)
    gain_grad[...] = jnp.sum(ep_gains[...], axis=0)
    def write(terms):
        for start in range(0, rows, 64):
            lines = slice(start, start + 64)
            value = total_of(terms, lines)
            gq_ref[lines, :] = value[:, 0:nq]
            gk_ref[lines, :] = value[:, nq : nq + nkv // 2]
            gv_ref[lines, :] = value[:, nq + nkv // 2 :]

    def write_out(terms):
        for start in range(0, rows, 128):
            lines = slice(start, start + 128)
            gout_ref[:, lines] = total_of(terms, lines).T

    reduce.own(0, write)
    reduce.own(1, write_out)
    reduce.sent()
    to_core(1 - x).wait_send()
    to_core(x).wait_send()
    to_x.wait_send()
    over_tp.sent(lambda t: gain_own, tp_gains)
    over_ep.sent(lambda e: tp_gain, ep_gains)
    sums.finish()


def projection_grads(
    normed, dq, dk, dv, heads, branch, wq, wk, wv, x_rows, d_hidden, gain, small_values, number
):
    rows, width = x_rows.shape
    ep_count, tp_count = lax.axis_size("ep"), lax.axis_size("tp")
    small = pack_small(small_values, tp_count, ep_count)
    if ep_count != 2 * Z_AXIS:

        def over_sequences(part, dim):
            return lax.psum_scatter(
                part.astype(BF), "ep", scatter_dimension=dim, tiled=True
            ).astype(F32)

        d_normed = (dot_nt(dq, wq) + dot_nt(dk, wk) + dot_nt(dv, wv)).astype(BF)
        d_mine = lax.psum_scatter(d_normed, "tp", scatter_dimension=0, tiled=True)
        back, gain_part = norm_back(d_mine.astype(F32), x_rows.astype(F32), gain)
        gain_sum, small_sum = lax.psum((gain_part, small), ("ep", "tp"))
        return (
            over_sequences(dot_tn(normed, dq), 0),
            over_sequences(dot_tn(normed, dk), 0),
            over_sequences(dot_tn(normed, dv), 0),
            over_sequences(dot_tn(heads, branch), 1),
            d_hidden + back,
            gain_sum,
            unpack_small(small_sum, small_values),
        )
    nq, nk = dq.shape[1], dk.shape[1]
    nh = heads.shape[1]
    dkv = jnp.concatenate([dk, dv], axis=1)
    parts = [dot_tn(a, b).astype(BF) for a, b in ((normed, dq), (normed, dkv), (branch, heads))]
    vmem = pl.BlockSpec(memory_space=pltpu.VMEM)
    dma = pltpu.SemaphoreType.DMA
    *grads, small_sum = pl.pallas_call(
        projection_grads_kernel,
        in_specs=[ANY] * 3 + [vmem] * 2 + [ANY] + [vmem] * 2 + [ANY] + [vmem] * 2,
        out_specs=[vmem] * 7,
        out_shape=[
            jax.ShapeDtypeStruct((rows, nq), F32),
            jax.ShapeDtypeStruct((rows, nk), F32),
            jax.ShapeDtypeStruct((rows, nk), F32),
            jax.ShapeDtypeStruct((nh, rows), F32),
            jax.ShapeDtypeStruct((rows, width), F32),
            jax.ShapeDtypeStruct((1, width), F32),
            jax.ShapeDtypeStruct(small.shape, F32),
        ],
        scratch_shapes=[
            pltpu.VMEM((ep_count, rows, nq + 2 * nk), BF),
            pltpu.VMEM((ep_count, rows, nh), BF),
            pltpu.VMEM((tp_count, rows, width), BF),
            pltpu.VMEM((2, rows, width), BF),
            pltpu.VMEM((rows, width), BF),
            pltpu.VMEM((1, width), F32),
            pltpu.VMEM((tp_count, 1, width), F32),
            pltpu.VMEM((1, width), F32),
            pltpu.VMEM((ep_count, 1, width), F32),
            pltpu.VMEM(wq.shape, BF),
            pltpu.VMEM((rows, width), F32),
            dma((2,)), dma((2,)), dma, dma, dma, dma, dma((ep_count, 3)),
        ]
        + sum_scratch(small.shape)
        + exchange_sems("tp")
        + exchange_sems("ep")
        + [pltpu.VMEM((n, rows, c), BF) for c in (nq + 2 * nk, nh) for n in (Z_AXIS, Z_AXIS + 1)]
        + reduce_sems(2),
        compiler_params=params(collective_id=number, has_side_effects=True),
        cost_estimate=link_cost(110.0),
        name="projection_grads",
    )(*parts, dq, dkv, wq, jnp.concatenate([wk, wv], axis=1), x_rows, d_hidden, gain, small)
    return *grads, unpack_small(small_sum, small_values)


def select_kernel(slot_ref, x_ref, c_ref, xs_ref, cs_ref):
    local, _, capacity, width = xs_ref.shape
    rows = x_ref.shape[1]
    place = jnp.concatenate(
        [
            (
                slot_ref[0, e : e + 1, :]
                == lax.broadcasted_iota(jnp.int32, (capacity, rows), 0)
            ).astype(F32)
            for e in range(local)
        ],
        axis=0,
    ).astype(BF)
    xs_ref[...] = dot_nn(place, x_ref[0]).astype(BF).reshape(xs_ref.shape)
    cs_ref[...] = dot_nn(place, c_ref[0]).astype(BF).reshape(cs_ref.shape)


def select_rows(slots, tokens, cots, capacity):
    blocks, local, rows = slots.shape
    width = tokens.shape[-1]
    block = pl.BlockSpec((1, rows, width), lambda b: (b, 0, 0))
    out = pl.BlockSpec((local, 1, capacity, width), lambda b: (0, b, 0, 0))
    shape = jax.ShapeDtypeStruct((local, blocks, capacity, width), BF)
    return pl.pallas_call(
        select_kernel,
        grid=(blocks,),
        in_specs=[pl.BlockSpec((1, local, rows), lambda b: (b, 0, 0)), block, block],
        out_specs=[out, out],
        out_shape=[shape, shape],
        compiler_params=params(),
        name="select_rows",
    )(slots, tokens, cots)


def pack_kernel(gate_ref, up_ref, down_ref, out_ref):
    for kind, ref in enumerate((gate_ref, up_ref, down_ref)):
        out_ref[kind, 0] = ref[0]


def pack_weights(weights, first, count):
    _, hidden, width = weights[0].shape
    block = pl.BlockSpec((1, hidden, width), lambda e: (first + e, 0, 0))
    return pl.pallas_call(
        pack_kernel,
        grid=(count,),
        in_specs=[block] * 3,
        out_specs=pl.BlockSpec((3, 1, hidden, width), lambda e: (0, e, 0, 0)),
        out_shape=jax.ShapeDtypeStruct((3, count, hidden, width), BF),
        compiler_params=params(),
        name="pack_weights",
    )(*weights)


def expert_kernel(
    x_ref, c_ref, w_ref, gate_ref, out_ref, dx_ref, act_ref, dg_ref, du_ref, dgate_ref
):
    width = x_ref.shape[-1]
    x, c = x_ref[0], c_ref[0]
    w_gate = w_ref[:, 0, 0].reshape(-1, width)
    w_up = w_ref[:, 1, 0].reshape(-1, width)
    w_down = w_ref[:, 2, 0].reshape(-1, width)
    gate = gate_ref[0]
    gate_pre = dot_nt(x, w_gate)
    up_pre = dot_nt(x, w_up)
    raw = dot_nt(c, w_down)
    sig = jax.nn.sigmoid(gate_pre)
    silu = gate_pre * sig
    act = silu * up_pre
    dgate_ref[0] = jnp.sum(act * raw, axis=-1, keepdims=True)
    act_low = (act * gate).astype(BF)
    d_act = raw * gate
    d_gate = (d_act * up_pre * sig * (1.0 + gate_pre * (1.0 - sig))).astype(BF)
    d_up = (d_act * silu).astype(BF)
    act_ref[0] = act_low
    dg_ref[0] = d_gate
    du_ref[0] = d_up
    out_ref[0] = dot_nn(act_low, w_down).astype(BF)
    dx_ref[0] = (dot_nn(d_gate, w_gate) + dot_nn(d_up, w_up)).astype(BF)


def experts_both_ways(x_slots, c_slots, w_all, slot_gate, first):
    _, number, width = x_slots.shape
    parts, _, local, hidden, _ = w_all.shape
    tile = number // 2
    taken = pl.BlockSpec((1, tile, width), lambda e, i: (first + e, i, 0))
    wide = pl.BlockSpec((1, tile, width), lambda e, i: (e, i, 0))
    mid = pl.BlockSpec((1, tile, parts * hidden), lambda e, i: (e, i, 0))
    thin = pl.BlockSpec((1, tile, 1), lambda e, i: (e, i, 0))
    wide_shape = jax.ShapeDtypeStruct((local, number, width), BF)
    mid_shape = jax.ShapeDtypeStruct((local, number, parts * hidden), BF)
    return pl.pallas_call(
        expert_kernel,
        grid=(local, 2),
        in_specs=[
            taken, taken,
            pl.BlockSpec((parts, 3, 1, hidden, width), lambda e, i: (0, 0, e, 0, 0)),
            pl.BlockSpec((1, tile, 1), lambda e, i: (first + e, i, 0)),
        ],
        out_specs=[wide, wide, mid, mid, mid, thin],
        out_shape=[
            wide_shape, wide_shape, mid_shape, mid_shape, mid_shape,
            jax.ShapeDtypeStruct((local, number, 1), F32),
        ],
        compiler_params=params(),
        name="experts_both_ways",
    )(x_slots, c_slots, w_all, slot_gate)


def expert_grads_kernel(x_ref, c_ref, act_ref, dg_ref, du_ref, out_ref):
    parts, _, _, hidden, width = out_ref.shape
    x, c = x_ref[0], c_ref[0]
    out_ref[:, 0, 0] = dot_tn(dg_ref[0], x).astype(BF).reshape(parts, hidden, width)
    out_ref[:, 1, 0] = dot_tn(du_ref[0], x).astype(BF).reshape(parts, hidden, width)
    out_ref[:, 2, 0] = dot_tn(act_ref[0], c).astype(BF).reshape(parts, hidden, width)


def expert_grads(x_slots, c_slots, act, d_gate, d_up, parts, first):
    local, number, inner = act.shape
    width = x_slots.shape[-1]
    wide = pl.BlockSpec((1, number, width), lambda e: (first + e, 0, 0))
    mid = pl.BlockSpec((1, number, inner), lambda e: (e, 0, 0))
    return pl.pallas_call(
        expert_grads_kernel,
        grid=(local,),
        in_specs=[wide, wide, mid, mid, mid],
        out_specs=pl.BlockSpec(
            (parts, 3, 1, inner // parts, width), lambda e: (0, 0, e, 0, 0)
        ),
        out_shape=jax.ShapeDtypeStruct((parts, 3, local, inner // parts, width), BF),
        compiler_params=params(),
        name="expert_grads",
    )(x_slots, c_slots, act, d_gate, d_up)


def combine_kernel(
    first_ref, slot_ref, dxa_ref, dxb_ref, outa_ref, outb_ref, dgate_ref, dx_sum_ref, out_sum_ref, pay_ref
):
    _, _, capacity, width = dxa_ref.shape
    local = slot_ref.shape[2]
    rows = slot_ref.shape[1]
    lane = lax.broadcasted_iota(jnp.int32, (rows, local * capacity), 1)
    half = pay_ref.shape[2] // 2
    column = lax.broadcasted_iota(jnp.int32, (rows, 2 * half), 1)
    total = jnp.zeros((rows, local * capacity), F32)
    pay = jnp.zeros(column.shape, F32)
    for e in range(local):
        hit = lane == slot_ref[0, :, e : e + 1] + e * capacity
        total = jnp.where(hit, 1.0, total)
        value = jnp.sum(jnp.where(hit, dgate_ref[0], 0.0), axis=1, keepdims=True)
        high = value.astype(BF).astype(F32)
        pay = jnp.where(column == first_ref[0, 0] + e, high, pay)
        pay = jnp.where(column == first_ref[0, 0] + e + half, value - high, pay)
    place = total.astype(BF)

    def both(a_ref, b_ref):
        pair = [ref[...].reshape(-1, width) for ref in (a_ref, b_ref)]
        return dot_nn(place, jnp.concatenate(pair, axis=0)).astype(BF)

    dx_sum_ref[0] = both(dxa_ref, dxb_ref)
    out_sum_ref[0] = both(outa_ref, outb_ref)
    pay_ref[0] = pay.astype(BF)


def combine_rows(first, slots_t, dx, out, d_gate_slots, experts):
    blocks, rows, local = slots_t.shape
    _, _, capacity, width = dx[0].shape
    lanes = -(-2 * experts // 128) * 128
    slot = pl.BlockSpec((local // 2, 1, capacity, width), lambda b: (0, b, 0, 0))
    block = pl.BlockSpec((1, rows, width), lambda b: (b, 0, 0))
    shape = jax.ShapeDtypeStruct((blocks, rows, width), BF)
    return pl.pallas_call(
        combine_kernel,
        grid=(blocks,),
        in_specs=[
            pl.BlockSpec(memory_space=pltpu.SMEM),
            pl.BlockSpec((1, rows, local), lambda b: (b, 0, 0)), slot, slot, slot, slot,
            pl.BlockSpec((1, 1, local * capacity), lambda b: (b, 0, 0)),
        ],
        out_specs=[block, block, pl.BlockSpec((1, rows, lanes), lambda b: (b, 0, 0))],
        out_shape=[shape, shape, jax.ShapeDtypeStruct((blocks, rows, lanes), BF)],
        compiler_params=params(),
        name="combine_rows",
    )(first, slots_t, *dx, *out, d_gate_slots)


def on_device(
    inputs,
    attn_gain,
    w_query,
    key_weight_matrix,
    value_weight_matrix,
    query_gain,
    key_gain,
    w_out,
    route_gain,
    w_router,
    w_gate,
    w_up,
    w_down,
    routes,
    image_starts,
    cotangent,
):
    tp_count = lax.axis_size("tp")
    ep_count = lax.axis_size("ep")
    tp_index = lax.axis_index("tp")
    ep_index = lax.axis_index("ep")
    length = inputs.shape[0]
    width = inputs.shape[1]
    rows = cotangent.shape[0]
    head_dim = query_gain.shape[0]
    local_experts = w_gate.shape[0]
    experts = local_experts * ep_count
    top = routes.shape[1]
    capacity = -(-(3 * rows * top // (2 * experts)) // 16) * 16

    pair = local_experts // 2

    weights = (w_gate.transpose(0, 2, 1), w_up.transpose(0, 2, 1), w_down)
    w_first = lax.all_gather(pack_weights(weights, 0, pair), "tp")

    normed, queries, key_rows, values = project(
        inputs, attn_gain[None], w_query, key_weight_matrix, value_weight_matrix
    )
    cosine, sine = rope_tables(length, head_dim)
    q_gain, k_gain = query_gain[None], key_gain[None]
    x_rows = lax.dynamic_slice_in_dim(inputs, tp_index * rows, rows, 0)
    queries, second = lax.optimization_barrier((queries, pack_weights(weights, pair, pair)))
    w_second = lax.all_gather(second, "tp")
    heads, lse, hidden, moe_in, cot_all = attention(
        image_starts, queries, key_rows, values, cosine, sine, q_gain, k_gain,
        w_out, cotangent, x_rows, route_gain[None], 0,
    )
    logits = dot_nn(moe_in, w_router)
    router_probs = plain_softmax(logits)
    expert_ids = jnp.arange(experts, dtype=jnp.int32)
    ring_routes = lax.dynamic_index_in_dim(
        routes.reshape(ep_count, tp_count, rows, top), tp_index, 1, keepdims=False
    )
    my_routes = lax.dynamic_index_in_dim(ring_routes, ep_index, 0, keepdims=False)

    def routed_softmax(scores, picked):
        kept = jnp.where(picked, scores, MASKED)
        expo = jnp.where(picked, jnp.exp(kept - jnp.max(kept, axis=-1, keepdims=True)), 0.0)
        return expo / jnp.sum(expo, axis=-1, keepdims=True)

    my_pick = jnp.any(my_routes[:, :, None] == expert_ids[None, None, :], axis=1)
    gates = routed_softmax(logits, my_pick)
    all_pick = jnp.any(ring_routes[..., None] == expert_ids, axis=2)
    mask = lax.dynamic_slice_in_dim(all_pick, ep_index * local_experts, local_experts, 2)
    earlier = (jnp.arange(rows)[:, None] > jnp.arange(rows)[None, :]).astype(BF)
    slots_t = jnp.einsum(
        "tu,bue->bte", earlier, mask.astype(BF), preferred_element_type=F32
    ).astype(jnp.int32)
    slots_t = jnp.where(mask, slots_t, NOWHERE)
    slots = slots_t.transpose(0, 2, 1)
    ring = ep_count == 2 * Z_AXIS
    if ring:
        turned = lax.rem(expert_ids + ep_index * local_experts, experts)
        x_slots, c_slots, slot_gate = gather_select(
            moe_in,
            cot_all,
            slots,
            all_pick.astype(jnp.int32)[..., turned].transpose(0, 2, 1),
            w_router.T[turned],
            capacity,
            1,
        )
        slot_gate = slot_gate.reshape(local_experts, ep_count * capacity, 1)
    else:
        tokens_all = lax.all_gather(moe_in, "ep")
        logits_all = dot_nn(tokens_all.reshape(-1, width), w_router).reshape(ep_count, rows, experts)
        gate_of = lax.dynamic_slice_in_dim(
            routed_softmax(logits_all, all_pick), ep_index * local_experts, local_experts, 2
        )
        place = slots[:, :, None, :] == jnp.arange(capacity, dtype=jnp.int32)[:, None]
        slot_gate = jnp.sum(
            jnp.where(place, gate_of.transpose(0, 2, 1)[:, :, None, :], 0.0), axis=-1
        )
        slot_gate = slot_gate.transpose(1, 0, 2).reshape(local_experts, ep_count * capacity, 1)
        x_slots, c_slots = select_rows(slots, tokens_all, cot_all, capacity)
    flat = (local_experts, ep_count * capacity, width)
    x_slots, c_slots = x_slots.reshape(flat), c_slots.reshape(flat)

    def over_rings(grads):
        return lax.psum_scatter(grads.reshape(-1, width), "tp", scatter_dimension=0, tiled=True)

    out_a, dx_a, *inner_a, dg_a = experts_both_ways(x_slots, c_slots, w_first, slot_gate, 0)
    grads_a = expert_grads(x_slots, c_slots, *inner_a, tp_count, 0)
    x_slots, grads_a = lax.optimization_barrier((x_slots, grads_a))
    mine_a = over_rings(grads_a)
    out_b, dx_b, *inner_b, dg_b = experts_both_ways(x_slots, c_slots, w_second, slot_gate, pair)
    deep = (pair, ep_count, capacity, width)
    dx_slots = [dx_a.reshape(deep), dx_b.reshape(deep)]
    out_slots = [out_a.reshape(deep), out_b.reshape(deep)]
    d_gate_slots = (
        jnp.concatenate([dg_a, dg_b])
        .reshape(local_experts, ep_count, capacity)
        .transpose(1, 0, 2)
        .reshape(ep_count, 1, local_experts * capacity)
    )
    counts = jnp.sum((routes[:, :, None] == expert_ids[None, None, :]).astype(F32), axis=(0, 1))
    total_tokens = routes.shape[0]
    share = counts / (total_tokens * top)
    coeff = AUX * experts * share
    if ring:
        d_hidden, d_rows, router_part, route_gain_part, grads_b = input_grads(
            slots_t, d_gate_slots, dx_slots, x_slots, c_slots, inner_b,
            [
                hidden, moe_in, cotangent, route_gain[None], gates, router_probs,
                coeff[None], w_router.T,
            ],
            experts, tp_count, 2,
        )
    else:
        grads_b = expert_grads(x_slots, c_slots, *inner_b, tp_count, pair)
        dx_part, out_slots, gate_part = combine_rows(
            (ep_index * local_experts).reshape(1, 1), slots_t, dx_slots, out_slots, d_gate_slots, experts
        )
        dx_mine = lax.psum_scatter(dx_part, "ep", scatter_dimension=0).astype(F32)
        gate_mine = lax.psum_scatter(gate_part, "ep", scatter_dimension=0).astype(F32)
        lanes = gate_mine.shape[1] // 2
        d_gates = gate_mine[:, :experts] + gate_mine[:, lanes : lanes + experts]
        d_logits = gates * (d_gates - jnp.sum(gates * d_gates, axis=-1, keepdims=True))
        d_logits = d_logits + router_probs * (
            coeff - jnp.sum(router_probs * coeff, axis=-1, keepdims=True)
        )
        d_low = d_logits.astype(BF)
        router_part = dot_tn(d_low, moe_in)
        d_moe = dot_nt(d_low, w_router) + dx_mine
        back, route_gain_part = norm_back(d_moe, hidden, route_gain[None])
        d_hidden = cotangent.astype(F32) + back
        d_rows = d_hidden.astype(BF)
    d_rows, mine_a, grads_b = lax.optimization_barrier((d_rows, mine_a, grads_b))
    mine_b = over_rings(grads_b)
    mine_a, mine_b = [m.reshape(3, pair, -1, width) for m in (mine_a, mine_b)]
    w_gate_grad, w_up_grad, w_down_grad = widen_grads(mine_a, mine_b)
    w_gate_grad, w_up_grad = w_gate_grad.transpose(0, 2, 1), w_up_grad.transpose(0, 2, 1)
    prob_local = jnp.sum(router_probs, axis=0)
    d_queries, d_keys, d_values, query_gain_part, key_gain_part, d_branch, output = attention_back(
        image_starts, queries, key_rows, values, lse, cosine, sine, q_gain, k_gain,
        w_out, d_rows, slots_t, out_slots, hidden, 3,
    )
    w_query_grad, w_key_grad, w_value_grad, w_out_grad, inputs_grad, attn_gain_grad, small = projection_grads(
        normed, d_queries, d_keys, d_values, heads, d_branch,
        w_query, key_weight_matrix, value_weight_matrix,
        x_rows, d_hidden, attn_gain[None],
        [router_part, route_gain_part[0], query_gain_part[0], key_gain_part[0], prob_local],
        5,
    )
    w_router_grad, route_gain_grad, query_gain_grad, key_gain_grad, prob_all = small
    w_router_grad = w_router_grad.T
    attn_gain_grad = attn_gain_grad[0]
    aux_loss = experts * jnp.sum(share * (prob_all / total_tokens))
    return (
        output,
        aux_loss,
        inputs_grad,
        attn_gain_grad,
        w_query_grad,
        w_key_grad,
        w_value_grad,
        query_gain_grad,
        key_gain_grad,
        w_out_grad,
        route_gain_grad,
        w_router_grad,
        w_gate_grad,
        w_up_grad,
        w_down_grad,
    )


def solution(mesh):
    return jax.shard_map(
        on_device,
        mesh=mesh,
        in_specs=(
            P("ep", None),
            P(),
            P(None, "tp"),
            P(None, "tp"),
            P(None, "tp"),
            P(),
            P(),
            P("tp", None),
            P(),
            P(),
            P("ep", None, "tp"),
            P("ep", None, "tp"),
            P("ep", "tp", None),
            P(),
            P("ep", None),
            P(("ep", "tp"), None),
        ),
        out_specs=(
            P(("ep", "tp"), None),
            P(),
            P(("ep", "tp"), None),
            P(),
            P("ep", "tp"),
            P("ep", "tp"),
            P("ep", "tp"),
            P(),
            P(),
            P("tp", "ep"),
            P(),
            P(),
            P("ep", None, "tp"),
            P("ep", None, "tp"),
            P("ep", "tp", None),
        ),
        check_vma=False,
    )
```

```python
import functools

import jax
import jax.numpy as jnp
import numpy as np
from jax import lax
from jax.experimental import pallas as pl
from jax.experimental.pallas import tpu as pltpu
from jax.sharding import PartitionSpec as P

IMG = 256
EPS = 1e-06
AUX = 0.04
THETA = 1000000.0
MASKED = -1e30
NOWHERE = -(1 << 20)
BF = jnp.bfloat16
F32 = jnp.float32
VMEM_BYTES = 60 * 1024 * 1024


def dot_nn(a, b):
    return lax.dot_general(a, b, (((1,), (0,)), ((), ())), preferred_element_type=F32)


def dot_nt(a, b):
    return lax.dot_general(a, b, (((1,), (1,)), ((), ())), preferred_element_type=F32)


def dot_tn(a, b):
    return lax.dot_general(a, b, (((0,), (0,)), ((), ())), preferred_element_type=F32)


def params(**kw):
    return pltpu.CompilerParams(vmem_limit_bytes=VMEM_BYTES, **kw)


def rms_scale(value_rows):
    return lax.rsqrt(jnp.mean(value_rows * value_rows, axis=-1, keepdims=True) + EPS)


def plain_softmax(value_rows):
    top = jnp.max(value_rows, axis=-1, keepdims=True)
    expo = jnp.exp(value_rows - top)
    return expo / jnp.sum(expo, axis=-1, keepdims=True)


def rope_tables(length, size):
    half = size // 2
    freq = THETA ** (-2.0 * np.arange(half) / size)
    angle = np.arange(length)[:, None] * freq[None, :]
    cosine, sine = np.cos(angle), np.sin(angle)
    tables = (np.concatenate([cosine, cosine], axis=-1), np.concatenate([-sine, sine], axis=-1))
    return tuple(jnp.asarray(t, F32) for t in tables)


def turn(rows, cosine, sine):
    return rows * cosine + pltpu.roll(rows, rows.shape[-1] // 2, 1) * sine


def turn_back(rows, cosine, sine):
    return rows * cosine - pltpu.roll(rows, rows.shape[-1] // 2, 1) * sine


MESH = pl.DeviceIdType.MESH
ANY = pl.BlockSpec(memory_space=pl.ANY)
Z_AXIS = 4


def link_cost(us):
    return pl.CostEstimate(flops=0, bytes_accessed=int(us * 3.0e6), transcendentals=0)


def greet(partners):
    barrier = pltpu.get_barrier_semaphore()
    count = 0
    for there, device in partners:
        flag = jnp.asarray(there, jnp.int32)

        @pl.when(there)
        def _(device=device):
            pl.semaphore_signal(barrier, inc=1, device_id=device, device_id_type=MESH)

        count = count + flag
    pl.semaphore_wait(barrier, count)


def remote(src, dst, send, recv, device):
    return pltpu.make_async_remote_copy(
        src_ref=src, dst_ref=dst, send_sem=send, recv_sem=recv, device_id=device, device_id_type=MESH
    )


def ring_place():
    me = lax.axis_index("ep")
    z, y = me // 2, me % 2
    return me, z, y, {"ep": me + 2}, {"ep": me - 2}, {"ep": me + 1 - 2 * y}


def ring_pieces(ref, axis):
    unit = ref.shape[axis] // 16
    lead = (slice(None),) * axis
    return [
        ref.at[lead + (pl.ds(start * unit, count * unit),)]
        for start, count in ((0, 7), (7, 6), (13, 3))
    ]


class EpGather:
    def __init__(self, ins, outs, sems):
        self.ins, self.outs = ins, outs
        self.own_sem, self.up_send, self.up_recv, self.dn_send, self.dn_recv = sems[:5]
        self.y_send, self.y_recv = sems[5:]
        self.me, self.z, self.y, self.up, self.down, self.beside = ring_place()
        self.last = len(ins) - 1
        self.streams = [(a, a, self.y) for a in range(len(ins))]
        self.other = (self.last, len(ins), 1 - self.y)

    def partners(self):
        z = self.z
        return [(z < Z_AXIS - 1, self.up), (z > 0, self.down), (z >= 0, self.beside)]

    def block(self, a, zt, y):
        return self.outs[a].at[zt * 2 + y]

    def upward(self, src, stream, zt):
        a, i, y = stream
        return remote(src, self.block(a, zt, y), self.up_send.at[i, zt], self.up_recv.at[i, zt], self.up)

    def downward(self, src, stream, zt):
        a, i, y = stream
        return remote(src, self.block(a, zt, y), self.dn_send.at[i, zt], self.dn_recv.at[i, zt], self.down)

    def sideways(self, src, a, zt):
        return remote(
            src, self.block(a, zt, self.y), self.y_send.at[a, zt], self.y_recv.at[a, zt], self.beside
        )

    def both_ways(self, src, stream):
        z = self.z

        @pl.when(z < Z_AXIS - 1)
        def _():
            self.upward(src, stream, z).start()

        @pl.when(z > 0)
        def _():
            self.downward(src, stream, z).start()

    def start(self):
        self.sideways(self.ins[self.last], self.last, self.z).start()
        for stream in self.streams:
            a = stream[0]
            self.both_ways(self.ins[a], stream)
            if a != self.last:
                self.sideways(self.ins[a], a, self.z).start()
            pltpu.make_async_copy(self.ins[a], self.block(a, self.z, self.y), self.own_sem.at[a]).start()

    def cross(self):
        self.side_arrived(self.last, self.z)
        self.both_ways(self.block(self.last, self.z, 1 - self.y), self.other)

    def hop(self, d):
        z = self.z
        for stream in [self.other] + self.streams:
            a, _, y = stream

            @pl.when(z >= d)
            def _(a=a, y=y, stream=stream, zt=z - d):
                rows = self.block(a, zt, y)
                self.upward(rows, stream, zt).wait_recv()

                @pl.when(z < Z_AXIS - 1)
                def _():
                    self.upward(rows, stream, zt).start()

                if a != self.last:
                    self.sideways(rows, a, zt).start()

            @pl.when(z + d < Z_AXIS)
            def _(a=a, y=y, stream=stream, zt=z + d):
                rows = self.block(a, zt, y)
                self.downward(rows, stream, zt).wait_recv()

                @pl.when(z > 0)
                def _():
                    self.downward(rows, stream, zt).start()

                if a != self.last:
                    self.sideways(rows, a, zt).start()

    def own_done(self):
        for a, x in enumerate(self.ins):
            pltpu.make_async_copy(x, self.block(a, self.z, self.y), self.own_sem.at[a]).wait()

    def side_arrived(self, a, zt):
        rows = self.block(a, zt, 1 - self.y)
        remote(rows, rows, self.y_send.at[a, zt], self.y_recv.at[a, zt], self.beside).wait_recv()

    def side_done(self, zt):
        for a in range(self.last):
            self.side_arrived(a, zt)

    def sent(self):
        z = self.z
        self.sideways(self.block(self.last, z, self.y), self.last, z).wait_send()
        for stream in self.streams + [self.other]:
            a, _, y = stream
            for zt in range(Z_AXIS):
                src = self.block(a, zt, y)
                if a != self.last:
                    self.sideways(src, a, zt).wait_send()

                @pl.when((zt <= z) & (z < Z_AXIS - 1))
                def _(src=src, zt=zt, stream=stream):
                    self.upward(src, stream, zt).wait_send()

                @pl.when((zt >= z) & (z > 0))
                def _(src=src, zt=zt, stream=stream):
                    self.downward(src, stream, zt).wait_send()

    def finish(self):
        self.own_done()
        for zt in range(Z_AXIS):
            self.side_done(zt)
        self.sent()


def gather_sems():
    dma = pltpu.SemaphoreType.DMA
    return [dma((3,))] + [dma((4, Z_AXIS))] * 6


def one_hot(slots, capacity):
    local, rows = slots.shape
    slot = lax.broadcasted_iota(jnp.int32, (capacity, rows), 0)
    return [slot == slots[e : e + 1, :] for e in range(local)]


def gather_select_kernel(
    x_ref, cots_ref, slots_ref, picks_ref, router_ref, xs_ref, cs_ref, gate_ref,
    tokens, cots, chosen, load_sem, store_sem, *sems,
):
    local, _, capacity, width = xs_ref.shape
    blocks = tokens.shape[0]
    gather = EpGather(ring_pieces(x_ref, 0), ring_pieces(tokens, 1), sems)
    z, y = gather.z, gather.y
    greet(gather.partners())
    gather.start()

    def chosen_rows(j, rows):
        hits = one_hot(slots_ref[j], capacity)
        place = jnp.concatenate([h.astype(F32) for h in hits], axis=0).astype(BF)
        return dot_nn(place, rows).astype(BF).reshape(local, capacity, width), hits

    def load(j, slot):
        return pltpu.make_async_copy(cots_ref.at[j], cots.at[slot], load_sem.at[slot])

    def store(to, j, slot):
        return pltpu.make_async_copy(chosen.at[slot], to.at[:, j], store_sem.at[slot])

    load(0, 0).start()

    @pl.loop(0, blocks)
    def _(j):
        slot = lax.rem(j, 2)

        @pl.when(j + 1 < blocks)
        def _():
            load(j + 1, 1 - slot).start()

        load(j, slot).wait()

        @pl.when(j == 3)
        def _():
            gather.cross()

        @pl.when(j >= 2)
        def _():
            store(cs_ref, j - 2, slot).wait()

        chosen[slot] = chosen_rows(j, cots[slot])[0]
        store(cs_ref, j, slot).start()

    store(cs_ref, blocks - 2, 0).wait()
    store(cs_ref, blocks - 1, 1).wait()

    def take(j):
        rows = tokens[j]
        chosen[0], hits = chosen_rows(j, rows)
        copy = store(xs_ref, j, 0)
        copy.start()
        logits = dot_nt(router_ref[...], rows)
        picked = picks_ref[j] > 0
        kept = jnp.where(picked, logits, MASKED)
        expo = jnp.exp(kept - jnp.max(kept, axis=0, keepdims=True))
        expo = jnp.where(picked, expo, 0.0)
        gates = expo / jnp.sum(expo, axis=0, keepdims=True)
        for e, hit in enumerate(hits):
            gate_ref[e, j] = jnp.sum(jnp.where(hit, gates[e : e + 1, :], 0.0), axis=1, keepdims=True)
        copy.wait()

    gather.own_done()
    take(gather.me)
    for d in range(1, Z_AXIS + 1):
        if d < Z_AXIS:
            gather.hop(d)

        @pl.loop(0, 4)
        def _(i, d=d):
            beside = i >= 2
            far = jnp.where(beside, d - 1, d)
            zt = jnp.where(lax.rem(i, 2) == 0, z - far, z + far)
            there = (zt >= 0) & (zt < Z_AXIS) & ((i < 3) | (d > 1))

            @pl.when(there & beside)
            def _():
                gather.side_done(zt)

            @pl.when(there)
            def _():
                take(zt * 2 + jnp.where(beside, 1 - y, y))

    gather.sent()


def gather_select(rows, cot_all, slots, picks, router, capacity, number):
    ep_count = lax.axis_size("ep")
    _, local, block = slots.shape
    width = rows.shape[1]
    vmem = pl.BlockSpec(memory_space=pltpu.VMEM)
    dma = pltpu.SemaphoreType.DMA
    shape = (local, ep_count, capacity, width)
    return pl.pallas_call(
        gather_select_kernel,
        in_specs=[ANY, ANY, vmem, vmem, vmem],
        out_specs=[ANY, ANY, vmem],
        out_shape=[
            jax.ShapeDtypeStruct(shape, BF),
            jax.ShapeDtypeStruct(shape, BF),
            jax.ShapeDtypeStruct(shape[:3] + (1,), F32),
        ],
        scratch_shapes=[
            pltpu.VMEM((ep_count, block, width), BF),
            pltpu.VMEM((2, block, width), BF),
            pltpu.VMEM((2, local, capacity, width), BF),
            dma((2,)), dma((2,)),
        ]
        + gather_sems(),
        compiler_params=params(collective_id=number, has_side_effects=True),
        cost_estimate=link_cost(90.0),
        name="gather_select",
    )(rows, cot_all, slots, picks, router)


def add_rows(total, terms, chunk=16):
    @pl.loop(0, total.shape[0] // chunk)
    def _(i):
        rows = pl.ds(pl.multiple_of(i * chunk, chunk), chunk)
        value = terms[0][rows, :].astype(F32)
        for term in terms[1:]:
            value = value + term[rows, :].astype(F32)
        total[rows, :] = value.astype(total.dtype)


def scatter_order(z):
    table = ((3, 2, 1, 0), (3, 0, 2, 1), (0, 3, 1, 2), (0, 1, 2, 3))
    return [
        jnp.where(
            z == 0,
            table[0][k],
            jnp.where(z == 1, table[1][k], jnp.where(z == 2, table[2][k], table[3][k])),
        )
        for k in range(Z_AXIS)
    ]


class EpReduce:
    def __init__(self, ins, by_z, bufs, sems):
        self.ins, self.by_z = ins, by_z
        self.bufs = [bufs[2 * a : 2 * a + 2] for a in range(len(ins))]
        self.up_send, self.up_recv, self.dn_send, self.dn_recv, self.y_send, self.y_recv = sems
        self.me, self.z, self.y, self.up, self.down, self.beside = ring_place()
        self.order = scatter_order(self.z)
        self.streams = [(a, 0, self.y) for a in range(len(ins))]
        self.crossing = [(a, 1, 1 - self.y) for a in range(len(ins)) if by_z[a]]

    def partners(self):
        z = self.z
        return [(z < Z_AXIS - 1, self.up), (z > 0, self.down), (z >= 0, self.beside)]

    def mine(self, stream, zt):
        return self.ins[stream[0]].at[zt * 2 + stream[2]]

    def side(self, a, zt):
        return self.bufs[a][0].at[0 if self.by_z[a] else zt]

    def below(self, stream, zt):
        return self.bufs[stream[0]][1].at[stream[1] * (Z_AXIS + 1) + zt]

    def above(self, stream, zt, z):
        return self.below(stream, jnp.where(zt == z, Z_AXIS, zt))

    def to_side(self, a, zt):
        src = self.ins[a].at[zt * 2 + 1 - self.y]
        return remote(src, self.side(a, zt), self.y_send.at[a, zt], self.y_recv.at[a, zt], self.beside)

    def rising(self, stream, zt):
        i = 2 * stream[0] + stream[1]
        return remote(
            self.mine(stream, zt), self.below(stream, zt), self.up_send.at[i, zt], self.up_recv.at[i, zt], self.up
        )

    def falling(self, stream, zt):
        i = 2 * stream[0] + stream[1]
        return remote(
            self.mine(stream, zt), self.above(stream, zt, self.z - 1),
            self.dn_send.at[i, zt], self.dn_recv.at[i, zt], self.down,
        )

    def send_side(self, k):
        for a, by_z in enumerate(self.by_z):
            if not by_z:
                self.to_side(a, self.order[k]).start()

    def step_y(self, k):
        self.step(k, [s for s in self.streams if not self.by_z[s[0]]])

    def step(self, k, streams):
        z, zt, last = self.z, self.order[k], Z_AXIS - 1
        for stream in streams:
            a = stream[0]
            mine = self.mine(stream, zt)
            terms = [mine]
            if not self.by_z[a]:
                self.to_side(a, zt).wait_recv()
                terms = [mine, self.side(a, zt)]
                ends = ((zt > z) & (z == 0)) | ((zt < z) & (z == last))

                @pl.when(ends)
                def _(mine=mine, terms=terms):
                    add_rows(mine, terms)

            @pl.when((zt > z) & (z > 0))
            def _(stream=stream, mine=mine, terms=terms):
                self.rising(stream, zt).wait_recv()
                add_rows(mine, terms + [self.below(stream, zt)])

            @pl.when((zt < z) & (z < last))
            def _(stream=stream, mine=mine, terms=terms):
                self.falling(stream, zt).wait_recv()
                add_rows(mine, terms + [self.above(stream, zt, z)])

            @pl.when(zt > z)
            def _(stream=stream):
                self.rising(stream, zt).start()

            @pl.when(zt < z)
            def _(stream=stream):
                self.falling(stream, zt).start()

    def gathered(self, stream, terms, write):
        z, last = self.z, Z_AXIS - 1

        @pl.when(z > 0)
        def _():
            self.rising(stream, z).wait_recv()

        @pl.when(z < last)
        def _():
            self.falling(stream, z).wait_recv()

        @pl.when(z == 0)
        def _():
            write(terms + [self.above(stream, z, z)])

        @pl.when(z == last)
        def _():
            write(terms + [self.below(stream, z)])

        @pl.when((z > 0) & (z < last))
        def _():
            write(terms + [self.below(stream, z), self.above(stream, z, z)])

    def own(self, a, write):
        if self.by_z[a]:
            self.to_side(a, self.z).wait_recv()
        stream = self.streams[a]
        self.gathered(stream, [self.mine(stream, self.z), self.side(a, self.z)], write)

    def sent(self):
        z = self.z
        for stream in self.streams + self.crossing:
            a = stream[0]
            for zt in range(Z_AXIS):
                if not self.by_z[a]:
                    self.to_side(a, zt).wait_send()

                @pl.when(zt > z)
                def _(stream=stream, zt=zt):
                    self.rising(stream, zt).wait_send()

                @pl.when(zt < z)
                def _(stream=stream, zt=zt):
                    self.falling(stream, zt).wait_send()

        for stream in self.crossing:
            self.to_side(stream[0], z).wait_send()


def reduce_scratch(rows, columns):
    return [pltpu.VMEM((n, rows // 2, columns), BF) for n in (Z_AXIS, Z_AXIS + 1)] * 2


BY_Z = [False, False]


def halves(ref, axis):
    n = ref.shape[axis] // 2
    lead = (slice(None),) * axis
    return [ref.at[lead + (pl.ds(h * n, n),)] for h in range(2)]


def reduce_sems(count):
    dma = pltpu.SemaphoreType.DMA
    return [dma((2 * count, Z_AXIS))] * 4 + [dma((count, Z_AXIS))] * 2


def widen_kernel(a_ref, b_ref, gate_ref, up_ref, down_ref):
    for kind, out in enumerate((gate_ref, up_ref, down_ref)):
        for half, ref in enumerate((a_ref, b_ref)):

            @pl.when(pl.program_id(0) == half)
            def _(kind=kind, out=out, ref=ref):
                out[...] = ref[kind].astype(F32)


def widen_grads(a, b):
    _, pair, hidden, width = a.shape
    shape = jax.ShapeDtypeStruct((2 * pair, hidden, width), F32)
    tile = width // 2
    return pl.pallas_call(
        widen_kernel,
        grid=(2, pair, 2),
        in_specs=[
            pl.BlockSpec(
                (3, 1, hidden, tile),
                lambda h, e, i: (0, jnp.where(h == 0, e, pair - 1), 0, jnp.where(h == 0, i, 1)),
            ),
            pl.BlockSpec(
                (3, 1, hidden, tile),
                lambda h, e, i: (0, jnp.where(h == 0, 0, e), 0, jnp.where(h == 0, 0, i)),
            ),
        ],
        out_specs=[pl.BlockSpec((1, hidden, tile), lambda h, e, i: (h * pair + e, 0, i))] * 3,
        out_shape=[shape] * 3,
        compiler_params=params(),
        name="widen_grads",
    )(a, b)


def token_hits(slots, capacity):
    rows, local = slots.shape
    lane = lax.broadcasted_iota(jnp.int32, (rows, local * capacity), 1)
    return [lane == slots[:, e : e + 1] + e * capacity for e in range(local)]


class SlotSums:
    def __init__(self, slots, first, second, buf, sem):
        self.slots, self.pair, self.buf, self.sem = slots, (first, second), buf, sem
        self.capacity = first.shape[2]

    def copies(self, j, at):
        n = self.pair[0].shape[0]
        return [
            pltpu.make_async_copy(
                ref.at[:, j], self.buf.at[at, pl.ds(i * n, n)], self.sem.at[at, i]
            )
            for i, ref in enumerate(self.pair)
        ]

    def fetch(self, j, at):
        for copy in self.copies(j, at):
            copy.start()

    def add(self, j, at, out):
        for copy in self.copies(j, at):
            copy.wait()
        place = jnp.zeros((), F32)
        for hit in token_hits(self.slots[j], self.capacity):
            place = jnp.where(hit, 1.0, place)
        rows = self.buf[at].reshape(-1, out.shape[1])
        out[...] = dot_nn(place.astype(BF), rows).astype(BF)

    def run(self, blocks, out, then):
        self.fetch(blocks[0], 0)
        for n, j in enumerate(blocks):
            if n + 1 < len(blocks):
                self.fetch(blocks[n + 1], (n + 1) % 2)
            self.add(j, n % 2, out.at[j])
            then(n)


def slot_sums_scratch(local, capacity, width):
    return [
        pltpu.VMEM((2, local, capacity, width), BF),
        pltpu.SemaphoreType.DMA((2, 2)),
    ]


def input_grads_kernel(
    slots, dgate, dx_a, dx_b, xs, cs, act, d_gate, d_up,
    residual, moe_in, cot, route_gain, gate_dense, probs, coeff, router,
    d_hidden, d_rows, router_part, gain_part, grads,
    out, gate_out, part, gates, buf, sem, x_in, c_in, h_in, w_buf, in_sem, w_sem, *refs,
):
    sums = SlotSums(slots, dx_a, dx_b, buf, sem)
    reduce = EpReduce(halves(part, 1) + [gates], BY_Z + [False], refs[:6], refs[6:])
    order, y = reduce.order, reduce.y
    pair, number, inner = act.shape
    parts, _, _, hidden, width = grads.shape
    first = xs.shape[0] - pair
    pieces = width // x_in.shape[1]
    wide = x_in.shape[1]
    greet(reduce.partners())

    def cols(piece):
        return pl.ds(piece * wide, wide)

    def wide_copies(unit):
        e, piece = unit // pieces, unit % pieces
        return [
            pltpu.make_async_copy(xs.at[first + e, :, cols(piece)], x_in, in_sem.at[0]),
            pltpu.make_async_copy(cs.at[first + e, :, cols(piece)], c_in, in_sem.at[1]),
        ]

    def inner_copies(e):
        return [
            pltpu.make_async_copy(ref.at[e], h_in.at[kind], in_sem.at[2 + kind])
            for kind, ref in enumerate((d_gate, d_up, act))
        ]

    def written(unit):
        e, piece = unit // pieces, unit % pieces
        return pltpu.make_async_copy(w_buf, grads.at[:, :, e, :, cols(piece)], w_sem)

    def prepare(unit):
        for copy in wide_copies(unit) + (inner_copies(unit // pieces) if unit % pieces == 0 else []):
            copy.start()

    def weights(unit):
        for copy in wide_copies(unit) + (inner_copies(unit // pieces) if unit % pieces == 0 else []):
            copy.wait()
        if unit > 0:
            written(unit - 1).wait()
        for kind, right in enumerate((x_in, x_in, c_in)):
            grad = dot_tn(h_in[kind], right[...]).astype(BF)
            w_buf[:, kind] = grad.reshape(parts, hidden, wide)
        written(unit).start()
        if unit + 1 < pair * pieces:
            prepare(unit + 1)

    def payload(j):
        lanes = gates.shape[2]
        column = lax.broadcasted_iota(jnp.int32, (gates.shape[1], lanes), 1)
        pay = jnp.zeros(column.shape, F32)
        mine = reduce.me * slots.shape[2]
        for e, hit in enumerate(token_hits(slots[j], sums.capacity)):
            value = jnp.sum(jnp.where(hit, dgate[j], 0.0), axis=1, keepdims=True)
            high = value.astype(BF).astype(F32)
            pay = jnp.where(column == mine + e, high, pay)
            pay = jnp.where(column == mine + e + lanes // 2, value - high, pay)
        gates[j] = pay.astype(BF)

    def send(k):
        payload(order[k] * 2 + 1 - y)
        reduce.send_side(k)

    units = pair * pieces
    quarter = [range(units * k // Z_AXIS, units * (k + 1) // Z_AXIS) for k in range(Z_AXIS)]
    sums.run([order[k] * 2 + 1 - y for k in range(Z_AXIS)], part, send)
    prepare(0)
    sums.run(
        [order[k] * 2 + y for k in range(Z_AXIS)], part, lambda k: payload(order[k] * 2 + y)
    )
    for k in range(Z_AXIS):
        for unit in quarter[k]:
            weights(unit)
        reduce.step_y(k)
    for a, rows in enumerate(halves(out, 0) + [gate_out]):
        reduce.own(a, functools.partial(add_rows, rows))

    experts, lanes = gate_dense.shape[1], gates.shape[2]
    d_gates = gate_out[:, 0:experts] + gate_out[:, lanes // 2 : lanes // 2 + experts]
    gate, prob = gate_dense[...], probs[...]
    d_logits = gate * (d_gates - jnp.sum(gate * d_gates, axis=-1, keepdims=True))
    d_logits = d_logits + prob * (coeff[...] - jnp.sum(prob * coeff[...], axis=-1, keepdims=True))
    d_low = d_logits.astype(BF)
    router_part[...] = dot_tn(d_low, moe_in[...])
    out[...] += dot_nn(d_low, router[...])
    gain_part[...] = jnp.zeros_like(gain_part)
    chunk = 16

    @pl.loop(0, out.shape[0] // chunk)
    def _(i):
        lines = pl.ds(pl.multiple_of(i * chunk, chunk), chunk)
        back, gain_rows = norm_back(out[lines, :], residual[lines, :], route_gain[...])
        total = back + cot[lines, :].astype(F32)
        d_hidden[lines, :] = total
        d_rows[lines, :] = total.astype(BF)
        gain_part[...] += gain_rows

    reduce.sent()
    written(units - 1).wait()


def input_grads(slots_t, dgate, dx, x_slots, c_slots, inner, row_values, experts, tp_count, number):
    ep_count, rows, local = slots_t.shape
    pair, _, capacity, width = dx[0].shape
    count, hidden = inner[0].shape[1:]
    lanes = -(-2 * experts // 128) * 128
    wide = width // 2
    dma = pltpu.SemaphoreType.DMA
    vmem = pl.BlockSpec(memory_space=pltpu.VMEM)
    return pl.pallas_call(
        input_grads_kernel,
        in_specs=[vmem, vmem] + [ANY] * 7 + [vmem] * 8,
        out_specs=[vmem] * 4 + [ANY],
        out_shape=[
            jax.ShapeDtypeStruct((rows, width), F32),
            jax.ShapeDtypeStruct((rows, width), BF),
            jax.ShapeDtypeStruct((experts, width), F32),
            jax.ShapeDtypeStruct((1, width), F32),
            jax.ShapeDtypeStruct((tp_count, 3, pair, hidden // tp_count, width), BF),
        ],
        scratch_shapes=[
            pltpu.VMEM((rows, width), F32),
            pltpu.VMEM((rows, lanes), F32),
            pltpu.VMEM((ep_count, rows, width), BF),
            pltpu.VMEM((ep_count, rows, lanes), BF),
        ]
        + slot_sums_scratch(local, capacity, width)
        + [
            pltpu.VMEM((count, wide), BF),
            pltpu.VMEM((count, wide), BF),
            pltpu.VMEM((3, count, hidden), BF),
            pltpu.VMEM((tp_count, 3, hidden // tp_count, wide), BF),
            dma((5,)), dma,
        ]
        + reduce_scratch(rows, width)
        + [pltpu.VMEM((n, rows, lanes), BF) for n in (Z_AXIS, Z_AXIS + 1)]
        + reduce_sems(3),
        compiler_params=params(collective_id=number, has_side_effects=True),
        cost_estimate=link_cost(100.0),
        name="input_grads",
    )(slots_t, dgate, *dx, x_slots, c_slots, *inner, *row_values)


class Exchange:
    def __init__(self, axis, send, recv):
        self.axis, self.send, self.recv = axis, send, recv
        self.count, self.me = lax.axis_size(axis), lax.axis_index(axis)

    def each(self, act):
        for i in range(1, self.count):
            act(i, lax.rem(self.me + i, self.count))

    def to(self, src, dst, i, other):
        return remote(src, dst, self.send.at[i], self.recv.at[self.me], {self.axis: other})

    def start(self, src_of, dst):
        self.each(lambda i, other: self.to(src_of(other), dst.at[self.me], i, other).start())

    def arrived(self, dst):
        self.each(
            lambda i, other: remote(
                dst.at[other], dst.at[other], self.send.at[i], self.recv.at[other], {self.axis: other}
            ).wait_recv()
        )

    def sent(self, src_of, dst):
        self.each(lambda i, other: self.to(src_of(other), dst.at[self.me], i, other).wait_send())


class SumAll:
    def __init__(self, x, out, over_tp, own_tp, over_ep, own, ring, sems):
        self.x, self.out, self.over_tp, self.own_tp = x, out, over_tp, own_tp
        self.over_ep, self.own, self.ring = over_ep, own, ring
        self.first = Exchange("tp", sems[0], sems[1])
        self.second = Exchange("ep", sems[2], sems[3])
        self.third = Exchange("ep", sems[4], sems[5])
        self.fourth = Exchange("tp", sems[6], sems[7])

    def slice_tp(self, t):
        return self.x.at[t]

    def slice_ep(self, e):
        return self.own_tp.at[e]

    def start(self):
        self.first.start(self.slice_tp, self.over_tp)
        me = self.first.me
        self.over_tp[pl.ds(me, 1)] = self.x[pl.ds(me, 1)]

    def across(self):
        self.first.arrived(self.over_tp)
        self.own_tp[...] = jnp.sum(self.over_tp[...], axis=0)
        self.second.start(self.slice_ep, self.over_ep)
        me = self.second.me
        self.over_ep[pl.ds(me, 1)] = self.own_tp[pl.ds(me, 1)]

    def back(self):
        self.second.arrived(self.over_ep)
        self.own[...] = jnp.sum(self.over_ep[...], axis=0)
        self.third.start(lambda e: self.own, self.ring)
        self.ring[pl.ds(self.third.me, 1)] = self.own[...][None]

    def home(self):
        self.third.arrived(self.ring)
        self.fourth.start(lambda t: self.ring, self.out)
        self.out[pl.ds(self.fourth.me, 1)] = self.ring[...][None]

    def finish(self):
        self.fourth.arrived(self.out)
        self.first.sent(self.slice_tp, self.over_tp)
        self.second.sent(self.slice_ep, self.over_ep)
        self.third.sent(lambda e: self.own, self.ring)
        self.fourth.sent(lambda t: self.ring, self.out)


def exchange_sems(axis):
    return [pltpu.SemaphoreType.DMA((lax.axis_size(axis),))] * 2


def sum_scratch(shape):
    tp, ep, rows, lanes = shape
    return [
        pltpu.VMEM(shape, F32), pltpu.VMEM((ep, rows, lanes), F32), pltpu.VMEM((ep, rows, lanes), F32),
        pltpu.VMEM((rows, lanes), F32), pltpu.VMEM((ep, rows, lanes), F32),
    ] + [sem for axis in ("tp", "ep", "ep", "tp") for sem in exchange_sems(axis)]


def pack_small(values, tp, ep):
    total = tp * ep
    flat = jnp.concatenate([v.reshape(-1) for v in values])
    rows = -(-flat.shape[0] // (total * 128 * 8)) * 8
    return jnp.pad(flat, (0, total * rows * 128 - flat.shape[0])).reshape(tp, ep, rows, 128)


def unpack_small(summed, values):
    summed = summed.reshape(-1)
    out, at = [], 0
    for v in values:
        out.append(summed[at : at + v.size].reshape(v.shape))
        at += v.size
    return out


def project_kernel(x_ref, gain_ref, wq_ref, wk_ref, wv_ref, normed_ref, q_ref, k_ref, v_ref):
    x = x_ref[...].astype(F32)
    normed = (x * rms_scale(x) * gain_ref[...]).astype(BF)
    normed_ref[...] = normed
    q_ref[...] = dot_nn(normed, wq_ref[...])
    k_ref[...] = dot_nn(normed, wk_ref[...])
    v_ref[...] = dot_nn(normed, wv_ref[...]).astype(BF)


def project(inputs, gain, wq, wk, wv):
    length, width = inputs.shape
    tile = min(256, length)

    def rows(columns):
        return pl.BlockSpec((tile, columns), lambda i: (i, 0))

    def fixed(array):
        return pl.BlockSpec(array.shape, lambda i: (0, 0), pipeline_mode=pl.Buffered(1))

    return pl.pallas_call(
        project_kernel,
        grid=(length // tile,),
        in_specs=[rows(width), fixed(gain), fixed(wq), fixed(wk), fixed(wv)],
        out_specs=[rows(width), rows(wq.shape[1]), rows(wk.shape[1]), rows(wv.shape[1])],
        out_shape=[
            jax.ShapeDtypeStruct((length, width), BF),
            jax.ShapeDtypeStruct((length, wq.shape[1]), F32),
            jax.ShapeDtypeStruct((length, wk.shape[1]), F32),
            jax.ShapeDtypeStruct((length, wv.shape[1]), BF),
        ],
        compiler_params=params(),
        name="project",
    )(inputs, gain, wq, wk, wv)


def fill_bias(span_ref, bias, chunk=256):
    keys, length = bias.shape
    query = lax.broadcasted_iota(jnp.int32, (1, length), 1)

    def spans(pos):
        first = (pos >= span_ref[0, 0]) & (pos < span_ref[0, 0] + IMG)
        second = (pos >= span_ref[0, 1]) & (pos < span_ref[0, 1] + IMG)
        return jnp.where(first, 0, jnp.where(second, 1, -1))

    query_span = spans(query)
    query_other = jnp.where(query_span < 0, -2, query_span)
    for start in range(0, keys, chunk):
        key = start + lax.broadcasted_iota(jnp.int32, (chunk, 1), 0)
        ok = (key <= query) | (spans(key) == query_other)
        bias[start : start + chunk, :] = jnp.where(ok, 0.0, MASKED)


def query_tiles(length):
    tile = min(IMG, length)
    return [
        (start, tile, min(length, start + tile + -(-IMG // tile) * tile))
        for start in range(0, length, tile)
    ]


def attention_kernel(
    span_ref, q_ref, k_ref, v_ref, cos_ref, sin_ref, qg_ref, kg_ref, w_out_ref, cot_ref, x_ref, gain_ref,
    out_ref, lse_ref, rows_ref, moe_ref, cots_ref,
    bias, k_rot, v_t, heads, part, core_rows, x_rows, core_send, core_recv, x_send, x_recv, *sems,
):
    factor = q_ref.shape[-1] ** (-0.5)
    cosine, sine = cos_ref[...], sin_ref[...]
    step = pl.program_id(0)
    size = q_ref.shape[-1]
    me = lax.axis_index("tp")
    x, c = me // 2, me % 2
    other_core, other_x = {"tp": x * 2 + 1 - c}, {"tp": (1 - x) * 2 + c}
    gather = EpGather(ring_pieces(cot_ref, 0), ring_pieces(cots_ref, 1), sems)

    @pl.when(step == 0)
    def _():
        greet(gather.partners() + [(x >= 0, other_core), (x >= 0, other_x)])
        gather.start()
        fill_bias(span_ref, bias)
        k = k_ref[...]
        k_rot[...] = turn(k * rms_scale(k) * kg_ref[...], cosine, sine).astype(BF)
        v_t[...] = v_ref[...].astype(F32).T.astype(BF)

    @pl.when(step == 2)
    def _():
        gather.cross()

    @pl.when(step == pl.num_programs(0) - 2)
    def _():
        gather.hop(1)

    q = q_ref[...]
    q_rot = turn(q * rms_scale(q) * qg_ref[...], cosine, sine).astype(BF)
    for start, tile, keys in query_tiles(q.shape[0]):
        cols = slice(start, start + tile)
        s = dot_nt(k_rot[:keys, :], q_rot[cols, :]) * factor + bias[:keys, cols]
        top = jnp.max(s, axis=0, keepdims=True)
        p = jnp.exp(s - top)
        total = jnp.sum(p, axis=0, keepdims=True)
        o_t = dot_nn(v_t[:, :keys], p.astype(BF)) / total
        rows = o_t.T.astype(BF)
        out_ref[cols, :] = rows
        heads[step, cols, :] = rows
        lse_ref[0, :, cols] = top + jnp.log(total)

    @pl.when(step == pl.num_programs(0) - 1)
    def _():
        count = heads.shape[0]
        block = rows_ref.shape[0]

        def project(tp):
            lines = pl.ds(pl.multiple_of(tp * block, block), block)
            rows = jnp.concatenate([heads[h, lines, :] for h in range(count)], axis=1)
            part[tp] = dot_nn(rows, w_out_ref[...]).astype(BF)

        def to_core(xt):
            return remote(
                part.at[xt * 2 + 1 - c], core_rows.at[xt],
                core_send.at[xt], core_recv.at[xt], other_core,
            )

        far, near = part.at[(1 - x) * 2 + c], part.at[x * 2 + c]
        to_x = remote(far, x_rows, x_send, x_recv, other_x)
        project((1 - x) * 2 + 1 - c)
        to_core(1 - x).start()
        project((1 - x) * 2 + c)
        to_core(1 - x).wait_recv()
        add_rows(far, [far, core_rows.at[1 - x]])
        to_x.start()
        project(x * 2 + 1 - c)
        to_core(x).start()
        project(x * 2 + c)
        gather.hop(2)
        to_core(x).wait_recv()
        gather.hop(3)
        to_x.wait_recv()
        chunk = 16

        @pl.loop(0, block // chunk)
        def _(i):
            lines = pl.ds(pl.multiple_of(i * chunk, chunk), chunk)
            total = near[lines, :].astype(F32) + core_rows[x, lines, :].astype(F32)
            hidden = x_ref[lines, :].astype(F32) + (total + x_rows[lines, :].astype(F32))
            rows_ref[lines, :] = hidden
            moe_ref[lines, :] = (hidden * rms_scale(hidden) * gain_ref[...]).astype(BF)

        gather.finish()
        to_core(1 - x).wait_send()
        to_core(x).wait_send()
        to_x.wait_send()


def plain_attention_kernel(
    span_ref, q_ref, k_ref, v_ref, cos_ref, sin_ref, qg_ref, kg_ref, out_ref, lse_ref,
    bias, k_rot, v_t,
):
    factor = q_ref.shape[-1] ** (-0.5)
    cosine, sine = cos_ref[...], sin_ref[...]

    @pl.when(pl.program_id(0) == 0)
    def _():
        fill_bias(span_ref, bias)
        k = k_ref[...]
        k_rot[...] = turn(k * rms_scale(k) * kg_ref[...], cosine, sine).astype(BF)
        v_t[...] = v_ref[...].astype(F32).T.astype(BF)

    q = q_ref[...]
    q_rot = turn(q * rms_scale(q) * qg_ref[...], cosine, sine).astype(BF)
    for start, tile, keys in query_tiles(q.shape[0]):
        cols = slice(start, start + tile)
        s = dot_nt(k_rot[:keys, :], q_rot[cols, :]) * factor + bias[:keys, cols]
        top = jnp.max(s, axis=0, keepdims=True)
        p = jnp.exp(s - top)
        total = jnp.sum(p, axis=0, keepdims=True)
        o_t = dot_nn(v_t[:, :keys], p.astype(BF)) / total
        out_ref[cols, :] = o_t.T.astype(BF)
        lse_ref[0, :, cols] = top + jnp.log(total)


def attention(span, q, k, v, cosine, sine, q_gain, k_gain, w_out, cotangent, x_rows, route_gain, number):
    length, size = k.shape
    heads = q.shape[1] // size
    whole = pl.BlockSpec((length, size), lambda h: (0, 0))
    head = pl.BlockSpec((length, size), lambda h: (0, h))
    gain = pl.BlockSpec((1, size), lambda h: (0, 0))
    in_specs = [
        pl.BlockSpec(memory_space=pltpu.SMEM), head, whole, whole, whole, whole, gain, gain,
    ]
    out_specs = [head, pl.BlockSpec((1, 1, length), lambda h: (h, 0, 0))]
    out_shape = [
        jax.ShapeDtypeStruct((length, heads * size), BF),
        jax.ShapeDtypeStruct((heads, 1, length), F32),
    ]
    scratch = [
        pltpu.VMEM((length, length), F32),
        pltpu.VMEM((length, size), BF),
        pltpu.VMEM((size, length), BF),
    ]
    args = (span, q, k, v, cosine, sine, q_gain, k_gain)
    ep_count, tp_count = lax.axis_size("ep"), lax.axis_size("tp")
    if ep_count != 2 * Z_AXIS:
        out, lse = pl.pallas_call(
            plain_attention_kernel,
            grid=(heads,),
            in_specs=in_specs,
            out_specs=out_specs,
            out_shape=out_shape,
            scratch_shapes=scratch,
            compiler_params=params(),
            name="plain_attention",
        )(*args)
        rows = lax.psum_scatter(
            dot_nn(out, w_out).astype(BF), "tp", scatter_dimension=0, tiled=True
        )
        hidden = x_rows.astype(F32) + rows.astype(F32)
        moe_in = (hidden * rms_scale(hidden) * route_gain).astype(BF)
        return out, lse, hidden, moe_in, lax.all_gather(cotangent, "ep")
    block, width = cotangent.shape
    dma = pltpu.SemaphoreType.DMA
    return pl.pallas_call(
        attention_kernel,
        grid=(heads,),
        in_specs=in_specs
        + [
            pl.BlockSpec(w_out.shape, lambda h: (0, 0), pipeline_mode=pl.Buffered(1)), ANY,
            pl.BlockSpec((block, width), lambda h: (0, 0)),
            pl.BlockSpec((1, width), lambda h: (0, 0)),
        ],
        out_specs=out_specs + [pl.BlockSpec((block, width), lambda h: (0, 0))] * 2 + [ANY],
        out_shape=out_shape
        + [
            jax.ShapeDtypeStruct((block, width), F32),
            jax.ShapeDtypeStruct((block, width), BF),
            jax.ShapeDtypeStruct((ep_count, block, width), BF),
        ],
        scratch_shapes=scratch
        + [
            pltpu.VMEM((heads, length, size), BF),
            pltpu.VMEM((tp_count, block, width), BF),
            pltpu.VMEM((2, block, width), BF),
            pltpu.VMEM((block, width), BF),
            dma((2,)), dma((2,)), dma, dma,
        ]
        + gather_sems(),
        compiler_params=params(collective_id=number, has_side_effects=True),
        cost_estimate=link_cost(90.0),
        name="attention",
    )(*args, w_out, cotangent, x_rows, route_gain)


def norm_back(grads, rows, gain):
    scale = rms_scale(rows)
    gain_part = jnp.sum(grads * rows * scale, axis=0, keepdims=True)
    inner = grads * gain
    mean = jnp.mean(inner * rows, axis=-1, keepdims=True)
    return scale * inner - rows * (scale * scale * scale * mean), gain_part


def plain_attention_back_kernel(
    span_ref, q_ref, k_ref, v_ref, grad_ref, lse_ref, cos_ref, sin_ref, qg_ref, kg_ref,
    dq_ref, dk_ref, dv_ref, dqg_ref, dkg_ref,
    bias, k_rot, k_t, dk_acc, dv_acc, dq_t,
):
    factor = q_ref.shape[-1] ** (-0.5)
    cosine, sine = cos_ref[...], sin_ref[...]
    step = pl.program_id(0)

    @pl.when(step == 0)
    def _():
        fill_bias(span_ref, bias)
        k = k_ref[...]
        rotated = turn(k * rms_scale(k) * kg_ref[...], cosine, sine)
        k_rot[...] = rotated.astype(BF)
        k_t[...] = rotated.T.astype(BF)
        dk_acc[...] = jnp.zeros_like(dk_acc)
        dv_acc[...] = jnp.zeros_like(dv_acc)
        dqg_ref[...] = jnp.zeros_like(dqg_ref)

    q = q_ref[...]
    q_rot = turn(q * rms_scale(q) * qg_ref[...], cosine, sine).astype(BF)
    for start, tile, keys in query_tiles(q.shape[0]):
        cols = slice(start, start + tile)
        s = dot_nt(k_rot[:keys, :], q_rot[cols, :]) * factor + bias[:keys, cols]
        p = jnp.exp(s - lse_ref[0, :, cols])
        grad = grad_ref[cols, :]
        dp = dot_nt(v_ref[:keys, :], grad)
        mean = jnp.sum(p * dp, axis=0, keepdims=True)
        raw = (p * (dp - mean) * factor).astype(BF)
        dq_t[:, cols] = dot_nn(k_t[:, :keys], raw)
        dk_acc[:keys, :] += dot_nn(raw, q_rot[cols, :])
        dv_acc[:keys, :] += dot_nn(p.astype(BF), grad)
    back, gain_part = norm_back(turn_back(dq_t[...].T, cosine, sine), q, qg_ref[...])
    dq_ref[...] = back.astype(BF)
    dqg_ref[...] += gain_part

    @pl.when(step == pl.num_programs(0) - 1)
    def _():
        back, gain_part = norm_back(turn_back(dk_acc[...], cosine, sine), k_ref[...], kg_ref[...])
        dk_ref[...] = back.astype(BF)
        dkg_ref[...] = gain_part
        dv_ref[...] = dv_acc[...].astype(BF)


def plain_attention_back(span, q, k, v, grads, lse, cosine, sine, q_gain, k_gain):
    length, size = k.shape
    heads = q.shape[1] // size
    whole = pl.BlockSpec((length, size), lambda h: (0, 0))
    head = pl.BlockSpec((length, size), lambda h: (0, h))
    gain = pl.BlockSpec((1, size), lambda h: (0, 0))
    return pl.pallas_call(
        plain_attention_back_kernel,
        grid=(heads,),
        in_specs=[
            pl.BlockSpec(memory_space=pltpu.SMEM), head, whole, whole, head,
            pl.BlockSpec((1, 1, length), lambda h: (h, 0, 0)), whole, whole, gain, gain,
        ],
        out_specs=[head, whole, whole, gain, gain],
        out_shape=[
            jax.ShapeDtypeStruct((length, heads * size), BF),
            jax.ShapeDtypeStruct((length, size), BF),
            jax.ShapeDtypeStruct((length, size), BF),
            jax.ShapeDtypeStruct((1, size), F32),
            jax.ShapeDtypeStruct((1, size), F32),
        ],
        scratch_shapes=[
            pltpu.VMEM((length, length), F32),
            pltpu.VMEM((length, size), BF),
            pltpu.VMEM((size, length), BF),
            pltpu.VMEM((length, size), F32),
            pltpu.VMEM((length, size), F32),
            pltpu.VMEM((size, length), F32),
        ],
        compiler_params=params(),
        name="plain_attention_back",
    )(span, q, k, v, grads, lse, cosine, sine, q_gain, k_gain)


def attention_back_kernel(
    span_ref, q_ref, k_ref, v_ref, lse_ref, cos_ref, sin_ref, qg_ref, kg_ref,
    w_out_ref, rows_ref, slots_ref, out_a, out_b, hidden_ref,
    dq_ref, dk_ref, dv_ref, dqg_ref, dkg_ref, branch_ref, output_ref,
    bias, k_rot, k_t, dk_acc, dv_acc, dq_t, branch, grads, part, buf, sem,
    own_sem, out_sem, core_send, core_recv, x_send, x_recv, *refs,
):
    factor = q_ref.shape[-1] ** (-0.5)
    size = q_ref.shape[-1]
    cosine, sine = cos_ref[...], sin_ref[...]
    step = pl.program_id(0)
    me = lax.axis_index("tp")
    x, c = me // 2, me % 2
    other_core, other_x = {"tp": x * 2 + 1 - c}, {"tp": (1 - x) * 2 + c}
    reduce = EpReduce(halves(part, 1), BY_Z, refs[:4], refs[4:])
    sums = SlotSums(slots_ref, out_a, out_b, buf, sem)
    order, y = reduce.order, reduce.y
    block = rows_ref.shape[0]
    near_other, far, far_other = x * 2 + 1 - c, (1 - x) * 2 + c, (1 - x) * 2 + 1 - c

    def to_core(slot, src, tp):
        return remote(src, branch.at[tp], core_send.at[slot], core_recv.at[slot], other_core)

    def to_x(tp):
        return remote(rows_ref, branch.at[tp], x_send, x_recv, other_x)

    def own_rows():
        return pltpu.make_async_copy(rows_ref, branch.at[me], own_sem)

    def whole_branch():
        return pltpu.make_async_copy(branch, branch_ref, out_sem)

    @pl.when(step == 0)
    def _():
        greet(reduce.partners() + [(x >= 0, other_core), (x >= 0, other_x)])
        to_x(me).start()
        to_core(0, rows_ref, me).start()
        own_rows().start()
        sums.run([order[k] * 2 + 1 - y for k in range(Z_AXIS)], part, reduce.send_side)
        fill_bias(span_ref, bias)
        k = k_ref[...]
        rotated = turn(k * rms_scale(k) * kg_ref[...], cosine, sine)
        k_rot[...] = rotated.astype(BF)
        k_t[...] = rotated.T.astype(BF)
        dk_acc[...] = jnp.zeros_like(dk_acc)
        dv_acc[...] = jnp.zeros_like(dv_acc)
        dqg_ref[...] = jnp.zeros_like(dqg_ref)

        def head_grads(tp):
            lines = pl.ds(pl.multiple_of(tp * block, block), block)
            rows = dot_nt(branch[tp], w_out_ref[...]).astype(BF)
            for h in range(grads.shape[0]):
                grads[h, lines, :] = rows[:, h * size : (h + 1) * size]

        own_rows().wait()
        head_grads(me)
        to_core(0, rows_ref, near_other).wait_recv()
        head_grads(near_other)
        sums.run([order[k] * 2 + y for k in range(Z_AXIS)], part, lambda k: None)
        reduce.step_y(0)
        to_x(far).wait_recv()
        to_core(1, branch.at[far], far).start()
        head_grads(far)
        to_core(1, branch.at[far], far_other).wait_recv()
        head_grads(far_other)
        whole_branch().start()

    for k, head in ((1, 1), (2, 5)):

        @pl.when(step == head)
        def _(k=k):
            reduce.step_y(k)

    q = q_ref[...]
    q_rot = turn(q * rms_scale(q) * qg_ref[...], cosine, sine).astype(BF)
    for start, tile, keys in query_tiles(q.shape[0]):
        cols = slice(start, start + tile)
        s = dot_nt(k_rot[:keys, :], q_rot[cols, :]) * factor + bias[:keys, cols]
        p = jnp.exp(s - lse_ref[0, :, cols])
        grad = grads[step, cols, :]
        dp = dot_nt(v_ref[:keys, :], grad)
        mean = jnp.sum(p * dp, axis=0, keepdims=True)
        raw = (p * (dp - mean) * factor).astype(BF)
        dq_t[:, cols] = dot_nn(k_t[:, :keys], raw)
        dk_acc[:keys, :] += dot_nn(raw, q_rot[cols, :])
        dv_acc[:keys, :] += dot_nn(p.astype(BF), grad)
    back, gain_part = norm_back(turn_back(dq_t[...].T, cosine, sine), q, qg_ref[...])
    dq_ref[...] = back.astype(BF)
    dqg_ref[...] += gain_part

    @pl.when(step == pl.num_programs(0) - 1)
    def _():
        back, gain_part = norm_back(turn_back(dk_acc[...], cosine, sine), k_ref[...], kg_ref[...])
        dk_ref[...] = back.astype(BF)
        dkg_ref[...] = gain_part
        dv_ref[...] = dv_acc[...].astype(BF)
        reduce.step_y(Z_AXIS - 1)
        pairs = zip(halves(output_ref, 0), halves(hidden_ref, 0))
        for a, (rows, residual) in enumerate(pairs):
            reduce.own(a, lambda terms, rows=rows, residual=residual: add_rows(rows, terms + [residual]))
        reduce.sent()
        whole_branch().wait()
        to_x(me).wait_send()
        to_core(0, rows_ref, me).wait_send()
        to_core(1, branch.at[far], far).wait_send()


def attention_back(
    span, q, k, v, lse, cosine, sine, q_gain, k_gain, w_out, d_rows, slots_t, out, hidden, number
):
    length, size = k.shape
    heads = q.shape[1] // size
    ep_count, tp_count = lax.axis_size("ep"), lax.axis_size("tp")
    if ep_count != 2 * Z_AXIS:
        branch = lax.all_gather(d_rows, "tp", axis=0, tiled=True)
        grads = dot_nt(branch, w_out).astype(BF)
        mine = lax.psum_scatter(out, "ep", scatter_dimension=0)
        back = plain_attention_back(span, q, k, v, grads, lse, cosine, sine, q_gain, k_gain)
        return *back, branch, (hidden + mine.astype(F32)).astype(BF)
    block, width = d_rows.shape
    whole = pl.BlockSpec((length, size), lambda h: (0, 0))
    head = pl.BlockSpec((length, size), lambda h: (0, h))
    gain = pl.BlockSpec((1, size), lambda h: (0, 0))
    rows = pl.BlockSpec((block, width), lambda h: (0, 0))
    dma = pltpu.SemaphoreType.DMA
    *back, branch, output = pl.pallas_call(
        attention_back_kernel,
        grid=(heads,),
        in_specs=[
            pl.BlockSpec(memory_space=pltpu.SMEM), head, whole, whole,
            pl.BlockSpec((1, 1, length), lambda h: (h, 0, 0)), whole, whole, gain, gain,
            pl.BlockSpec(w_out.shape, lambda h: (0, 0), pipeline_mode=pl.Buffered(1)), ANY,
            pl.BlockSpec(slots_t.shape, lambda h: (0, 0, 0), pipeline_mode=pl.Buffered(1)), ANY, ANY,
            pl.BlockSpec((block, width), lambda h: (0, 0), pipeline_mode=pl.Buffered(1)),
        ],
        out_specs=[head, whole, whole, gain, gain, ANY, rows],
        out_shape=[
            jax.ShapeDtypeStruct((length, heads * size), BF),
            jax.ShapeDtypeStruct((length, size), BF),
            jax.ShapeDtypeStruct((length, size), BF),
            jax.ShapeDtypeStruct((1, size), F32),
            jax.ShapeDtypeStruct((1, size), F32),
            jax.ShapeDtypeStruct((tp_count, block, width), BF),
            jax.ShapeDtypeStruct((block, width), BF),
        ],
        scratch_shapes=[
            pltpu.VMEM((length, length), F32),
            pltpu.VMEM((length, size), BF),
            pltpu.VMEM((size, length), BF),
            pltpu.VMEM((length, size), F32),
            pltpu.VMEM((length, size), F32),
            pltpu.VMEM((size, length), F32),
            pltpu.VMEM((tp_count, block, width), BF),
            pltpu.VMEM((heads, length, size), BF),
        ]
        + [pltpu.VMEM((ep_count, block, width), BF)]
        + slot_sums_scratch(slots_t.shape[2], out[0].shape[2], width)
        + [dma, dma, dma((2,)), dma((2,)), dma, dma]
        + reduce_scratch(block, width)
        + reduce_sems(2),
        compiler_params=params(collective_id=number, has_side_effects=True),
        cost_estimate=link_cost(100.0),
        name="attention_back",
    )(span, q, k, v, lse, cosine, sine, q_gain, k_gain, w_out, d_rows, slots_t, *out, hidden)
    return *back, branch.reshape(-1, width), output


def projection_grads_kernel(
    normed, dq, dk, dv, heads, branch, wq_hbm, wk, wv, x_rows, d_hbm, gain, small,
    gq_ref, gk_ref, gv_ref, gout_ref, inputs_grad, gain_grad, small_sum,
    blocks, out_blocks, part, core_rows, far_rows, gain_own, tp_gains, tp_gain, ep_gains, wq, d_hidden,
    core_send, core_recv, x_send, x_recv, wq_sem, d_sem, *refs,
):
    me = lax.axis_index("tp")
    x, c = me // 2, me % 2
    other_core, other_x = {"tp": x * 2 + 1 - c}, {"tp": (1 - x) * 2 + c}
    sums = SumAll(small, small_sum, *refs[:5], refs[5:13])
    over_tp, over_ep = Exchange("tp", refs[13], refs[14]), Exchange("ep", refs[15], refs[16])
    reduce = EpReduce([blocks, out_blocks], BY_Z, refs[17:21], refs[21:])
    order, y = reduce.order, reduce.y
    rows, width = inputs_grad.shape
    nq, nk = dq.shape[1], dk.shape[1]

    load_wq = pltpu.make_async_copy(wq_hbm, wq, wq_sem)
    load_d = pltpu.make_async_copy(d_hbm, d_hidden, d_sem)
    load_wq.start()
    load_d.start()
    everyone = []
    for exchange in (over_tp, over_ep):
        exchange.each(
            lambda i, other, axis=exchange.axis: everyone.append((other >= 0, {axis: other}))
        )
    greet(everyone)

    def fill(j):
        cols = pl.ds(pl.multiple_of(j * rows, rows), rows)
        left = normed[:, cols].T
        blocks[j, :, 0:nq] = dot_nn(left, dq[...]).astype(BF)
        blocks[j, :, nq : nq + nk] = dot_nn(left, dk[...]).astype(BF)
        blocks[j, :, nq + nk : nq + 2 * nk] = dot_nn(left, dv[...]).astype(BF)
        out_blocks[j] = dot_nn(branch[:, cols].T, heads[...]).astype(BF)

    def spread_back(tp):
        lines = pl.ds(pl.multiple_of(tp * rows, rows), rows)
        for start in range(0, width, width // 4):
            cols = slice(start, start + width // 4)
            part[tp, :, cols] = (
                dot_nt(dq[lines, :], wq[cols, :])
                + dot_nt(dk[lines, :], wk[cols, :])
                + dot_nt(dv[lines, :], wv[cols, :])
            ).astype(BF)

    def to_core(xt):
        return remote(
            part.at[xt * 2 + 1 - c], core_rows.at[xt], core_send.at[xt], core_recv.at[xt], other_core
        )

    far, near = part.at[(1 - x) * 2 + c], part.at[x * 2 + c]
    to_x = remote(far, far_rows, x_send, x_recv, other_x)

    def fill_side(k):
        fill(order[k] * 2 + 1 - y)

    def fill_own(k):
        fill(order[k] * 2 + y)

    z = reduce.z
    at_end = (z == 0) | (z == Z_AXIS - 1)

    def step_if(there, *ks):
        @pl.when(there)
        def _():
            for k in ks:
                reduce.step_y(k)

    sums.start()
    fill_side(0)
    reduce.send_side(0)
    load_wq.wait()
    spread_back((1 - x) * 2 + 1 - c)
    to_core(1 - x).start()
    sums.across()
    fill_side(1)
    reduce.send_side(1)
    spread_back((1 - x) * 2 + c)
    to_core(1 - x).wait_recv()
    add_rows(far, [far, core_rows.at[1 - x]])
    to_x.start()
    fill_own(0)
    fill_side(2)
    reduce.send_side(2)
    step_if(at_end, 0)
    spread_back(x * 2 + 1 - c)
    to_core(x).start()
    spread_back(x * 2 + c)
    for k in range(1, Z_AXIS):
        fill_own(k)
    fill_side(3)
    step_if(at_end, 1)
    step_if(~at_end, 0)
    sums.back()
    to_core(x).wait_recv()
    to_x.wait_recv()
    load_d.wait()

    chunk = 32
    gain_own[...] = jnp.zeros_like(gain_own)

    @pl.loop(0, rows // chunk)
    def _(i):
        lines = pl.ds(pl.multiple_of(i * chunk, chunk), chunk)
        grad = near[lines, :].astype(F32) + core_rows[x, lines, :].astype(F32)
        grad = grad + far_rows[lines, :].astype(F32)
        back, gain_part = norm_back(grad, x_rows[lines, :].astype(F32), gain[...])
        inputs_grad[lines, :] = d_hidden[lines, :] + back
        gain_own[...] += gain_part

    over_tp.start(lambda t: gain_own, tp_gains)
    tp_gains[pl.ds(over_tp.me, 1)] = gain_own[...][None]
    over_tp.arrived(tp_gains)
    tp_gain[...] = jnp.sum(tp_gains[...], axis=0)
    over_ep.start(lambda e: tp_gain, ep_gains)
    ep_gains[pl.ds(over_ep.me, 1)] = tp_gain[...][None]
    reduce.send_side(3)
    step_if(at_end, 2)
    step_if(~at_end, 1, 2)
    sums.home()
    reduce.step_y(3)

    def total_of(terms, lines):
        value = terms[0][lines, :].astype(F32)
        for term in terms[1:]:
            value = value + term[lines, :].astype(F32)
        return value

    over_ep.arrived(ep_gains)
    gain_grad[...] = jnp.sum(ep_gains[...], axis=0)
    def write(terms):
        for start in range(0, rows, 64):
            lines = slice(start, start + 64)
            value = total_of(terms, lines)
            gq_ref[lines, :] = value[:, 0:nq]
            gk_ref[lines, :] = value[:, nq : nq + nk]
            gv_ref[lines, :] = value[:, nq + nk :]

    def write_out(terms):
        for start in range(0, rows, 128):
            lines = slice(start, start + 128)
            gout_ref[:, lines] = total_of(terms, lines).T

    reduce.own(0, write)
    reduce.own(1, write_out)
    reduce.sent()
    to_core(1 - x).wait_send()
    to_core(x).wait_send()
    to_x.wait_send()
    over_tp.sent(lambda t: gain_own, tp_gains)
    over_ep.sent(lambda e: tp_gain, ep_gains)
    sums.finish()


def projection_grads(
    normed, dq, dk, dv, heads, branch, wq, wk, wv, x_rows, d_hidden, gain, small_values, number
):
    rows, width = x_rows.shape
    ep_count, tp_count = lax.axis_size("ep"), lax.axis_size("tp")
    small = pack_small(small_values, tp_count, ep_count)
    if ep_count != 2 * Z_AXIS:

        def over_sequences(part, dim):
            return lax.psum_scatter(
                part.astype(BF), "ep", scatter_dimension=dim, tiled=True
            ).astype(F32)

        d_normed = (dot_nt(dq, wq) + dot_nt(dk, wk) + dot_nt(dv, wv)).astype(BF)
        d_mine = lax.psum_scatter(d_normed, "tp", scatter_dimension=0, tiled=True)
        back, gain_part = norm_back(d_mine.astype(F32), x_rows.astype(F32), gain)
        gain_sum, small_sum = lax.psum((gain_part, small), ("ep", "tp"))
        return (
            over_sequences(dot_tn(normed, dq), 0),
            over_sequences(dot_tn(normed, dk), 0),
            over_sequences(dot_tn(normed, dv), 0),
            over_sequences(dot_tn(heads, branch), 1),
            d_hidden + back,
            gain_sum,
            unpack_small(small_sum, small_values),
        )
    nq, nk = dq.shape[1], dk.shape[1]
    nh = heads.shape[1]
    vmem = pl.BlockSpec(memory_space=pltpu.VMEM)
    dma = pltpu.SemaphoreType.DMA
    *grads, small_sum = pl.pallas_call(
        projection_grads_kernel,
        in_specs=[vmem] * 6 + [ANY] + [vmem] * 3 + [ANY] + [vmem] * 2,
        out_specs=[vmem] * 7,
        out_shape=[
            jax.ShapeDtypeStruct((rows, nq), F32),
            jax.ShapeDtypeStruct((rows, nk), F32),
            jax.ShapeDtypeStruct((rows, nk), F32),
            jax.ShapeDtypeStruct((nh, rows), F32),
            jax.ShapeDtypeStruct((rows, width), F32),
            jax.ShapeDtypeStruct((1, width), F32),
            jax.ShapeDtypeStruct(small.shape, F32),
        ],
        scratch_shapes=[
            pltpu.VMEM((ep_count, rows, nq + 2 * nk), BF),
            pltpu.VMEM((ep_count, rows, nh), BF),
            pltpu.VMEM((tp_count, rows, width), BF),
            pltpu.VMEM((2, rows, width), BF),
            pltpu.VMEM((rows, width), BF),
            pltpu.VMEM((1, width), F32),
            pltpu.VMEM((tp_count, 1, width), F32),
            pltpu.VMEM((1, width), F32),
            pltpu.VMEM((ep_count, 1, width), F32),
            pltpu.VMEM(wq.shape, BF),
            pltpu.VMEM((rows, width), F32),
            dma((2,)), dma((2,)), dma, dma, dma, dma,
        ]
        + sum_scratch(small.shape)
        + exchange_sems("tp")
        + exchange_sems("ep")
        + [pltpu.VMEM((n, rows, c), BF) for c in (nq + 2 * nk, nh) for n in (Z_AXIS, Z_AXIS + 1)]
        + reduce_sems(2),
        compiler_params=params(collective_id=number, has_side_effects=True),
        cost_estimate=link_cost(110.0),
        name="projection_grads",
    )(normed, dq, dk, dv, heads, branch, wq, wk, wv, x_rows, d_hidden, gain, small)
    return *grads, unpack_small(small_sum, small_values)


def select_kernel(slot_ref, x_ref, c_ref, xs_ref, cs_ref):
    local, _, capacity, width = xs_ref.shape
    rows = x_ref.shape[1]
    place = jnp.concatenate(
        [
            (
                slot_ref[0, e : e + 1, :]
                == lax.broadcasted_iota(jnp.int32, (capacity, rows), 0)
            ).astype(F32)
            for e in range(local)
        ],
        axis=0,
    ).astype(BF)
    xs_ref[...] = dot_nn(place, x_ref[0]).astype(BF).reshape(xs_ref.shape)
    cs_ref[...] = dot_nn(place, c_ref[0]).astype(BF).reshape(cs_ref.shape)


def select_rows(slots, tokens, cots, capacity):
    blocks, local, rows = slots.shape
    width = tokens.shape[-1]
    block = pl.BlockSpec((1, rows, width), lambda b: (b, 0, 0))
    out = pl.BlockSpec((local, 1, capacity, width), lambda b: (0, b, 0, 0))
    shape = jax.ShapeDtypeStruct((local, blocks, capacity, width), BF)
    return pl.pallas_call(
        select_kernel,
        grid=(blocks,),
        in_specs=[pl.BlockSpec((1, local, rows), lambda b: (b, 0, 0)), block, block],
        out_specs=[out, out],
        out_shape=[shape, shape],
        compiler_params=params(),
        name="select_rows",
    )(slots, tokens, cots)


def pack_kernel(gate_ref, up_ref, down_ref, out_ref):
    for kind, ref in enumerate((gate_ref, up_ref, down_ref)):
        out_ref[kind, 0] = ref[0]


def pack_weights(weights, first, count):
    _, hidden, width = weights[0].shape
    block = pl.BlockSpec((1, hidden, width), lambda e: (first + e, 0, 0))
    return pl.pallas_call(
        pack_kernel,
        grid=(count,),
        in_specs=[block] * 3,
        out_specs=pl.BlockSpec((3, 1, hidden, width), lambda e: (0, e, 0, 0)),
        out_shape=jax.ShapeDtypeStruct((3, count, hidden, width), BF),
        compiler_params=params(),
        name="pack_weights",
    )(*weights)


def expert_kernel(
    x_ref, c_ref, w_ref, gate_ref, out_ref, dx_ref, act_ref, dg_ref, du_ref, dgate_ref
):
    width = x_ref.shape[-1]
    x, c = x_ref[0], c_ref[0]
    w_gate = w_ref[:, 0, 0].reshape(-1, width)
    w_up = w_ref[:, 1, 0].reshape(-1, width)
    w_down = w_ref[:, 2, 0].reshape(-1, width)
    gate = gate_ref[0]
    gate_pre = dot_nt(x, w_gate)
    up_pre = dot_nt(x, w_up)
    raw = dot_nt(c, w_down)
    sig = jax.nn.sigmoid(gate_pre)
    silu = gate_pre * sig
    act = silu * up_pre
    dgate_ref[0] = jnp.sum(act * raw, axis=-1, keepdims=True)
    act_low = (act * gate).astype(BF)
    d_act = raw * gate
    d_gate = (d_act * up_pre * sig * (1.0 + gate_pre * (1.0 - sig))).astype(BF)
    d_up = (d_act * silu).astype(BF)
    act_ref[0] = act_low
    dg_ref[0] = d_gate
    du_ref[0] = d_up
    out_ref[0] = dot_nn(act_low, w_down).astype(BF)
    dx_ref[0] = (dot_nn(d_gate, w_gate) + dot_nn(d_up, w_up)).astype(BF)


def experts_both_ways(x_slots, c_slots, w_all, slot_gate, first):
    _, number, width = x_slots.shape
    parts, _, local, hidden, _ = w_all.shape
    tile = number // 2
    taken = pl.BlockSpec((1, tile, width), lambda e, i: (first + e, i, 0))
    wide = pl.BlockSpec((1, tile, width), lambda e, i: (e, i, 0))
    mid = pl.BlockSpec((1, tile, parts * hidden), lambda e, i: (e, i, 0))
    thin = pl.BlockSpec((1, tile, 1), lambda e, i: (e, i, 0))
    wide_shape = jax.ShapeDtypeStruct((local, number, width), BF)
    mid_shape = jax.ShapeDtypeStruct((local, number, parts * hidden), BF)
    return pl.pallas_call(
        expert_kernel,
        grid=(local, 2),
        in_specs=[
            taken, taken,
            pl.BlockSpec((parts, 3, 1, hidden, width), lambda e, i: (0, 0, e, 0, 0)),
            pl.BlockSpec((1, tile, 1), lambda e, i: (first + e, i, 0)),
        ],
        out_specs=[wide, wide, mid, mid, mid, thin],
        out_shape=[
            wide_shape, wide_shape, mid_shape, mid_shape, mid_shape,
            jax.ShapeDtypeStruct((local, number, 1), F32),
        ],
        compiler_params=params(),
        name="experts_both_ways",
    )(x_slots, c_slots, w_all, slot_gate)


def expert_grads_kernel(x_ref, c_ref, act_ref, dg_ref, du_ref, out_ref):
    parts, _, _, hidden, width = out_ref.shape
    x, c = x_ref[0], c_ref[0]
    out_ref[:, 0, 0] = dot_tn(dg_ref[0], x).astype(BF).reshape(parts, hidden, width)
    out_ref[:, 1, 0] = dot_tn(du_ref[0], x).astype(BF).reshape(parts, hidden, width)
    out_ref[:, 2, 0] = dot_tn(act_ref[0], c).astype(BF).reshape(parts, hidden, width)


def expert_grads(x_slots, c_slots, act, d_gate, d_up, parts, first):
    local, number, inner = act.shape
    width = x_slots.shape[-1]
    wide = pl.BlockSpec((1, number, width), lambda e: (first + e, 0, 0))
    mid = pl.BlockSpec((1, number, inner), lambda e: (e, 0, 0))
    return pl.pallas_call(
        expert_grads_kernel,
        grid=(local,),
        in_specs=[wide, wide, mid, mid, mid],
        out_specs=pl.BlockSpec(
            (parts, 3, 1, inner // parts, width), lambda e: (0, 0, e, 0, 0)
        ),
        out_shape=jax.ShapeDtypeStruct((parts, 3, local, inner // parts, width), BF),
        compiler_params=params(),
        name="expert_grads",
    )(x_slots, c_slots, act, d_gate, d_up)


def combine_kernel(
    first_ref, slot_ref, dxa_ref, dxb_ref, outa_ref, outb_ref, dgate_ref, dx_sum_ref, out_sum_ref, pay_ref
):
    _, _, capacity, width = dxa_ref.shape
    local = slot_ref.shape[2]
    rows = slot_ref.shape[1]
    lane = lax.broadcasted_iota(jnp.int32, (rows, local * capacity), 1)
    half = pay_ref.shape[2] // 2
    column = lax.broadcasted_iota(jnp.int32, (rows, 2 * half), 1)
    total = jnp.zeros((rows, local * capacity), F32)
    pay = jnp.zeros(column.shape, F32)
    for e in range(local):
        hit = lane == slot_ref[0, :, e : e + 1] + e * capacity
        total = jnp.where(hit, 1.0, total)
        value = jnp.sum(jnp.where(hit, dgate_ref[0], 0.0), axis=1, keepdims=True)
        high = value.astype(BF).astype(F32)
        pay = jnp.where(column == first_ref[0, 0] + e, high, pay)
        pay = jnp.where(column == first_ref[0, 0] + e + half, value - high, pay)
    place = total.astype(BF)

    def both(a_ref, b_ref):
        pair = [ref[...].reshape(-1, width) for ref in (a_ref, b_ref)]
        return dot_nn(place, jnp.concatenate(pair, axis=0)).astype(BF)

    dx_sum_ref[0] = both(dxa_ref, dxb_ref)
    out_sum_ref[0] = both(outa_ref, outb_ref)
    pay_ref[0] = pay.astype(BF)


def combine_rows(first, slots_t, dx, out, d_gate_slots, experts):
    blocks, rows, local = slots_t.shape
    _, _, capacity, width = dx[0].shape
    lanes = -(-2 * experts // 128) * 128
    slot = pl.BlockSpec((local // 2, 1, capacity, width), lambda b: (0, b, 0, 0))
    block = pl.BlockSpec((1, rows, width), lambda b: (b, 0, 0))
    shape = jax.ShapeDtypeStruct((blocks, rows, width), BF)
    return pl.pallas_call(
        combine_kernel,
        grid=(blocks,),
        in_specs=[
            pl.BlockSpec(memory_space=pltpu.SMEM),
            pl.BlockSpec((1, rows, local), lambda b: (b, 0, 0)), slot, slot, slot, slot,
            pl.BlockSpec((1, 1, local * capacity), lambda b: (b, 0, 0)),
        ],
        out_specs=[block, block, pl.BlockSpec((1, rows, lanes), lambda b: (b, 0, 0))],
        out_shape=[shape, shape, jax.ShapeDtypeStruct((blocks, rows, lanes), BF)],
        compiler_params=params(),
        name="combine_rows",
    )(first, slots_t, *dx, *out, d_gate_slots)


def on_device(
    inputs,
    attn_gain,
    w_query,
    key_weight_matrix,
    value_weight_matrix,
    query_gain,
    key_gain,
    w_out,
    route_gain,
    w_router,
    w_gate,
    w_up,
    w_down,
    routes,
    image_starts,
    cotangent,
):
    tp_count = lax.axis_size("tp")
    ep_count = lax.axis_size("ep")
    tp_index = lax.axis_index("tp")
    ep_index = lax.axis_index("ep")
    length = inputs.shape[0]
    width = inputs.shape[1]
    rows = cotangent.shape[0]
    head_dim = query_gain.shape[0]
    local_experts = w_gate.shape[0]
    experts = local_experts * ep_count
    top = routes.shape[1]
    capacity = -(-(3 * rows * top // (2 * experts)) // 16) * 16

    pair = local_experts // 2

    weights = (w_gate.transpose(0, 2, 1), w_up.transpose(0, 2, 1), w_down)
    w_first = lax.all_gather(pack_weights(weights, 0, pair), "tp")

    normed, queries, key_rows, values = project(
        inputs, attn_gain[None], w_query, key_weight_matrix, value_weight_matrix
    )
    cosine, sine = rope_tables(length, head_dim)
    q_gain, k_gain = query_gain[None], key_gain[None]
    x_rows = lax.dynamic_slice_in_dim(inputs, tp_index * rows, rows, 0)
    queries, second = lax.optimization_barrier((queries, pack_weights(weights, pair, pair)))
    w_second = lax.all_gather(second, "tp")
    heads, lse, hidden, moe_in, cot_all = attention(
        image_starts, queries, key_rows, values, cosine, sine, q_gain, k_gain,
        w_out, cotangent, x_rows, route_gain[None], 0,
    )
    logits = dot_nn(moe_in, w_router)
    router_probs = plain_softmax(logits)
    expert_ids = jnp.arange(experts, dtype=jnp.int32)
    ring_routes = lax.dynamic_index_in_dim(
        routes.reshape(ep_count, tp_count, rows, top), tp_index, 1, keepdims=False
    )
    my_routes = lax.dynamic_index_in_dim(ring_routes, ep_index, 0, keepdims=False)

    def routed_softmax(scores, picked):
        kept = jnp.where(picked, scores, MASKED)
        expo = jnp.where(picked, jnp.exp(kept - jnp.max(kept, axis=-1, keepdims=True)), 0.0)
        return expo / jnp.sum(expo, axis=-1, keepdims=True)

    my_pick = jnp.any(my_routes[:, :, None] == expert_ids[None, None, :], axis=1)
    gates = routed_softmax(logits, my_pick)
    all_pick = jnp.any(ring_routes[..., None] == expert_ids, axis=2)
    mask = lax.dynamic_slice_in_dim(all_pick, ep_index * local_experts, local_experts, 2)
    earlier = (jnp.arange(rows)[:, None] > jnp.arange(rows)[None, :]).astype(BF)
    slots_t = jnp.einsum(
        "tu,bue->bte", earlier, mask.astype(BF), preferred_element_type=F32
    ).astype(jnp.int32)
    slots_t = jnp.where(mask, slots_t, NOWHERE)
    slots = slots_t.transpose(0, 2, 1)
    ring = ep_count == 2 * Z_AXIS
    if ring:
        turned = lax.rem(expert_ids + ep_index * local_experts, experts)
        x_slots, c_slots, slot_gate = gather_select(
            moe_in,
            cot_all,
            slots,
            all_pick.astype(jnp.int32)[..., turned].transpose(0, 2, 1),
            w_router.T[turned],
            capacity,
            1,
        )
        slot_gate = slot_gate.reshape(local_experts, ep_count * capacity, 1)
    else:
        tokens_all = lax.all_gather(moe_in, "ep")
        logits_all = dot_nn(tokens_all.reshape(-1, width), w_router).reshape(ep_count, rows, experts)
        gate_of = lax.dynamic_slice_in_dim(
            routed_softmax(logits_all, all_pick), ep_index * local_experts, local_experts, 2
        )
        place = slots[:, :, None, :] == jnp.arange(capacity, dtype=jnp.int32)[:, None]
        slot_gate = jnp.sum(
            jnp.where(place, gate_of.transpose(0, 2, 1)[:, :, None, :], 0.0), axis=-1
        )
        slot_gate = slot_gate.transpose(1, 0, 2).reshape(local_experts, ep_count * capacity, 1)
        x_slots, c_slots = select_rows(slots, tokens_all, cot_all, capacity)
    flat = (local_experts, ep_count * capacity, width)
    x_slots, c_slots = x_slots.reshape(flat), c_slots.reshape(flat)

    def over_rings(grads):
        return lax.psum_scatter(grads.reshape(-1, width), "tp", scatter_dimension=0, tiled=True)

    out_a, dx_a, *inner_a, dg_a = experts_both_ways(x_slots, c_slots, w_first, slot_gate, 0)
    grads_a = expert_grads(x_slots, c_slots, *inner_a, tp_count, 0)
    x_slots, grads_a = lax.optimization_barrier((x_slots, grads_a))
    mine_a = over_rings(grads_a)
    out_b, dx_b, *inner_b, dg_b = experts_both_ways(x_slots, c_slots, w_second, slot_gate, pair)
    deep = (pair, ep_count, capacity, width)
    dx_slots = [dx_a.reshape(deep), dx_b.reshape(deep)]
    out_slots = [out_a.reshape(deep), out_b.reshape(deep)]
    d_gate_slots = (
        jnp.concatenate([dg_a, dg_b])
        .reshape(local_experts, ep_count, capacity)
        .transpose(1, 0, 2)
        .reshape(ep_count, 1, local_experts * capacity)
    )
    counts = jnp.sum((routes[:, :, None] == expert_ids[None, None, :]).astype(F32), axis=(0, 1))
    total_tokens = routes.shape[0]
    share = counts / (total_tokens * top)
    coeff = AUX * experts * share
    if ring:
        d_hidden, d_rows, router_part, route_gain_part, grads_b = input_grads(
            slots_t, d_gate_slots, dx_slots, x_slots, c_slots, inner_b,
            [
                hidden, moe_in, cotangent, route_gain[None], gates, router_probs,
                coeff[None], w_router.T,
            ],
            experts, tp_count, 2,
        )
    else:
        grads_b = expert_grads(x_slots, c_slots, *inner_b, tp_count, pair)
        dx_part, out_slots, gate_part = combine_rows(
            (ep_index * local_experts).reshape(1, 1), slots_t, dx_slots, out_slots, d_gate_slots, experts
        )
        dx_mine = lax.psum_scatter(dx_part, "ep", scatter_dimension=0).astype(F32)
        gate_mine = lax.psum_scatter(gate_part, "ep", scatter_dimension=0).astype(F32)
        lanes = gate_mine.shape[1] // 2
        d_gates = gate_mine[:, :experts] + gate_mine[:, lanes : lanes + experts]
        d_logits = gates * (d_gates - jnp.sum(gates * d_gates, axis=-1, keepdims=True))
        d_logits = d_logits + router_probs * (
            coeff - jnp.sum(router_probs * coeff, axis=-1, keepdims=True)
        )
        d_low = d_logits.astype(BF)
        router_part = dot_tn(d_low, moe_in)
        d_moe = dot_nt(d_low, w_router) + dx_mine
        back, route_gain_part = norm_back(d_moe, hidden, route_gain[None])
        d_hidden = cotangent.astype(F32) + back
        d_rows = d_hidden.astype(BF)
    d_rows, mine_a, grads_b = lax.optimization_barrier((d_rows, mine_a, grads_b))
    mine_b = over_rings(grads_b)
    mine_a, mine_b = [m.reshape(3, pair, -1, width) for m in (mine_a, mine_b)]
    w_gate_grad, w_up_grad, w_down_grad = widen_grads(mine_a, mine_b)
    w_gate_grad, w_up_grad = w_gate_grad.transpose(0, 2, 1), w_up_grad.transpose(0, 2, 1)
    prob_local = jnp.sum(router_probs, axis=0)
    d_queries, d_keys, d_values, query_gain_part, key_gain_part, d_branch, output = attention_back(
        image_starts, queries, key_rows, values, lse, cosine, sine, q_gain, k_gain,
        w_out, d_rows, slots_t, out_slots, hidden, 3,
    )
    w_query_grad, w_key_grad, w_value_grad, w_out_grad, inputs_grad, attn_gain_grad, small = projection_grads(
        normed, d_queries, d_keys, d_values, heads, d_branch,
        w_query, key_weight_matrix, value_weight_matrix,
        x_rows, d_hidden, attn_gain[None],
        [router_part, route_gain_part[0], query_gain_part[0], key_gain_part[0], prob_local],
        5,
    )
    w_router_grad, route_gain_grad, query_gain_grad, key_gain_grad, prob_all = small
    w_router_grad = w_router_grad.T
    attn_gain_grad = attn_gain_grad[0]
    aux_loss = experts * jnp.sum(share * (prob_all / total_tokens))
    return (
        output,
        aux_loss,
        inputs_grad,
        attn_gain_grad,
        w_query_grad,
        w_key_grad,
        w_value_grad,
        query_gain_grad,
        key_gain_grad,
        w_out_grad,
        route_gain_grad,
        w_router_grad,
        w_gate_grad,
        w_up_grad,
        w_down_grad,
    )


def solution(mesh):
    return jax.shard_map(
        on_device,
        mesh=mesh,
        in_specs=(
            P("ep", None),
            P(),
            P(None, "tp"),
            P(None, "tp"),
            P(None, "tp"),
            P(),
            P(),
            P("tp", None),
            P(),
            P(),
            P("ep", None, "tp"),
            P("ep", None, "tp"),
            P("ep", "tp", None),
            P(),
            P("ep", None),
            P(("ep", "tp"), None),
        ),
        out_specs=(
            P(("ep", "tp"), None),
            P(),
            P(("ep", "tp"), None),
            P(),
            P("ep", "tp"),
            P("ep", "tp"),
            P("ep", "tp"),
            P(),
            P(),
            P("tp", "ep"),
            P(),
            P(),
            P("ep", None, "tp"),
            P("ep", None, "tp"),
            P("ep", "tp", None),
        ),
        check_vma=False,
    )
```

```python
import functools

import jax
import jax.numpy as jnp
import numpy as np
from jax import lax
from jax.experimental import pallas as pl
from jax.experimental.pallas import tpu as pltpu
from jax.sharding import PartitionSpec as P

IMG = 256
EPS = 1e-06
AUX = 0.04
THETA = 1000000.0
MASKED = -1e30
NOWHERE = -(1 << 20)
BF = jnp.bfloat16
F32 = jnp.float32
VMEM_BYTES = 60 * 1024 * 1024


def dot_nn(a, b):
    return lax.dot_general(a, b, (((1,), (0,)), ((), ())), preferred_element_type=F32)


def dot_nt(a, b):
    return lax.dot_general(a, b, (((1,), (1,)), ((), ())), preferred_element_type=F32)


def dot_tn(a, b):
    return lax.dot_general(a, b, (((0,), (0,)), ((), ())), preferred_element_type=F32)


def params(**kw):
    return pltpu.CompilerParams(vmem_limit_bytes=VMEM_BYTES, **kw)


def rms_scale(value_rows):
    return lax.rsqrt(jnp.mean(value_rows * value_rows, axis=-1, keepdims=True) + EPS)


def plain_softmax(value_rows):
    top = jnp.max(value_rows, axis=-1, keepdims=True)
    expo = jnp.exp(value_rows - top)
    return expo / jnp.sum(expo, axis=-1, keepdims=True)


def rope_tables(length, size):
    half = size // 2
    freq = THETA ** (-2.0 * np.arange(half) / size)
    angle = np.arange(length)[:, None] * freq[None, :]
    cosine, sine = np.cos(angle), np.sin(angle)
    tables = (np.concatenate([cosine, cosine], axis=-1), np.concatenate([-sine, sine], axis=-1))
    return tuple(jnp.asarray(t, F32) for t in tables)


def turn(rows, cosine, sine):
    return rows * cosine + pltpu.roll(rows, rows.shape[-1] // 2, 1) * sine


def turn_back(rows, cosine, sine):
    return rows * cosine - pltpu.roll(rows, rows.shape[-1] // 2, 1) * sine


MESH = pl.DeviceIdType.MESH
ANY = pl.BlockSpec(memory_space=pl.ANY)
Z_AXIS = 4


def link_cost(us):
    return pl.CostEstimate(flops=0, bytes_accessed=int(us * 3.0e6), transcendentals=0)


def greet(partners):
    barrier = pltpu.get_barrier_semaphore()
    count = 0
    for there, device in partners:
        flag = jnp.asarray(there, jnp.int32)

        @pl.when(there)
        def _(device=device):
            pl.semaphore_signal(barrier, inc=1, device_id=device, device_id_type=MESH)

        count = count + flag
    pl.semaphore_wait(barrier, count)


def remote(src, dst, send, recv, device):
    return pltpu.make_async_remote_copy(
        src_ref=src, dst_ref=dst, send_sem=send, recv_sem=recv, device_id=device, device_id_type=MESH
    )


def ring_place():
    me = lax.axis_index("ep")
    z, y = me // 2, me % 2
    return me, z, y, {"ep": me + 2}, {"ep": me - 2}, {"ep": me + 1 - 2 * y}


def ring_pieces(ref, axis):
    unit = ref.shape[axis] // 16
    lead = (slice(None),) * axis
    return [
        ref.at[lead + (pl.ds(start * unit, count * unit),)]
        for start, count in ((0, 7), (7, 6), (13, 3))
    ]


class EpGather:
    def __init__(self, ins, outs, sems):
        self.ins, self.outs = ins, outs
        self.own_sem, self.up_send, self.up_recv, self.dn_send, self.dn_recv = sems[:5]
        self.y_send, self.y_recv = sems[5:]
        self.me, self.z, self.y, self.up, self.down, self.beside = ring_place()
        self.last = len(ins) - 1
        self.streams = [(a, a, self.y) for a in range(len(ins))]
        self.other = (self.last, len(ins), 1 - self.y)

    def partners(self):
        z = self.z
        return [(z < Z_AXIS - 1, self.up), (z > 0, self.down), (z >= 0, self.beside)]

    def block(self, a, zt, y):
        return self.outs[a].at[zt * 2 + y]

    def upward(self, src, stream, zt):
        a, i, y = stream
        return remote(src, self.block(a, zt, y), self.up_send.at[i, zt], self.up_recv.at[i, zt], self.up)

    def downward(self, src, stream, zt):
        a, i, y = stream
        return remote(src, self.block(a, zt, y), self.dn_send.at[i, zt], self.dn_recv.at[i, zt], self.down)

    def sideways(self, src, a, zt):
        return remote(
            src, self.block(a, zt, self.y), self.y_send.at[a, zt], self.y_recv.at[a, zt], self.beside
        )

    def both_ways(self, src, stream):
        z = self.z

        @pl.when(z < Z_AXIS - 1)
        def _():
            self.upward(src, stream, z).start()

        @pl.when(z > 0)
        def _():
            self.downward(src, stream, z).start()

    def start(self):
        self.sideways(self.ins[self.last], self.last, self.z).start()
        for stream in self.streams:
            a = stream[0]
            self.both_ways(self.ins[a], stream)
            if a != self.last:
                self.sideways(self.ins[a], a, self.z).start()
            pltpu.make_async_copy(self.ins[a], self.block(a, self.z, self.y), self.own_sem.at[a]).start()

    def cross(self):
        self.side_arrived(self.last, self.z)
        self.both_ways(self.block(self.last, self.z, 1 - self.y), self.other)

    def hop(self, d):
        z = self.z
        for stream in [self.other] + self.streams:
            a, _, y = stream

            @pl.when(z >= d)
            def _(a=a, y=y, stream=stream, zt=z - d):
                rows = self.block(a, zt, y)
                self.upward(rows, stream, zt).wait_recv()

                @pl.when(z < Z_AXIS - 1)
                def _():
                    self.upward(rows, stream, zt).start()

                if a != self.last:
                    self.sideways(rows, a, zt).start()

            @pl.when(z + d < Z_AXIS)
            def _(a=a, y=y, stream=stream, zt=z + d):
                rows = self.block(a, zt, y)
                self.downward(rows, stream, zt).wait_recv()

                @pl.when(z > 0)
                def _():
                    self.downward(rows, stream, zt).start()

                if a != self.last:
                    self.sideways(rows, a, zt).start()

    def own_done(self):
        for a, x in enumerate(self.ins):
            pltpu.make_async_copy(x, self.block(a, self.z, self.y), self.own_sem.at[a]).wait()

    def side_arrived(self, a, zt):
        rows = self.block(a, zt, 1 - self.y)
        remote(rows, rows, self.y_send.at[a, zt], self.y_recv.at[a, zt], self.beside).wait_recv()

    def side_done(self, zt):
        for a in range(self.last):
            self.side_arrived(a, zt)

    def sent(self):
        z = self.z
        self.sideways(self.block(self.last, z, self.y), self.last, z).wait_send()
        for stream in self.streams + [self.other]:
            a, _, y = stream
            for zt in range(Z_AXIS):
                src = self.block(a, zt, y)
                if a != self.last:
                    self.sideways(src, a, zt).wait_send()

                @pl.when((zt <= z) & (z < Z_AXIS - 1))
                def _(src=src, zt=zt, stream=stream):
                    self.upward(src, stream, zt).wait_send()

                @pl.when((zt >= z) & (z > 0))
                def _(src=src, zt=zt, stream=stream):
                    self.downward(src, stream, zt).wait_send()

    def finish(self):
        self.own_done()
        for zt in range(Z_AXIS):
            self.side_done(zt)
        self.sent()


def gather_sems():
    dma = pltpu.SemaphoreType.DMA
    return [dma((3,))] + [dma((4, Z_AXIS))] * 6


def one_hot(slots, capacity):
    local, rows = slots.shape
    slot = lax.broadcasted_iota(jnp.int32, (capacity, rows), 0)
    return [slot == slots[e : e + 1, :] for e in range(local)]


def gather_select_kernel(
    x_ref, cots_ref, slots_ref, picks_ref, router_ref, xs_ref, cs_ref, gate_ref,
    tokens, cots, chosen, load_sem, store_sem, *sems,
):
    local, _, capacity, width = xs_ref.shape
    blocks = tokens.shape[0]
    gather = EpGather(ring_pieces(x_ref, 0), ring_pieces(tokens, 1), sems)
    z, y = gather.z, gather.y
    greet(gather.partners())
    gather.start()

    def chosen_rows(j, rows):
        hits = one_hot(slots_ref[j], capacity)
        place = jnp.concatenate([h.astype(F32) for h in hits], axis=0).astype(BF)
        return dot_nn(place, rows).astype(BF).reshape(local, capacity, width), hits

    def load(j, slot):
        return pltpu.make_async_copy(cots_ref.at[j], cots.at[slot], load_sem.at[slot])

    def store(to, j, slot):
        return pltpu.make_async_copy(chosen.at[slot], to.at[:, j], store_sem.at[slot])

    load(0, 0).start()

    @pl.loop(0, blocks)
    def _(j):
        slot = lax.rem(j, 2)

        @pl.when(j + 1 < blocks)
        def _():
            load(j + 1, 1 - slot).start()

        load(j, slot).wait()

        @pl.when(j == 3)
        def _():
            gather.cross()

        @pl.when(j >= 2)
        def _():
            store(cs_ref, j - 2, slot).wait()

        chosen[slot] = chosen_rows(j, cots[slot])[0]
        store(cs_ref, j, slot).start()

    store(cs_ref, blocks - 2, 0).wait()
    store(cs_ref, blocks - 1, 1).wait()

    def take(j):
        rows = tokens[j]
        chosen[0], hits = chosen_rows(j, rows)
        copy = store(xs_ref, j, 0)
        copy.start()
        logits = dot_nt(router_ref[...], rows)
        picked = picks_ref[j] > 0
        kept = jnp.where(picked, logits, MASKED)
        expo = jnp.exp(kept - jnp.max(kept, axis=0, keepdims=True))
        expo = jnp.where(picked, expo, 0.0)
        gates = expo / jnp.sum(expo, axis=0, keepdims=True)
        for e, hit in enumerate(hits):
            gate_ref[e, j] = jnp.sum(jnp.where(hit, gates[e : e + 1, :], 0.0), axis=1, keepdims=True)
        copy.wait()

    gather.own_done()
    take(gather.me)
    for d in range(1, Z_AXIS + 1):
        if d < Z_AXIS:
            gather.hop(d)

        @pl.loop(0, 4)
        def _(i, d=d):
            beside = i >= 2
            far = jnp.where(beside, d - 1, d)
            zt = jnp.where(lax.rem(i, 2) == 0, z - far, z + far)
            there = (zt >= 0) & (zt < Z_AXIS) & ((i < 3) | (d > 1))

            @pl.when(there & beside)
            def _():
                gather.side_done(zt)

            @pl.when(there)
            def _():
                take(zt * 2 + jnp.where(beside, 1 - y, y))

    gather.sent()


def gather_select(rows, cot_all, slots, picks, router, capacity, number):
    ep_count = lax.axis_size("ep")
    _, local, block = slots.shape
    width = rows.shape[1]
    vmem = pl.BlockSpec(memory_space=pltpu.VMEM)
    dma = pltpu.SemaphoreType.DMA
    shape = (local, ep_count, capacity, width)
    return pl.pallas_call(
        gather_select_kernel,
        in_specs=[ANY, ANY, vmem, vmem, vmem],
        out_specs=[ANY, ANY, vmem],
        out_shape=[
            jax.ShapeDtypeStruct(shape, BF),
            jax.ShapeDtypeStruct(shape, BF),
            jax.ShapeDtypeStruct(shape[:3] + (1,), F32),
        ],
        scratch_shapes=[
            pltpu.VMEM((ep_count, block, width), BF),
            pltpu.VMEM((2, block, width), BF),
            pltpu.VMEM((2, local, capacity, width), BF),
            dma((2,)), dma((2,)),
        ]
        + gather_sems(),
        compiler_params=params(collective_id=number, has_side_effects=True),
        cost_estimate=link_cost(90.0),
        name="gather_select",
    )(rows, cot_all, slots, picks, router)


def add_rows(total, terms, chunk=16):
    @pl.loop(0, total.shape[0] // chunk)
    def _(i):
        rows = pl.ds(pl.multiple_of(i * chunk, chunk), chunk)
        value = terms[0][rows, :].astype(F32)
        for term in terms[1:]:
            value = value + term[rows, :].astype(F32)
        total[rows, :] = value.astype(total.dtype)


def scatter_order(z):
    table = ((3, 2, 1, 0), (3, 0, 2, 1), (0, 3, 1, 2), (0, 1, 2, 3))
    return [
        jnp.where(
            z == 0,
            table[0][k],
            jnp.where(z == 1, table[1][k], jnp.where(z == 2, table[2][k], table[3][k])),
        )
        for k in range(Z_AXIS)
    ]


class EpReduce:
    def __init__(self, ins, by_z, bufs, sems):
        self.ins, self.by_z = ins, by_z
        self.bufs = [bufs[2 * a : 2 * a + 2] for a in range(len(ins))]
        self.up_send, self.up_recv, self.dn_send, self.dn_recv, self.y_send, self.y_recv = sems
        self.me, self.z, self.y, self.up, self.down, self.beside = ring_place()
        self.order = scatter_order(self.z)
        self.streams = [(a, 0, self.y) for a in range(len(ins))]
        self.crossing = [(a, 1, 1 - self.y) for a in range(len(ins)) if by_z[a]]

    def partners(self):
        z = self.z
        return [(z < Z_AXIS - 1, self.up), (z > 0, self.down), (z >= 0, self.beside)]

    def mine(self, stream, zt):
        return self.ins[stream[0]].at[zt * 2 + stream[2]]

    def side(self, a, zt):
        return self.bufs[a][0].at[0 if self.by_z[a] else zt]

    def below(self, stream, zt):
        return self.bufs[stream[0]][1].at[stream[1] * (Z_AXIS + 1) + zt]

    def above(self, stream, zt, z):
        return self.below(stream, jnp.where(zt == z, Z_AXIS, zt))

    def to_side(self, a, zt):
        src = self.ins[a].at[zt * 2 + 1 - self.y]
        return remote(src, self.side(a, zt), self.y_send.at[a, zt], self.y_recv.at[a, zt], self.beside)

    def rising(self, stream, zt):
        i = 2 * stream[0] + stream[1]
        return remote(
            self.mine(stream, zt), self.below(stream, zt), self.up_send.at[i, zt], self.up_recv.at[i, zt], self.up
        )

    def falling(self, stream, zt):
        i = 2 * stream[0] + stream[1]
        return remote(
            self.mine(stream, zt), self.above(stream, zt, self.z - 1),
            self.dn_send.at[i, zt], self.dn_recv.at[i, zt], self.down,
        )

    def send_side(self, k):
        for a, by_z in enumerate(self.by_z):
            if not by_z:
                self.to_side(a, self.order[k]).start()

    def step_y(self, k):
        self.step(k, [s for s in self.streams if not self.by_z[s[0]]])

    def step(self, k, streams):
        z, zt, last = self.z, self.order[k], Z_AXIS - 1
        for stream in streams:
            a = stream[0]
            mine = self.mine(stream, zt)
            terms = [mine]
            if not self.by_z[a]:
                self.to_side(a, zt).wait_recv()
                terms = [mine, self.side(a, zt)]
                ends = ((zt > z) & (z == 0)) | ((zt < z) & (z == last))

                @pl.when(ends)
                def _(mine=mine, terms=terms):
                    add_rows(mine, terms)

            @pl.when((zt > z) & (z > 0))
            def _(stream=stream, mine=mine, terms=terms):
                self.rising(stream, zt).wait_recv()
                add_rows(mine, terms + [self.below(stream, zt)])

            @pl.when((zt < z) & (z < last))
            def _(stream=stream, mine=mine, terms=terms):
                self.falling(stream, zt).wait_recv()
                add_rows(mine, terms + [self.above(stream, zt, z)])

            @pl.when(zt > z)
            def _(stream=stream):
                self.rising(stream, zt).start()

            @pl.when(zt < z)
            def _(stream=stream):
                self.falling(stream, zt).start()

    def gathered(self, stream, terms, write):
        z, last = self.z, Z_AXIS - 1

        @pl.when(z > 0)
        def _():
            self.rising(stream, z).wait_recv()

        @pl.when(z < last)
        def _():
            self.falling(stream, z).wait_recv()

        @pl.when(z == 0)
        def _():
            write(terms + [self.above(stream, z, z)])

        @pl.when(z == last)
        def _():
            write(terms + [self.below(stream, z)])

        @pl.when((z > 0) & (z < last))
        def _():
            write(terms + [self.below(stream, z), self.above(stream, z, z)])

    def own(self, a, write):
        if self.by_z[a]:
            self.to_side(a, self.z).wait_recv()
        stream = self.streams[a]
        self.gathered(stream, [self.mine(stream, self.z), self.side(a, self.z)], write)

    def sent(self):
        z = self.z
        for stream in self.streams + self.crossing:
            a = stream[0]
            for zt in range(Z_AXIS):
                if not self.by_z[a]:
                    self.to_side(a, zt).wait_send()

                @pl.when(zt > z)
                def _(stream=stream, zt=zt):
                    self.rising(stream, zt).wait_send()

                @pl.when(zt < z)
                def _(stream=stream, zt=zt):
                    self.falling(stream, zt).wait_send()

        for stream in self.crossing:
            self.to_side(stream[0], z).wait_send()


def reduce_scratch(rows, columns):
    return [pltpu.VMEM((n, rows // 2, columns), BF) for n in (Z_AXIS, Z_AXIS + 1)] * 2


BY_Z = [False, False]


def halves(ref, axis):
    n = ref.shape[axis] // 2
    lead = (slice(None),) * axis
    return [ref.at[lead + (pl.ds(h * n, n),)] for h in range(2)]


def reduce_sems(count):
    dma = pltpu.SemaphoreType.DMA
    return [dma((2 * count, Z_AXIS))] * 4 + [dma((count, Z_AXIS))] * 2


def widen_kernel(a_ref, b_ref, gate_ref, up_ref, down_ref):
    for kind, out in enumerate((gate_ref, up_ref, down_ref)):
        for half, ref in enumerate((a_ref, b_ref)):

            @pl.when(pl.program_id(0) == half)
            def _(kind=kind, out=out, ref=ref):
                out[...] = ref[kind].astype(F32)


def widen_grads(a, b):
    _, pair, hidden, width = a.shape
    shape = jax.ShapeDtypeStruct((2 * pair, hidden, width), F32)
    tile = width // 2
    return pl.pallas_call(
        widen_kernel,
        grid=(2, pair, 2),
        in_specs=[
            pl.BlockSpec(
                (3, 1, hidden, tile),
                lambda h, e, i: (0, jnp.where(h == 0, e, pair - 1), 0, jnp.where(h == 0, i, 1)),
            ),
            pl.BlockSpec(
                (3, 1, hidden, tile),
                lambda h, e, i: (0, jnp.where(h == 0, 0, e), 0, jnp.where(h == 0, 0, i)),
            ),
        ],
        out_specs=[pl.BlockSpec((1, hidden, tile), lambda h, e, i: (h * pair + e, 0, i))] * 3,
        out_shape=[shape] * 3,
        compiler_params=params(),
        name="widen_grads",
    )(a, b)


def token_hits(slots, capacity):
    rows, local = slots.shape
    lane = lax.broadcasted_iota(jnp.int32, (rows, local * capacity), 1)
    return [lane == slots[:, e : e + 1] + e * capacity for e in range(local)]


class SlotSums:
    def __init__(self, slots, first, second, buf, sem):
        self.slots, self.pair, self.buf, self.sem = slots, (first, second), buf, sem
        self.capacity = first.shape[2]

    def copies(self, j, at):
        n = self.pair[0].shape[0]
        return [
            pltpu.make_async_copy(
                ref.at[:, j], self.buf.at[at, pl.ds(i * n, n)], self.sem.at[at, i]
            )
            for i, ref in enumerate(self.pair)
        ]

    def fetch(self, j, at):
        for copy in self.copies(j, at):
            copy.start()

    def add(self, j, at, out):
        for copy in self.copies(j, at):
            copy.wait()
        place = jnp.zeros((), F32)
        for hit in token_hits(self.slots[j], self.capacity):
            place = jnp.where(hit, 1.0, place)
        rows = self.buf[at].reshape(-1, out.shape[1])
        out[...] = dot_nn(place.astype(BF), rows).astype(BF)

    def run(self, blocks, out, then):
        self.fetch(blocks[0], 0)
        for n, j in enumerate(blocks):
            if n + 1 < len(blocks):
                self.fetch(blocks[n + 1], (n + 1) % 2)
            self.add(j, n % 2, out.at[j])
            then(n)


def slot_sums_scratch(local, capacity, width):
    return [
        pltpu.VMEM((2, local, capacity, width), BF),
        pltpu.SemaphoreType.DMA((2, 2)),
    ]


def input_grads_kernel(
    slots, dgate, dx_a, dx_b, xs, cs, act, d_gate, d_up,
    residual, moe_in, cot, route_gain, gate_dense, probs, coeff, router,
    d_hidden, d_rows, router_part, gain_part, grads,
    out, gate_out, part, gates, buf, sem, x_in, c_in, h_in, w_buf, in_sem, w_sem, *refs,
):
    sums = SlotSums(slots, dx_a, dx_b, buf, sem)
    reduce = EpReduce(halves(part, 1) + [gates], BY_Z + [False], refs[:6], refs[6:])
    order, y = reduce.order, reduce.y
    pair, number, inner = act.shape
    parts, _, _, hidden, width = grads.shape
    first = xs.shape[0] - pair
    pieces = width // x_in.shape[1]
    wide = x_in.shape[1]
    greet(reduce.partners())

    def cols(piece):
        return pl.ds(piece * wide, wide)

    def wide_copies(unit):
        e, piece = unit // pieces, unit % pieces
        return [
            pltpu.make_async_copy(xs.at[first + e, :, cols(piece)], x_in, in_sem.at[0]),
            pltpu.make_async_copy(cs.at[first + e, :, cols(piece)], c_in, in_sem.at[1]),
        ]

    def inner_copies(e):
        return [
            pltpu.make_async_copy(ref.at[e], h_in.at[kind], in_sem.at[2 + kind])
            for kind, ref in enumerate((d_gate, d_up, act))
        ]

    def written(unit):
        e, piece = unit // pieces, unit % pieces
        return pltpu.make_async_copy(w_buf, grads.at[:, :, e, :, cols(piece)], w_sem)

    def prepare(unit):
        for copy in wide_copies(unit) + (inner_copies(unit // pieces) if unit % pieces == 0 else []):
            copy.start()

    def weights(unit):
        for copy in wide_copies(unit) + (inner_copies(unit // pieces) if unit % pieces == 0 else []):
            copy.wait()
        if unit > 0:
            written(unit - 1).wait()
        for kind, right in enumerate((x_in, x_in, c_in)):
            grad = dot_tn(h_in[kind], right[...]).astype(BF)
            w_buf[:, kind] = grad.reshape(parts, hidden, wide)
        written(unit).start()
        if unit + 1 < pair * pieces:
            prepare(unit + 1)

    def payload(j):
        lanes = gates.shape[2]
        column = lax.broadcasted_iota(jnp.int32, (gates.shape[1], lanes), 1)
        pay = jnp.zeros(column.shape, F32)
        mine = reduce.me * slots.shape[2]
        for e, hit in enumerate(token_hits(slots[j], sums.capacity)):
            value = jnp.sum(jnp.where(hit, dgate[j], 0.0), axis=1, keepdims=True)
            high = value.astype(BF).astype(F32)
            pay = jnp.where(column == mine + e, high, pay)
            pay = jnp.where(column == mine + e + lanes // 2, value - high, pay)
        gates[j] = pay.astype(BF)

    def send(k):
        payload(order[k] * 2 + 1 - y)
        reduce.send_side(k)

    units = pair * pieces
    quarter = [range(units * k // Z_AXIS, units * (k + 1) // Z_AXIS) for k in range(Z_AXIS)]
    sums.run([order[k] * 2 + 1 - y for k in range(Z_AXIS)], part, send)
    prepare(0)
    sums.run(
        [order[k] * 2 + y for k in range(Z_AXIS)], part, lambda k: payload(order[k] * 2 + y)
    )
    for k in range(Z_AXIS):
        for unit in quarter[k]:
            weights(unit)
        reduce.step_y(k)
    for a, rows in enumerate(halves(out, 0) + [gate_out]):
        reduce.own(a, functools.partial(add_rows, rows))

    experts, lanes = gate_dense.shape[1], gates.shape[2]
    d_gates = gate_out[:, 0:experts] + gate_out[:, lanes // 2 : lanes // 2 + experts]
    gate, prob = gate_dense[...], probs[...]
    d_logits = gate * (d_gates - jnp.sum(gate * d_gates, axis=-1, keepdims=True))
    d_logits = d_logits + prob * (coeff[...] - jnp.sum(prob * coeff[...], axis=-1, keepdims=True))
    d_low = d_logits.astype(BF)
    router_part[...] = dot_tn(d_low, moe_in[...])
    out[...] += dot_nn(d_low, router[...])
    gain_part[...] = jnp.zeros_like(gain_part)
    chunk = 16

    @pl.loop(0, out.shape[0] // chunk)
    def _(i):
        lines = pl.ds(pl.multiple_of(i * chunk, chunk), chunk)
        back, gain_rows = norm_back(out[lines, :], residual[lines, :], route_gain[...])
        total = back + cot[lines, :].astype(F32)
        d_hidden[lines, :] = total
        d_rows[lines, :] = total.astype(BF)
        gain_part[...] += gain_rows

    reduce.sent()
    written(units - 1).wait()


def input_grads(slots_t, dgate, dx, x_slots, c_slots, inner, row_values, experts, tp_count, number):
    ep_count, rows, local = slots_t.shape
    pair, _, capacity, width = dx[0].shape
    count, hidden = inner[0].shape[1:]
    lanes = -(-2 * experts // 128) * 128
    wide = width // 2
    dma = pltpu.SemaphoreType.DMA
    vmem = pl.BlockSpec(memory_space=pltpu.VMEM)
    return pl.pallas_call(
        input_grads_kernel,
        in_specs=[vmem, vmem] + [ANY] * 7 + [vmem] * 8,
        out_specs=[vmem] * 4 + [ANY],
        out_shape=[
            jax.ShapeDtypeStruct((rows, width), F32),
            jax.ShapeDtypeStruct((rows, width), BF),
            jax.ShapeDtypeStruct((experts, width), F32),
            jax.ShapeDtypeStruct((1, width), F32),
            jax.ShapeDtypeStruct((tp_count, 3, pair, hidden // tp_count, width), BF),
        ],
        scratch_shapes=[
            pltpu.VMEM((rows, width), F32),
            pltpu.VMEM((rows, lanes), F32),
            pltpu.VMEM((ep_count, rows, width), BF),
            pltpu.VMEM((ep_count, rows, lanes), BF),
        ]
        + slot_sums_scratch(local, capacity, width)
        + [
            pltpu.VMEM((count, wide), BF),
            pltpu.VMEM((count, wide), BF),
            pltpu.VMEM((3, count, hidden), BF),
            pltpu.VMEM((tp_count, 3, hidden // tp_count, wide), BF),
            dma((5,)), dma,
        ]
        + reduce_scratch(rows, width)
        + [pltpu.VMEM((n, rows, lanes), BF) for n in (Z_AXIS, Z_AXIS + 1)]
        + reduce_sems(3),
        compiler_params=params(collective_id=number, has_side_effects=True),
        cost_estimate=link_cost(100.0),
        name="input_grads",
    )(slots_t, dgate, *dx, x_slots, c_slots, *inner, *row_values)


class Exchange:
    def __init__(self, axis, send, recv):
        self.axis, self.send, self.recv = axis, send, recv
        self.count, self.me = lax.axis_size(axis), lax.axis_index(axis)

    def each(self, act):
        for i in range(1, self.count):
            act(i, lax.rem(self.me + i, self.count))

    def to(self, src, dst, i, other):
        return remote(src, dst, self.send.at[i], self.recv.at[self.me], {self.axis: other})

    def start(self, src_of, dst):
        self.each(lambda i, other: self.to(src_of(other), dst.at[self.me], i, other).start())

    def arrived(self, dst):
        self.each(
            lambda i, other: remote(
                dst.at[other], dst.at[other], self.send.at[i], self.recv.at[other], {self.axis: other}
            ).wait_recv()
        )

    def sent(self, src_of, dst):
        self.each(lambda i, other: self.to(src_of(other), dst.at[self.me], i, other).wait_send())


class SumAll:
    def __init__(self, x, out, over_tp, own_tp, over_ep, own, ring, sems):
        self.x, self.out, self.over_tp, self.own_tp = x, out, over_tp, own_tp
        self.over_ep, self.own, self.ring = over_ep, own, ring
        self.first = Exchange("tp", sems[0], sems[1])
        self.second = Exchange("ep", sems[2], sems[3])
        self.third = Exchange("ep", sems[4], sems[5])
        self.fourth = Exchange("tp", sems[6], sems[7])

    def slice_tp(self, t):
        return self.x.at[t]

    def slice_ep(self, e):
        return self.own_tp.at[e]

    def start(self):
        self.first.start(self.slice_tp, self.over_tp)
        me = self.first.me
        self.over_tp[pl.ds(me, 1)] = self.x[pl.ds(me, 1)]

    def across(self):
        self.first.arrived(self.over_tp)
        self.own_tp[...] = jnp.sum(self.over_tp[...], axis=0)
        self.second.start(self.slice_ep, self.over_ep)
        me = self.second.me
        self.over_ep[pl.ds(me, 1)] = self.own_tp[pl.ds(me, 1)]

    def back(self):
        self.second.arrived(self.over_ep)
        self.own[...] = jnp.sum(self.over_ep[...], axis=0)
        self.third.start(lambda e: self.own, self.ring)
        self.ring[pl.ds(self.third.me, 1)] = self.own[...][None]

    def home(self):
        self.third.arrived(self.ring)
        self.fourth.start(lambda t: self.ring, self.out)
        self.out[pl.ds(self.fourth.me, 1)] = self.ring[...][None]

    def finish(self):
        self.fourth.arrived(self.out)
        self.first.sent(self.slice_tp, self.over_tp)
        self.second.sent(self.slice_ep, self.over_ep)
        self.third.sent(lambda e: self.own, self.ring)
        self.fourth.sent(lambda t: self.ring, self.out)


def exchange_sems(axis):
    return [pltpu.SemaphoreType.DMA((lax.axis_size(axis),))] * 2


def sum_scratch(shape):
    tp, ep, rows, lanes = shape
    return [
        pltpu.VMEM(shape, F32), pltpu.VMEM((ep, rows, lanes), F32), pltpu.VMEM((ep, rows, lanes), F32),
        pltpu.VMEM((rows, lanes), F32), pltpu.VMEM((ep, rows, lanes), F32),
    ] + [sem for axis in ("tp", "ep", "ep", "tp") for sem in exchange_sems(axis)]


def pack_small(values, tp, ep):
    total = tp * ep
    flat = jnp.concatenate([v.reshape(-1) for v in values])
    rows = -(-flat.shape[0] // (total * 128 * 8)) * 8
    return jnp.pad(flat, (0, total * rows * 128 - flat.shape[0])).reshape(tp, ep, rows, 128)


def unpack_small(summed, values):
    summed = summed.reshape(-1)
    out, at = [], 0
    for v in values:
        out.append(summed[at : at + v.size].reshape(v.shape))
        at += v.size
    return out


def project_kernel(x_ref, gain_ref, wq_ref, wk_ref, wv_ref, normed_ref, q_ref, k_ref, v_ref):
    x = x_ref[...].astype(F32)
    normed = (x * rms_scale(x) * gain_ref[...]).astype(BF)
    normed_ref[...] = normed
    q_ref[...] = dot_nn(normed, wq_ref[...])
    k_ref[...] = dot_nn(normed, wk_ref[...])
    v_ref[...] = dot_nn(normed, wv_ref[...]).astype(BF)


def project(inputs, gain, wq, wk, wv):
    length, width = inputs.shape
    tile = min(256, length)

    def rows(columns):
        return pl.BlockSpec((tile, columns), lambda i: (i, 0))

    def fixed(array):
        return pl.BlockSpec(array.shape, lambda i: (0, 0), pipeline_mode=pl.Buffered(1))

    return pl.pallas_call(
        project_kernel,
        grid=(length // tile,),
        in_specs=[rows(width), fixed(gain), fixed(wq), fixed(wk), fixed(wv)],
        out_specs=[rows(width), rows(wq.shape[1]), rows(wk.shape[1]), rows(wv.shape[1])],
        out_shape=[
            jax.ShapeDtypeStruct((length, width), BF),
            jax.ShapeDtypeStruct((length, wq.shape[1]), F32),
            jax.ShapeDtypeStruct((length, wk.shape[1]), F32),
            jax.ShapeDtypeStruct((length, wv.shape[1]), BF),
        ],
        compiler_params=params(),
        name="project",
    )(inputs, gain, wq, wk, wv)


def fill_bias(span_ref, bias, chunk=256):
    keys, length = bias.shape
    query = lax.broadcasted_iota(jnp.int32, (1, length), 1)

    def spans(pos):
        first = (pos >= span_ref[0, 0]) & (pos < span_ref[0, 0] + IMG)
        second = (pos >= span_ref[0, 1]) & (pos < span_ref[0, 1] + IMG)
        return jnp.where(first, 0, jnp.where(second, 1, -1))

    query_span = spans(query)
    query_other = jnp.where(query_span < 0, -2, query_span)
    for start in range(0, keys, chunk):
        key = start + lax.broadcasted_iota(jnp.int32, (chunk, 1), 0)
        ok = (key <= query) | (spans(key) == query_other)
        bias[start : start + chunk, :] = jnp.where(ok, 0.0, MASKED)


def query_tiles(length):
    tile = min(IMG, length)
    return [
        (start, tile, min(length, start + tile + -(-IMG // tile) * tile))
        for start in range(0, length, tile)
    ]


def attention_kernel(
    span_ref, q_ref, k_ref, v_ref, cos_ref, sin_ref, qg_ref, kg_ref, w_out_ref, cot_ref, x_ref, gain_ref, wg_ref, wu_ref, wd_ref,
    out_ref, lse_ref, rows_ref, moe_ref, cots_ref, pack_ref,
    bias, k_rot, v_t, heads, part, core_rows, x_rows, core_send, core_recv, x_send, x_recv, *sems,
):
    factor = q_ref.shape[-1] ** (-0.5)
    cosine, sine = cos_ref[...], sin_ref[...]
    step = pl.program_id(0)
    size = q_ref.shape[-1]
    me = lax.axis_index("tp")
    x, c = me // 2, me % 2
    other_core, other_x = {"tp": x * 2 + 1 - c}, {"tp": (1 - x) * 2 + c}
    gather = EpGather(ring_pieces(cot_ref, 0), ring_pieces(cots_ref, 1), sems)
    for kind, ref in enumerate((wg_ref, wu_ref, wd_ref)):
        pack_ref[kind] = ref[...]

    @pl.when(step == 0)
    def _():
        greet(gather.partners() + [(x >= 0, other_core), (x >= 0, other_x)])
        gather.start()
        fill_bias(span_ref, bias)
        k = k_ref[...]
        k_rot[...] = turn(k * rms_scale(k) * kg_ref[...], cosine, sine).astype(BF)
        v_t[...] = v_ref[...].astype(F32).T.astype(BF)

    @pl.when(step == 2)
    def _():
        gather.cross()

    @pl.when(step == pl.num_programs(0) - 2)
    def _():
        gather.hop(1)

    q = q_ref[...]
    q_rot = turn(q * rms_scale(q) * qg_ref[...], cosine, sine).astype(BF)
    for start, tile, keys in query_tiles(q.shape[0]):
        cols = slice(start, start + tile)
        s = dot_nt(k_rot[:keys, :], q_rot[cols, :]) * factor + bias[:keys, cols]
        top = jnp.max(s, axis=0, keepdims=True)
        p = jnp.exp(s - top)
        total = jnp.sum(p, axis=0, keepdims=True)
        o_t = dot_nn(v_t[:, :keys], p.astype(BF)) / total
        rows = o_t.T.astype(BF)
        out_ref[cols, :] = rows
        heads[step, cols, :] = rows
        lse_ref[0, :, cols] = top + jnp.log(total)

    @pl.when(step == pl.num_programs(0) - 1)
    def _():
        count = heads.shape[0]
        block = rows_ref.shape[0]

        def project(tp):
            lines = pl.ds(pl.multiple_of(tp * block, block), block)
            rows = jnp.concatenate([heads[h, lines, :] for h in range(count)], axis=1)
            part[tp] = dot_nn(rows, w_out_ref[...]).astype(BF)

        def to_core(xt):
            return remote(
                part.at[xt * 2 + 1 - c], core_rows.at[xt],
                core_send.at[xt], core_recv.at[xt], other_core,
            )

        far, near = part.at[(1 - x) * 2 + c], part.at[x * 2 + c]
        to_x = remote(far, x_rows, x_send, x_recv, other_x)
        project((1 - x) * 2 + 1 - c)
        to_core(1 - x).start()
        project((1 - x) * 2 + c)
        to_core(1 - x).wait_recv()
        add_rows(far, [far, core_rows.at[1 - x]])
        to_x.start()
        project(x * 2 + 1 - c)
        to_core(x).start()
        project(x * 2 + c)
        gather.hop(2)
        to_core(x).wait_recv()
        gather.hop(3)
        to_x.wait_recv()
        chunk = 16

        @pl.loop(0, block // chunk)
        def _(i):
            lines = pl.ds(pl.multiple_of(i * chunk, chunk), chunk)
            total = near[lines, :].astype(F32) + core_rows[x, lines, :].astype(F32)
            hidden = x_ref[lines, :].astype(F32) + (total + x_rows[lines, :].astype(F32))
            rows_ref[lines, :] = hidden
            moe_ref[lines, :] = (hidden * rms_scale(hidden) * gain_ref[...]).astype(BF)

        gather.finish()
        to_core(1 - x).wait_send()
        to_core(x).wait_send()
        to_x.wait_send()


def plain_attention_kernel(
    span_ref, q_ref, k_ref, v_ref, cos_ref, sin_ref, qg_ref, kg_ref, out_ref, lse_ref,
    bias, k_rot, v_t,
):
    factor = q_ref.shape[-1] ** (-0.5)
    cosine, sine = cos_ref[...], sin_ref[...]

    @pl.when(pl.program_id(0) == 0)
    def _():
        fill_bias(span_ref, bias)
        k = k_ref[...]
        k_rot[...] = turn(k * rms_scale(k) * kg_ref[...], cosine, sine).astype(BF)
        v_t[...] = v_ref[...].astype(F32).T.astype(BF)

    q = q_ref[...]
    q_rot = turn(q * rms_scale(q) * qg_ref[...], cosine, sine).astype(BF)
    for start, tile, keys in query_tiles(q.shape[0]):
        cols = slice(start, start + tile)
        s = dot_nt(k_rot[:keys, :], q_rot[cols, :]) * factor + bias[:keys, cols]
        top = jnp.max(s, axis=0, keepdims=True)
        p = jnp.exp(s - top)
        total = jnp.sum(p, axis=0, keepdims=True)
        o_t = dot_nn(v_t[:, :keys], p.astype(BF)) / total
        out_ref[cols, :] = o_t.T.astype(BF)
        lse_ref[0, :, cols] = top + jnp.log(total)


def attention(span, q, k, v, cosine, sine, q_gain, k_gain, w_out, cotangent, x_rows, route_gain, weights, pair, number):
    length, size = k.shape
    heads = q.shape[1] // size
    whole = pl.BlockSpec((length, size), lambda h: (0, 0))
    head = pl.BlockSpec((length, size), lambda h: (0, h))
    gain = pl.BlockSpec((1, size), lambda h: (0, 0))
    in_specs = [
        pl.BlockSpec(memory_space=pltpu.SMEM), head, whole, whole, whole, whole, gain, gain,
    ]
    out_specs = [head, pl.BlockSpec((1, 1, length), lambda h: (h, 0, 0))]
    out_shape = [
        jax.ShapeDtypeStruct((length, heads * size), BF),
        jax.ShapeDtypeStruct((heads, 1, length), F32),
    ]
    scratch = [
        pltpu.VMEM((length, length), F32),
        pltpu.VMEM((length, size), BF),
        pltpu.VMEM((size, length), BF),
    ]
    args = (span, q, k, v, cosine, sine, q_gain, k_gain)
    ep_count, tp_count = lax.axis_size("ep"), lax.axis_size("tp")
    if ep_count != 2 * Z_AXIS:
        out, lse = pl.pallas_call(
            plain_attention_kernel,
            grid=(heads,),
            in_specs=in_specs,
            out_specs=out_specs,
            out_shape=out_shape,
            scratch_shapes=scratch,
            compiler_params=params(),
            name="plain_attention",
        )(*args)
        rows = lax.psum_scatter(
            dot_nn(out, w_out).astype(BF), "tp", scatter_dimension=0, tiled=True
        )
        hidden = x_rows.astype(F32) + rows.astype(F32)
        moe_in = (hidden * rms_scale(hidden) * route_gain).astype(BF)
        packed = pack_weights(weights, weights[0].shape[0] - pair, pair)
        return out, lse, hidden, moe_in, lax.all_gather(cotangent, "ep"), packed
    block, width = cotangent.shape
    dma = pltpu.SemaphoreType.DMA
    first, hidden_units = weights[0].shape[0] - pair, weights[0].shape[1]
    pieces = heads // pair
    wide = width // pieces
    some = pl.BlockSpec((1, hidden_units, wide), lambda h: (first + h // pieces, 0, h % pieces))
    return pl.pallas_call(
        attention_kernel,
        grid=(heads,),
        in_specs=in_specs
        + [
            pl.BlockSpec(w_out.shape, lambda h: (0, 0), pipeline_mode=pl.Buffered(1)), ANY,
            pl.BlockSpec((block, width), lambda h: (0, 0)),
            pl.BlockSpec((1, width), lambda h: (0, 0)), some, some, some,
        ],
        out_specs=out_specs
        + [pl.BlockSpec((block, width), lambda h: (0, 0))] * 2
        + [ANY, pl.BlockSpec((3, 1, hidden_units, wide), lambda h: (0, h // pieces, 0, h % pieces))],
        out_shape=out_shape
        + [
            jax.ShapeDtypeStruct((block, width), F32),
            jax.ShapeDtypeStruct((block, width), BF),
            jax.ShapeDtypeStruct((ep_count, block, width), BF),
            jax.ShapeDtypeStruct((3, pair, hidden_units, width), BF),
        ],
        scratch_shapes=scratch
        + [
            pltpu.VMEM((heads, length, size), BF),
            pltpu.VMEM((tp_count, block, width), BF),
            pltpu.VMEM((2, block, width), BF),
            pltpu.VMEM((block, width), BF),
            dma((2,)), dma((2,)), dma, dma,
        ]
        + gather_sems(),
        compiler_params=params(collective_id=number, has_side_effects=True),
        cost_estimate=link_cost(90.0),
        name="attention",
    )(*args, w_out, cotangent, x_rows, route_gain, *weights)


def norm_back(grads, rows, gain):
    scale = rms_scale(rows)
    gain_part = jnp.sum(grads * rows * scale, axis=0, keepdims=True)
    inner = grads * gain
    mean = jnp.mean(inner * rows, axis=-1, keepdims=True)
    return scale * inner - rows * (scale * scale * scale * mean), gain_part


def plain_attention_back_kernel(
    span_ref, q_ref, k_ref, v_ref, grad_ref, lse_ref, cos_ref, sin_ref, qg_ref, kg_ref,
    dq_ref, dk_ref, dv_ref, dqg_ref, dkg_ref,
    bias, k_rot, k_t, dk_acc, dv_acc, dq_t,
):
    factor = q_ref.shape[-1] ** (-0.5)
    cosine, sine = cos_ref[...], sin_ref[...]
    step = pl.program_id(0)

    @pl.when(step == 0)
    def _():
        fill_bias(span_ref, bias)
        k = k_ref[...]
        rotated = turn(k * rms_scale(k) * kg_ref[...], cosine, sine)
        k_rot[...] = rotated.astype(BF)
        k_t[...] = rotated.T.astype(BF)
        dk_acc[...] = jnp.zeros_like(dk_acc)
        dv_acc[...] = jnp.zeros_like(dv_acc)
        dqg_ref[...] = jnp.zeros_like(dqg_ref)

    q = q_ref[...]
    q_rot = turn(q * rms_scale(q) * qg_ref[...], cosine, sine).astype(BF)
    for start, tile, keys in query_tiles(q.shape[0]):
        cols = slice(start, start + tile)
        s = dot_nt(k_rot[:keys, :], q_rot[cols, :]) * factor + bias[:keys, cols]
        p = jnp.exp(s - lse_ref[0, :, cols])
        grad = grad_ref[cols, :]
        dp = dot_nt(v_ref[:keys, :], grad)
        mean = jnp.sum(p * dp, axis=0, keepdims=True)
        raw = (p * (dp - mean) * factor).astype(BF)
        dq_t[:, cols] = dot_nn(k_t[:, :keys], raw)
        dk_acc[:keys, :] += dot_nn(raw, q_rot[cols, :])
        dv_acc[:keys, :] += dot_nn(p.astype(BF), grad)
    back, gain_part = norm_back(turn_back(dq_t[...].T, cosine, sine), q, qg_ref[...])
    dq_ref[...] = back.astype(BF)
    dqg_ref[...] += gain_part

    @pl.when(step == pl.num_programs(0) - 1)
    def _():
        back, gain_part = norm_back(turn_back(dk_acc[...], cosine, sine), k_ref[...], kg_ref[...])
        dk_ref[...] = back.astype(BF)
        dkg_ref[...] = gain_part
        dv_ref[...] = dv_acc[...].astype(BF)


def plain_attention_back(span, q, k, v, grads, lse, cosine, sine, q_gain, k_gain):
    length, size = k.shape
    heads = q.shape[1] // size
    whole = pl.BlockSpec((length, size), lambda h: (0, 0))
    head = pl.BlockSpec((length, size), lambda h: (0, h))
    gain = pl.BlockSpec((1, size), lambda h: (0, 0))
    return pl.pallas_call(
        plain_attention_back_kernel,
        grid=(heads,),
        in_specs=[
            pl.BlockSpec(memory_space=pltpu.SMEM), head, whole, whole, head,
            pl.BlockSpec((1, 1, length), lambda h: (h, 0, 0)), whole, whole, gain, gain,
        ],
        out_specs=[head, whole, whole, gain, gain],
        out_shape=[
            jax.ShapeDtypeStruct((length, heads * size), BF),
            jax.ShapeDtypeStruct((length, size), BF),
            jax.ShapeDtypeStruct((length, size), BF),
            jax.ShapeDtypeStruct((1, size), F32),
            jax.ShapeDtypeStruct((1, size), F32),
        ],
        scratch_shapes=[
            pltpu.VMEM((length, length), F32),
            pltpu.VMEM((length, size), BF),
            pltpu.VMEM((size, length), BF),
            pltpu.VMEM((length, size), F32),
            pltpu.VMEM((length, size), F32),
            pltpu.VMEM((size, length), F32),
        ],
        compiler_params=params(),
        name="plain_attention_back",
    )(span, q, k, v, grads, lse, cosine, sine, q_gain, k_gain)


def attention_back_kernel(
    span_ref, q_ref, k_ref, v_ref, lse_ref, cos_ref, sin_ref, qg_ref, kg_ref,
    w_out_ref, rows_ref, slots_ref, out_a, out_b, hidden_ref,
    dq_ref, dk_ref, dv_ref, dqg_ref, dkg_ref, branch_ref, output_ref,
    bias, k_rot, k_t, dk_acc, dv_acc, dq_t, branch, grads, part, buf, sem,
    own_sem, out_sem, core_send, core_recv, x_send, x_recv, *refs,
):
    factor = q_ref.shape[-1] ** (-0.5)
    size = q_ref.shape[-1]
    cosine, sine = cos_ref[...], sin_ref[...]
    step = pl.program_id(0)
    me = lax.axis_index("tp")
    x, c = me // 2, me % 2
    other_core, other_x = {"tp": x * 2 + 1 - c}, {"tp": (1 - x) * 2 + c}
    reduce = EpReduce(halves(part, 1), BY_Z, refs[:4], refs[4:])
    sums = SlotSums(slots_ref, out_a, out_b, buf, sem)
    order, y = reduce.order, reduce.y
    block = rows_ref.shape[0]
    near_other, far, far_other = x * 2 + 1 - c, (1 - x) * 2 + c, (1 - x) * 2 + 1 - c

    def to_core(slot, src, tp):
        return remote(src, branch.at[tp], core_send.at[slot], core_recv.at[slot], other_core)

    def to_x(tp):
        return remote(rows_ref, branch.at[tp], x_send, x_recv, other_x)

    def own_rows():
        return pltpu.make_async_copy(rows_ref, branch.at[me], own_sem)

    def whole_branch():
        return pltpu.make_async_copy(branch, branch_ref, out_sem)

    @pl.when(step == 0)
    def _():
        greet(reduce.partners() + [(x >= 0, other_core), (x >= 0, other_x)])
        to_x(me).start()
        to_core(0, rows_ref, me).start()
        own_rows().start()
        sums.run([order[k] * 2 + 1 - y for k in range(Z_AXIS)], part, reduce.send_side)
        fill_bias(span_ref, bias)
        k = k_ref[...]
        rotated = turn(k * rms_scale(k) * kg_ref[...], cosine, sine)
        k_rot[...] = rotated.astype(BF)
        k_t[...] = rotated.T.astype(BF)
        dk_acc[...] = jnp.zeros_like(dk_acc)
        dv_acc[...] = jnp.zeros_like(dv_acc)
        dqg_ref[...] = jnp.zeros_like(dqg_ref)

        def head_grads(tp):
            lines = pl.ds(pl.multiple_of(tp * block, block), block)
            rows = dot_nt(branch[tp], w_out_ref[...]).astype(BF)
            for h in range(grads.shape[0]):
                grads[h, lines, :] = rows[:, h * size : (h + 1) * size]

        own_rows().wait()
        head_grads(me)
        to_core(0, rows_ref, near_other).wait_recv()
        head_grads(near_other)
        sums.run([order[k] * 2 + y for k in range(Z_AXIS)], part, lambda k: None)
        reduce.step_y(0)
        to_x(far).wait_recv()
        to_core(1, branch.at[far], far).start()
        head_grads(far)
        to_core(1, branch.at[far], far_other).wait_recv()
        head_grads(far_other)
        whole_branch().start()

    for k, head in ((1, 1), (2, 5)):

        @pl.when(step == head)
        def _(k=k):
            reduce.step_y(k)

    q = q_ref[...]
    q_rot = turn(q * rms_scale(q) * qg_ref[...], cosine, sine).astype(BF)
    for start, tile, keys in query_tiles(q.shape[0]):
        cols = slice(start, start + tile)
        s = dot_nt(k_rot[:keys, :], q_rot[cols, :]) * factor + bias[:keys, cols]
        p = jnp.exp(s - lse_ref[0, :, cols])
        grad = grads[step, cols, :]
        dp = dot_nt(v_ref[:keys, :], grad)
        mean = jnp.sum(p * dp, axis=0, keepdims=True)
        raw = (p * (dp - mean) * factor).astype(BF)
        dq_t[:, cols] = dot_nn(k_t[:, :keys], raw)
        dk_acc[:keys, :] += dot_nn(raw, q_rot[cols, :])
        dv_acc[:keys, :] += dot_nn(p.astype(BF), grad)
    back, gain_part = norm_back(turn_back(dq_t[...].T, cosine, sine), q, qg_ref[...])
    dq_ref[...] = back.astype(BF)
    dqg_ref[...] += gain_part

    @pl.when(step == pl.num_programs(0) - 1)
    def _():
        back, gain_part = norm_back(turn_back(dk_acc[...], cosine, sine), k_ref[...], kg_ref[...])
        dk_ref[...] = back.astype(BF)
        dkg_ref[...] = gain_part
        dv_ref[...] = dv_acc[...].astype(BF)
        reduce.step_y(Z_AXIS - 1)
        pairs = zip(halves(output_ref, 0), halves(hidden_ref, 0))
        for a, (rows, residual) in enumerate(pairs):
            reduce.own(a, lambda terms, rows=rows, residual=residual: add_rows(rows, terms + [residual]))
        reduce.sent()
        whole_branch().wait()
        to_x(me).wait_send()
        to_core(0, rows_ref, me).wait_send()
        to_core(1, branch.at[far], far).wait_send()


def attention_back(
    span, q, k, v, lse, cosine, sine, q_gain, k_gain, w_out, d_rows, slots_t, out, hidden, number
):
    length, size = k.shape
    heads = q.shape[1] // size
    ep_count, tp_count = lax.axis_size("ep"), lax.axis_size("tp")
    if ep_count != 2 * Z_AXIS:
        branch = lax.all_gather(d_rows, "tp", axis=0, tiled=True)
        grads = dot_nt(branch, w_out).astype(BF)
        mine = lax.psum_scatter(out, "ep", scatter_dimension=0)
        back = plain_attention_back(span, q, k, v, grads, lse, cosine, sine, q_gain, k_gain)
        return *back, branch, (hidden + mine.astype(F32)).astype(BF)
    block, width = d_rows.shape
    whole = pl.BlockSpec((length, size), lambda h: (0, 0))
    head = pl.BlockSpec((length, size), lambda h: (0, h))
    gain = pl.BlockSpec((1, size), lambda h: (0, 0))
    rows = pl.BlockSpec((block, width), lambda h: (0, 0))
    dma = pltpu.SemaphoreType.DMA
    *back, branch, output = pl.pallas_call(
        attention_back_kernel,
        grid=(heads,),
        in_specs=[
            pl.BlockSpec(memory_space=pltpu.SMEM), head, whole, whole,
            pl.BlockSpec((1, 1, length), lambda h: (h, 0, 0)), whole, whole, gain, gain,
            pl.BlockSpec(w_out.shape, lambda h: (0, 0), pipeline_mode=pl.Buffered(1)), ANY,
            pl.BlockSpec(slots_t.shape, lambda h: (0, 0, 0), pipeline_mode=pl.Buffered(1)), ANY, ANY,
            pl.BlockSpec((block, width), lambda h: (0, 0), pipeline_mode=pl.Buffered(1)),
        ],
        out_specs=[head, whole, whole, gain, gain, ANY, rows],
        out_shape=[
            jax.ShapeDtypeStruct((length, heads * size), BF),
            jax.ShapeDtypeStruct((length, size), BF),
            jax.ShapeDtypeStruct((length, size), BF),
            jax.ShapeDtypeStruct((1, size), F32),
            jax.ShapeDtypeStruct((1, size), F32),
            jax.ShapeDtypeStruct((tp_count, block, width), BF),
            jax.ShapeDtypeStruct((block, width), BF),
        ],
        scratch_shapes=[
            pltpu.VMEM((length, length), F32),
            pltpu.VMEM((length, size), BF),
            pltpu.VMEM((size, length), BF),
            pltpu.VMEM((length, size), F32),
            pltpu.VMEM((length, size), F32),
            pltpu.VMEM((size, length), F32),
            pltpu.VMEM((tp_count, block, width), BF),
            pltpu.VMEM((heads, length, size), BF),
        ]
        + [pltpu.VMEM((ep_count, block, width), BF)]
        + slot_sums_scratch(slots_t.shape[2], out[0].shape[2], width)
        + [dma, dma, dma((2,)), dma((2,)), dma, dma]
        + reduce_scratch(block, width)
        + reduce_sems(2),
        compiler_params=params(collective_id=number, has_side_effects=True),
        cost_estimate=link_cost(100.0),
        name="attention_back",
    )(span, q, k, v, lse, cosine, sine, q_gain, k_gain, w_out, d_rows, slots_t, *out, hidden)
    return *back, branch.reshape(-1, width), output


def projection_grads_kernel(
    normed, dq, dk, dv, heads, branch, wq_hbm, wk, wv, x_rows, d_hbm, gain, small,
    gq_ref, gk_ref, gv_ref, gout_ref, inputs_grad, gain_grad, small_sum,
    blocks, out_blocks, part, core_rows, far_rows, gain_own, tp_gains, tp_gain, ep_gains, wq, d_hidden,
    core_send, core_recv, x_send, x_recv, wq_sem, d_sem, *refs,
):
    me = lax.axis_index("tp")
    x, c = me // 2, me % 2
    other_core, other_x = {"tp": x * 2 + 1 - c}, {"tp": (1 - x) * 2 + c}
    sums = SumAll(small, small_sum, *refs[:5], refs[5:13])
    over_tp, over_ep = Exchange("tp", refs[13], refs[14]), Exchange("ep", refs[15], refs[16])
    reduce = EpReduce([blocks, out_blocks], BY_Z, refs[17:21], refs[21:])
    order, y = reduce.order, reduce.y
    rows, width = inputs_grad.shape
    nq, nk = dq.shape[1], dk.shape[1]

    load_wq = pltpu.make_async_copy(wq_hbm, wq, wq_sem)
    load_d = pltpu.make_async_copy(d_hbm, d_hidden, d_sem)
    load_wq.start()
    load_d.start()
    everyone = []
    for exchange in (over_tp, over_ep):
        exchange.each(
            lambda i, other, axis=exchange.axis: everyone.append((other >= 0, {axis: other}))
        )
    greet(everyone)

    def fill(j):
        cols = pl.ds(pl.multiple_of(j * rows, rows), rows)
        left = normed[:, cols].T
        blocks[j, :, 0:nq] = dot_nn(left, dq[...]).astype(BF)
        blocks[j, :, nq : nq + nk] = dot_nn(left, dk[...]).astype(BF)
        blocks[j, :, nq + nk : nq + 2 * nk] = dot_nn(left, dv[...]).astype(BF)
        out_blocks[j] = dot_nn(branch[:, cols].T, heads[...]).astype(BF)

    def spread_back(tp):
        lines = pl.ds(pl.multiple_of(tp * rows, rows), rows)
        for start in range(0, width, width // 4):
            cols = slice(start, start + width // 4)
            part[tp, :, cols] = (
                dot_nt(dq[lines, :], wq[cols, :])
                + dot_nt(dk[lines, :], wk[cols, :])
                + dot_nt(dv[lines, :], wv[cols, :])
            ).astype(BF)

    def to_core(xt):
        return remote(
            part.at[xt * 2 + 1 - c], core_rows.at[xt], core_send.at[xt], core_recv.at[xt], other_core
        )

    far, near = part.at[(1 - x) * 2 + c], part.at[x * 2 + c]
    to_x = remote(far, far_rows, x_send, x_recv, other_x)

    def fill_side(k):
        fill(order[k] * 2 + 1 - y)

    def fill_own(k):
        fill(order[k] * 2 + y)

    z = reduce.z
    at_end = (z == 0) | (z == Z_AXIS - 1)

    def step_if(there, *ks):
        @pl.when(there)
        def _():
            for k in ks:
                reduce.step_y(k)

    sums.start()
    fill_side(0)
    reduce.send_side(0)
    load_wq.wait()
    spread_back((1 - x) * 2 + 1 - c)
    to_core(1 - x).start()
    sums.across()
    fill_side(1)
    reduce.send_side(1)
    spread_back((1 - x) * 2 + c)
    to_core(1 - x).wait_recv()
    add_rows(far, [far, core_rows.at[1 - x]])
    to_x.start()
    fill_own(0)
    fill_side(2)
    reduce.send_side(2)
    step_if(at_end, 0)
    spread_back(x * 2 + 1 - c)
    to_core(x).start()
    spread_back(x * 2 + c)
    for k in range(1, Z_AXIS):
        fill_own(k)
    fill_side(3)
    step_if(at_end, 1)
    step_if(~at_end, 0)
    sums.back()
    to_core(x).wait_recv()
    to_x.wait_recv()
    load_d.wait()

    chunk = 32
    gain_own[...] = jnp.zeros_like(gain_own)

    @pl.loop(0, rows // chunk)
    def _(i):
        lines = pl.ds(pl.multiple_of(i * chunk, chunk), chunk)
        grad = near[lines, :].astype(F32) + core_rows[x, lines, :].astype(F32)
        grad = grad + far_rows[lines, :].astype(F32)
        back, gain_part = norm_back(grad, x_rows[lines, :].astype(F32), gain[...])
        inputs_grad[lines, :] = d_hidden[lines, :] + back
        gain_own[...] += gain_part

    over_tp.start(lambda t: gain_own, tp_gains)
    tp_gains[pl.ds(over_tp.me, 1)] = gain_own[...][None]
    over_tp.arrived(tp_gains)
    tp_gain[...] = jnp.sum(tp_gains[...], axis=0)
    over_ep.start(lambda e: tp_gain, ep_gains)
    ep_gains[pl.ds(over_ep.me, 1)] = tp_gain[...][None]
    reduce.send_side(3)
    step_if(at_end, 2)
    step_if(~at_end, 1, 2)
    sums.home()
    reduce.step_y(3)

    def total_of(terms, lines):
        value = terms[0][lines, :].astype(F32)
        for term in terms[1:]:
            value = value + term[lines, :].astype(F32)
        return value

    over_ep.arrived(ep_gains)
    gain_grad[...] = jnp.sum(ep_gains[...], axis=0)
    def write(terms):
        for start in range(0, rows, 64):
            lines = slice(start, start + 64)
            value = total_of(terms, lines)
            gq_ref[lines, :] = value[:, 0:nq]
            gk_ref[lines, :] = value[:, nq : nq + nk]
            gv_ref[lines, :] = value[:, nq + nk :]

    def write_out(terms):
        for start in range(0, rows, 128):
            lines = slice(start, start + 128)
            gout_ref[:, lines] = total_of(terms, lines).T

    reduce.own(0, write)
    reduce.own(1, write_out)
    reduce.sent()
    to_core(1 - x).wait_send()
    to_core(x).wait_send()
    to_x.wait_send()
    over_tp.sent(lambda t: gain_own, tp_gains)
    over_ep.sent(lambda e: tp_gain, ep_gains)
    sums.finish()


def projection_grads(
    normed, dq, dk, dv, heads, branch, wq, wk, wv, x_rows, d_hidden, gain, small_values, number
):
    rows, width = x_rows.shape
    ep_count, tp_count = lax.axis_size("ep"), lax.axis_size("tp")
    small = pack_small(small_values, tp_count, ep_count)
    if ep_count != 2 * Z_AXIS:

        def over_sequences(part, dim):
            return lax.psum_scatter(
                part.astype(BF), "ep", scatter_dimension=dim, tiled=True
            ).astype(F32)

        d_normed = (dot_nt(dq, wq) + dot_nt(dk, wk) + dot_nt(dv, wv)).astype(BF)
        d_mine = lax.psum_scatter(d_normed, "tp", scatter_dimension=0, tiled=True)
        back, gain_part = norm_back(d_mine.astype(F32), x_rows.astype(F32), gain)
        gain_sum, small_sum = lax.psum((gain_part, small), ("ep", "tp"))
        return (
            over_sequences(dot_tn(normed, dq), 0),
            over_sequences(dot_tn(normed, dk), 0),
            over_sequences(dot_tn(normed, dv), 0),
            over_sequences(dot_tn(heads, branch), 1),
            d_hidden + back,
            gain_sum,
            unpack_small(small_sum, small_values),
        )
    nq, nk = dq.shape[1], dk.shape[1]
    nh = heads.shape[1]
    vmem = pl.BlockSpec(memory_space=pltpu.VMEM)
    dma = pltpu.SemaphoreType.DMA
    *grads, small_sum = pl.pallas_call(
        projection_grads_kernel,
        in_specs=[vmem] * 6 + [ANY] + [vmem] * 3 + [ANY] + [vmem] * 2,
        out_specs=[vmem] * 7,
        out_shape=[
            jax.ShapeDtypeStruct((rows, nq), F32),
            jax.ShapeDtypeStruct((rows, nk), F32),
            jax.ShapeDtypeStruct((rows, nk), F32),
            jax.ShapeDtypeStruct((nh, rows), F32),
            jax.ShapeDtypeStruct((rows, width), F32),
            jax.ShapeDtypeStruct((1, width), F32),
            jax.ShapeDtypeStruct(small.shape, F32),
        ],
        scratch_shapes=[
            pltpu.VMEM((ep_count, rows, nq + 2 * nk), BF),
            pltpu.VMEM((ep_count, rows, nh), BF),
            pltpu.VMEM((tp_count, rows, width), BF),
            pltpu.VMEM((2, rows, width), BF),
            pltpu.VMEM((rows, width), BF),
            pltpu.VMEM((1, width), F32),
            pltpu.VMEM((tp_count, 1, width), F32),
            pltpu.VMEM((1, width), F32),
            pltpu.VMEM((ep_count, 1, width), F32),
            pltpu.VMEM(wq.shape, BF),
            pltpu.VMEM((rows, width), F32),
            dma((2,)), dma((2,)), dma, dma, dma, dma,
        ]
        + sum_scratch(small.shape)
        + exchange_sems("tp")
        + exchange_sems("ep")
        + [pltpu.VMEM((n, rows, c), BF) for c in (nq + 2 * nk, nh) for n in (Z_AXIS, Z_AXIS + 1)]
        + reduce_sems(2),
        compiler_params=params(collective_id=number, has_side_effects=True),
        cost_estimate=link_cost(110.0),
        name="projection_grads",
    )(normed, dq, dk, dv, heads, branch, wq, wk, wv, x_rows, d_hidden, gain, small)
    return *grads, unpack_small(small_sum, small_values)


def select_kernel(slot_ref, x_ref, c_ref, xs_ref, cs_ref):
    local, _, capacity, width = xs_ref.shape
    rows = x_ref.shape[1]
    place = jnp.concatenate(
        [
            (
                slot_ref[0, e : e + 1, :]
                == lax.broadcasted_iota(jnp.int32, (capacity, rows), 0)
            ).astype(F32)
            for e in range(local)
        ],
        axis=0,
    ).astype(BF)
    xs_ref[...] = dot_nn(place, x_ref[0]).astype(BF).reshape(xs_ref.shape)
    cs_ref[...] = dot_nn(place, c_ref[0]).astype(BF).reshape(cs_ref.shape)


def select_rows(slots, tokens, cots, capacity):
    blocks, local, rows = slots.shape
    width = tokens.shape[-1]
    block = pl.BlockSpec((1, rows, width), lambda b: (b, 0, 0))
    out = pl.BlockSpec((local, 1, capacity, width), lambda b: (0, b, 0, 0))
    shape = jax.ShapeDtypeStruct((local, blocks, capacity, width), BF)
    return pl.pallas_call(
        select_kernel,
        grid=(blocks,),
        in_specs=[pl.BlockSpec((1, local, rows), lambda b: (b, 0, 0)), block, block],
        out_specs=[out, out],
        out_shape=[shape, shape],
        compiler_params=params(),
        name="select_rows",
    )(slots, tokens, cots)


def pack_kernel(gate_ref, up_ref, down_ref, out_ref):
    for kind, ref in enumerate((gate_ref, up_ref, down_ref)):
        out_ref[kind, 0] = ref[0]


def pack_weights(weights, first, count):
    _, hidden, width = weights[0].shape
    block = pl.BlockSpec((1, hidden, width), lambda e: (first + e, 0, 0))
    return pl.pallas_call(
        pack_kernel,
        grid=(count,),
        in_specs=[block] * 3,
        out_specs=pl.BlockSpec((3, 1, hidden, width), lambda e: (0, e, 0, 0)),
        out_shape=jax.ShapeDtypeStruct((3, count, hidden, width), BF),
        compiler_params=params(),
        name="pack_weights",
    )(*weights)


def expert_kernel(
    x_ref, c_ref, w_ref, gate_ref, out_ref, dx_ref, act_ref, dg_ref, du_ref, dgate_ref
):
    width = x_ref.shape[-1]
    x, c = x_ref[0], c_ref[0]
    w_gate = w_ref[:, 0, 0].reshape(-1, width)
    w_up = w_ref[:, 1, 0].reshape(-1, width)
    w_down = w_ref[:, 2, 0].reshape(-1, width)
    gate = gate_ref[0]
    gate_pre = dot_nt(x, w_gate)
    up_pre = dot_nt(x, w_up)
    raw = dot_nt(c, w_down)
    sig = jax.nn.sigmoid(gate_pre)
    silu = gate_pre * sig
    act = silu * up_pre
    dgate_ref[0] = jnp.sum(act * raw, axis=-1, keepdims=True)
    act_low = (act * gate).astype(BF)
    d_act = raw * gate
    d_gate = (d_act * up_pre * sig * (1.0 + gate_pre * (1.0 - sig))).astype(BF)
    d_up = (d_act * silu).astype(BF)
    act_ref[0] = act_low
    dg_ref[0] = d_gate
    du_ref[0] = d_up
    out_ref[0] = dot_nn(act_low, w_down).astype(BF)
    dx_ref[0] = (dot_nn(d_gate, w_gate) + dot_nn(d_up, w_up)).astype(BF)


def experts_both_ways(x_slots, c_slots, w_all, slot_gate, first):
    _, number, width = x_slots.shape
    parts, _, local, hidden, _ = w_all.shape
    tile = number // 2
    taken = pl.BlockSpec((1, tile, width), lambda e, i: (first + e, i, 0))
    wide = pl.BlockSpec((1, tile, width), lambda e, i: (e, i, 0))
    mid = pl.BlockSpec((1, tile, parts * hidden), lambda e, i: (e, i, 0))
    thin = pl.BlockSpec((1, tile, 1), lambda e, i: (e, i, 0))
    wide_shape = jax.ShapeDtypeStruct((local, number, width), BF)
    mid_shape = jax.ShapeDtypeStruct((local, number, parts * hidden), BF)
    return pl.pallas_call(
        expert_kernel,
        grid=(local, 2),
        in_specs=[
            taken, taken,
            pl.BlockSpec((parts, 3, 1, hidden, width), lambda e, i: (0, 0, e, 0, 0)),
            pl.BlockSpec((1, tile, 1), lambda e, i: (first + e, i, 0)),
        ],
        out_specs=[wide, wide, mid, mid, mid, thin],
        out_shape=[
            wide_shape, wide_shape, mid_shape, mid_shape, mid_shape,
            jax.ShapeDtypeStruct((local, number, 1), F32),
        ],
        compiler_params=params(),
        name="experts_both_ways",
    )(x_slots, c_slots, w_all, slot_gate)


def expert_grads_kernel(x_ref, c_ref, act_ref, dg_ref, du_ref, out_ref):
    parts, _, _, hidden, width = out_ref.shape
    x, c = x_ref[0], c_ref[0]
    out_ref[:, 0, 0] = dot_tn(dg_ref[0], x).astype(BF).reshape(parts, hidden, width)
    out_ref[:, 1, 0] = dot_tn(du_ref[0], x).astype(BF).reshape(parts, hidden, width)
    out_ref[:, 2, 0] = dot_tn(act_ref[0], c).astype(BF).reshape(parts, hidden, width)


def expert_grads(x_slots, c_slots, act, d_gate, d_up, parts, first):
    local, number, inner = act.shape
    width = x_slots.shape[-1]
    wide = pl.BlockSpec((1, number, width), lambda e: (first + e, 0, 0))
    mid = pl.BlockSpec((1, number, inner), lambda e: (e, 0, 0))
    return pl.pallas_call(
        expert_grads_kernel,
        grid=(local,),
        in_specs=[wide, wide, mid, mid, mid],
        out_specs=pl.BlockSpec(
            (parts, 3, 1, inner // parts, width), lambda e: (0, 0, e, 0, 0)
        ),
        out_shape=jax.ShapeDtypeStruct((parts, 3, local, inner // parts, width), BF),
        compiler_params=params(),
        name="expert_grads",
    )(x_slots, c_slots, act, d_gate, d_up)


def combine_kernel(
    first_ref, slot_ref, dxa_ref, dxb_ref, outa_ref, outb_ref, dgate_ref, dx_sum_ref, out_sum_ref, pay_ref
):
    _, _, capacity, width = dxa_ref.shape
    local = slot_ref.shape[2]
    rows = slot_ref.shape[1]
    lane = lax.broadcasted_iota(jnp.int32, (rows, local * capacity), 1)
    half = pay_ref.shape[2] // 2
    column = lax.broadcasted_iota(jnp.int32, (rows, 2 * half), 1)
    total = jnp.zeros((rows, local * capacity), F32)
    pay = jnp.zeros(column.shape, F32)
    for e in range(local):
        hit = lane == slot_ref[0, :, e : e + 1] + e * capacity
        total = jnp.where(hit, 1.0, total)
        value = jnp.sum(jnp.where(hit, dgate_ref[0], 0.0), axis=1, keepdims=True)
        high = value.astype(BF).astype(F32)
        pay = jnp.where(column == first_ref[0, 0] + e, high, pay)
        pay = jnp.where(column == first_ref[0, 0] + e + half, value - high, pay)
    place = total.astype(BF)

    def both(a_ref, b_ref):
        pair = [ref[...].reshape(-1, width) for ref in (a_ref, b_ref)]
        return dot_nn(place, jnp.concatenate(pair, axis=0)).astype(BF)

    dx_sum_ref[0] = both(dxa_ref, dxb_ref)
    out_sum_ref[0] = both(outa_ref, outb_ref)
    pay_ref[0] = pay.astype(BF)


def combine_rows(first, slots_t, dx, out, d_gate_slots, experts):
    blocks, rows, local = slots_t.shape
    _, _, capacity, width = dx[0].shape
    lanes = -(-2 * experts // 128) * 128
    slot = pl.BlockSpec((local // 2, 1, capacity, width), lambda b: (0, b, 0, 0))
    block = pl.BlockSpec((1, rows, width), lambda b: (b, 0, 0))
    shape = jax.ShapeDtypeStruct((blocks, rows, width), BF)
    return pl.pallas_call(
        combine_kernel,
        grid=(blocks,),
        in_specs=[
            pl.BlockSpec(memory_space=pltpu.SMEM),
            pl.BlockSpec((1, rows, local), lambda b: (b, 0, 0)), slot, slot, slot, slot,
            pl.BlockSpec((1, 1, local * capacity), lambda b: (b, 0, 0)),
        ],
        out_specs=[block, block, pl.BlockSpec((1, rows, lanes), lambda b: (b, 0, 0))],
        out_shape=[shape, shape, jax.ShapeDtypeStruct((blocks, rows, lanes), BF)],
        compiler_params=params(),
        name="combine_rows",
    )(first, slots_t, *dx, *out, d_gate_slots)


def on_device(
    inputs,
    attn_gain,
    w_query,
    key_weight_matrix,
    value_weight_matrix,
    query_gain,
    key_gain,
    w_out,
    route_gain,
    w_router,
    w_gate,
    w_up,
    w_down,
    routes,
    image_starts,
    cotangent,
):
    tp_count = lax.axis_size("tp")
    ep_count = lax.axis_size("ep")
    tp_index = lax.axis_index("tp")
    ep_index = lax.axis_index("ep")
    length = inputs.shape[0]
    width = inputs.shape[1]
    rows = cotangent.shape[0]
    head_dim = query_gain.shape[0]
    local_experts = w_gate.shape[0]
    experts = local_experts * ep_count
    top = routes.shape[1]
    capacity = -(-(3 * rows * top // (2 * experts)) // 16) * 16

    pair = local_experts // 2

    weights = (w_gate.transpose(0, 2, 1), w_up.transpose(0, 2, 1), w_down)
    w_first = lax.all_gather(pack_weights(weights, 0, pair), "tp")

    normed, queries, key_rows, values = project(
        inputs, attn_gain[None], w_query, key_weight_matrix, value_weight_matrix
    )
    cosine, sine = rope_tables(length, head_dim)
    q_gain, k_gain = query_gain[None], key_gain[None]
    x_rows = lax.dynamic_slice_in_dim(inputs, tp_index * rows, rows, 0)
    heads, lse, hidden, moe_in, cot_all, second = attention(
        image_starts, queries, key_rows, values, cosine, sine, q_gain, k_gain,
        w_out, cotangent, x_rows, route_gain[None], weights, pair, 0,
    )
    w_second = lax.all_gather(second, "tp")
    logits = dot_nn(moe_in, w_router)
    router_probs = plain_softmax(logits)
    expert_ids = jnp.arange(experts, dtype=jnp.int32)
    ring_routes = lax.dynamic_index_in_dim(
        routes.reshape(ep_count, tp_count, rows, top), tp_index, 1, keepdims=False
    )
    my_routes = lax.dynamic_index_in_dim(ring_routes, ep_index, 0, keepdims=False)

    def routed_softmax(scores, picked):
        kept = jnp.where(picked, scores, MASKED)
        expo = jnp.where(picked, jnp.exp(kept - jnp.max(kept, axis=-1, keepdims=True)), 0.0)
        return expo / jnp.sum(expo, axis=-1, keepdims=True)

    my_pick = jnp.any(my_routes[:, :, None] == expert_ids[None, None, :], axis=1)
    gates = routed_softmax(logits, my_pick)
    all_pick = jnp.any(ring_routes[..., None] == expert_ids, axis=2)
    mask = lax.dynamic_slice_in_dim(all_pick, ep_index * local_experts, local_experts, 2)
    earlier = (jnp.arange(rows)[:, None] > jnp.arange(rows)[None, :]).astype(BF)
    slots_t = jnp.einsum(
        "tu,bue->bte", earlier, mask.astype(BF), preferred_element_type=F32
    ).astype(jnp.int32)
    slots_t = jnp.where(mask, slots_t, NOWHERE)
    slots = slots_t.transpose(0, 2, 1)
    ring = ep_count == 2 * Z_AXIS
    if ring:
        turned = lax.rem(expert_ids + ep_index * local_experts, experts)
        x_slots, c_slots, slot_gate = gather_select(
            moe_in,
            cot_all,
            slots,
            all_pick.astype(jnp.int32)[..., turned].transpose(0, 2, 1),
            w_router.T[turned],
            capacity,
            1,
        )
        slot_gate = slot_gate.reshape(local_experts, ep_count * capacity, 1)
    else:
        tokens_all = lax.all_gather(moe_in, "ep")
        logits_all = dot_nn(tokens_all.reshape(-1, width), w_router).reshape(ep_count, rows, experts)
        gate_of = lax.dynamic_slice_in_dim(
            routed_softmax(logits_all, all_pick), ep_index * local_experts, local_experts, 2
        )
        place = slots[:, :, None, :] == jnp.arange(capacity, dtype=jnp.int32)[:, None]
        slot_gate = jnp.sum(
            jnp.where(place, gate_of.transpose(0, 2, 1)[:, :, None, :], 0.0), axis=-1
        )
        slot_gate = slot_gate.transpose(1, 0, 2).reshape(local_experts, ep_count * capacity, 1)
        x_slots, c_slots = select_rows(slots, tokens_all, cot_all, capacity)
    flat = (local_experts, ep_count * capacity, width)
    x_slots, c_slots = x_slots.reshape(flat), c_slots.reshape(flat)

    def over_rings(grads):
        return lax.psum_scatter(grads.reshape(-1, width), "tp", scatter_dimension=0, tiled=True)

    out_a, dx_a, *inner_a, dg_a = experts_both_ways(x_slots, c_slots, w_first, slot_gate, 0)
    grads_a = expert_grads(x_slots, c_slots, *inner_a, tp_count, 0)
    x_slots, grads_a = lax.optimization_barrier((x_slots, grads_a))
    mine_a = over_rings(grads_a)
    out_b, dx_b, *inner_b, dg_b = experts_both_ways(x_slots, c_slots, w_second, slot_gate, pair)
    deep = (pair, ep_count, capacity, width)
    dx_slots = [dx_a.reshape(deep), dx_b.reshape(deep)]
    out_slots = [out_a.reshape(deep), out_b.reshape(deep)]
    d_gate_slots = (
        jnp.concatenate([dg_a, dg_b])
        .reshape(local_experts, ep_count, capacity)
        .transpose(1, 0, 2)
        .reshape(ep_count, 1, local_experts * capacity)
    )
    counts = jnp.sum((routes[:, :, None] == expert_ids[None, None, :]).astype(F32), axis=(0, 1))
    total_tokens = routes.shape[0]
    share = counts / (total_tokens * top)
    coeff = AUX * experts * share
    if ring:
        d_hidden, d_rows, router_part, route_gain_part, grads_b = input_grads(
            slots_t, d_gate_slots, dx_slots, x_slots, c_slots, inner_b,
            [
                hidden, moe_in, cotangent, route_gain[None], gates, router_probs,
                coeff[None], w_router.T,
            ],
            experts, tp_count, 2,
        )
    else:
        grads_b = expert_grads(x_slots, c_slots, *inner_b, tp_count, pair)
        dx_part, out_slots, gate_part = combine_rows(
            (ep_index * local_experts).reshape(1, 1), slots_t, dx_slots, out_slots, d_gate_slots, experts
        )
        dx_mine = lax.psum_scatter(dx_part, "ep", scatter_dimension=0).astype(F32)
        gate_mine = lax.psum_scatter(gate_part, "ep", scatter_dimension=0).astype(F32)
        lanes = gate_mine.shape[1] // 2
        d_gates = gate_mine[:, :experts] + gate_mine[:, lanes : lanes + experts]
        d_logits = gates * (d_gates - jnp.sum(gates * d_gates, axis=-1, keepdims=True))
        d_logits = d_logits + router_probs * (
            coeff - jnp.sum(router_probs * coeff, axis=-1, keepdims=True)
        )
        d_low = d_logits.astype(BF)
        router_part = dot_tn(d_low, moe_in)
        d_moe = dot_nt(d_low, w_router) + dx_mine
        back, route_gain_part = norm_back(d_moe, hidden, route_gain[None])
        d_hidden = cotangent.astype(F32) + back
        d_rows = d_hidden.astype(BF)
    d_rows, mine_a, grads_b = lax.optimization_barrier((d_rows, mine_a, grads_b))
    mine_b = over_rings(grads_b)
    mine_a, mine_b = [m.reshape(3, pair, -1, width) for m in (mine_a, mine_b)]
    w_gate_grad, w_up_grad, w_down_grad = widen_grads(mine_a, mine_b)
    w_gate_grad, w_up_grad = w_gate_grad.transpose(0, 2, 1), w_up_grad.transpose(0, 2, 1)
    prob_local = jnp.sum(router_probs, axis=0)
    d_queries, d_keys, d_values, query_gain_part, key_gain_part, d_branch, output = attention_back(
        image_starts, queries, key_rows, values, lse, cosine, sine, q_gain, k_gain,
        w_out, d_rows, slots_t, out_slots, hidden, 3,
    )
    w_query_grad, w_key_grad, w_value_grad, w_out_grad, inputs_grad, attn_gain_grad, small = projection_grads(
        normed, d_queries, d_keys, d_values, heads, d_branch,
        w_query, key_weight_matrix, value_weight_matrix,
        x_rows, d_hidden, attn_gain[None],
        [router_part, route_gain_part[0], query_gain_part[0], key_gain_part[0], prob_local],
        5,
    )
    w_router_grad, route_gain_grad, query_gain_grad, key_gain_grad, prob_all = small
    w_router_grad = w_router_grad.T
    attn_gain_grad = attn_gain_grad[0]
    aux_loss = experts * jnp.sum(share * (prob_all / total_tokens))
    return (
        output,
        aux_loss,
        inputs_grad,
        attn_gain_grad,
        w_query_grad,
        w_key_grad,
        w_value_grad,
        query_gain_grad,
        key_gain_grad,
        w_out_grad,
        route_gain_grad,
        w_router_grad,
        w_gate_grad,
        w_up_grad,
        w_down_grad,
    )


def solution(mesh):
    return jax.shard_map(
        on_device,
        mesh=mesh,
        in_specs=(
            P("ep", None),
            P(),
            P(None, "tp"),
            P(None, "tp"),
            P(None, "tp"),
            P(),
            P(),
            P("tp", None),
            P(),
            P(),
            P("ep", None, "tp"),
            P("ep", None, "tp"),
            P("ep", "tp", None),
            P(),
            P("ep", None),
            P(("ep", "tp"), None),
        ),
        out_specs=(
            P(("ep", "tp"), None),
            P(),
            P(("ep", "tp"), None),
            P(),
            P("ep", "tp"),
            P("ep", "tp"),
            P("ep", "tp"),
            P(),
            P(),
            P("tp", "ep"),
            P(),
            P(),
            P("ep", None, "tp"),
            P("ep", None, "tp"),
            P("ep", "tp", None),
        ),
        check_vma=False,
    )
```
